32 devices in a mesh: dp: 16 (over z, x, core), tensor: 2 (over y).
Axes of the slice: x: 2, y: 2, z: 4, core: 2. Of those that a mesh axis runs over, the one named last changes fastest.
Arguments:
- tokens_in: bfloat16 [16384, 1024], P(('dp', 'tensor')), may hold values from -6 to 6
- segments: int32 [16, 1024], P('dp'), may hold values from 0 to 7, never falling along the last dimension, each value on 1 to 256 neighbouring positions
- w_qkv: bfloat16 [2, 1024, 3, 1024], P(None, None, None, 'tensor'), may hold values from -0.1875 to 0.1875
- qv_bias: float32 [2, 2, 1024], P(None, None, 'tensor'), may hold values from -3 to 3
- w_out: bfloat16 [2, 1024, 1024], P(None, 'tensor'), may hold values from -1.5 to 1.5
- w_up: bfloat16 [2, 1024, 4096], P(None, None, 'tensor'), may hold values from -0.1875 to 0.1875
- up_bias: float32 [2, 4096], P(None, 'tensor'), may hold values from -3 to 3
- w_down: bfloat16 [2, 4096, 1024], P(None, 'tensor'), may hold values from -0.09375 to 0.09375
- out_bias: float32 [2, 2, 1024], replicated, may hold values from -2 to 2
- ln_gain: float32 [2, 2, 1024], replicated, may hold values from 0.5 to 1.5
- ln_bias: float32 [2, 2, 1024], replicated, may hold values from -2 to 2
- cotangent: bfloat16 [16384, 1024], P(('dp', 'tensor')), may hold values from -6 to 6
Outputs:
- out_act: bfloat16 [16384, 1024], P(('dp', 'tensor'))
- grad_in: bfloat16 [16384, 1024], P(('dp', 'tensor'))
- grad_qkv: float32 [2, 1024, 3, 1024], P(None, None, None, 'tensor')
- grad_qv_bias: float32 [2, 2, 1024], P(None, None, 'tensor')
- grad_out_w: float32 [2, 1024, 1024], P(None, 'tensor')
- grad_up: float32 [2, 1024, 4096], P(None, None, 'tensor')
- grad_up_bias: float32 [2, 4096], P(None, 'tensor')
- grad_down: float32 [2, 4096, 1024], P(None, 'tensor')
- grad_out_bias: float32 [2, 2, 1024], replicated
- grad_ln_gain: float32 [2, 2, 1024], replicated
- grad_ln_bias: float32 [2, 2, 1024], replicated
The draws below stay inside these ranges and needn't reach their ends.
Inputs may be any that keep to these rules, and one draw needn't show every extreme that they name: `segments`: within each window the episode numbers never fall, start at 0, and take every value from 0 to 7, each on at most 256 positions.
All inputs are finite; a program needn't handle non-finite values.
Results may differ from the reference program's by a relative error of at most 0.025.
Values may be sent and summed in bfloat16 or wider, within the bound.
A program may use at most 320 MiB of HBM per device.

```python
import math
import jax
import jax.numpy as jnp
import numpy as np
from jax import lax

D = 1024
HEAD_DIM = 64
FF = 4096
WINDOW = 1024
LAYERS = 2
NSEQ = 16
TOKENS = 16384


def block_levels(stream_key, shape, split, smallest, high):
    level = 1.0
    for position, shards_of in split:
        heights = jax.random.uniform(jax.random.fold_in(jax.random.fold_in(stream_key, 6), position), (shards_of,), jnp.float32, smallest / len(split), high / len(split))
        level = level * jnp.repeat(jnp.exp(heights), shape[position] // shards_of).reshape((-1,) + (1,) * (len(shape) - 1 - position))
    return level


def length_profile(number_of, total, most, slope):
    weights = [(1 << 20) // math.isqrt(rank ** slope) + 1 for rank in range(2, number_of + 1)]
    spare, counts = total - most - (number_of - 1), [1] * (number_of - 1)
    while spare > 0:
        free = [i for i in range(number_of - 1) if counts[i] < most]
        mass, budget = sum([weights[i] for i in free]), spare
        for i in free:
            more = min(most - counts[i], max(1, budget * weights[i] // mass), spare)
            counts[i] = counts[i] + more
            spare = spare - more
    return np.array([most] + counts)


def ragged_sizes(rng, amount, total, limit, lean):
    if amount == 2:
        one = jax.random.randint(rng, (), max(1, total - limit), min(limit, total - 1) + 1)
        return jnp.stack([one, total - one])
    lengths = jnp.asarray(length_profile(amount, total, limit, lean), jnp.int32)
    twos = (amount - 1) // 2
    donor, taker = lengths[1:1 + 2 * twos:2], lengths[2:2 + 2 * twos:2]
    slack = jnp.minimum(donor - 1, limit - taker)
    passed = jax.random.randint(jax.random.fold_in(rng, 1), (twos,), 0, 1 << 20) % (slack + 1)
    lengths = lengths.at[1:1 + 2 * twos:2].set(donor - passed).at[2:2 + 2 * twos:2].set(taker + passed)
    return lengths[jax.random.permutation(jax.random.fold_in(rng, 2), amount)]


def bell_draw(own_key, dims, scale, most, split=(), kind=jnp.bfloat16):
    drawn = scale * jax.random.normal(own_key, dims, jnp.float32)
    if split:
        drawn = drawn * block_levels(own_key, dims, split, -0.22, 0.18)
    return jnp.clip(drawn, -most, most).astype(kind)


def setup_inputs(seed: int = 0) -> dict:
    seeds = jax.random.split(jax.random.key(seed), 13)
    return {
        "tokens_in": bell_draw(seeds[0], (TOKENS, D), 1.0, 6.0, ((0, 32),)),
        "segments": jax.vmap(lambda own: jnp.searchsorted(jnp.cumsum(ragged_sizes(own, 8, WINDOW, WINDOW // 4, 1)), jnp.arange(WINDOW), side="right"))(jax.random.split(seeds[1], NSEQ)).reshape((NSEQ, WINDOW)).astype(jnp.int32),
        "w_qkv": bell_draw(seeds[2], (LAYERS, D, 3, D), D ** -0.5, 0.1875, ((3, 2),)),
        "qv_bias": bell_draw(seeds[3], (LAYERS, 2, D), 0.5, 3.0, ((2, 2),), jnp.float32),
        "w_out": bell_draw(seeds[4], (LAYERS, D, D), (max(D // 64, 4)) ** -0.5, 1.5, ((1, 2),)),
        "w_up": bell_draw(seeds[5], (LAYERS, D, FF), D ** -0.5, 0.1875, ((2, 2),)),
        "up_bias": bell_draw(seeds[6], (LAYERS, FF), 0.5, 3.0, ((1, 2),), jnp.float32),
        "w_down": bell_draw(seeds[7], (LAYERS, FF, D), FF ** -0.5, 0.09375, ((1, 2),)),
        "out_bias": bell_draw(seeds[8], (LAYERS, 2, D), 0.3, 2.0, (), jnp.float32),
        "ln_gain": jnp.clip(1.0 + 0.1 * jax.random.normal(seeds[9], (LAYERS, 2, D), jnp.float32), 0.5, 1.5),
        "ln_bias": bell_draw(seeds[10], (LAYERS, 2, D), 0.3, 2.0, (), jnp.float32),
        "cotangent": bell_draw(seeds[11], (TOKENS, D), 1.0, 6.0, ((0, 32),)),
    }


@jax.custom_vjp
def low(v):
    return lax.optimization_barrier(v.astype(jnp.bfloat16)).astype(jnp.float32)

@jax.custom_vjp
def low_back(v):
    return v

def low_keep(v):
    return (low(v), None)

def low_pass(kept, grad):
    return (grad,)

def back_keep(v):
    return (v, None)

def back_low(kept, grad):
    return (low(grad),)
low.defvjp(low_keep, low_pass)
low_back.defvjp(back_keep, back_low)
epsilon = 1e-05
gelu_coeff = 0.7978845608028654
cubic_coeff = 0.044715
masked_score = -1e+30
highest_mode = lax.Precision.HIGHEST

def layer_norm(values, gain, shift):
    average = lax.optimization_barrier(jnp.mean(values, axis=-1, keepdims=True))
    centred = values - average
    variance = lax.optimization_barrier(jnp.mean(centred * centred, axis=-1, keepdims=True))
    return centred * lax.rsqrt(variance + epsilon) * gain + shift

def gelu_tanh(before):
    tanh_input = gelu_coeff * (before + cubic_coeff * before * before * before)
    return 0.5 * before * (1.0 + jnp.tanh(tanh_input))

def block_forward(residual, segment_ids, params):
    w_qkv, qv_bias, w_out, w_up, up_bias, w_down, out_bias, gains, shifts = params
    groups, window, model_width = residual.shape
    heads_total = model_width // HEAD_DIM
    normed = low(layer_norm(residual, gains[0], shifts[0]))
    projected = jnp.einsum('gwd,dsc->gwsc', normed, w_qkv, precision=highest_mode)
    query_rows = low(low_back(projected[:, :, 0] + qv_bias[0])).reshape(groups, window, heads_total, HEAD_DIM)
    key_rows = low(low_back(projected[:, :, 1])).reshape(groups, window, heads_total, HEAD_DIM)
    value_rows = low(low_back(projected[:, :, 2] + qv_bias[1])).reshape(groups, window, heads_total, HEAD_DIM)
    scores = jnp.einsum('gqhe,gkhe->ghqk', query_rows, key_rows, precision=highest_mode) * HEAD_DIM ** (-0.5)
    scores = low_back(scores)
    places = jnp.arange(window, dtype=jnp.int32)
    allowed = (places[:, None] >= places[None, :])[None] & (segment_ids[:, :, None] == segment_ids[:, None, :])
    scores = jnp.where(allowed[:, None], scores, masked_score)
    softmax_low = low(jax.nn.softmax(scores, axis=-1))
    attended = jnp.einsum('ghqk,gkhe->gqhe', softmax_low, value_rows, precision=highest_mode)
    attended = low(low_back(attended.reshape(groups, window, model_width)))
    attn_branch = jnp.einsum('gwc,cd->gwd', attended, w_out, precision=highest_mode) + out_bias[0]
    middle = residual + low_back(attn_branch)
    normed_two = low(layer_norm(middle, gains[1], shifts[1]))
    before = low_back(jnp.einsum('gwd,df->gwf', normed_two, w_up, precision=highest_mode) + up_bias)
    activated = low(gelu_tanh(before))
    ffn_branch = jnp.einsum('gwf,fd->gwd', activated, w_down, precision=highest_mode) + out_bias[1]
    return middle + low_back(ffn_branch)

def forward_layers(residual, segment_ids, params):
    for layer_index in range(LAYERS):
        residual = block_forward(residual, segment_ids, tuple((member[layer_index] for member in params)))
    return residual

def reference(tokens_in, segments, w_qkv, qv_bias, w_out, w_up, up_bias, w_down, out_bias, ln_gain, ln_bias, cotangent):
    params = tuple((member.astype(jnp.float32) for member in (w_qkv, qv_bias, w_out, w_up, up_bias, w_down, out_bias, ln_gain, ln_bias)))
    seq_count, window = segments.shape
    model_width = tokens_in.shape[1]
    group_size = 2 if seq_count % 2 == 0 else 1
    group_count = seq_count // group_size
    inputs_grouped = tokens_in.astype(jnp.float32).reshape(group_count, group_size, window, model_width)
    cotangent_grouped = cotangent.astype(jnp.float32).reshape(group_count, group_size, window, model_width)
    segment_grouped = segments.reshape(group_count, group_size, window)

    def one_group(running, member_group):
        input_group, segment_group, cotangent_group = member_group
        output_group, pullback = jax.vjp(lambda values, weights: forward_layers(values, segment_group, weights), input_group, params)
        grad_group, grad_params = pullback(cotangent_group)
        return (jax.tree.map(jnp.add, running, grad_params), (output_group, grad_group))
    running = jax.tree.map(jnp.zeros_like, params)
    running, (outputs, gradients) = lax.scan(one_group, running, (inputs_grouped, segment_grouped, cotangent_grouped))
    out_act = outputs.reshape(tokens_in.shape).astype(jnp.bfloat16)
    grad_in = gradients.reshape(tokens_in.shape).astype(jnp.bfloat16)
    return (out_act, grad_in, running[0], running[1], running[2], running[3], running[4], running[5], running[6], running[7], running[8])
```

```python
import jax
import jax.numpy as jnp
from jax import lax
from jax.experimental import pallas as pl
from jax.experimental.pallas import tpu as pltpu
from jax.sharding import PartitionSpec as P

HEAD_DIM = 64


epsilon = 1e-05
gelu_coeff = 0.7978845608028654
cubic_coeff = 0.044715
masked_score = -1e30


def as_sent(shard):

    def short(part):
        return part.astype(jnp.bfloat16) if part.dtype == jnp.float32 else part

    return jax.tree.map(short, shard)


def layer_norm(values, gain, shift):
    average = jnp.mean(values, axis=-1, keepdims=True)
    centred = values - average
    inverse = lax.rsqrt(jnp.mean(centred * centred, axis=-1, keepdims=True) + epsilon)
    unit_rows = centred * inverse
    return (unit_rows * gain + shift, unit_rows, inverse)


def norm_backward(incoming, unit_rows, inverse, gain):
    scaled = incoming * gain
    first_mean = jnp.mean(scaled, axis=-1, keepdims=True)
    second_mean = jnp.mean(scaled * unit_rows, axis=-1, keepdims=True)
    through = inverse * (scaled - first_mean - unit_rows * second_mean)
    return (through, jnp.sum(incoming * unit_rows, axis=0), jnp.sum(incoming, axis=0))


def gelu_tanh(before):
    tanh_input = gelu_coeff * (before + cubic_coeff * before * before * before)
    return 0.5 * before * (1.0 + jnp.tanh(tanh_input))


def gelu_slope(before):
    tanh_input = gelu_coeff * (before + cubic_coeff * before * before * before)
    tangent = jnp.tanh(tanh_input)
    return 0.5 * (1.0 + tangent) + 0.5 * before * (1.0 - tangent * tangent) * gelu_coeff * (
        1.0 + 3.0 * cubic_coeff * before * before
    )


def masked_scores(query_block, key_seq, segment_row, offset, block_rows):
    window = key_seq.shape[0]
    scores = jnp.einsum(
        "qhe,khe->hqk", query_block, key_seq, preferred_element_type=jnp.float32
    ) * HEAD_DIM ** (-0.5)
    query_place = offset + lax.iota(jnp.int32, block_rows)
    key_place = lax.iota(jnp.int32, window)
    query_segment = segment_row[offset : offset + block_rows]
    allowed = (query_place[:, None] >= key_place[None, :]) & (
        query_segment[:, None] == segment_row[None, :]
    )
    return jnp.where(allowed[None], scores, masked_score)


def split_heads(flat_rows, seq_count):
    return flat_rows.reshape(
        seq_count, flat_rows.shape[0] // seq_count, flat_rows.shape[1] // HEAD_DIM, HEAD_DIM
    )


def attend_forward(query_rows, key_rows, value_rows, segments):
    seq_count, window = segments.shape
    block_rows = min(512, window)

    def one_sequence(member):
        query_seq, key_seq, value_seq, segment_row = member
        outputs = []
        totals = []
        for block_index in range(window // block_rows):
            offset = block_index * block_rows
            scores = masked_scores(
                query_seq[offset : offset + block_rows], key_seq, segment_row, offset, block_rows
            )
            highest = jnp.max(scores, axis=-1, keepdims=True)
            raised = jnp.exp(scores - highest)
            summed = jnp.sum(raised, axis=-1, keepdims=True)
            softmax_low = (raised / summed).astype(jnp.bfloat16)
            block_out = jnp.einsum(
                "hqk,khe->qhe", softmax_low, value_seq, preferred_element_type=jnp.float32
            )
            outputs.append(block_out.astype(jnp.bfloat16))
            totals.append(highest[..., 0] + jnp.log(summed[..., 0]))
        return (jnp.concatenate(outputs, axis=0), jnp.stack(totals, axis=0))

    attended, log_totals = lax.map(
        one_sequence,
        (
            split_heads(query_rows, seq_count),
            split_heads(key_rows, seq_count),
            split_heads(value_rows, seq_count),
            segments,
        ),
    )
    return (attended.reshape(query_rows.shape), log_totals)


def attend_backward(query_rows, key_rows, value_rows, segments, log_totals, grad_attended):
    seq_count, window = segments.shape
    block_rows = min(512, window)
    scaling = HEAD_DIM ** (-0.5)

    def one_sequence(member):
        query_seq, key_seq, value_seq, segment_row, totals_seq, grad_seq = member
        query_parts = []
        grad_keys = jnp.zeros(key_seq.shape, jnp.float32)
        grad_values = jnp.zeros(value_seq.shape, jnp.float32)
        for block_index in range(window // block_rows):
            offset = block_index * block_rows
            query_block = query_seq[offset : offset + block_rows]
            grad_block = grad_seq[offset : offset + block_rows]
            scores = masked_scores(query_block, key_seq, segment_row, offset, block_rows)
            softmax_exact = jnp.exp(scores - totals_seq[block_index][..., None])
            softmax_low = softmax_exact.astype(jnp.bfloat16)
            grad_softmax = jnp.einsum(
                "qhe,khe->hqk", grad_block, value_seq, preferred_element_type=jnp.float32
            )
            row_terms = jnp.sum(softmax_exact * grad_softmax, axis=-1, keepdims=True)
            grad_scores = (softmax_exact * (grad_softmax - row_terms)).astype(jnp.bfloat16)
            query_parts.append(
                jnp.einsum("hqk,khe->qhe", grad_scores, key_seq, preferred_element_type=jnp.float32)
                * scaling
            )
            grad_keys = (
                grad_keys
                + jnp.einsum(
                    "hqk,qhe->khe", grad_scores, query_block, preferred_element_type=jnp.float32
                )
                * scaling
            )
            grad_values = grad_values + jnp.einsum(
                "hqk,qhe->khe", softmax_low, grad_block, preferred_element_type=jnp.float32
            )
        grad_query = jnp.concatenate(query_parts, axis=0)
        return (
            grad_query.astype(jnp.bfloat16),
            grad_keys.astype(jnp.bfloat16),
            grad_values.astype(jnp.bfloat16),
        )

    grad_query, grad_keys, grad_values = lax.map(
        one_sequence,
        (
            split_heads(query_rows, seq_count),
            split_heads(key_rows, seq_count),
            split_heads(value_rows, seq_count),
            segments,
            log_totals,
            split_heads(grad_attended, seq_count),
        ),
    )
    return (
        grad_query.reshape(query_rows.shape),
        grad_keys.reshape(query_rows.shape),
        grad_values.reshape(query_rows.shape),
    )


def layer_forward(residual, segments, weights):
    w_qkv, qv_bias, w_out, w_up, up_bias, w_down, out_bias, gains, shifts = weights
    row_count = residual.shape[0]
    normed, unit_one, inverse_one = layer_norm(residual, gains[0], shifts[0])
    normed_all = lax.all_gather(normed.astype(jnp.bfloat16), "tensor", axis=0, tiled=True)
    projected = jnp.einsum("td,dsc->tsc", normed_all, w_qkv, preferred_element_type=jnp.float32)
    query_rows = (projected[:, 0] + qv_bias[0]).astype(jnp.bfloat16)
    key_rows = projected[:, 1].astype(jnp.bfloat16)
    value_rows = (projected[:, 2] + qv_bias[1]).astype(jnp.bfloat16)
    attended, log_totals = attend_forward(query_rows, key_rows, value_rows, segments)
    middle = (
        residual
        + lax.psum_scatter(
            jnp.dot(
                lax.slice_in_dim(attended, 0, row_count * lax.axis_size("tensor"), axis=0),
                w_out,
                preferred_element_type=jnp.float32,
            ).astype(jnp.bfloat16),
            "tensor",
            scatter_dimension=0,
            tiled=True,
        ).astype(jnp.float32)
        + out_bias[0]
    )
    normed_two, unit_two, inverse_two = layer_norm(middle, gains[1], shifts[1])
    normed_low = normed_two.astype(jnp.bfloat16)
    ffn_rows = lax.all_gather(normed_low, "tensor", axis=0, tiled=True)
    before = jnp.dot(ffn_rows, w_up, preferred_element_type=jnp.float32) + up_bias
    activated = gelu_tanh(before).astype(jnp.bfloat16)
    ffn_branch = lax.psum_scatter(
        jnp.dot(
            lax.slice_in_dim(activated, 0, row_count * lax.axis_size("tensor"), axis=0),
            w_down,
            preferred_element_type=jnp.float32,
        ).astype(jnp.bfloat16),
        "tensor",
        scatter_dimension=0,
        tiled=True,
    ).astype(jnp.float32)
    kept_ffn = (w_up, w_down)
    result = middle + ffn_branch + out_bias[1]
    kept_state = (
        unit_one,
        inverse_one,
        normed_all,
        query_rows,
        key_rows,
        value_rows,
        attended,
        log_totals,
        unit_two,
        inverse_two,
        ffn_rows,
        before,
        activated,
        kept_ffn,
    )
    return (result, kept_state)


def layer_backward(grad_residual, segments, weights, kept_state):
    w_qkv, qv_bias, w_out, w_up, up_bias, w_down, out_bias, gains, shifts = weights
    (
        unit_one,
        inverse_one,
        normed_all,
        query_rows,
        key_rows,
        value_rows,
        attended,
        log_totals,
        unit_two,
        inverse_two,
        ffn_rows,
        before,
        activated,
        kept_ffn,
    ) = kept_state
    up_used, down_used = kept_ffn
    row_count = grad_residual.shape[0]
    grad_branch = grad_residual.astype(jnp.bfloat16)
    bias_down = jnp.sum(grad_branch, axis=0, dtype=jnp.float32)
    grad_rows = lax.all_gather(grad_branch, "tensor", axis=0, tiled=True)
    grad_hidden = jnp.einsum("td,fd->tf", grad_rows, down_used, preferred_element_type=jnp.float32)
    grad_before = (grad_hidden * gelu_slope(before)).astype(jnp.bfloat16)
    grad_down = jnp.einsum("tf,td->fd", activated, grad_rows, preferred_element_type=jnp.float32)
    grad_up = jnp.einsum("td,tf->df", ffn_rows, grad_before, preferred_element_type=jnp.float32)
    grad_up_bias = jnp.sum(grad_before, axis=0, dtype=jnp.float32)
    piece_rows = lax.slice_in_dim(grad_before, 0, row_count * lax.axis_size("tensor"), axis=0)
    grad_normed_two = lax.psum_scatter(
        jnp.einsum("tf,df->td", piece_rows, w_up, preferred_element_type=jnp.float32).astype(
            jnp.bfloat16
        ),
        "tensor",
        scatter_dimension=0,
        tiled=True,
    ).astype(jnp.float32)
    through_two, gain_two, shift_two = norm_backward(
        grad_normed_two, unit_two, inverse_two, gains[1]
    )
    grad_middle = grad_residual + through_two
    grad_attn_branch = grad_middle.astype(jnp.bfloat16)
    bias_attn = jnp.sum(grad_attn_branch, axis=0, dtype=jnp.float32)
    grad_attn_all = lax.all_gather(grad_attn_branch, "tensor", axis=0, tiled=True)
    grad_out_w = jnp.einsum(
        "tc,td->cd", attended, grad_attn_all, preferred_element_type=jnp.float32
    )
    grad_attended = jnp.einsum(
        "td,cd->tc", grad_attn_all, w_out, preferred_element_type=jnp.float32
    ).astype(jnp.bfloat16)
    grad_query, grad_keys, grad_values = attend_backward(
        query_rows, key_rows, value_rows, segments, log_totals, grad_attended
    )
    grad_projected = jnp.stack((grad_query, grad_keys, grad_values), axis=1)
    grad_qkv = jnp.einsum(
        "td,tsc->dsc", normed_all, grad_projected, preferred_element_type=jnp.float32
    )
    grad_qv_bias = jnp.stack(
        (
            jnp.sum(grad_query, axis=0, dtype=jnp.float32),
            jnp.sum(grad_values, axis=0, dtype=jnp.float32),
        )
    )
    piece_rows = lax.slice_in_dim(grad_projected, 0, row_count * lax.axis_size("tensor"), axis=0)
    grad_normed = lax.psum_scatter(
        jnp.einsum("tsc,dsc->td", piece_rows, w_qkv, preferred_element_type=jnp.float32).astype(
            jnp.bfloat16
        ),
        "tensor",
        scatter_dimension=0,
        tiled=True,
    ).astype(jnp.float32)
    through_one, gain_one, shift_one = norm_backward(grad_normed, unit_one, inverse_one, gains[0])
    grad_input = grad_middle + through_one
    spread = (grad_qkv, grad_qv_bias, grad_out_w, grad_up, grad_up_bias, grad_down)
    shared = (
        jnp.stack((bias_attn, bias_down)),
        jnp.stack((gain_one, gain_two)),
        jnp.stack((shift_one, shift_two)),
    )
    return (grad_input, spread, shared)


def local_general(
    tokens_in,
    segments,
    w_qkv,
    qv_bias,
    w_out,
    w_up,
    up_bias,
    w_down,
    out_bias,
    ln_gain,
    ln_bias,
    cotangent,
):
    layers_total = w_qkv.shape[0]
    all_params = (w_qkv, qv_bias, w_out, w_up, up_bias, w_down, out_bias, ln_gain, ln_bias)
    residual = tokens_in.astype(jnp.float32)
    kept_layers = []
    for layer_index in range(layers_total):
        weights = tuple((member_array[layer_index] for member_array in all_params))
        residual, kept_state = layer_forward(residual, segments, weights)
        kept_layers.append(kept_state)
    out_act = residual.astype(jnp.bfloat16)
    grad_residual = cotangent.astype(jnp.float32)
    spread_layers = []
    shared_layers = []
    for layer_index in reversed(range(layers_total)):
        weights = tuple((member_array[layer_index] for member_array in all_params))
        grad_residual, spread, shared = layer_backward(
            grad_residual, segments, weights, kept_layers[layer_index]
        )
        spread_layers.insert(0, spread)
        shared_layers.insert(0, shared)
    spread_stack = tuple(
        (
            jnp.stack([spread_layers[layer_index][position] for layer_index in range(layers_total)])
            for position in range(6)
        )
    )
    spread_stack = jax.tree.map(
        lambda part: part.astype(jnp.float32), lax.psum(as_sent(spread_stack), "dp")
    )
    shared_stack = tuple(
        (
            jnp.stack([shared_layers[layer_index][position] for layer_index in range(layers_total)])
            for position in range(3)
        )
    )
    shared_stack = lax.psum(shared_stack, ("dp", "tensor"))
    grad_in = grad_residual.astype(jnp.bfloat16)
    return (out_act, grad_in) + tuple(spread_stack) + tuple(shared_stack)


CORE_BIT = 1
X_BIT = 2
Z_BIT = 4
BAND = 256
LANES = 128
VMEM_ASKED = 56 * 2**20


def dot_nt(left, right):
    return lax.dot_general(left, right, (((1,), (1,)), ((), ())), preferred_element_type=jnp.float32)


def dot_tn(left, right):
    return lax.dot_general(left, right, (((0,), (0,)), ((), ())), preferred_element_type=jnp.float32)


def fill_band_bias(segq_ref, segk_ref, bias_ref):
    blocks = bias_ref.shape[0]
    for block in range(blocks):
        rows = slice(block * BAND, (block + 1) * BAND)
        columns = slice(block * BAND, (block + 2) * BAND)
        row_place = lax.broadcasted_iota(jnp.int32, (BAND, 2 * BAND), 0) + BAND
        column_place = lax.broadcasted_iota(jnp.int32, (BAND, 2 * BAND), 1)
        allowed = (segq_ref[rows, :] == segk_ref[:, columns]) & (column_place <= row_place)
        bias_ref[block] = jnp.where(allowed, 0.0, masked_score)


def band_rows(halo_ref, rows_ref, block):
    if block == 0:
        return jnp.concatenate([halo_ref[...], rows_ref[0:BAND, :]], axis=0)
    return rows_ref[(block - 1) * BAND : (block + 1) * BAND, :]


def attention_forward_kernel(
    q_ref, k_ref, v_ref, kh_ref, vh_ref, segq_ref, segk_ref, out_ref, total_ref, bias_ref
):
    pair = pl.program_id(0)

    @pl.when(pair == 0)
    def _():
        fill_band_bias(segq_ref, segk_ref, bias_ref)
        total_ref[...] = jnp.zeros_like(total_ref)

    lane = lax.broadcasted_iota(jnp.int32, (BAND, LANES), 1)
    for block in range(bias_ref.shape[0]):
        rows = slice(block * BAND, (block + 1) * BAND)
        query = q_ref[rows, :]
        keys = band_rows(kh_ref, k_ref, block)
        values = band_rows(vh_ref, v_ref, block)
        parts = []
        kept = total_ref[rows, :]
        for head in range(2):
            mine = (lane // HEAD_DIM) == head
            scores = dot_nt(jnp.where(mine, query, 0), keys) * HEAD_DIM ** (-0.5) + bias_ref[block]
            highest = jnp.max(scores, axis=-1, keepdims=True)
            raised = jnp.exp(scores - highest)
            summed = jnp.sum(raised, axis=-1, keepdims=True)
            weighted = jnp.dot(
                raised.astype(jnp.bfloat16), values, preferred_element_type=jnp.float32
            )
            parts.append(weighted / summed)
            kept = jnp.where(lane == 2 * pair + head, highest + jnp.log(summed), kept)
        total_ref[rows, :] = kept
        out_ref[rows, :] = jnp.where(lane < HEAD_DIM, parts[0], parts[1]).astype(out_ref.dtype)


def attention_backward_kernel(
    q_ref,
    k_ref,
    v_ref,
    kh_ref,
    vh_ref,
    segq_ref,
    segk_ref,
    grad_ref,
    total_ref,
    dq_ref,
    dk_ref,
    dv_ref,
    dkh_ref,
    dvh_ref,
    bias_ref,
):
    pair = pl.program_id(0)

    @pl.when(pair == 0)
    def _():
        fill_band_bias(segq_ref, segk_ref, bias_ref)

    lane = lax.broadcasted_iota(jnp.int32, (BAND, LANES), 1)
    scaling = HEAD_DIM ** (-0.5)
    blocks = bias_ref.shape[0]
    key_parts = [None] * (blocks + 1)
    value_parts = [None] * (blocks + 1)
    for block in range(blocks):
        rows = slice(block * BAND, (block + 1) * BAND)
        query = q_ref[rows, :]
        grad = grad_ref[rows, :]
        keys = band_rows(kh_ref, k_ref, block)
        values = band_rows(vh_ref, v_ref, block)
        grad_query = []
        grad_keys = 0.0
        grad_values = 0.0
        for head in range(2):
            mine = (lane // HEAD_DIM) == head
            query_head = jnp.where(mine, query, 0)
            grad_head = jnp.where(mine, grad, 0)
            scores = dot_nt(query_head, keys) * scaling + bias_ref[block]
            total = jnp.sum(
                jnp.where(lane == 2 * pair + head, total_ref[rows, :], 0.0), axis=-1, keepdims=True
            )
            exact = jnp.exp(scores - total)
            low = exact.astype(jnp.bfloat16)
            grad_probs = dot_nt(grad_head, values)
            row_terms = jnp.sum(exact * grad_probs, axis=-1, keepdims=True)
            grad_scores = (exact * (grad_probs - row_terms)).astype(jnp.bfloat16)
            grad_query.append(jnp.dot(grad_scores, keys, preferred_element_type=jnp.float32))
            grad_keys = grad_keys + dot_tn(grad_scores, query_head)
            grad_values = grad_values + dot_tn(low, grad_head)
        dq_ref[rows, :] = (jnp.where(lane < HEAD_DIM, grad_query[0], grad_query[1]) * scaling).astype(
            dq_ref.dtype
        )
        grad_keys = grad_keys * scaling
        for part in range(2):
            cut = slice(part * BAND, (part + 1) * BAND)
            before_k, before_v = key_parts[block + part], value_parts[block + part]
            key_parts[block + part] = (
                grad_keys[cut] if before_k is None else before_k + grad_keys[cut]
            )
            value_parts[block + part] = (
                grad_values[cut] if before_v is None else before_v + grad_values[cut]
            )
    dkh_ref[...] = key_parts[0].astype(dkh_ref.dtype)
    dvh_ref[...] = value_parts[0].astype(dvh_ref.dtype)
    for block in range(blocks):
        rows = slice(block * BAND, (block + 1) * BAND)
        dk_ref[rows, :] = key_parts[block + 1]
        dv_ref[rows, :] = value_parts[block + 1]


def attention_specs(rows, pairs):
    whole = lambda pair: (0, 0)
    return [
        pl.BlockSpec((rows, LANES), lambda pair: (0, pair)),
        pl.BlockSpec((rows, LANES), lambda pair: (0, pairs + pair)),
        pl.BlockSpec((rows, LANES), lambda pair: (0, 2 * pairs + pair)),
        pl.BlockSpec((BAND, LANES), lambda pair: (0, pair)),
        pl.BlockSpec((BAND, LANES), lambda pair: (0, pairs + pair)),
        pl.BlockSpec((rows, 1), whole),
        pl.BlockSpec((1, rows + BAND), whole),
    ]


def attention_forward(projected, halo, segq, segk):
    rows, wide = projected.shape
    width = wide // 3
    pairs = width // LANES
    return pl.pallas_call(
        attention_forward_kernel,
        grid=(pairs,),
        in_specs=attention_specs(rows, pairs),
        out_specs=[
            pl.BlockSpec((rows, LANES), lambda pair: (0, pair)),
            pl.BlockSpec((rows, LANES), lambda pair: (0, 0)),
        ],
        out_shape=[
            jax.ShapeDtypeStruct((rows, width), jnp.bfloat16),
            jax.ShapeDtypeStruct((rows, LANES), jnp.float32),
        ],
        scratch_shapes=[pltpu.VMEM((rows // BAND, BAND, 2 * BAND), jnp.float32)],
        compiler_params=pltpu.CompilerParams(vmem_limit_bytes=VMEM_ASKED),
        cost_estimate=pl.CostEstimate(
            flops=8 * rows * BAND * width, bytes_accessed=10 * rows * width, transcendentals=rows * width * 8
        ),
        name="attention_forward",
    )(projected, projected, projected, halo, halo, segq, segk)


def attention_backward(projected, halo, segq, segk, grad, totals):
    rows, wide = projected.shape
    width = wide // 3
    pairs = width // LANES
    by_pair = lambda pair: (0, pair)
    return pl.pallas_call(
        attention_backward_kernel,
        grid=(pairs,),
        in_specs=attention_specs(rows, pairs)
        + [pl.BlockSpec((rows, LANES), by_pair), pl.BlockSpec((rows, LANES), lambda pair: (0, 0))],
        out_specs=[
            pl.BlockSpec((rows, LANES), by_pair),
            pl.BlockSpec((rows, LANES), by_pair),
            pl.BlockSpec((rows, LANES), by_pair),
            pl.BlockSpec((BAND, LANES), by_pair),
            pl.BlockSpec((BAND, LANES), by_pair),
        ],
        out_shape=[
            jax.ShapeDtypeStruct((rows, width), jnp.bfloat16),
            jax.ShapeDtypeStruct((rows, width), jnp.float32),
            jax.ShapeDtypeStruct((rows, width), jnp.float32),
            jax.ShapeDtypeStruct((BAND, width), jnp.bfloat16),
            jax.ShapeDtypeStruct((BAND, width), jnp.bfloat16),
        ],
        scratch_shapes=[pltpu.VMEM((rows // BAND, BAND, 2 * BAND), jnp.float32)],
        compiler_params=pltpu.CompilerParams(vmem_limit_bytes=VMEM_ASKED),
        cost_estimate=pl.CostEstimate(
            flops=20 * rows * BAND * width, bytes_accessed=20 * rows * width, transcendentals=rows * width * 8
        ),
        name="attention_backward",
    )(projected, projected, projected, halo, halo, segq, segk, grad, totals)


def swap_dp(array, bit):
    count = lax.axis_size("dp")
    return lax.ppermute(array, "dp", [(i, i ^ bit) for i in range(count)])


def swap_y(array):
    return lax.ppermute(array, "tensor", [(0, 1), (1, 0)])


def swap_windows(array):
    pairs = []
    for group in range(lax.axis_size("dp") // 2):
        for core in range(2):
            for y in range(2):
                pairs.append(((2 * group + core) * 2 + y, (2 * group + y) * 2 + core))
    return lax.ppermute(array, ("dp", "tensor"), pairs)


def half_of(array, bit):
    rows = array.shape[0] // 2
    return lax.dynamic_slice_in_dim(array, bit * rows, rows, axis=0)


def join_halves(bit, mine, other):
    return jnp.where(
        bit == 0, jnp.concatenate([mine, other], axis=0), jnp.concatenate([other, mine], axis=0)
    )


def other_half(array, hops):
    if not hops:
        return swap_y(array)
    bit, place = hops[-1]
    mine = other_half(half_of(array, place), hops[:-1])
    return join_halves(place, mine, swap_dp(mine, bit))


def add_low(left, right):
    return (left.astype(jnp.float32) + right.astype(jnp.float32)).astype(jnp.bfloat16)


def reduce_grad(own, other, core):
    own_kept = add_low(half_of(own, core), swap_dp(half_of(own, 1 - core), CORE_BIT))
    other_kept = add_low(half_of(other, core), swap_dp(half_of(other, 1 - core), CORE_BIT))
    mine = add_low(own_kept, swap_y(other_kept))
    count = lax.axis_size("dp")
    groups = [[i for i in range(count) if i % 2 == member] for member in range(2)]
    summed = lax.psum(mine, "dp", axis_index_groups=groups)
    return join_halves(core, summed, swap_dp(summed, CORE_BIT)).astype(jnp.float32)


def dot_low(left, right):
    return jnp.dot(left, right, preferred_element_type=jnp.float32)


def local_split(
    tokens_in,
    segments,
    w_qkv,
    qv_bias,
    w_out,
    w_up,
    up_bias,
    w_down,
    out_bias,
    ln_gain,
    ln_bias,
    cotangent,
):
    layers, width = w_qkv.shape[0], w_qkv.shape[1]
    rows = tokens_in.shape[0]
    place = lax.axis_index("dp")
    y = lax.axis_index("tensor")
    core, x = place % 2, (place // 2) % 2
    hops = [(X_BIT, x), (CORE_BIT, core)]

    residual = swap_windows(tokens_in).astype(jnp.float32)
    grad_residual = swap_windows(cotangent)
    window_segments = jnp.where(core == y, segments, swap_dp(segments, CORE_BIT))
    own_segments = lax.dynamic_slice_in_dim(window_segments, core * rows, rows, axis=1)
    halo_segments = jnp.where(core == 1, window_segments[:, rows - BAND : rows], -1)
    segq = own_segments.reshape(rows, 1)
    segk = jnp.concatenate([halo_segments, own_segments], axis=1)

    def natural(own, other):
        return join_halves(y, own, other)

    qkv_rows = [w_qkv[l].reshape(width, -1) for l in range(layers)]
    weights = []
    for l in range(layers):
        own = (qkv_rows[l], w_out[l], w_up[l], w_down[l])
        other = tuple(other_half(member, hops) for member in own)
        bias_own = (qv_bias[l].reshape(-1), up_bias[l])
        bias_other = tuple(swap_y(member) for member in bias_own)
        weights.append(tuple(zip(own + bias_own, other + bias_other)))

    kept = []
    count = lax.axis_size("dp")
    to_second = [(2 * i, 2 * i + 1) for i in range(count // 2)]
    to_first = [(2 * i + 1, 2 * i) for i in range(count // 2)]
    for l in range(layers):
        qkv, out_w, up, down, qv, upb = weights[l]
        normed, _, _ = layer_norm(residual, ln_gain[l, 0], ln_bias[l, 0])
        normed = normed.astype(jnp.bfloat16)
        saved_attention = []
        branch = 0.0
        for half in range(2):
            third = qkv[half].shape[1] // 3
            bias = jnp.concatenate(
                [qv[half][:third], jnp.zeros((third,), jnp.float32), qv[half][third:]]
            )
            projected = (dot_low(normed, qkv[half]) + bias).astype(jnp.bfloat16)
            halo = lax.ppermute(projected[rows - BAND :, third:], "dp", to_second)
            attended, totals = attention_forward(projected, halo, segq, segk)
            branch = branch + dot_low(attended, out_w[half])
            saved_attention.append((projected, halo, attended, totals))
        middle = residual + branch + out_bias[l, 0]
        normed_two, _, _ = layer_norm(middle, ln_gain[l, 1], ln_bias[l, 1])
        normed_two = normed_two.astype(jnp.bfloat16)
        saved_ffn = []
        branch = 0.0
        for half in range(2):
            before = dot_low(normed_two, up[half]) + upb[half]
            activated = gelu_tanh(before).astype(jnp.bfloat16)
            slope = gelu_slope(before).astype(jnp.bfloat16)
            branch = branch + dot_low(activated, down[half])
            saved_ffn.append((activated, slope))
        kept.append((residual, normed, saved_attention, middle, normed_two, saved_ffn))
        residual = middle + branch + out_bias[l, 1]
    out_act = swap_windows(residual.astype(jnp.bfloat16))

    grad_residual = grad_residual.astype(jnp.float32)
    grads = [None] * layers
    vectors = [None] * layers
    for l in reversed(range(layers)):
        qkv, out_w, up, down, qv, upb = weights[l]
        residual, normed, saved_attention, middle, normed_two, saved_ffn = kept[l]
        grad_branch = grad_residual.astype(jnp.bfloat16)
        grad_down, grad_up, grad_up_bias = [], [], []
        incoming = 0.0
        for half in range(2):
            activated, slope = saved_ffn[half]
            grad_before = (dot_nt(grad_branch, down[half]) * slope.astype(jnp.float32)).astype(
                jnp.bfloat16
            )
            grad_down.append(dot_tn(activated, grad_branch).astype(jnp.bfloat16))
            grad_up.append(dot_tn(normed_two, grad_before).astype(jnp.bfloat16))
            grad_up_bias.append(jnp.sum(grad_before, axis=0, dtype=jnp.float32))
            incoming = incoming + dot_nt(grad_before, up[half])
        _, unit, inverse = layer_norm(middle, ln_gain[l, 1], ln_bias[l, 1])
        through, gain_two, shift_two = norm_backward(incoming, unit, inverse, ln_gain[l, 1])
        grad_middle = grad_residual + through
        grad_attn = grad_middle.astype(jnp.bfloat16)
        grad_out, grad_qkv, grad_qv = [], [], []
        incoming = 0.0
        for half in range(2):
            projected, halo, attended, totals = saved_attention[half]
            grad_out.append(dot_tn(attended, grad_attn).astype(jnp.bfloat16))
            grad_attended = dot_nt(grad_attn, out_w[half]).astype(jnp.bfloat16)
            dq, dk, dv, dkh, dvh = attention_backward(
                projected, halo, segq, segk, grad_attended, totals
            )
            sent = lax.ppermute(jnp.concatenate([dkh, dvh], axis=1), "dp", to_first)
            whole = jnp.pad(sent, ((rows - BAND, 0), (0, 0))).astype(jnp.float32)
            third = dk.shape[1]
            grad_projected = jnp.concatenate(
                [
                    dq,
                    (dk + whole[:, :third]).astype(jnp.bfloat16),
                    (dv + whole[:, third:]).astype(jnp.bfloat16),
                ],
                axis=1,
            )
            grad_qkv.append(dot_tn(normed, grad_projected).astype(jnp.bfloat16))
            sums = jnp.sum(grad_projected, axis=0, dtype=jnp.float32)
            grad_qv.append(jnp.stack([sums[:third], sums[2 * third :]]))
            incoming = incoming + dot_nt(grad_projected, qkv[half])
        _, unit, inverse = layer_norm(residual, ln_gain[l, 0], ln_bias[l, 0])
        through, gain_one, shift_one = norm_backward(incoming, unit, inverse, ln_gain[l, 0])
        grads[l] = tuple(
            reduce_grad(pair[0], pair[1], core) for pair in (grad_qkv, grad_out, grad_up, grad_down)
        )
        vectors[l] = jnp.concatenate(
            [
                natural(grad_qv[0].T, grad_qv[1].T).T.reshape(-1),
                natural(grad_up_bias[0], grad_up_bias[1]),
                jnp.sum(grad_attn, axis=0, dtype=jnp.float32),
                jnp.sum(grad_branch, axis=0, dtype=jnp.float32),
                gain_one,
                gain_two,
                shift_one,
                shift_two,
            ]
        )
        grad_residual = grad_middle + through
    grad_in = swap_windows(grad_residual.astype(jnp.bfloat16))
    summed = lax.psum(jnp.stack(vectors), ("dp", "tensor"))
    hidden = 2 * up_bias.shape[1]
    ends = [2 * width, 2 * width + hidden, 4 * width + hidden, 6 * width + hidden]
    qv_sum = summed[:, : ends[0]].reshape(layers, 2, width)
    grad_qv_bias = lax.dynamic_slice_in_dim(qv_sum, y * (width // 2), width // 2, axis=2)
    grad_up_bias = lax.dynamic_slice_in_dim(
        summed[:, ends[0] : ends[1]], y * (hidden // 2), hidden // 2, axis=1
    )
    stacked = [jnp.stack([grads[l][member] for l in range(layers)]) for member in range(4)]
    return (
        out_act,
        grad_in,
        stacked[0].reshape(w_qkv.shape),
        grad_qv_bias,
        stacked[1],
        stacked[2],
        grad_up_bias,
        stacked[3],
        summed[:, ends[1] : ends[2]].reshape(layers, 2, width),
        summed[:, ends[2] : ends[3]].reshape(layers, 2, width),
        summed[:, ends[3] :].reshape(layers, 2, width),
    )


def solution(mesh):
    sizes = (mesh.shape["dp"], mesh.shape["tensor"])
    local = local_split if sizes == (16, 2) else local_general
    return jax.shard_map(
        local,
        mesh=mesh,
        in_specs=(
            P(("dp", "tensor"), None),
            P("dp", None),
            P(None, None, None, "tensor"),
            P(None, None, "tensor"),
            P(None, "tensor", None),
            P(None, None, "tensor"),
            P(None, "tensor"),
            P(None, "tensor", None),
            P(),
            P(),
            P(),
            P(("dp", "tensor"), None),
        ),
        out_specs=(
            P(("dp", "tensor"), None),
            P(("dp", "tensor"), None),
            P(None, None, None, "tensor"),
            P(None, None, "tensor"),
            P(None, "tensor", None),
            P(None, None, "tensor"),
            P(None, "tensor"),
            P(None, "tensor", None),
            P(),
            P(),
            P(),
        ),
        check_vma=False,
    )
```

```python
import functools

import jax
import jax.numpy as jnp
from jax import lax
from jax.experimental import pallas as pl
from jax.experimental.pallas import tpu as pltpu
from jax.sharding import PartitionSpec as P

HEAD_DIM = 64


epsilon = 1e-05
gelu_coeff = 0.7978845608028654
cubic_coeff = 0.044715
masked_score = -1e30


def as_sent(shard):

    def short(part):
        return part.astype(jnp.bfloat16) if part.dtype == jnp.float32 else part

    return jax.tree.map(short, shard)


def layer_norm(values, gain, shift):
    average = jnp.mean(values, axis=-1, keepdims=True)
    centred = values - average
    inverse = lax.rsqrt(jnp.mean(centred * centred, axis=-1, keepdims=True) + epsilon)
    unit_rows = centred * inverse
    return (unit_rows * gain + shift, unit_rows, inverse)


def norm_backward(incoming, unit_rows, inverse, gain):
    scaled = incoming * gain
    first_mean = jnp.mean(scaled, axis=-1, keepdims=True)
    second_mean = jnp.mean(scaled * unit_rows, axis=-1, keepdims=True)
    through = inverse * (scaled - first_mean - unit_rows * second_mean)
    return (through, jnp.sum(incoming * unit_rows, axis=0), jnp.sum(incoming, axis=0))


def gelu_tanh(before):
    tanh_input = gelu_coeff * (before + cubic_coeff * before * before * before)
    return 0.5 * before * (1.0 + jnp.tanh(tanh_input))


def gelu_slope(before):
    tanh_input = gelu_coeff * (before + cubic_coeff * before * before * before)
    tangent = jnp.tanh(tanh_input)
    return 0.5 * (1.0 + tangent) + 0.5 * before * (1.0 - tangent * tangent) * gelu_coeff * (
        1.0 + 3.0 * cubic_coeff * before * before
    )


def masked_scores(query_block, key_seq, segment_row, offset, block_rows):
    window = key_seq.shape[0]
    scores = jnp.einsum(
        "qhe,khe->hqk", query_block, key_seq, preferred_element_type=jnp.float32
    ) * HEAD_DIM ** (-0.5)
    query_place = offset + lax.iota(jnp.int32, block_rows)
    key_place = lax.iota(jnp.int32, window)
    query_segment = segment_row[offset : offset + block_rows]
    allowed = (query_place[:, None] >= key_place[None, :]) & (
        query_segment[:, None] == segment_row[None, :]
    )
    return jnp.where(allowed[None], scores, masked_score)


def split_heads(flat_rows, seq_count):
    return flat_rows.reshape(
        seq_count, flat_rows.shape[0] // seq_count, flat_rows.shape[1] // HEAD_DIM, HEAD_DIM
    )


def attend_forward(query_rows, key_rows, value_rows, segments):
    seq_count, window = segments.shape
    block_rows = min(512, window)

    def one_sequence(member):
        query_seq, key_seq, value_seq, segment_row = member
        outputs = []
        totals = []
        for block_index in range(window // block_rows):
            offset = block_index * block_rows
            scores = masked_scores(
                query_seq[offset : offset + block_rows], key_seq, segment_row, offset, block_rows
            )
            highest = jnp.max(scores, axis=-1, keepdims=True)
            raised = jnp.exp(scores - highest)
            summed = jnp.sum(raised, axis=-1, keepdims=True)
            softmax_low = (raised / summed).astype(jnp.bfloat16)
            block_out = jnp.einsum(
                "hqk,khe->qhe", softmax_low, value_seq, preferred_element_type=jnp.float32
            )
            outputs.append(block_out.astype(jnp.bfloat16))
            totals.append(highest[..., 0] + jnp.log(summed[..., 0]))
        return (jnp.concatenate(outputs, axis=0), jnp.stack(totals, axis=0))

    attended, log_totals = lax.map(
        one_sequence,
        (
            split_heads(query_rows, seq_count),
            split_heads(key_rows, seq_count),
            split_heads(value_rows, seq_count),
            segments,
        ),
    )
    return (attended.reshape(query_rows.shape), log_totals)


def attend_backward(query_rows, key_rows, value_rows, segments, log_totals, grad_attended):
    seq_count, window = segments.shape
    block_rows = min(512, window)
    scaling = HEAD_DIM ** (-0.5)

    def one_sequence(member):
        query_seq, key_seq, value_seq, segment_row, totals_seq, grad_seq = member
        query_parts = []
        grad_keys = jnp.zeros(key_seq.shape, jnp.float32)
        grad_values = jnp.zeros(value_seq.shape, jnp.float32)
        for block_index in range(window // block_rows):
            offset = block_index * block_rows
            query_block = query_seq[offset : offset + block_rows]
            grad_block = grad_seq[offset : offset + block_rows]
            scores = masked_scores(query_block, key_seq, segment_row, offset, block_rows)
            softmax_exact = jnp.exp(scores - totals_seq[block_index][..., None])
            softmax_low = softmax_exact.astype(jnp.bfloat16)
            grad_softmax = jnp.einsum(
                "qhe,khe->hqk", grad_block, value_seq, preferred_element_type=jnp.float32
            )
            row_terms = jnp.sum(softmax_exact * grad_softmax, axis=-1, keepdims=True)
            grad_scores = (softmax_exact * (grad_softmax - row_terms)).astype(jnp.bfloat16)
            query_parts.append(
                jnp.einsum("hqk,khe->qhe", grad_scores, key_seq, preferred_element_type=jnp.float32)
                * scaling
            )
            grad_keys = (
                grad_keys
                + jnp.einsum(
                    "hqk,qhe->khe", grad_scores, query_block, preferred_element_type=jnp.float32
                )
                * scaling
            )
            grad_values = grad_values + jnp.einsum(
                "hqk,qhe->khe", softmax_low, grad_block, preferred_element_type=jnp.float32
            )
        grad_query = jnp.concatenate(query_parts, axis=0)
        return (
            grad_query.astype(jnp.bfloat16),
            grad_keys.astype(jnp.bfloat16),
            grad_values.astype(jnp.bfloat16),
        )

    grad_query, grad_keys, grad_values = lax.map(
        one_sequence,
        (
            split_heads(query_rows, seq_count),
            split_heads(key_rows, seq_count),
            split_heads(value_rows, seq_count),
            segments,
            log_totals,
            split_heads(grad_attended, seq_count),
        ),
    )
    return (
        grad_query.reshape(query_rows.shape),
        grad_keys.reshape(query_rows.shape),
        grad_values.reshape(query_rows.shape),
    )


def layer_forward(residual, segments, weights):
    w_qkv, qv_bias, w_out, w_up, up_bias, w_down, out_bias, gains, shifts = weights
    row_count = residual.shape[0]
    normed, unit_one, inverse_one = layer_norm(residual, gains[0], shifts[0])
    normed_all = lax.all_gather(normed.astype(jnp.bfloat16), "tensor", axis=0, tiled=True)
    projected = jnp.einsum("td,dsc->tsc", normed_all, w_qkv, preferred_element_type=jnp.float32)
    query_rows = (projected[:, 0] + qv_bias[0]).astype(jnp.bfloat16)
    key_rows = projected[:, 1].astype(jnp.bfloat16)
    value_rows = (projected[:, 2] + qv_bias[1]).astype(jnp.bfloat16)
    attended, log_totals = attend_forward(query_rows, key_rows, value_rows, segments)
    middle = (
        residual
        + lax.psum_scatter(
            jnp.dot(
                lax.slice_in_dim(attended, 0, row_count * lax.axis_size("tensor"), axis=0),
                w_out,
                preferred_element_type=jnp.float32,
            ).astype(jnp.bfloat16),
            "tensor",
            scatter_dimension=0,
            tiled=True,
        ).astype(jnp.float32)
        + out_bias[0]
    )
    normed_two, unit_two, inverse_two = layer_norm(middle, gains[1], shifts[1])
    normed_low = normed_two.astype(jnp.bfloat16)
    ffn_rows = lax.all_gather(normed_low, "tensor", axis=0, tiled=True)
    before = jnp.dot(ffn_rows, w_up, preferred_element_type=jnp.float32) + up_bias
    activated = gelu_tanh(before).astype(jnp.bfloat16)
    ffn_branch = lax.psum_scatter(
        jnp.dot(
            lax.slice_in_dim(activated, 0, row_count * lax.axis_size("tensor"), axis=0),
            w_down,
            preferred_element_type=jnp.float32,
        ).astype(jnp.bfloat16),
        "tensor",
        scatter_dimension=0,
        tiled=True,
    ).astype(jnp.float32)
    kept_ffn = (w_up, w_down)
    result = middle + ffn_branch + out_bias[1]
    kept_state = (
        unit_one,
        inverse_one,
        normed_all,
        query_rows,
        key_rows,
        value_rows,
        attended,
        log_totals,
        unit_two,
        inverse_two,
        ffn_rows,
        before,
        activated,
        kept_ffn,
    )
    return (result, kept_state)


def layer_backward(grad_residual, segments, weights, kept_state):
    w_qkv, qv_bias, w_out, w_up, up_bias, w_down, out_bias, gains, shifts = weights
    (
        unit_one,
        inverse_one,
        normed_all,
        query_rows,
        key_rows,
        value_rows,
        attended,
        log_totals,
        unit_two,
        inverse_two,
        ffn_rows,
        before,
        activated,
        kept_ffn,
    ) = kept_state
    up_used, down_used = kept_ffn
    row_count = grad_residual.shape[0]
    grad_branch = grad_residual.astype(jnp.bfloat16)
    bias_down = jnp.sum(grad_branch, axis=0, dtype=jnp.float32)
    grad_rows = lax.all_gather(grad_branch, "tensor", axis=0, tiled=True)
    grad_hidden = jnp.einsum("td,fd->tf", grad_rows, down_used, preferred_element_type=jnp.float32)
    grad_before = (grad_hidden * gelu_slope(before)).astype(jnp.bfloat16)
    grad_down = jnp.einsum("tf,td->fd", activated, grad_rows, preferred_element_type=jnp.float32)
    grad_up = jnp.einsum("td,tf->df", ffn_rows, grad_before, preferred_element_type=jnp.float32)
    grad_up_bias = jnp.sum(grad_before, axis=0, dtype=jnp.float32)
    piece_rows = lax.slice_in_dim(grad_before, 0, row_count * lax.axis_size("tensor"), axis=0)
    grad_normed_two = lax.psum_scatter(
        jnp.einsum("tf,df->td", piece_rows, w_up, preferred_element_type=jnp.float32).astype(
            jnp.bfloat16
        ),
        "tensor",
        scatter_dimension=0,
        tiled=True,
    ).astype(jnp.float32)
    through_two, gain_two, shift_two = norm_backward(
        grad_normed_two, unit_two, inverse_two, gains[1]
    )
    grad_middle = grad_residual + through_two
    grad_attn_branch = grad_middle.astype(jnp.bfloat16)
    bias_attn = jnp.sum(grad_attn_branch, axis=0, dtype=jnp.float32)
    grad_attn_all = lax.all_gather(grad_attn_branch, "tensor", axis=0, tiled=True)
    grad_out_w = jnp.einsum(
        "tc,td->cd", attended, grad_attn_all, preferred_element_type=jnp.float32
    )
    grad_attended = jnp.einsum(
        "td,cd->tc", grad_attn_all, w_out, preferred_element_type=jnp.float32
    ).astype(jnp.bfloat16)
    grad_query, grad_keys, grad_values = attend_backward(
        query_rows, key_rows, value_rows, segments, log_totals, grad_attended
    )
    grad_projected = jnp.stack((grad_query, grad_keys, grad_values), axis=1)
    grad_qkv = jnp.einsum(
        "td,tsc->dsc", normed_all, grad_projected, preferred_element_type=jnp.float32
    )
    grad_qv_bias = jnp.stack(
        (
            jnp.sum(grad_query, axis=0, dtype=jnp.float32),
            jnp.sum(grad_values, axis=0, dtype=jnp.float32),
        )
    )
    piece_rows = lax.slice_in_dim(grad_projected, 0, row_count * lax.axis_size("tensor"), axis=0)
    grad_normed = lax.psum_scatter(
        jnp.einsum("tsc,dsc->td", piece_rows, w_qkv, preferred_element_type=jnp.float32).astype(
            jnp.bfloat16
        ),
        "tensor",
        scatter_dimension=0,
        tiled=True,
    ).astype(jnp.float32)
    through_one, gain_one, shift_one = norm_backward(grad_normed, unit_one, inverse_one, gains[0])
    grad_input = grad_middle + through_one
    spread = (grad_qkv, grad_qv_bias, grad_out_w, grad_up, grad_up_bias, grad_down)
    shared = (
        jnp.stack((bias_attn, bias_down)),
        jnp.stack((gain_one, gain_two)),
        jnp.stack((shift_one, shift_two)),
    )
    return (grad_input, spread, shared)


def local_general(
    tokens_in,
    segments,
    w_qkv,
    qv_bias,
    w_out,
    w_up,
    up_bias,
    w_down,
    out_bias,
    ln_gain,
    ln_bias,
    cotangent,
):
    layers_total = w_qkv.shape[0]
    all_params = (w_qkv, qv_bias, w_out, w_up, up_bias, w_down, out_bias, ln_gain, ln_bias)
    residual = tokens_in.astype(jnp.float32)
    kept_layers = []
    for layer_index in range(layers_total):
        weights = tuple((member_array[layer_index] for member_array in all_params))
        residual, kept_state = layer_forward(residual, segments, weights)
        kept_layers.append(kept_state)
    out_act = residual.astype(jnp.bfloat16)
    grad_residual = cotangent.astype(jnp.float32)
    spread_layers = []
    shared_layers = []
    for layer_index in reversed(range(layers_total)):
        weights = tuple((member_array[layer_index] for member_array in all_params))
        grad_residual, spread, shared = layer_backward(
            grad_residual, segments, weights, kept_layers[layer_index]
        )
        spread_layers.insert(0, spread)
        shared_layers.insert(0, shared)
    spread_stack = tuple(
        (
            jnp.stack([spread_layers[layer_index][position] for layer_index in range(layers_total)])
            for position in range(6)
        )
    )
    spread_stack = jax.tree.map(
        lambda part: part.astype(jnp.float32), lax.psum(as_sent(spread_stack), "dp")
    )
    shared_stack = tuple(
        (
            jnp.stack([shared_layers[layer_index][position] for layer_index in range(layers_total)])
            for position in range(3)
        )
    )
    shared_stack = lax.psum(shared_stack, ("dp", "tensor"))
    grad_in = grad_residual.astype(jnp.bfloat16)
    return (out_act, grad_in) + tuple(spread_stack) + tuple(shared_stack)


CORE_BIT = 1
X_BIT = 2
Z_BIT = 4
BAND = 256
LANES = 128
VMEM_ASKED = 56 * 2**20


def dot_nt(left, right):
    return lax.dot_general(left, right, (((1,), (1,)), ((), ())), preferred_element_type=jnp.float32)


def dot_tn(left, right):
    return lax.dot_general(left, right, (((0,), (0,)), ((), ())), preferred_element_type=jnp.float32)


def fill_band_bias(segq_ref, segk_ref, bias_ref):
    blocks = bias_ref.shape[0]
    for block in range(blocks):
        rows = slice(block * BAND, (block + 1) * BAND)
        columns = slice(block * BAND, (block + 2) * BAND)
        row_place = lax.broadcasted_iota(jnp.int32, (BAND, 2 * BAND), 0) + BAND
        column_place = lax.broadcasted_iota(jnp.int32, (BAND, 2 * BAND), 1)
        allowed = (segq_ref[rows, :] == segk_ref[:, columns]) & (column_place <= row_place)
        bias_ref[block] = jnp.where(allowed, 0.0, masked_score)


def band_rows(halo_ref, rows_ref, block):
    if block == 0:
        return jnp.concatenate([halo_ref[...], rows_ref[0:BAND, :]], axis=0)
    return rows_ref[(block - 1) * BAND : (block + 1) * BAND, :]


def attention_forward_kernel(
    q_ref, k_ref, v_ref, kh_ref, vh_ref, segq_ref, segk_ref, out_ref, total_ref, bias_ref
):
    pair = pl.program_id(0)

    @pl.when(pair == 0)
    def _():
        fill_band_bias(segq_ref, segk_ref, bias_ref)
        total_ref[...] = jnp.zeros_like(total_ref)

    lane = lax.broadcasted_iota(jnp.int32, (BAND, LANES), 1)
    for block in range(bias_ref.shape[0]):
        rows = slice(block * BAND, (block + 1) * BAND)
        query = q_ref[rows, :]
        keys = band_rows(kh_ref, k_ref, block)
        values = band_rows(vh_ref, v_ref, block)
        parts = []
        kept = total_ref[rows, :]
        for head in range(2):
            mine = (lane // HEAD_DIM) == head
            scores = dot_nt(jnp.where(mine, query, 0), keys) * HEAD_DIM ** (-0.5) + bias_ref[block]
            highest = jnp.max(scores, axis=-1, keepdims=True)
            raised = jnp.exp(scores - highest)
            summed = jnp.sum(raised, axis=-1, keepdims=True)
            weighted = jnp.dot(
                raised.astype(jnp.bfloat16), values, preferred_element_type=jnp.float32
            )
            parts.append(weighted / summed)
            kept = jnp.where(lane == 2 * pair + head, highest + jnp.log(summed), kept)
        total_ref[rows, :] = kept
        out_ref[rows, :] = jnp.where(lane < HEAD_DIM, parts[0], parts[1]).astype(out_ref.dtype)


def attention_backward_kernel(
    q_ref,
    k_ref,
    v_ref,
    kh_ref,
    vh_ref,
    segq_ref,
    segk_ref,
    grad_ref,
    total_ref,
    dq_ref,
    dk_ref,
    dv_ref,
    dkh_ref,
    dvh_ref,
    bias_ref,
):
    pair = pl.program_id(0)

    @pl.when(pair == 0)
    def _():
        fill_band_bias(segq_ref, segk_ref, bias_ref)

    lane = lax.broadcasted_iota(jnp.int32, (BAND, LANES), 1)
    scaling = HEAD_DIM ** (-0.5)
    blocks = bias_ref.shape[0]
    key_parts = [None] * (blocks + 1)
    value_parts = [None] * (blocks + 1)
    for block in range(blocks):
        rows = slice(block * BAND, (block + 1) * BAND)
        query = q_ref[rows, :]
        grad = grad_ref[rows, :]
        keys = band_rows(kh_ref, k_ref, block)
        values = band_rows(vh_ref, v_ref, block)
        grad_query = []
        grad_keys = 0.0
        grad_values = 0.0
        for head in range(2):
            mine = (lane // HEAD_DIM) == head
            query_head = jnp.where(mine, query, 0)
            grad_head = jnp.where(mine, grad, 0)
            scores = dot_nt(query_head, keys) * scaling + bias_ref[block]
            total = jnp.sum(
                jnp.where(lane == 2 * pair + head, total_ref[rows, :], 0.0), axis=-1, keepdims=True
            )
            exact = jnp.exp(scores - total)
            low = exact.astype(jnp.bfloat16)
            grad_probs = dot_nt(grad_head, values)
            row_terms = jnp.sum(exact * grad_probs, axis=-1, keepdims=True)
            grad_scores = (exact * (grad_probs - row_terms)).astype(jnp.bfloat16)
            grad_query.append(jnp.dot(grad_scores, keys, preferred_element_type=jnp.float32))
            grad_keys = grad_keys + dot_tn(grad_scores, query_head)
            grad_values = grad_values + dot_tn(low, grad_head)
        dq_ref[rows, :] = (jnp.where(lane < HEAD_DIM, grad_query[0], grad_query[1]) * scaling).astype(
            dq_ref.dtype
        )
        grad_keys = grad_keys * scaling
        for part in range(2):
            cut = slice(part * BAND, (part + 1) * BAND)
            before_k, before_v = key_parts[block + part], value_parts[block + part]
            key_parts[block + part] = (
                grad_keys[cut] if before_k is None else before_k + grad_keys[cut]
            )
            value_parts[block + part] = (
                grad_values[cut] if before_v is None else before_v + grad_values[cut]
            )
    dkh_ref[...] = key_parts[0].astype(dkh_ref.dtype)
    dvh_ref[...] = value_parts[0].astype(dvh_ref.dtype)
    for block in range(blocks):
        rows = slice(block * BAND, (block + 1) * BAND)
        dk_ref[rows, :] = key_parts[block + 1]
        dv_ref[rows, :] = value_parts[block + 1]


def attention_specs(rows, pairs):
    whole = lambda pair: (0, 0)
    return [
        pl.BlockSpec((rows, LANES), lambda pair: (0, pair)),
        pl.BlockSpec((rows, LANES), lambda pair: (0, pairs + pair)),
        pl.BlockSpec((rows, LANES), lambda pair: (0, 2 * pairs + pair)),
        pl.BlockSpec((BAND, LANES), lambda pair: (0, pair)),
        pl.BlockSpec((BAND, LANES), lambda pair: (0, pairs + pair)),
        pl.BlockSpec((rows, 1), whole),
        pl.BlockSpec((1, rows + BAND), whole),
    ]


def attention_forward(projected, halo, segq, segk):
    rows, wide = projected.shape
    width = wide // 3
    pairs = width // LANES
    return pl.pallas_call(
        attention_forward_kernel,
        grid=(pairs,),
        in_specs=attention_specs(rows, pairs),
        out_specs=[
            pl.BlockSpec((rows, LANES), lambda pair: (0, pair)),
            pl.BlockSpec((rows, LANES), lambda pair: (0, 0)),
        ],
        out_shape=[
            jax.ShapeDtypeStruct((rows, width), jnp.bfloat16),
            jax.ShapeDtypeStruct((rows, LANES), jnp.float32),
        ],
        scratch_shapes=[pltpu.VMEM((rows // BAND, BAND, 2 * BAND), jnp.float32)],
        compiler_params=pltpu.CompilerParams(vmem_limit_bytes=VMEM_ASKED),
        cost_estimate=pl.CostEstimate(
            flops=8 * rows * BAND * width, bytes_accessed=10 * rows * width, transcendentals=rows * width * 8
        ),
        name="attention_forward",
    )(projected, projected, projected, halo, halo, segq, segk)


def attention_backward(projected, halo, segq, segk, grad, totals):
    rows, wide = projected.shape
    width = wide // 3
    pairs = width // LANES
    by_pair = lambda pair: (0, pair)
    return pl.pallas_call(
        attention_backward_kernel,
        grid=(pairs,),
        in_specs=attention_specs(rows, pairs)
        + [pl.BlockSpec((rows, LANES), by_pair), pl.BlockSpec((rows, LANES), lambda pair: (0, 0))],
        out_specs=[
            pl.BlockSpec((rows, LANES), by_pair),
            pl.BlockSpec((rows, LANES), by_pair),
            pl.BlockSpec((rows, LANES), by_pair),
            pl.BlockSpec((BAND, LANES), by_pair),
            pl.BlockSpec((BAND, LANES), by_pair),
        ],
        out_shape=[
            jax.ShapeDtypeStruct((rows, width), jnp.bfloat16),
            jax.ShapeDtypeStruct((rows, width), jnp.float32),
            jax.ShapeDtypeStruct((rows, width), jnp.float32),
            jax.ShapeDtypeStruct((BAND, width), jnp.bfloat16),
            jax.ShapeDtypeStruct((BAND, width), jnp.bfloat16),
        ],
        scratch_shapes=[pltpu.VMEM((rows // BAND, BAND, 2 * BAND), jnp.float32)],
        compiler_params=pltpu.CompilerParams(vmem_limit_bytes=VMEM_ASKED),
        cost_estimate=pl.CostEstimate(
            flops=20 * rows * BAND * width, bytes_accessed=20 * rows * width, transcendentals=rows * width * 8
        ),
        name="attention_backward",
    )(projected, projected, projected, halo, halo, segq, segk, grad, totals)


def swap_dp(array, bit):
    count = lax.axis_size("dp")
    return lax.ppermute(array, "dp", [(i, i ^ bit) for i in range(count)])


def swap_y(array):
    return lax.ppermute(array, "tensor", [(0, 1), (1, 0)])


def swap_windows(array):
    pairs = []
    for group in range(lax.axis_size("dp") // 2):
        for core in range(2):
            for y in range(2):
                pairs.append(((2 * group + core) * 2 + y, (2 * group + y) * 2 + core))
    return lax.ppermute(array, ("dp", "tensor"), pairs)


def half_of(array, bit):
    rows = array.shape[0] // 2
    return lax.dynamic_slice_in_dim(array, bit * rows, rows, axis=0)


def join_halves(bit, mine, other):
    return jnp.where(
        bit == 0, jnp.concatenate([mine, other], axis=0), jnp.concatenate([other, mine], axis=0)
    )


def other_half(array, hops):
    if not hops:
        return swap_y(array)
    bit, place = hops[-1]
    mine = other_half(half_of(array, place), hops[:-1])
    return join_halves(place, mine, swap_dp(mine, bit))


SLOTS = 12
STAGED = 3
LAGS = dict(core=1, y=3, x=5, outer=7, inner=9, back=11, gather=13, whole=14, stored=15)
VECTOR_TICKS = (1, 4, 7, 10, 13, 16, 19)
MESH = pl.DeviceIdType.MESH


def added(left, right):
    return (left.astype(jnp.float32) + right.astype(jnp.float32)).astype(jnp.bfloat16)


def reduce_kernel(plan, block, *refs):
    count = len(plan)
    chunks = sum(rows * columns for _, rows, columns in plan)
    operand_refs = refs[: 3 * count]
    vector_ref = refs[3 * count]
    out_refs = refs[3 * count + 1 : 4 * count + 1]
    vector_out = refs[4 * count + 1]
    (
        pair_buf,
        one_buf,
        part_buf,
        core_in,
        own_kept,
        other_kept,
        y_in,
        x_kept,
        x_out,
        x_in,
        z_kept,
        outer_in,
        inner_in,
        result,
        vec_in,
        staged_sem,
        send_sems,
        recv_sems,
        store_sem,
        vec_send,
        vec_recv,
    ) = refs[4 * count + 2 :]
    half, quarter = block // 2, block // 4
    place = lax.axis_index("dp")
    y = lax.axis_index("tensor")
    core = place % 2
    x = (place // 2) % 2
    z = place // 4
    z_low = z % 2
    inner = (z + 1) // 2 % 2
    core_partner = {"dp": place + 1 - 2 * core, "tensor": y}
    x_partner = {"dp": place + 2 - 4 * x, "tensor": y}
    y_partner = {"dp": place, "tensor": 1 - y}
    z_partner = {"dp": place + 4 - 8 * z_low, "tensor": y}
    middle_partner = {"dp": place + 4 * (3 - 2 * z), "tensor": y}

    barrier = pltpu.get_barrier_semaphore()
    for partner in (core_partner, x_partner, y_partner, z_partner):
        pl.semaphore_signal(barrier, inc=1, device_id=partner, device_id_type=MESH)

    @pl.when(inner == 1)
    def _():
        pl.semaphore_signal(barrier, inc=1, device_id=middle_partner, device_id_type=MESH)
        pl.semaphore_wait(barrier, 5)

    @pl.when(inner == 0)
    def _():
        pl.semaphore_wait(barrier, 4)

    starts = []
    total = 0
    for _, rows, columns in plan:
        starts.append(total)
        total += rows * columns

    def for_matrix(chunk, action):
        for member, (kind, rows, columns) in enumerate(plan):

            @pl.when((chunk >= starts[member]) & (chunk < starts[member] + rows * columns))
            def _(member=member, kind=kind, columns=columns):
                local = chunk - starts[member]
                action(member, kind, local // columns, local % columns)

    def cut(ref, column):
        return ref.at[:, pl.ds(pl.multiple_of(column * block, block), block)]

    def staged_copies(chunk, shared, own, other):
        slot = chunk % STAGED
        return (
            pltpu.make_async_copy(own, pair_buf.at[slot, 0], staged_sem.at[slot, 0]),
            pltpu.make_async_copy(other, pair_buf.at[slot, 1], staged_sem.at[slot, 1]),
            pltpu.make_async_copy(shared, one_buf.at[slot], staged_sem.at[slot, 2]),
        )

    def stage_operands(chunk):
        def action(member, kind, i, j):
            shared, own, other = operand_refs[3 * member : 3 * member + 3]
            split, single = (i, j) if kind == "rows" else (j, i)
            for copy in staged_copies(
                chunk, cut(shared, single), cut(own, split), cut(other, split)
            ):
                copy.start()

        for_matrix(chunk, action)

    def wait_operands(chunk):
        slot = chunk % STAGED
        for copy in staged_copies(chunk, one_buf.at[slot], pair_buf.at[slot, 0], pair_buf.at[slot, 1]):
            copy.wait()

    def remote(step, chunk, source, target, partner):
        slot = chunk % SLOTS
        return pltpu.make_async_remote_copy(
            src_ref=source,
            dst_ref=target,
            send_sem=send_sems.at[step, slot],
            recv_sem=recv_sems.at[step, slot],
            device_id=partner,
            device_id_type=MESH,
        )

    def rows_at(index, size):
        return pl.ds(pl.multiple_of(index * size, size), size)

    def core_copy(chunk):
        return remote(
            0,
            chunk,
            part_buf.at[chunk % STAGED, :, rows_at(1 - core, half)],
            core_in.at[chunk % SLOTS],
            core_partner,
        )

    def y_copy(chunk):
        slot = chunk % SLOTS
        return remote(1, chunk, other_kept.at[slot], y_in.at[slot], y_partner)

    def x_copy(chunk):
        slot = chunk % SLOTS
        return remote(2, chunk, x_out.at[slot], x_in.at[slot], x_partner)

    def outer_copy(chunk):
        slot = chunk % SLOTS
        return remote(3, chunk, z_kept.at[slot], outer_in.at[slot], z_partner)

    def inner_copy(chunk):
        slot = chunk % SLOTS
        return remote(4, chunk, z_kept.at[slot], inner_in.at[slot], middle_partner)

    own_rows = rows_at(2 * core + x, quarter)

    def back_copy(chunk):
        piece = result.at[chunk % SLOTS, own_rows]
        return remote(5, chunk, piece, piece, z_partner)

    def gather_copy(chunk):
        piece = result.at[chunk % SLOTS, own_rows]
        return remote(6, chunk, piece, piece, x_partner)

    def whole_copy(chunk):
        piece = result.at[chunk % SLOTS, rows_at(core, half)]
        return remote(7, chunk, piece, piece, core_partner)

    def store_copy(chunk, target):
        slot = chunk % SLOTS
        return pltpu.make_async_copy(result.at[slot], target, store_sem.at[slot])

    def multiply(chunk):
        slot = chunk % STAGED
        wait_operands(chunk)

        def action(member, kind, i, j):
            single = one_buf[slot]
            for which in range(2):
                split = pair_buf[slot, which]
                product = dot_tn(split, single) if kind == "rows" else dot_tn(single, split)
                part_buf[slot, which] = product.astype(jnp.bfloat16)

        kinds = {}
        for member, (kind, rows, columns) in enumerate(plan):
            inside = (chunk >= starts[member]) & (chunk < starts[member] + rows * columns)
            kinds[kind] = kinds[kind] | inside if kind in kinds else inside
        for kind, inside in kinds.items():

            @pl.when(inside)
            def _(kind=kind):
                action(None, kind, None, None)

        core_copy(chunk).start()

    def after_core(chunk):
        slot = chunk % SLOTS
        core_copy(chunk).wait()
        mine = rows_at(core, half)
        other_kept[slot] = added(part_buf[chunk % STAGED, 1, mine, :], core_in[slot, 1])
        y_copy(chunk).start()
        own_kept[slot] = added(part_buf[chunk % STAGED, 0, mine, :], core_in[slot, 0])

    def after_y(chunk):
        slot = chunk % SLOTS
        y_copy(chunk).wait()
        away, here = rows_at(1 - x, quarter), rows_at(x, quarter)
        x_out[slot] = added(own_kept[slot, away, :], y_in[slot, away, :])
        x_copy(chunk).start()
        x_kept[slot] = added(own_kept[slot, here, :], y_in[slot, here, :])

    def after_x(chunk):
        slot = chunk % SLOTS
        x_copy(chunk).wait()
        z_kept[slot] = added(x_kept[slot], x_in[slot])

        @pl.when(inner == 0)
        def _():
            outer_copy(chunk).start()

    def after_outer(chunk):
        slot = chunk % SLOTS

        @pl.when(inner == 0)
        def _():
            outer_copy(chunk).wait_send()

        @pl.when(inner == 1)
        def _():
            outer_copy(chunk).wait_recv()
            z_kept[slot] = added(z_kept[slot], outer_in[slot])
            inner_copy(chunk).start()

    def after_inner(chunk):
        slot = chunk % SLOTS

        @pl.when(inner == 1)
        def _():
            inner_copy(chunk).wait()
            result[slot, own_rows, :] = added(z_kept[slot], inner_in[slot])
            back_copy(chunk).start()

    def after_back(chunk):
        @pl.when(inner == 0)
        def _():
            back_copy(chunk).wait_recv()

        @pl.when(inner == 1)
        def _():
            back_copy(chunk).wait_send()

        gather_copy(chunk).start()

    def after_gather(chunk):
        gather_copy(chunk).wait()
        whole_copy(chunk).start()

    def after_whole(chunk):
        whole_copy(chunk).wait()

        def action(member, kind, i, j):
            store_copy(chunk, out_refs[member].at[rows_at(i, block), rows_at(j, block)]).start()

        for_matrix(chunk, action)

    def after_store(chunk):
        store_copy(chunk, result.at[chunk % SLOTS]).wait()

    vector_partners = (core_partner, y_partner, x_partner, z_partner, middle_partner, z_partner)

    def vector_copy(step):
        target = vector_out if step == 5 else vec_in.at[step]
        return pltpu.make_async_remote_copy(
            src_ref=vector_out,
            dst_ref=target,
            send_sem=vec_send.at[step],
            recv_sem=vec_recv.at[step],
            device_id=vector_partners[step],
            device_id_type=MESH,
        )

    def add_vector(step):
        vector_out[...] = vector_out[...] + vec_in[step]

    def vector_tick(step):
        if step == 0:
            vector_out[...] = vector_ref[...]
            vector_copy(0).start()
        elif step <= 3:
            vector_copy(step - 1).wait()
            add_vector(step - 1)
            if step < 3:
                vector_copy(step).start()
            else:

                @pl.when(inner == 0)
                def _():
                    vector_copy(3).start()

        elif step == 4:

            @pl.when(inner == 0)
            def _():
                vector_copy(3).wait_send()

            @pl.when(inner == 1)
            def _():
                vector_copy(3).wait_recv()
                add_vector(3)
                vector_copy(4).start()

        elif step == 5:

            @pl.when(inner == 1)
            def _():
                vector_copy(4).wait()
                add_vector(4)
                vector_copy(5).start()

        else:

            @pl.when(inner == 1)
            def _():
                vector_copy(5).wait_send()

            @pl.when(inner == 0)
            def _():
                vector_copy(5).wait_recv()

    stages = (
        (LAGS["core"], after_core),
        (0, multiply),
        (LAGS["y"], after_y),
        (LAGS["x"], after_x),
        (LAGS["outer"], after_outer),
        (LAGS["inner"], after_inner),
        (LAGS["back"], after_back),
        (LAGS["gather"], after_gather),
        (LAGS["stored"], after_store),
        (LAGS["whole"], after_whole),
    )

    stage_operands(0)

    def tick(t, carry):
        @pl.when(t + 1 < chunks)
        def _():
            stage_operands(t + 1)

        for lag, action in stages:
            chunk = t - lag

            @pl.when((chunk >= 0) & (chunk < chunks))
            def _(chunk=chunk, action=action):
                action(chunk)

        for step, when in enumerate(VECTOR_TICKS):

            @pl.when(t == when)
            def _(step=step):
                vector_tick(step)

        return carry

    lax.fori_loop(0, max(chunks + LAGS["stored"], VECTOR_TICKS[-1] + 1), tick, 0)


def reduce_grads(plan, operands, vector, block):
    half, quarter = block // 2, block // 4
    kept = operands[0][0].shape[0]
    low = jnp.bfloat16
    shapes = [jax.ShapeDtypeStruct((rows * block, columns * block), low) for _, rows, columns in plan]
    shapes.append(jax.ShapeDtypeStruct(vector.shape, jnp.float32))
    anywhere = pl.BlockSpec(memory_space=pl.ANY)
    in_vmem = pl.BlockSpec(memory_space=pltpu.VMEM)
    chunks = sum(rows * columns for _, rows, columns in plan)
    return pl.pallas_call(
        functools.partial(reduce_kernel, plan, block),
        in_specs=[anywhere] * (3 * len(plan)) + [in_vmem],
        out_specs=[anywhere] * len(plan) + [in_vmem],
        out_shape=shapes,
        scratch_shapes=[
            pltpu.VMEM((STAGED, 2, kept, block), low),
            pltpu.VMEM((STAGED, kept, block), low),
            pltpu.VMEM((STAGED, 2, block, block), low),
            pltpu.VMEM((SLOTS, 2, half, block), low),
            pltpu.VMEM((SLOTS, half, block), low),
            pltpu.VMEM((SLOTS, half, block), low),
            pltpu.VMEM((SLOTS, half, block), low),
            pltpu.VMEM((SLOTS, quarter, block), low),
            pltpu.VMEM((SLOTS, quarter, block), low),
            pltpu.VMEM((SLOTS, quarter, block), low),
            pltpu.VMEM((SLOTS, quarter, block), low),
            pltpu.VMEM((SLOTS, quarter, block), low),
            pltpu.VMEM((SLOTS, quarter, block), low),
            pltpu.VMEM((SLOTS, block, block), low),
            pltpu.VMEM((5,) + vector.shape, jnp.float32),
            pltpu.SemaphoreType.DMA((STAGED, 3)),
            pltpu.SemaphoreType.DMA((8, SLOTS)),
            pltpu.SemaphoreType.DMA((8, SLOTS)),
            pltpu.SemaphoreType.DMA((SLOTS,)),
            pltpu.SemaphoreType.DMA((6,)),
            pltpu.SemaphoreType.DMA((6,)),
        ],
        compiler_params=pltpu.CompilerParams(
            collective_id=0, has_side_effects=True, vmem_limit_bytes=VMEM_ASKED
        ),
        cost_estimate=pl.CostEstimate(
            flops=4 * chunks * block * block * kept,
            bytes_accessed=chunks * block * (3 * kept + block) * 2,
            transcendentals=0,
        ),
        name="reduce_grads",
    )(*[member for triple in operands for member in triple], vector)


def dot_low(left, right):
    return jnp.dot(left, right, preferred_element_type=jnp.float32)


def local_split(
    tokens_in,
    segments,
    w_qkv,
    qv_bias,
    w_out,
    w_up,
    up_bias,
    w_down,
    out_bias,
    ln_gain,
    ln_bias,
    cotangent,
):
    layers, width = w_qkv.shape[0], w_qkv.shape[1]
    rows = tokens_in.shape[0]
    place = lax.axis_index("dp")
    y = lax.axis_index("tensor")
    core, x = place % 2, (place // 2) % 2
    hops = [(X_BIT, x), (CORE_BIT, core)]

    residual = swap_windows(tokens_in).astype(jnp.float32)
    grad_residual = swap_windows(cotangent)
    window_segments = jnp.where(core == y, segments, swap_dp(segments, CORE_BIT))
    own_segments = lax.dynamic_slice_in_dim(window_segments, core * rows, rows, axis=1)
    halo_segments = jnp.where(core == 1, window_segments[:, rows - BAND : rows], -1)
    segq = own_segments.reshape(rows, 1)
    segk = jnp.concatenate([halo_segments, own_segments], axis=1)

    def natural(own, other):
        return join_halves(y, own, other)

    qkv_rows = [w_qkv[l].reshape(width, -1) for l in range(layers)]
    weights = []
    for l in range(layers):
        own = (qkv_rows[l], w_out[l], w_up[l], w_down[l])
        other = tuple(other_half(member, hops) for member in own)
        bias_own = (qv_bias[l].reshape(-1), up_bias[l])
        bias_other = tuple(swap_y(member) for member in bias_own)
        weights.append(tuple(zip(own + bias_own, other + bias_other)))

    kept = []
    count = lax.axis_size("dp")
    to_second = [(2 * i, 2 * i + 1) for i in range(count // 2)]
    to_first = [(2 * i + 1, 2 * i) for i in range(count // 2)]
    for l in range(layers):
        qkv, out_w, up, down, qv, upb = weights[l]
        normed, _, _ = layer_norm(residual, ln_gain[l, 0], ln_bias[l, 0])
        normed = normed.astype(jnp.bfloat16)
        saved_attention = []
        branch = 0.0
        for half in range(2):
            third = qkv[half].shape[1] // 3
            bias = jnp.concatenate(
                [qv[half][:third], jnp.zeros((third,), jnp.float32), qv[half][third:]]
            )
            projected = (dot_low(normed, qkv[half]) + bias).astype(jnp.bfloat16)
            halo = lax.ppermute(projected[rows - BAND :, third:], "dp", to_second)
            attended, totals = attention_forward(projected, halo, segq, segk)
            branch = branch + dot_low(attended, out_w[half])
            saved_attention.append((projected, halo, attended, totals))
        middle = residual + branch + out_bias[l, 0]
        normed_two, _, _ = layer_norm(middle, ln_gain[l, 1], ln_bias[l, 1])
        normed_two = normed_two.astype(jnp.bfloat16)
        saved_ffn = []
        branch = 0.0
        for half in range(2):
            before = dot_low(normed_two, up[half]) + upb[half]
            activated = gelu_tanh(before).astype(jnp.bfloat16)
            slope = gelu_slope(before).astype(jnp.bfloat16)
            branch = branch + dot_low(activated, down[half])
            saved_ffn.append((activated, slope))
        kept.append((residual, normed, saved_attention, middle, normed_two, saved_ffn))
        residual = middle + branch + out_bias[l, 1]
    out_act = swap_windows(residual.astype(jnp.bfloat16))

    grad_residual = grad_residual.astype(jnp.float32)
    triples = []
    vectors = [None] * layers
    for l in reversed(range(layers)):
        qkv, out_w, up, down, qv, upb = weights[l]
        residual, normed, saved_attention, middle, normed_two, saved_ffn = kept[l]
        grad_branch = grad_residual.astype(jnp.bfloat16)
        grad_down, grad_up, grad_up_bias = [], [], []
        incoming = 0.0
        for half in range(2):
            activated, slope = saved_ffn[half]
            grad_before = (dot_nt(grad_branch, down[half]) * slope.astype(jnp.float32)).astype(
                jnp.bfloat16
            )
            grad_down.append(activated)
            grad_up.append(grad_before)
            grad_up_bias.append(jnp.sum(grad_before, axis=0, dtype=jnp.float32))
            incoming = incoming + dot_nt(grad_before, up[half])
        _, unit, inverse = layer_norm(middle, ln_gain[l, 1], ln_bias[l, 1])
        through, gain_two, shift_two = norm_backward(incoming, unit, inverse, ln_gain[l, 1])
        grad_middle = grad_residual + through
        grad_attn = grad_middle.astype(jnp.bfloat16)
        grad_out, grad_qkv, grad_qv = [], [], []
        incoming = 0.0
        for half in range(2):
            projected, halo, attended, totals = saved_attention[half]
            grad_out.append(attended)
            grad_attended = dot_nt(grad_attn, out_w[half]).astype(jnp.bfloat16)
            dq, dk, dv, dkh, dvh = attention_backward(
                projected, halo, segq, segk, grad_attended, totals
            )
            sent = lax.ppermute(jnp.concatenate([dkh, dvh], axis=1), "dp", to_first)
            whole = jnp.pad(sent, ((rows - BAND, 0), (0, 0))).astype(jnp.float32)
            third = dk.shape[1]
            grad_projected = jnp.concatenate(
                [
                    dq,
                    (dk + whole[:, :third]).astype(jnp.bfloat16),
                    (dv + whole[:, third:]).astype(jnp.bfloat16),
                ],
                axis=1,
            )
            grad_qkv.append(grad_projected)
            sums = jnp.sum(grad_projected, axis=0, dtype=jnp.float32)
            grad_qv.append(jnp.stack([sums[:third], sums[2 * third :]]))
            incoming = incoming + dot_nt(grad_projected, qkv[half])
        _, unit, inverse = layer_norm(residual, ln_gain[l, 0], ln_bias[l, 0])
        through, gain_one, shift_one = norm_backward(incoming, unit, inverse, ln_gain[l, 0])
        triples += [
            (grad_branch, *grad_down),
            (normed_two, *grad_up),
            (grad_attn, *grad_out),
            (normed, *grad_qkv),
        ]
        vectors[l] = jnp.concatenate(
            [
                natural(grad_qv[0].T, grad_qv[1].T).T.reshape(-1),
                natural(grad_up_bias[0], grad_up_bias[1]),
                jnp.sum(grad_attn, axis=0, dtype=jnp.float32),
                jnp.sum(grad_branch, axis=0, dtype=jnp.float32),
                gain_one,
                gain_two,
                shift_one,
                shift_two,
            ]
        )
        grad_residual = grad_middle + through
    grad_in = swap_windows(grad_residual.astype(jnp.bfloat16))
    block = width // 2
    plan = []
    for shared, own, _ in triples:
        by_rows = shared is not None and len(plan) % 2 == 0
        split, single = own.shape[1] // block, shared.shape[1] // block
        plan.append(("rows", split, single) if by_rows else ("columns", single, split))
    vector = jnp.stack(vectors)
    *reduced, summed = reduce_grads(tuple(plan), triples, vector.reshape(-1, LANES), block)
    summed = summed.reshape(vector.shape)
    hidden = 2 * up_bias.shape[1]
    ends = [2 * width, 2 * width + hidden, 4 * width + hidden, 6 * width + hidden]
    qv_sum = summed[:, : ends[0]].reshape(layers, 2, width)
    grad_qv_bias = lax.dynamic_slice_in_dim(qv_sum, y * (width // 2), width // 2, axis=2)
    grad_up_bias = lax.dynamic_slice_in_dim(
        summed[:, ends[0] : ends[1]], y * (hidden // 2), hidden // 2, axis=1
    )
    stacked = [
        jnp.stack(
            [reduced[4 * (layers - 1 - l) + 3 - member] for l in range(layers)]
        ).astype(jnp.float32)
        for member in range(4)
    ]
    return (
        out_act,
        grad_in,
        stacked[0].reshape(w_qkv.shape),
        grad_qv_bias,
        stacked[1],
        stacked[2],
        grad_up_bias,
        stacked[3],
        summed[:, ends[1] : ends[2]].reshape(layers, 2, width),
        summed[:, ends[2] : ends[3]].reshape(layers, 2, width),
        summed[:, ends[3] :].reshape(layers, 2, width),
    )


def solution(mesh):
    sizes = (mesh.shape["dp"], mesh.shape["tensor"])
    local = local_split if sizes == (16, 2) else local_general
    return jax.shard_map(
        local,
        mesh=mesh,
        in_specs=(
            P(("dp", "tensor"), None),
            P("dp", None),
            P(None, None, None, "tensor"),
            P(None, None, "tensor"),
            P(None, "tensor", None),
            P(None, None, "tensor"),
            P(None, "tensor"),
            P(None, "tensor", None),
            P(),
            P(),
            P(),
            P(("dp", "tensor"), None),
        ),
        out_specs=(
            P(("dp", "tensor"), None),
            P(("dp", "tensor"), None),
            P(None, None, None, "tensor"),
            P(None, None, "tensor"),
            P(None, "tensor", None),
            P(None, None, "tensor"),
            P(None, "tensor"),
            P(None, "tensor", None),
            P(),
            P(),
            P(),
        ),
        check_vma=False,
    )
```

```python
import functools

import jax
import jax.numpy as jnp
from jax import lax
from jax.experimental import pallas as pl
from jax.experimental.pallas import tpu as pltpu
from jax.sharding import PartitionSpec as P

HEAD_DIM = 64


epsilon = 1e-05
gelu_coeff = 0.7978845608028654
cubic_coeff = 0.044715
masked_score = -1e30


def as_sent(shard):

    def short(part):
        return part.astype(jnp.bfloat16) if part.dtype == jnp.float32 else part

    return jax.tree.map(short, shard)


def layer_norm(values, gain, shift):
    average = jnp.mean(values, axis=-1, keepdims=True)
    centred = values - average
    inverse = lax.rsqrt(jnp.mean(centred * centred, axis=-1, keepdims=True) + epsilon)
    unit_rows = centred * inverse
    return (unit_rows * gain + shift, unit_rows, inverse)


def norm_backward(incoming, unit_rows, inverse, gain):
    scaled = incoming * gain
    first_mean = jnp.mean(scaled, axis=-1, keepdims=True)
    second_mean = jnp.mean(scaled * unit_rows, axis=-1, keepdims=True)
    through = inverse * (scaled - first_mean - unit_rows * second_mean)
    return (through, jnp.sum(incoming * unit_rows, axis=0), jnp.sum(incoming, axis=0))


def gelu_tanh(before):
    tanh_input = gelu_coeff * (before + cubic_coeff * before * before * before)
    return 0.5 * before * (1.0 + jnp.tanh(tanh_input))


def gelu_slope(before):
    tanh_input = gelu_coeff * (before + cubic_coeff * before * before * before)
    tangent = jnp.tanh(tanh_input)
    return 0.5 * (1.0 + tangent) + 0.5 * before * (1.0 - tangent * tangent) * gelu_coeff * (
        1.0 + 3.0 * cubic_coeff * before * before
    )


def masked_scores(query_block, key_seq, segment_row, offset, block_rows):
    window = key_seq.shape[0]
    scores = jnp.einsum(
        "qhe,khe->hqk", query_block, key_seq, preferred_element_type=jnp.float32
    ) * HEAD_DIM ** (-0.5)
    query_place = offset + lax.iota(jnp.int32, block_rows)
    key_place = lax.iota(jnp.int32, window)
    query_segment = segment_row[offset : offset + block_rows]
    allowed = (query_place[:, None] >= key_place[None, :]) & (
        query_segment[:, None] == segment_row[None, :]
    )
    return jnp.where(allowed[None], scores, masked_score)


def split_heads(flat_rows, seq_count):
    return flat_rows.reshape(
        seq_count, flat_rows.shape[0] // seq_count, flat_rows.shape[1] // HEAD_DIM, HEAD_DIM
    )


def attend_forward(query_rows, key_rows, value_rows, segments):
    seq_count, window = segments.shape
    block_rows = min(512, window)

    def one_sequence(member):
        query_seq, key_seq, value_seq, segment_row = member
        outputs = []
        totals = []
        for block_index in range(window // block_rows):
            offset = block_index * block_rows
            scores = masked_scores(
                query_seq[offset : offset + block_rows], key_seq, segment_row, offset, block_rows
            )
            highest = jnp.max(scores, axis=-1, keepdims=True)
            raised = jnp.exp(scores - highest)
            summed = jnp.sum(raised, axis=-1, keepdims=True)
            softmax_low = (raised / summed).astype(jnp.bfloat16)
            block_out = jnp.einsum(
                "hqk,khe->qhe", softmax_low, value_seq, preferred_element_type=jnp.float32
            )
            outputs.append(block_out.astype(jnp.bfloat16))
            totals.append(highest[..., 0] + jnp.log(summed[..., 0]))
        return (jnp.concatenate(outputs, axis=0), jnp.stack(totals, axis=0))

    attended, log_totals = lax.map(
        one_sequence,
        (
            split_heads(query_rows, seq_count),
            split_heads(key_rows, seq_count),
            split_heads(value_rows, seq_count),
            segments,
        ),
    )
    return (attended.reshape(query_rows.shape), log_totals)


def attend_backward(query_rows, key_rows, value_rows, segments, log_totals, grad_attended):
    seq_count, window = segments.shape
    block_rows = min(512, window)
    scaling = HEAD_DIM ** (-0.5)

    def one_sequence(member):
        query_seq, key_seq, value_seq, segment_row, totals_seq, grad_seq = member
        query_parts = []
        grad_keys = jnp.zeros(key_seq.shape, jnp.float32)
        grad_values = jnp.zeros(value_seq.shape, jnp.float32)
        for block_index in range(window // block_rows):
            offset = block_index * block_rows
            query_block = query_seq[offset : offset + block_rows]
            grad_block = grad_seq[offset : offset + block_rows]
            scores = masked_scores(query_block, key_seq, segment_row, offset, block_rows)
            softmax_exact = jnp.exp(scores - totals_seq[block_index][..., None])
            softmax_low = softmax_exact.astype(jnp.bfloat16)
            grad_softmax = jnp.einsum(
                "qhe,khe->hqk", grad_block, value_seq, preferred_element_type=jnp.float32
            )
            row_terms = jnp.sum(softmax_exact * grad_softmax, axis=-1, keepdims=True)
            grad_scores = (softmax_exact * (grad_softmax - row_terms)).astype(jnp.bfloat16)
            query_parts.append(
                jnp.einsum("hqk,khe->qhe", grad_scores, key_seq, preferred_element_type=jnp.float32)
                * scaling
            )
            grad_keys = (
                grad_keys
                + jnp.einsum(
                    "hqk,qhe->khe", grad_scores, query_block, preferred_element_type=jnp.float32
                )
                * scaling
            )
            grad_values = grad_values + jnp.einsum(
                "hqk,qhe->khe", softmax_low, grad_block, preferred_element_type=jnp.float32
            )
        grad_query = jnp.concatenate(query_parts, axis=0)
        return (
            grad_query.astype(jnp.bfloat16),
            grad_keys.astype(jnp.bfloat16),
            grad_values.astype(jnp.bfloat16),
        )

    grad_query, grad_keys, grad_values = lax.map(
        one_sequence,
        (
            split_heads(query_rows, seq_count),
            split_heads(key_rows, seq_count),
            split_heads(value_rows, seq_count),
            segments,
            log_totals,
            split_heads(grad_attended, seq_count),
        ),
    )
    return (
        grad_query.reshape(query_rows.shape),
        grad_keys.reshape(query_rows.shape),
        grad_values.reshape(query_rows.shape),
    )


def layer_forward(residual, segments, weights):
    w_qkv, qv_bias, w_out, w_up, up_bias, w_down, out_bias, gains, shifts = weights
    row_count = residual.shape[0]
    normed, unit_one, inverse_one = layer_norm(residual, gains[0], shifts[0])
    normed_all = lax.all_gather(normed.astype(jnp.bfloat16), "tensor", axis=0, tiled=True)
    projected = jnp.einsum("td,dsc->tsc", normed_all, w_qkv, preferred_element_type=jnp.float32)
    query_rows = (projected[:, 0] + qv_bias[0]).astype(jnp.bfloat16)
    key_rows = projected[:, 1].astype(jnp.bfloat16)
    value_rows = (projected[:, 2] + qv_bias[1]).astype(jnp.bfloat16)
    attended, log_totals = attend_forward(query_rows, key_rows, value_rows, segments)
    middle = (
        residual
        + lax.psum_scatter(
            jnp.dot(
                lax.slice_in_dim(attended, 0, row_count * lax.axis_size("tensor"), axis=0),
                w_out,
                preferred_element_type=jnp.float32,
            ).astype(jnp.bfloat16),
            "tensor",
            scatter_dimension=0,
            tiled=True,
        ).astype(jnp.float32)
        + out_bias[0]
    )
    normed_two, unit_two, inverse_two = layer_norm(middle, gains[1], shifts[1])
    normed_low = normed_two.astype(jnp.bfloat16)
    ffn_rows = lax.all_gather(normed_low, "tensor", axis=0, tiled=True)
    before = jnp.dot(ffn_rows, w_up, preferred_element_type=jnp.float32) + up_bias
    activated = gelu_tanh(before).astype(jnp.bfloat16)
    ffn_branch = lax.psum_scatter(
        jnp.dot(
            lax.slice_in_dim(activated, 0, row_count * lax.axis_size("tensor"), axis=0),
            w_down,
            preferred_element_type=jnp.float32,
        ).astype(jnp.bfloat16),
        "tensor",
        scatter_dimension=0,
        tiled=True,
    ).astype(jnp.float32)
    kept_ffn = (w_up, w_down)
    result = middle + ffn_branch + out_bias[1]
    kept_state = (
        unit_one,
        inverse_one,
        normed_all,
        query_rows,
        key_rows,
        value_rows,
        attended,
        log_totals,
        unit_two,
        inverse_two,
        ffn_rows,
        before,
        activated,
        kept_ffn,
    )
    return (result, kept_state)


def layer_backward(grad_residual, segments, weights, kept_state):
    w_qkv, qv_bias, w_out, w_up, up_bias, w_down, out_bias, gains, shifts = weights
    (
        unit_one,
        inverse_one,
        normed_all,
        query_rows,
        key_rows,
        value_rows,
        attended,
        log_totals,
        unit_two,
        inverse_two,
        ffn_rows,
        before,
        activated,
        kept_ffn,
    ) = kept_state
    up_used, down_used = kept_ffn
    row_count = grad_residual.shape[0]
    grad_branch = grad_residual.astype(jnp.bfloat16)
    bias_down = jnp.sum(grad_branch, axis=0, dtype=jnp.float32)
    grad_rows = lax.all_gather(grad_branch, "tensor", axis=0, tiled=True)
    grad_hidden = jnp.einsum("td,fd->tf", grad_rows, down_used, preferred_element_type=jnp.float32)
    grad_before = (grad_hidden * gelu_slope(before)).astype(jnp.bfloat16)
    grad_down = jnp.einsum("tf,td->fd", activated, grad_rows, preferred_element_type=jnp.float32)
    grad_up = jnp.einsum("td,tf->df", ffn_rows, grad_before, preferred_element_type=jnp.float32)
    grad_up_bias = jnp.sum(grad_before, axis=0, dtype=jnp.float32)
    piece_rows = lax.slice_in_dim(grad_before, 0, row_count * lax.axis_size("tensor"), axis=0)
    grad_normed_two = lax.psum_scatter(
        jnp.einsum("tf,df->td", piece_rows, w_up, preferred_element_type=jnp.float32).astype(
            jnp.bfloat16
        ),
        "tensor",
        scatter_dimension=0,
        tiled=True,
    ).astype(jnp.float32)
    through_two, gain_two, shift_two = norm_backward(
        grad_normed_two, unit_two, inverse_two, gains[1]
    )
    grad_middle = grad_residual + through_two
    grad_attn_branch = grad_middle.astype(jnp.bfloat16)
    bias_attn = jnp.sum(grad_attn_branch, axis=0, dtype=jnp.float32)
    grad_attn_all = lax.all_gather(grad_attn_branch, "tensor", axis=0, tiled=True)
    grad_out_w = jnp.einsum(
        "tc,td->cd", attended, grad_attn_all, preferred_element_type=jnp.float32
    )
    grad_attended = jnp.einsum(
        "td,cd->tc", grad_attn_all, w_out, preferred_element_type=jnp.float32
    ).astype(jnp.bfloat16)
    grad_query, grad_keys, grad_values = attend_backward(
        query_rows, key_rows, value_rows, segments, log_totals, grad_attended
    )
    grad_projected = jnp.stack((grad_query, grad_keys, grad_values), axis=1)
    grad_qkv = jnp.einsum(
        "td,tsc->dsc", normed_all, grad_projected, preferred_element_type=jnp.float32
    )
    grad_qv_bias = jnp.stack(
        (
            jnp.sum(grad_query, axis=0, dtype=jnp.float32),
            jnp.sum(grad_values, axis=0, dtype=jnp.float32),
        )
    )
    piece_rows = lax.slice_in_dim(grad_projected, 0, row_count * lax.axis_size("tensor"), axis=0)
    grad_normed = lax.psum_scatter(
        jnp.einsum("tsc,dsc->td", piece_rows, w_qkv, preferred_element_type=jnp.float32).astype(
            jnp.bfloat16
        ),
        "tensor",
        scatter_dimension=0,
        tiled=True,
    ).astype(jnp.float32)
    through_one, gain_one, shift_one = norm_backward(grad_normed, unit_one, inverse_one, gains[0])
    grad_input = grad_middle + through_one
    spread = (grad_qkv, grad_qv_bias, grad_out_w, grad_up, grad_up_bias, grad_down)
    shared = (
        jnp.stack((bias_attn, bias_down)),
        jnp.stack((gain_one, gain_two)),
        jnp.stack((shift_one, shift_two)),
    )
    return (grad_input, spread, shared)


def local_general(
    tokens_in,
    segments,
    w_qkv,
    qv_bias,
    w_out,
    w_up,
    up_bias,
    w_down,
    out_bias,
    ln_gain,
    ln_bias,
    cotangent,
):
    layers_total = w_qkv.shape[0]
    all_params = (w_qkv, qv_bias, w_out, w_up, up_bias, w_down, out_bias, ln_gain, ln_bias)
    residual = tokens_in.astype(jnp.float32)
    kept_layers = []
    for layer_index in range(layers_total):
        weights = tuple((member_array[layer_index] for member_array in all_params))
        residual, kept_state = layer_forward(residual, segments, weights)
        kept_layers.append(kept_state)
    out_act = residual.astype(jnp.bfloat16)
    grad_residual = cotangent.astype(jnp.float32)
    spread_layers = []
    shared_layers = []
    for layer_index in reversed(range(layers_total)):
        weights = tuple((member_array[layer_index] for member_array in all_params))
        grad_residual, spread, shared = layer_backward(
            grad_residual, segments, weights, kept_layers[layer_index]
        )
        spread_layers.insert(0, spread)
        shared_layers.insert(0, shared)
    spread_stack = tuple(
        (
            jnp.stack([spread_layers[layer_index][position] for layer_index in range(layers_total)])
            for position in range(6)
        )
    )
    spread_stack = jax.tree.map(
        lambda part: part.astype(jnp.float32), lax.psum(as_sent(spread_stack), "dp")
    )
    shared_stack = tuple(
        (
            jnp.stack([shared_layers[layer_index][position] for layer_index in range(layers_total)])
            for position in range(3)
        )
    )
    shared_stack = lax.psum(shared_stack, ("dp", "tensor"))
    grad_in = grad_residual.astype(jnp.bfloat16)
    return (out_act, grad_in) + tuple(spread_stack) + tuple(shared_stack)


CORE_BIT = 1
X_BIT = 2
Z_BIT = 4
BAND = 256
LANES = 128
VMEM_ASKED = 60 * 2**20


def dot_nt(left, right):
    return lax.dot_general(left, right, (((1,), (1,)), ((), ())), preferred_element_type=jnp.float32)


def dot_tn(left, right):
    return lax.dot_general(left, right, (((0,), (0,)), ((), ())), preferred_element_type=jnp.float32)


def fill_band_bias(segq_ref, segk_ref, bias_ref):
    blocks = bias_ref.shape[0]
    for block in range(blocks):
        rows = slice(block * BAND, (block + 1) * BAND)
        columns = slice(block * BAND, (block + 2) * BAND)
        row_place = lax.broadcasted_iota(jnp.int32, (BAND, 2 * BAND), 0) + BAND
        column_place = lax.broadcasted_iota(jnp.int32, (BAND, 2 * BAND), 1)
        allowed = (segq_ref[rows, :] == segk_ref[:, columns]) & (column_place <= row_place)
        bias_ref[block] = jnp.where(allowed, 0.0, masked_score)


def band_rows(halo_ref, rows_ref, block):
    if block == 0:
        return jnp.concatenate([halo_ref[...], rows_ref[0:BAND, :]], axis=0)
    return rows_ref[(block - 1) * BAND : (block + 1) * BAND, :]


def attention_forward_kernel(
    q_ref, k_ref, v_ref, kh_ref, vh_ref, segq_ref, segk_ref, out_ref, total_ref, bias_ref
):
    pair = pl.program_id(0)

    @pl.when(pair == 0)
    def _():
        fill_band_bias(segq_ref, segk_ref, bias_ref)
        total_ref[...] = jnp.zeros_like(total_ref)

    lane = lax.broadcasted_iota(jnp.int32, (BAND, LANES), 1)
    for block in range(bias_ref.shape[0]):
        rows = slice(block * BAND, (block + 1) * BAND)
        query = q_ref[rows, :]
        keys = band_rows(kh_ref, k_ref, block)
        values = band_rows(vh_ref, v_ref, block)
        parts = []
        kept = total_ref[rows, :]
        for head in range(2):
            mine = (lane // HEAD_DIM) == head
            scores = dot_nt(jnp.where(mine, query, 0), keys) * HEAD_DIM ** (-0.5) + bias_ref[block]
            highest = jnp.max(scores, axis=-1, keepdims=True)
            raised = jnp.exp(scores - highest)
            summed = jnp.sum(raised, axis=-1, keepdims=True)
            weighted = jnp.dot(
                raised.astype(jnp.bfloat16), values, preferred_element_type=jnp.float32
            )
            parts.append(weighted / summed)
            kept = jnp.where(lane == 2 * pair + head, highest + jnp.log(summed), kept)
        total_ref[rows, :] = kept
        out_ref[rows, :] = jnp.where(lane < HEAD_DIM, parts[0], parts[1]).astype(out_ref.dtype)


def attention_specs(rows, pairs):
    whole = lambda pair: (0, 0)
    return [
        pl.BlockSpec((rows, LANES), lambda pair: (0, pair)),
        pl.BlockSpec((rows, LANES), lambda pair: (0, pairs + pair)),
        pl.BlockSpec((rows, LANES), lambda pair: (0, 2 * pairs + pair)),
        pl.BlockSpec((BAND, LANES), lambda pair: (0, pair)),
        pl.BlockSpec((BAND, LANES), lambda pair: (0, pairs + pair)),
        pl.BlockSpec((rows, 1), whole),
        pl.BlockSpec((1, rows + BAND), whole),
    ]


def attention_forward(projected, halo, segq, segk):
    rows, wide = projected.shape
    width = wide // 3
    pairs = width // LANES
    return pl.pallas_call(
        attention_forward_kernel,
        grid=(pairs,),
        in_specs=attention_specs(rows, pairs),
        out_specs=[
            pl.BlockSpec((rows, LANES), lambda pair: (0, pair)),
            pl.BlockSpec((rows, LANES), lambda pair: (0, 0)),
        ],
        out_shape=[
            jax.ShapeDtypeStruct((rows, width), jnp.bfloat16),
            jax.ShapeDtypeStruct((rows, LANES), jnp.float32),
        ],
        scratch_shapes=[pltpu.VMEM((rows // BAND, BAND, 2 * BAND), jnp.float32)],
        compiler_params=pltpu.CompilerParams(vmem_limit_bytes=VMEM_ASKED),
        cost_estimate=pl.CostEstimate(
            flops=8 * rows * BAND * width, bytes_accessed=10 * rows * width, transcendentals=rows * width * 8
        ),
        name="attention_forward",
    )(projected, projected, projected, halo, halo, segq, segk)


def swap_dp(array, bit):
    count = lax.axis_size("dp")
    return lax.ppermute(array, "dp", [(i, i ^ bit) for i in range(count)])


def swap_y(array):
    return lax.ppermute(array, "tensor", [(0, 1), (1, 0)])


def swap_windows(array):
    pairs = []
    for group in range(lax.axis_size("dp") // 2):
        for core in range(2):
            for y in range(2):
                pairs.append(((2 * group + core) * 2 + y, (2 * group + y) * 2 + core))
    return lax.ppermute(array, ("dp", "tensor"), pairs)


def half_of(array, bit):
    rows = array.shape[0] // 2
    return lax.dynamic_slice_in_dim(array, bit * rows, rows, axis=0)


def join_halves(bit, mine, other):
    return jnp.where(
        bit == 0, jnp.concatenate([mine, other], axis=0), jnp.concatenate([other, mine], axis=0)
    )


def other_half(array, hops):
    if not hops:
        return swap_y(array)
    bit, place = hops[-1]
    mine = other_half(half_of(array, place), hops[:-1])
    return join_halves(place, mine, swap_dp(mine, bit))


SLOTS = 8
CORE_SLOTS = 4
RESULT_SLOTS = 11
STAGED = 2
FIRST = 2
LAGS = dict(core=1, y=3, x=5, outer=7, inner=9, back=11, gather=13, whole=14, stored=15)
VECTOR_STEP = 3
VECTOR_ROWS = 12
MESH = pl.DeviceIdType.MESH
FFN_STEPS = 4
QKV_STEPS = 3


def added(left, right):
    return (left.astype(jnp.float32) + right.astype(jnp.float32)).astype(jnp.bfloat16)


def backward_kernel(layers, block, hidden_half, *refs):
    (
        cot_ref,
        gain_ref,
        segq_ref,
        segk_ref,
        act_ref,
        slope_ref,
        normed_two_ref,
        middle_ref,
        attended_ref,
        proj_ref,
        halo_ref,
        totals_ref,
        normed_ref,
        resid_ref,
        qkv_own,
        qkv_other,
        out_own,
        out_other,
        up_own,
        up_other,
        down_own,
        down_other,
        grad_in_ref,
        out_down,
        out_up,
        out_out,
        out_qkv,
        vector_out,
        grad_branch,
        grad_attn,
        grad_before,
        grad_proj,
        grad_res,
        collected,
        grad_attended,
        qkv_buf,
        halo_buf,
        totals_buf,
        kept_kv,
        halo_send,
        halo_in,
        rows_weight,
        columns_weight,
        slope_buf,
        wide_buf,
        bias_buf,
        sums_buf,
        pair_buf,
        one_buf,
        part_buf,
        core_in,
        own_kept,
        other_kept,
        y_in,
        x_kept,
        x_out,
        x_in,
        z_kept,
        outer_in,
        inner_in,
        result,
        vec_in,
        load_sem,
        io_sem,
        halo_send_sem,
        halo_recv_sem,
        staged_sem,
        send_sems,
        recv_sems,
        store_sem,
        vec_send,
        vec_recv,
    ) = refs
    half, quarter = block // 2, block // 4
    width = 2 * block
    rows_all = grad_branch.shape[0]
    pairs_half = block // LANES
    pairs = 2 * pairs_half
    low = jnp.bfloat16
    place = lax.axis_index("dp")
    y = lax.axis_index("tensor")
    core = place % 2
    x = (place // 2) % 2
    z = place // 4
    z_low = z % 2
    inner = (z + 1) // 2 % 2
    core_partner = {"dp": place + 1 - 2 * core, "tensor": y}
    x_partner = {"dp": place + 2 - 4 * x, "tensor": y}
    y_partner = {"dp": place, "tensor": 1 - y}
    z_partner = {"dp": place + 4 - 8 * z_low, "tensor": y}
    middle_partner = {"dp": place + 4 * (3 - 2 * z), "tensor": y}

    barrier = pltpu.get_barrier_semaphore()
    for partner in (core_partner, x_partner, y_partner, z_partner):
        pl.semaphore_signal(barrier, inc=1, device_id=partner, device_id_type=MESH)

    @pl.when(inner == 1)
    def _():
        pl.semaphore_signal(barrier, inc=1, device_id=middle_partner, device_id_type=MESH)
        pl.semaphore_wait(barrier, 5)

    @pl.when(inner == 0)
    def _():
        pl.semaphore_wait(barrier, 4)

    blocks_hidden = hidden_half // block
    plan = (
        ("rows", blocks_hidden, 2),
        ("columns", 2, blocks_hidden),
        ("rows", 1, 2),
        ("columns", 2, 3),
    )
    starts = []
    per_layer = 0
    for _, down_count, across_count in plan:
        starts.append(per_layer)
        per_layer += down_count * across_count
    chunks = layers * per_layer
    out_refs = (out_down, out_up, out_out, out_qkv)

    def block_of(index):
        return pl.ds(pl.multiple_of(index * block, block), block)

    def for_matrix(chunk, action):
        layer = layers - 1 - chunk // per_layer
        inside = chunk % per_layer
        for member, (_, down_count, across_count) in enumerate(plan):
            begin = starts[member]

            @pl.when((inside >= begin) & (inside < begin + down_count * across_count))
            def _(member=member, begin=begin, across_count=across_count):
                local = inside - begin
                action(member, layer, local // across_count, local % across_count)

    def operands_of(member, layer, i, j):
        if member == 0:
            return (
                grad_branch.at[:, block_of(j)],
                act_ref.at[layer, 0, :, block_of(i)],
                act_ref.at[layer, 1, :, block_of(i)],
            )
        if member == 1:
            return (
                normed_two_ref.at[layer, :, block_of(i)],
                grad_before.at[j // 2, :, block_of(j % 2)],
                grad_before.at[blocks_hidden // 2 + j // 2, :, block_of(j % 2)],
            )
        if member == 2:
            return (
                grad_attn.at[:, block_of(j)],
                attended_ref.at[layer, 0, :, block_of(i)],
                attended_ref.at[layer, 1, :, block_of(i)],
            )
        return (
            normed_ref.at[layer, :, block_of(i)],
            grad_proj.at[:, block_of(j)],
            grad_proj.at[:, block_of(3 + j)],
        )

    def staged_copies(chunk, shared, own, other):
        slot = chunk % STAGED
        return (
            pltpu.make_async_copy(own, pair_buf.at[slot, 0], staged_sem.at[slot, 0]),
            pltpu.make_async_copy(other, pair_buf.at[slot, 1], staged_sem.at[slot, 1]),
            pltpu.make_async_copy(shared, one_buf.at[slot], staged_sem.at[slot, 2]),
        )

    def stage_operands(chunk):
        def action(member, layer, i, j):
            for copy in staged_copies(chunk, *operands_of(member, layer, i, j)):
                copy.start()

        for_matrix(chunk, action)

    def remote(step, chunk, source, target, partner):
        slot = chunk % SLOTS
        return pltpu.make_async_remote_copy(
            src_ref=source,
            dst_ref=target,
            send_sem=send_sems.at[step, slot],
            recv_sem=recv_sems.at[step, slot],
            device_id=partner,
            device_id_type=MESH,
        )

    def rows_at(index, size):
        return pl.ds(pl.multiple_of(index * size, size), size)

    def core_copy(chunk):
        return remote(
            0,
            chunk,
            part_buf.at[chunk % STAGED, :, rows_at(1 - core, half)],
            core_in.at[chunk % CORE_SLOTS],
            core_partner,
        )

    def y_copy(chunk):
        slot = chunk % SLOTS
        return remote(1, chunk, other_kept.at[slot], y_in.at[slot], y_partner)

    def x_copy(chunk):
        slot = chunk % SLOTS
        return remote(2, chunk, x_out.at[slot], x_in.at[slot], x_partner)

    def outer_copy(chunk):
        slot = chunk % SLOTS
        return remote(3, chunk, z_kept.at[slot], outer_in.at[slot], z_partner)

    def inner_copy(chunk):
        slot = chunk % SLOTS
        return remote(4, chunk, z_kept.at[slot], inner_in.at[slot], middle_partner)

    own_rows = rows_at(2 * core + x, quarter)

    def back_copy(chunk):
        piece = result.at[chunk % RESULT_SLOTS, own_rows]
        return remote(5, chunk, piece, piece, z_partner)

    def gather_copy(chunk):
        piece = result.at[chunk % RESULT_SLOTS, own_rows]
        return remote(6, chunk, piece, piece, x_partner)

    def whole_copy(chunk):
        piece = result.at[chunk % RESULT_SLOTS, rows_at(core, half)]
        return remote(7, chunk, piece, piece, core_partner)

    def store_copy(chunk, target):
        slot = chunk % RESULT_SLOTS
        return pltpu.make_async_copy(result.at[slot], target, store_sem.at[slot])

    def multiply(chunk):
        slot = chunk % STAGED
        for copy in staged_copies(chunk, one_buf.at[slot], pair_buf.at[slot, 0], pair_buf.at[slot, 1]):
            copy.wait()
        inside = chunk % per_layer
        by_rows = (inside < starts[1]) | ((inside >= starts[2]) & (inside < starts[3]))

        @pl.when(by_rows)
        def _():
            single = one_buf[slot]
            for which in range(2):
                part_buf[slot, which] = dot_tn(pair_buf[slot, which], single).astype(low)

        @pl.when(jnp.logical_not(by_rows))
        def _():
            single = one_buf[slot]
            for which in range(2):
                part_buf[slot, which] = dot_tn(single, pair_buf[slot, which]).astype(low)

        core_copy(chunk).start()

    def after_core(chunk):
        slot = chunk % SLOTS
        core_copy(chunk).wait()
        mine = rows_at(core, half)
        other_kept[slot] = added(part_buf[chunk % STAGED, 1, mine, :], core_in[chunk % CORE_SLOTS, 1])
        y_copy(chunk).start()
        own_kept[slot] = added(part_buf[chunk % STAGED, 0, mine, :], core_in[chunk % CORE_SLOTS, 0])

    def after_y(chunk):
        slot = chunk % SLOTS
        y_copy(chunk).wait()
        away, here = rows_at(1 - x, quarter), rows_at(x, quarter)
        x_out[slot] = added(own_kept[slot, away, :], y_in[slot, away, :])
        x_copy(chunk).start()
        x_kept[slot] = added(own_kept[slot, here, :], y_in[slot, here, :])

    def after_x(chunk):
        slot = chunk % SLOTS
        x_copy(chunk).wait()
        z_kept[slot] = added(x_kept[slot], x_in[slot])

        @pl.when(inner == 0)
        def _():
            outer_copy(chunk).start()

    def after_outer(chunk):
        slot = chunk % SLOTS

        @pl.when(inner == 0)
        def _():
            outer_copy(chunk).wait_send()

        @pl.when(inner == 1)
        def _():
            outer_copy(chunk).wait_recv()
            z_kept[slot] = added(z_kept[slot], outer_in[slot])
            inner_copy(chunk).start()

    def after_inner(chunk):
        slot = chunk % SLOTS

        @pl.when(inner == 1)
        def _():
            inner_copy(chunk).wait()
            result[chunk % RESULT_SLOTS, own_rows, :] = added(z_kept[slot], inner_in[slot])
            back_copy(chunk).start()

    def after_back(chunk):
        @pl.when(inner == 0)
        def _():
            back_copy(chunk).wait_recv()

        @pl.when(inner == 1)
        def _():
            back_copy(chunk).wait_send()

        gather_copy(chunk).start()

    def after_gather(chunk):
        gather_copy(chunk).wait()
        whole_copy(chunk).start()

    def after_whole(chunk):
        whole_copy(chunk).wait()

        def action(member, layer, i, j):
            store_copy(chunk, out_refs[member].at[layer, block_of(i), block_of(j)]).start()

        for_matrix(chunk, action)

    def after_store(chunk):
        store_copy(chunk, result.at[chunk % RESULT_SLOTS]).wait()

    vector_partners = (core_partner, y_partner, x_partner, z_partner, middle_partner, z_partner)

    def vector_copy(step):
        target = vector_out if step == 5 else vec_in.at[step]
        return pltpu.make_async_remote_copy(
            src_ref=vector_out,
            dst_ref=target,
            send_sem=vec_send.at[step],
            recv_sem=vec_recv.at[step],
            device_id=vector_partners[step],
            device_id_type=MESH,
        )

    def add_vector(step):
        vector_out[...] = vector_out[...] + vec_in[step]

    def vector_tick(step):
        if step == 0:
            vector_copy(0).start()
        elif step <= 3:
            vector_copy(step - 1).wait()
            add_vector(step - 1)
            if step < 3:
                vector_copy(step).start()
            else:

                @pl.when(inner == 0)
                def _():
                    vector_copy(3).start()

        elif step == 4:

            @pl.when(inner == 0)
            def _():
                vector_copy(3).wait_send()

            @pl.when(inner == 1)
            def _():
                vector_copy(3).wait_recv()
                add_vector(3)
                vector_copy(4).start()

        elif step == 5:

            @pl.when(inner == 1)
            def _():
                vector_copy(4).wait()
                add_vector(4)
                vector_copy(5).start()

        else:

            @pl.when(inner == 1)
            def _():
                vector_copy(5).wait_send()

            @pl.when(inner == 0)
            def _():
                vector_copy(5).wait_recv()

    norm_two_step = FFN_STEPS
    out_step = norm_two_step + 1
    attention_step = out_step + 1
    qkv_step = attention_step + pairs + 1
    norm_one_step = qkv_step + QKV_STEPS
    period = norm_one_step + 1
    jobs = layers * period
    hidden_step = 2 * hidden_half // FFN_STEPS

    def loads(kind, slot, *sources):
        targets = {
            "ffn": (rows_weight.at[slot], columns_weight.at[slot], slope_buf.at[slot]),
            "wide": (wide_buf,),
            "out": (rows_weight.at[slot, pl.ds(0, block)], rows_weight.at[slot, pl.ds(block, block)]),
            "attention": (
                qkv_buf.at[slot, 0],
                qkv_buf.at[slot, 1],
                qkv_buf.at[slot, 2],
                halo_buf.at[slot, 0],
                halo_buf.at[slot, 1],
                totals_buf.at[slot],
            ),
            "qkv": (
                columns_weight.at[slot, :, pl.ds(0, block)],
                columns_weight.at[slot, :, pl.ds(block, block)],
            ),
        }[kind]
        sources = sources or targets
        return [
            pltpu.make_async_copy(source, target, load_sem.at[slot, index])
            for index, (source, target) in enumerate(zip(sources, targets))
        ]

    def prefetch(t):
        slot = t % 2
        layer = layers - 1 - t // period
        step = t % period

        for which, (up_ref, down_ref) in enumerate(((up_own, down_own), (up_other, down_other))):

            @pl.when((step < FFN_STEPS) & (step // (FFN_STEPS // 2) == which))
            def _(which=which, up_ref=up_ref, down_ref=down_ref):
                cut = rows_at(step % (FFN_STEPS // 2), hidden_step)
                for copy in loads(
                    "ffn",
                    slot,
                    down_ref.at[layer, cut, :],
                    up_ref.at[layer, :, cut],
                    slope_ref.at[layer, which, :, cut],
                ):
                    copy.start()

        for at, source in ((norm_two_step, middle_ref), (norm_one_step, resid_ref)):

            @pl.when(step == at)
            def _(source=source):
                for copy in loads("wide", slot, source.at[layer]):
                    copy.start()

        @pl.when(step == out_step)
        def _():
            for copy in loads("out", slot, out_own.at[layer], out_other.at[layer]):
                copy.start()

        @pl.when((step >= attention_step) & (step < attention_step + pairs))
        def _():
            pair = step - attention_step
            which, inside = pair // pairs_half, pair % pairs_half

            def lanes(third):
                return rows_at(third * pairs_half + inside, LANES)

            for copy in loads(
                "attention",
                slot,
                *[proj_ref.at[layer, which, :, lanes(third)] for third in range(3)],
                *[halo_ref.at[layer, which, :, lanes(third)] for third in range(2)],
                totals_ref.at[layer, which],
            ):
                copy.start()

        @pl.when((step >= qkv_step) & (step < qkv_step + QKV_STEPS))
        def _():
            for part in range(2):
                index = 2 * (step - qkv_step) + part
                for which, source in enumerate((qkv_own, qkv_other)):

                    @pl.when(index // 3 == which)
                    def _(part=part, index=index, source=source):
                        pltpu.make_async_copy(
                            source.at[layer, :, block_of(index % 3)],
                            columns_weight.at[slot, :, pl.ds(part * block, block)],
                            load_sem.at[slot, part],
                        ).start()

    def wait_loads(kind, slot):
        for copy in loads(kind, slot):
            copy.wait()

    tiles = [slice(r, r + BAND) for r in range(0, rows_all, BAND)]
    fine_tiles = [slice(r, r + LANES) for r in range(0, rows_all, LANES)]

    def vector_row(layer, row):
        return pl.ds(layer * VECTOR_ROWS + row, 1)

    def column_sum(values):
        return jnp.sum(values.astype(jnp.float32), axis=0, keepdims=True)

    def ffn_job(layer, step, slot):
        wait_loads("ffn", slot)
        sums = 0.0
        for tile in tiles:
            grad_hidden = dot_nt(grad_branch[tile, :], rows_weight[slot])
            before = (grad_hidden * slope_buf[slot, tile, :].astype(jnp.float32)).astype(low)
            grad_before[step, tile, :] = before
            sums = sums + column_sum(before)
            product = dot_nt(before, columns_weight[slot])

            @pl.when(step == 0)
            def _(tile=tile, product=product):
                collected[tile, :] = product

            @pl.when(step > 0)
            def _(tile=tile, product=product):
                collected[tile, :] = collected[tile, :] + product

        per_half = FFN_STEPS // 2
        which = step // per_half
        owner = which + y - 2 * which * y
        vector_out[vector_row(layer, 2 + owner * per_half + step % per_half), :] = sums

    def norm_job(layer, index, slot):
        wait_loads("wide", slot)
        gain = gain_ref[pl.ds(2 * layer + index, 1), :]
        gain_sum, shift_sum, attn_sum, branch_sum = 0.0, 0.0, 0.0, 0.0
        for tile in fine_tiles:
            incoming = collected[tile, :]
            values = wide_buf[tile, :]
            average = jnp.mean(values, axis=-1, keepdims=True)
            centred = values - average
            inverse = lax.rsqrt(jnp.mean(centred * centred, axis=-1, keepdims=True) + epsilon)
            unit = centred * inverse
            scaled = incoming * gain
            first_mean = jnp.mean(scaled, axis=-1, keepdims=True)
            second_mean = jnp.mean(scaled * unit, axis=-1, keepdims=True)
            total = grad_res[tile, :] + inverse * (scaled - first_mean - unit * second_mean)
            grad_res[tile, :] = total
            rounded = total.astype(low)
            gain_sum = gain_sum + column_sum(incoming * unit)
            shift_sum = shift_sum + column_sum(incoming)
            if index == 1:
                attn_sum = attn_sum + column_sum(rounded)
                branch_sum = branch_sum + column_sum(grad_branch[tile, :])
                grad_attn[tile, :] = rounded
            else:
                grad_branch[tile, :] = rounded
        vector_out[vector_row(layer, 8 + index), :] = gain_sum
        vector_out[vector_row(layer, 10 + index), :] = shift_sum
        if index == 1:
            vector_out[vector_row(layer, 6), :] = attn_sum
            vector_out[vector_row(layer, 7), :] = branch_sum

    def out_job(slot):
        wait_loads("out", slot)
        for tile in tiles:
            grad_attended[tile, :] = dot_nt(grad_attn[tile, :], rows_weight[slot]).astype(low)

    def halo_copy(pair):
        return pltpu.make_async_remote_copy(
            src_ref=halo_send.at[pair % 2],
            dst_ref=halo_in.at[pair],
            send_sem=halo_send_sem.at[pair],
            recv_sem=halo_recv_sem.at[pair],
            device_id=core_partner,
            device_id_type=MESH,
        )

    def proj_lanes(pair, third):
        which, inside = pair // pairs_half, pair % pairs_half
        return rows_at(which * 3 * pairs_half + third * pairs_half + inside, LANES)

    def attention_job(pair, slot):
        wait_loads("attention", slot)
        lane = lax.broadcasted_iota(jnp.int32, (BAND, LANES), 1)
        scaling = HEAD_DIM ** (-0.5)
        count = len(tiles)
        key_parts = [None] * (count + 1)
        value_parts = [None] * (count + 1)
        here = rows_at(pair, LANES)
        for index, tile in enumerate(tiles):
            query = qkv_buf[slot, 0, tile, :]
            grad = grad_attended[tile, here]
            keys = band_rows(halo_buf.at[slot, 0], qkv_buf.at[slot, 1], index)
            values = band_rows(halo_buf.at[slot, 1], qkv_buf.at[slot, 2], index)
            grad_query = []
            grad_keys = 0.0
            grad_values = 0.0
            for head in range(2):
                mine = (lane // HEAD_DIM) == head
                query_head = jnp.where(mine, query, 0)
                grad_head = jnp.where(mine, grad, 0)
                scores = dot_nt(query_head, keys) * scaling + bias_buf[index]
                total = jnp.sum(
                    jnp.where(
                        lane == 2 * (pair % pairs_half) + head, totals_buf[slot, tile, :], 0.0
                    ),
                    axis=-1,
                    keepdims=True,
                )
                exact = jnp.exp(scores - total)
                grad_probs = dot_nt(grad_head, values)
                row_terms = jnp.sum(exact * grad_probs, axis=-1, keepdims=True)
                grad_scores = (exact * (grad_probs - row_terms)).astype(low)
                grad_query.append(jnp.dot(grad_scores, keys, preferred_element_type=jnp.float32))
                grad_keys = grad_keys + dot_tn(grad_scores, query_head)
                grad_values = grad_values + dot_tn(exact.astype(low), grad_head)
            grad_proj[tile, proj_lanes(pair, 0)] = (
                jnp.where(lane < HEAD_DIM, grad_query[0], grad_query[1]) * scaling
            ).astype(low)
            grad_keys = grad_keys * scaling
            for part in range(2):
                cut = slice(part * BAND, (part + 1) * BAND)
                old_k, old_v = key_parts[index + part], value_parts[index + part]
                key_parts[index + part] = grad_keys[cut] if old_k is None else old_k + grad_keys[cut]
                value_parts[index + part] = (
                    grad_values[cut] if old_v is None else old_v + grad_values[cut]
                )
        for index in range(count - 1):
            grad_proj[tiles[index], proj_lanes(pair, 1)] = key_parts[index + 1].astype(low)
            grad_proj[tiles[index], proj_lanes(pair, 2)] = value_parts[index + 1].astype(low)
        kept_kv[pair % 2, 0] = key_parts[count]
        kept_kv[pair % 2, 1] = value_parts[count]

        @pl.when(core == 1)
        def _():
            halo_send[pair % 2, 0] = key_parts[0].astype(low)
            halo_send[pair % 2, 1] = value_parts[0].astype(low)
            halo_copy(pair).start()

    def finish_pair(pair):
        last = tiles[-1]

        @pl.when(core == 0)
        def _():
            halo_copy(pair).wait_recv()
            for third in range(2):
                grad_proj[last, proj_lanes(pair, third + 1)] = (
                    kept_kv[pair % 2, third] + halo_in[pair, third].astype(jnp.float32)
                ).astype(low)

        @pl.when(core == 1)
        def _():
            halo_copy(pair).wait_send()
            for third in range(2):
                grad_proj[last, proj_lanes(pair, third + 1)] = kept_kv[pair % 2, third].astype(low)

    def qkv_job(layer, step, slot):
        wait_loads("qkv", slot)
        sums = 0.0
        for tile in tiles:
            grad = grad_proj[tile, rows_at(step, width)]
            sums = sums + column_sum(grad)
            product = dot_nt(grad, columns_weight[slot])

            @pl.when(step == 0)
            def _(tile=tile, product=product):
                collected[tile, :] = product

            @pl.when(step > 0)
            def _(tile=tile, product=product):
                collected[tile, :] = collected[tile, :] + product

        sums_buf[...] = sums
        for when, part, which, row in ((0, 0, 0, 0), (1, 0, 0, 1), (1, 1, 1, 0), (2, 1, 1, 1)):

            @pl.when(step == when)
            def _(part=part, which=which, row=row):
                owner = 1 - y if which else y
                vector_out[vector_row(layer, row), block_of(owner)] = sums_buf[
                    :, part * block : (part + 1) * block
                ]

    def job(t):
        slot = t % 2
        layer = layers - 1 - t // period
        step = t % period

        @pl.when(step < FFN_STEPS)
        def _():
            ffn_job(layer, step, slot)

        @pl.when(step == norm_two_step)
        def _():
            norm_job(layer, 1, slot)

        @pl.when(step == out_step)
        def _():
            out_job(slot)

        @pl.when((step > attention_step) & (step <= attention_step + pairs))
        def _():
            finish_pair(step - attention_step - 1)

        @pl.when((step >= attention_step) & (step < attention_step + pairs))
        def _():
            attention_job(step - attention_step, slot)

        @pl.when((step >= qkv_step) & (step < qkv_step + QKV_STEPS))
        def _():
            qkv_job(layer, step - qkv_step, slot)

        @pl.when(step == norm_one_step)
        def _():
            norm_job(layer, 0, slot)

    stages = (
        (LAGS["core"], after_core),
        (0, multiply),
        (None, job),
        (LAGS["y"], after_y),
        (LAGS["x"], after_x),
        (LAGS["outer"], after_outer),
        (LAGS["inner"], after_inner),
        (LAGS["back"], after_back),
        (LAGS["gather"], after_gather),
        (LAGS["stored"], after_store),
        (LAGS["whole"], after_whole),
    )

    first_load = pltpu.make_async_copy(cot_ref, grad_branch, io_sem.at[0])
    first_load.start()
    prefetch(0)
    fill_band_bias(segq_ref, segk_ref, bias_buf)
    first_load.wait()
    for tile in tiles:
        grad_res[tile, :] = grad_branch[tile, :].astype(jnp.float32)
    vector_ticks = [jobs + VECTOR_STEP * step for step in range(7)]

    def tick(t, carry):
        @pl.when(t + 1 < jobs)
        def _():
            prefetch(t + 1)

        ahead = t + 1 - FIRST

        @pl.when((ahead >= 0) & (ahead < chunks))
        def _():
            stage_operands(ahead)

        for lag, action in stages:
            if lag is None:

                @pl.when(t < jobs)
                def _():
                    job(t)

                continue
            chunk = t - FIRST - lag

            @pl.when((chunk >= 0) & (chunk < chunks))
            def _(chunk=chunk, action=action):
                action(chunk)

        for step, when in enumerate(vector_ticks):

            @pl.when(t == when)
            def _(step=step):
                vector_tick(step)

        return carry

    lax.fori_loop(0, max(chunks + FIRST + LAGS["stored"], vector_ticks[-1] + 1), tick, 0)
    last_store = pltpu.make_async_copy(grad_branch, grad_in_ref, io_sem.at[1])
    last_store.start()
    last_store.wait()


def run_backward(cotangent, gain, segq, segk, saved, weights, block):
    rows, width = cotangent.shape
    layers, hidden_half = weights[-1].shape[0], weights[-1].shape[1]
    half, quarter = block // 2, block // 4
    low, wide = jnp.bfloat16, jnp.float32
    pairs = width // LANES
    anywhere = pl.BlockSpec(memory_space=pl.ANY)
    in_vmem = pl.BlockSpec(memory_space=pltpu.VMEM)
    vector = (layers * VECTOR_ROWS, width)
    hidden_step = 2 * hidden_half // FFN_STEPS
    vmem = pltpu.VMEM
    return pl.pallas_call(
        functools.partial(backward_kernel, layers, block, hidden_half),
        in_specs=[anywhere] + [in_vmem] * 3 + [anywhere] * (len(saved) + len(weights)),
        out_specs=[anywhere] * 5 + [in_vmem],
        out_shape=[
            jax.ShapeDtypeStruct((rows, width), low),
            jax.ShapeDtypeStruct((layers, hidden_half, width), low),
            jax.ShapeDtypeStruct((layers, width, hidden_half), low),
            jax.ShapeDtypeStruct((layers, block, width), low),
            jax.ShapeDtypeStruct((layers, width, 3 * block), low),
            jax.ShapeDtypeStruct(vector, wide),
        ],
        scratch_shapes=[
            vmem((rows, width), low),
            vmem((rows, width), low),
            vmem((FFN_STEPS, rows, hidden_step), low),
            vmem((rows, 6 * block), low),
            vmem((rows, width), wide),
            vmem((rows, width), wide),
            vmem((rows, width), low),
            vmem((2, 3, rows, LANES), low),
            vmem((2, 2, BAND, LANES), low),
            vmem((2, rows, LANES), wide),
            vmem((2, 2, BAND, LANES), wide),
            vmem((2, 2, BAND, LANES), low),
            vmem((pairs, 2, BAND, LANES), low),
            vmem((2, hidden_step, width), low),
            vmem((2, width, hidden_step), low),
            vmem((2, rows, hidden_step), low),
            vmem((rows, width), wide),
            vmem((rows // BAND, BAND, 2 * BAND), wide),
            vmem((1, width), wide),
            vmem((STAGED, 2, rows, block), low),
            vmem((STAGED, rows, block), low),
            vmem((STAGED, 2, block, block), low),
            vmem((CORE_SLOTS, 2, half, block), low),
            vmem((SLOTS, half, block), low),
            vmem((SLOTS, half, block), low),
            vmem((SLOTS, half, block), low),
            vmem((SLOTS, quarter, block), low),
            vmem((SLOTS, quarter, block), low),
            vmem((SLOTS, quarter, block), low),
            vmem((SLOTS, quarter, block), low),
            vmem((SLOTS, quarter, block), low),
            vmem((SLOTS, quarter, block), low),
            vmem((RESULT_SLOTS, block, block), low),
            vmem((5,) + vector, wide),
            pltpu.SemaphoreType.DMA((2, 6)),
            pltpu.SemaphoreType.DMA((2,)),
            pltpu.SemaphoreType.DMA((pairs,)),
            pltpu.SemaphoreType.DMA((pairs,)),
            pltpu.SemaphoreType.DMA((STAGED, 3)),
            pltpu.SemaphoreType.DMA((8, SLOTS)),
            pltpu.SemaphoreType.DMA((8, SLOTS)),
            pltpu.SemaphoreType.DMA((RESULT_SLOTS,)),
            pltpu.SemaphoreType.DMA((6,)),
            pltpu.SemaphoreType.DMA((6,)),
        ],
        compiler_params=pltpu.CompilerParams(
            collective_id=0, has_side_effects=True, vmem_limit_bytes=VMEM_ASKED
        ),
        name="backward",
    )(cotangent, gain, segq, segk, *saved, *weights)


def dot_low(left, right):
    return jnp.dot(left, right, preferred_element_type=jnp.float32)


def local_split(
    tokens_in,
    segments,
    w_qkv,
    qv_bias,
    w_out,
    w_up,
    up_bias,
    w_down,
    out_bias,
    ln_gain,
    ln_bias,
    cotangent,
):
    layers, width = w_qkv.shape[0], w_qkv.shape[1]
    rows = tokens_in.shape[0]
    place = lax.axis_index("dp")
    y = lax.axis_index("tensor")
    core, x = place % 2, (place // 2) % 2
    hops = [(X_BIT, x), (CORE_BIT, core)]

    residual = swap_windows(tokens_in).astype(jnp.float32)
    grad_residual = swap_windows(cotangent)
    window_segments = jnp.where(core == y, segments, swap_dp(segments, CORE_BIT))
    own_segments = lax.dynamic_slice_in_dim(window_segments, core * rows, rows, axis=1)
    halo_segments = jnp.where(core == 1, window_segments[:, rows - BAND : rows], -1)
    segq = own_segments.reshape(rows, 1)
    segk = jnp.concatenate([halo_segments, own_segments], axis=1)

    qkv_rows = [w_qkv[l].reshape(width, -1) for l in range(layers)]
    weights = []
    for l in range(layers):
        own = (qkv_rows[l], w_out[l], w_up[l], w_down[l])
        other = tuple(other_half(member, hops) for member in own)
        bias_own = (qv_bias[l].reshape(-1), up_bias[l])
        bias_other = tuple(swap_y(member) for member in bias_own)
        weights.append(tuple(zip(own + bias_own, other + bias_other)))

    kept = []
    count = lax.axis_size("dp")
    to_second = [(2 * i, 2 * i + 1) for i in range(count // 2)]
    to_first = [(2 * i + 1, 2 * i) for i in range(count // 2)]
    for l in range(layers):
        qkv, out_w, up, down, qv, upb = weights[l]
        normed, _, _ = layer_norm(residual, ln_gain[l, 0], ln_bias[l, 0])
        normed = normed.astype(jnp.bfloat16)
        saved_attention = []
        branch = 0.0
        for half in range(2):
            third = qkv[half].shape[1] // 3
            bias = jnp.concatenate(
                [qv[half][:third], jnp.zeros((third,), jnp.float32), qv[half][third:]]
            )
            projected = (dot_low(normed, qkv[half]) + bias).astype(jnp.bfloat16)
            halo = lax.ppermute(projected[rows - BAND :, third:], "dp", to_second)
            attended, totals = attention_forward(projected, halo, segq, segk)
            branch = branch + dot_low(attended, out_w[half])
            saved_attention.append((projected, halo, attended, totals))
        middle = residual + branch + out_bias[l, 0]
        normed_two, _, _ = layer_norm(middle, ln_gain[l, 1], ln_bias[l, 1])
        normed_two = normed_two.astype(jnp.bfloat16)
        saved_ffn = []
        branch = 0.0
        for half in range(2):
            before = dot_low(normed_two, up[half]) + upb[half]
            activated = gelu_tanh(before).astype(jnp.bfloat16)
            slope = gelu_slope(before).astype(jnp.bfloat16)
            branch = branch + dot_low(activated, down[half])
            saved_ffn.append((activated, slope))
        kept.append((residual, normed, saved_attention, middle, normed_two, saved_ffn))
        residual = middle + branch + out_bias[l, 1]
    out_act = swap_windows(residual.astype(jnp.bfloat16))

    def stacked(pick):
        return jnp.stack([pick(kept[l]) for l in range(layers)])

    def stacked_halves(group, member):
        return jnp.stack(
            [jnp.stack([kept[l][group][half][member] for half in range(2)]) for l in range(layers)]
        )

    saved = (
        stacked_halves(5, 0),
        stacked_halves(5, 1),
        stacked(lambda state: state[4]),
        stacked(lambda state: state[3]),
        stacked_halves(2, 2),
        stacked_halves(2, 0),
        stacked_halves(2, 1),
        stacked_halves(2, 3),
        stacked(lambda state: state[1]),
        stacked(lambda state: state[0]),
    )
    both = []
    for member in range(4):
        for half in range(2):
            both.append(jnp.stack([weights[l][member][half] for l in range(layers)]))
    grad_in, *reduced, summed = run_backward(
        grad_residual, ln_gain.reshape(-1, width), segq, segk, saved, both, width // 2
    )
    grad_in = swap_windows(grad_in)
    summed = summed.reshape(layers, -1)
    hidden = 2 * up_bias.shape[1]
    ends = [2 * width, 2 * width + hidden, 4 * width + hidden, 6 * width + hidden]
    qv_sum = summed[:, : ends[0]].reshape(layers, 2, width)
    grad_qv_bias = lax.dynamic_slice_in_dim(qv_sum, y * (width // 2), width // 2, axis=2)
    grad_up_bias = lax.dynamic_slice_in_dim(
        summed[:, ends[0] : ends[1]], y * (hidden // 2), hidden // 2, axis=1
    )
    grad_down, grad_up, grad_out, grad_qkv = [member.astype(jnp.float32) for member in reduced]
    return (
        out_act,
        grad_in,
        grad_qkv.reshape(w_qkv.shape),
        grad_qv_bias,
        grad_out,
        grad_up,
        grad_up_bias,
        grad_down,
        summed[:, ends[1] : ends[2]].reshape(layers, 2, width),
        summed[:, ends[2] : ends[3]].reshape(layers, 2, width),
        summed[:, ends[3] :].reshape(layers, 2, width),
    )


def solution(mesh):
    sizes = (mesh.shape["dp"], mesh.shape["tensor"])
    local = local_split if sizes == (16, 2) else local_general
    return jax.shard_map(
        local,
        mesh=mesh,
        in_specs=(
            P(("dp", "tensor"), None),
            P("dp", None),
            P(None, None, None, "tensor"),
            P(None, None, "tensor"),
            P(None, "tensor", None),
            P(None, None, "tensor"),
            P(None, "tensor"),
            P(None, "tensor", None),
            P(),
            P(),
            P(),
            P(("dp", "tensor"), None),
        ),
        out_specs=(
            P(("dp", "tensor"), None),
            P(("dp", "tensor"), None),
            P(None, None, None, "tensor"),
            P(None, None, "tensor"),
            P(None, "tensor", None),
            P(None, None, "tensor"),
            P(None, "tensor"),
            P(None, "tensor", None),
            P(),
            P(),
            P(),
        ),
        check_vma=False,
    )
```

```python
import functools

import jax
import jax.numpy as jnp
from jax import lax
from jax.experimental import pallas as pl
from jax.experimental.pallas import tpu as pltpu
from jax.sharding import PartitionSpec as P

HEAD_DIM = 64


epsilon = 1e-05
gelu_coeff = 0.7978845608028654
cubic_coeff = 0.044715
masked_score = -1e30


def as_sent(shard):

    def short(part):
        return part.astype(jnp.bfloat16) if part.dtype == jnp.float32 else part

    return jax.tree.map(short, shard)


def layer_norm(values, gain, shift):
    average = jnp.mean(values, axis=-1, keepdims=True)
    centred = values - average
    inverse = lax.rsqrt(jnp.mean(centred * centred, axis=-1, keepdims=True) + epsilon)
    unit_rows = centred * inverse
    return (unit_rows * gain + shift, unit_rows, inverse)


def norm_backward(incoming, unit_rows, inverse, gain):
    scaled = incoming * gain
    first_mean = jnp.mean(scaled, axis=-1, keepdims=True)
    second_mean = jnp.mean(scaled * unit_rows, axis=-1, keepdims=True)
    through = inverse * (scaled - first_mean - unit_rows * second_mean)
    return (through, jnp.sum(incoming * unit_rows, axis=0), jnp.sum(incoming, axis=0))


def gelu_tanh(before):
    tanh_input = gelu_coeff * (before + cubic_coeff * before * before * before)
    return 0.5 * before * (1.0 + jnp.tanh(tanh_input))


def gelu_slope(before):
    tanh_input = gelu_coeff * (before + cubic_coeff * before * before * before)
    tangent = jnp.tanh(tanh_input)
    return 0.5 * (1.0 + tangent) + 0.5 * before * (1.0 - tangent * tangent) * gelu_coeff * (
        1.0 + 3.0 * cubic_coeff * before * before
    )


def masked_scores(query_block, key_seq, segment_row, offset, block_rows):
    window = key_seq.shape[0]
    scores = jnp.einsum(
        "qhe,khe->hqk", query_block, key_seq, preferred_element_type=jnp.float32
    ) * HEAD_DIM ** (-0.5)
    query_place = offset + lax.iota(jnp.int32, block_rows)
    key_place = lax.iota(jnp.int32, window)
    query_segment = segment_row[offset : offset + block_rows]
    allowed = (query_place[:, None] >= key_place[None, :]) & (
        query_segment[:, None] == segment_row[None, :]
    )
    return jnp.where(allowed[None], scores, masked_score)


def split_heads(flat_rows, seq_count):
    return flat_rows.reshape(
        seq_count, flat_rows.shape[0] // seq_count, flat_rows.shape[1] // HEAD_DIM, HEAD_DIM
    )


def attend_forward(query_rows, key_rows, value_rows, segments):
    seq_count, window = segments.shape
    block_rows = min(512, window)

    def one_sequence(member):
        query_seq, key_seq, value_seq, segment_row = member
        outputs = []
        totals = []
        for block_index in range(window // block_rows):
            offset = block_index * block_rows
            scores = masked_scores(
                query_seq[offset : offset + block_rows], key_seq, segment_row, offset, block_rows
            )
            highest = jnp.max(scores, axis=-1, keepdims=True)
            raised = jnp.exp(scores - highest)
            summed = jnp.sum(raised, axis=-1, keepdims=True)
            softmax_low = (raised / summed).astype(jnp.bfloat16)
            block_out = jnp.einsum(
                "hqk,khe->qhe", softmax_low, value_seq, preferred_element_type=jnp.float32
            )
            outputs.append(block_out.astype(jnp.bfloat16))
            totals.append(highest[..., 0] + jnp.log(summed[..., 0]))
        return (jnp.concatenate(outputs, axis=0), jnp.stack(totals, axis=0))

    attended, log_totals = lax.map(
        one_sequence,
        (
            split_heads(query_rows, seq_count),
            split_heads(key_rows, seq_count),
            split_heads(value_rows, seq_count),
            segments,
        ),
    )
    return (attended.reshape(query_rows.shape), log_totals)


def attend_backward(query_rows, key_rows, value_rows, segments, log_totals, grad_attended):
    seq_count, window = segments.shape
    block_rows = min(512, window)
    scaling = HEAD_DIM ** (-0.5)

    def one_sequence(member):
        query_seq, key_seq, value_seq, segment_row, totals_seq, grad_seq = member
        query_parts = []
        grad_keys = jnp.zeros(key_seq.shape, jnp.float32)
        grad_values = jnp.zeros(value_seq.shape, jnp.float32)
        for block_index in range(window // block_rows):
            offset = block_index * block_rows
            query_block = query_seq[offset : offset + block_rows]
            grad_block = grad_seq[offset : offset + block_rows]
            scores = masked_scores(query_block, key_seq, segment_row, offset, block_rows)
            softmax_exact = jnp.exp(scores - totals_seq[block_index][..., None])
            softmax_low = softmax_exact.astype(jnp.bfloat16)
            grad_softmax = jnp.einsum(
                "qhe,khe->hqk", grad_block, value_seq, preferred_element_type=jnp.float32
            )
            row_terms = jnp.sum(softmax_exact * grad_softmax, axis=-1, keepdims=True)
            grad_scores = (softmax_exact * (grad_softmax - row_terms)).astype(jnp.bfloat16)
            query_parts.append(
                jnp.einsum("hqk,khe->qhe", grad_scores, key_seq, preferred_element_type=jnp.float32)
                * scaling
            )
            grad_keys = (
                grad_keys
                + jnp.einsum(
                    "hqk,qhe->khe", grad_scores, query_block, preferred_element_type=jnp.float32
                )
                * scaling
            )
            grad_values = grad_values + jnp.einsum(
                "hqk,qhe->khe", softmax_low, grad_block, preferred_element_type=jnp.float32
            )
        grad_query = jnp.concatenate(query_parts, axis=0)
        return (
            grad_query.astype(jnp.bfloat16),
            grad_keys.astype(jnp.bfloat16),
            grad_values.astype(jnp.bfloat16),
        )

    grad_query, grad_keys, grad_values = lax.map(
        one_sequence,
        (
            split_heads(query_rows, seq_count),
            split_heads(key_rows, seq_count),
            split_heads(value_rows, seq_count),
            segments,
            log_totals,
            split_heads(grad_attended, seq_count),
        ),
    )
    return (
        grad_query.reshape(query_rows.shape),
        grad_keys.reshape(query_rows.shape),
        grad_values.reshape(query_rows.shape),
    )


def layer_forward(residual, segments, weights):
    w_qkv, qv_bias, w_out, w_up, up_bias, w_down, out_bias, gains, shifts = weights
    row_count = residual.shape[0]
    normed, unit_one, inverse_one = layer_norm(residual, gains[0], shifts[0])
    normed_all = lax.all_gather(normed.astype(jnp.bfloat16), "tensor", axis=0, tiled=True)
    projected = jnp.einsum("td,dsc->tsc", normed_all, w_qkv, preferred_element_type=jnp.float32)
    query_rows = (projected[:, 0] + qv_bias[0]).astype(jnp.bfloat16)
    key_rows = projected[:, 1].astype(jnp.bfloat16)
    value_rows = (projected[:, 2] + qv_bias[1]).astype(jnp.bfloat16)
    attended, log_totals = attend_forward(query_rows, key_rows, value_rows, segments)
    middle = (
        residual
        + lax.psum_scatter(
            jnp.dot(
                lax.slice_in_dim(attended, 0, row_count * lax.axis_size("tensor"), axis=0),
                w_out,
                preferred_element_type=jnp.float32,
            ).astype(jnp.bfloat16),
            "tensor",
            scatter_dimension=0,
            tiled=True,
        ).astype(jnp.float32)
        + out_bias[0]
    )
    normed_two, unit_two, inverse_two = layer_norm(middle, gains[1], shifts[1])
    normed_low = normed_two.astype(jnp.bfloat16)
    ffn_rows = lax.all_gather(normed_low, "tensor", axis=0, tiled=True)
    before = jnp.dot(ffn_rows, w_up, preferred_element_type=jnp.float32) + up_bias
    activated = gelu_tanh(before).astype(jnp.bfloat16)
    ffn_branch = lax.psum_scatter(
        jnp.dot(
            lax.slice_in_dim(activated, 0, row_count * lax.axis_size("tensor"), axis=0),
            w_down,
            preferred_element_type=jnp.float32,
        ).astype(jnp.bfloat16),
        "tensor",
        scatter_dimension=0,
        tiled=True,
    ).astype(jnp.float32)
    kept_ffn = (w_up, w_down)
    result = middle + ffn_branch + out_bias[1]
    kept_state = (
        unit_one,
        inverse_one,
        normed_all,
        query_rows,
        key_rows,
        value_rows,
        attended,
        log_totals,
        unit_two,
        inverse_two,
        ffn_rows,
        before,
        activated,
        kept_ffn,
    )
    return (result, kept_state)


def layer_backward(grad_residual, segments, weights, kept_state):
    w_qkv, qv_bias, w_out, w_up, up_bias, w_down, out_bias, gains, shifts = weights
    (
        unit_one,
        inverse_one,
        normed_all,
        query_rows,
        key_rows,
        value_rows,
        attended,
        log_totals,
        unit_two,
        inverse_two,
        ffn_rows,
        before,
        activated,
        kept_ffn,
    ) = kept_state
    up_used, down_used = kept_ffn
    row_count = grad_residual.shape[0]
    grad_branch = grad_residual.astype(jnp.bfloat16)
    bias_down = jnp.sum(grad_branch, axis=0, dtype=jnp.float32)
    grad_rows = lax.all_gather(grad_branch, "tensor", axis=0, tiled=True)
    grad_hidden = jnp.einsum("td,fd->tf", grad_rows, down_used, preferred_element_type=jnp.float32)
    grad_before = (grad_hidden * gelu_slope(before)).astype(jnp.bfloat16)
    grad_down = jnp.einsum("tf,td->fd", activated, grad_rows, preferred_element_type=jnp.float32)
    grad_up = jnp.einsum("td,tf->df", ffn_rows, grad_before, preferred_element_type=jnp.float32)
    grad_up_bias = jnp.sum(grad_before, axis=0, dtype=jnp.float32)
    piece_rows = lax.slice_in_dim(grad_before, 0, row_count * lax.axis_size("tensor"), axis=0)
    grad_normed_two = lax.psum_scatter(
        jnp.einsum("tf,df->td", piece_rows, w_up, preferred_element_type=jnp.float32).astype(
            jnp.bfloat16
        ),
        "tensor",
        scatter_dimension=0,
        tiled=True,
    ).astype(jnp.float32)
    through_two, gain_two, shift_two = norm_backward(
        grad_normed_two, unit_two, inverse_two, gains[1]
    )
    grad_middle = grad_residual + through_two
    grad_attn_branch = grad_middle.astype(jnp.bfloat16)
    bias_attn = jnp.sum(grad_attn_branch, axis=0, dtype=jnp.float32)
    grad_attn_all = lax.all_gather(grad_attn_branch, "tensor", axis=0, tiled=True)
    grad_out_w = jnp.einsum(
        "tc,td->cd", attended, grad_attn_all, preferred_element_type=jnp.float32
    )
    grad_attended = jnp.einsum(
        "td,cd->tc", grad_attn_all, w_out, preferred_element_type=jnp.float32
    ).astype(jnp.bfloat16)
    grad_query, grad_keys, grad_values = attend_backward(
        query_rows, key_rows, value_rows, segments, log_totals, grad_attended
    )
    grad_projected = jnp.stack((grad_query, grad_keys, grad_values), axis=1)
    grad_qkv = jnp.einsum(
        "td,tsc->dsc", normed_all, grad_projected, preferred_element_type=jnp.float32
    )
    grad_qv_bias = jnp.stack(
        (
            jnp.sum(grad_query, axis=0, dtype=jnp.float32),
            jnp.sum(grad_values, axis=0, dtype=jnp.float32),
        )
    )
    piece_rows = lax.slice_in_dim(grad_projected, 0, row_count * lax.axis_size("tensor"), axis=0)
    grad_normed = lax.psum_scatter(
        jnp.einsum("tsc,dsc->td", piece_rows, w_qkv, preferred_element_type=jnp.float32).astype(
            jnp.bfloat16
        ),
        "tensor",
        scatter_dimension=0,
        tiled=True,
    ).astype(jnp.float32)
    through_one, gain_one, shift_one = norm_backward(grad_normed, unit_one, inverse_one, gains[0])
    grad_input = grad_middle + through_one
    spread = (grad_qkv, grad_qv_bias, grad_out_w, grad_up, grad_up_bias, grad_down)
    shared = (
        jnp.stack((bias_attn, bias_down)),
        jnp.stack((gain_one, gain_two)),
        jnp.stack((shift_one, shift_two)),
    )
    return (grad_input, spread, shared)


def local_general(
    tokens_in,
    segments,
    w_qkv,
    qv_bias,
    w_out,
    w_up,
    up_bias,
    w_down,
    out_bias,
    ln_gain,
    ln_bias,
    cotangent,
):
    layers_total = w_qkv.shape[0]
    all_params = (w_qkv, qv_bias, w_out, w_up, up_bias, w_down, out_bias, ln_gain, ln_bias)
    residual = tokens_in.astype(jnp.float32)
    kept_layers = []
    for layer_index in range(layers_total):
        weights = tuple((member_array[layer_index] for member_array in all_params))
        residual, kept_state = layer_forward(residual, segments, weights)
        kept_layers.append(kept_state)
    out_act = residual.astype(jnp.bfloat16)
    grad_residual = cotangent.astype(jnp.float32)
    spread_layers = []
    shared_layers = []
    for layer_index in reversed(range(layers_total)):
        weights = tuple((member_array[layer_index] for member_array in all_params))
        grad_residual, spread, shared = layer_backward(
            grad_residual, segments, weights, kept_layers[layer_index]
        )
        spread_layers.insert(0, spread)
        shared_layers.insert(0, shared)
    spread_stack = tuple(
        (
            jnp.stack([spread_layers[layer_index][position] for layer_index in range(layers_total)])
            for position in range(6)
        )
    )
    spread_stack = jax.tree.map(
        lambda part: part.astype(jnp.float32), lax.psum(as_sent(spread_stack), "dp")
    )
    shared_stack = tuple(
        (
            jnp.stack([shared_layers[layer_index][position] for layer_index in range(layers_total)])
            for position in range(3)
        )
    )
    shared_stack = lax.psum(shared_stack, ("dp", "tensor"))
    grad_in = grad_residual.astype(jnp.bfloat16)
    return (out_act, grad_in) + tuple(spread_stack) + tuple(shared_stack)


BAND = 256
LANES = 128
VMEM_ASKED = 60 * 2**20


def dot_nt(left, right):
    return lax.dot_general(left, right, (((1,), (1,)), ((), ())), preferred_element_type=jnp.float32)


def dot_tn(left, right):
    return lax.dot_general(left, right, (((0,), (0,)), ((), ())), preferred_element_type=jnp.float32)


def dot_low(left, right):
    return jnp.dot(left, right, preferred_element_type=jnp.float32)


UNITS_LAYER = 12
BEATS_EVERY_TICK = 18
Y_AHEAD = 2


def fill_band_bias(segk_ref, bias_ref):
    wide = segk_ref.shape[1]
    values = lax.broadcasted_iota(jnp.int32, (16, wide), 0)
    member = (values == segk_ref[...]).astype(jnp.float32).astype(jnp.bfloat16)
    for block in range(bias_ref.shape[0]):
        queries = member[:, (block + 1) * BAND : (block + 2) * BAND]
        keys = member[:, block * BAND : (block + 2) * BAND]
        row_place = lax.broadcasted_iota(jnp.int32, (BAND, 2 * BAND), 0) + BAND
        column_place = lax.broadcasted_iota(jnp.int32, (BAND, 2 * BAND), 1)
        allowed = (dot_tn(queries, keys) > 0.5) & (column_place <= row_place)
        bias_ref[block] = jnp.where(allowed, 0.0, masked_score)


def band_rows(halo, rows, block):
    if block == 0:
        return jnp.concatenate([halo, rows[0:BAND, :]], axis=0)
    return rows[(block - 1) * BAND : (block + 1) * BAND, :]


def aligned(index, size):
    return pl.ds(pl.multiple_of(index * size, size), size)


def forward_kernel(layers, block, hidden_half, *refs):
    (
        tokens_ref,
        cot_ref,
        segments_ref,
        qkv_own,
        out_own,
        up_own,
        down_own,
        qv_bias_ref,
        up_bias_ref,
        out_bias_ref,
        gain_ref,
        shift_ref,
        out_act_ref,
        cot_out,
        segk_out,
        qkv_other,
        out_other,
        up_other,
        down_other,
        act_out,
        slope_out,
        normed_two_out,
        middle_out,
        attended_out,
        proj_out,
        halo_out,
        totals_out,
        normed_out,
        resid_out,
        tokens_buf,
        segments_in,
        qv_bias_in,
        up_bias_in,
        resid,
        collected,
        normed,
        normed_two,
        proj,
        halo,
        attended,
        totals,
        act_buf,
        slope_buf,
        qkv_weight,
        out_weight,
        up_weight,
        down_weight,
        bias_buf,
        start_send,
        start_recv,
        swap_sem,
        relay_send,
        relay_recv,
        halo_send_sem,
        halo_recv_sem,
        load_sem,
        store_sem,
        pair_store_sem,
    ) = refs
    width = 2 * block
    rows_all = tokens_buf.shape[0]
    pairs_half = block // LANES
    blocks_hidden = hidden_half // block
    low = jnp.bfloat16
    place = lax.axis_index("dp")
    y = lax.axis_index("tensor")
    core = place % 2
    x = (place // 2) % 2
    z = place // 4
    z_low = z % 2
    core_partner = {"dp": place + 1 - 2 * core, "tensor": y}
    x_partner = {"dp": place + 2 - 4 * x, "tensor": y}
    y_partner = {"dp": place, "tensor": 1 - y}
    z_partner = {"dp": place + 4 - 8 * z_low, "tensor": y}
    swap_partner = {"dp": place + 1 - 2 * core, "tensor": 1 - y}
    swaps = core + y - 2 * core * y

    barrier = pltpu.get_barrier_semaphore()
    for partner in (core_partner, x_partner, y_partner, z_partner, swap_partner):
        pl.semaphore_signal(barrier, inc=1, device_id=partner, device_id_type=MESH)
    pl.semaphore_wait(barrier, 5)

    def remote(source, target, send, recv, partner):
        return pltpu.make_async_remote_copy(
            src_ref=source,
            dst_ref=target,
            send_sem=send,
            recv_sem=recv,
            device_id=partner,
            device_id_type=MESH,
        )

    def swap_copy(index, source, target):
        return remote(source, target, start_send.at[index], start_recv.at[index], swap_partner)

    def swap_start(index, source, target):
        @pl.when(swaps == 1)
        def _():
            swap_copy(index, source, target).start()

        @pl.when(swaps == 0)
        def _():
            pltpu.make_async_copy(source, target, swap_sem.at[index]).start()

    def swap_wait(index, source, target):
        @pl.when(swaps == 1)
        def _():
            swap_copy(index, source, target).wait()

        @pl.when(swaps == 0)
        def _():
            pltpu.make_async_copy(source, target, swap_sem.at[index]).wait()

    segments_copy = remote(
        segments_ref, segments_in, start_send.at[2], start_recv.at[2], core_partner
    )
    qv_copy = remote(qv_bias_ref, qv_bias_in, start_send.at[3], start_recv.at[3], y_partner)
    up_copy = remote(up_bias_ref, up_bias_in, start_send.at[4], start_recv.at[4], y_partner)

    units = layers * UNITS_LAYER

    def for_unit(unit, action):
        layer, inside = unit // UNITS_LAYER, unit % UNITS_LAYER

        @pl.when(inside < 3)
        def _():
            action(qkv_own.at[layer, inside], qkv_other.at[layer, inside])

        @pl.when(inside == 3)
        def _():
            action(out_own.at[layer], out_other.at[layer])

        @pl.when((inside >= 4) & (inside % 2 == 0))
        def _():
            cut = aligned((inside - 4) // 2, block)
            action(up_own.at[layer, :, cut], up_other.at[layer, :, cut])

        @pl.when((inside >= 4) & (inside % 2 == 1))
        def _():
            cut = aligned((inside - 4) // 2, block)
            action(down_own.at[layer, cut, :], down_other.at[layer, cut, :])

    def hop_copy(hop, unit, source, target):
        partner = (y_partner, x_partner, z_partner, core_partner)[hop]
        return remote(source, target, relay_send.at[hop, unit], relay_recv.at[hop, unit], partner)

    def piece_of(view, hop, short):
        rows = view.shape[0]
        if hop == 3:
            return view.at[aligned(core, rows // 2)]
        if hop == 2:
            return view.at[aligned(2 * core + z_low, rows // 4)]
        if short:
            return view.at[aligned(4 * core + 2 * z_low + x, rows // 8)]
        return view.at[aligned(2 * core + x, rows // 4)]

    def by_length(unit, hop, action):
        if hop == 3:
            action(False)
            return

        @pl.when(unit % 3 != 0)
        def _():
            action(True)

        if hop < 2:

            @pl.when(unit % 3 == 0)
            def _():
                action(False)

    def hop_start(hop, unit):
        def go(own, other):
            def one(short):
                source = piece_of(own if hop == 0 else other, hop, short)
                hop_copy(hop, unit, source, piece_of(other, hop, short)).start()

            by_length(unit, hop, one)

        for_unit(unit, go)

    def hop_wait(hop, unit):
        def one(short):
            piece = piece_of(down_other.at[0, pl.ds(0, block), :], hop, short)
            hop_copy(hop, unit, piece, piece).wait()

        by_length(unit, hop, one)

    def when_unit(unit, action):
        @pl.when((unit >= 0) & (unit < units))
        def _():
            action(unit)

    def beat(b):
        def after_y(unit):
            hop_wait(0, unit)
            hop_start(1, unit)

        def after_x(unit):
            hop_wait(1, unit)
            hop_start(2, unit)

        def after_z(unit):
            hop_wait(2, unit)
            hop_start(3, unit)

        when_unit(b + Y_AHEAD, lambda unit: hop_start(0, unit))
        when_unit(b - 1, after_y)
        when_unit(b - 2, after_x)
        when_unit(b - 3, after_z)
        when_unit(b - 4, lambda unit: hop_wait(3, unit))

    other_step = 3 + pairs_half
    out_step = other_step + 1 + pairs_half
    norm_two_step = out_step + 1
    ffn_step = norm_two_step + 1
    end_step = ffn_step + 2 * blocks_hidden
    period = end_step + 1
    jobs = layers * period

    def loads(kind, slot, *sources):
        targets = {
            "qkv": (qkv_weight,),
            "out": (out_weight.at[0], out_weight.at[1]),
            "ffn": (up_weight.at[slot], down_weight.at[slot]),
        }[kind]
        sources = sources or targets
        return [
            pltpu.make_async_copy(source, target, load_sem.at[slot, index])
            for index, (source, target) in enumerate(zip(sources, targets))
        ]

    def start_all(copies):
        for copy in copies:
            copy.start()

    def wait_all(copies):
        for copy in copies:
            copy.wait()

    def prefetch(t):
        slot = t % 2
        layer, step = t // period, t % period
        for at, source in ((1, qkv_own), (other_step, qkv_other)):

            @pl.when(step == at)
            def _(source=source):
                start_all(loads("qkv", slot, source.at[layer]))

        @pl.when(step == out_step)
        def _():
            start_all(loads("out", slot, out_own.at[layer], out_other.at[layer]))

        for which, (up_ref, down_ref) in enumerate(((up_own, down_own), (up_other, down_other))):
            begin = ffn_step + which * blocks_hidden

            @pl.when((step >= begin) & (step < begin + blocks_hidden))
            def _(begin=begin, up_ref=up_ref, down_ref=down_ref):
                cut = aligned(step - begin, block)
                start_all(loads("ffn", slot, up_ref.at[layer, :, cut], down_ref.at[layer, cut, :]))

    tiles = [slice(r, r + BAND) for r in range(0, rows_all, BAND)]
    fine_tiles = [slice(r, r + LANES) for r in range(0, rows_all, LANES)]

    def normalize(layer, index, target):
        gain = gain_ref[pl.ds(2 * layer + index, 1), :]
        shift = shift_ref[pl.ds(2 * layer + index, 1), :]
        for tile in fine_tiles:
            values, _, _ = layer_norm(resid[tile, :], gain, shift)
            target[tile, :] = values.astype(low)

    def store(index, source, target):
        return pltpu.make_async_copy(source, target, store_sem.at[index])

    def first_stores(layer):
        return [store(0, resid, resid_out.at[layer]), store(1, normed, normed_out.at[layer])]

    def proj_stores(layer, which):
        return [
            store(
                2 + 3 * which + third,
                proj.at[which, third],
                proj_out.at[layer, which, :, pl.ds(third * block, block)],
            )
            for third in range(3)
        ]

    def halo_store(layer, which):
        return store(8 + which, halo.at[layer, which], halo_out.at[layer, which])

    def attended_stores(layer, which):
        return [
            store(10 + which, attended.at[which], attended_out.at[layer, which]),
            store(12 + which, totals.at[which], totals_out.at[layer, which]),
        ]

    def second_stores(layer):
        return [
            store(14, resid, middle_out.at[layer]),
            store(15, normed_two, normed_two_out.at[layer]),
        ]

    def ffn_stores(layer, index, slot):
        which, inside = index // blocks_hidden, index % blocks_hidden
        cut = aligned(inside, block)
        return [
            pltpu.make_async_copy(
                buf.at[slot], out.at[layer, which, :, cut], pair_store_sem.at[slot, kind]
            )
            for kind, (buf, out) in enumerate(((act_buf, act_out), (slope_buf, slope_out)))
        ]

    def halo_copy(layer, which):
        return remote(
            proj.at[which, pl.ds(1, 2), pl.ds(rows_all - BAND, BAND)],
            halo.at[layer, which],
            halo_send_sem.at[layer, which],
            halo_recv_sem.at[layer, which],
            core_partner,
        )

    def first_job(layer):
        normalize(layer, 0, normed)
        start_all(first_stores(layer))

    def qkv_job(layer, which, slot):
        wait_all(loads("qkv", slot))
        bias = qv_bias_in if which else qv_bias_ref
        for third in range(3):
            for tile in tiles:
                product = dot_low(normed[tile, :], qkv_weight[third])
                if third != 1:
                    product = product + bias[pl.ds(2 * layer + third // 2, 1), :]
                proj[which, third, tile, :] = product.astype(low)

        @pl.when(core == 0)
        def _():
            halo_copy(layer, which).start()

        start_all(proj_stores(layer, which))

    def attention_job(layer, which, pair):
        @pl.when(pair == 0)
        def _():
            @pl.when(core == 0)
            def _():
                halo_copy(layer, which).wait_send()

            @pl.when(core == 1)
            def _():
                halo_copy(layer, which).wait_recv()

            halo_store(layer, which).start()
            totals[which] = jnp.zeros_like(totals[which])

        lane = lax.broadcasted_iota(jnp.int32, (BAND, LANES), 1)
        here = aligned(pair, LANES)
        for index, tile in enumerate(tiles):
            query = proj[which, 0, tile, here]
            keys = band_rows(halo[layer, which, 0, :, here], proj[which, 1, :, here], index)
            values = band_rows(halo[layer, which, 1, :, here], proj[which, 2, :, here], index)
            parts = []
            kept = totals[which, tile, :]
            for head in range(2):
                mine = (lane // HEAD_DIM) == head
                scores = (
                    dot_nt(jnp.where(mine, query, 0), keys) * HEAD_DIM ** (-0.5) + bias_buf[index]
                )
                highest = jnp.max(scores, axis=-1, keepdims=True)
                raised = jnp.exp(scores - highest)
                summed = jnp.sum(raised, axis=-1, keepdims=True)
                parts.append(dot_low(raised.astype(low), values) / summed)
                kept = jnp.where(lane == 2 * pair + head, highest + jnp.log(summed), kept)
            totals[which, tile, :] = kept
            attended[which, tile, here] = jnp.where(lane < HEAD_DIM, parts[0], parts[1]).astype(low)

        @pl.when(pair == pairs_half - 1)
        def _():
            start_all(attended_stores(layer, which))

    def out_job(layer, slot):
        wait_all(loads("out", slot))
        wait_all(first_stores(layer))
        for which in range(2):
            wait_all(proj_stores(layer, which))
            halo_store(layer, which).wait()
        bias = out_bias_ref[pl.ds(2 * layer, 1), :]
        for tile in tiles:
            branch = dot_low(attended[0, tile, :], out_weight[0])
            branch = branch + dot_low(attended[1, tile, :], out_weight[1])
            resid[tile, :] = resid[tile, :] + branch + bias

    def second_job(layer):
        normalize(layer, 1, normed_two)
        start_all(second_stores(layer))

    def ffn_job(layer, which, inside, slot):
        index = which * blocks_hidden + inside
        wait_all(loads("ffn", slot))

        @pl.when(index >= 2)
        def _():
            wait_all(ffn_stores(layer, index - 2, slot))

        bias = (up_bias_in if which else up_bias_ref)[pl.ds(layer, 1), aligned(inside, block)]
        for tile in tiles:
            before = dot_low(normed_two[tile, :], up_weight[slot]) + bias
            square = before * before
            tangent = jnp.tanh(gelu_coeff * before * (1.0 + cubic_coeff * square))
            raised = 0.5 * (1.0 + tangent)
            activated = (before * raised).astype(low)
            act_buf[slot, tile, :] = activated
            slope_buf[slot, tile, :] = (
                raised
                + 0.5
                * before
                * (1.0 - tangent * tangent)
                * gelu_coeff
                * (1.0 + 3.0 * cubic_coeff * square)
            ).astype(low)
            product = dot_low(activated, down_weight[slot])
            if which:
                collected[tile, :] = collected[tile, :] + product
                continue

            @pl.when(inside == 0)
            def _(tile=tile, product=product):
                collected[tile, :] = product

            @pl.when(inside > 0)
            def _(tile=tile, product=product):
                collected[tile, :] = collected[tile, :] + product

        start_all(ffn_stores(layer, index, slot))

    def end_job(layer, slot):
        wait_all(ffn_stores(layer, 2 * blocks_hidden - 2, slot))
        wait_all(ffn_stores(layer, 2 * blocks_hidden - 1, 1 - slot))
        wait_all(second_stores(layer))
        for which in range(2):
            wait_all(attended_stores(layer, which))
        bias = out_bias_ref[pl.ds(2 * layer + 1, 1), :]
        for tile in tiles:
            resid[tile, :] = resid[tile, :] + collected[tile, :] + bias

    def job(t):
        slot = t % 2
        layer, step = t // period, t % period

        def at(first, count, action):
            @pl.when((step >= first) & (step < first + count))
            def _():
                action(step - first)

        at(0, 1, lambda _: first_job(layer))
        at(1, 1, lambda _: qkv_job(layer, 0, slot))
        at(2, pairs_half, lambda pair: attention_job(layer, 0, pair))
        at(other_step, 1, lambda _: qkv_job(layer, 1, slot))
        at(other_step + 1, pairs_half, lambda pair: attention_job(layer, 1, pair))
        at(out_step, 1, lambda _: out_job(layer, slot))
        at(norm_two_step, 1, lambda _: second_job(layer))
        at(ffn_step, blocks_hidden, lambda inside: ffn_job(layer, 0, inside, slot))
        at(ffn_step + blocks_hidden, blocks_hidden, lambda inside: ffn_job(layer, 1, inside, slot))
        at(end_step, 1, lambda _: end_job(layer, slot))

    swap_start(0, tokens_ref, tokens_buf)
    halo[...] = jnp.zeros_like(halo)
    segments_copy.start()
    qv_copy.start()
    up_copy.start()
    for unit in range(Y_AHEAD):
        hop_start(0, unit)
    segments_copy.wait()
    window = jnp.where(core == y, segments_ref[...], segments_in[...])

    @pl.when(core == 0)
    def _():
        segk_out[:, 0:BAND] = jnp.full((1, BAND), -1, jnp.int32)
        segk_out[:, BAND:] = window[:, 0:rows_all]

    @pl.when(core == 1)
    def _():
        segk_out[...] = window[:, rows_all - BAND :]

    fill_band_bias(segk_out, bias_buf)
    qv_copy.wait()
    up_copy.wait()
    swap_wait(0, tokens_ref, tokens_buf)
    for tile in tiles:
        resid[tile, :] = tokens_buf[tile, :].astype(jnp.float32)
    cot_tick = BEATS_EVERY_TICK + 6

    def tick(t, carry):
        @pl.when(t <= BEATS_EVERY_TICK)
        def _():
            beat(t)

        late = t - BEATS_EVERY_TICK

        @pl.when((late > 0) & (late % 2 == 0))
        def _():
            beat(BEATS_EVERY_TICK + late // 2)

        @pl.when(t == cot_tick)
        def _():
            swap_start(1, cot_ref, cot_out)

        @pl.when(t + 1 < jobs)
        def _():
            prefetch(t + 1)

        job(t)
        return carry

    lax.fori_loop(0, jobs, tick, 0)
    for tile in tiles:
        normed_two[tile, :] = resid[tile, :].astype(low)
    last_store = store(0, normed_two, out_act_ref)
    last_store.start()
    last_store.wait()
    swap_wait(1, cot_ref, cot_out)


def run_forward(tokens, cotangent, segments, weights, biases, out_bias, gain, shift, block):
    rows, width = tokens.shape
    layers, hidden_half = weights[-1].shape[0], weights[-1].shape[1]
    low, wide = jnp.bfloat16, jnp.float32
    anywhere = pl.BlockSpec(memory_space=pl.ANY)
    in_vmem = pl.BlockSpec(memory_space=pltpu.VMEM)
    vmem = pltpu.VMEM
    units = layers * UNITS_LAYER
    shape = jax.ShapeDtypeStruct
    saved = [
        shape((layers, 2, rows, hidden_half), low),
        shape((layers, 2, rows, hidden_half), low),
        shape((layers, rows, width), low),
        shape((layers, rows, width), wide),
        shape((layers, 2, rows, block), low),
        shape((layers, 2, rows, 3 * block), low),
        shape((layers, 2, 2, BAND, block), low),
        shape((layers, 2, rows, LANES), wide),
        shape((layers, rows, width), low),
        shape((layers, rows, width), wide),
    ]
    others = [shape(member.shape, low) for member in weights]
    return pl.pallas_call(
        functools.partial(forward_kernel, layers, block, hidden_half),
        in_specs=[anywhere] * 2 + [in_vmem] + [anywhere] * 4 + [in_vmem] * 5,
        out_specs=[anywhere] * 2 + [in_vmem] + [anywhere] * (len(others) + len(saved)),
        out_shape=[
            shape((rows, width), low),
            shape((rows, width), low),
            shape((1, rows + BAND), jnp.int32),
        ]
        + others
        + saved,
        scratch_shapes=[
            vmem((rows, width), low),
            vmem(segments.shape, jnp.int32),
            vmem(biases[0].shape, wide),
            vmem(biases[1].shape, wide),
            vmem((rows, width), wide),
            vmem((rows, width), wide),
            vmem((rows, width), low),
            vmem((rows, width), low),
            vmem((2, 3, rows, block), low),
            vmem((layers, 2, 2, BAND, block), low),
            vmem((2, rows, block), low),
            vmem((2, rows, LANES), wide),
            vmem((2, rows, block), low),
            vmem((2, rows, block), low),
            vmem((3, width, block), low),
            vmem((2, block, width), low),
            vmem((2, width, block), low),
            vmem((2, block, width), low),
            vmem((rows // BAND, BAND, 2 * BAND), wide),
            pltpu.SemaphoreType.DMA((5,)),
            pltpu.SemaphoreType.DMA((5,)),
            pltpu.SemaphoreType.DMA((2,)),
            pltpu.SemaphoreType.DMA((4, units)),
            pltpu.SemaphoreType.DMA((4, units)),
            pltpu.SemaphoreType.DMA((layers, 2)),
            pltpu.SemaphoreType.DMA((layers, 2)),
            pltpu.SemaphoreType.DMA((2, 2)),
            pltpu.SemaphoreType.DMA((16,)),
            pltpu.SemaphoreType.DMA((2, 2)),
        ],
        compiler_params=pltpu.CompilerParams(
            collective_id=1, has_side_effects=True, vmem_limit_bytes=VMEM_ASKED
        ),
        name="forward",
    )(tokens, cotangent, segments, *weights, *biases, out_bias, gain, shift)


SLOTS = 8
CORE_SLOTS = 4
RESULT_SLOTS = 11
STAGED = 2
FIRST = 2
LAGS = dict(core=1, y=3, x=5, outer=7, inner=9, back=11, gather=13, whole=14, stored=15)
VECTOR_STEP = 3
VECTOR_ROWS = 12
MESH = pl.DeviceIdType.MESH
FFN_STEPS = 4
QKV_STEPS = 3


def added(left, right):
    return (left.astype(jnp.float32) + right.astype(jnp.float32)).astype(jnp.bfloat16)


def backward_kernel(layers, block, hidden_half, *refs):
    (
        cot_ref,
        gain_ref,
        segk_ref,
        out_act_ref,
        act_ref,
        slope_ref,
        normed_two_ref,
        middle_ref,
        attended_ref,
        proj_ref,
        halo_ref,
        totals_ref,
        normed_ref,
        resid_ref,
        qkv_own,
        qkv_other,
        out_own,
        out_other,
        up_own,
        up_other,
        down_own,
        down_other,
        out_act_out,
        grad_in_ref,
        out_down,
        out_up,
        out_out,
        out_qkv,
        vector_out,
        grad_branch,
        grad_attn,
        grad_before,
        grad_proj,
        grad_res,
        collected,
        grad_attended,
        qkv_buf,
        halo_buf,
        totals_buf,
        kept_kv,
        halo_send,
        halo_in,
        rows_weight,
        columns_weight,
        slope_buf,
        wide_buf,
        bias_buf,
        sums_buf,
        pair_buf,
        one_buf,
        part_buf,
        core_in,
        own_kept,
        other_kept,
        y_in,
        x_kept,
        x_out,
        x_in,
        z_kept,
        outer_in,
        inner_in,
        result,
        vec_in,
        load_sem,
        io_sem,
        halo_send_sem,
        halo_recv_sem,
        staged_sem,
        send_sems,
        recv_sems,
        store_sem,
        vec_send,
        vec_recv,
        swap_send,
        swap_recv,
    ) = refs
    half, quarter = block // 2, block // 4
    width = 2 * block
    rows_all = grad_branch.shape[0]
    pairs_half = block // LANES
    pairs = 2 * pairs_half
    low = jnp.bfloat16
    place = lax.axis_index("dp")
    y = lax.axis_index("tensor")
    core = place % 2
    x = (place // 2) % 2
    z = place // 4
    z_low = z % 2
    inner = (z + 1) // 2 % 2
    core_partner = {"dp": place + 1 - 2 * core, "tensor": y}
    x_partner = {"dp": place + 2 - 4 * x, "tensor": y}
    y_partner = {"dp": place, "tensor": 1 - y}
    z_partner = {"dp": place + 4 - 8 * z_low, "tensor": y}
    middle_partner = {"dp": place + 4 * (3 - 2 * z), "tensor": y}
    swap_partner = {"dp": place + 1 - 2 * core, "tensor": 1 - y}

    barrier = pltpu.get_barrier_semaphore()
    for partner in (core_partner, x_partner, y_partner, z_partner, swap_partner):
        pl.semaphore_signal(barrier, inc=1, device_id=partner, device_id_type=MESH)

    @pl.when(inner == 1)
    def _():
        pl.semaphore_signal(barrier, inc=1, device_id=middle_partner, device_id_type=MESH)
        pl.semaphore_wait(barrier, 6)

    @pl.when(inner == 0)
    def _():
        pl.semaphore_wait(barrier, 5)

    blocks_hidden = hidden_half // block
    plan = (
        ("rows", blocks_hidden, 2),
        ("columns", 2, blocks_hidden),
        ("rows", 1, 2),
        ("columns", 2, 3),
    )
    starts = []
    per_layer = 0
    for _, down_count, across_count in plan:
        starts.append(per_layer)
        per_layer += down_count * across_count
    chunks = layers * per_layer
    out_refs = (out_down, out_up, out_out, out_qkv)

    def block_of(index):
        return pl.ds(pl.multiple_of(index * block, block), block)

    def for_matrix(chunk, action):
        layer = layers - 1 - chunk // per_layer
        inside = chunk % per_layer
        for member, (_, down_count, across_count) in enumerate(plan):
            begin = starts[member]

            @pl.when((inside >= begin) & (inside < begin + down_count * across_count))
            def _(member=member, begin=begin, across_count=across_count):
                local = inside - begin
                action(member, layer, local // across_count, local % across_count)

    def operands_of(member, layer, i, j):
        if member == 0:
            return (
                grad_branch.at[:, block_of(j)],
                act_ref.at[layer, 0, :, block_of(i)],
                act_ref.at[layer, 1, :, block_of(i)],
            )
        if member == 1:
            return (
                normed_two_ref.at[layer, :, block_of(i)],
                grad_before.at[j // 2, :, block_of(j % 2)],
                grad_before.at[blocks_hidden // 2 + j // 2, :, block_of(j % 2)],
            )
        if member == 2:
            return (
                grad_attn.at[:, block_of(j)],
                attended_ref.at[layer, 0, :, block_of(i)],
                attended_ref.at[layer, 1, :, block_of(i)],
            )
        return (
            normed_ref.at[layer, :, block_of(i)],
            grad_proj.at[:, block_of(j)],
            grad_proj.at[:, block_of(3 + j)],
        )

    def staged_copies(chunk, shared, own, other):
        slot = chunk % STAGED
        return (
            pltpu.make_async_copy(own, pair_buf.at[slot, 0], staged_sem.at[slot, 0]),
            pltpu.make_async_copy(other, pair_buf.at[slot, 1], staged_sem.at[slot, 1]),
            pltpu.make_async_copy(shared, one_buf.at[slot], staged_sem.at[slot, 2]),
        )

    def stage_operands(chunk):
        def action(member, layer, i, j):
            for copy in staged_copies(chunk, *operands_of(member, layer, i, j)):
                copy.start()

        for_matrix(chunk, action)

    def remote(step, chunk, source, target, partner):
        slot = chunk % SLOTS
        return pltpu.make_async_remote_copy(
            src_ref=source,
            dst_ref=target,
            send_sem=send_sems.at[step, slot],
            recv_sem=recv_sems.at[step, slot],
            device_id=partner,
            device_id_type=MESH,
        )

    def core_copy(chunk):
        return remote(
            0,
            chunk,
            part_buf.at[chunk % STAGED, :, aligned(1 - core, half)],
            core_in.at[chunk % CORE_SLOTS],
            core_partner,
        )

    def y_copy(chunk):
        slot = chunk % SLOTS
        return remote(1, chunk, other_kept.at[slot], y_in.at[slot], y_partner)

    def x_copy(chunk):
        slot = chunk % SLOTS
        return remote(2, chunk, x_out.at[slot], x_in.at[slot], x_partner)

    def outer_copy(chunk):
        slot = chunk % SLOTS
        return remote(3, chunk, z_kept.at[slot], outer_in.at[slot], z_partner)

    def inner_copy(chunk):
        slot = chunk % SLOTS
        return remote(4, chunk, z_kept.at[slot], inner_in.at[slot], middle_partner)

    own_rows = aligned(2 * core + x, quarter)

    def back_copy(chunk):
        piece = result.at[chunk % RESULT_SLOTS, own_rows]
        return remote(5, chunk, piece, piece, z_partner)

    def gather_copy(chunk):
        piece = result.at[chunk % RESULT_SLOTS, own_rows]
        return remote(6, chunk, piece, piece, x_partner)

    def whole_copy(chunk):
        piece = result.at[chunk % RESULT_SLOTS, aligned(core, half)]
        return remote(7, chunk, piece, piece, core_partner)

    def store_copy(chunk, target):
        slot = chunk % RESULT_SLOTS
        return pltpu.make_async_copy(result.at[slot], target, store_sem.at[slot])

    def multiply(chunk):
        slot = chunk % STAGED
        for copy in staged_copies(chunk, one_buf.at[slot], pair_buf.at[slot, 0], pair_buf.at[slot, 1]):
            copy.wait()
        inside = chunk % per_layer
        by_rows = (inside < starts[1]) | ((inside >= starts[2]) & (inside < starts[3]))

        @pl.when(by_rows)
        def _():
            single = one_buf[slot]
            for which in range(2):
                part_buf[slot, which] = dot_tn(pair_buf[slot, which], single).astype(low)

        @pl.when(jnp.logical_not(by_rows))
        def _():
            single = one_buf[slot]
            for which in range(2):
                part_buf[slot, which] = dot_tn(single, pair_buf[slot, which]).astype(low)

        core_copy(chunk).start()

    def after_core(chunk):
        slot = chunk % SLOTS
        core_copy(chunk).wait()
        mine = aligned(core, half)
        other_kept[slot] = added(part_buf[chunk % STAGED, 1, mine, :], core_in[chunk % CORE_SLOTS, 1])
        y_copy(chunk).start()
        own_kept[slot] = added(part_buf[chunk % STAGED, 0, mine, :], core_in[chunk % CORE_SLOTS, 0])

    def after_y(chunk):
        slot = chunk % SLOTS
        y_copy(chunk).wait()
        away, here = aligned(1 - x, quarter), aligned(x, quarter)
        x_out[slot] = added(own_kept[slot, away, :], y_in[slot, away, :])
        x_copy(chunk).start()
        x_kept[slot] = added(own_kept[slot, here, :], y_in[slot, here, :])

    def after_x(chunk):
        slot = chunk % SLOTS
        x_copy(chunk).wait()
        z_kept[slot] = added(x_kept[slot], x_in[slot])

        @pl.when(inner == 0)
        def _():
            outer_copy(chunk).start()

    def after_outer(chunk):
        slot = chunk % SLOTS

        @pl.when(inner == 0)
        def _():
            outer_copy(chunk).wait_send()

        @pl.when(inner == 1)
        def _():
            outer_copy(chunk).wait_recv()
            z_kept[slot] = added(z_kept[slot], outer_in[slot])
            inner_copy(chunk).start()

    def after_inner(chunk):
        slot = chunk % SLOTS

        @pl.when(inner == 1)
        def _():
            inner_copy(chunk).wait()
            result[chunk % RESULT_SLOTS, own_rows, :] = added(z_kept[slot], inner_in[slot])
            back_copy(chunk).start()

    def after_back(chunk):
        @pl.when(inner == 0)
        def _():
            back_copy(chunk).wait_recv()

        @pl.when(inner == 1)
        def _():
            back_copy(chunk).wait_send()

        gather_copy(chunk).start()

    def after_gather(chunk):
        gather_copy(chunk).wait()
        whole_copy(chunk).start()

    def after_whole(chunk):
        whole_copy(chunk).wait()

        def action(member, layer, i, j):
            if member == 3:
                target = out_qkv.at[layer, j, block_of(i)]
            else:
                target = out_refs[member].at[layer, block_of(i), block_of(j)]
            store_copy(chunk, target).start()

        for_matrix(chunk, action)

    def after_store(chunk):
        store_copy(chunk, result.at[chunk % RESULT_SLOTS]).wait()

    vector_partners = (core_partner, y_partner, x_partner, z_partner, middle_partner, z_partner)

    def vector_copy(step):
        target = vector_out if step == 5 else vec_in.at[step]
        return pltpu.make_async_remote_copy(
            src_ref=vector_out,
            dst_ref=target,
            send_sem=vec_send.at[step],
            recv_sem=vec_recv.at[step],
            device_id=vector_partners[step],
            device_id_type=MESH,
        )

    def add_vector(step):
        vector_out[...] = vector_out[...] + vec_in[step]

    def vector_tick(step):
        if step == 0:
            vector_copy(0).start()
        elif step <= 3:
            vector_copy(step - 1).wait()
            add_vector(step - 1)
            if step < 3:
                vector_copy(step).start()
            else:

                @pl.when(inner == 0)
                def _():
                    vector_copy(3).start()

        elif step == 4:

            @pl.when(inner == 0)
            def _():
                vector_copy(3).wait_send()

            @pl.when(inner == 1)
            def _():
                vector_copy(3).wait_recv()
                add_vector(3)
                vector_copy(4).start()

        elif step == 5:

            @pl.when(inner == 1)
            def _():
                vector_copy(4).wait()
                add_vector(4)
                vector_copy(5).start()

        else:

            @pl.when(inner == 1)
            def _():
                vector_copy(5).wait_send()

            @pl.when(inner == 0)
            def _():
                vector_copy(5).wait_recv()

    norm_two_step = FFN_STEPS
    out_step = norm_two_step + 1
    attention_step = out_step + 1
    qkv_step = attention_step + pairs + 1
    norm_one_step = qkv_step + QKV_STEPS
    period = norm_one_step + 1
    jobs = layers * period
    hidden_step = 2 * hidden_half // FFN_STEPS

    def loads(kind, slot, *sources):
        targets = {
            "ffn": (rows_weight.at[slot], columns_weight.at[slot], slope_buf.at[slot]),
            "wide": (wide_buf,),
            "out": (rows_weight.at[slot, pl.ds(0, block)], rows_weight.at[slot, pl.ds(block, block)]),
            "attention": (
                qkv_buf.at[slot, 0],
                qkv_buf.at[slot, 1],
                qkv_buf.at[slot, 2],
                halo_buf.at[slot, 0],
                halo_buf.at[slot, 1],
                totals_buf.at[slot],
            ),
            "qkv": (
                columns_weight.at[slot, :, pl.ds(0, block)],
                columns_weight.at[slot, :, pl.ds(block, block)],
            ),
        }[kind]
        sources = sources or targets
        return [
            pltpu.make_async_copy(source, target, load_sem.at[slot, index])
            for index, (source, target) in enumerate(zip(sources, targets))
        ]

    def prefetch(t):
        slot = t % 2
        layer = layers - 1 - t // period
        step = t % period

        for which, (up_ref, down_ref) in enumerate(((up_own, down_own), (up_other, down_other))):

            @pl.when((step < FFN_STEPS) & (step // (FFN_STEPS // 2) == which))
            def _(which=which, up_ref=up_ref, down_ref=down_ref):
                cut = aligned(step % (FFN_STEPS // 2), hidden_step)
                for copy in loads(
                    "ffn",
                    slot,
                    down_ref.at[layer, cut, :],
                    up_ref.at[layer, :, cut],
                    slope_ref.at[layer, which, :, cut],
                ):
                    copy.start()

        for at, source in ((norm_two_step, middle_ref), (norm_one_step, resid_ref)):

            @pl.when(step == at)
            def _(source=source):
                for copy in loads("wide", slot, source.at[layer]):
                    copy.start()

        @pl.when(step == out_step)
        def _():
            for copy in loads("out", slot, out_own.at[layer], out_other.at[layer]):
                copy.start()

        @pl.when((step >= attention_step) & (step < attention_step + pairs))
        def _():
            pair = step - attention_step
            which, inside = pair // pairs_half, pair % pairs_half

            def lanes(third):
                return aligned(third * pairs_half + inside, LANES)

            for copy in loads(
                "attention",
                slot,
                *[proj_ref.at[layer, which, :, lanes(third)] for third in range(3)],
                *[halo_ref.at[layer, which, third, :, lanes(0)] for third in range(2)],
                totals_ref.at[layer, which],
            ):
                copy.start()

        @pl.when((step >= qkv_step) & (step < qkv_step + QKV_STEPS))
        def _():
            for part in range(2):
                index = 2 * (step - qkv_step) + part
                for which, source in enumerate((qkv_own, qkv_other)):

                    @pl.when(index // 3 == which)
                    def _(part=part, index=index, source=source):
                        pltpu.make_async_copy(
                            source.at[layer, index % 3],
                            columns_weight.at[slot, :, pl.ds(part * block, block)],
                            load_sem.at[slot, part],
                        ).start()

    def wait_loads(kind, slot):
        for copy in loads(kind, slot):
            copy.wait()

    tiles = [slice(r, r + BAND) for r in range(0, rows_all, BAND)]
    fine_tiles = [slice(r, r + LANES) for r in range(0, rows_all, LANES)]

    def vector_row(layer, row):
        return pl.ds(layer * VECTOR_ROWS + row, 1)

    def column_sum(values):
        return jnp.sum(values.astype(jnp.float32), axis=0, keepdims=True)

    def ffn_job(layer, step, slot):
        wait_loads("ffn", slot)
        sums = 0.0
        for tile in tiles:
            grad_hidden = dot_nt(grad_branch[tile, :], rows_weight[slot])
            before = (grad_hidden * slope_buf[slot, tile, :].astype(jnp.float32)).astype(low)
            grad_before[step, tile, :] = before
            sums = sums + column_sum(before)
            product = dot_nt(before, columns_weight[slot])

            @pl.when(step == 0)
            def _(tile=tile, product=product):
                collected[tile, :] = product

            @pl.when(step > 0)
            def _(tile=tile, product=product):
                collected[tile, :] = collected[tile, :] + product

        per_half = FFN_STEPS // 2
        which = step // per_half
        owner = which + y - 2 * which * y
        vector_out[vector_row(layer, 2 + owner * per_half + step % per_half), :] = sums

    def norm_job(layer, index, slot):
        wait_loads("wide", slot)
        gain = gain_ref[pl.ds(2 * layer + index, 1), :]
        gain_sum, shift_sum, attn_sum, branch_sum = 0.0, 0.0, 0.0, 0.0
        for tile in fine_tiles:
            incoming = collected[tile, :]
            values = wide_buf[tile, :]
            average = jnp.mean(values, axis=-1, keepdims=True)
            centred = values - average
            inverse = lax.rsqrt(jnp.mean(centred * centred, axis=-1, keepdims=True) + epsilon)
            unit = centred * inverse
            scaled = incoming * gain
            first_mean = jnp.mean(scaled, axis=-1, keepdims=True)
            second_mean = jnp.mean(scaled * unit, axis=-1, keepdims=True)
            total = grad_res[tile, :] + inverse * (scaled - first_mean - unit * second_mean)
            grad_res[tile, :] = total
            rounded = total.astype(low)
            gain_sum = gain_sum + column_sum(incoming * unit)
            shift_sum = shift_sum + column_sum(incoming)
            if index == 1:
                attn_sum = attn_sum + column_sum(rounded)
                branch_sum = branch_sum + column_sum(grad_branch[tile, :])
                grad_attn[tile, :] = rounded
            else:
                grad_branch[tile, :] = rounded
        vector_out[vector_row(layer, 8 + index), :] = gain_sum
        vector_out[vector_row(layer, 10 + index), :] = shift_sum
        if index == 1:
            vector_out[vector_row(layer, 6), :] = attn_sum
            vector_out[vector_row(layer, 7), :] = branch_sum

    def out_job(slot):
        wait_loads("out", slot)
        for tile in tiles:
            grad_attended[tile, :] = dot_nt(grad_attn[tile, :], rows_weight[slot]).astype(low)

    def halo_copy(pair):
        return pltpu.make_async_remote_copy(
            src_ref=halo_send.at[pair % 2],
            dst_ref=halo_in.at[pair],
            send_sem=halo_send_sem.at[pair],
            recv_sem=halo_recv_sem.at[pair],
            device_id=core_partner,
            device_id_type=MESH,
        )

    def proj_lanes(pair, third):
        which, inside = pair // pairs_half, pair % pairs_half
        return aligned(which * 3 * pairs_half + third * pairs_half + inside, LANES)

    def attention_job(pair, slot):
        wait_loads("attention", slot)
        lane = lax.broadcasted_iota(jnp.int32, (BAND, LANES), 1)
        scaling = HEAD_DIM ** (-0.5)
        count = len(tiles)
        key_parts = [None] * (count + 1)
        value_parts = [None] * (count + 1)
        here = aligned(pair, LANES)
        for index, tile in enumerate(tiles):
            query = qkv_buf[slot, 0, tile, :]
            grad = grad_attended[tile, here]
            keys = band_rows(halo_buf[slot, 0], qkv_buf[slot, 1], index)
            values = band_rows(halo_buf[slot, 1], qkv_buf[slot, 2], index)
            grad_query = []
            grad_keys = 0.0
            grad_values = 0.0
            for head in range(2):
                mine = (lane // HEAD_DIM) == head
                query_head = jnp.where(mine, query, 0)
                grad_head = jnp.where(mine, grad, 0)
                scores = dot_nt(query_head, keys) * scaling + bias_buf[index]
                total = jnp.sum(
                    jnp.where(
                        lane == 2 * (pair % pairs_half) + head, totals_buf[slot, tile, :], 0.0
                    ),
                    axis=-1,
                    keepdims=True,
                )
                exact = jnp.exp(scores - total)
                grad_probs = dot_nt(grad_head, values)
                row_terms = jnp.sum(exact * grad_probs, axis=-1, keepdims=True)
                grad_scores = (exact * (grad_probs - row_terms)).astype(low)
                grad_query.append(jnp.dot(grad_scores, keys, preferred_element_type=jnp.float32))
                grad_keys = grad_keys + dot_tn(grad_scores, query_head)
                grad_values = grad_values + dot_tn(exact.astype(low), grad_head)
            grad_proj[tile, proj_lanes(pair, 0)] = (
                jnp.where(lane < HEAD_DIM, grad_query[0], grad_query[1]) * scaling
            ).astype(low)
            grad_keys = grad_keys * scaling
            for part in range(2):
                cut = slice(part * BAND, (part + 1) * BAND)
                old_k, old_v = key_parts[index + part], value_parts[index + part]
                key_parts[index + part] = grad_keys[cut] if old_k is None else old_k + grad_keys[cut]
                value_parts[index + part] = (
                    grad_values[cut] if old_v is None else old_v + grad_values[cut]
                )
        for index in range(count - 1):
            grad_proj[tiles[index], proj_lanes(pair, 1)] = key_parts[index + 1].astype(low)
            grad_proj[tiles[index], proj_lanes(pair, 2)] = value_parts[index + 1].astype(low)
        kept_kv[pair % 2, 0] = key_parts[count]
        kept_kv[pair % 2, 1] = value_parts[count]

        @pl.when(core == 1)
        def _():
            halo_send[pair % 2, 0] = key_parts[0].astype(low)
            halo_send[pair % 2, 1] = value_parts[0].astype(low)
            halo_copy(pair).start()

    def finish_pair(pair):
        last = tiles[-1]

        @pl.when(core == 0)
        def _():
            halo_copy(pair).wait_recv()
            for third in range(2):
                grad_proj[last, proj_lanes(pair, third + 1)] = (
                    kept_kv[pair % 2, third] + halo_in[pair, third].astype(jnp.float32)
                ).astype(low)

        @pl.when(core == 1)
        def _():
            halo_copy(pair).wait_send()
            for third in range(2):
                grad_proj[last, proj_lanes(pair, third + 1)] = kept_kv[pair % 2, third].astype(low)

    def qkv_job(layer, step, slot):
        wait_loads("qkv", slot)
        sums = 0.0
        for tile in tiles:
            grad = grad_proj[tile, aligned(step, width)]
            sums = sums + column_sum(grad)
            product = dot_nt(grad, columns_weight[slot])

            @pl.when(step == 0)
            def _(tile=tile, product=product):
                collected[tile, :] = product

            @pl.when(step > 0)
            def _(tile=tile, product=product):
                collected[tile, :] = collected[tile, :] + product

        sums_buf[...] = sums
        for when, part, which, row in ((0, 0, 0, 0), (1, 0, 0, 1), (1, 1, 1, 0), (2, 1, 1, 1)):

            @pl.when(step == when)
            def _(part=part, which=which, row=row):
                owner = 1 - y if which else y
                vector_out[vector_row(layer, row), block_of(owner)] = sums_buf[
                    :, part * block : (part + 1) * block
                ]

    def job(t):
        slot = t % 2
        layer = layers - 1 - t // period
        step = t % period

        @pl.when(step < FFN_STEPS)
        def _():
            ffn_job(layer, step, slot)

        @pl.when(step == norm_two_step)
        def _():
            norm_job(layer, 1, slot)

        @pl.when(step == out_step)
        def _():
            out_job(slot)

        @pl.when((step > attention_step) & (step <= attention_step + pairs))
        def _():
            finish_pair(step - attention_step - 1)

        @pl.when((step >= attention_step) & (step < attention_step + pairs))
        def _():
            attention_job(step - attention_step, slot)

        @pl.when((step >= qkv_step) & (step < qkv_step + QKV_STEPS))
        def _():
            qkv_job(layer, step - qkv_step, slot)

        @pl.when(step == norm_one_step)
        def _():
            norm_job(layer, 0, slot)

    stages = (
        (LAGS["core"], after_core),
        (0, multiply),
        (None, job),
        (LAGS["y"], after_y),
        (LAGS["x"], after_x),
        (LAGS["outer"], after_outer),
        (LAGS["inner"], after_inner),
        (LAGS["back"], after_back),
        (LAGS["gather"], after_gather),
        (LAGS["stored"], after_store),
        (LAGS["whole"], after_whole),
    )

    swaps = core + y - 2 * core * y

    def swap_copy(index, source, target):
        return pltpu.make_async_remote_copy(
            src_ref=source,
            dst_ref=target,
            send_sem=swap_send.at[index],
            recv_sem=swap_recv.at[index],
            device_id=swap_partner,
            device_id_type=MESH,
        )

    def swap_start(index, source, target):
        @pl.when(swaps == 1)
        def _():
            swap_copy(index, source, target).start()

        @pl.when(swaps == 0)
        def _():
            pltpu.make_async_copy(source, target, io_sem.at[1 + index]).start()

    def swap_wait(index, source, target):
        @pl.when(swaps == 1)
        def _():
            swap_copy(index, source, target).wait()

        @pl.when(swaps == 0)
        def _():
            pltpu.make_async_copy(source, target, io_sem.at[1 + index]).wait()

    first_load = pltpu.make_async_copy(cot_ref, grad_branch, io_sem.at[0])
    first_load.start()
    prefetch(0)
    fill_band_bias(segk_ref, bias_buf)
    first_load.wait()
    for tile in tiles:
        grad_res[tile, :] = grad_branch[tile, :].astype(jnp.float32)
    swap_start(0, out_act_ref, out_act_out)
    vector_ticks = [jobs + VECTOR_STEP * step for step in range(7)]

    def tick(t, carry):
        @pl.when(t + 1 < jobs)
        def _():
            prefetch(t + 1)

        ahead = t + 1 - FIRST

        @pl.when((ahead >= 0) & (ahead < chunks))
        def _():
            stage_operands(ahead)

        for lag, action in stages:
            if lag is None:

                @pl.when(t < jobs)
                def _():
                    job(t)

                continue
            chunk = t - FIRST - lag

            @pl.when((chunk >= 0) & (chunk < chunks))
            def _(chunk=chunk, action=action):
                action(chunk)

        @pl.when(t == jobs)
        def _():
            swap_start(1, grad_branch, grad_in_ref)

        for step, when in enumerate(vector_ticks):

            @pl.when(t == when)
            def _(step=step):
                vector_tick(step)

        return carry

    lax.fori_loop(0, max(chunks + FIRST + LAGS["stored"], vector_ticks[-1] + 1), tick, 0)
    swap_wait(0, out_act_ref, out_act_out)
    swap_wait(1, grad_branch, grad_in_ref)


def run_backward(cotangent, gain, segk, out_act, saved, weights, block):
    rows, width = cotangent.shape
    layers, hidden_half = weights[-1].shape[0], weights[-1].shape[1]
    half, quarter = block // 2, block // 4
    low, wide = jnp.bfloat16, jnp.float32
    pairs = width // LANES
    anywhere = pl.BlockSpec(memory_space=pl.ANY)
    in_vmem = pl.BlockSpec(memory_space=pltpu.VMEM)
    vector = (layers * VECTOR_ROWS, width)
    hidden_step = 2 * hidden_half // FFN_STEPS
    vmem = pltpu.VMEM
    return pl.pallas_call(
        functools.partial(backward_kernel, layers, block, hidden_half),
        in_specs=[anywhere] + [in_vmem] * 2 + [anywhere] * (1 + len(saved) + len(weights)),
        out_specs=[anywhere] * 6 + [in_vmem],
        out_shape=[
            jax.ShapeDtypeStruct((rows, width), low),
            jax.ShapeDtypeStruct((rows, width), low),
            jax.ShapeDtypeStruct((layers, hidden_half, width), low),
            jax.ShapeDtypeStruct((layers, width, hidden_half), low),
            jax.ShapeDtypeStruct((layers, block, width), low),
            jax.ShapeDtypeStruct((layers, 3, width, block), low),
            jax.ShapeDtypeStruct(vector, wide),
        ],
        scratch_shapes=[
            vmem((rows, width), low),
            vmem((rows, width), low),
            vmem((FFN_STEPS, rows, hidden_step), low),
            vmem((rows, 6 * block), low),
            vmem((rows, width), wide),
            vmem((rows, width), wide),
            vmem((rows, width), low),
            vmem((2, 3, rows, LANES), low),
            vmem((2, 2, BAND, LANES), low),
            vmem((2, rows, LANES), wide),
            vmem((2, 2, BAND, LANES), wide),
            vmem((2, 2, BAND, LANES), low),
            vmem((pairs, 2, BAND, LANES), low),
            vmem((2, hidden_step, width), low),
            vmem((2, width, hidden_step), low),
            vmem((2, rows, hidden_step), low),
            vmem((rows, width), wide),
            vmem((rows // BAND, BAND, 2 * BAND), wide),
            vmem((1, width), wide),
            vmem((STAGED, 2, rows, block), low),
            vmem((STAGED, rows, block), low),
            vmem((STAGED, 2, block, block), low),
            vmem((CORE_SLOTS, 2, half, block), low),
            vmem((SLOTS, half, block), low),
            vmem((SLOTS, half, block), low),
            vmem((SLOTS, half, block), low),
            vmem((SLOTS, quarter, block), low),
            vmem((SLOTS, quarter, block), low),
            vmem((SLOTS, quarter, block), low),
            vmem((SLOTS, quarter, block), low),
            vmem((SLOTS, quarter, block), low),
            vmem((SLOTS, quarter, block), low),
            vmem((RESULT_SLOTS, block, block), low),
            vmem((5,) + vector, wide),
            pltpu.SemaphoreType.DMA((2, 6)),
            pltpu.SemaphoreType.DMA((3,)),
            pltpu.SemaphoreType.DMA((pairs,)),
            pltpu.SemaphoreType.DMA((pairs,)),
            pltpu.SemaphoreType.DMA((STAGED, 3)),
            pltpu.SemaphoreType.DMA((8, SLOTS)),
            pltpu.SemaphoreType.DMA((8, SLOTS)),
            pltpu.SemaphoreType.DMA((RESULT_SLOTS,)),
            pltpu.SemaphoreType.DMA((6,)),
            pltpu.SemaphoreType.DMA((6,)),
            pltpu.SemaphoreType.DMA((2,)),
            pltpu.SemaphoreType.DMA((2,)),
        ],
        compiler_params=pltpu.CompilerParams(
            collective_id=0, has_side_effects=True, vmem_limit_bytes=VMEM_ASKED
        ),
        name="backward",
    )(cotangent, gain, segk, out_act, *saved, *weights)


def local_split(
    tokens_in,
    segments,
    w_qkv,
    qv_bias,
    w_out,
    w_up,
    up_bias,
    w_down,
    out_bias,
    ln_gain,
    ln_bias,
    cotangent,
):
    layers, width = w_qkv.shape[0], w_qkv.shape[1]
    block = w_qkv.shape[3]
    y = lax.axis_index("tensor")
    weights = (w_qkv.transpose(0, 2, 1, 3), w_out, w_up, w_down)
    gain = ln_gain.reshape(-1, width)
    out_act, cot, segk, *rest = run_forward(
        tokens_in,
        cotangent,
        segments,
        weights,
        (qv_bias.reshape(-1, block), up_bias),
        out_bias.reshape(-1, width),
        gain,
        ln_bias.reshape(-1, width),
        block,
    )
    others, saved = rest[: len(weights)], rest[len(weights) :]
    both = [member for pair in zip(weights, others) for member in pair]
    out_act, grad_in, *reduced, summed = run_backward(
        cot, gain, segk, out_act, saved, both, block
    )
    summed = summed.reshape(layers, -1)
    hidden = 2 * up_bias.shape[1]
    ends = [2 * width, 2 * width + hidden, 4 * width + hidden, 6 * width + hidden]
    qv_sum = summed[:, : ends[0]].reshape(layers, 2, width)
    grad_qv_bias = lax.dynamic_slice_in_dim(qv_sum, y * (width // 2), width // 2, axis=2)
    grad_up_bias = lax.dynamic_slice_in_dim(
        summed[:, ends[0] : ends[1]], y * (hidden // 2), hidden // 2, axis=1
    )
    grad_down, grad_up, grad_out, grad_qkv = [member.astype(jnp.float32) for member in reduced]
    return (
        out_act,
        grad_in,
        grad_qkv.transpose(0, 2, 1, 3),
        grad_qv_bias,
        grad_out,
        grad_up,
        grad_up_bias,
        grad_down,
        summed[:, ends[1] : ends[2]].reshape(layers, 2, width),
        summed[:, ends[2] : ends[3]].reshape(layers, 2, width),
        summed[:, ends[3] :].reshape(layers, 2, width),
    )


def solution(mesh):
    sizes = (mesh.shape["dp"], mesh.shape["tensor"])
    local = local_split if sizes == (16, 2) else local_general
    return jax.shard_map(
        local,
        mesh=mesh,
        in_specs=(
            P(("dp", "tensor"), None),
            P("dp", None),
            P(None, None, None, "tensor"),
            P(None, None, "tensor"),
            P(None, "tensor", None),
            P(None, None, "tensor"),
            P(None, "tensor"),
            P(None, "tensor", None),
            P(),
            P(),
            P(),
            P(("dp", "tensor"), None),
        ),
        out_specs=(
            P(("dp", "tensor"), None),
            P(("dp", "tensor"), None),
            P(None, None, None, "tensor"),
            P(None, None, "tensor"),
            P(None, "tensor", None),
            P(None, None, "tensor"),
            P(None, "tensor"),
            P(None, "tensor", None),
            P(),
            P(),
            P(),
        ),
        check_vma=False,
    )
```

```python
import functools

import jax
import jax.numpy as jnp
from jax import lax
from jax.experimental import pallas as pl
from jax.experimental.pallas import tpu as pltpu
from jax.sharding import PartitionSpec as P

HEAD_DIM = 64


epsilon = 1e-05
gelu_coeff = 0.7978845608028654
cubic_coeff = 0.044715
masked_score = -1e30


def as_sent(shard):

    def short(part):
        return part.astype(jnp.bfloat16) if part.dtype == jnp.float32 else part

    return jax.tree.map(short, shard)


def layer_norm(values, gain, shift):
    average = jnp.mean(values, axis=-1, keepdims=True)
    centred = values - average
    inverse = lax.rsqrt(jnp.mean(centred * centred, axis=-1, keepdims=True) + epsilon)
    unit_rows = centred * inverse
    return (unit_rows * gain + shift, unit_rows, inverse)


def norm_backward(incoming, unit_rows, inverse, gain):
    scaled = incoming * gain
    first_mean = jnp.mean(scaled, axis=-1, keepdims=True)
    second_mean = jnp.mean(scaled * unit_rows, axis=-1, keepdims=True)
    through = inverse * (scaled - first_mean - unit_rows * second_mean)
    return (through, jnp.sum(incoming * unit_rows, axis=0), jnp.sum(incoming, axis=0))


def gelu_tanh(before):
    tanh_input = gelu_coeff * (before + cubic_coeff * before * before * before)
    return 0.5 * before * (1.0 + jnp.tanh(tanh_input))


def gelu_slope(before):
    tanh_input = gelu_coeff * (before + cubic_coeff * before * before * before)
    tangent = jnp.tanh(tanh_input)
    return 0.5 * (1.0 + tangent) + 0.5 * before * (1.0 - tangent * tangent) * gelu_coeff * (
        1.0 + 3.0 * cubic_coeff * before * before
    )


def masked_scores(query_block, key_seq, segment_row, offset, block_rows):
    window = key_seq.shape[0]
    scores = jnp.einsum(
        "qhe,khe->hqk", query_block, key_seq, preferred_element_type=jnp.float32
    ) * HEAD_DIM ** (-0.5)
    query_place = offset + lax.iota(jnp.int32, block_rows)
    key_place = lax.iota(jnp.int32, window)
    query_segment = segment_row[offset : offset + block_rows]
    allowed = (query_place[:, None] >= key_place[None, :]) & (
        query_segment[:, None] == segment_row[None, :]
    )
    return jnp.where(allowed[None], scores, masked_score)


def split_heads(flat_rows, seq_count):
    return flat_rows.reshape(
        seq_count, flat_rows.shape[0] // seq_count, flat_rows.shape[1] // HEAD_DIM, HEAD_DIM
    )


def attend_forward(query_rows, key_rows, value_rows, segments):
    seq_count, window = segments.shape
    block_rows = min(512, window)

    def one_sequence(member):
        query_seq, key_seq, value_seq, segment_row = member
        outputs = []
        totals = []
        for block_index in range(window // block_rows):
            offset = block_index * block_rows
            scores = masked_scores(
                query_seq[offset : offset + block_rows], key_seq, segment_row, offset, block_rows
            )
            highest = jnp.max(scores, axis=-1, keepdims=True)
            raised = jnp.exp(scores - highest)
            summed = jnp.sum(raised, axis=-1, keepdims=True)
            softmax_low = (raised / summed).astype(jnp.bfloat16)
            block_out = jnp.einsum(
                "hqk,khe->qhe", softmax_low, value_seq, preferred_element_type=jnp.float32
            )
            outputs.append(block_out.astype(jnp.bfloat16))
            totals.append(highest[..., 0] + jnp.log(summed[..., 0]))
        return (jnp.concatenate(outputs, axis=0), jnp.stack(totals, axis=0))

    attended, log_totals = lax.map(
        one_sequence,
        (
            split_heads(query_rows, seq_count),
            split_heads(key_rows, seq_count),
            split_heads(value_rows, seq_count),
            segments,
        ),
    )
    return (attended.reshape(query_rows.shape), log_totals)


def attend_backward(query_rows, key_rows, value_rows, segments, log_totals, grad_attended):
    seq_count, window = segments.shape
    block_rows = min(512, window)
    scaling = HEAD_DIM ** (-0.5)

    def one_sequence(member):
        query_seq, key_seq, value_seq, segment_row, totals_seq, grad_seq = member
        query_parts = []
        grad_keys = jnp.zeros(key_seq.shape, jnp.float32)
        grad_values = jnp.zeros(value_seq.shape, jnp.float32)
        for block_index in range(window // block_rows):
            offset = block_index * block_rows
            query_block = query_seq[offset : offset + block_rows]
            grad_block = grad_seq[offset : offset + block_rows]
            scores = masked_scores(query_block, key_seq, segment_row, offset, block_rows)
            softmax_exact = jnp.exp(scores - totals_seq[block_index][..., None])
            softmax_low = softmax_exact.astype(jnp.bfloat16)
            grad_softmax = jnp.einsum(
                "qhe,khe->hqk", grad_block, value_seq, preferred_element_type=jnp.float32
            )
            row_terms = jnp.sum(softmax_exact * grad_softmax, axis=-1, keepdims=True)
            grad_scores = (softmax_exact * (grad_softmax - row_terms)).astype(jnp.bfloat16)
            query_parts.append(
                jnp.einsum("hqk,khe->qhe", grad_scores, key_seq, preferred_element_type=jnp.float32)
                * scaling
            )
            grad_keys = (
                grad_keys
                + jnp.einsum(
                    "hqk,qhe->khe", grad_scores, query_block, preferred_element_type=jnp.float32
                )
                * scaling
            )
            grad_values = grad_values + jnp.einsum(
                "hqk,qhe->khe", softmax_low, grad_block, preferred_element_type=jnp.float32
            )
        grad_query = jnp.concatenate(query_parts, axis=0)
        return (
            grad_query.astype(jnp.bfloat16),
            grad_keys.astype(jnp.bfloat16),
            grad_values.astype(jnp.bfloat16),
        )

    grad_query, grad_keys, grad_values = lax.map(
        one_sequence,
        (
            split_heads(query_rows, seq_count),
            split_heads(key_rows, seq_count),
            split_heads(value_rows, seq_count),
            segments,
            log_totals,
            split_heads(grad_attended, seq_count),
        ),
    )
    return (
        grad_query.reshape(query_rows.shape),
        grad_keys.reshape(query_rows.shape),
        grad_values.reshape(query_rows.shape),
    )


def layer_forward(residual, segments, weights):
    w_qkv, qv_bias, w_out, w_up, up_bias, w_down, out_bias, gains, shifts = weights
    row_count = residual.shape[0]
    normed, unit_one, inverse_one = layer_norm(residual, gains[0], shifts[0])
    normed_all = lax.all_gather(normed.astype(jnp.bfloat16), "tensor", axis=0, tiled=True)
    projected = jnp.einsum("td,dsc->tsc", normed_all, w_qkv, preferred_element_type=jnp.float32)
    query_rows = (projected[:, 0] + qv_bias[0]).astype(jnp.bfloat16)
    key_rows = projected[:, 1].astype(jnp.bfloat16)
    value_rows = (projected[:, 2] + qv_bias[1]).astype(jnp.bfloat16)
    attended, log_totals = attend_forward(query_rows, key_rows, value_rows, segments)
    middle = (
        residual
        + lax.psum_scatter(
            jnp.dot(
                lax.slice_in_dim(attended, 0, row_count * lax.axis_size("tensor"), axis=0),
                w_out,
                preferred_element_type=jnp.float32,
            ).astype(jnp.bfloat16),
            "tensor",
            scatter_dimension=0,
            tiled=True,
        ).astype(jnp.float32)
        + out_bias[0]
    )
    normed_two, unit_two, inverse_two = layer_norm(middle, gains[1], shifts[1])
    normed_low = normed_two.astype(jnp.bfloat16)
    ffn_rows = lax.all_gather(normed_low, "tensor", axis=0, tiled=True)
    before = jnp.dot(ffn_rows, w_up, preferred_element_type=jnp.float32) + up_bias
    activated = gelu_tanh(before).astype(jnp.bfloat16)
    ffn_branch = lax.psum_scatter(
        jnp.dot(
            lax.slice_in_dim(activated, 0, row_count * lax.axis_size("tensor"), axis=0),
            w_down,
            preferred_element_type=jnp.float32,
        ).astype(jnp.bfloat16),
        "tensor",
        scatter_dimension=0,
        tiled=True,
    ).astype(jnp.float32)
    kept_ffn = (w_up, w_down)
    result = middle + ffn_branch + out_bias[1]
    kept_state = (
        unit_one,
        inverse_one,
        normed_all,
        query_rows,
        key_rows,
        value_rows,
        attended,
        log_totals,
        unit_two,
        inverse_two,
        ffn_rows,
        before,
        activated,
        kept_ffn,
    )
    return (result, kept_state)


def layer_backward(grad_residual, segments, weights, kept_state):
    w_qkv, qv_bias, w_out, w_up, up_bias, w_down, out_bias, gains, shifts = weights
    (
        unit_one,
        inverse_one,
        normed_all,
        query_rows,
        key_rows,
        value_rows,
        attended,
        log_totals,
        unit_two,
        inverse_two,
        ffn_rows,
        before,
        activated,
        kept_ffn,
    ) = kept_state
    up_used, down_used = kept_ffn
    row_count = grad_residual.shape[0]
    grad_branch = grad_residual.astype(jnp.bfloat16)
    bias_down = jnp.sum(grad_branch, axis=0, dtype=jnp.float32)
    grad_rows = lax.all_gather(grad_branch, "tensor", axis=0, tiled=True)
    grad_hidden = jnp.einsum("td,fd->tf", grad_rows, down_used, preferred_element_type=jnp.float32)
    grad_before = (grad_hidden * gelu_slope(before)).astype(jnp.bfloat16)
    grad_down = jnp.einsum("tf,td->fd", activated, grad_rows, preferred_element_type=jnp.float32)
    grad_up = jnp.einsum("td,tf->df", ffn_rows, grad_before, preferred_element_type=jnp.float32)
    grad_up_bias = jnp.sum(grad_before, axis=0, dtype=jnp.float32)
    piece_rows = lax.slice_in_dim(grad_before, 0, row_count * lax.axis_size("tensor"), axis=0)
    grad_normed_two = lax.psum_scatter(
        jnp.einsum("tf,df->td", piece_rows, w_up, preferred_element_type=jnp.float32).astype(
            jnp.bfloat16
        ),
        "tensor",
        scatter_dimension=0,
        tiled=True,
    ).astype(jnp.float32)
    through_two, gain_two, shift_two = norm_backward(
        grad_normed_two, unit_two, inverse_two, gains[1]
    )
    grad_middle = grad_residual + through_two
    grad_attn_branch = grad_middle.astype(jnp.bfloat16)
    bias_attn = jnp.sum(grad_attn_branch, axis=0, dtype=jnp.float32)
    grad_attn_all = lax.all_gather(grad_attn_branch, "tensor", axis=0, tiled=True)
    grad_out_w = jnp.einsum(
        "tc,td->cd", attended, grad_attn_all, preferred_element_type=jnp.float32
    )
    grad_attended = jnp.einsum(
        "td,cd->tc", grad_attn_all, w_out, preferred_element_type=jnp.float32
    ).astype(jnp.bfloat16)
    grad_query, grad_keys, grad_values = attend_backward(
        query_rows, key_rows, value_rows, segments, log_totals, grad_attended
    )
    grad_projected = jnp.stack((grad_query, grad_keys, grad_values), axis=1)
    grad_qkv = jnp.einsum(
        "td,tsc->dsc", normed_all, grad_projected, preferred_element_type=jnp.float32
    )
    grad_qv_bias = jnp.stack(
        (
            jnp.sum(grad_query, axis=0, dtype=jnp.float32),
            jnp.sum(grad_values, axis=0, dtype=jnp.float32),
        )
    )
    piece_rows = lax.slice_in_dim(grad_projected, 0, row_count * lax.axis_size("tensor"), axis=0)
    grad_normed = lax.psum_scatter(
        jnp.einsum("tsc,dsc->td", piece_rows, w_qkv, preferred_element_type=jnp.float32).astype(
            jnp.bfloat16
        ),
        "tensor",
        scatter_dimension=0,
        tiled=True,
    ).astype(jnp.float32)
    through_one, gain_one, shift_one = norm_backward(grad_normed, unit_one, inverse_one, gains[0])
    grad_input = grad_middle + through_one
    spread = (grad_qkv, grad_qv_bias, grad_out_w, grad_up, grad_up_bias, grad_down)
    shared = (
        jnp.stack((bias_attn, bias_down)),
        jnp.stack((gain_one, gain_two)),
        jnp.stack((shift_one, shift_two)),
    )
    return (grad_input, spread, shared)


def local_general(
    tokens_in,
    segments,
    w_qkv,
    qv_bias,
    w_out,
    w_up,
    up_bias,
    w_down,
    out_bias,
    ln_gain,
    ln_bias,
    cotangent,
):
    layers_total = w_qkv.shape[0]
    all_params = (w_qkv, qv_bias, w_out, w_up, up_bias, w_down, out_bias, ln_gain, ln_bias)
    residual = tokens_in.astype(jnp.float32)
    kept_layers = []
    for layer_index in range(layers_total):
        weights = tuple((member_array[layer_index] for member_array in all_params))
        residual, kept_state = layer_forward(residual, segments, weights)
        kept_layers.append(kept_state)
    out_act = residual.astype(jnp.bfloat16)
    grad_residual = cotangent.astype(jnp.float32)
    spread_layers = []
    shared_layers = []
    for layer_index in reversed(range(layers_total)):
        weights = tuple((member_array[layer_index] for member_array in all_params))
        grad_residual, spread, shared = layer_backward(
            grad_residual, segments, weights, kept_layers[layer_index]
        )
        spread_layers.insert(0, spread)
        shared_layers.insert(0, shared)
    spread_stack = tuple(
        (
            jnp.stack([spread_layers[layer_index][position] for layer_index in range(layers_total)])
            for position in range(6)
        )
    )
    spread_stack = jax.tree.map(
        lambda part: part.astype(jnp.float32), lax.psum(as_sent(spread_stack), "dp")
    )
    shared_stack = tuple(
        (
            jnp.stack([shared_layers[layer_index][position] for layer_index in range(layers_total)])
            for position in range(3)
        )
    )
    shared_stack = lax.psum(shared_stack, ("dp", "tensor"))
    grad_in = grad_residual.astype(jnp.bfloat16)
    return (out_act, grad_in) + tuple(spread_stack) + tuple(shared_stack)


BAND = 256
LANES = 128
VMEM_ASKED = 60 * 2**20


def dot_nt(left, right):
    return lax.dot_general(left, right, (((1,), (1,)), ((), ())), preferred_element_type=jnp.float32)


def dot_tn(left, right):
    return lax.dot_general(left, right, (((0,), (0,)), ((), ())), preferred_element_type=jnp.float32)


def dot_low(left, right):
    return jnp.dot(left, right, preferred_element_type=jnp.float32)


UNITS_LAYER = 12
BEATS_EVERY_TICK = 18
Y_AHEAD = 2


def fill_band_bias(segk_ref, bias_ref):
    wide = segk_ref.shape[1]
    values = lax.broadcasted_iota(jnp.int32, (16, wide), 0)
    member = (values == segk_ref[...]).astype(jnp.float32).astype(jnp.bfloat16)
    for block in range(bias_ref.shape[0]):
        queries = member[:, (block + 1) * BAND : (block + 2) * BAND]
        keys = member[:, block * BAND : (block + 2) * BAND]
        row_place = lax.broadcasted_iota(jnp.int32, (BAND, 2 * BAND), 0) + BAND
        column_place = lax.broadcasted_iota(jnp.int32, (BAND, 2 * BAND), 1)
        allowed = (dot_tn(queries, keys) > 0.5) & (column_place <= row_place)
        bias_ref[block] = jnp.where(allowed, 0.0, masked_score)


def band_rows(halo, rows, block):
    if block == 0:
        return jnp.concatenate([halo, rows[0:BAND, :]], axis=0)
    return rows[(block - 1) * BAND : (block + 1) * BAND, :]


def aligned(index, size):
    return pl.ds(pl.multiple_of(index * size, size), size)


def forward_kernel(layers, block, hidden_half, *refs):
    (
        tokens_ref,
        cot_ref,
        segments_ref,
        qkv_own,
        out_own,
        up_own,
        down_own,
        qv_bias_ref,
        up_bias_ref,
        out_bias_ref,
        gain_ref,
        shift_ref,
        out_act_ref,
        cot_out,
        segk_out,
        qkv_other,
        out_other,
        up_other,
        down_other,
        act_out,
        slope_out,
        normed_two_out,
        middle_out,
        attended_out,
        proj_out,
        halo_out,
        totals_out,
        normed_out,
        resid_out,
        tokens_buf,
        segments_in,
        qv_bias_in,
        up_bias_in,
        resid,
        collected,
        normed,
        normed_two,
        proj,
        halo,
        attended,
        totals,
        act_buf,
        slope_buf,
        qkv_weight,
        out_weight,
        up_weight,
        down_weight,
        bias_buf,
        start_send,
        start_recv,
        swap_sem,
        relay_send,
        relay_recv,
        halo_send_sem,
        halo_recv_sem,
        load_sem,
        store_sem,
        pair_store_sem,
    ) = refs
    width = 2 * block
    rows_all = tokens_buf.shape[0]
    pairs_half = block // LANES
    blocks_hidden = hidden_half // block
    low = jnp.bfloat16
    place = lax.axis_index("dp")
    y = lax.axis_index("tensor")
    core = place % 2
    x = (place // 2) % 2
    z = place // 4
    z_low = z % 2
    core_partner = {"dp": place + 1 - 2 * core, "tensor": y}
    x_partner = {"dp": place + 2 - 4 * x, "tensor": y}
    y_partner = {"dp": place, "tensor": 1 - y}
    z_partner = {"dp": place + 4 - 8 * z_low, "tensor": y}
    swap_partner = {"dp": place + 1 - 2 * core, "tensor": 1 - y}
    swaps = core + y - 2 * core * y

    barrier = pltpu.get_barrier_semaphore()
    for partner in (core_partner, x_partner, y_partner, z_partner, swap_partner):
        pl.semaphore_signal(barrier, inc=1, device_id=partner, device_id_type=MESH)
    pl.semaphore_wait(barrier, 5)

    def remote(source, target, send, recv, partner):
        return pltpu.make_async_remote_copy(
            src_ref=source,
            dst_ref=target,
            send_sem=send,
            recv_sem=recv,
            device_id=partner,
            device_id_type=MESH,
        )

    def swap_copy(index, source, target):
        return remote(source, target, start_send.at[index], start_recv.at[index], swap_partner)

    def swap_start(index, source, target):
        @pl.when(swaps == 1)
        def _():
            swap_copy(index, source, target).start()

        @pl.when(swaps == 0)
        def _():
            pltpu.make_async_copy(source, target, swap_sem.at[index]).start()

    def swap_wait(index, source, target):
        @pl.when(swaps == 1)
        def _():
            swap_copy(index, source, target).wait()

        @pl.when(swaps == 0)
        def _():
            pltpu.make_async_copy(source, target, swap_sem.at[index]).wait()

    segments_copy = remote(
        segments_ref, segments_in, start_send.at[2], start_recv.at[2], core_partner
    )
    qv_copy = remote(qv_bias_ref, qv_bias_in, start_send.at[3], start_recv.at[3], y_partner)
    up_copy = remote(up_bias_ref, up_bias_in, start_send.at[4], start_recv.at[4], y_partner)

    units = layers * UNITS_LAYER

    def for_unit(unit, action):
        layer, inside = unit // UNITS_LAYER, unit % UNITS_LAYER

        @pl.when(inside < 3)
        def _():
            action(qkv_own.at[layer, inside], qkv_other.at[layer, inside])

        @pl.when(inside == 3)
        def _():
            action(out_own.at[layer], out_other.at[layer])

        @pl.when((inside >= 4) & (inside % 2 == 0))
        def _():
            cut = aligned((inside - 4) // 2, block)
            action(up_own.at[layer, :, cut], up_other.at[layer, :, cut])

        @pl.when((inside >= 4) & (inside % 2 == 1))
        def _():
            cut = aligned((inside - 4) // 2, block)
            action(down_own.at[layer, cut, :], down_other.at[layer, cut, :])

    def hop_copy(hop, unit, source, target):
        partner = (y_partner, x_partner, z_partner, core_partner)[hop]
        return remote(source, target, relay_send.at[hop, unit], relay_recv.at[hop, unit], partner)

    def piece_of(view, hop, short):
        rows = view.shape[0]
        if hop == 3:
            return view.at[aligned(core, rows // 2)]
        if hop == 2:
            return view.at[aligned(2 * core + z_low, rows // 4)]
        if short:
            return view.at[aligned(4 * core + 2 * z_low + x, rows // 8)]
        return view.at[aligned(2 * core + x, rows // 4)]

    def by_length(unit, hop, action):
        if hop == 3:
            action(False)
            return

        @pl.when(unit % 3 != 0)
        def _():
            action(True)

        if hop < 2:

            @pl.when(unit % 3 == 0)
            def _():
                action(False)

    def hop_start(hop, unit):
        def go(own, other):
            def one(short):
                source = piece_of(own if hop == 0 else other, hop, short)
                hop_copy(hop, unit, source, piece_of(other, hop, short)).start()

            by_length(unit, hop, one)

        for_unit(unit, go)

    def hop_wait(hop, unit):
        def one(short):
            piece = piece_of(down_other.at[0, pl.ds(0, block), :], hop, short)
            hop_copy(hop, unit, piece, piece).wait()

        by_length(unit, hop, one)

    def when_unit(unit, action):
        @pl.when((unit >= 0) & (unit < units))
        def _():
            action(unit)

    def beat(b):
        def after_y(unit):
            hop_wait(0, unit)
            hop_start(1, unit)

        def after_x(unit):
            hop_wait(1, unit)
            hop_start(2, unit)

        def after_z(unit):
            hop_wait(2, unit)
            hop_start(3, unit)

        when_unit(b + Y_AHEAD, lambda unit: hop_start(0, unit))
        when_unit(b - 1, after_y)
        when_unit(b - 2, after_x)
        when_unit(b - 3, after_z)
        when_unit(b - 4, lambda unit: hop_wait(3, unit))

    other_step = 3 + pairs_half
    out_step = other_step + 1 + pairs_half
    norm_two_step = out_step + 1
    ffn_step = norm_two_step + 1
    end_step = ffn_step + 2 * blocks_hidden
    period = end_step + 1
    jobs = layers * period

    def loads(kind, slot, *sources):
        targets = {
            "qkv": (qkv_weight,),
            "out": (out_weight.at[0], out_weight.at[1]),
            "ffn": (up_weight.at[slot], down_weight.at[slot]),
        }[kind]
        sources = sources or targets
        return [
            pltpu.make_async_copy(source, target, load_sem.at[slot, index])
            for index, (source, target) in enumerate(zip(sources, targets))
        ]

    def start_all(copies):
        for copy in copies:
            copy.start()

    def wait_all(copies):
        for copy in copies:
            copy.wait()

    def prefetch(t):
        slot = t % 2
        layer, step = t // period, t % period
        for at, source in ((1, qkv_own), (other_step, qkv_other)):

            @pl.when(step == at)
            def _(source=source):
                start_all(loads("qkv", slot, source.at[layer]))

        @pl.when(step == out_step)
        def _():
            start_all(loads("out", slot, out_own.at[layer], out_other.at[layer]))

        for which, (up_ref, down_ref) in enumerate(((up_own, down_own), (up_other, down_other))):
            begin = ffn_step + which * blocks_hidden

            @pl.when((step >= begin) & (step < begin + blocks_hidden))
            def _(begin=begin, up_ref=up_ref, down_ref=down_ref):
                cut = aligned(step - begin, block)
                start_all(loads("ffn", slot, up_ref.at[layer, :, cut], down_ref.at[layer, cut, :]))

    tiles = [slice(r, r + BAND) for r in range(0, rows_all, BAND)]
    fine_tiles = [slice(r, r + LANES) for r in range(0, rows_all, LANES)]

    def normalize(layer, index, target):
        gain = gain_ref[pl.ds(2 * layer + index, 1), :]
        shift = shift_ref[pl.ds(2 * layer + index, 1), :]
        for tile in fine_tiles:
            values, _, _ = layer_norm(resid[tile, :], gain, shift)
            target[tile, :] = values.astype(low)

    def store(index, source, target):
        return pltpu.make_async_copy(source, target, store_sem.at[index])

    def first_stores(layer):
        return [store(0, resid, resid_out.at[layer]), store(1, normed, normed_out.at[layer])]

    def proj_stores(layer, which):
        return [
            store(
                2 + 3 * which + third,
                proj.at[which, third],
                proj_out.at[layer, which, :, pl.ds(third * block, block)],
            )
            for third in range(3)
        ]

    def halo_store(layer, which):
        return store(8 + which, halo.at[layer, which], halo_out.at[layer, which])

    def attended_stores(layer, which):
        return [
            store(10 + which, attended.at[which], attended_out.at[layer, which]),
            store(12 + which, totals.at[which], totals_out.at[layer, which]),
        ]

    def second_stores(layer):
        return [
            store(14, resid, middle_out.at[layer]),
            store(15, normed_two, normed_two_out.at[layer]),
        ]

    def ffn_stores(layer, index, slot):
        which, inside = index // blocks_hidden, index % blocks_hidden
        cut = aligned(inside, block)
        return [
            pltpu.make_async_copy(
                buf.at[slot], out.at[layer, which, :, cut], pair_store_sem.at[slot, kind]
            )
            for kind, (buf, out) in enumerate(((act_buf, act_out), (slope_buf, slope_out)))
        ]

    def halo_copy(layer, which):
        return remote(
            proj.at[which, pl.ds(1, 2), pl.ds(rows_all - BAND, BAND)],
            halo.at[layer, which],
            halo_send_sem.at[layer, which],
            halo_recv_sem.at[layer, which],
            core_partner,
        )

    def first_job(layer):
        normalize(layer, 0, normed)
        start_all(first_stores(layer))

    def qkv_job(layer, which, slot):
        wait_all(loads("qkv", slot))
        bias = qv_bias_in if which else qv_bias_ref
        for third in range(3):
            for tile in tiles:
                product = dot_low(normed[tile, :], qkv_weight[third])
                if third != 1:
                    product = product + bias[pl.ds(2 * layer + third // 2, 1), :]
                proj[which, third, tile, :] = product.astype(low)

        @pl.when(core == 0)
        def _():
            halo_copy(layer, which).start()

        start_all(proj_stores(layer, which))

    def attention_job(layer, which, pair):
        @pl.when(pair == 0)
        def _():
            @pl.when(core == 0)
            def _():
                halo_copy(layer, which).wait_send()

            @pl.when(core == 1)
            def _():
                halo_copy(layer, which).wait_recv()

            halo_store(layer, which).start()
            totals[which] = jnp.zeros_like(totals[which])

        lane = lax.broadcasted_iota(jnp.int32, (BAND, LANES), 1)
        here = aligned(pair, LANES)
        for index, tile in enumerate(tiles):
            query = proj[which, 0, tile, here]
            keys = band_rows(halo[layer, which, 0, :, here], proj[which, 1, :, here], index)
            values = band_rows(halo[layer, which, 1, :, here], proj[which, 2, :, here], index)
            parts = []
            kept = totals[which, tile, :]
            for head in range(2):
                mine = (lane // HEAD_DIM) == head
                scores = (
                    dot_nt(jnp.where(mine, query, 0), keys) * HEAD_DIM ** (-0.5) + bias_buf[index]
                )
                highest = jnp.max(scores, axis=-1, keepdims=True)
                raised = jnp.exp(scores - highest)
                summed = jnp.sum(raised, axis=-1, keepdims=True)
                parts.append(dot_low(raised.astype(low), values) / summed)
                kept = jnp.where(lane == 2 * pair + head, highest + jnp.log(summed), kept)
            totals[which, tile, :] = kept
            attended[which, tile, here] = jnp.where(lane < HEAD_DIM, parts[0], parts[1]).astype(low)

        @pl.when(pair == pairs_half - 1)
        def _():
            start_all(attended_stores(layer, which))

    def out_job(layer, slot):
        wait_all(loads("out", slot))
        wait_all(first_stores(layer))
        for which in range(2):
            wait_all(proj_stores(layer, which))
            halo_store(layer, which).wait()
        bias = out_bias_ref[pl.ds(2 * layer, 1), :]
        for tile in tiles:
            branch = dot_low(attended[0, tile, :], out_weight[0])
            branch = branch + dot_low(attended[1, tile, :], out_weight[1])
            resid[tile, :] = resid[tile, :] + branch + bias

    def second_job(layer):
        normalize(layer, 1, normed_two)
        start_all(second_stores(layer))

    def ffn_job(layer, which, inside, slot):
        index = which * blocks_hidden + inside
        wait_all(loads("ffn", slot))

        @pl.when(index >= 2)
        def _():
            wait_all(ffn_stores(layer, index - 2, slot))

        bias = (up_bias_in if which else up_bias_ref)[pl.ds(layer, 1), aligned(inside, block)]
        for tile in tiles:
            before = dot_low(normed_two[tile, :], up_weight[slot]) + bias
            square = before * before
            tangent = jnp.tanh(gelu_coeff * before * (1.0 + cubic_coeff * square))
            raised = 0.5 * (1.0 + tangent)
            activated = (before * raised).astype(low)
            act_buf[slot, tile, :] = activated
            slope_buf[slot, tile, :] = (
                raised
                + 0.5
                * before
                * (1.0 - tangent * tangent)
                * gelu_coeff
                * (1.0 + 3.0 * cubic_coeff * square)
            ).astype(low)
            product = dot_low(activated, down_weight[slot])
            if which:
                collected[tile, :] = collected[tile, :] + product
                continue

            @pl.when(inside == 0)
            def _(tile=tile, product=product):
                collected[tile, :] = product

            @pl.when(inside > 0)
            def _(tile=tile, product=product):
                collected[tile, :] = collected[tile, :] + product

        start_all(ffn_stores(layer, index, slot))

    def end_job(layer, slot):
        wait_all(ffn_stores(layer, 2 * blocks_hidden - 2, slot))
        wait_all(ffn_stores(layer, 2 * blocks_hidden - 1, 1 - slot))
        wait_all(second_stores(layer))
        for which in range(2):
            wait_all(attended_stores(layer, which))
        bias = out_bias_ref[pl.ds(2 * layer + 1, 1), :]
        for tile in tiles:
            resid[tile, :] = resid[tile, :] + collected[tile, :] + bias

    def job(t):
        slot = t % 2
        layer, step = t // period, t % period

        def at(first, count, action):
            @pl.when((step >= first) & (step < first + count))
            def _():
                action(step - first)

        at(0, 1, lambda _: first_job(layer))
        at(1, 1, lambda _: qkv_job(layer, 0, slot))
        at(2, pairs_half, lambda pair: attention_job(layer, 0, pair))
        at(other_step, 1, lambda _: qkv_job(layer, 1, slot))
        at(other_step + 1, pairs_half, lambda pair: attention_job(layer, 1, pair))
        at(out_step, 1, lambda _: out_job(layer, slot))
        at(norm_two_step, 1, lambda _: second_job(layer))
        at(ffn_step, blocks_hidden, lambda inside: ffn_job(layer, 0, inside, slot))
        at(ffn_step + blocks_hidden, blocks_hidden, lambda inside: ffn_job(layer, 1, inside, slot))
        at(end_step, 1, lambda _: end_job(layer, slot))

    swap_start(0, tokens_ref, tokens_buf)
    halo[...] = jnp.zeros_like(halo)
    segments_copy.start()
    qv_copy.start()
    up_copy.start()
    for unit in range(Y_AHEAD):
        hop_start(0, unit)
    segments_copy.wait()
    window = jnp.where(core == y, segments_ref[...], segments_in[...])

    @pl.when(core == 0)
    def _():
        segk_out[:, 0:BAND] = jnp.full((1, BAND), -1, jnp.int32)
        segk_out[:, BAND:] = window[:, 0:rows_all]

    @pl.when(core == 1)
    def _():
        segk_out[...] = window[:, rows_all - BAND :]

    fill_band_bias(segk_out, bias_buf)
    qv_copy.wait()
    up_copy.wait()
    swap_wait(0, tokens_ref, tokens_buf)
    for tile in tiles:
        resid[tile, :] = tokens_buf[tile, :].astype(jnp.float32)
    cot_tick = BEATS_EVERY_TICK + 6

    def tick(t, carry):
        @pl.when(t <= BEATS_EVERY_TICK)
        def _():
            beat(t)

        late = t - BEATS_EVERY_TICK

        @pl.when((late > 0) & (late % 2 == 0))
        def _():
            beat(BEATS_EVERY_TICK + late // 2)

        @pl.when(t == cot_tick)
        def _():
            swap_start(1, cot_ref, cot_out)

        @pl.when(t + 1 < jobs)
        def _():
            prefetch(t + 1)

        job(t)
        return carry

    lax.fori_loop(0, jobs, tick, 0)
    for tile in tiles:
        normed_two[tile, :] = resid[tile, :].astype(low)
    last_store = store(0, normed_two, out_act_ref)
    last_store.start()
    last_store.wait()
    swap_wait(1, cot_ref, cot_out)


def run_forward(tokens, cotangent, segments, weights, biases, out_bias, gain, shift, block):
    rows, width = tokens.shape
    layers, hidden_half = weights[-1].shape[0], weights[-1].shape[1]
    low, wide = jnp.bfloat16, jnp.float32
    anywhere = pl.BlockSpec(memory_space=pl.ANY)
    in_vmem = pl.BlockSpec(memory_space=pltpu.VMEM)
    vmem = pltpu.VMEM
    units = layers * UNITS_LAYER
    shape = jax.ShapeDtypeStruct
    saved = [
        shape((layers, 2, rows, hidden_half), low),
        shape((layers, 2, rows, hidden_half), low),
        shape((layers, rows, width), low),
        shape((layers, rows, width), wide),
        shape((layers, 2, rows, block), low),
        shape((layers, 2, rows, 3 * block), low),
        shape((layers, 2, 2, BAND, block), low),
        shape((layers, 2, rows, LANES), wide),
        shape((layers, rows, width), low),
        shape((layers, rows, width), wide),
    ]
    others = [shape(member.shape, low) for member in weights]
    return pl.pallas_call(
        functools.partial(forward_kernel, layers, block, hidden_half),
        in_specs=[anywhere] * 2 + [in_vmem] + [anywhere] * 4 + [in_vmem] * 5,
        out_specs=[anywhere] * 2 + [in_vmem] + [anywhere] * (len(others) + len(saved)),
        out_shape=[
            shape((rows, width), low),
            shape((rows, width), low),
            shape((1, rows + BAND), jnp.int32),
        ]
        + others
        + saved,
        scratch_shapes=[
            vmem((rows, width), low),
            vmem(segments.shape, jnp.int32),
            vmem(biases[0].shape, wide),
            vmem(biases[1].shape, wide),
            vmem((rows, width), wide),
            vmem((rows, width), wide),
            vmem((rows, width), low),
            vmem((rows, width), low),
            vmem((2, 3, rows, block), low),
            vmem((layers, 2, 2, BAND, block), low),
            vmem((2, rows, block), low),
            vmem((2, rows, LANES), wide),
            vmem((2, rows, block), low),
            vmem((2, rows, block), low),
            vmem((3, width, block), low),
            vmem((2, block, width), low),
            vmem((2, width, block), low),
            vmem((2, block, width), low),
            vmem((rows // BAND, BAND, 2 * BAND), wide),
            pltpu.SemaphoreType.DMA((5,)),
            pltpu.SemaphoreType.DMA((5,)),
            pltpu.SemaphoreType.DMA((2,)),
            pltpu.SemaphoreType.DMA((4, units)),
            pltpu.SemaphoreType.DMA((4, units)),
            pltpu.SemaphoreType.DMA((layers, 2)),
            pltpu.SemaphoreType.DMA((layers, 2)),
            pltpu.SemaphoreType.DMA((2, 2)),
            pltpu.SemaphoreType.DMA((16,)),
            pltpu.SemaphoreType.DMA((2, 2)),
        ],
        compiler_params=pltpu.CompilerParams(
            collective_id=1, has_side_effects=True, vmem_limit_bytes=VMEM_ASKED
        ),
        name="forward",
    )(tokens, cotangent, segments, *weights, *biases, out_bias, gain, shift)


SLOTS = 8
CORE_SLOTS = 4
RESULT_SLOTS = 11
STAGED = 2
FIRST = 2
LAGS = dict(
    core=1, first=3, second=5, third=7, fourth=9, fifth=11, sixth=13, whole=14, stored=15
)
VECTOR_STEP = 3
VECTOR_ROWS = 12
MESH = pl.DeviceIdType.MESH
FFN_STEPS = 4
QKV_STEPS = 3


def added(left, right):
    return (left.astype(jnp.float32) + right.astype(jnp.float32)).astype(jnp.bfloat16)


def backward_kernel(layers, block, hidden_half, *refs):
    (
        cot_ref,
        gain_ref,
        segk_ref,
        out_act_ref,
        act_ref,
        slope_ref,
        normed_two_ref,
        middle_ref,
        attended_ref,
        proj_ref,
        halo_ref,
        totals_ref,
        normed_ref,
        resid_ref,
        qkv_own,
        qkv_other,
        out_own,
        out_other,
        up_own,
        up_other,
        down_own,
        down_other,
        out_act_out,
        grad_in_ref,
        out_down,
        out_up,
        out_out,
        out_qkv,
        vector_out,
        grad_branch,
        grad_attn,
        grad_before,
        grad_proj,
        grad_res,
        collected,
        grad_attended,
        qkv_buf,
        halo_buf,
        totals_buf,
        kept_kv,
        halo_send,
        halo_in,
        rows_weight,
        columns_weight,
        slope_buf,
        wide_buf,
        bias_buf,
        sums_buf,
        pair_buf,
        one_buf,
        part_buf,
        core_in,
        sent,
        held,
        kept,
        first_in,
        second_in,
        third_in,
        result,
        vec_in,
        load_sem,
        io_sem,
        halo_send_sem,
        halo_recv_sem,
        staged_sem,
        send_sems,
        recv_sems,
        store_sem,
        vec_send,
        vec_recv,
        swap_send,
        swap_recv,
    ) = refs
    half, quarter = block // 2, block // 4
    width = 2 * block
    rows_all = grad_branch.shape[0]
    pairs_half = block // LANES
    pairs = 2 * pairs_half
    low = jnp.bfloat16
    place = lax.axis_index("dp")
    y = lax.axis_index("tensor")
    core = place % 2
    x = (place // 2) % 2
    z = place // 4
    z_low = z % 2
    inner = (z + 1) // 2 % 2
    core_partner = {"dp": place + 1 - 2 * core, "tensor": y}
    x_partner = {"dp": place + 2 - 4 * x, "tensor": y}
    y_partner = {"dp": place, "tensor": 1 - y}
    z_partner = {"dp": place + 4 - 8 * z_low, "tensor": y}
    middle_partner = {"dp": place + 4 * (3 - 2 * z), "tensor": y}
    swap_partner = {"dp": place + 1 - 2 * core, "tensor": 1 - y}

    barrier = pltpu.get_barrier_semaphore()
    for partner in (core_partner, x_partner, y_partner, z_partner, swap_partner):
        pl.semaphore_signal(barrier, inc=1, device_id=partner, device_id_type=MESH)

    @pl.when(inner == 1)
    def _():
        pl.semaphore_signal(barrier, inc=1, device_id=middle_partner, device_id_type=MESH)
        pl.semaphore_wait(barrier, 6)

    @pl.when(inner == 0)
    def _():
        pl.semaphore_wait(barrier, 5)

    blocks_hidden = hidden_half // block
    plan = (
        ("rows", blocks_hidden, 2),
        ("columns", 2, blocks_hidden),
        ("rows", 1, 2),
        ("columns", 2, 3),
    )
    starts = []
    per_layer = 0
    for _, down_count, across_count in plan:
        starts.append(per_layer)
        per_layer += down_count * across_count
    chunks = layers * per_layer
    out_refs = (out_down, out_up, out_out, out_qkv)

    def block_of(index):
        return pl.ds(pl.multiple_of(index * block, block), block)

    def for_matrix(chunk, action):
        layer = layers - 1 - chunk // per_layer
        inside = chunk % per_layer
        for member, (_, down_count, across_count) in enumerate(plan):
            begin = starts[member]

            @pl.when((inside >= begin) & (inside < begin + down_count * across_count))
            def _(member=member, begin=begin, across_count=across_count):
                local = inside - begin
                action(member, layer, local // across_count, local % across_count)

    def operands_of(member, layer, i, j):
        if member == 0:
            return (
                grad_branch.at[:, block_of(j)],
                act_ref.at[layer, 0, :, block_of(i)],
                act_ref.at[layer, 1, :, block_of(i)],
            )
        if member == 1:
            return (
                normed_two_ref.at[layer, :, block_of(i)],
                grad_before.at[j // 2, :, block_of(j % 2)],
                grad_before.at[blocks_hidden // 2 + j // 2, :, block_of(j % 2)],
            )
        if member == 2:
            return (
                grad_attn.at[:, block_of(j)],
                attended_ref.at[layer, 0, :, block_of(i)],
                attended_ref.at[layer, 1, :, block_of(i)],
            )
        return (
            normed_ref.at[layer, :, block_of(i)],
            grad_proj.at[:, block_of(j)],
            grad_proj.at[:, block_of(3 + j)],
        )

    def staged_copies(chunk, shared, own, other):
        slot = chunk % STAGED
        return (
            pltpu.make_async_copy(own, pair_buf.at[slot, 0], staged_sem.at[slot, 0]),
            pltpu.make_async_copy(other, pair_buf.at[slot, 1], staged_sem.at[slot, 1]),
            pltpu.make_async_copy(shared, one_buf.at[slot], staged_sem.at[slot, 2]),
        )

    def stage_operands(chunk):
        def action(member, layer, i, j):
            for copy in staged_copies(chunk, *operands_of(member, layer, i, j)):
                copy.start()

        for_matrix(chunk, action)

    def remote(step, chunk, source, target, partner):
        slot = chunk % SLOTS
        return pltpu.make_async_remote_copy(
            src_ref=source,
            dst_ref=target,
            send_sem=send_sems.at[step, slot],
            recv_sem=recv_sems.at[step, slot],
            device_id=partner,
            device_id_type=MESH,
        )

    def x_first(chunk):
        return ((3 * chunk) % 8 < 3) | (chunk >= chunks - 1)

    def core_copy(chunk):
        return remote(
            0,
            chunk,
            part_buf.at[chunk % STAGED, :, aligned(1 - core, half)],
            core_in.at[chunk % CORE_SLOTS],
            core_partner,
        )

    low_middle = z - 1
    far_middle = 2 - z

    def first_copy(chunk, partner):
        slot = chunk % SLOTS
        return remote(1, chunk, sent.at[slot], first_in.at[slot], partner)

    def y_copy(chunk):
        slot = chunk % SLOTS
        return remote(2, chunk, kept.at[slot, 1], second_in.at[slot, 0], y_partner)

    def pair_copy(chunk):
        slot = chunk % SLOTS
        return remote(2, chunk, kept.at[slot], second_in.at[slot], z_partner)

    def single_copy(chunk):
        slot = chunk % SLOTS
        return remote(3, chunk, kept.at[slot, 0], third_in.at[slot, 0], z_partner)

    def split_copy(chunk):
        slot = chunk % SLOTS
        return remote(3, chunk, kept.at[slot, far_middle], third_in.at[slot, 0], middle_partner)

    def middle_copy(chunk):
        slot = chunk % SLOTS
        return remote(4, chunk, kept.at[slot, 0], third_in.at[slot, 1], middle_partner)

    def across_copy(chunk):
        slot = chunk % SLOTS
        return remote(4, chunk, kept.at[slot, low_middle], third_in.at[slot, 1], x_partner)

    def result_copy(step, chunk, rows, partner):
        piece = result.at[chunk % RESULT_SLOTS, rows]
        return remote(step, chunk, piece, piece, partner)

    x_rows = aligned(2 * core + x, quarter)
    core_rows = aligned(core, half)

    def middle_rows():
        return aligned(2 * core + low_middle, quarter)

    def store_copy(chunk, target):
        slot = chunk % RESULT_SLOTS
        return pltpu.make_async_copy(result.at[slot], target, store_sem.at[slot])

    def multiply(chunk):
        slot = chunk % STAGED
        for copy in staged_copies(chunk, one_buf.at[slot], pair_buf.at[slot, 0], pair_buf.at[slot, 1]):
            copy.wait()
        inside = chunk % per_layer
        by_rows = (inside < starts[1]) | ((inside >= starts[2]) & (inside < starts[3]))

        @pl.when(by_rows)
        def _():
            single = one_buf[slot]
            for which in range(2):
                part_buf[slot, which] = dot_tn(pair_buf[slot, which], single).astype(low)

        @pl.when(jnp.logical_not(by_rows))
        def _():
            single = one_buf[slot]
            for which in range(2):
                part_buf[slot, which] = dot_tn(single, pair_buf[slot, which]).astype(low)

        core_copy(chunk).start()

    def branch(chunk, by_x, by_y):
        is_x = x_first(chunk)

        @pl.when(is_x)
        def _():
            by_x()

        @pl.when(jnp.logical_not(is_x))
        def _():
            by_y()

    def on_middle(action):
        @pl.when(inner == 1)
        def _():
            action()

    def by_place(at_end, at_middle):
        @pl.when(inner == 0)
        def _():
            at_end()

        on_middle(at_middle)

    def after_core(chunk):
        slot, core_slot, part_slot = chunk % SLOTS, chunk % CORE_SLOTS, chunk % STAGED
        core_copy(chunk).wait()
        is_x = x_first(chunk).astype(jnp.int32)

        def summed(which, row):
            near = part_buf[part_slot, which, aligned(2 * core + row, quarter), :]
            return added(near, core_in[core_slot, which, aligned(row, quarter), :])

        for index in range(2):
            sent[slot, index] = summed(
                is_x * index + (1 - is_x), is_x * (1 - x) + (1 - is_x) * index
            )
        branch(
            chunk,
            lambda: first_copy(chunk, x_partner).start(),
            lambda: first_copy(chunk, y_partner).start(),
        )
        for index in range(2):
            held[slot, index] = summed(is_x * index, is_x * x + (1 - is_x) * index)

    def after_first(chunk):
        slot = chunk % SLOTS
        first_copy(chunk, y_partner).wait()
        for index in (1, 0):
            kept[slot, index] = added(held[slot, index], first_in[slot, index])

        def by_y():
            @pl.when(inner == 0)
            def _():
                pair_copy(chunk).start()

        branch(chunk, lambda: y_copy(chunk).start(), by_y)

    def after_second(chunk):
        slot = chunk % SLOTS

        def by_x():
            y_copy(chunk).wait()
            kept[slot, 0] = added(kept[slot, 0], second_in[slot, 0])

            @pl.when(inner == 0)
            def _():
                single_copy(chunk).start()

        def at_middle():
            pair_copy(chunk).wait_recv()
            kept[slot, far_middle] = added(kept[slot, far_middle], second_in[slot, far_middle])
            split_copy(chunk).start()
            kept[slot, low_middle] = added(kept[slot, low_middle], second_in[slot, low_middle])

        branch(chunk, by_x, lambda: by_place(lambda: pair_copy(chunk).wait_send(), at_middle))

    def after_third(chunk):
        slot = chunk % SLOTS

        def one_at_middle():
            single_copy(chunk).wait_recv()
            kept[slot, 0] = added(kept[slot, 0], third_in[slot, 0])
            middle_copy(chunk).start()

        def by_y():
            split_copy(chunk).wait()
            kept[slot, low_middle] = added(kept[slot, low_middle], third_in[slot, 0])
            across_copy(chunk).start()

        branch(
            chunk,
            lambda: by_place(lambda: single_copy(chunk).wait_send(), one_at_middle),
            lambda: on_middle(by_y),
        )

    def after_fourth(chunk):
        slot, result_slot = chunk % SLOTS, chunk % RESULT_SLOTS

        def by_x():
            middle_copy(chunk).wait()
            result[result_slot, x_rows, :] = added(kept[slot, 0], third_in[slot, 1])
            result_copy(5, chunk, x_rows, z_partner).start()

        def by_y():
            across_copy(chunk).wait()
            result[result_slot, middle_rows(), :] = added(
                kept[slot, low_middle], third_in[slot, 1]
            )
            result_copy(5, chunk, middle_rows(), middle_partner).start()

        branch(chunk, lambda: on_middle(by_x), lambda: on_middle(by_y))

    def after_fifth(chunk):
        def by_x():
            back = result_copy(5, chunk, x_rows, z_partner)
            by_place(back.wait_recv, back.wait_send)
            result_copy(6, chunk, x_rows, x_partner).start()

        def by_y():
            result_copy(5, chunk, middle_rows(), middle_partner).wait()
            result_copy(6, chunk, core_rows, z_partner).start()

        branch(chunk, by_x, lambda: on_middle(by_y))

    def after_sixth(chunk):
        def by_y():
            back = result_copy(6, chunk, core_rows, z_partner)
            by_place(back.wait_recv, back.wait_send)

        branch(chunk, lambda: result_copy(6, chunk, x_rows, x_partner).wait(), by_y)
        result_copy(7, chunk, core_rows, core_partner).start()

    def after_whole(chunk):
        result_copy(7, chunk, core_rows, core_partner).wait()

        def action(member, layer, i, j):
            if member == 3:
                target = out_qkv.at[layer, j, block_of(i)]
            else:
                target = out_refs[member].at[layer, block_of(i), block_of(j)]
            store_copy(chunk, target).start()

        for_matrix(chunk, action)

    def after_store(chunk):
        store_copy(chunk, result.at[chunk % RESULT_SLOTS]).wait()

    vector_partners = (core_partner, y_partner, x_partner, z_partner, middle_partner, z_partner)

    def vector_copy(step):
        target = vec_in.at[min(step, 4)]
        return pltpu.make_async_remote_copy(
            src_ref=vector_out,
            dst_ref=target,
            send_sem=vec_send.at[step],
            recv_sem=vec_recv.at[step],
            device_id=vector_partners[step],
            device_id_type=MESH,
        )

    def add_vector(step):
        vector_out[...] = vector_out[...] + vec_in[step]

    def vector_tick(step):
        if step == 0:
            vector_copy(0).start()
        elif step <= 3:
            vector_copy(step - 1).wait()
            add_vector(step - 1)
            if step < 3:
                vector_copy(step).start()
            else:

                @pl.when(inner == 0)
                def _():
                    vector_copy(3).start()

        elif step == 4:

            @pl.when(inner == 0)
            def _():
                vector_copy(3).wait_send()

            @pl.when(inner == 1)
            def _():
                vector_copy(3).wait_recv()
                add_vector(3)
                vector_copy(4).start()

        elif step == 5:

            @pl.when(inner == 1)
            def _():
                vector_copy(4).wait()
                add_vector(4)
                vector_copy(5).start()

        else:

            @pl.when(inner == 1)
            def _():
                vector_copy(5).wait_send()

            @pl.when(inner == 0)
            def _():
                vector_copy(5).wait_recv()
                vector_out[...] = vec_in[4]

    norm_two_step = FFN_STEPS
    out_step = norm_two_step + 1
    attention_step = out_step + 1
    qkv_step = attention_step + pairs + 1
    norm_one_step = qkv_step + QKV_STEPS
    period = norm_one_step + 1
    jobs = layers * period
    hidden_step = 2 * hidden_half // FFN_STEPS

    def loads(kind, slot, *sources):
        targets = {
            "ffn": (rows_weight.at[slot], columns_weight.at[slot], slope_buf.at[slot]),
            "wide": (wide_buf,),
            "out": (rows_weight.at[slot, pl.ds(0, block)], rows_weight.at[slot, pl.ds(block, block)]),
            "attention": (
                qkv_buf.at[slot, 0],
                qkv_buf.at[slot, 1],
                qkv_buf.at[slot, 2],
                halo_buf.at[slot, 0],
                halo_buf.at[slot, 1],
                totals_buf.at[slot],
            ),
            "qkv": (
                columns_weight.at[slot, :, pl.ds(0, block)],
                columns_weight.at[slot, :, pl.ds(block, block)],
            ),
        }[kind]
        sources = sources or targets
        return [
            pltpu.make_async_copy(source, target, load_sem.at[slot, index])
            for index, (source, target) in enumerate(zip(sources, targets))
        ]

    def prefetch(t):
        slot = t % 2
        layer = layers - 1 - t // period
        step = t % period

        for which, (up_ref, down_ref) in enumerate(((up_own, down_own), (up_other, down_other))):

            @pl.when((step < FFN_STEPS) & (step // (FFN_STEPS // 2) == which))
            def _(which=which, up_ref=up_ref, down_ref=down_ref):
                cut = aligned(step % (FFN_STEPS // 2), hidden_step)
                for copy in loads(
                    "ffn",
                    slot,
                    down_ref.at[layer, cut, :],
                    up_ref.at[layer, :, cut],
                    slope_ref.at[layer, which, :, cut],
                ):
                    copy.start()

        for at, source in ((norm_two_step, middle_ref), (norm_one_step, resid_ref)):

            @pl.when(step == at)
            def _(source=source):
                for copy in loads("wide", slot, source.at[layer]):
                    copy.start()

        @pl.when(step == out_step)
        def _():
            for copy in loads("out", slot, out_own.at[layer], out_other.at[layer]):
                copy.start()

        @pl.when((step >= attention_step) & (step < attention_step + pairs))
        def _():
            pair = step - attention_step
            which, inside = pair // pairs_half, pair % pairs_half

            def lanes(third):
                return aligned(third * pairs_half + inside, LANES)

            for copy in loads(
                "attention",
                slot,
                *[proj_ref.at[layer, which, :, lanes(third)] for third in range(3)],
                *[halo_ref.at[layer, which, third, :, lanes(0)] for third in range(2)],
                totals_ref.at[layer, which],
            ):
                copy.start()

        @pl.when((step >= qkv_step) & (step < qkv_step + QKV_STEPS))
        def _():
            for part in range(2):
                index = 2 * (step - qkv_step) + part
                for which, source in enumerate((qkv_own, qkv_other)):

                    @pl.when(index // 3 == which)
                    def _(part=part, index=index, source=source):
                        pltpu.make_async_copy(
                            source.at[layer, index % 3],
                            columns_weight.at[slot, :, pl.ds(part * block, block)],
                            load_sem.at[slot, part],
                        ).start()

    def wait_loads(kind, slot):
        for copy in loads(kind, slot):
            copy.wait()

    tiles = [slice(r, r + BAND) for r in range(0, rows_all, BAND)]
    fine_tiles = [slice(r, r + LANES) for r in range(0, rows_all, LANES)]

    def vector_row(layer, row):
        return pl.ds(layer * VECTOR_ROWS + row, 1)

    def column_sum(values):
        return jnp.sum(values.astype(jnp.float32), axis=0, keepdims=True)

    def ffn_job(layer, step, slot):
        wait_loads("ffn", slot)
        sums = 0.0
        for tile in tiles:
            grad_hidden = dot_nt(grad_branch[tile, :], rows_weight[slot])
            before = (grad_hidden * slope_buf[slot, tile, :].astype(jnp.float32)).astype(low)
            grad_before[step, tile, :] = before
            sums = sums + column_sum(before)
            product = dot_nt(before, columns_weight[slot])

            @pl.when(step == 0)
            def _(tile=tile, product=product):
                collected[tile, :] = product

            @pl.when(step > 0)
            def _(tile=tile, product=product):
                collected[tile, :] = collected[tile, :] + product

        per_half = FFN_STEPS // 2
        which = step // per_half
        owner = which + y - 2 * which * y
        vector_out[vector_row(layer, 2 + owner * per_half + step % per_half), :] = sums

    def norm_job(layer, index, slot):
        wait_loads("wide", slot)
        gain = gain_ref[pl.ds(2 * layer + index, 1), :]
        gain_sum, shift_sum, attn_sum, branch_sum = 0.0, 0.0, 0.0, 0.0
        for tile in fine_tiles:
            incoming = collected[tile, :]
            values = wide_buf[tile, :]
            average = jnp.mean(values, axis=-1, keepdims=True)
            centred = values - average
            inverse = lax.rsqrt(jnp.mean(centred * centred, axis=-1, keepdims=True) + epsilon)
            unit = centred * inverse
            scaled = incoming * gain
            first_mean = jnp.mean(scaled, axis=-1, keepdims=True)
            second_mean = jnp.mean(scaled * unit, axis=-1, keepdims=True)
            total = grad_res[tile, :] + inverse * (scaled - first_mean - unit * second_mean)
            grad_res[tile, :] = total
            rounded = total.astype(low)
            gain_sum = gain_sum + column_sum(incoming * unit)
            shift_sum = shift_sum + column_sum(incoming)
            if index == 1:
                attn_sum = attn_sum + column_sum(rounded)
                branch_sum = branch_sum + column_sum(grad_branch[tile, :])
                grad_attn[tile, :] = rounded
            else:
                grad_branch[tile, :] = rounded
        vector_out[vector_row(layer, 8 + index), :] = gain_sum
        vector_out[vector_row(layer, 10 + index), :] = shift_sum
        if index == 1:
            vector_out[vector_row(layer, 6), :] = attn_sum
            vector_out[vector_row(layer, 7), :] = branch_sum

    def out_job(slot):
        wait_loads("out", slot)
        for tile in tiles:
            grad_attended[tile, :] = dot_nt(grad_attn[tile, :], rows_weight[slot]).astype(low)

    def halo_copy(pair):
        return pltpu.make_async_remote_copy(
            src_ref=halo_send.at[pair % 2],
            dst_ref=halo_in.at[pair],
            send_sem=halo_send_sem.at[pair],
            recv_sem=halo_recv_sem.at[pair],
            device_id=core_partner,
            device_id_type=MESH,
        )

    def proj_lanes(pair, third):
        which, inside = pair // pairs_half, pair % pairs_half
        return aligned(which * 3 * pairs_half + third * pairs_half + inside, LANES)

    def attention_job(pair, slot):
        wait_loads("attention", slot)
        lane = lax.broadcasted_iota(jnp.int32, (BAND, LANES), 1)
        scaling = HEAD_DIM ** (-0.5)
        count = len(tiles)
        key_parts = [None] * (count + 1)
        value_parts = [None] * (count + 1)
        here = aligned(pair, LANES)
        for index, tile in enumerate(tiles):
            query = qkv_buf[slot, 0, tile, :]
            grad = grad_attended[tile, here]
            keys = band_rows(halo_buf[slot, 0], qkv_buf[slot, 1], index)
            values = band_rows(halo_buf[slot, 1], qkv_buf[slot, 2], index)
            grad_query = []
            grad_keys = 0.0
            grad_values = 0.0
            for head in range(2):
                mine = (lane // HEAD_DIM) == head
                query_head = jnp.where(mine, query, 0)
                grad_head = jnp.where(mine, grad, 0)
                scores = dot_nt(query_head, keys) * scaling + bias_buf[index]
                total = jnp.sum(
                    jnp.where(
                        lane == 2 * (pair % pairs_half) + head, totals_buf[slot, tile, :], 0.0
                    ),
                    axis=-1,
                    keepdims=True,
                )
                exact = jnp.exp(scores - total)
                grad_probs = dot_nt(grad_head, values)
                row_terms = jnp.sum(exact * grad_probs, axis=-1, keepdims=True)
                grad_scores = (exact * (grad_probs - row_terms)).astype(low)
                grad_query.append(jnp.dot(grad_scores, keys, preferred_element_type=jnp.float32))
                grad_keys = grad_keys + dot_tn(grad_scores, query_head)
                grad_values = grad_values + dot_tn(exact.astype(low), grad_head)
            grad_proj[tile, proj_lanes(pair, 0)] = (
                jnp.where(lane < HEAD_DIM, grad_query[0], grad_query[1]) * scaling
            ).astype(low)
            grad_keys = grad_keys * scaling
            for part in range(2):
                cut = slice(part * BAND, (part + 1) * BAND)
                old_k, old_v = key_parts[index + part], value_parts[index + part]
                key_parts[index + part] = grad_keys[cut] if old_k is None else old_k + grad_keys[cut]
                value_parts[index + part] = (
                    grad_values[cut] if old_v is None else old_v + grad_values[cut]
                )
        for index in range(count - 1):
            grad_proj[tiles[index], proj_lanes(pair, 1)] = key_parts[index + 1].astype(low)
            grad_proj[tiles[index], proj_lanes(pair, 2)] = value_parts[index + 1].astype(low)
        kept_kv[pair % 2, 0] = key_parts[count]
        kept_kv[pair % 2, 1] = value_parts[count]

        @pl.when(core == 1)
        def _():
            halo_send[pair % 2, 0] = key_parts[0].astype(low)
            halo_send[pair % 2, 1] = value_parts[0].astype(low)
            halo_copy(pair).start()

    def finish_pair(pair):
        last = tiles[-1]

        @pl.when(core == 0)
        def _():
            halo_copy(pair).wait_recv()
            for third in range(2):
                grad_proj[last, proj_lanes(pair, third + 1)] = (
                    kept_kv[pair % 2, third] + halo_in[pair, third].astype(jnp.float32)
                ).astype(low)

        @pl.when(core == 1)
        def _():
            halo_copy(pair).wait_send()
            for third in range(2):
                grad_proj[last, proj_lanes(pair, third + 1)] = kept_kv[pair % 2, third].astype(low)

    def qkv_job(layer, step, slot):
        wait_loads("qkv", slot)
        sums = 0.0
        for tile in tiles:
            grad = grad_proj[tile, aligned(step, width)]
            sums = sums + column_sum(grad)
            product = dot_nt(grad, columns_weight[slot])

            @pl.when(step == 0)
            def _(tile=tile, product=product):
                collected[tile, :] = product

            @pl.when(step > 0)
            def _(tile=tile, product=product):
                collected[tile, :] = collected[tile, :] + product

        sums_buf[...] = sums
        for when, part, which, row in ((0, 0, 0, 0), (1, 0, 0, 1), (1, 1, 1, 0), (2, 1, 1, 1)):

            @pl.when(step == when)
            def _(part=part, which=which, row=row):
                owner = 1 - y if which else y
                vector_out[vector_row(layer, row), block_of(owner)] = sums_buf[
                    :, part * block : (part + 1) * block
                ]

    def job(t):
        slot = t % 2
        layer = layers - 1 - t // period
        step = t % period

        @pl.when(step < FFN_STEPS)
        def _():
            ffn_job(layer, step, slot)

        @pl.when(step == norm_two_step)
        def _():
            norm_job(layer, 1, slot)

        @pl.when(step == out_step)
        def _():
            out_job(slot)

        @pl.when((step > attention_step) & (step <= attention_step + pairs))
        def _():
            finish_pair(step - attention_step - 1)

        @pl.when((step >= attention_step) & (step < attention_step + pairs))
        def _():
            attention_job(step - attention_step, slot)

        @pl.when((step >= qkv_step) & (step < qkv_step + QKV_STEPS))
        def _():
            qkv_job(layer, step - qkv_step, slot)

        @pl.when(step == norm_one_step)
        def _():
            norm_job(layer, 0, slot)

    stages = (
        (LAGS["core"], after_core),
        (0, multiply),
        (None, job),
        (LAGS["first"], after_first),
        (LAGS["second"], after_second),
        (LAGS["third"], after_third),
        (LAGS["fourth"], after_fourth),
        (LAGS["fifth"], after_fifth),
        (LAGS["sixth"], after_sixth),
        (LAGS["stored"], after_store),
        (LAGS["whole"], after_whole),
    )

    swaps = core + y - 2 * core * y

    def swap_copy(index, source, target):
        return pltpu.make_async_remote_copy(
            src_ref=source,
            dst_ref=target,
            send_sem=swap_send.at[index],
            recv_sem=swap_recv.at[index],
            device_id=swap_partner,
            device_id_type=MESH,
        )

    def swap_start(index, source, target):
        @pl.when(swaps == 1)
        def _():
            swap_copy(index, source, target).start()

        @pl.when(swaps == 0)
        def _():
            pltpu.make_async_copy(source, target, io_sem.at[1 + index]).start()

    def swap_wait(index, source, target):
        @pl.when(swaps == 1)
        def _():
            swap_copy(index, source, target).wait()

        @pl.when(swaps == 0)
        def _():
            pltpu.make_async_copy(source, target, io_sem.at[1 + index]).wait()

    first_load = pltpu.make_async_copy(cot_ref, grad_branch, io_sem.at[0])
    first_load.start()
    prefetch(0)
    fill_band_bias(segk_ref, bias_buf)
    first_load.wait()
    for tile in tiles:
        grad_res[tile, :] = grad_branch[tile, :].astype(jnp.float32)
    swap_start(0, out_act_ref, out_act_out)
    vector_ticks = [jobs + VECTOR_STEP * step for step in range(7)]

    def tick(t, carry):
        @pl.when(t + 1 < jobs)
        def _():
            prefetch(t + 1)

        ahead = t + 1 - FIRST

        @pl.when((ahead >= 0) & (ahead < chunks))
        def _():
            stage_operands(ahead)

        for lag, action in stages:
            if lag is None:

                @pl.when(t < jobs)
                def _():
                    job(t)

                continue
            chunk = t - FIRST - lag

            @pl.when((chunk >= 0) & (chunk < chunks))
            def _(chunk=chunk, action=action):
                action(chunk)

        @pl.when(t == jobs)
        def _():
            swap_start(1, grad_branch, grad_in_ref)

        for step, when in enumerate(vector_ticks):

            @pl.when(t == when)
            def _(step=step):
                vector_tick(step)

        return carry

    lax.fori_loop(0, max(chunks + FIRST + LAGS["stored"], vector_ticks[-1] + 1), tick, 0)
    swap_wait(0, out_act_ref, out_act_out)
    swap_wait(1, grad_branch, grad_in_ref)


def run_backward(cotangent, gain, segk, out_act, saved, weights, block):
    rows, width = cotangent.shape
    layers, hidden_half = weights[-1].shape[0], weights[-1].shape[1]
    half, quarter = block // 2, block // 4
    low, wide = jnp.bfloat16, jnp.float32
    pairs = width // LANES
    anywhere = pl.BlockSpec(memory_space=pl.ANY)
    in_vmem = pl.BlockSpec(memory_space=pltpu.VMEM)
    vector = (layers * VECTOR_ROWS, width)
    hidden_step = 2 * hidden_half // FFN_STEPS
    vmem = pltpu.VMEM
    return pl.pallas_call(
        functools.partial(backward_kernel, layers, block, hidden_half),
        in_specs=[anywhere] + [in_vmem] * 2 + [anywhere] * (1 + len(saved) + len(weights)),
        out_specs=[anywhere] * 6 + [in_vmem],
        out_shape=[
            jax.ShapeDtypeStruct((rows, width), low),
            jax.ShapeDtypeStruct((rows, width), low),
            jax.ShapeDtypeStruct((layers, hidden_half, width), low),
            jax.ShapeDtypeStruct((layers, width, hidden_half), low),
            jax.ShapeDtypeStruct((layers, block, width), low),
            jax.ShapeDtypeStruct((layers, 3, width, block), low),
            jax.ShapeDtypeStruct(vector, wide),
        ],
        scratch_shapes=[
            vmem((rows, width), low),
            vmem((rows, width), low),
            vmem((FFN_STEPS, rows, hidden_step), low),
            vmem((rows, 6 * block), low),
            vmem((rows, width), wide),
            vmem((rows, width), wide),
            vmem((rows, width), low),
            vmem((2, 3, rows, LANES), low),
            vmem((2, 2, BAND, LANES), low),
            vmem((2, rows, LANES), wide),
            vmem((2, 2, BAND, LANES), wide),
            vmem((2, 2, BAND, LANES), low),
            vmem((pairs, 2, BAND, LANES), low),
            vmem((2, hidden_step, width), low),
            vmem((2, width, hidden_step), low),
            vmem((2, rows, hidden_step), low),
            vmem((rows, width), wide),
            vmem((rows // BAND, BAND, 2 * BAND), wide),
            vmem((1, width), wide),
            vmem((STAGED, 2, rows, block), low),
            vmem((STAGED, rows, block), low),
            vmem((STAGED, 2, block, block), low),
            vmem((CORE_SLOTS, 2, half, block), low),
            vmem((SLOTS, 2, quarter, block), low),
            vmem((SLOTS, 2, quarter, block), low),
            vmem((SLOTS, 2, quarter, block), low),
            vmem((SLOTS, 2, quarter, block), low),
            vmem((SLOTS, 2, quarter, block), low),
            vmem((SLOTS, 2, quarter, block), low),
            vmem((RESULT_SLOTS, block, block), low),
            vmem((5,) + vector, wide),
            pltpu.SemaphoreType.DMA((2, 6)),
            pltpu.SemaphoreType.DMA((3,)),
            pltpu.SemaphoreType.DMA((pairs,)),
            pltpu.SemaphoreType.DMA((pairs,)),
            pltpu.SemaphoreType.DMA((STAGED, 3)),
            pltpu.SemaphoreType.DMA((8, SLOTS)),
            pltpu.SemaphoreType.DMA((8, SLOTS)),
            pltpu.SemaphoreType.DMA((RESULT_SLOTS,)),
            pltpu.SemaphoreType.DMA((6,)),
            pltpu.SemaphoreType.DMA((6,)),
            pltpu.SemaphoreType.DMA((2,)),
            pltpu.SemaphoreType.DMA((2,)),
        ],
        compiler_params=pltpu.CompilerParams(
            collective_id=0, has_side_effects=True, vmem_limit_bytes=VMEM_ASKED
        ),
        name="backward",
    )(cotangent, gain, segk, out_act, *saved, *weights)


def local_split(
    tokens_in,
    segments,
    w_qkv,
    qv_bias,
    w_out,
    w_up,
    up_bias,
    w_down,
    out_bias,
    ln_gain,
    ln_bias,
    cotangent,
):
    layers, width = w_qkv.shape[0], w_qkv.shape[1]
    block = w_qkv.shape[3]
    y = lax.axis_index("tensor")
    weights = (w_qkv.transpose(0, 2, 1, 3), w_out, w_up, w_down)
    gain = ln_gain.reshape(-1, width)
    out_act, cot, segk, *rest = run_forward(
        tokens_in,
        cotangent,
        segments,
        weights,
        (qv_bias.reshape(-1, block), up_bias),
        out_bias.reshape(-1, width),
        gain,
        ln_bias.reshape(-1, width),
        block,
    )
    others, saved = rest[: len(weights)], rest[len(weights) :]
    both = [member for pair in zip(weights, others) for member in pair]
    out_act, grad_in, *reduced, summed = run_backward(
        cot, gain, segk, out_act, saved, both, block
    )
    summed = summed.reshape(layers, -1)
    hidden = 2 * up_bias.shape[1]
    ends = [2 * width, 2 * width + hidden, 4 * width + hidden, 6 * width + hidden]
    qv_sum = summed[:, : ends[0]].reshape(layers, 2, width)
    grad_qv_bias = lax.dynamic_slice_in_dim(qv_sum, y * (width // 2), width // 2, axis=2)
    grad_up_bias = lax.dynamic_slice_in_dim(
        summed[:, ends[0] : ends[1]], y * (hidden // 2), hidden // 2, axis=1
    )
    grad_down, grad_up, grad_out, grad_qkv = [member.astype(jnp.float32) for member in reduced]
    return (
        out_act,
        grad_in,
        grad_qkv.transpose(0, 2, 1, 3),
        grad_qv_bias,
        grad_out,
        grad_up,
        grad_up_bias,
        grad_down,
        summed[:, ends[1] : ends[2]].reshape(layers, 2, width),
        summed[:, ends[2] : ends[3]].reshape(layers, 2, width),
        summed[:, ends[3] :].reshape(layers, 2, width),
    )


def solution(mesh):
    sizes = (mesh.shape["dp"], mesh.shape["tensor"])
    local = local_split if sizes == (16, 2) else local_general
    return jax.shard_map(
        local,
        mesh=mesh,
        in_specs=(
            P(("dp", "tensor"), None),
            P("dp", None),
            P(None, None, None, "tensor"),
            P(None, None, "tensor"),
            P(None, "tensor", None),
            P(None, None, "tensor"),
            P(None, "tensor"),
            P(None, "tensor", None),
            P(),
            P(),
            P(),
            P(("dp", "tensor"), None),
        ),
        out_specs=(
            P(("dp", "tensor"), None),
            P(("dp", "tensor"), None),
            P(None, None, None, "tensor"),
            P(None, None, "tensor"),
            P(None, "tensor", None),
            P(None, None, "tensor"),
            P(None, "tensor"),
            P(None, "tensor", None),
            P(),
            P(),
            P(),
        ),
        check_vma=False,
    )
```

```python
import functools

import jax
import jax.numpy as jnp
from jax import lax
from jax.experimental import pallas as pl
from jax.experimental.pallas import tpu as pltpu
from jax.sharding import PartitionSpec as P

HEAD_DIM = 64


epsilon = 1e-05
gelu_coeff = 0.7978845608028654
cubic_coeff = 0.044715
masked_score = -1e30


def as_sent(shard):

    def short(part):
        return part.astype(jnp.bfloat16) if part.dtype == jnp.float32 else part

    return jax.tree.map(short, shard)


def layer_norm(values, gain, shift):
    average = jnp.mean(values, axis=-1, keepdims=True)
    centred = values - average
    inverse = lax.rsqrt(jnp.mean(centred * centred, axis=-1, keepdims=True) + epsilon)
    unit_rows = centred * inverse
    return (unit_rows * gain + shift, unit_rows, inverse)


def norm_backward(incoming, unit_rows, inverse, gain):
    scaled = incoming * gain
    first_mean = jnp.mean(scaled, axis=-1, keepdims=True)
    second_mean = jnp.mean(scaled * unit_rows, axis=-1, keepdims=True)
    through = inverse * (scaled - first_mean - unit_rows * second_mean)
    return (through, jnp.sum(incoming * unit_rows, axis=0), jnp.sum(incoming, axis=0))


def gelu_tanh(before):
    tanh_input = gelu_coeff * (before + cubic_coeff * before * before * before)
    return 0.5 * before * (1.0 + jnp.tanh(tanh_input))


def gelu_slope(before):
    tanh_input = gelu_coeff * (before + cubic_coeff * before * before * before)
    tangent = jnp.tanh(tanh_input)
    return 0.5 * (1.0 + tangent) + 0.5 * before * (1.0 - tangent * tangent) * gelu_coeff * (
        1.0 + 3.0 * cubic_coeff * before * before
    )


def masked_scores(query_block, key_seq, segment_row, offset, block_rows):
    window = key_seq.shape[0]
    scores = jnp.einsum(
        "qhe,khe->hqk", query_block, key_seq, preferred_element_type=jnp.float32
    ) * HEAD_DIM ** (-0.5)
    query_place = offset + lax.iota(jnp.int32, block_rows)
    key_place = lax.iota(jnp.int32, window)
    query_segment = segment_row[offset : offset + block_rows]
    allowed = (query_place[:, None] >= key_place[None, :]) & (
        query_segment[:, None] == segment_row[None, :]
    )
    return jnp.where(allowed[None], scores, masked_score)


def split_heads(flat_rows, seq_count):
    return flat_rows.reshape(
        seq_count, flat_rows.shape[0] // seq_count, flat_rows.shape[1] // HEAD_DIM, HEAD_DIM
    )


def attend_forward(query_rows, key_rows, value_rows, segments):
    seq_count, window = segments.shape
    block_rows = min(512, window)

    def one_sequence(member):
        query_seq, key_seq, value_seq, segment_row = member
        outputs = []
        totals = []
        for block_index in range(window // block_rows):
            offset = block_index * block_rows
            scores = masked_scores(
                query_seq[offset : offset + block_rows], key_seq, segment_row, offset, block_rows
            )
            highest = jnp.max(scores, axis=-1, keepdims=True)
            raised = jnp.exp(scores - highest)
            summed = jnp.sum(raised, axis=-1, keepdims=True)
            softmax_low = (raised / summed).astype(jnp.bfloat16)
            block_out = jnp.einsum(
                "hqk,khe->qhe", softmax_low, value_seq, preferred_element_type=jnp.float32
            )
            outputs.append(block_out.astype(jnp.bfloat16))
            totals.append(highest[..., 0] + jnp.log(summed[..., 0]))
        return (jnp.concatenate(outputs, axis=0), jnp.stack(totals, axis=0))

    attended, log_totals = lax.map(
        one_sequence,
        (
            split_heads(query_rows, seq_count),
            split_heads(key_rows, seq_count),
            split_heads(value_rows, seq_count),
            segments,
        ),
    )
    return (attended.reshape(query_rows.shape), log_totals)


def attend_backward(query_rows, key_rows, value_rows, segments, log_totals, grad_attended):
    seq_count, window = segments.shape
    block_rows = min(512, window)
    scaling = HEAD_DIM ** (-0.5)

    def one_sequence(member):
        query_seq, key_seq, value_seq, segment_row, totals_seq, grad_seq = member
        query_parts = []
        grad_keys = jnp.zeros(key_seq.shape, jnp.float32)
        grad_values = jnp.zeros(value_seq.shape, jnp.float32)
        for block_index in range(window // block_rows):
            offset = block_index * block_rows
            query_block = query_seq[offset : offset + block_rows]
            grad_block = grad_seq[offset : offset + block_rows]
            scores = masked_scores(query_block, key_seq, segment_row, offset, block_rows)
            softmax_exact = jnp.exp(scores - totals_seq[block_index][..., None])
            softmax_low = softmax_exact.astype(jnp.bfloat16)
            grad_softmax = jnp.einsum(
                "qhe,khe->hqk", grad_block, value_seq, preferred_element_type=jnp.float32
            )
            row_terms = jnp.sum(softmax_exact * grad_softmax, axis=-1, keepdims=True)
            grad_scores = (softmax_exact * (grad_softmax - row_terms)).astype(jnp.bfloat16)
            query_parts.append(
                jnp.einsum("hqk,khe->qhe", grad_scores, key_seq, preferred_element_type=jnp.float32)
                * scaling
            )
            grad_keys = (
                grad_keys
                + jnp.einsum(
                    "hqk,qhe->khe", grad_scores, query_block, preferred_element_type=jnp.float32
                )
                * scaling
            )
            grad_values = grad_values + jnp.einsum(
                "hqk,qhe->khe", softmax_low, grad_block, preferred_element_type=jnp.float32
            )
        grad_query = jnp.concatenate(query_parts, axis=0)
        return (
            grad_query.astype(jnp.bfloat16),
            grad_keys.astype(jnp.bfloat16),
            grad_values.astype(jnp.bfloat16),
        )

    grad_query, grad_keys, grad_values = lax.map(
        one_sequence,
        (
            split_heads(query_rows, seq_count),
            split_heads(key_rows, seq_count),
            split_heads(value_rows, seq_count),
            segments,
            log_totals,
            split_heads(grad_attended, seq_count),
        ),
    )
    return (
        grad_query.reshape(query_rows.shape),
        grad_keys.reshape(query_rows.shape),
        grad_values.reshape(query_rows.shape),
    )


def layer_forward(residual, segments, weights):
    w_qkv, qv_bias, w_out, w_up, up_bias, w_down, out_bias, gains, shifts = weights
    row_count = residual.shape[0]
    normed, unit_one, inverse_one = layer_norm(residual, gains[0], shifts[0])
    normed_all = lax.all_gather(normed.astype(jnp.bfloat16), "tensor", axis=0, tiled=True)
    projected = jnp.einsum("td,dsc->tsc", normed_all, w_qkv, preferred_element_type=jnp.float32)
    query_rows = (projected[:, 0] + qv_bias[0]).astype(jnp.bfloat16)
    key_rows = projected[:, 1].astype(jnp.bfloat16)
    value_rows = (projected[:, 2] + qv_bias[1]).astype(jnp.bfloat16)
    attended, log_totals = attend_forward(query_rows, key_rows, value_rows, segments)
    middle = (
        residual
        + lax.psum_scatter(
            jnp.dot(
                lax.slice_in_dim(attended, 0, row_count * lax.axis_size("tensor"), axis=0),
                w_out,
                preferred_element_type=jnp.float32,
            ).astype(jnp.bfloat16),
            "tensor",
            scatter_dimension=0,
            tiled=True,
        ).astype(jnp.float32)
        + out_bias[0]
    )
    normed_two, unit_two, inverse_two = layer_norm(middle, gains[1], shifts[1])
    normed_low = normed_two.astype(jnp.bfloat16)
    ffn_rows = lax.all_gather(normed_low, "tensor", axis=0, tiled=True)
    before = jnp.dot(ffn_rows, w_up, preferred_element_type=jnp.float32) + up_bias
    activated = gelu_tanh(before).astype(jnp.bfloat16)
    ffn_branch = lax.psum_scatter(
        jnp.dot(
            lax.slice_in_dim(activated, 0, row_count * lax.axis_size("tensor"), axis=0),
            w_down,
            preferred_element_type=jnp.float32,
        ).astype(jnp.bfloat16),
        "tensor",
        scatter_dimension=0,
        tiled=True,
    ).astype(jnp.float32)
    kept_ffn = (w_up, w_down)
    result = middle + ffn_branch + out_bias[1]
    kept_state = (
        unit_one,
        inverse_one,
        normed_all,
        query_rows,
        key_rows,
        value_rows,
        attended,
        log_totals,
        unit_two,
        inverse_two,
        ffn_rows,
        before,
        activated,
        kept_ffn,
    )
    return (result, kept_state)


def layer_backward(grad_residual, segments, weights, kept_state):
    w_qkv, qv_bias, w_out, w_up, up_bias, w_down, out_bias, gains, shifts = weights
    (
        unit_one,
        inverse_one,
        normed_all,
        query_rows,
        key_rows,
        value_rows,
        attended,
        log_totals,
        unit_two,
        inverse_two,
        ffn_rows,
        before,
        activated,
        kept_ffn,
    ) = kept_state
    up_used, down_used = kept_ffn
    row_count = grad_residual.shape[0]
    grad_branch = grad_residual.astype(jnp.bfloat16)
    bias_down = jnp.sum(grad_branch, axis=0, dtype=jnp.float32)
    grad_rows = lax.all_gather(grad_branch, "tensor", axis=0, tiled=True)
    grad_hidden = jnp.einsum("td,fd->tf", grad_rows, down_used, preferred_element_type=jnp.float32)
    grad_before = (grad_hidden * gelu_slope(before)).astype(jnp.bfloat16)
    grad_down = jnp.einsum("tf,td->fd", activated, grad_rows, preferred_element_type=jnp.float32)
    grad_up = jnp.einsum("td,tf->df", ffn_rows, grad_before, preferred_element_type=jnp.float32)
    grad_up_bias = jnp.sum(grad_before, axis=0, dtype=jnp.float32)
    piece_rows = lax.slice_in_dim(grad_before, 0, row_count * lax.axis_size("tensor"), axis=0)
    grad_normed_two = lax.psum_scatter(
        jnp.einsum("tf,df->td", piece_rows, w_up, preferred_element_type=jnp.float32).astype(
            jnp.bfloat16
        ),
        "tensor",
        scatter_dimension=0,
        tiled=True,
    ).astype(jnp.float32)
    through_two, gain_two, shift_two = norm_backward(
        grad_normed_two, unit_two, inverse_two, gains[1]
    )
    grad_middle = grad_residual + through_two
    grad_attn_branch = grad_middle.astype(jnp.bfloat16)
    bias_attn = jnp.sum(grad_attn_branch, axis=0, dtype=jnp.float32)
    grad_attn_all = lax.all_gather(grad_attn_branch, "tensor", axis=0, tiled=True)
    grad_out_w = jnp.einsum(
        "tc,td->cd", attended, grad_attn_all, preferred_element_type=jnp.float32
    )
    grad_attended = jnp.einsum(
        "td,cd->tc", grad_attn_all, w_out, preferred_element_type=jnp.float32
    ).astype(jnp.bfloat16)
    grad_query, grad_keys, grad_values = attend_backward(
        query_rows, key_rows, value_rows, segments, log_totals, grad_attended
    )
    grad_projected = jnp.stack((grad_query, grad_keys, grad_values), axis=1)
    grad_qkv = jnp.einsum(
        "td,tsc->dsc", normed_all, grad_projected, preferred_element_type=jnp.float32
    )
    grad_qv_bias = jnp.stack(
        (
            jnp.sum(grad_query, axis=0, dtype=jnp.float32),
            jnp.sum(grad_values, axis=0, dtype=jnp.float32),
        )
    )
    piece_rows = lax.slice_in_dim(grad_projected, 0, row_count * lax.axis_size("tensor"), axis=0)
    grad_normed = lax.psum_scatter(
        jnp.einsum("tsc,dsc->td", piece_rows, w_qkv, preferred_element_type=jnp.float32).astype(
            jnp.bfloat16
        ),
        "tensor",
        scatter_dimension=0,
        tiled=True,
    ).astype(jnp.float32)
    through_one, gain_one, shift_one = norm_backward(grad_normed, unit_one, inverse_one, gains[0])
    grad_input = grad_middle + through_one
    spread = (grad_qkv, grad_qv_bias, grad_out_w, grad_up, grad_up_bias, grad_down)
    shared = (
        jnp.stack((bias_attn, bias_down)),
        jnp.stack((gain_one, gain_two)),
        jnp.stack((shift_one, shift_two)),
    )
    return (grad_input, spread, shared)


def local_general(
    tokens_in,
    segments,
    w_qkv,
    qv_bias,
    w_out,
    w_up,
    up_bias,
    w_down,
    out_bias,
    ln_gain,
    ln_bias,
    cotangent,
):
    layers_total = w_qkv.shape[0]
    all_params = (w_qkv, qv_bias, w_out, w_up, up_bias, w_down, out_bias, ln_gain, ln_bias)
    residual = tokens_in.astype(jnp.float32)
    kept_layers = []
    for layer_index in range(layers_total):
        weights = tuple((member_array[layer_index] for member_array in all_params))
        residual, kept_state = layer_forward(residual, segments, weights)
        kept_layers.append(kept_state)
    out_act = residual.astype(jnp.bfloat16)
    grad_residual = cotangent.astype(jnp.float32)
    spread_layers = []
    shared_layers = []
    for layer_index in reversed(range(layers_total)):
        weights = tuple((member_array[layer_index] for member_array in all_params))
        grad_residual, spread, shared = layer_backward(
            grad_residual, segments, weights, kept_layers[layer_index]
        )
        spread_layers.insert(0, spread)
        shared_layers.insert(0, shared)
    spread_stack = tuple(
        (
            jnp.stack([spread_layers[layer_index][position] for layer_index in range(layers_total)])
            for position in range(6)
        )
    )
    spread_stack = jax.tree.map(
        lambda part: part.astype(jnp.float32), lax.psum(as_sent(spread_stack), "dp")
    )
    shared_stack = tuple(
        (
            jnp.stack([shared_layers[layer_index][position] for layer_index in range(layers_total)])
            for position in range(3)
        )
    )
    shared_stack = lax.psum(shared_stack, ("dp", "tensor"))
    grad_in = grad_residual.astype(jnp.bfloat16)
    return (out_act, grad_in) + tuple(spread_stack) + tuple(shared_stack)


BAND = 256
LANES = 128
VMEM_ASKED = 60 * 2**20


def dot_nt(left, right):
    return lax.dot_general(left, right, (((1,), (1,)), ((), ())), preferred_element_type=jnp.float32)


def dot_tn(left, right):
    return lax.dot_general(left, right, (((0,), (0,)), ((), ())), preferred_element_type=jnp.float32)


def dot_low(left, right):
    return jnp.dot(left, right, preferred_element_type=jnp.float32)


UNITS_LAYER = 12
BEATS_EVERY_TICK = 18
Y_AHEAD = 2


def fill_band_bias(segk_ref, bias_ref):
    wide = segk_ref.shape[1]
    values = lax.broadcasted_iota(jnp.int32, (16, wide), 0)
    member = (values == segk_ref[...]).astype(jnp.float32).astype(jnp.bfloat16)
    for block in range(bias_ref.shape[0]):
        queries = member[:, (block + 1) * BAND : (block + 2) * BAND]
        keys = member[:, block * BAND : (block + 2) * BAND]
        row_place = lax.broadcasted_iota(jnp.int32, (BAND, 2 * BAND), 0) + BAND
        column_place = lax.broadcasted_iota(jnp.int32, (BAND, 2 * BAND), 1)
        allowed = (dot_tn(queries, keys) > 0.5) & (column_place <= row_place)
        bias_ref[block] = jnp.where(allowed, 0.0, masked_score)


def band_rows(halo, rows, block):
    if block == 0:
        return jnp.concatenate([halo, rows[0:BAND, :]], axis=0)
    return rows[(block - 1) * BAND : (block + 1) * BAND, :]


def aligned(index, size):
    return pl.ds(pl.multiple_of(index * size, size), size)


def forward_kernel(layers, block, hidden_half, *refs):
    (
        tokens_ref,
        cot_ref,
        segments_ref,
        qkv_own,
        out_own,
        up_own,
        down_own,
        qv_bias_ref,
        up_bias_ref,
        out_bias_ref,
        gain_ref,
        shift_ref,
        out_act_ref,
        cot_out,
        segk_out,
        qkv_other,
        out_other,
        up_other,
        down_other,
        act_out,
        slope_out,
        normed_two_out,
        middle_out,
        attended_out,
        proj_out,
        halo_out,
        totals_out,
        normed_out,
        resid_out,
        tokens_buf,
        segments_in,
        qv_bias_in,
        up_bias_in,
        resid,
        collected,
        normed,
        normed_two,
        proj,
        halo,
        attended,
        totals,
        act_buf,
        slope_buf,
        qkv_weight,
        out_weight,
        up_weight,
        down_weight,
        bias_buf,
        start_send,
        start_recv,
        swap_sem,
        relay_send,
        relay_recv,
        halo_send_sem,
        halo_recv_sem,
        load_sem,
        store_sem,
        pair_store_sem,
    ) = refs
    width = 2 * block
    rows_all = tokens_buf.shape[0]
    pairs_half = block // LANES
    blocks_hidden = hidden_half // block
    low = jnp.bfloat16
    place = lax.axis_index("dp")
    y = lax.axis_index("tensor")
    core = place % 2
    x = (place // 2) % 2
    z = place // 4
    z_low = z % 2
    core_partner = {"dp": place + 1 - 2 * core, "tensor": y}
    x_partner = {"dp": place + 2 - 4 * x, "tensor": y}
    y_partner = {"dp": place, "tensor": 1 - y}
    z_partner = {"dp": place + 4 - 8 * z_low, "tensor": y}
    swap_partner = {"dp": place + 1 - 2 * core, "tensor": 1 - y}
    swaps = core + y - 2 * core * y

    barrier = pltpu.get_barrier_semaphore()
    for partner in (core_partner, x_partner, y_partner, z_partner, swap_partner):
        pl.semaphore_signal(barrier, inc=1, device_id=partner, device_id_type=MESH)
    pl.semaphore_wait(barrier, 5)

    def remote(source, target, send, recv, partner):
        return pltpu.make_async_remote_copy(
            src_ref=source,
            dst_ref=target,
            send_sem=send,
            recv_sem=recv,
            device_id=partner,
            device_id_type=MESH,
        )

    def swap_copy(index, source, target):
        return remote(source, target, start_send.at[index], start_recv.at[index], swap_partner)

    def swap_start(index, source, target):
        @pl.when(swaps == 1)
        def _():
            swap_copy(index, source, target).start()

        @pl.when(swaps == 0)
        def _():
            pltpu.make_async_copy(source, target, swap_sem.at[index]).start()

    def swap_wait(index, source, target):
        @pl.when(swaps == 1)
        def _():
            swap_copy(index, source, target).wait()

        @pl.when(swaps == 0)
        def _():
            pltpu.make_async_copy(source, target, swap_sem.at[index]).wait()

    segments_copy = remote(
        segments_ref, segments_in, start_send.at[2], start_recv.at[2], core_partner
    )
    qv_copy = remote(qv_bias_ref, qv_bias_in, start_send.at[3], start_recv.at[3], y_partner)
    up_copy = remote(up_bias_ref, up_bias_in, start_send.at[4], start_recv.at[4], y_partner)

    units = layers * UNITS_LAYER

    def for_unit(unit, action):
        layer, inside = unit // UNITS_LAYER, unit % UNITS_LAYER

        @pl.when(inside < 3)
        def _():
            action(qkv_own.at[layer, inside], qkv_other.at[layer, inside])

        @pl.when(inside == 3)
        def _():
            action(out_own.at[layer], out_other.at[layer])

        @pl.when((inside >= 4) & (inside % 2 == 0))
        def _():
            cut = aligned((inside - 4) // 2, block)
            action(up_own.at[layer, :, cut], up_other.at[layer, :, cut])

        @pl.when((inside >= 4) & (inside % 2 == 1))
        def _():
            cut = aligned((inside - 4) // 2, block)
            action(down_own.at[layer, cut, :], down_other.at[layer, cut, :])

    def hop_copy(hop, unit, source, target):
        partner = (y_partner, x_partner, z_partner, core_partner)[hop]
        return remote(source, target, relay_send.at[hop, unit], relay_recv.at[hop, unit], partner)

    def piece_of(view, hop, short):
        rows = view.shape[0]
        if hop == 3:
            return view.at[aligned(core, rows // 2)]
        if hop == 2:
            return view.at[aligned(2 * core + z_low, rows // 4)]
        if short:
            return view.at[aligned(4 * core + 2 * z_low + x, rows // 8)]
        return view.at[aligned(2 * core + x, rows // 4)]

    def by_length(unit, hop, action):
        if hop == 3:
            action(False)
            return

        @pl.when(unit % 3 != 0)
        def _():
            action(True)

        if hop < 2:

            @pl.when(unit % 3 == 0)
            def _():
                action(False)

    def hop_start(hop, unit):
        def go(own, other):
            def one(short):
                source = piece_of(own if hop == 0 else other, hop, short)
                hop_copy(hop, unit, source, piece_of(other, hop, short)).start()

            by_length(unit, hop, one)

        for_unit(unit, go)

    def hop_wait(hop, unit):
        def one(short):
            piece = piece_of(down_other.at[0, pl.ds(0, block), :], hop, short)
            hop_copy(hop, unit, piece, piece).wait()

        by_length(unit, hop, one)

    def when_unit(unit, action):
        @pl.when((unit >= 0) & (unit < units))
        def _():
            action(unit)

    def beat(b):
        def after_y(unit):
            hop_wait(0, unit)
            hop_start(1, unit)

        def after_x(unit):
            hop_wait(1, unit)
            hop_start(2, unit)

        def after_z(unit):
            hop_wait(2, unit)
            hop_start(3, unit)

        when_unit(b + Y_AHEAD, lambda unit: hop_start(0, unit))
        when_unit(b - 1, after_y)
        when_unit(b - 2, after_x)
        when_unit(b - 3, after_z)
        when_unit(b - 4, lambda unit: hop_wait(3, unit))

    other_step = 3 + pairs_half
    out_step = other_step + 1 + pairs_half
    norm_two_step = out_step + 1
    ffn_step = norm_two_step + 1
    end_step = ffn_step + 2 * blocks_hidden
    period = end_step + 1
    jobs = layers * period

    def loads(kind, slot, *sources):
        targets = {
            "qkv": (qkv_weight,),
            "out": (out_weight.at[0], out_weight.at[1]),
            "ffn": (up_weight.at[slot], down_weight.at[slot]),
        }[kind]
        sources = sources or targets
        return [
            pltpu.make_async_copy(source, target, load_sem.at[slot, index])
            for index, (source, target) in enumerate(zip(sources, targets))
        ]

    def start_all(copies):
        for copy in copies:
            copy.start()

    def wait_all(copies):
        for copy in copies:
            copy.wait()

    def prefetch(t):
        slot = t % 2
        layer, step = t // period, t % period
        for at, source in ((1, qkv_own), (other_step, qkv_other)):

            @pl.when(step == at)
            def _(source=source):
                start_all(loads("qkv", slot, source.at[layer]))

        @pl.when(step == out_step)
        def _():
            start_all(loads("out", slot, out_own.at[layer], out_other.at[layer]))

        for which, (up_ref, down_ref) in enumerate(((up_own, down_own), (up_other, down_other))):
            begin = ffn_step + which * blocks_hidden

            @pl.when((step >= begin) & (step < begin + blocks_hidden))
            def _(begin=begin, up_ref=up_ref, down_ref=down_ref):
                cut = aligned(step - begin, block)
                start_all(loads("ffn", slot, up_ref.at[layer, :, cut], down_ref.at[layer, cut, :]))

    tiles = [slice(r, r + BAND) for r in range(0, rows_all, BAND)]
    fine_tiles = [slice(r, r + LANES) for r in range(0, rows_all, LANES)]

    def normalize(layer, index, target):
        gain = gain_ref[layer, pl.ds(index, 1), :]
        shift = shift_ref[layer, pl.ds(index, 1), :]
        for tile in fine_tiles:
            values, _, _ = layer_norm(resid[tile, :], gain, shift)
            target[tile, :] = values.astype(low)

    def store(index, source, target):
        return pltpu.make_async_copy(source, target, store_sem.at[index])

    def first_stores(layer):
        return [store(0, resid, resid_out.at[layer]), store(1, normed, normed_out.at[layer])]

    def proj_stores(layer, which):
        return [
            store(
                2 + 3 * which + third,
                proj.at[which, third],
                proj_out.at[layer, which, :, pl.ds(third * block, block)],
            )
            for third in range(3)
        ]

    def halo_store(layer, which):
        return store(8 + which, halo.at[layer, which], halo_out.at[layer, which])

    def attended_stores(layer, which):
        return [
            store(10 + which, attended.at[which], attended_out.at[layer, which]),
            store(12 + which, totals.at[which], totals_out.at[layer, which]),
        ]

    def second_stores(layer):
        return [
            store(14, resid, middle_out.at[layer]),
            store(15, normed_two, normed_two_out.at[layer]),
        ]

    def ffn_stores(layer, index, slot):
        which, inside = index // blocks_hidden, index % blocks_hidden
        cut = aligned(inside, block)
        return [
            pltpu.make_async_copy(
                buf.at[slot], out.at[layer, which, :, cut], pair_store_sem.at[slot, kind]
            )
            for kind, (buf, out) in enumerate(((act_buf, act_out), (slope_buf, slope_out)))
        ]

    def halo_copy(layer, which):
        return remote(
            proj.at[which, pl.ds(1, 2), pl.ds(rows_all - BAND, BAND)],
            halo.at[layer, which],
            halo_send_sem.at[layer, which],
            halo_recv_sem.at[layer, which],
            core_partner,
        )

    def first_job(layer):
        normalize(layer, 0, normed)
        start_all(first_stores(layer))

    def qkv_job(layer, which, slot):
        wait_all(loads("qkv", slot))
        bias = qv_bias_in if which else qv_bias_ref
        for third in range(3):
            for tile in tiles:
                product = dot_low(normed[tile, :], qkv_weight[third])
                if third != 1:
                    product = product + bias[layer, pl.ds(third // 2, 1), :]
                proj[which, third, tile, :] = product.astype(low)

        @pl.when(core == 0)
        def _():
            halo_copy(layer, which).start()

        start_all(proj_stores(layer, which))

    def attention_job(layer, which, pair):
        @pl.when(pair == 0)
        def _():
            @pl.when(core == 0)
            def _():
                halo_copy(layer, which).wait_send()

            @pl.when(core == 1)
            def _():
                halo_copy(layer, which).wait_recv()

            halo_store(layer, which).start()
            totals[which] = jnp.zeros_like(totals[which])

        lane = lax.broadcasted_iota(jnp.int32, (BAND, LANES), 1)
        here = aligned(pair, LANES)
        for index, tile in enumerate(tiles):
            query = proj[which, 0, tile, here]
            keys = band_rows(halo[layer, which, 0, :, here], proj[which, 1, :, here], index)
            values = band_rows(halo[layer, which, 1, :, here], proj[which, 2, :, here], index)
            parts = []
            kept = totals[which, tile, :]
            for head in range(2):
                mine = (lane // HEAD_DIM) == head
                scores = (
                    dot_nt(jnp.where(mine, query, 0), keys) * HEAD_DIM ** (-0.5) + bias_buf[index]
                )
                highest = jnp.max(scores, axis=-1, keepdims=True)
                raised = jnp.exp(scores - highest)
                summed = jnp.sum(raised, axis=-1, keepdims=True)
                parts.append(dot_low(raised.astype(low), values) / summed)
                kept = jnp.where(lane == 2 * pair + head, highest + jnp.log(summed), kept)
            totals[which, tile, :] = kept
            attended[which, tile, here] = jnp.where(lane < HEAD_DIM, parts[0], parts[1]).astype(low)

        @pl.when(pair == pairs_half - 1)
        def _():
            start_all(attended_stores(layer, which))

    def out_job(layer, slot):
        wait_all(loads("out", slot))
        wait_all(first_stores(layer))
        for which in range(2):
            wait_all(proj_stores(layer, which))
            halo_store(layer, which).wait()
        bias = out_bias_ref[layer, pl.ds(0, 1), :]
        for tile in tiles:
            branch = dot_low(attended[0, tile, :], out_weight[0])
            branch = branch + dot_low(attended[1, tile, :], out_weight[1])
            resid[tile, :] = resid[tile, :] + branch + bias

    def second_job(layer):
        normalize(layer, 1, normed_two)
        start_all(second_stores(layer))

    def ffn_job(layer, which, inside, slot):
        index = which * blocks_hidden + inside
        wait_all(loads("ffn", slot))

        @pl.when(index >= 2)
        def _():
            wait_all(ffn_stores(layer, index - 2, slot))

        bias = (up_bias_in if which else up_bias_ref)[pl.ds(layer, 1), aligned(inside, block)]
        for tile in tiles:
            before = dot_low(normed_two[tile, :], up_weight[slot]) + bias
            square = before * before
            tangent = jnp.tanh(gelu_coeff * before * (1.0 + cubic_coeff * square))
            raised = 0.5 * (1.0 + tangent)
            activated = (before * raised).astype(low)
            act_buf[slot, tile, :] = activated
            slope_buf[slot, tile, :] = (
                raised
                + 0.5
                * before
                * (1.0 - tangent * tangent)
                * gelu_coeff
                * (1.0 + 3.0 * cubic_coeff * square)
            ).astype(low)
            product = dot_low(activated, down_weight[slot])
            if which:
                collected[tile, :] = collected[tile, :] + product
                continue

            @pl.when(inside == 0)
            def _(tile=tile, product=product):
                collected[tile, :] = product

            @pl.when(inside > 0)
            def _(tile=tile, product=product):
                collected[tile, :] = collected[tile, :] + product

        start_all(ffn_stores(layer, index, slot))

    def end_job(layer, slot):
        wait_all(ffn_stores(layer, 2 * blocks_hidden - 2, slot))
        wait_all(ffn_stores(layer, 2 * blocks_hidden - 1, 1 - slot))
        wait_all(second_stores(layer))
        for which in range(2):
            wait_all(attended_stores(layer, which))
        bias = out_bias_ref[layer, pl.ds(1, 1), :]
        for tile in tiles:
            resid[tile, :] = resid[tile, :] + collected[tile, :] + bias

    def job(t):
        slot = t % 2
        layer, step = t // period, t % period

        def at(first, count, action):
            @pl.when((step >= first) & (step < first + count))
            def _():
                action(step - first)

        at(0, 1, lambda _: first_job(layer))
        at(1, 1, lambda _: qkv_job(layer, 0, slot))
        at(2, pairs_half, lambda pair: attention_job(layer, 0, pair))
        at(other_step, 1, lambda _: qkv_job(layer, 1, slot))
        at(other_step + 1, pairs_half, lambda pair: attention_job(layer, 1, pair))
        at(out_step, 1, lambda _: out_job(layer, slot))
        at(norm_two_step, 1, lambda _: second_job(layer))
        at(ffn_step, blocks_hidden, lambda inside: ffn_job(layer, 0, inside, slot))
        at(ffn_step + blocks_hidden, blocks_hidden, lambda inside: ffn_job(layer, 1, inside, slot))
        at(end_step, 1, lambda _: end_job(layer, slot))

    swap_start(0, tokens_ref, tokens_buf)
    halo[...] = jnp.zeros_like(halo)
    segments_copy.start()
    qv_copy.start()
    up_copy.start()
    for unit in range(Y_AHEAD):
        hop_start(0, unit)
    segments_copy.wait()
    window = jnp.where(core == y, segments_ref[...], segments_in[...])

    @pl.when(core == 0)
    def _():
        segk_out[:, 0:BAND] = jnp.full((1, BAND), -1, jnp.int32)
        segk_out[:, BAND:] = window[:, 0:rows_all]

    @pl.when(core == 1)
    def _():
        segk_out[...] = window[:, rows_all - BAND :]

    fill_band_bias(segk_out, bias_buf)
    qv_copy.wait()
    up_copy.wait()
    swap_wait(0, tokens_ref, tokens_buf)
    for tile in tiles:
        resid[tile, :] = tokens_buf[tile, :].astype(jnp.float32)
    cot_tick = BEATS_EVERY_TICK + 6

    def tick(t, carry):
        @pl.when(t <= BEATS_EVERY_TICK)
        def _():
            beat(t)

        late = t - BEATS_EVERY_TICK

        @pl.when((late > 0) & (late % 2 == 0))
        def _():
            beat(BEATS_EVERY_TICK + late // 2)

        @pl.when(t == cot_tick)
        def _():
            swap_start(1, cot_ref, cot_out)

        @pl.when(t + 1 < jobs)
        def _():
            prefetch(t + 1)

        job(t)
        return carry

    lax.fori_loop(0, jobs, tick, 0)
    for tile in tiles:
        normed_two[tile, :] = resid[tile, :].astype(low)
    last_store = store(0, normed_two, out_act_ref)
    last_store.start()
    last_store.wait()
    swap_wait(1, cot_ref, cot_out)


def run_forward(tokens, cotangent, segments, weights, biases, out_bias, gain, shift, block):
    rows, width = tokens.shape
    layers, hidden_half = weights[-1].shape[0], weights[-1].shape[1]
    low, wide = jnp.bfloat16, jnp.float32
    anywhere = pl.BlockSpec(memory_space=pl.ANY)
    in_vmem = pl.BlockSpec(memory_space=pltpu.VMEM)
    vmem = pltpu.VMEM
    units = layers * UNITS_LAYER
    shape = jax.ShapeDtypeStruct
    saved = [
        shape((layers, 2, rows, hidden_half), low),
        shape((layers, 2, rows, hidden_half), low),
        shape((layers, rows, width), low),
        shape((layers, rows, width), wide),
        shape((layers, 2, rows, block), low),
        shape((layers, 2, rows, 3 * block), low),
        shape((layers, 2, 2, BAND, block), low),
        shape((layers, 2, rows, LANES), wide),
        shape((layers, rows, width), low),
        shape((layers, rows, width), wide),
    ]
    others = [shape(member.shape, low) for member in weights]
    return pl.pallas_call(
        functools.partial(forward_kernel, layers, block, hidden_half),
        in_specs=[anywhere] * 2 + [in_vmem] + [anywhere] * 4 + [in_vmem] * 5,
        out_specs=[anywhere] * 2 + [in_vmem] + [anywhere] * (len(others) + len(saved)),
        out_shape=[
            shape((rows, width), low),
            shape((rows, width), low),
            shape((1, rows + BAND), jnp.int32),
        ]
        + others
        + saved,
        scratch_shapes=[
            vmem((rows, width), low),
            vmem(segments.shape, jnp.int32),
            vmem(biases[0].shape, wide),
            vmem(biases[1].shape, wide),
            vmem((rows, width), wide),
            vmem((rows, width), wide),
            vmem((rows, width), low),
            vmem((rows, width), low),
            vmem((2, 3, rows, block), low),
            vmem((layers, 2, 2, BAND, block), low),
            vmem((2, rows, block), low),
            vmem((2, rows, LANES), wide),
            vmem((2, rows, block), low),
            vmem((2, rows, block), low),
            vmem((3, width, block), low),
            vmem((2, block, width), low),
            vmem((2, width, block), low),
            vmem((2, block, width), low),
            vmem((rows // BAND, BAND, 2 * BAND), wide),
            pltpu.SemaphoreType.DMA((5,)),
            pltpu.SemaphoreType.DMA((5,)),
            pltpu.SemaphoreType.DMA((2,)),
            pltpu.SemaphoreType.DMA((4, units)),
            pltpu.SemaphoreType.DMA((4, units)),
            pltpu.SemaphoreType.DMA((layers, 2)),
            pltpu.SemaphoreType.DMA((layers, 2)),
            pltpu.SemaphoreType.DMA((2, 2)),
            pltpu.SemaphoreType.DMA((16,)),
            pltpu.SemaphoreType.DMA((2, 2)),
        ],
        compiler_params=pltpu.CompilerParams(
            collective_id=1, has_side_effects=True, vmem_limit_bytes=VMEM_ASKED
        ),
        name="forward",
    )(tokens, cotangent, segments, *weights, *biases, out_bias, gain, shift)


SLOTS = 8
CORE_SLOTS = 4
RESULT_SLOTS = 11
STAGED = 2
FIRST = 0
LAGS = dict(
    core=1, first=3, second=5, third=7, fourth=9, fifth=11, sixth=13, whole=14, stored=15
)
VECTOR_STEP = 3
VECTOR_ROWS = 12
MESH = pl.DeviceIdType.MESH
FFN_STEPS = 4
QKV_STEPS = 3


def added(left, right):
    return (left.astype(jnp.float32) + right.astype(jnp.float32)).astype(jnp.bfloat16)


def backward_kernel(layers, block, hidden_half, *refs):
    (
        cot_ref,
        gain_ref,
        segk_ref,
        out_act_ref,
        act_ref,
        slope_ref,
        normed_two_ref,
        middle_ref,
        attended_ref,
        proj_ref,
        halo_ref,
        totals_ref,
        normed_ref,
        resid_ref,
        qkv_own,
        qkv_other,
        out_own,
        out_other,
        up_own,
        up_other,
        down_own,
        down_other,
        out_act_out,
        grad_in_ref,
        out_down,
        out_up,
        out_out,
        out_qkv,
        vector_out,
        grad_branch,
        grad_attn,
        grad_before,
        grad_proj,
        grad_res,
        collected,
        grad_attended,
        qkv_buf,
        halo_buf,
        totals_buf,
        kept_kv,
        halo_send,
        halo_in,
        rows_weight,
        columns_weight,
        slope_buf,
        wide_buf,
        bias_buf,
        sums_buf,
        pair_buf,
        one_buf,
        part_buf,
        core_in,
        sent,
        held,
        kept,
        first_in,
        second_in,
        third_in,
        result,
        vec_in,
        load_sem,
        io_sem,
        halo_send_sem,
        halo_recv_sem,
        staged_sem,
        send_sems,
        recv_sems,
        store_sem,
        vec_send,
        vec_recv,
        swap_send,
        swap_recv,
    ) = refs
    half, quarter = block // 2, block // 4
    width = 2 * block
    rows_all = grad_branch.shape[0]
    pairs_half = block // LANES
    pairs = 2 * pairs_half
    low = jnp.bfloat16
    place = lax.axis_index("dp")
    y = lax.axis_index("tensor")
    core = place % 2
    x = (place // 2) % 2
    z = place // 4
    z_low = z % 2
    inner = (z + 1) // 2 % 2
    core_partner = {"dp": place + 1 - 2 * core, "tensor": y}
    x_partner = {"dp": place + 2 - 4 * x, "tensor": y}
    y_partner = {"dp": place, "tensor": 1 - y}
    z_partner = {"dp": place + 4 - 8 * z_low, "tensor": y}
    middle_partner = {"dp": place + 4 * (3 - 2 * z), "tensor": y}
    swap_partner = {"dp": place + 1 - 2 * core, "tensor": 1 - y}

    barrier = pltpu.get_barrier_semaphore()
    for partner in (core_partner, x_partner, y_partner, z_partner, swap_partner):
        pl.semaphore_signal(barrier, inc=1, device_id=partner, device_id_type=MESH)

    @pl.when(inner == 1)
    def _():
        pl.semaphore_signal(barrier, inc=1, device_id=middle_partner, device_id_type=MESH)
        pl.semaphore_wait(barrier, 6)

    @pl.when(inner == 0)
    def _():
        pl.semaphore_wait(barrier, 5)

    blocks_hidden = hidden_half // block
    plan = (
        ("rows", blocks_hidden, 2),
        ("columns", 2, blocks_hidden),
        ("rows", 1, 2),
        ("columns", 2, 3),
    )
    starts = []
    per_layer = 0
    for _, down_count, across_count in plan:
        starts.append(per_layer)
        per_layer += down_count * across_count
    chunks = layers * per_layer
    out_refs = (out_down, out_up, out_out, out_qkv)

    def block_of(index):
        return pl.ds(pl.multiple_of(index * block, block), block)

    def for_matrix(chunk, action):
        layer = layers - 1 - chunk // per_layer
        inside = chunk % per_layer
        for member, (_, down_count, across_count) in enumerate(plan):
            begin = starts[member]

            @pl.when((inside >= begin) & (inside < begin + down_count * across_count))
            def _(member=member, begin=begin, across_count=across_count):
                local = inside - begin
                action(member, layer, local // across_count, local % across_count)

    def operands_of(member, layer, i, j):
        if member == 0:
            return (
                grad_branch.at[:, block_of(j)],
                act_ref.at[layer, 0, :, block_of(i)],
                act_ref.at[layer, 1, :, block_of(i)],
            )
        if member == 1:
            return (
                normed_two_ref.at[layer, :, block_of(i)],
                grad_before.at[j // 2, :, block_of(j % 2)],
                grad_before.at[blocks_hidden // 2 + j // 2, :, block_of(j % 2)],
            )
        if member == 2:
            return (
                grad_attn.at[:, block_of(j)],
                attended_ref.at[layer, 0, :, block_of(i)],
                attended_ref.at[layer, 1, :, block_of(i)],
            )
        return (
            normed_ref.at[layer, :, block_of(i)],
            grad_proj.at[:, block_of(j)],
            grad_proj.at[:, block_of(3 + j)],
        )

    def staged_copies(chunk, shared, own, other):
        slot = chunk % STAGED
        return (
            pltpu.make_async_copy(own, pair_buf.at[slot, 0], staged_sem.at[slot, 0]),
            pltpu.make_async_copy(other, pair_buf.at[slot, 1], staged_sem.at[slot, 1]),
            pltpu.make_async_copy(shared, one_buf.at[slot], staged_sem.at[slot, 2]),
        )

    def stage_operands(chunk):
        def action(member, layer, i, j):
            for copy in staged_copies(chunk, *operands_of(member, layer, i, j)):
                copy.start()

        for_matrix(chunk, action)

    def remote(step, chunk, source, target, partner):
        slot = chunk % SLOTS
        return pltpu.make_async_remote_copy(
            src_ref=source,
            dst_ref=target,
            send_sem=send_sems.at[step, slot],
            recv_sem=recv_sems.at[step, slot],
            device_id=partner,
            device_id_type=MESH,
        )

    def x_first(chunk):
        return ((5 * chunk) % 8 < 3) | (chunk >= chunks - 1)

    def core_copy(chunk):
        return remote(
            0,
            chunk,
            part_buf.at[chunk % STAGED, :, aligned(1 - core, half)],
            core_in.at[chunk % CORE_SLOTS],
            core_partner,
        )

    low_middle = z - 1
    far_middle = 2 - z

    def first_copy(chunk, partner):
        slot = chunk % SLOTS
        return remote(1, chunk, sent.at[slot], first_in.at[slot], partner)

    def y_copy(chunk):
        slot = chunk % SLOTS
        return remote(2, chunk, kept.at[slot, 1], second_in.at[slot, 0], y_partner)

    def pair_copy(chunk):
        slot = chunk % SLOTS
        return remote(2, chunk, kept.at[slot], second_in.at[slot], z_partner)

    def single_copy(chunk):
        slot = chunk % SLOTS
        return remote(3, chunk, kept.at[slot, 0], third_in.at[slot, 0], z_partner)

    def split_copy(chunk):
        slot = chunk % SLOTS
        return remote(3, chunk, kept.at[slot, far_middle], third_in.at[slot, 0], middle_partner)

    def middle_copy(chunk):
        slot = chunk % SLOTS
        return remote(4, chunk, kept.at[slot, 0], third_in.at[slot, 1], middle_partner)

    def across_copy(chunk):
        slot = chunk % SLOTS
        return remote(4, chunk, kept.at[slot, low_middle], third_in.at[slot, 1], x_partner)

    def result_copy(step, chunk, rows, partner):
        piece = result.at[chunk % RESULT_SLOTS, rows]
        return remote(step, chunk, piece, piece, partner)

    x_rows = aligned(2 * core + x, quarter)
    core_rows = aligned(core, half)

    def middle_rows():
        return aligned(2 * core + low_middle, quarter)

    def store_copy(chunk, target):
        slot = chunk % RESULT_SLOTS
        return pltpu.make_async_copy(result.at[slot], target, store_sem.at[slot])

    def multiply(chunk):
        slot = chunk % STAGED
        for copy in staged_copies(chunk, one_buf.at[slot], pair_buf.at[slot, 0], pair_buf.at[slot, 1]):
            copy.wait()
        inside = chunk % per_layer
        by_rows = (inside < starts[1]) | ((inside >= starts[2]) & (inside < starts[3]))

        @pl.when(by_rows)
        def _():
            single = one_buf[slot]
            for which in range(2):
                part_buf[slot, which] = dot_tn(pair_buf[slot, which], single).astype(low)

        @pl.when(jnp.logical_not(by_rows))
        def _():
            single = one_buf[slot]
            for which in range(2):
                part_buf[slot, which] = dot_tn(single, pair_buf[slot, which]).astype(low)

        core_copy(chunk).start()

    def branch(chunk, by_x, by_y):
        is_x = x_first(chunk)

        @pl.when(is_x)
        def _():
            by_x()

        @pl.when(jnp.logical_not(is_x))
        def _():
            by_y()

    def on_middle(action):
        @pl.when(inner == 1)
        def _():
            action()

    def by_place(at_end, at_middle):
        @pl.when(inner == 0)
        def _():
            at_end()

        on_middle(at_middle)

    def after_core(chunk):
        slot, core_slot, part_slot = chunk % SLOTS, chunk % CORE_SLOTS, chunk % STAGED
        core_copy(chunk).wait()
        is_x = x_first(chunk).astype(jnp.int32)

        def summed(which, row):
            near = part_buf[part_slot, which, aligned(2 * core + row, quarter), :]
            return added(near, core_in[core_slot, which, aligned(row, quarter), :])

        for index in range(2):
            sent[slot, index] = summed(
                is_x * index + (1 - is_x), is_x * (1 - x) + (1 - is_x) * index
            )
        branch(
            chunk,
            lambda: first_copy(chunk, x_partner).start(),
            lambda: first_copy(chunk, y_partner).start(),
        )
        for index in range(2):
            held[slot, index] = summed(is_x * index, is_x * x + (1 - is_x) * index)

    def after_first(chunk):
        slot = chunk % SLOTS
        first_copy(chunk, y_partner).wait()
        for index in (1, 0):
            kept[slot, index] = added(held[slot, index], first_in[slot, index])

        def by_y():
            @pl.when(inner == 0)
            def _():
                pair_copy(chunk).start()

        branch(chunk, lambda: y_copy(chunk).start(), by_y)

    def after_second(chunk):
        slot = chunk % SLOTS

        def by_x():
            y_copy(chunk).wait()
            kept[slot, 0] = added(kept[slot, 0], second_in[slot, 0])

            @pl.when(inner == 0)
            def _():
                single_copy(chunk).start()

        def at_middle():
            pair_copy(chunk).wait_recv()
            kept[slot, far_middle] = added(kept[slot, far_middle], second_in[slot, far_middle])
            split_copy(chunk).start()
            kept[slot, low_middle] = added(kept[slot, low_middle], second_in[slot, low_middle])

        branch(chunk, by_x, lambda: by_place(lambda: pair_copy(chunk).wait_send(), at_middle))

    def after_third(chunk):
        slot = chunk % SLOTS

        def one_at_middle():
            single_copy(chunk).wait_recv()
            kept[slot, 0] = added(kept[slot, 0], third_in[slot, 0])
            middle_copy(chunk).start()

        def by_y():
            split_copy(chunk).wait()
            kept[slot, low_middle] = added(kept[slot, low_middle], third_in[slot, 0])
            across_copy(chunk).start()

        branch(
            chunk,
            lambda: by_place(lambda: single_copy(chunk).wait_send(), one_at_middle),
            lambda: on_middle(by_y),
        )

    def after_fourth(chunk):
        slot, result_slot = chunk % SLOTS, chunk % RESULT_SLOTS

        def by_x():
            middle_copy(chunk).wait()
            result[result_slot, x_rows, :] = added(kept[slot, 0], third_in[slot, 1])
            result_copy(5, chunk, x_rows, z_partner).start()

        def by_y():
            across_copy(chunk).wait()
            result[result_slot, middle_rows(), :] = added(
                kept[slot, low_middle], third_in[slot, 1]
            )
            result_copy(5, chunk, middle_rows(), middle_partner).start()

        branch(chunk, lambda: on_middle(by_x), lambda: on_middle(by_y))

    def after_fifth(chunk):
        def by_x():
            back = result_copy(5, chunk, x_rows, z_partner)
            by_place(back.wait_recv, back.wait_send)
            result_copy(6, chunk, x_rows, x_partner).start()

        def by_y():
            result_copy(5, chunk, middle_rows(), middle_partner).wait()
            result_copy(6, chunk, core_rows, z_partner).start()

        branch(chunk, by_x, lambda: on_middle(by_y))

    def after_sixth(chunk):
        def by_y():
            back = result_copy(6, chunk, core_rows, z_partner)
            by_place(back.wait_recv, back.wait_send)

        branch(chunk, lambda: result_copy(6, chunk, x_rows, x_partner).wait(), by_y)
        result_copy(7, chunk, core_rows, core_partner).start()

    def after_whole(chunk):
        result_copy(7, chunk, core_rows, core_partner).wait()

        def action(member, layer, i, j):
            if member == 3:
                target = out_qkv.at[layer, j, block_of(i)]
            else:
                target = out_refs[member].at[layer, block_of(i), block_of(j)]
            store_copy(chunk, target).start()

        for_matrix(chunk, action)

    def after_store(chunk):
        store_copy(chunk, result.at[chunk % RESULT_SLOTS]).wait()

    vector_partners = (core_partner, y_partner, x_partner, z_partner, middle_partner, z_partner)

    def vector_copy(step):
        target = vec_in.at[min(step, 4)]
        return pltpu.make_async_remote_copy(
            src_ref=vector_out,
            dst_ref=target,
            send_sem=vec_send.at[step],
            recv_sem=vec_recv.at[step],
            device_id=vector_partners[step],
            device_id_type=MESH,
        )

    def add_vector(step):
        vector_out[...] = vector_out[...] + vec_in[step]

    def vector_tick(step):
        if step == 0:
            vector_copy(0).start()
        elif step <= 3:
            vector_copy(step - 1).wait()
            add_vector(step - 1)
            if step < 3:
                vector_copy(step).start()
            else:

                @pl.when(inner == 0)
                def _():
                    vector_copy(3).start()

        elif step == 4:

            @pl.when(inner == 0)
            def _():
                vector_copy(3).wait_send()

            @pl.when(inner == 1)
            def _():
                vector_copy(3).wait_recv()
                add_vector(3)
                vector_copy(4).start()

        elif step == 5:

            @pl.when(inner == 1)
            def _():
                vector_copy(4).wait()
                add_vector(4)
                vector_copy(5).start()

        else:

            @pl.when(inner == 1)
            def _():
                vector_copy(5).wait_send()

            @pl.when(inner == 0)
            def _():
                vector_copy(5).wait_recv()
                vector_out[...] = vec_in[4]

    norm_two_step = FFN_STEPS
    out_step = norm_two_step + 1
    attention_step = out_step + 1
    qkv_step = attention_step + pairs + 1
    norm_one_step = qkv_step + QKV_STEPS
    period = norm_one_step + 1
    jobs = layers * period
    hidden_step = 2 * hidden_half // FFN_STEPS

    def loads(kind, slot, *sources):
        targets = {
            "ffn": (rows_weight.at[slot], columns_weight.at[slot], slope_buf.at[slot]),
            "wide": (wide_buf,),
            "out": (rows_weight.at[slot, pl.ds(0, block)], rows_weight.at[slot, pl.ds(block, block)]),
            "attention": (
                qkv_buf.at[slot, 0],
                qkv_buf.at[slot, 1],
                qkv_buf.at[slot, 2],
                halo_buf.at[slot, 0],
                halo_buf.at[slot, 1],
                totals_buf.at[slot],
            ),
            "qkv": (
                columns_weight.at[slot, :, pl.ds(0, block)],
                columns_weight.at[slot, :, pl.ds(block, block)],
            ),
        }[kind]
        sources = sources or targets
        return [
            pltpu.make_async_copy(source, target, load_sem.at[slot, index])
            for index, (source, target) in enumerate(zip(sources, targets))
        ]

    def prefetch(t):
        slot = t % 2
        layer = layers - 1 - t // period
        step = t % period

        for which, (up_ref, down_ref) in enumerate(((up_own, down_own), (up_other, down_other))):

            @pl.when((step < FFN_STEPS) & (step // (FFN_STEPS // 2) == which))
            def _(which=which, up_ref=up_ref, down_ref=down_ref):
                cut = aligned(step % (FFN_STEPS // 2), hidden_step)
                for copy in loads(
                    "ffn",
                    slot,
                    down_ref.at[layer, cut, :],
                    up_ref.at[layer, :, cut],
                    slope_ref.at[layer, which, :, cut],
                ):
                    copy.start()

        for at, source in ((norm_two_step, middle_ref), (norm_one_step, resid_ref)):

            @pl.when(step == at)
            def _(source=source):
                for copy in loads("wide", slot, source.at[layer]):
                    copy.start()

        @pl.when(step == out_step)
        def _():
            for copy in loads("out", slot, out_own.at[layer], out_other.at[layer]):
                copy.start()

        @pl.when((step >= attention_step) & (step < attention_step + pairs))
        def _():
            pair = step - attention_step
            which, inside = pair // pairs_half, pair % pairs_half

            def lanes(third):
                return aligned(third * pairs_half + inside, LANES)

            for copy in loads(
                "attention",
                slot,
                *[proj_ref.at[layer, which, :, lanes(third)] for third in range(3)],
                *[halo_ref.at[layer, which, third, :, lanes(0)] for third in range(2)],
                totals_ref.at[layer, which],
            ):
                copy.start()

        @pl.when((step >= qkv_step) & (step < qkv_step + QKV_STEPS))
        def _():
            for part in range(2):
                index = 2 * (step - qkv_step) + part
                for which, source in enumerate((qkv_own, qkv_other)):

                    @pl.when(index // 3 == which)
                    def _(part=part, index=index, source=source):
                        pltpu.make_async_copy(
                            source.at[layer, index % 3],
                            columns_weight.at[slot, :, pl.ds(part * block, block)],
                            load_sem.at[slot, part],
                        ).start()

    def wait_loads(kind, slot):
        for copy in loads(kind, slot):
            copy.wait()

    tiles = [slice(r, r + BAND) for r in range(0, rows_all, BAND)]
    fine_tiles = [slice(r, r + LANES) for r in range(0, rows_all, LANES)]

    def vector_row(layer, row):
        return pl.ds(layer * VECTOR_ROWS + row, 1)

    def column_sum(values):
        return jnp.sum(values.astype(jnp.float32), axis=0, keepdims=True)

    def ffn_job(layer, step, slot):
        wait_loads("ffn", slot)
        sums = 0.0
        for tile in tiles:
            grad_hidden = dot_nt(grad_branch[tile, :], rows_weight[slot])
            before = (grad_hidden * slope_buf[slot, tile, :].astype(jnp.float32)).astype(low)
            grad_before[step, tile, :] = before
            sums = sums + column_sum(before)
            product = dot_nt(before, columns_weight[slot])

            @pl.when(step == 0)
            def _(tile=tile, product=product):
                collected[tile, :] = product

            @pl.when(step > 0)
            def _(tile=tile, product=product):
                collected[tile, :] = collected[tile, :] + product

        per_half = FFN_STEPS // 2
        which = step // per_half
        owner = which + y - 2 * which * y
        vector_out[vector_row(layer, 2 + owner * per_half + step % per_half), :] = sums

    def norm_job(layer, index, slot):
        wait_loads("wide", slot)
        gain = gain_ref[layer, pl.ds(index, 1), :]
        gain_sum, shift_sum, attn_sum, branch_sum = 0.0, 0.0, 0.0, 0.0
        for tile in fine_tiles:
            incoming = collected[tile, :]
            values = wide_buf[tile, :]
            average = jnp.mean(values, axis=-1, keepdims=True)
            centred = values - average
            inverse = lax.rsqrt(jnp.mean(centred * centred, axis=-1, keepdims=True) + epsilon)
            unit = centred * inverse
            scaled = incoming * gain
            first_mean = jnp.mean(scaled, axis=-1, keepdims=True)
            second_mean = jnp.mean(scaled * unit, axis=-1, keepdims=True)
            total = grad_res[tile, :] + inverse * (scaled - first_mean - unit * second_mean)
            grad_res[tile, :] = total
            rounded = total.astype(low)
            gain_sum = gain_sum + column_sum(incoming * unit)
            shift_sum = shift_sum + column_sum(incoming)
            if index == 1:
                attn_sum = attn_sum + column_sum(rounded)
                branch_sum = branch_sum + column_sum(grad_branch[tile, :])
                grad_attn[tile, :] = rounded
            else:
                grad_branch[tile, :] = rounded
        vector_out[vector_row(layer, 8 + index), :] = gain_sum
        vector_out[vector_row(layer, 10 + index), :] = shift_sum
        if index == 1:
            vector_out[vector_row(layer, 6), :] = attn_sum
            vector_out[vector_row(layer, 7), :] = branch_sum

    def out_job(slot):
        wait_loads("out", slot)
        for tile in tiles:
            grad_attended[tile, :] = dot_nt(grad_attn[tile, :], rows_weight[slot]).astype(low)

    def halo_copy(pair):
        return pltpu.make_async_remote_copy(
            src_ref=halo_send.at[pair % 2],
            dst_ref=halo_in.at[pair],
            send_sem=halo_send_sem.at[pair],
            recv_sem=halo_recv_sem.at[pair],
            device_id=core_partner,
            device_id_type=MESH,
        )

    def proj_lanes(pair, third):
        which, inside = pair // pairs_half, pair % pairs_half
        return aligned(which * 3 * pairs_half + third * pairs_half + inside, LANES)

    def attention_job(pair, slot):
        wait_loads("attention", slot)
        lane = lax.broadcasted_iota(jnp.int32, (BAND, LANES), 1)
        scaling = HEAD_DIM ** (-0.5)
        count = len(tiles)
        key_parts = [None] * (count + 1)
        value_parts = [None] * (count + 1)
        here = aligned(pair, LANES)
        for index, tile in enumerate(tiles):
            query = qkv_buf[slot, 0, tile, :]
            grad = grad_attended[tile, here]
            keys = band_rows(halo_buf[slot, 0], qkv_buf[slot, 1], index)
            values = band_rows(halo_buf[slot, 1], qkv_buf[slot, 2], index)
            grad_query = []
            grad_keys = 0.0
            grad_values = 0.0
            for head in range(2):
                mine = (lane // HEAD_DIM) == head
                query_head = jnp.where(mine, query, 0)
                grad_head = jnp.where(mine, grad, 0)
                scores = dot_nt(query_head, keys) * scaling + bias_buf[index]
                total = jnp.sum(
                    jnp.where(
                        lane == 2 * (pair % pairs_half) + head, totals_buf[slot, tile, :], 0.0
                    ),
                    axis=-1,
                    keepdims=True,
                )
                exact = jnp.exp(scores - total)
                grad_probs = dot_nt(grad_head, values)
                row_terms = jnp.sum(exact * grad_probs, axis=-1, keepdims=True)
                grad_scores = (exact * (grad_probs - row_terms)).astype(low)
                grad_query.append(jnp.dot(grad_scores, keys, preferred_element_type=jnp.float32))
                grad_keys = grad_keys + dot_tn(grad_scores, query_head)
                grad_values = grad_values + dot_tn(exact.astype(low), grad_head)
            grad_proj[tile, proj_lanes(pair, 0)] = (
                jnp.where(lane < HEAD_DIM, grad_query[0], grad_query[1]) * scaling
            ).astype(low)
            grad_keys = grad_keys * scaling
            for part in range(2):
                cut = slice(part * BAND, (part + 1) * BAND)
                old_k, old_v = key_parts[index + part], value_parts[index + part]
                key_parts[index + part] = grad_keys[cut] if old_k is None else old_k + grad_keys[cut]
                value_parts[index + part] = (
                    grad_values[cut] if old_v is None else old_v + grad_values[cut]
                )
        for index in range(count - 1):
            grad_proj[tiles[index], proj_lanes(pair, 1)] = key_parts[index + 1].astype(low)
            grad_proj[tiles[index], proj_lanes(pair, 2)] = value_parts[index + 1].astype(low)
        kept_kv[pair % 2, 0] = key_parts[count]
        kept_kv[pair % 2, 1] = value_parts[count]

        @pl.when(core == 1)
        def _():
            halo_send[pair % 2, 0] = key_parts[0].astype(low)
            halo_send[pair % 2, 1] = value_parts[0].astype(low)
            halo_copy(pair).start()

    def finish_pair(pair):
        last = tiles[-1]

        @pl.when(core == 0)
        def _():
            halo_copy(pair).wait_recv()
            for third in range(2):
                grad_proj[last, proj_lanes(pair, third + 1)] = (
                    kept_kv[pair % 2, third] + halo_in[pair, third].astype(jnp.float32)
                ).astype(low)

        @pl.when(core == 1)
        def _():
            halo_copy(pair).wait_send()
            for third in range(2):
                grad_proj[last, proj_lanes(pair, third + 1)] = kept_kv[pair % 2, third].astype(low)

    def qkv_job(layer, step, slot):
        wait_loads("qkv", slot)
        sums = 0.0
        for tile in tiles:
            grad = grad_proj[tile, aligned(step, width)]
            sums = sums + column_sum(grad)
            product = dot_nt(grad, columns_weight[slot])

            @pl.when(step == 0)
            def _(tile=tile, product=product):
                collected[tile, :] = product

            @pl.when(step > 0)
            def _(tile=tile, product=product):
                collected[tile, :] = collected[tile, :] + product

        sums_buf[...] = sums
        for when, part, which, row in ((0, 0, 0, 0), (1, 0, 0, 1), (1, 1, 1, 0), (2, 1, 1, 1)):

            @pl.when(step == when)
            def _(part=part, which=which, row=row):
                owner = 1 - y if which else y
                vector_out[vector_row(layer, row), block_of(owner)] = sums_buf[
                    :, part * block : (part + 1) * block
                ]

    def job(t):
        slot = t % 2
        layer = layers - 1 - t // period
        step = t % period

        @pl.when(step < FFN_STEPS)
        def _():
            ffn_job(layer, step, slot)

        @pl.when(step == norm_two_step)
        def _():
            norm_job(layer, 1, slot)

        @pl.when(step == out_step)
        def _():
            out_job(slot)

        @pl.when((step > attention_step) & (step <= attention_step + pairs))
        def _():
            finish_pair(step - attention_step - 1)

        @pl.when((step >= attention_step) & (step < attention_step + pairs))
        def _():
            attention_job(step - attention_step, slot)

        @pl.when((step >= qkv_step) & (step < qkv_step + QKV_STEPS))
        def _():
            qkv_job(layer, step - qkv_step, slot)

        @pl.when(step == norm_one_step)
        def _():
            norm_job(layer, 0, slot)

    stages = (
        (LAGS["core"], after_core),
        (0, multiply),
        (None, job),
        (LAGS["first"], after_first),
        (LAGS["second"], after_second),
        (LAGS["third"], after_third),
        (LAGS["fourth"], after_fourth),
        (LAGS["fifth"], after_fifth),
        (LAGS["sixth"], after_sixth),
        (LAGS["stored"], after_store),
        (LAGS["whole"], after_whole),
    )

    swaps = core + y - 2 * core * y

    def swap_copy(index, source, target):
        return pltpu.make_async_remote_copy(
            src_ref=source,
            dst_ref=target,
            send_sem=swap_send.at[index],
            recv_sem=swap_recv.at[index],
            device_id=swap_partner,
            device_id_type=MESH,
        )

    def swap_start(index, source, target):
        @pl.when(swaps == 1)
        def _():
            swap_copy(index, source, target).start()

        @pl.when(swaps == 0)
        def _():
            pltpu.make_async_copy(source, target, io_sem.at[1 + index]).start()

    def swap_wait(index, source, target):
        @pl.when(swaps == 1)
        def _():
            swap_copy(index, source, target).wait()

        @pl.when(swaps == 0)
        def _():
            pltpu.make_async_copy(source, target, io_sem.at[1 + index]).wait()

    first_load = pltpu.make_async_copy(cot_ref, grad_branch, io_sem.at[0])
    first_load.start()
    prefetch(0)
    fill_band_bias(segk_ref, bias_buf)
    first_load.wait()
    for tile in tiles:
        grad_res[tile, :] = grad_branch[tile, :].astype(jnp.float32)
    stage_operands(0)
    swap_start(0, out_act_ref, out_act_out)
    vector_ticks = [jobs + VECTOR_STEP * step for step in range(7)]

    def tick(t, carry):
        @pl.when(t + 1 < jobs)
        def _():
            prefetch(t + 1)

        ahead = t + 1 - FIRST

        @pl.when((ahead > 0) & (ahead < chunks))
        def _():
            stage_operands(ahead)

        for lag, action in stages:
            if lag is None:

                @pl.when(t < jobs)
                def _():
                    job(t)

                continue
            chunk = t - FIRST - lag

            @pl.when((chunk >= 0) & (chunk < chunks))
            def _(chunk=chunk, action=action):
                action(chunk)

        @pl.when(t == chunks + FIRST + LAGS["second"] - 1)
        def _():
            swap_start(1, grad_branch, grad_in_ref)

        for step, when in enumerate(vector_ticks):

            @pl.when(t == when)
            def _(step=step):
                vector_tick(step)

        return carry

    lax.fori_loop(0, max(chunks + FIRST + LAGS["stored"], vector_ticks[-1] + 1), tick, 0)
    swap_wait(0, out_act_ref, out_act_out)
    swap_wait(1, grad_branch, grad_in_ref)


def run_backward(cotangent, gain, segk, out_act, saved, weights, block):
    rows, width = cotangent.shape
    layers, hidden_half = weights[-1].shape[0], weights[-1].shape[1]
    half, quarter = block // 2, block // 4
    low, wide = jnp.bfloat16, jnp.float32
    pairs = width // LANES
    anywhere = pl.BlockSpec(memory_space=pl.ANY)
    in_vmem = pl.BlockSpec(memory_space=pltpu.VMEM)
    vector = (layers * VECTOR_ROWS, width)
    hidden_step = 2 * hidden_half // FFN_STEPS
    vmem = pltpu.VMEM
    return pl.pallas_call(
        functools.partial(backward_kernel, layers, block, hidden_half),
        in_specs=[anywhere] + [in_vmem] * 2 + [anywhere] * (1 + len(saved) + len(weights)),
        out_specs=[anywhere] * 6 + [in_vmem],
        out_shape=[
            jax.ShapeDtypeStruct((rows, width), low),
            jax.ShapeDtypeStruct((rows, width), low),
            jax.ShapeDtypeStruct((layers, hidden_half, width), low),
            jax.ShapeDtypeStruct((layers, width, hidden_half), low),
            jax.ShapeDtypeStruct((layers, block, width), low),
            jax.ShapeDtypeStruct((layers, 3, width, block), low),
            jax.ShapeDtypeStruct(vector, wide),
        ],
        scratch_shapes=[
            vmem((rows, width), low),
            vmem((rows, width), low),
            vmem((FFN_STEPS, rows, hidden_step), low),
            vmem((rows, 6 * block), low),
            vmem((rows, width), wide),
            vmem((rows, width), wide),
            vmem((rows, width), low),
            vmem((2, 3, rows, LANES), low),
            vmem((2, 2, BAND, LANES), low),
            vmem((2, rows, LANES), wide),
            vmem((2, 2, BAND, LANES), wide),
            vmem((2, 2, BAND, LANES), low),
            vmem((pairs, 2, BAND, LANES), low),
            vmem((2, hidden_step, width), low),
            vmem((2, width, hidden_step), low),
            vmem((2, rows, hidden_step), low),
            vmem((rows, width), wide),
            vmem((rows // BAND, BAND, 2 * BAND), wide),
            vmem((1, width), wide),
            vmem((STAGED, 2, rows, block), low),
            vmem((STAGED, rows, block), low),
            vmem((STAGED, 2, block, block), low),
            vmem((CORE_SLOTS, 2, half, block), low),
            vmem((SLOTS, 2, quarter, block), low),
            vmem((SLOTS, 2, quarter, block), low),
            vmem((SLOTS, 2, quarter, block), low),
            vmem((SLOTS, 2, quarter, block), low),
            vmem((SLOTS, 2, quarter, block), low),
            vmem((SLOTS, 2, quarter, block), low),
            vmem((RESULT_SLOTS, block, block), low),
            vmem((5,) + vector, wide),
            pltpu.SemaphoreType.DMA((2, 6)),
            pltpu.SemaphoreType.DMA((3,)),
            pltpu.SemaphoreType.DMA((pairs,)),
            pltpu.SemaphoreType.DMA((pairs,)),
            pltpu.SemaphoreType.DMA((STAGED, 3)),
            pltpu.SemaphoreType.DMA((8, SLOTS)),
            pltpu.SemaphoreType.DMA((8, SLOTS)),
            pltpu.SemaphoreType.DMA((RESULT_SLOTS,)),
            pltpu.SemaphoreType.DMA((6,)),
            pltpu.SemaphoreType.DMA((6,)),
            pltpu.SemaphoreType.DMA((2,)),
            pltpu.SemaphoreType.DMA((2,)),
        ],
        compiler_params=pltpu.CompilerParams(
            collective_id=0, has_side_effects=True, vmem_limit_bytes=VMEM_ASKED
        ),
        name="backward",
    )(cotangent, gain, segk, out_act, *saved, *weights)


FINISH_DEPTH = 4


def finish_kernel(layers, copies, steps, *refs):
    count = len(steps)
    ins, refs = refs[:count], refs[count:]
    vector_ref, refs = refs[0], refs[1:]
    copy_ins, refs = refs[:copies], refs[copies:]
    outs, refs = refs[:count], refs[count:]
    qv_out, up_out, bias_out, gain_out, shift_out = refs[:5]
    copy_outs, refs = refs[5 : 5 + copies], refs[5 + copies :]
    in_bufs, refs = refs[:count], refs[count:]
    out_bufs, (in_sem, out_sem, copy_sem) = refs[:count], refs[count:]
    moved = [
        pltpu.make_async_copy(source, target, copy_sem.at[index])
        for index, (source, target) in enumerate(zip(copy_ins, copy_outs))
    ]
    for copy in moved:
        copy.start()
    plan = []
    for member, (rows, parts) in enumerate(steps):
        for layer in range(layers):
            for part in range(parts):
                plan.append((member, layer, part * rows, rows, (layer * parts + part) % FINISH_DEPTH))

    def view(ref, layer, begin, rows):
        if len(ref.shape) == 4:
            return ref.at[layer, begin // rows]
        return ref.at[layer, pl.ds(begin, rows)]

    def load(entry):
        member, layer, begin, rows, slot = entry
        return pltpu.make_async_copy(
            view(ins[member], layer, begin, rows), in_bufs[member].at[slot], in_sem.at[member, slot]
        )

    def save(entry):
        member, layer, begin, rows, slot = entry
        return pltpu.make_async_copy(
            out_bufs[member].at[slot], view(outs[member], layer, begin, rows), out_sem.at[member, slot]
        )

    for entry in plan[:FINISH_DEPTH]:
        load(entry).start()
    y = lax.axis_index("tensor")
    half = qv_out.shape[2]
    for layer in range(layers):
        base = layer * VECTOR_ROWS
        for index in range(2):
            mine = pl.ds(pl.multiple_of(y * half, half), half)
            qv_out[layer, pl.ds(index, 1), :] = vector_ref[pl.ds(base + index, 1), mine]
            width = vector_ref.shape[1]
            up_out[pl.ds(layer, 1), index * width : (index + 1) * width] = vector_ref[
                pl.ds(base + 2 + 2 * y + index, 1), :
            ]
            for row, target in ((6, bias_out), (8, gain_out), (10, shift_out)):
                target[layer, pl.ds(index, 1), :] = vector_ref[pl.ds(base + row + index, 1), :]
    busy = {}
    for place, entry in enumerate(plan):
        member, slot = entry[0], entry[4]
        load(entry).wait()
        if (member, slot) in busy:
            save(busy.pop((member, slot))).wait()
        out_bufs[member][slot] = in_bufs[member][slot].astype(jnp.float32)
        save(entry).start()
        busy[(member, slot)] = entry
        if place + FINISH_DEPTH < len(plan):
            load(plan[place + FINISH_DEPTH]).start()
    for entry in busy.values():
        save(entry).wait()
    for copy in moved:
        copy.wait()


def run_finish(reduced, vector, whole, block):
    layers, width = reduced[0].shape[0], vector.shape[1]
    hidden_half = reduced[0].shape[1]
    wide, low = jnp.float32, jnp.bfloat16
    shape = jax.ShapeDtypeStruct
    anywhere = pl.BlockSpec(memory_space=pl.ANY)
    in_vmem = pl.BlockSpec(memory_space=pltpu.VMEM)
    steps = (
        (block, hidden_half // block),
        (block // 2, width * 2 // block),
        (block, 1),
        (width, 3),
    )
    blocks = ((block, width), (block // 2, hidden_half), (block, width), (width, block))
    deep = lambda kind: [pltpu.VMEM((FINISH_DEPTH,) + size, kind) for size in blocks]
    return pl.pallas_call(
        functools.partial(finish_kernel, layers, len(whole), steps),
        in_specs=[anywhere] * len(reduced) + [in_vmem] + [anywhere] * len(whole),
        out_specs=[anywhere] * len(reduced) + [in_vmem] * 5 + [anywhere] * len(whole),
        out_shape=[shape(member.shape, wide) for member in reduced]
        + [
            shape((layers, 2, block), wide),
            shape((layers, hidden_half), wide),
            shape((layers, 2, width), wide),
            shape((layers, 2, width), wide),
            shape((layers, 2, width), wide),
        ]
        + [shape(member.shape, member.dtype) for member in whole],
        scratch_shapes=deep(low)
        + deep(wide)
        + [
            pltpu.SemaphoreType.DMA((4, FINISH_DEPTH)),
            pltpu.SemaphoreType.DMA((4, FINISH_DEPTH)),
            pltpu.SemaphoreType.DMA((len(whole),)),
        ],
        compiler_params=pltpu.CompilerParams(vmem_limit_bytes=VMEM_ASKED),
        name="finish",
    )(*reduced, vector, *whole)


def local_split(
    tokens_in,
    segments,
    w_qkv,
    qv_bias,
    w_out,
    w_up,
    up_bias,
    w_down,
    out_bias,
    ln_gain,
    ln_bias,
    cotangent,
):
    block = w_qkv.shape[3]
    weights = (w_qkv.transpose(0, 2, 1, 3), w_out, w_up, w_down)
    out_act, cot, segk, *rest = run_forward(
        tokens_in,
        cotangent,
        segments,
        weights,
        (qv_bias, up_bias),
        out_bias,
        ln_gain,
        ln_bias,
        block,
    )
    others, saved = rest[: len(weights)], rest[len(weights) :]
    both = [member for pair in zip(weights, others) for member in pair]
    out_act, grad_in, *reduced, summed = run_backward(
        cot, ln_gain, segk, out_act, saved, both, block
    )
    *grads, grad_qv, grad_up_bias, grad_bias, grad_gain, grad_shift, out_act, grad_in = run_finish(
        reduced, summed, (out_act, grad_in), block
    )
    grad_down, grad_up, grad_out, grad_qkv = grads
    return (
        out_act,
        grad_in,
        grad_qkv.transpose(0, 2, 1, 3),
        grad_qv,
        grad_out,
        grad_up,
        grad_up_bias,
        grad_down,
        grad_bias,
        grad_gain,
        grad_shift,
    )


def solution(mesh):
    sizes = (mesh.shape["dp"], mesh.shape["tensor"])
    local = local_split if sizes == (16, 2) else local_general
    return jax.shard_map(
        local,
        mesh=mesh,
        in_specs=(
            P(("dp", "tensor"), None),
            P("dp", None),
            P(None, None, None, "tensor"),
            P(None, None, "tensor"),
            P(None, "tensor", None),
            P(None, None, "tensor"),
            P(None, "tensor"),
            P(None, "tensor", None),
            P(),
            P(),
            P(),
            P(("dp", "tensor"), None),
        ),
        out_specs=(
            P(("dp", "tensor"), None),
            P(("dp", "tensor"), None),
            P(None, None, None, "tensor"),
            P(None, None, "tensor"),
            P(None, "tensor", None),
            P(None, None, "tensor"),
            P(None, "tensor"),
            P(None, "tensor", None),
            P(),
            P(),
            P(),
        ),
        check_vma=False,
    )
```

```python
import functools

import jax
import jax.numpy as jnp
from jax import lax
from jax.experimental import pallas as pl
from jax.experimental.pallas import tpu as pltpu
from jax.sharding import PartitionSpec as P

HEAD_DIM = 64


epsilon = 1e-05
gelu_coeff = 0.7978845608028654
cubic_coeff = 0.044715
masked_score = -1e30


def as_sent(shard):

    def short(part):
        return part.astype(jnp.bfloat16) if part.dtype == jnp.float32 else part

    return jax.tree.map(short, shard)


def layer_norm(values, gain, shift):
    average = jnp.mean(values, axis=-1, keepdims=True)
    centred = values - average
    inverse = lax.rsqrt(jnp.mean(centred * centred, axis=-1, keepdims=True) + epsilon)
    unit_rows = centred * inverse
    return (unit_rows * gain + shift, unit_rows, inverse)


def norm_backward(incoming, unit_rows, inverse, gain):
    scaled = incoming * gain
    first_mean = jnp.mean(scaled, axis=-1, keepdims=True)
    second_mean = jnp.mean(scaled * unit_rows, axis=-1, keepdims=True)
    through = inverse * (scaled - first_mean - unit_rows * second_mean)
    return (through, jnp.sum(incoming * unit_rows, axis=0), jnp.sum(incoming, axis=0))


def gelu_tanh(before):
    tanh_input = gelu_coeff * (before + cubic_coeff * before * before * before)
    return 0.5 * before * (1.0 + jnp.tanh(tanh_input))


def gelu_slope(before):
    tanh_input = gelu_coeff * (before + cubic_coeff * before * before * before)
    tangent = jnp.tanh(tanh_input)
    return 0.5 * (1.0 + tangent) + 0.5 * before * (1.0 - tangent * tangent) * gelu_coeff * (
        1.0 + 3.0 * cubic_coeff * before * before
    )


def masked_scores(query_block, key_seq, segment_row, offset, block_rows):
    window = key_seq.shape[0]
    scores = jnp.einsum(
        "qhe,khe->hqk", query_block, key_seq, preferred_element_type=jnp.float32
    ) * HEAD_DIM ** (-0.5)
    query_place = offset + lax.iota(jnp.int32, block_rows)
    key_place = lax.iota(jnp.int32, window)
    query_segment = segment_row[offset : offset + block_rows]
    allowed = (query_place[:, None] >= key_place[None, :]) & (
        query_segment[:, None] == segment_row[None, :]
    )
    return jnp.where(allowed[None], scores, masked_score)


def split_heads(flat_rows, seq_count):
    return flat_rows.reshape(
        seq_count, flat_rows.shape[0] // seq_count, flat_rows.shape[1] // HEAD_DIM, HEAD_DIM
    )


def attend_forward(query_rows, key_rows, value_rows, segments):
    seq_count, window = segments.shape
    block_rows = min(512, window)

    def one_sequence(member):
        query_seq, key_seq, value_seq, segment_row = member
        outputs = []
        totals = []
        for block_index in range(window // block_rows):
            offset = block_index * block_rows
            scores = masked_scores(
                query_seq[offset : offset + block_rows], key_seq, segment_row, offset, block_rows
            )
            highest = jnp.max(scores, axis=-1, keepdims=True)
            raised = jnp.exp(scores - highest)
            summed = jnp.sum(raised, axis=-1, keepdims=True)
            softmax_low = (raised / summed).astype(jnp.bfloat16)
            block_out = jnp.einsum(
                "hqk,khe->qhe", softmax_low, value_seq, preferred_element_type=jnp.float32
            )
            outputs.append(block_out.astype(jnp.bfloat16))
            totals.append(highest[..., 0] + jnp.log(summed[..., 0]))
        return (jnp.concatenate(outputs, axis=0), jnp.stack(totals, axis=0))

    attended, log_totals = lax.map(
        one_sequence,
        (
            split_heads(query_rows, seq_count),
            split_heads(key_rows, seq_count),
            split_heads(value_rows, seq_count),
            segments,
        ),
    )
    return (attended.reshape(query_rows.shape), log_totals)


def attend_backward(query_rows, key_rows, value_rows, segments, log_totals, grad_attended):
    seq_count, window = segments.shape
    block_rows = min(512, window)
    scaling = HEAD_DIM ** (-0.5)

    def one_sequence(member):
        query_seq, key_seq, value_seq, segment_row, totals_seq, grad_seq = member
        query_parts = []
        grad_keys = jnp.zeros(key_seq.shape, jnp.float32)
        grad_values = jnp.zeros(value_seq.shape, jnp.float32)
        for block_index in range(window // block_rows):
            offset = block_index * block_rows
            query_block = query_seq[offset : offset + block_rows]
            grad_block = grad_seq[offset : offset + block_rows]
            scores = masked_scores(query_block, key_seq, segment_row, offset, block_rows)
            softmax_exact = jnp.exp(scores - totals_seq[block_index][..., None])
            softmax_low = softmax_exact.astype(jnp.bfloat16)
            grad_softmax = jnp.einsum(
                "qhe,khe->hqk", grad_block, value_seq, preferred_element_type=jnp.float32
            )
            row_terms = jnp.sum(softmax_exact * grad_softmax, axis=-1, keepdims=True)
            grad_scores = (softmax_exact * (grad_softmax - row_terms)).astype(jnp.bfloat16)
            query_parts.append(
                jnp.einsum("hqk,khe->qhe", grad_scores, key_seq, preferred_element_type=jnp.float32)
                * scaling
            )
            grad_keys = (
                grad_keys
                + jnp.einsum(
                    "hqk,qhe->khe", grad_scores, query_block, preferred_element_type=jnp.float32
                )
                * scaling
            )
            grad_values = grad_values + jnp.einsum(
                "hqk,qhe->khe", softmax_low, grad_block, preferred_element_type=jnp.float32
            )
        grad_query = jnp.concatenate(query_parts, axis=0)
        return (
            grad_query.astype(jnp.bfloat16),
            grad_keys.astype(jnp.bfloat16),
            grad_values.astype(jnp.bfloat16),
        )

    grad_query, grad_keys, grad_values = lax.map(
        one_sequence,
        (
            split_heads(query_rows, seq_count),
            split_heads(key_rows, seq_count),
            split_heads(value_rows, seq_count),
            segments,
            log_totals,
            split_heads(grad_attended, seq_count),
        ),
    )
    return (
        grad_query.reshape(query_rows.shape),
        grad_keys.reshape(query_rows.shape),
        grad_values.reshape(query_rows.shape),
    )


def layer_forward(residual, segments, weights):
    w_qkv, qv_bias, w_out, w_up, up_bias, w_down, out_bias, gains, shifts = weights
    row_count = residual.shape[0]
    normed, unit_one, inverse_one = layer_norm(residual, gains[0], shifts[0])
    normed_all = lax.all_gather(normed.astype(jnp.bfloat16), "tensor", axis=0, tiled=True)
    projected = jnp.einsum("td,dsc->tsc", normed_all, w_qkv, preferred_element_type=jnp.float32)
    query_rows = (projected[:, 0] + qv_bias[0]).astype(jnp.bfloat16)
    key_rows = projected[:, 1].astype(jnp.bfloat16)
    value_rows = (projected[:, 2] + qv_bias[1]).astype(jnp.bfloat16)
    attended, log_totals = attend_forward(query_rows, key_rows, value_rows, segments)
    middle = (
        residual
        + lax.psum_scatter(
            jnp.dot(
                lax.slice_in_dim(attended, 0, row_count * lax.axis_size("tensor"), axis=0),
                w_out,
                preferred_element_type=jnp.float32,
            ).astype(jnp.bfloat16),
            "tensor",
            scatter_dimension=0,
            tiled=True,
        ).astype(jnp.float32)
        + out_bias[0]
    )
    normed_two, unit_two, inverse_two = layer_norm(middle, gains[1], shifts[1])
    normed_low = normed_two.astype(jnp.bfloat16)
    ffn_rows = lax.all_gather(normed_low, "tensor", axis=0, tiled=True)
    before = jnp.dot(ffn_rows, w_up, preferred_element_type=jnp.float32) + up_bias
    activated = gelu_tanh(before).astype(jnp.bfloat16)
    ffn_branch = lax.psum_scatter(
        jnp.dot(
            lax.slice_in_dim(activated, 0, row_count * lax.axis_size("tensor"), axis=0),
            w_down,
            preferred_element_type=jnp.float32,
        ).astype(jnp.bfloat16),
        "tensor",
        scatter_dimension=0,
        tiled=True,
    ).astype(jnp.float32)
    kept_ffn = (w_up, w_down)
    result = middle + ffn_branch + out_bias[1]
    kept_state = (
        unit_one,
        inverse_one,
        normed_all,
        query_rows,
        key_rows,
        value_rows,
        attended,
        log_totals,
        unit_two,
        inverse_two,
        ffn_rows,
        before,
        activated,
        kept_ffn,
    )
    return (result, kept_state)


def layer_backward(grad_residual, segments, weights, kept_state):
    w_qkv, qv_bias, w_out, w_up, up_bias, w_down, out_bias, gains, shifts = weights
    (
        unit_one,
        inverse_one,
        normed_all,
        query_rows,
        key_rows,
        value_rows,
        attended,
        log_totals,
        unit_two,
        inverse_two,
        ffn_rows,
        before,
        activated,
        kept_ffn,
    ) = kept_state
    up_used, down_used = kept_ffn
    row_count = grad_residual.shape[0]
    grad_branch = grad_residual.astype(jnp.bfloat16)
    bias_down = jnp.sum(grad_branch, axis=0, dtype=jnp.float32)
    grad_rows = lax.all_gather(grad_branch, "tensor", axis=0, tiled=True)
    grad_hidden = jnp.einsum("td,fd->tf", grad_rows, down_used, preferred_element_type=jnp.float32)
    grad_before = (grad_hidden * gelu_slope(before)).astype(jnp.bfloat16)
    grad_down = jnp.einsum("tf,td->fd", activated, grad_rows, preferred_element_type=jnp.float32)
    grad_up = jnp.einsum("td,tf->df", ffn_rows, grad_before, preferred_element_type=jnp.float32)
    grad_up_bias = jnp.sum(grad_before, axis=0, dtype=jnp.float32)
    piece_rows = lax.slice_in_dim(grad_before, 0, row_count * lax.axis_size("tensor"), axis=0)
    grad_normed_two = lax.psum_scatter(
        jnp.einsum("tf,df->td", piece_rows, w_up, preferred_element_type=jnp.float32).astype(
            jnp.bfloat16
        ),
        "tensor",
        scatter_dimension=0,
        tiled=True,
    ).astype(jnp.float32)
    through_two, gain_two, shift_two = norm_backward(
        grad_normed_two, unit_two, inverse_two, gains[1]
    )
    grad_middle = grad_residual + through_two
    grad_attn_branch = grad_middle.astype(jnp.bfloat16)
    bias_attn = jnp.sum(grad_attn_branch, axis=0, dtype=jnp.float32)
    grad_attn_all = lax.all_gather(grad_attn_branch, "tensor", axis=0, tiled=True)
    grad_out_w = jnp.einsum(
        "tc,td->cd", attended, grad_attn_all, preferred_element_type=jnp.float32
    )
    grad_attended = jnp.einsum(
        "td,cd->tc", grad_attn_all, w_out, preferred_element_type=jnp.float32
    ).astype(jnp.bfloat16)
    grad_query, grad_keys, grad_values = attend_backward(
        query_rows, key_rows, value_rows, segments, log_totals, grad_attended
    )
    grad_projected = jnp.stack((grad_query, grad_keys, grad_values), axis=1)
    grad_qkv = jnp.einsum(
        "td,tsc->dsc", normed_all, grad_projected, preferred_element_type=jnp.float32
    )
    grad_qv_bias = jnp.stack(
        (
            jnp.sum(grad_query, axis=0, dtype=jnp.float32),
            jnp.sum(grad_values, axis=0, dtype=jnp.float32),
        )
    )
    piece_rows = lax.slice_in_dim(grad_projected, 0, row_count * lax.axis_size("tensor"), axis=0)
    grad_normed = lax.psum_scatter(
        jnp.einsum("tsc,dsc->td", piece_rows, w_qkv, preferred_element_type=jnp.float32).astype(
            jnp.bfloat16
        ),
        "tensor",
        scatter_dimension=0,
        tiled=True,
    ).astype(jnp.float32)
    through_one, gain_one, shift_one = norm_backward(grad_normed, unit_one, inverse_one, gains[0])
    grad_input = grad_middle + through_one
    spread = (grad_qkv, grad_qv_bias, grad_out_w, grad_up, grad_up_bias, grad_down)
    shared = (
        jnp.stack((bias_attn, bias_down)),
        jnp.stack((gain_one, gain_two)),
        jnp.stack((shift_one, shift_two)),
    )
    return (grad_input, spread, shared)


def local_general(
    tokens_in,
    segments,
    w_qkv,
    qv_bias,
    w_out,
    w_up,
    up_bias,
    w_down,
    out_bias,
    ln_gain,
    ln_bias,
    cotangent,
):
    layers_total = w_qkv.shape[0]
    all_params = (w_qkv, qv_bias, w_out, w_up, up_bias, w_down, out_bias, ln_gain, ln_bias)
    residual = tokens_in.astype(jnp.float32)
    kept_layers = []
    for layer_index in range(layers_total):
        weights = tuple((member_array[layer_index] for member_array in all_params))
        residual, kept_state = layer_forward(residual, segments, weights)
        kept_layers.append(kept_state)
    out_act = residual.astype(jnp.bfloat16)
    grad_residual = cotangent.astype(jnp.float32)
    spread_layers = []
    shared_layers = []
    for layer_index in reversed(range(layers_total)):
        weights = tuple((member_array[layer_index] for member_array in all_params))
        grad_residual, spread, shared = layer_backward(
            grad_residual, segments, weights, kept_layers[layer_index]
        )
        spread_layers.insert(0, spread)
        shared_layers.insert(0, shared)
    spread_stack = tuple(
        (
            jnp.stack([spread_layers[layer_index][position] for layer_index in range(layers_total)])
            for position in range(6)
        )
    )
    spread_stack = jax.tree.map(
        lambda part: part.astype(jnp.float32), lax.psum(as_sent(spread_stack), "dp")
    )
    shared_stack = tuple(
        (
            jnp.stack([shared_layers[layer_index][position] for layer_index in range(layers_total)])
            for position in range(3)
        )
    )
    shared_stack = lax.psum(shared_stack, ("dp", "tensor"))
    grad_in = grad_residual.astype(jnp.bfloat16)
    return (out_act, grad_in) + tuple(spread_stack) + tuple(shared_stack)


BAND = 256
LANES = 128
VMEM_ASKED = 60 * 2**20


def dot_nt(left, right):
    return lax.dot_general(left, right, (((1,), (1,)), ((), ())), preferred_element_type=jnp.float32)


def dot_tn(left, right):
    return lax.dot_general(left, right, (((0,), (0,)), ((), ())), preferred_element_type=jnp.float32)


def dot_low(left, right):
    return jnp.dot(left, right, preferred_element_type=jnp.float32)


UNITS_LAYER = 12
BEATS_EVERY_TICK = 18
Y_AHEAD = 2


def fill_band_bias(segk_ref, bias_ref):
    wide = segk_ref.shape[1]
    values = lax.broadcasted_iota(jnp.int32, (16, wide), 0)
    member = (values == segk_ref[...]).astype(jnp.float32).astype(jnp.bfloat16)
    for block in range(bias_ref.shape[0]):
        queries = member[:, (block + 1) * BAND : (block + 2) * BAND]
        keys = member[:, block * BAND : (block + 2) * BAND]
        row_place = lax.broadcasted_iota(jnp.int32, (BAND, 2 * BAND), 0) + BAND
        column_place = lax.broadcasted_iota(jnp.int32, (BAND, 2 * BAND), 1)
        allowed = (dot_tn(queries, keys) > 0.5) & (column_place <= row_place)
        bias_ref[block] = jnp.where(allowed, 0.0, masked_score)


def band_rows(halo, rows, block):
    if block == 0:
        return jnp.concatenate([halo, rows[0:BAND, :]], axis=0)
    return rows[(block - 1) * BAND : (block + 1) * BAND, :]


def aligned(index, size):
    return pl.ds(pl.multiple_of(index * size, size), size)


def forward_kernel(layers, block, hidden_half, *refs):
    (
        tokens_ref,
        cot_ref,
        segments_ref,
        qkv_own,
        out_own,
        up_own,
        down_own,
        qv_bias_ref,
        up_bias_ref,
        out_bias_ref,
        gain_ref,
        shift_ref,
        out_act_ref,
        cot_out,
        segk_out,
        qkv_other,
        out_other,
        up_other,
        down_other,
        act_out,
        slope_out,
        normed_two_out,
        middle_out,
        attended_out,
        proj_out,
        halo_out,
        totals_out,
        normed_out,
        resid_out,
        tokens_buf,
        segments_in,
        qv_bias_in,
        up_bias_in,
        resid,
        collected,
        normed,
        normed_two,
        proj,
        halo,
        attended,
        totals,
        act_buf,
        slope_buf,
        qkv_weight,
        out_weight,
        up_weight,
        down_weight,
        bias_buf,
        start_send,
        start_recv,
        swap_sem,
        relay_send,
        relay_recv,
        halo_send_sem,
        halo_recv_sem,
        load_sem,
        store_sem,
        pair_store_sem,
    ) = refs
    width = 2 * block
    rows_all = tokens_buf.shape[0]
    pairs_half = block // LANES
    blocks_hidden = hidden_half // block
    low = jnp.bfloat16
    place = lax.axis_index("dp")
    y = lax.axis_index("tensor")
    core = place % 2
    x = (place // 2) % 2
    z = place // 4
    z_low = z % 2
    core_partner = {"dp": place + 1 - 2 * core, "tensor": y}
    x_partner = {"dp": place + 2 - 4 * x, "tensor": y}
    y_partner = {"dp": place, "tensor": 1 - y}
    z_partner = {"dp": place + 4 - 8 * z_low, "tensor": y}
    swap_partner = {"dp": place + 1 - 2 * core, "tensor": 1 - y}
    swaps = core + y - 2 * core * y

    barrier = pltpu.get_barrier_semaphore()
    for partner in (core_partner, x_partner, y_partner, z_partner, swap_partner):
        pl.semaphore_signal(barrier, inc=1, device_id=partner, device_id_type=MESH)
    pl.semaphore_wait(barrier, 5)

    def remote(source, target, send, recv, partner):
        return pltpu.make_async_remote_copy(
            src_ref=source,
            dst_ref=target,
            send_sem=send,
            recv_sem=recv,
            device_id=partner,
            device_id_type=MESH,
        )

    def swap_copy(index, source, target):
        return remote(source, target, start_send.at[index], start_recv.at[index], swap_partner)

    def swap_start(index, source, target):
        @pl.when(swaps == 1)
        def _():
            swap_copy(index, source, target).start()

        @pl.when(swaps == 0)
        def _():
            pltpu.make_async_copy(source, tokens_buf, swap_sem.at[index]).start()

    def swap_wait(index, source, target):
        @pl.when(swaps == 1)
        def _():
            swap_copy(index, source, target).wait()

        @pl.when(swaps == 0)
        def _():
            pltpu.make_async_copy(source, tokens_buf, swap_sem.at[index]).wait()

    segments_copy = remote(
        segments_ref, segments_in, start_send.at[2], start_recv.at[2], core_partner
    )
    qv_copy = remote(qv_bias_ref, qv_bias_in, start_send.at[3], start_recv.at[3], y_partner)
    up_copy = remote(up_bias_ref, up_bias_in, start_send.at[4], start_recv.at[4], y_partner)

    units = layers * UNITS_LAYER

    def for_unit(unit, action):
        layer, inside = unit // UNITS_LAYER, unit % UNITS_LAYER

        @pl.when(inside < 3)
        def _():
            action(qkv_own.at[layer, inside], qkv_other.at[layer, inside])

        @pl.when(inside == 3)
        def _():
            action(out_own.at[layer], out_other.at[layer])

        @pl.when((inside >= 4) & (inside % 2 == 0))
        def _():
            cut = aligned((inside - 4) // 2, block)
            action(up_own.at[layer, :, cut], up_other.at[layer, :, cut])

        @pl.when((inside >= 4) & (inside % 2 == 1))
        def _():
            cut = aligned((inside - 4) // 2, block)
            action(down_own.at[layer, cut, :], down_other.at[layer, cut, :])

    def hop_copy(hop, unit, source, target):
        partner = (y_partner, x_partner, z_partner, core_partner)[hop]
        return remote(source, target, relay_send.at[hop, unit], relay_recv.at[hop, unit], partner)

    def piece_of(view, hop, short):
        rows = view.shape[0]
        if hop == 3:
            return view.at[aligned(core, rows // 2)]
        if hop == 2:
            return view.at[aligned(2 * core + z_low, rows // 4)]
        if short:
            return view.at[aligned(4 * core + 2 * z_low + x, rows // 8)]
        return view.at[aligned(2 * core + x, rows // 4)]

    def by_length(unit, hop, action):
        if hop == 3:
            action(False)
            return

        @pl.when(unit % 3 != 0)
        def _():
            action(True)

        if hop < 2:

            @pl.when(unit % 3 == 0)
            def _():
                action(False)

    def hop_start(hop, unit):
        def go(own, other):
            def one(short):
                source = piece_of(own if hop == 0 else other, hop, short)
                hop_copy(hop, unit, source, piece_of(other, hop, short)).start()

            by_length(unit, hop, one)

        for_unit(unit, go)

    def hop_wait(hop, unit):
        def one(short):
            piece = piece_of(down_other.at[0, pl.ds(0, block), :], hop, short)
            hop_copy(hop, unit, piece, piece).wait()

        by_length(unit, hop, one)

    def when_unit(unit, action):
        @pl.when((unit >= 0) & (unit < units))
        def _():
            action(unit)

    def beat(b):
        def after_y(unit):
            hop_wait(0, unit)
            hop_start(1, unit)

        def after_x(unit):
            hop_wait(1, unit)
            hop_start(2, unit)

        def after_z(unit):
            hop_wait(2, unit)
            hop_start(3, unit)

        when_unit(b + Y_AHEAD, lambda unit: hop_start(0, unit))
        when_unit(b - 1, after_y)
        when_unit(b - 2, after_x)
        when_unit(b - 3, after_z)
        when_unit(b - 4, lambda unit: hop_wait(3, unit))

    other_step = 3 + pairs_half
    out_step = other_step + 1 + pairs_half
    norm_two_step = out_step + 1
    ffn_step = norm_two_step + 1
    end_step = ffn_step + 2 * blocks_hidden
    period = end_step + 1
    jobs = layers * period

    def loads(kind, slot, *sources):
        targets = {
            "qkv": (qkv_weight,),
            "out": (out_weight.at[0], out_weight.at[1]),
            "ffn": (up_weight.at[slot], down_weight.at[slot]),
        }[kind]
        sources = sources or targets
        return [
            pltpu.make_async_copy(source, target, load_sem.at[slot, index])
            for index, (source, target) in enumerate(zip(sources, targets))
        ]

    def start_all(copies):
        for copy in copies:
            copy.start()

    def wait_all(copies):
        for copy in copies:
            copy.wait()

    def prefetch(t):
        slot = t % 2
        layer, step = t // period, t % period
        for at, source in ((1, qkv_own), (other_step, qkv_other)):

            @pl.when(step == at)
            def _(source=source):
                start_all(loads("qkv", slot, source.at[layer]))

        @pl.when(step == out_step)
        def _():
            start_all(loads("out", slot, out_own.at[layer], out_other.at[layer]))

        for which, (up_ref, down_ref) in enumerate(((up_own, down_own), (up_other, down_other))):
            begin = ffn_step + which * blocks_hidden

            @pl.when((step >= begin) & (step < begin + blocks_hidden))
            def _(begin=begin, up_ref=up_ref, down_ref=down_ref):
                cut = aligned(step - begin, block)
                start_all(loads("ffn", slot, up_ref.at[layer, :, cut], down_ref.at[layer, cut, :]))

    tiles = [slice(r, r + BAND) for r in range(0, rows_all, BAND)]
    fine_tiles = [slice(r, r + LANES) for r in range(0, rows_all, LANES)]

    def normalize(layer, index, target):
        gain = gain_ref[layer, pl.ds(index, 1), :]
        shift = shift_ref[layer, pl.ds(index, 1), :]
        for tile in fine_tiles:
            values, _, _ = layer_norm(resid[tile, :], gain, shift)
            target[tile, :] = values.astype(low)

    def store(index, source, target):
        return pltpu.make_async_copy(source, target, store_sem.at[index])

    def first_stores(layer):
        return [store(0, resid, resid_out.at[layer]), store(1, normed, normed_out.at[layer])]

    def proj_stores(layer, which):
        return [
            store(
                2 + 3 * which + third,
                proj.at[which, third],
                proj_out.at[layer, which, :, pl.ds(third * block, block)],
            )
            for third in range(3)
        ]

    def halo_store(layer, which):
        return store(8 + which, halo.at[layer, which], halo_out.at[layer, which])

    def attended_stores(layer, which):
        return [
            store(10 + which, attended.at[which], attended_out.at[layer, which]),
            store(12 + which, totals.at[which], totals_out.at[layer, which]),
        ]

    def second_stores(layer):
        return [
            store(14, resid, middle_out.at[layer]),
            store(15, normed_two, normed_two_out.at[layer]),
        ]

    def ffn_stores(layer, index, slot):
        which, inside = index // blocks_hidden, index % blocks_hidden
        cut = aligned(inside, block)
        return [
            pltpu.make_async_copy(
                buf.at[slot], out.at[layer, which, :, cut], pair_store_sem.at[slot, kind]
            )
            for kind, (buf, out) in enumerate(((act_buf, act_out), (slope_buf, slope_out)))
        ]

    def halo_copy(layer, which):
        return remote(
            proj.at[which, pl.ds(1, 2), pl.ds(rows_all - BAND, BAND)],
            halo.at[layer, which],
            halo_send_sem.at[layer, which],
            halo_recv_sem.at[layer, which],
            core_partner,
        )

    def first_job(layer):
        normalize(layer, 0, normed)
        start_all(first_stores(layer))

    def qkv_job(layer, which, slot):
        wait_all(loads("qkv", slot))
        bias = qv_bias_in if which else qv_bias_ref
        for third in range(3):
            for tile in tiles:
                product = dot_low(normed[tile, :], qkv_weight[third])
                if third != 1:
                    product = product + bias[layer, pl.ds(third // 2, 1), :]
                proj[which, third, tile, :] = product.astype(low)

        @pl.when(core == 0)
        def _():
            halo_copy(layer, which).start()

        start_all(proj_stores(layer, which))

    def attention_job(layer, which, pair):
        @pl.when(pair == 0)
        def _():
            @pl.when(core == 0)
            def _():
                halo_copy(layer, which).wait_send()

            @pl.when(core == 1)
            def _():
                halo_copy(layer, which).wait_recv()

            halo_store(layer, which).start()
            totals[which] = jnp.zeros_like(totals[which])

        lane = lax.broadcasted_iota(jnp.int32, (BAND, LANES), 1)
        here = aligned(pair, LANES)
        for index, tile in enumerate(tiles):
            query = proj[which, 0, tile, here]
            keys = band_rows(halo[layer, which, 0, :, here], proj[which, 1, :, here], index)
            values = band_rows(halo[layer, which, 1, :, here], proj[which, 2, :, here], index)
            parts = []
            kept = totals[which, tile, :]
            for head in range(2):
                mine = (lane // HEAD_DIM) == head
                scores = (
                    dot_nt(jnp.where(mine, query, 0), keys) * HEAD_DIM ** (-0.5) + bias_buf[index]
                )
                highest = jnp.max(scores, axis=-1, keepdims=True)
                raised = jnp.exp(scores - highest)
                summed = jnp.sum(raised, axis=-1, keepdims=True)
                parts.append(dot_low(raised.astype(low), values) / summed)
                kept = jnp.where(lane == 2 * pair + head, highest + jnp.log(summed), kept)
            totals[which, tile, :] = kept
            attended[which, tile, here] = jnp.where(lane < HEAD_DIM, parts[0], parts[1]).astype(low)

        @pl.when(pair == pairs_half - 1)
        def _():
            start_all(attended_stores(layer, which))

    def out_job(layer, slot):
        wait_all(loads("out", slot))
        wait_all(first_stores(layer))
        for which in range(2):
            wait_all(proj_stores(layer, which))
            halo_store(layer, which).wait()
        bias = out_bias_ref[layer, pl.ds(0, 1), :]
        for tile in tiles:
            branch = dot_low(attended[0, tile, :], out_weight[0])
            branch = branch + dot_low(attended[1, tile, :], out_weight[1])
            resid[tile, :] = resid[tile, :] + branch + bias

    def second_job(layer):
        normalize(layer, 1, normed_two)
        start_all(second_stores(layer))

    def ffn_job(layer, which, inside, slot):
        index = which * blocks_hidden + inside
        wait_all(loads("ffn", slot))

        @pl.when(index >= 2)
        def _():
            wait_all(ffn_stores(layer, index - 2, slot))

        bias = (up_bias_in if which else up_bias_ref)[pl.ds(layer, 1), aligned(inside, block)]
        for tile in tiles:
            before = dot_low(normed_two[tile, :], up_weight[slot]) + bias
            square = before * before
            tangent = jnp.tanh(gelu_coeff * before * (1.0 + cubic_coeff * square))
            raised = 0.5 * (1.0 + tangent)
            activated = (before * raised).astype(low)
            act_buf[slot, tile, :] = activated
            slope_buf[slot, tile, :] = (
                raised
                + 0.5
                * before
                * (1.0 - tangent * tangent)
                * gelu_coeff
                * (1.0 + 3.0 * cubic_coeff * square)
            ).astype(low)
            product = dot_low(activated, down_weight[slot])
            if which:
                collected[tile, :] = collected[tile, :] + product
                continue

            @pl.when(inside == 0)
            def _(tile=tile, product=product):
                collected[tile, :] = product

            @pl.when(inside > 0)
            def _(tile=tile, product=product):
                collected[tile, :] = collected[tile, :] + product

        start_all(ffn_stores(layer, index, slot))

    def end_job(layer, slot):
        wait_all(ffn_stores(layer, 2 * blocks_hidden - 2, slot))
        wait_all(ffn_stores(layer, 2 * blocks_hidden - 1, 1 - slot))
        wait_all(second_stores(layer))
        for which in range(2):
            wait_all(attended_stores(layer, which))
        bias = out_bias_ref[layer, pl.ds(1, 1), :]
        for tile in tiles:
            resid[tile, :] = resid[tile, :] + collected[tile, :] + bias

    def job(t):
        slot = t % 2
        layer, step = t // period, t % period

        def at(first, count, action):
            @pl.when((step >= first) & (step < first + count))
            def _():
                action(step - first)

        at(0, 1, lambda _: first_job(layer))
        at(1, 1, lambda _: qkv_job(layer, 0, slot))
        at(2, pairs_half, lambda pair: attention_job(layer, 0, pair))
        at(other_step, 1, lambda _: qkv_job(layer, 1, slot))
        at(other_step + 1, pairs_half, lambda pair: attention_job(layer, 1, pair))
        at(out_step, 1, lambda _: out_job(layer, slot))
        at(norm_two_step, 1, lambda _: second_job(layer))
        at(ffn_step, blocks_hidden, lambda inside: ffn_job(layer, 0, inside, slot))
        at(ffn_step + blocks_hidden, blocks_hidden, lambda inside: ffn_job(layer, 1, inside, slot))
        at(end_step, 1, lambda _: end_job(layer, slot))

    swap_start(0, tokens_ref, tokens_buf)
    halo[...] = jnp.zeros_like(halo)
    segments_copy.start()
    qv_copy.start()
    up_copy.start()
    for unit in range(Y_AHEAD):
        hop_start(0, unit)
    segments_copy.wait()
    window = jnp.where(core == y, segments_ref[...], segments_in[...])

    @pl.when(core == 0)
    def _():
        segk_out[:, 0:BAND] = jnp.full((1, BAND), -1, jnp.int32)
        segk_out[:, BAND:] = window[:, 0:rows_all]

    @pl.when(core == 1)
    def _():
        segk_out[...] = window[:, rows_all - BAND :]

    fill_band_bias(segk_out, bias_buf)
    qv_copy.wait()
    up_copy.wait()
    swap_wait(0, tokens_ref, tokens_buf)
    for tile in tiles:
        resid[tile, :] = tokens_buf[tile, :].astype(jnp.float32)
    cot_tick = BEATS_EVERY_TICK + 6

    def tick(t, carry):
        @pl.when(t <= BEATS_EVERY_TICK)
        def _():
            beat(t)

        late = t - BEATS_EVERY_TICK

        @pl.when((late > 0) & (late % 2 == 0))
        def _():
            beat(BEATS_EVERY_TICK + late // 2)

        @pl.when(t == cot_tick)
        def _():
            swap_start(1, cot_ref, cot_out)

        @pl.when((t == cot_tick + 4) & (swaps == 0))
        def _():
            pltpu.make_async_copy(cot_ref, tokens_buf, swap_sem.at[1]).wait()
            pltpu.make_async_copy(tokens_buf, cot_out, swap_sem.at[1]).start()

        @pl.when(t + 1 < jobs)
        def _():
            prefetch(t + 1)

        job(t)
        return carry

    lax.fori_loop(0, jobs, tick, 0)
    for tile in tiles:
        normed_two[tile, :] = resid[tile, :].astype(low)
    last_store = store(0, normed_two, out_act_ref)
    last_store.start()
    last_store.wait()
    swap_wait(1, cot_ref, cot_out)


def run_forward(tokens, cotangent, segments, weights, biases, out_bias, gain, shift, block):
    rows, width = tokens.shape
    layers, hidden_half = weights[-1].shape[0], weights[-1].shape[1]
    low, wide = jnp.bfloat16, jnp.float32
    anywhere = pl.BlockSpec(memory_space=pl.ANY)
    in_vmem = pl.BlockSpec(memory_space=pltpu.VMEM)
    vmem = pltpu.VMEM
    units = layers * UNITS_LAYER
    shape = jax.ShapeDtypeStruct
    saved = [
        shape((layers, 2, rows, hidden_half), low),
        shape((layers, 2, rows, hidden_half), low),
        shape((layers, rows, width), low),
        shape((layers, rows, width), wide),
        shape((layers, 2, rows, block), low),
        shape((layers, 2, rows, 3 * block), low),
        shape((layers, 2, 2, BAND, block), low),
        shape((layers, 2, rows, LANES), wide),
        shape((layers, rows, width), low),
        shape((layers, rows, width), wide),
    ]
    others = [shape(member.shape, low) for member in weights]
    return pl.pallas_call(
        functools.partial(forward_kernel, layers, block, hidden_half),
        in_specs=[anywhere] * 2 + [in_vmem] + [anywhere] * 4 + [in_vmem] * 5,
        out_specs=[anywhere] * 2 + [in_vmem] + [anywhere] * (len(others) + len(saved)),
        out_shape=[
            shape((rows, width), low),
            shape((rows, width), low),
            shape((1, rows + BAND), jnp.int32),
        ]
        + others
        + saved,
        scratch_shapes=[
            vmem((rows, width), low),
            vmem(segments.shape, jnp.int32),
            vmem(biases[0].shape, wide),
            vmem(biases[1].shape, wide),
            vmem((rows, width), wide),
            vmem((rows, width), wide),
            vmem((rows, width), low),
            vmem((rows, width), low),
            vmem((2, 3, rows, block), low),
            vmem((layers, 2, 2, BAND, block), low),
            vmem((2, rows, block), low),
            vmem((2, rows, LANES), wide),
            vmem((2, rows, block), low),
            vmem((2, rows, block), low),
            vmem((3, width, block), low),
            vmem((2, block, width), low),
            vmem((2, width, block), low),
            vmem((2, block, width), low),
            vmem((rows // BAND, BAND, 2 * BAND), wide),
            pltpu.SemaphoreType.DMA((5,)),
            pltpu.SemaphoreType.DMA((5,)),
            pltpu.SemaphoreType.DMA((2,)),
            pltpu.SemaphoreType.DMA((4, units)),
            pltpu.SemaphoreType.DMA((4, units)),
            pltpu.SemaphoreType.DMA((layers, 2)),
            pltpu.SemaphoreType.DMA((layers, 2)),
            pltpu.SemaphoreType.DMA((2, 2)),
            pltpu.SemaphoreType.DMA((16,)),
            pltpu.SemaphoreType.DMA((2, 2)),
        ],
        compiler_params=pltpu.CompilerParams(
            collective_id=1, has_side_effects=True, vmem_limit_bytes=VMEM_ASKED
        ),
        name="forward",
    )(tokens, cotangent, segments, *weights, *biases, out_bias, gain, shift)


SLOTS = 8
CORE_SLOTS = 4
RESULT_SLOTS = 11
STAGED = 2
FIRST = 0
LAGS = dict(
    core=1, first=3, second=5, third=7, fourth=9, fifth=11, sixth=13, whole=14, stored=15
)
VECTOR_STEP = 3
VECTOR_ROWS = 12
MESH = pl.DeviceIdType.MESH
FFN_STEPS = 4
QKV_STEPS = 3


def added(left, right):
    return (left.astype(jnp.float32) + right.astype(jnp.float32)).astype(jnp.bfloat16)


def backward_kernel(layers, block, hidden_half, *refs):
    (
        cot_ref,
        gain_ref,
        segk_ref,
        out_act_ref,
        act_ref,
        slope_ref,
        normed_two_ref,
        middle_ref,
        attended_ref,
        proj_ref,
        halo_ref,
        totals_ref,
        normed_ref,
        resid_ref,
        qkv_own,
        qkv_other,
        out_own,
        out_other,
        up_own,
        up_other,
        down_own,
        down_other,
        out_act_out,
        grad_in_ref,
        out_down,
        out_up,
        out_out,
        out_qkv,
        vector_out,
        grad_branch,
        grad_attn,
        grad_before,
        grad_proj,
        grad_res,
        collected,
        grad_attended,
        qkv_buf,
        halo_buf,
        totals_buf,
        kept_kv,
        halo_send,
        halo_in,
        rows_weight,
        columns_weight,
        slope_buf,
        wide_buf,
        bias_buf,
        sums_buf,
        pair_buf,
        one_buf,
        part_buf,
        core_in,
        sent,
        held,
        kept,
        first_in,
        second_in,
        third_in,
        result,
        vec_in,
        load_sem,
        io_sem,
        halo_send_sem,
        halo_recv_sem,
        staged_sem,
        send_sems,
        recv_sems,
        store_sem,
        vec_send,
        vec_recv,
        swap_send,
        swap_recv,
    ) = refs
    half, quarter = block // 2, block // 4
    width = 2 * block
    rows_all = grad_branch.shape[0]
    pairs_half = block // LANES
    pairs = 2 * pairs_half
    low = jnp.bfloat16
    place = lax.axis_index("dp")
    y = lax.axis_index("tensor")
    core = place % 2
    x = (place // 2) % 2
    z = place // 4
    z_low = z % 2
    inner = (z + 1) // 2 % 2
    core_partner = {"dp": place + 1 - 2 * core, "tensor": y}
    x_partner = {"dp": place + 2 - 4 * x, "tensor": y}
    y_partner = {"dp": place, "tensor": 1 - y}
    z_partner = {"dp": place + 4 - 8 * z_low, "tensor": y}
    middle_partner = {"dp": place + 4 * (3 - 2 * z), "tensor": y}
    swap_partner = {"dp": place + 1 - 2 * core, "tensor": 1 - y}

    barrier = pltpu.get_barrier_semaphore()
    for partner in (core_partner, x_partner, y_partner, z_partner, swap_partner):
        pl.semaphore_signal(barrier, inc=1, device_id=partner, device_id_type=MESH)

    @pl.when(inner == 1)
    def _():
        pl.semaphore_signal(barrier, inc=1, device_id=middle_partner, device_id_type=MESH)
        pl.semaphore_wait(barrier, 6)

    @pl.when(inner == 0)
    def _():
        pl.semaphore_wait(barrier, 5)

    blocks_hidden = hidden_half // block
    plan = (
        ("rows", blocks_hidden, 2),
        ("columns", 2, blocks_hidden),
        ("rows", 1, 2),
        ("columns", 2, 3),
    )
    starts = []
    per_layer = 0
    for _, down_count, across_count in plan:
        starts.append(per_layer)
        per_layer += down_count * across_count
    chunks = layers * per_layer
    out_refs = (out_down, out_up, out_out, out_qkv)

    def block_of(index):
        return pl.ds(pl.multiple_of(index * block, block), block)

    def for_matrix(chunk, action):
        layer = layers - 1 - chunk // per_layer
        inside = chunk % per_layer
        for member, (_, down_count, across_count) in enumerate(plan):
            begin = starts[member]

            @pl.when((inside >= begin) & (inside < begin + down_count * across_count))
            def _(member=member, begin=begin, across_count=across_count):
                local = inside - begin
                action(member, layer, local // across_count, local % across_count)

    def operands_of(member, layer, i, j):
        if member == 0:
            return (
                grad_branch.at[:, block_of(j)],
                act_ref.at[layer, 0, :, block_of(i)],
                act_ref.at[layer, 1, :, block_of(i)],
            )
        if member == 1:
            return (
                normed_two_ref.at[layer, :, block_of(i)],
                grad_before.at[j // 2, :, block_of(j % 2)],
                grad_before.at[blocks_hidden // 2 + j // 2, :, block_of(j % 2)],
            )
        if member == 2:
            return (
                grad_attn.at[:, block_of(j)],
                attended_ref.at[layer, 0, :, block_of(i)],
                attended_ref.at[layer, 1, :, block_of(i)],
            )
        return (
            normed_ref.at[layer, :, block_of(i)],
            grad_proj.at[:, block_of(j)],
            grad_proj.at[:, block_of(3 + j)],
        )

    def staged_copies(chunk, shared, own, other):
        slot = chunk % STAGED
        return (
            pltpu.make_async_copy(own, pair_buf.at[slot, 0], staged_sem.at[slot, 0]),
            pltpu.make_async_copy(other, pair_buf.at[slot, 1], staged_sem.at[slot, 1]),
            pltpu.make_async_copy(shared, one_buf.at[slot], staged_sem.at[slot, 2]),
        )

    def stage_operands(chunk):
        def action(member, layer, i, j):
            for copy in staged_copies(chunk, *operands_of(member, layer, i, j)):
                copy.start()

        for_matrix(chunk, action)

    def remote(step, chunk, source, target, partner):
        slot = chunk % SLOTS
        return pltpu.make_async_remote_copy(
            src_ref=source,
            dst_ref=target,
            send_sem=send_sems.at[step, slot],
            recv_sem=recv_sems.at[step, slot],
            device_id=partner,
            device_id_type=MESH,
        )

    def x_first(chunk):
        return ((5 * chunk) % 8 < 3) | (chunk >= chunks - 1)

    def core_copy(chunk):
        return remote(
            0,
            chunk,
            part_buf.at[chunk % STAGED, :, aligned(1 - core, half)],
            core_in.at[chunk % CORE_SLOTS],
            core_partner,
        )

    low_middle = z - 1
    far_middle = 2 - z

    def first_copy(chunk, partner):
        slot = chunk % SLOTS
        return remote(1, chunk, sent.at[slot], first_in.at[slot], partner)

    def y_copy(chunk):
        slot = chunk % SLOTS
        return remote(2, chunk, kept.at[slot, 1], second_in.at[slot, 0], y_partner)

    def pair_copy(chunk):
        slot = chunk % SLOTS
        return remote(2, chunk, kept.at[slot], second_in.at[slot], z_partner)

    def single_copy(chunk):
        slot = chunk % SLOTS
        return remote(3, chunk, kept.at[slot, 0], third_in.at[slot, 0], z_partner)

    def split_copy(chunk):
        slot = chunk % SLOTS
        return remote(3, chunk, kept.at[slot, far_middle], third_in.at[slot, 0], middle_partner)

    def middle_copy(chunk):
        slot = chunk % SLOTS
        return remote(4, chunk, kept.at[slot, 0], third_in.at[slot, 1], middle_partner)

    def across_copy(chunk):
        slot = chunk % SLOTS
        return remote(4, chunk, kept.at[slot, low_middle], third_in.at[slot, 1], x_partner)

    def result_copy(step, chunk, rows, partner):
        piece = result.at[chunk % RESULT_SLOTS, rows]
        return remote(step, chunk, piece, piece, partner)

    x_rows = aligned(2 * core + x, quarter)
    core_rows = aligned(core, half)

    def middle_rows():
        return aligned(2 * core + low_middle, quarter)

    def store_copy(chunk, target):
        slot = chunk % RESULT_SLOTS
        return pltpu.make_async_copy(result.at[slot], target, store_sem.at[slot])

    def multiply(chunk):
        slot = chunk % STAGED
        for copy in staged_copies(chunk, one_buf.at[slot], pair_buf.at[slot, 0], pair_buf.at[slot, 1]):
            copy.wait()
        inside = chunk % per_layer
        by_rows = (inside < starts[1]) | ((inside >= starts[2]) & (inside < starts[3]))

        @pl.when(by_rows)
        def _():
            single = one_buf[slot]
            for which in range(2):
                part_buf[slot, which] = dot_tn(pair_buf[slot, which], single).astype(low)

        @pl.when(jnp.logical_not(by_rows))
        def _():
            single = one_buf[slot]
            for which in range(2):
                part_buf[slot, which] = dot_tn(single, pair_buf[slot, which]).astype(low)

        core_copy(chunk).start()

    def branch(chunk, by_x, by_y):
        is_x = x_first(chunk)

        @pl.when(is_x)
        def _():
            by_x()

        @pl.when(jnp.logical_not(is_x))
        def _():
            by_y()

    def on_middle(action):
        @pl.when(inner == 1)
        def _():
            action()

    def by_place(at_end, at_middle):
        @pl.when(inner == 0)
        def _():
            at_end()

        on_middle(at_middle)

    def after_core(chunk):
        slot, core_slot, part_slot = chunk % SLOTS, chunk % CORE_SLOTS, chunk % STAGED
        core_copy(chunk).wait()
        is_x = x_first(chunk).astype(jnp.int32)

        def summed(which, row):
            near = part_buf[part_slot, which, aligned(2 * core + row, quarter), :]
            return added(near, core_in[core_slot, which, aligned(row, quarter), :])

        for index in range(2):
            sent[slot, index] = summed(
                is_x * index + (1 - is_x), is_x * (1 - x) + (1 - is_x) * index
            )
        branch(
            chunk,
            lambda: first_copy(chunk, x_partner).start(),
            lambda: first_copy(chunk, y_partner).start(),
        )
        for index in range(2):
            held[slot, index] = summed(is_x * index, is_x * x + (1 - is_x) * index)

    def after_first(chunk):
        slot = chunk % SLOTS
        first_copy(chunk, y_partner).wait()
        for index in (1, 0):
            kept[slot, index] = added(held[slot, index], first_in[slot, index])

        def by_y():
            @pl.when(inner == 0)
            def _():
                pair_copy(chunk).start()

        branch(chunk, lambda: y_copy(chunk).start(), by_y)

    def after_second(chunk):
        slot = chunk % SLOTS

        def by_x():
            y_copy(chunk).wait()
            kept[slot, 0] = added(kept[slot, 0], second_in[slot, 0])

            @pl.when(inner == 0)
            def _():
                single_copy(chunk).start()

        def at_middle():
            pair_copy(chunk).wait_recv()
            kept[slot, far_middle] = added(kept[slot, far_middle], second_in[slot, far_middle])
            split_copy(chunk).start()
            kept[slot, low_middle] = added(kept[slot, low_middle], second_in[slot, low_middle])

        branch(chunk, by_x, lambda: by_place(lambda: pair_copy(chunk).wait_send(), at_middle))

    def after_third(chunk):
        slot = chunk % SLOTS

        def one_at_middle():
            single_copy(chunk).wait_recv()
            kept[slot, 0] = added(kept[slot, 0], third_in[slot, 0])
            middle_copy(chunk).start()

        def by_y():
            split_copy(chunk).wait()
            kept[slot, low_middle] = added(kept[slot, low_middle], third_in[slot, 0])
            across_copy(chunk).start()

        branch(
            chunk,
            lambda: by_place(lambda: single_copy(chunk).wait_send(), one_at_middle),
            lambda: on_middle(by_y),
        )

    def after_fourth(chunk):
        slot, result_slot = chunk % SLOTS, chunk % RESULT_SLOTS

        def by_x():
            middle_copy(chunk).wait()
            result[result_slot, x_rows, :] = added(kept[slot, 0], third_in[slot, 1])
            result_copy(5, chunk, x_rows, z_partner).start()

        def by_y():
            across_copy(chunk).wait()
            result[result_slot, middle_rows(), :] = added(
                kept[slot, low_middle], third_in[slot, 1]
            )
            result_copy(5, chunk, middle_rows(), middle_partner).start()

        branch(chunk, lambda: on_middle(by_x), lambda: on_middle(by_y))

    def after_fifth(chunk):
        def by_x():
            back = result_copy(5, chunk, x_rows, z_partner)
            by_place(back.wait_recv, back.wait_send)
            result_copy(6, chunk, x_rows, x_partner).start()

        def by_y():
            result_copy(5, chunk, middle_rows(), middle_partner).wait()
            result_copy(6, chunk, core_rows, z_partner).start()

        branch(chunk, by_x, lambda: on_middle(by_y))

    def after_sixth(chunk):
        def by_y():
            back = result_copy(6, chunk, core_rows, z_partner)
            by_place(back.wait_recv, back.wait_send)

        branch(chunk, lambda: result_copy(6, chunk, x_rows, x_partner).wait(), by_y)
        result_copy(7, chunk, core_rows, core_partner).start()

    def after_whole(chunk):
        result_copy(7, chunk, core_rows, core_partner).wait()

        def action(member, layer, i, j):
            if member == 3:
                target = out_qkv.at[layer, j, block_of(i)]
            else:
                target = out_refs[member].at[layer, block_of(i), block_of(j)]
            store_copy(chunk, target).start()

        for_matrix(chunk, action)

    def after_store(chunk):
        store_copy(chunk, result.at[chunk % RESULT_SLOTS]).wait()

    vector_partners = (core_partner, y_partner, x_partner, z_partner, middle_partner, z_partner)

    def vector_copy(step):
        target = vec_in.at[min(step, 4)]
        return pltpu.make_async_remote_copy(
            src_ref=vector_out,
            dst_ref=target,
            send_sem=vec_send.at[step],
            recv_sem=vec_recv.at[step],
            device_id=vector_partners[step],
            device_id_type=MESH,
        )

    def add_vector(step):
        vector_out[...] = vector_out[...] + vec_in[step]

    def vector_tick(step):
        if step == 0:
            vector_copy(0).start()
        elif step <= 3:
            vector_copy(step - 1).wait()
            add_vector(step - 1)
            if step < 3:
                vector_copy(step).start()
            else:

                @pl.when(inner == 0)
                def _():
                    vector_copy(3).start()

        elif step == 4:

            @pl.when(inner == 0)
            def _():
                vector_copy(3).wait_send()

            @pl.when(inner == 1)
            def _():
                vector_copy(3).wait_recv()
                add_vector(3)
                vector_copy(4).start()

        elif step == 5:

            @pl.when(inner == 1)
            def _():
                vector_copy(4).wait()
                add_vector(4)
                vector_copy(5).start()

        else:

            @pl.when(inner == 1)
            def _():
                vector_copy(5).wait_send()

            @pl.when(inner == 0)
            def _():
                vector_copy(5).wait_recv()
                vector_out[...] = vec_in[4]

    norm_two_step = FFN_STEPS
    out_step = norm_two_step + 1
    attention_step = out_step + 1
    qkv_step = attention_step + pairs + 1
    norm_one_step = qkv_step + QKV_STEPS
    period = norm_one_step + 1
    jobs = layers * period
    hidden_step = 2 * hidden_half // FFN_STEPS

    def loads(kind, slot, *sources):
        targets = {
            "ffn": (rows_weight.at[slot], columns_weight.at[slot], slope_buf.at[slot]),
            "wide": (wide_buf,),
            "out": (rows_weight.at[slot, pl.ds(0, block)], rows_weight.at[slot, pl.ds(block, block)]),
            "attention": (
                qkv_buf.at[slot, 0],
                qkv_buf.at[slot, 1],
                qkv_buf.at[slot, 2],
                halo_buf.at[slot, 0],
                halo_buf.at[slot, 1],
                totals_buf.at[slot],
            ),
            "qkv": (
                columns_weight.at[slot, :, pl.ds(0, block)],
                columns_weight.at[slot, :, pl.ds(block, block)],
            ),
        }[kind]
        sources = sources or targets
        return [
            pltpu.make_async_copy(source, target, load_sem.at[slot, index])
            for index, (source, target) in enumerate(zip(sources, targets))
        ]

    def prefetch(t):
        slot = t % 2
        layer = layers - 1 - t // period
        step = t % period

        for which, (up_ref, down_ref) in enumerate(((up_own, down_own), (up_other, down_other))):

            @pl.when((step < FFN_STEPS) & (step // (FFN_STEPS // 2) == which))
            def _(which=which, up_ref=up_ref, down_ref=down_ref):
                cut = aligned(step % (FFN_STEPS // 2), hidden_step)
                for copy in loads(
                    "ffn",
                    slot,
                    down_ref.at[layer, cut, :],
                    up_ref.at[layer, :, cut],
                    slope_ref.at[layer, which, :, cut],
                ):
                    copy.start()

        for at, source in ((norm_two_step, middle_ref), (norm_one_step, resid_ref)):

            @pl.when(step == at)
            def _(source=source):
                for copy in loads("wide", slot, source.at[layer]):
                    copy.start()

        @pl.when(step == out_step)
        def _():
            for copy in loads("out", slot, out_own.at[layer], out_other.at[layer]):
                copy.start()

        @pl.when((step >= attention_step) & (step < attention_step + pairs))
        def _():
            pair = step - attention_step
            which, inside = pair // pairs_half, pair % pairs_half

            def lanes(third):
                return aligned(third * pairs_half + inside, LANES)

            for copy in loads(
                "attention",
                slot,
                *[proj_ref.at[layer, which, :, lanes(third)] for third in range(3)],
                *[halo_ref.at[layer, which, third, :, lanes(0)] for third in range(2)],
                totals_ref.at[layer, which],
            ):
                copy.start()

        @pl.when((step >= qkv_step) & (step < qkv_step + QKV_STEPS))
        def _():
            for part in range(2):
                index = 2 * (step - qkv_step) + part
                for which, source in enumerate((qkv_own, qkv_other)):

                    @pl.when(index // 3 == which)
                    def _(part=part, index=index, source=source):
                        pltpu.make_async_copy(
                            source.at[layer, index % 3],
                            columns_weight.at[slot, :, pl.ds(part * block, block)],
                            load_sem.at[slot, part],
                        ).start()

    def wait_loads(kind, slot):
        for copy in loads(kind, slot):
            copy.wait()

    tiles = [slice(r, r + BAND) for r in range(0, rows_all, BAND)]
    fine_tiles = [slice(r, r + LANES) for r in range(0, rows_all, LANES)]

    def vector_row(layer, row):
        return pl.ds(layer * VECTOR_ROWS + row, 1)

    def column_sum(values):
        return jnp.sum(values.astype(jnp.float32), axis=0, keepdims=True)

    def ffn_job(layer, step, slot):
        wait_loads("ffn", slot)
        sums = 0.0
        for tile in tiles:
            grad_hidden = dot_nt(grad_branch[tile, :], rows_weight[slot])
            before = (grad_hidden * slope_buf[slot, tile, :].astype(jnp.float32)).astype(low)
            grad_before[step, tile, :] = before
            sums = sums + column_sum(before)
            product = dot_nt(before, columns_weight[slot])

            @pl.when(step == 0)
            def _(tile=tile, product=product):
                collected[tile, :] = product

            @pl.when(step > 0)
            def _(tile=tile, product=product):
                collected[tile, :] = collected[tile, :] + product

        per_half = FFN_STEPS // 2
        which = step // per_half
        owner = which + y - 2 * which * y
        vector_out[vector_row(layer, 2 + owner * per_half + step % per_half), :] = sums

    def norm_job(layer, index, slot):
        wait_loads("wide", slot)
        gain = gain_ref[layer, pl.ds(index, 1), :]
        gain_sum, shift_sum, attn_sum, branch_sum = 0.0, 0.0, 0.0, 0.0
        for tile in fine_tiles:
            incoming = collected[tile, :]
            values = wide_buf[tile, :]
            average = jnp.mean(values, axis=-1, keepdims=True)
            centred = values - average
            inverse = lax.rsqrt(jnp.mean(centred * centred, axis=-1, keepdims=True) + epsilon)
            unit = centred * inverse
            scaled = incoming * gain
            first_mean = jnp.mean(scaled, axis=-1, keepdims=True)
            second_mean = jnp.mean(scaled * unit, axis=-1, keepdims=True)
            total = grad_res[tile, :] + inverse * (scaled - first_mean - unit * second_mean)
            grad_res[tile, :] = total
            rounded = total.astype(low)
            gain_sum = gain_sum + column_sum(incoming * unit)
            shift_sum = shift_sum + column_sum(incoming)
            if index == 1:
                attn_sum = attn_sum + column_sum(rounded)
                branch_sum = branch_sum + column_sum(grad_branch[tile, :])
                grad_attn[tile, :] = rounded
            else:
                grad_branch[tile, :] = rounded
        vector_out[vector_row(layer, 8 + index), :] = gain_sum
        vector_out[vector_row(layer, 10 + index), :] = shift_sum
        if index == 1:
            vector_out[vector_row(layer, 6), :] = attn_sum
            vector_out[vector_row(layer, 7), :] = branch_sum

    def out_job(slot):
        wait_loads("out", slot)
        for tile in tiles:
            grad_attended[tile, :] = dot_nt(grad_attn[tile, :], rows_weight[slot]).astype(low)

    def halo_copy(pair):
        return pltpu.make_async_remote_copy(
            src_ref=halo_send.at[pair % 2],
            dst_ref=halo_in.at[pair],
            send_sem=halo_send_sem.at[pair],
            recv_sem=halo_recv_sem.at[pair],
            device_id=core_partner,
            device_id_type=MESH,
        )

    def proj_lanes(pair, third):
        which, inside = pair // pairs_half, pair % pairs_half
        return aligned(which * 3 * pairs_half + third * pairs_half + inside, LANES)

    def attention_job(pair, slot):
        wait_loads("attention", slot)
        lane = lax.broadcasted_iota(jnp.int32, (BAND, LANES), 1)
        scaling = HEAD_DIM ** (-0.5)
        count = len(tiles)
        key_parts = [None] * (count + 1)
        value_parts = [None] * (count + 1)
        here = aligned(pair, LANES)
        for index, tile in enumerate(tiles):
            query = qkv_buf[slot, 0, tile, :]
            grad = grad_attended[tile, here]
            keys = band_rows(halo_buf[slot, 0], qkv_buf[slot, 1], index)
            values = band_rows(halo_buf[slot, 1], qkv_buf[slot, 2], index)
            grad_query = []
            grad_keys = 0.0
            grad_values = 0.0
            for head in range(2):
                mine = (lane // HEAD_DIM) == head
                query_head = jnp.where(mine, query, 0)
                grad_head = jnp.where(mine, grad, 0)
                scores = dot_nt(query_head, keys) * scaling + bias_buf[index]
                total = jnp.sum(
                    jnp.where(
                        lane == 2 * (pair % pairs_half) + head, totals_buf[slot, tile, :], 0.0
                    ),
                    axis=-1,
                    keepdims=True,
                )
                exact = jnp.exp(scores - total)
                grad_probs = dot_nt(grad_head, values)
                row_terms = jnp.sum(exact * grad_probs, axis=-1, keepdims=True)
                grad_scores = (exact * (grad_probs - row_terms)).astype(low)
                grad_query.append(jnp.dot(grad_scores, keys, preferred_element_type=jnp.float32))
                grad_keys = grad_keys + dot_tn(grad_scores, query_head)
                grad_values = grad_values + dot_tn(exact.astype(low), grad_head)
            grad_proj[tile, proj_lanes(pair, 0)] = (
                jnp.where(lane < HEAD_DIM, grad_query[0], grad_query[1]) * scaling
            ).astype(low)
            grad_keys = grad_keys * scaling
            for part in range(2):
                cut = slice(part * BAND, (part + 1) * BAND)
                old_k, old_v = key_parts[index + part], value_parts[index + part]
                key_parts[index + part] = grad_keys[cut] if old_k is None else old_k + grad_keys[cut]
                value_parts[index + part] = (
                    grad_values[cut] if old_v is None else old_v + grad_values[cut]
                )
        for index in range(count - 1):
            grad_proj[tiles[index], proj_lanes(pair, 1)] = key_parts[index + 1].astype(low)
            grad_proj[tiles[index], proj_lanes(pair, 2)] = value_parts[index + 1].astype(low)
        kept_kv[pair % 2, 0] = key_parts[count]
        kept_kv[pair % 2, 1] = value_parts[count]

        @pl.when(core == 1)
        def _():
            halo_send[pair % 2, 0] = key_parts[0].astype(low)
            halo_send[pair % 2, 1] = value_parts[0].astype(low)
            halo_copy(pair).start()

    def finish_pair(pair):
        last = tiles[-1]

        @pl.when(core == 0)
        def _():
            halo_copy(pair).wait_recv()
            for third in range(2):
                grad_proj[last, proj_lanes(pair, third + 1)] = (
                    kept_kv[pair % 2, third] + halo_in[pair, third].astype(jnp.float32)
                ).astype(low)

        @pl.when(core == 1)
        def _():
            halo_copy(pair).wait_send()
            for third in range(2):
                grad_proj[last, proj_lanes(pair, third + 1)] = kept_kv[pair % 2, third].astype(low)

    def qkv_job(layer, step, slot):
        wait_loads("qkv", slot)
        sums = 0.0
        for tile in tiles:
            grad = grad_proj[tile, aligned(step, width)]
            sums = sums + column_sum(grad)
            product = dot_nt(grad, columns_weight[slot])

            @pl.when(step == 0)
            def _(tile=tile, product=product):
                collected[tile, :] = product

            @pl.when(step > 0)
            def _(tile=tile, product=product):
                collected[tile, :] = collected[tile, :] + product

        sums_buf[...] = sums
        for when, part, which, row in ((0, 0, 0, 0), (1, 0, 0, 1), (1, 1, 1, 0), (2, 1, 1, 1)):

            @pl.when(step == when)
            def _(part=part, which=which, row=row):
                owner = 1 - y if which else y
                vector_out[vector_row(layer, row), block_of(owner)] = sums_buf[
                    :, part * block : (part + 1) * block
                ]

    def job(t):
        slot = t % 2
        layer = layers - 1 - t // period
        step = t % period

        @pl.when(step < FFN_STEPS)
        def _():
            ffn_job(layer, step, slot)

        @pl.when(step == norm_two_step)
        def _():
            norm_job(layer, 1, slot)

        @pl.when(step == out_step)
        def _():
            out_job(slot)

        @pl.when((step > attention_step) & (step <= attention_step + pairs))
        def _():
            finish_pair(step - attention_step - 1)

        @pl.when((step >= attention_step) & (step < attention_step + pairs))
        def _():
            attention_job(step - attention_step, slot)

        @pl.when((step >= qkv_step) & (step < qkv_step + QKV_STEPS))
        def _():
            qkv_job(layer, step - qkv_step, slot)

        @pl.when(step == norm_one_step)
        def _():
            norm_job(layer, 0, slot)

    stages = (
        (LAGS["core"], after_core),
        (0, multiply),
        (None, job),
        (LAGS["first"], after_first),
        (LAGS["second"], after_second),
        (LAGS["third"], after_third),
        (LAGS["fourth"], after_fourth),
        (LAGS["fifth"], after_fifth),
        (LAGS["sixth"], after_sixth),
        (LAGS["stored"], after_store),
        (LAGS["whole"], after_whole),
    )

    swaps = core + y - 2 * core * y

    def swap_copy(index, source, target):
        return pltpu.make_async_remote_copy(
            src_ref=source,
            dst_ref=target,
            send_sem=swap_send.at[index],
            recv_sem=swap_recv.at[index],
            device_id=swap_partner,
            device_id_type=MESH,
        )

    def swap_start(index, source, target):
        @pl.when(swaps == 1)
        def _():
            swap_copy(index, source, target).start()

        if index:

            @pl.when(swaps == 0)
            def _():
                pltpu.make_async_copy(source, target, io_sem.at[1]).start()

    def swap_wait(index, source, target):
        @pl.when(swaps == 1)
        def _():
            swap_copy(index, source, target).wait()

        if index:

            @pl.when(swaps == 0)
            def _():
                pltpu.make_async_copy(source, target, io_sem.at[1]).wait()

    first_load = pltpu.make_async_copy(cot_ref, grad_branch, io_sem.at[0])
    first_load.start()
    prefetch(0)
    fill_band_bias(segk_ref, bias_buf)
    first_load.wait()
    for tile in tiles:
        grad_res[tile, :] = grad_branch[tile, :].astype(jnp.float32)
    stage_operands(0)
    swap_start(0, out_act_ref, out_act_out)
    vector_ticks = [jobs + VECTOR_STEP * step for step in range(7)]

    def tick(t, carry):
        @pl.when(t + 1 < jobs)
        def _():
            prefetch(t + 1)

        ahead = t + 1 - FIRST

        @pl.when((ahead > 0) & (ahead < chunks))
        def _():
            stage_operands(ahead)

        for lag, action in stages:
            if lag is None:

                @pl.when(t < jobs)
                def _():
                    job(t)

                continue
            chunk = t - FIRST - lag

            @pl.when((chunk >= 0) & (chunk < chunks))
            def _(chunk=chunk, action=action):
                action(chunk)

        @pl.when(t == chunks + FIRST + LAGS["second"] - 1)
        def _():
            swap_start(1, grad_branch, grad_in_ref)

        for step, when in enumerate(vector_ticks):

            @pl.when(t == when)
            def _(step=step):
                vector_tick(step)

        return carry

    lax.fori_loop(0, max(chunks + FIRST + LAGS["stored"], vector_ticks[-1] + 1), tick, 0)
    swap_wait(0, out_act_ref, out_act_out)
    swap_wait(1, grad_branch, grad_in_ref)


def run_backward(cotangent, gain, segk, out_act, saved, weights, block):
    rows, width = cotangent.shape
    layers, hidden_half = weights[-1].shape[0], weights[-1].shape[1]
    half, quarter = block // 2, block // 4
    low, wide = jnp.bfloat16, jnp.float32
    pairs = width // LANES
    anywhere = pl.BlockSpec(memory_space=pl.ANY)
    in_vmem = pl.BlockSpec(memory_space=pltpu.VMEM)
    vector = (layers * VECTOR_ROWS, width)
    hidden_step = 2 * hidden_half // FFN_STEPS
    vmem = pltpu.VMEM
    return pl.pallas_call(
        functools.partial(backward_kernel, layers, block, hidden_half),
        in_specs=[anywhere] + [in_vmem] * 2 + [anywhere] * (1 + len(saved) + len(weights)),
        out_specs=[anywhere] * 6 + [in_vmem],
        out_shape=[
            jax.ShapeDtypeStruct((rows, width), low),
            jax.ShapeDtypeStruct((rows, width), low),
            jax.ShapeDtypeStruct((layers, hidden_half, width), low),
            jax.ShapeDtypeStruct((layers, width, hidden_half), low),
            jax.ShapeDtypeStruct((layers, block, width), low),
            jax.ShapeDtypeStruct((layers, 3, width, block), low),
            jax.ShapeDtypeStruct(vector, wide),
        ],
        scratch_shapes=[
            vmem((rows, width), low),
            vmem((rows, width), low),
            vmem((FFN_STEPS, rows, hidden_step), low),
            vmem((rows, 6 * block), low),
            vmem((rows, width), wide),
            vmem((rows, width), wide),
            vmem((rows, width), low),
            vmem((2, 3, rows, LANES), low),
            vmem((2, 2, BAND, LANES), low),
            vmem((2, rows, LANES), wide),
            vmem((2, 2, BAND, LANES), wide),
            vmem((2, 2, BAND, LANES), low),
            vmem((pairs, 2, BAND, LANES), low),
            vmem((2, hidden_step, width), low),
            vmem((2, width, hidden_step), low),
            vmem((2, rows, hidden_step), low),
            vmem((rows, width), wide),
            vmem((rows // BAND, BAND, 2 * BAND), wide),
            vmem((1, width), wide),
            vmem((STAGED, 2, rows, block), low),
            vmem((STAGED, rows, block), low),
            vmem((STAGED, 2, block, block), low),
            vmem((CORE_SLOTS, 2, half, block), low),
            vmem((SLOTS, 2, quarter, block), low),
            vmem((SLOTS, 2, quarter, block), low),
            vmem((SLOTS, 2, quarter, block), low),
            vmem((SLOTS, 2, quarter, block), low),
            vmem((SLOTS, 2, quarter, block), low),
            vmem((SLOTS, 2, quarter, block), low),
            vmem((RESULT_SLOTS, block, block), low),
            vmem((5,) + vector, wide),
            pltpu.SemaphoreType.DMA((2, 6)),
            pltpu.SemaphoreType.DMA((2,)),
            pltpu.SemaphoreType.DMA((pairs,)),
            pltpu.SemaphoreType.DMA((pairs,)),
            pltpu.SemaphoreType.DMA((STAGED, 3)),
            pltpu.SemaphoreType.DMA((8, SLOTS)),
            pltpu.SemaphoreType.DMA((8, SLOTS)),
            pltpu.SemaphoreType.DMA((RESULT_SLOTS,)),
            pltpu.SemaphoreType.DMA((6,)),
            pltpu.SemaphoreType.DMA((6,)),
            pltpu.SemaphoreType.DMA((2,)),
            pltpu.SemaphoreType.DMA((2,)),
        ],
        compiler_params=pltpu.CompilerParams(
            collective_id=0, has_side_effects=True, vmem_limit_bytes=VMEM_ASKED
        ),
        name="backward",
    )(cotangent, gain, segk, out_act, *saved, *weights)


FINISH_DEPTH = 4


def finish_kernel(layers, steps, *refs):
    count = len(steps)
    ins, refs = refs[:count], refs[count:]
    vector_ref, refs = refs[0], refs[1:]
    (act_own, act_swapped, grad_in_ref), refs = refs[:3], refs[3:]
    outs, refs = refs[:count], refs[count:]
    qv_out, up_out, bias_out, gain_out, shift_out = refs[:5]
    (act_out, grad_in_out), refs = refs[5:7], refs[7:]
    in_bufs, refs = refs[:count], refs[count:]
    out_bufs, (moved_buf, in_sem, out_sem, copy_sem) = refs[:count], refs[count:]
    y = lax.axis_index("tensor")
    core = lax.axis_index("dp") % 2

    def fetch(index, source):
        return pltpu.make_async_copy(source, moved_buf.at[index], copy_sem.at[index])

    def put(index, target):
        return pltpu.make_async_copy(moved_buf.at[index], target, copy_sem.at[index])

    @pl.when(core == y)
    def _():
        fetch(0, act_own).start()

    @pl.when(core != y)
    def _():
        fetch(0, act_swapped).start()

    fetch(1, grad_in_ref).start()
    plan = []
    for member, (rows, parts) in enumerate(steps):
        for layer in range(layers):
            for part in range(parts):
                plan.append((member, layer, part * rows, rows, (layer * parts + part) % FINISH_DEPTH))

    def view(ref, layer, begin, rows):
        if len(ref.shape) == 4:
            return ref.at[layer, begin // rows]
        return ref.at[layer, pl.ds(begin, rows)]

    def load(entry):
        member, layer, begin, rows, slot = entry
        return pltpu.make_async_copy(
            view(ins[member], layer, begin, rows), in_bufs[member].at[slot], in_sem.at[member, slot]
        )

    def save(entry):
        member, layer, begin, rows, slot = entry
        return pltpu.make_async_copy(
            out_bufs[member].at[slot], view(outs[member], layer, begin, rows), out_sem.at[member, slot]
        )

    for entry in plan[:FINISH_DEPTH]:
        load(entry).start()
    half = qv_out.shape[2]
    for layer in range(layers):
        base = layer * VECTOR_ROWS
        for index in range(2):
            mine = pl.ds(pl.multiple_of(y * half, half), half)
            qv_out[layer, pl.ds(index, 1), :] = vector_ref[pl.ds(base + index, 1), mine]
            width = vector_ref.shape[1]
            up_out[pl.ds(layer, 1), index * width : (index + 1) * width] = vector_ref[
                pl.ds(base + 2 + 2 * y + index, 1), :
            ]
            for row, target in ((6, bias_out), (8, gain_out), (10, shift_out)):
                target[layer, pl.ds(index, 1), :] = vector_ref[pl.ds(base + row + index, 1), :]
    for index, target in enumerate((act_out, grad_in_out)):
        fetch(index, target).wait()
        put(index, target).start()
    busy = {}
    for place, entry in enumerate(plan):
        member, slot = entry[0], entry[4]
        load(entry).wait()
        if (member, slot) in busy:
            save(busy.pop((member, slot))).wait()
        out_bufs[member][slot] = in_bufs[member][slot].astype(jnp.float32)
        save(entry).start()
        busy[(member, slot)] = entry
        if place + FINISH_DEPTH < len(plan):
            load(plan[place + FINISH_DEPTH]).start()
    for entry in busy.values():
        save(entry).wait()
    for index, target in enumerate((act_out, grad_in_out)):
        put(index, target).wait()


def run_finish(reduced, vector, acts, grad_in, block):
    layers, width = reduced[0].shape[0], vector.shape[1]
    hidden_half = reduced[0].shape[1]
    wide, low = jnp.float32, jnp.bfloat16
    shape = jax.ShapeDtypeStruct
    anywhere = pl.BlockSpec(memory_space=pl.ANY)
    in_vmem = pl.BlockSpec(memory_space=pltpu.VMEM)
    steps = (
        (block, hidden_half // block),
        (block // 2, width * 2 // block),
        (block, 1),
        (width, 3),
    )
    blocks = ((block, width), (block // 2, hidden_half), (block, width), (width, block))
    deep = lambda kind: [pltpu.VMEM((FINISH_DEPTH,) + size, kind) for size in blocks]
    return pl.pallas_call(
        functools.partial(finish_kernel, layers, steps),
        in_specs=[anywhere] * len(reduced) + [in_vmem] + [anywhere] * 3,
        out_specs=[anywhere] * len(reduced) + [in_vmem] * 5 + [anywhere] * 2,
        out_shape=[shape(member.shape, wide) for member in reduced]
        + [
            shape((layers, 2, block), wide),
            shape((layers, hidden_half), wide),
            shape((layers, 2, width), wide),
            shape((layers, 2, width), wide),
            shape((layers, 2, width), wide),
        ]
        + [shape(grad_in.shape, low)] * 2,
        scratch_shapes=deep(low)
        + deep(wide)
        + [
            pltpu.VMEM((2,) + grad_in.shape, low),
            pltpu.SemaphoreType.DMA((4, FINISH_DEPTH)),
            pltpu.SemaphoreType.DMA((4, FINISH_DEPTH)),
            pltpu.SemaphoreType.DMA((2,)),
        ],
        compiler_params=pltpu.CompilerParams(vmem_limit_bytes=VMEM_ASKED),
        name="finish",
    )(*reduced, vector, *acts, grad_in)


def local_split(
    tokens_in,
    segments,
    w_qkv,
    qv_bias,
    w_out,
    w_up,
    up_bias,
    w_down,
    out_bias,
    ln_gain,
    ln_bias,
    cotangent,
):
    block = w_qkv.shape[3]
    weights = (w_qkv.transpose(0, 2, 1, 3), w_out, w_up, w_down)
    act_own, cot, segk, *rest = run_forward(
        tokens_in,
        cotangent,
        segments,
        weights,
        (qv_bias, up_bias),
        out_bias,
        ln_gain,
        ln_bias,
        block,
    )
    others, saved = rest[: len(weights)], rest[len(weights) :]
    both = [member for pair in zip(weights, others) for member in pair]
    act_swapped, grad_in, *reduced, summed = run_backward(
        cot, ln_gain, segk, act_own, saved, both, block
    )
    *grads, grad_qv, grad_up_bias, grad_bias, grad_gain, grad_shift, out_act, grad_in = run_finish(
        reduced, summed, (act_own, act_swapped), grad_in, block
    )
    grad_down, grad_up, grad_out, grad_qkv = grads
    return (
        out_act,
        grad_in,
        grad_qkv.transpose(0, 2, 1, 3),
        grad_qv,
        grad_out,
        grad_up,
        grad_up_bias,
        grad_down,
        grad_bias,
        grad_gain,
        grad_shift,
    )


def solution(mesh):
    sizes = (mesh.shape["dp"], mesh.shape["tensor"])
    local = local_split if sizes == (16, 2) else local_general
    return jax.shard_map(
        local,
        mesh=mesh,
        in_specs=(
            P(("dp", "tensor"), None),
            P("dp", None),
            P(None, None, None, "tensor"),
            P(None, None, "tensor"),
            P(None, "tensor", None),
            P(None, None, "tensor"),
            P(None, "tensor"),
            P(None, "tensor", None),
            P(),
            P(),
            P(),
            P(("dp", "tensor"), None),
        ),
        out_specs=(
            P(("dp", "tensor"), None),
            P(("dp", "tensor"), None),
            P(None, None, None, "tensor"),
            P(None, None, "tensor"),
            P(None, "tensor", None),
            P(None, None, "tensor"),
            P(None, "tensor"),
            P(None, "tensor", None),
            P(),
            P(),
            P(),
        ),
        check_vma=False,
    )
```

```python
import functools

import jax
import jax.numpy as jnp
from jax import lax
from jax.experimental import pallas as pl
from jax.experimental.pallas import tpu as pltpu
from jax.sharding import PartitionSpec as P

HEAD_DIM = 64


epsilon = 1e-05
gelu_coeff = 0.7978845608028654
cubic_coeff = 0.044715
masked_score = -1e30


def as_sent(shard):

    def short(part):
        return part.astype(jnp.bfloat16) if part.dtype == jnp.float32 else part

    return jax.tree.map(short, shard)


def layer_norm(values, gain, shift):
    average = jnp.mean(values, axis=-1, keepdims=True)
    centred = values - average
    inverse = lax.rsqrt(jnp.mean(centred * centred, axis=-1, keepdims=True) + epsilon)
    unit_rows = centred * inverse
    return (unit_rows * gain + shift, unit_rows, inverse)


def norm_backward(incoming, unit_rows, inverse, gain):
    scaled = incoming * gain
    first_mean = jnp.mean(scaled, axis=-1, keepdims=True)
    second_mean = jnp.mean(scaled * unit_rows, axis=-1, keepdims=True)
    through = inverse * (scaled - first_mean - unit_rows * second_mean)
    return (through, jnp.sum(incoming * unit_rows, axis=0), jnp.sum(incoming, axis=0))


def gelu_tanh(before):
    tanh_input = gelu_coeff * (before + cubic_coeff * before * before * before)
    return 0.5 * before * (1.0 + jnp.tanh(tanh_input))


def gelu_slope(before):
    tanh_input = gelu_coeff * (before + cubic_coeff * before * before * before)
    tangent = jnp.tanh(tanh_input)
    return 0.5 * (1.0 + tangent) + 0.5 * before * (1.0 - tangent * tangent) * gelu_coeff * (
        1.0 + 3.0 * cubic_coeff * before * before
    )


def masked_scores(query_block, key_seq, segment_row, offset, block_rows):
    window = key_seq.shape[0]
    scores = jnp.einsum(
        "qhe,khe->hqk", query_block, key_seq, preferred_element_type=jnp.float32
    ) * HEAD_DIM ** (-0.5)
    query_place = offset + lax.iota(jnp.int32, block_rows)
    key_place = lax.iota(jnp.int32, window)
    query_segment = segment_row[offset : offset + block_rows]
    allowed = (query_place[:, None] >= key_place[None, :]) & (
        query_segment[:, None] == segment_row[None, :]
    )
    return jnp.where(allowed[None], scores, masked_score)


def split_heads(flat_rows, seq_count):
    return flat_rows.reshape(
        seq_count, flat_rows.shape[0] // seq_count, flat_rows.shape[1] // HEAD_DIM, HEAD_DIM
    )


def attend_forward(query_rows, key_rows, value_rows, segments):
    seq_count, window = segments.shape
    block_rows = min(512, window)

    def one_sequence(member):
        query_seq, key_seq, value_seq, segment_row = member
        outputs = []
        totals = []
        for block_index in range(window // block_rows):
            offset = block_index * block_rows
            scores = masked_scores(
                query_seq[offset : offset + block_rows], key_seq, segment_row, offset, block_rows
            )
            highest = jnp.max(scores, axis=-1, keepdims=True)
            raised = jnp.exp(scores - highest)
            summed = jnp.sum(raised, axis=-1, keepdims=True)
            softmax_low = (raised / summed).astype(jnp.bfloat16)
            block_out = jnp.einsum(
                "hqk,khe->qhe", softmax_low, value_seq, preferred_element_type=jnp.float32
            )
            outputs.append(block_out.astype(jnp.bfloat16))
            totals.append(highest[..., 0] + jnp.log(summed[..., 0]))
        return (jnp.concatenate(outputs, axis=0), jnp.stack(totals, axis=0))

    attended, log_totals = lax.map(
        one_sequence,
        (
            split_heads(query_rows, seq_count),
            split_heads(key_rows, seq_count),
            split_heads(value_rows, seq_count),
            segments,
        ),
    )
    return (attended.reshape(query_rows.shape), log_totals)


def attend_backward(query_rows, key_rows, value_rows, segments, log_totals, grad_attended):
    seq_count, window = segments.shape
    block_rows = min(512, window)
    scaling = HEAD_DIM ** (-0.5)

    def one_sequence(member):
        query_seq, key_seq, value_seq, segment_row, totals_seq, grad_seq = member
        query_parts = []
        grad_keys = jnp.zeros(key_seq.shape, jnp.float32)
        grad_values = jnp.zeros(value_seq.shape, jnp.float32)
        for block_index in range(window // block_rows):
            offset = block_index * block_rows
            query_block = query_seq[offset : offset + block_rows]
            grad_block = grad_seq[offset : offset + block_rows]
            scores = masked_scores(query_block, key_seq, segment_row, offset, block_rows)
            softmax_exact = jnp.exp(scores - totals_seq[block_index][..., None])
            softmax_low = softmax_exact.astype(jnp.bfloat16)
            grad_softmax = jnp.einsum(
                "qhe,khe->hqk", grad_block, value_seq, preferred_element_type=jnp.float32
            )
            row_terms = jnp.sum(softmax_exact * grad_softmax, axis=-1, keepdims=True)
            grad_scores = (softmax_exact * (grad_softmax - row_terms)).astype(jnp.bfloat16)
            query_parts.append(
                jnp.einsum("hqk,khe->qhe", grad_scores, key_seq, preferred_element_type=jnp.float32)
                * scaling
            )
            grad_keys = (
                grad_keys
                + jnp.einsum(
                    "hqk,qhe->khe", grad_scores, query_block, preferred_element_type=jnp.float32
                )
                * scaling
            )
            grad_values = grad_values + jnp.einsum(
                "hqk,qhe->khe", softmax_low, grad_block, preferred_element_type=jnp.float32
            )
        grad_query = jnp.concatenate(query_parts, axis=0)
        return (
            grad_query.astype(jnp.bfloat16),
            grad_keys.astype(jnp.bfloat16),
            grad_values.astype(jnp.bfloat16),
        )

    grad_query, grad_keys, grad_values = lax.map(
        one_sequence,
        (
            split_heads(query_rows, seq_count),
            split_heads(key_rows, seq_count),
            split_heads(value_rows, seq_count),
            segments,
            log_totals,
            split_heads(grad_attended, seq_count),
        ),
    )
    return (
        grad_query.reshape(query_rows.shape),
        grad_keys.reshape(query_rows.shape),
        grad_values.reshape(query_rows.shape),
    )


def layer_forward(residual, segments, weights):
    w_qkv, qv_bias, w_out, w_up, up_bias, w_down, out_bias, gains, shifts = weights
    row_count = residual.shape[0]
    normed, unit_one, inverse_one = layer_norm(residual, gains[0], shifts[0])
    normed_all = lax.all_gather(normed.astype(jnp.bfloat16), "tensor", axis=0, tiled=True)
    projected = jnp.einsum("td,dsc->tsc", normed_all, w_qkv, preferred_element_type=jnp.float32)
    query_rows = (projected[:, 0] + qv_bias[0]).astype(jnp.bfloat16)
    key_rows = projected[:, 1].astype(jnp.bfloat16)
    value_rows = (projected[:, 2] + qv_bias[1]).astype(jnp.bfloat16)
    attended, log_totals = attend_forward(query_rows, key_rows, value_rows, segments)
    middle = (
        residual
        + lax.psum_scatter(
            jnp.dot(
                lax.slice_in_dim(attended, 0, row_count * lax.axis_size("tensor"), axis=0),
                w_out,
                preferred_element_type=jnp.float32,
            ).astype(jnp.bfloat16),
            "tensor",
            scatter_dimension=0,
            tiled=True,
        ).astype(jnp.float32)
        + out_bias[0]
    )
    normed_two, unit_two, inverse_two = layer_norm(middle, gains[1], shifts[1])
    normed_low = normed_two.astype(jnp.bfloat16)
    ffn_rows = lax.all_gather(normed_low, "tensor", axis=0, tiled=True)
    before = jnp.dot(ffn_rows, w_up, preferred_element_type=jnp.float32) + up_bias
    activated = gelu_tanh(before).astype(jnp.bfloat16)
    ffn_branch = lax.psum_scatter(
        jnp.dot(
            lax.slice_in_dim(activated, 0, row_count * lax.axis_size("tensor"), axis=0),
            w_down,
            preferred_element_type=jnp.float32,
        ).astype(jnp.bfloat16),
        "tensor",
        scatter_dimension=0,
        tiled=True,
    ).astype(jnp.float32)
    kept_ffn = (w_up, w_down)
    result = middle + ffn_branch + out_bias[1]
    kept_state = (
        unit_one,
        inverse_one,
        normed_all,
        query_rows,
        key_rows,
        value_rows,
        attended,
        log_totals,
        unit_two,
        inverse_two,
        ffn_rows,
        before,
        activated,
        kept_ffn,
    )
    return (result, kept_state)


def layer_backward(grad_residual, segments, weights, kept_state):
    w_qkv, qv_bias, w_out, w_up, up_bias, w_down, out_bias, gains, shifts = weights
    (
        unit_one,
        inverse_one,
        normed_all,
        query_rows,
        key_rows,
        value_rows,
        attended,
        log_totals,
        unit_two,
        inverse_two,
        ffn_rows,
        before,
        activated,
        kept_ffn,
    ) = kept_state
    up_used, down_used = kept_ffn
    row_count = grad_residual.shape[0]
    grad_branch = grad_residual.astype(jnp.bfloat16)
    bias_down = jnp.sum(grad_branch, axis=0, dtype=jnp.float32)
    grad_rows = lax.all_gather(grad_branch, "tensor", axis=0, tiled=True)
    grad_hidden = jnp.einsum("td,fd->tf", grad_rows, down_used, preferred_element_type=jnp.float32)
    grad_before = (grad_hidden * gelu_slope(before)).astype(jnp.bfloat16)
    grad_down = jnp.einsum("tf,td->fd", activated, grad_rows, preferred_element_type=jnp.float32)
    grad_up = jnp.einsum("td,tf->df", ffn_rows, grad_before, preferred_element_type=jnp.float32)
    grad_up_bias = jnp.sum(grad_before, axis=0, dtype=jnp.float32)
    piece_rows = lax.slice_in_dim(grad_before, 0, row_count * lax.axis_size("tensor"), axis=0)
    grad_normed_two = lax.psum_scatter(
        jnp.einsum("tf,df->td", piece_rows, w_up, preferred_element_type=jnp.float32).astype(
            jnp.bfloat16
        ),
        "tensor",
        scatter_dimension=0,
        tiled=True,
    ).astype(jnp.float32)
    through_two, gain_two, shift_two = norm_backward(
        grad_normed_two, unit_two, inverse_two, gains[1]
    )
    grad_middle = grad_residual + through_two
    grad_attn_branch = grad_middle.astype(jnp.bfloat16)
    bias_attn = jnp.sum(grad_attn_branch, axis=0, dtype=jnp.float32)
    grad_attn_all = lax.all_gather(grad_attn_branch, "tensor", axis=0, tiled=True)
    grad_out_w = jnp.einsum(
        "tc,td->cd", attended, grad_attn_all, preferred_element_type=jnp.float32
    )
    grad_attended = jnp.einsum(
        "td,cd->tc", grad_attn_all, w_out, preferred_element_type=jnp.float32
    ).astype(jnp.bfloat16)
    grad_query, grad_keys, grad_values = attend_backward(
        query_rows, key_rows, value_rows, segments, log_totals, grad_attended
    )
    grad_projected = jnp.stack((grad_query, grad_keys, grad_values), axis=1)
    grad_qkv = jnp.einsum(
        "td,tsc->dsc", normed_all, grad_projected, preferred_element_type=jnp.float32
    )
    grad_qv_bias = jnp.stack(
        (
            jnp.sum(grad_query, axis=0, dtype=jnp.float32),
            jnp.sum(grad_values, axis=0, dtype=jnp.float32),
        )
    )
    piece_rows = lax.slice_in_dim(grad_projected, 0, row_count * lax.axis_size("tensor"), axis=0)
    grad_normed = lax.psum_scatter(
        jnp.einsum("tsc,dsc->td", piece_rows, w_qkv, preferred_element_type=jnp.float32).astype(
            jnp.bfloat16
        ),
        "tensor",
        scatter_dimension=0,
        tiled=True,
    ).astype(jnp.float32)
    through_one, gain_one, shift_one = norm_backward(grad_normed, unit_one, inverse_one, gains[0])
    grad_input = grad_middle + through_one
    spread = (grad_qkv, grad_qv_bias, grad_out_w, grad_up, grad_up_bias, grad_down)
    shared = (
        jnp.stack((bias_attn, bias_down)),
        jnp.stack((gain_one, gain_two)),
        jnp.stack((shift_one, shift_two)),
    )
    return (grad_input, spread, shared)


def local_general(
    tokens_in,
    segments,
    w_qkv,
    qv_bias,
    w_out,
    w_up,
    up_bias,
    w_down,
    out_bias,
    ln_gain,
    ln_bias,
    cotangent,
):
    layers_total = w_qkv.shape[0]
    all_params = (w_qkv, qv_bias, w_out, w_up, up_bias, w_down, out_bias, ln_gain, ln_bias)
    residual = tokens_in.astype(jnp.float32)
    kept_layers = []
    for layer_index in range(layers_total):
        weights = tuple((member_array[layer_index] for member_array in all_params))
        residual, kept_state = layer_forward(residual, segments, weights)
        kept_layers.append(kept_state)
    out_act = residual.astype(jnp.bfloat16)
    grad_residual = cotangent.astype(jnp.float32)
    spread_layers = []
    shared_layers = []
    for layer_index in reversed(range(layers_total)):
        weights = tuple((member_array[layer_index] for member_array in all_params))
        grad_residual, spread, shared = layer_backward(
            grad_residual, segments, weights, kept_layers[layer_index]
        )
        spread_layers.insert(0, spread)
        shared_layers.insert(0, shared)
    spread_stack = tuple(
        (
            jnp.stack([spread_layers[layer_index][position] for layer_index in range(layers_total)])
            for position in range(6)
        )
    )
    spread_stack = jax.tree.map(
        lambda part: part.astype(jnp.float32), lax.psum(as_sent(spread_stack), "dp")
    )
    shared_stack = tuple(
        (
            jnp.stack([shared_layers[layer_index][position] for layer_index in range(layers_total)])
            for position in range(3)
        )
    )
    shared_stack = lax.psum(shared_stack, ("dp", "tensor"))
    grad_in = grad_residual.astype(jnp.bfloat16)
    return (out_act, grad_in) + tuple(spread_stack) + tuple(shared_stack)


BAND = 256
LANES = 128
VMEM_ASKED = 60 * 2**20


def dot_nt(left, right):
    return lax.dot_general(left, right, (((1,), (1,)), ((), ())), preferred_element_type=jnp.float32)


def dot_tn(left, right):
    return lax.dot_general(left, right, (((0,), (0,)), ((), ())), preferred_element_type=jnp.float32)


def dot_low(left, right):
    return jnp.dot(left, right, preferred_element_type=jnp.float32)


UNITS_LAYER = 12
Y_AHEAD = 6
HOP_BEATS = (1, 3, 5, 6)
IDLE_STEPS = 3
LOADS_AHEAD = 2


def fill_band_bias(segk_ref, bias_ref):
    wide = segk_ref.shape[1]
    values = lax.broadcasted_iota(jnp.int32, (16, wide), 0)
    member = (values == segk_ref[...]).astype(jnp.float32).astype(jnp.bfloat16)
    for block in range(bias_ref.shape[0]):
        queries = member[:, (block + 1) * BAND : (block + 2) * BAND]
        keys = member[:, block * BAND : (block + 2) * BAND]
        row_place = lax.broadcasted_iota(jnp.int32, (BAND, 2 * BAND), 0) + BAND
        column_place = lax.broadcasted_iota(jnp.int32, (BAND, 2 * BAND), 1)
        allowed = (dot_tn(queries, keys) > 0.5) & (column_place <= row_place)
        bias_ref[block] = jnp.where(allowed, 0.0, masked_score)


def band_rows(halo, rows, block):
    if block == 0:
        return jnp.concatenate([halo, rows[0:BAND, :]], axis=0)
    return rows[(block - 1) * BAND : (block + 1) * BAND, :]


def aligned(index, size):
    return pl.ds(pl.multiple_of(index * size, size), size)


def forward_kernel(layers, block, hidden_half, *refs):
    (
        tokens_ref,
        cot_ref,
        segments_ref,
        qkv_own,
        out_own,
        up_own,
        down_own,
        qv_bias_ref,
        up_bias_ref,
        out_bias_ref,
        gain_ref,
        shift_ref,
        out_act_ref,
        cot_out,
        segk_out,
        qkv_other,
        out_other,
        up_other,
        down_other,
        act_out,
        slope_out,
        normed_two_out,
        middle_out,
        attended_out,
        proj_out,
        halo_out,
        totals_out,
        normed_out,
        resid_out,
        tokens_buf,
        segments_in,
        qv_bias_in,
        up_bias_in,
        resid,
        collected,
        normed,
        normed_two,
        proj,
        halo,
        attended,
        totals,
        act_buf,
        slope_buf,
        qkv_weight,
        out_weight,
        up_weight,
        down_weight,
        qkv_arrived,
        out_arrived,
        up_arrived,
        down_arrived,
        bias_buf,
        start_send,
        start_recv,
        swap_sem,
        relay_send,
        relay_recv,
        halo_send_sem,
        halo_recv_sem,
        load_sem,
        store_sem,
        pair_store_sem,
        unit_store_sem,
    ) = refs
    width = 2 * block
    rows_all = tokens_buf.shape[0]
    pairs_half = block // LANES
    blocks_hidden = hidden_half // block
    low = jnp.bfloat16
    place = lax.axis_index("dp")
    y = lax.axis_index("tensor")
    core = place % 2
    x = (place // 2) % 2
    z = place // 4
    z_low = z % 2
    core_partner = {"dp": place + 1 - 2 * core, "tensor": y}
    x_partner = {"dp": place + 2 - 4 * x, "tensor": y}
    y_partner = {"dp": place, "tensor": 1 - y}
    z_partner = {"dp": place + 4 - 8 * z_low, "tensor": y}
    swap_partner = {"dp": place + 1 - 2 * core, "tensor": 1 - y}
    swaps = core + y - 2 * core * y

    barrier = pltpu.get_barrier_semaphore()
    for partner in (core_partner, x_partner, y_partner, z_partner, swap_partner):
        pl.semaphore_signal(barrier, inc=1, device_id=partner, device_id_type=MESH)
    pl.semaphore_wait(barrier, 5)

    def remote(source, target, send, recv, partner):
        return pltpu.make_async_remote_copy(
            src_ref=source,
            dst_ref=target,
            send_sem=send,
            recv_sem=recv,
            device_id=partner,
            device_id_type=MESH,
        )

    def swap_copy(index, source, target):
        return remote(source, target, start_send.at[index], start_recv.at[index], swap_partner)

    def swap_start(index, source, target):
        @pl.when(swaps == 1)
        def _():
            swap_copy(index, source, target).start()

        @pl.when(swaps == 0)
        def _():
            pltpu.make_async_copy(source, tokens_buf, swap_sem.at[index]).start()

    def swap_wait(index, source, target):
        @pl.when(swaps == 1)
        def _():
            swap_copy(index, source, target).wait()

        @pl.when(swaps == 0)
        def _():
            pltpu.make_async_copy(source, tokens_buf, swap_sem.at[index]).wait()

    segments_copy = remote(
        segments_ref, segments_in, start_send.at[2], start_recv.at[2], core_partner
    )
    qv_copy = remote(qv_bias_ref, qv_bias_in, start_send.at[3], start_recv.at[3], y_partner)
    up_copy = remote(up_bias_ref, up_bias_in, start_send.at[4], start_recv.at[4], y_partner)

    units = layers * UNITS_LAYER

    def for_unit(unit, action):
        layer, inside = unit // UNITS_LAYER, unit % UNITS_LAYER

        @pl.when(inside < 3)
        def _():
            action(*[ref.at[layer, inside] for ref in (qkv_own, qkv_arrived, qkv_other)])

        @pl.when(inside == 3)
        def _():
            action(*[ref.at[layer] for ref in (out_own, out_arrived, out_other)])

        cut = aligned((inside - 4) // 2, block)

        @pl.when((inside >= 4) & (inside % 2 == 0))
        def _():
            action(*[ref.at[layer, :, cut] for ref in (up_own, up_arrived, up_other)])

        @pl.when((inside >= 4) & (inside % 2 == 1))
        def _():
            action(*[ref.at[layer, cut, :] for ref in (down_own, down_arrived, down_other)])

    def hop_copy(hop, unit, source, target):
        partner = (y_partner, x_partner, z_partner, core_partner)[hop]
        return remote(source, target, relay_send.at[hop, unit], relay_recv.at[hop, unit], partner)

    def piece_of(view, hop, short):
        rows = view.shape[0]
        if hop == 3:
            return view.at[aligned(core, rows // 2)]
        if hop == 2:
            return view.at[aligned(2 * core + z_low, rows // 4)]
        if short:
            return view.at[aligned(4 * core + 2 * z_low + x, rows // 8)]
        return view.at[aligned(2 * core + x, rows // 4)]

    def by_length(unit, hop, action):
        if hop == 3:
            action(False)
            return

        @pl.when(unit % 3 != 0)
        def _():
            action(True)

        if hop < 2:

            @pl.when(unit % 3 == 0)
            def _():
                action(False)

    def hop_start(hop, unit):
        def go(own, arrived, _):
            def one(short):
                source = piece_of(own if hop == 0 else arrived, hop, short)
                hop_copy(hop, unit, source, piece_of(arrived, hop, short)).start()

            by_length(unit, hop, one)

        for_unit(unit, go)

    def hop_wait(hop, unit):
        def one(short):
            piece = piece_of(down_arrived.at[0, pl.ds(0, block), :], hop, short)
            hop_copy(hop, unit, piece, piece).wait()

        by_length(unit, hop, one)

    def when_unit(unit, action):
        @pl.when((unit >= 0) & (unit < units))
        def _():
            action(unit)

    def beat(b):
        def after_y(unit):
            hop_wait(0, unit)
            hop_start(1, unit)

        def after_x(unit):
            hop_wait(1, unit)
            hop_start(2, unit)

        def after_z(unit):
            hop_wait(2, unit)
            hop_start(3, unit)

        def after_all(unit):
            hop_wait(3, unit)

            def keep(_, arrived, other):
                pltpu.make_async_copy(arrived, other, unit_store_sem.at[unit]).start()

            for_unit(unit, keep)

        when_unit(b + Y_AHEAD, lambda unit: hop_start(0, unit))
        for lag, action in zip(HOP_BEATS, (after_y, after_x, after_z, after_all)):
            when_unit(b - lag, action)

    other_step = 2 + pairs_half + IDLE_STEPS
    out_step = other_step + 1 + pairs_half
    norm_two_step = out_step + 1
    ffn_step = norm_two_step + 1
    end_step = ffn_step + 2 * blocks_hidden
    period = end_step + 1
    jobs = layers * period

    def loads(kind, slot, *sources):
        place, targets = {
            "qkv": (blocks_hidden, (qkv_weight,)),
            "out": (blocks_hidden + 1, (out_weight,)),
            "ffn": (slot, (up_weight.at[slot], down_weight.at[slot])),
        }[kind]
        sources = sources or targets
        return [
            pltpu.make_async_copy(source, target, load_sem.at[place, index])
            for index, (source, target) in enumerate(zip(sources, targets))
        ]

    def start_all(copies):
        for copy in copies:
            copy.start()

    def wait_all(copies):
        for copy in copies:
            copy.wait()

    def prefetch(t):
        layer, step = t // period, t % period

        @pl.when(step == 1)
        def _():
            start_all(loads("qkv", 0, qkv_own.at[layer]))

        @pl.when(step == out_step)
        def _():
            start_all(loads("out", 0, out_own.at[layer]))

        @pl.when((step >= ffn_step) & (step < ffn_step + blocks_hidden))
        def _():
            inside = step - ffn_step
            cut = aligned(inside, block)
            start_all(
                loads("ffn", inside, up_own.at[layer, :, cut], down_own.at[layer, cut, :])
            )

    tiles = [slice(r, r + BAND) for r in range(0, rows_all, BAND)]
    fine_tiles = [slice(r, r + LANES) for r in range(0, rows_all, LANES)]

    def normalize(layer, index, target):
        gain = gain_ref[layer, pl.ds(index, 1), :]
        shift = shift_ref[layer, pl.ds(index, 1), :]
        for tile in fine_tiles:
            values, _, _ = layer_norm(resid[tile, :], gain, shift)
            target[tile, :] = values.astype(low)

    def store(index, source, target):
        return pltpu.make_async_copy(source, target, store_sem.at[index])

    def first_stores(layer):
        return [store(0, resid, resid_out.at[layer]), store(1, normed, normed_out.at[layer])]

    def proj_stores(layer, which):
        return [
            store(
                2 + 3 * which + third,
                proj.at[which, third],
                proj_out.at[layer, which, :, pl.ds(third * block, block)],
            )
            for third in range(3)
        ]

    def halo_store(layer, which):
        return store(8 + which, halo.at[layer, which], halo_out.at[layer, which])

    def attended_stores(layer, which):
        return [
            store(10 + which, attended.at[which], attended_out.at[layer, which]),
            store(12 + which, totals.at[which], totals_out.at[layer, which]),
        ]

    def second_stores(layer):
        return [
            store(14, resid, middle_out.at[layer]),
            store(15, normed_two, normed_two_out.at[layer]),
        ]

    def ffn_stores(layer, index, slot):
        which, inside = index // blocks_hidden, index % blocks_hidden
        cut = aligned(inside, block)
        return [
            pltpu.make_async_copy(
                buf.at[slot], out.at[layer, which, :, cut], pair_store_sem.at[slot, kind]
            )
            for kind, (buf, out) in enumerate(((act_buf, act_out), (slope_buf, slope_out)))
        ]

    def halo_copy(layer, which):
        return remote(
            proj.at[which, pl.ds(1, 2), pl.ds(rows_all - BAND, BAND)],
            halo.at[layer, which],
            halo_send_sem.at[layer, which],
            halo_recv_sem.at[layer, which],
            core_partner,
        )

    def first_job(layer):
        normalize(layer, 0, normed)
        start_all(first_stores(layer))

    def qkv_job(layer, which):
        if not which:
            wait_all(loads("qkv", 0))
        bias = qv_bias_in if which else qv_bias_ref
        for third in range(3):
            for tile in tiles:
                weight = qkv_arrived[layer, third] if which else qkv_weight[third]
                product = dot_low(normed[tile, :], weight)
                if third != 1:
                    product = product + bias[layer, pl.ds(third // 2, 1), :]
                proj[which, third, tile, :] = product.astype(low)

        @pl.when(core == 0)
        def _():
            halo_copy(layer, which).start()

        start_all(proj_stores(layer, which))

    def attention_job(layer, which, pair):
        @pl.when(pair == 0)
        def _():
            @pl.when(core == 0)
            def _():
                halo_copy(layer, which).wait_send()

            @pl.when(core == 1)
            def _():
                halo_copy(layer, which).wait_recv()

            halo_store(layer, which).start()
            totals[which] = jnp.zeros_like(totals[which])

        lane = lax.broadcasted_iota(jnp.int32, (BAND, LANES), 1)
        here = aligned(pair, LANES)
        for index, tile in enumerate(tiles):
            query = proj[which, 0, tile, here]
            keys = band_rows(halo[layer, which, 0, :, here], proj[which, 1, :, here], index)
            values = band_rows(halo[layer, which, 1, :, here], proj[which, 2, :, here], index)
            parts = []
            kept = totals[which, tile, :]
            for head in range(2):
                mine = (lane // HEAD_DIM) == head
                scores = (
                    dot_nt(jnp.where(mine, query, 0), keys) * HEAD_DIM ** (-0.5) + bias_buf[index]
                )
                highest = jnp.max(scores, axis=-1, keepdims=True)
                raised = jnp.exp(scores - highest)
                summed = jnp.sum(raised, axis=-1, keepdims=True)
                parts.append(dot_low(raised.astype(low), values) / summed)
                kept = jnp.where(lane == 2 * pair + head, highest + jnp.log(summed), kept)
            totals[which, tile, :] = kept
            attended[which, tile, here] = jnp.where(lane < HEAD_DIM, parts[0], parts[1]).astype(low)

        @pl.when(pair == pairs_half - 1)
        def _():
            start_all(attended_stores(layer, which))

    def out_job(layer):
        wait_all(loads("out", 0))
        wait_all(first_stores(layer))
        for which in range(2):
            wait_all(proj_stores(layer, which))
            halo_store(layer, which).wait()
        bias = out_bias_ref[layer, pl.ds(0, 1), :]
        for tile in tiles:
            branch = dot_low(attended[0, tile, :], out_weight[...])
            branch = branch + dot_low(attended[1, tile, :], out_arrived[layer])
            resid[tile, :] = resid[tile, :] + branch + bias

    def second_job(layer):
        normalize(layer, 1, normed_two)
        start_all(second_stores(layer))

    def ffn_job(layer, which, inside, slot):
        index = which * blocks_hidden + inside
        if not which:
            wait_all(loads("ffn", inside))

        @pl.when(index >= 2)
        def _():
            wait_all(ffn_stores(layer, index - 2, slot))

        bias = (up_bias_in if which else up_bias_ref)[pl.ds(layer, 1), aligned(inside, block)]
        cut = aligned(inside, block)
        for tile in tiles:
            up_block = up_arrived[layer, :, cut] if which else up_weight[inside]
            before = dot_low(normed_two[tile, :], up_block) + bias
            square = before * before
            tangent = jnp.tanh(gelu_coeff * before * (1.0 + cubic_coeff * square))
            raised = 0.5 * (1.0 + tangent)
            activated = (before * raised).astype(low)
            act_buf[slot, tile, :] = activated
            slope_buf[slot, tile, :] = (
                raised
                + 0.5
                * before
                * (1.0 - tangent * tangent)
                * gelu_coeff
                * (1.0 + 3.0 * cubic_coeff * square)
            ).astype(low)
            down_block = down_arrived[layer, cut, :] if which else down_weight[inside]
            product = dot_low(activated, down_block)
            if which:
                collected[tile, :] = collected[tile, :] + product
                continue

            @pl.when(inside == 0)
            def _(tile=tile, product=product):
                collected[tile, :] = product

            @pl.when(inside > 0)
            def _(tile=tile, product=product):
                collected[tile, :] = collected[tile, :] + product

        start_all(ffn_stores(layer, index, slot))

    def end_job(layer, slot):
        wait_all(ffn_stores(layer, 2 * blocks_hidden - 2, slot))
        wait_all(ffn_stores(layer, 2 * blocks_hidden - 1, 1 - slot))
        wait_all(second_stores(layer))
        for which in range(2):
            wait_all(attended_stores(layer, which))
        bias = out_bias_ref[layer, pl.ds(1, 1), :]
        for tile in tiles:
            resid[tile, :] = resid[tile, :] + collected[tile, :] + bias

    def job(t):
        slot = t % 2
        layer, step = t // period, t % period

        def at(first, count, action):
            @pl.when((step >= first) & (step < first + count))
            def _():
                action(step - first)

        at(0, 1, lambda _: first_job(layer))
        at(1, 1, lambda _: qkv_job(layer, 0))
        at(2, pairs_half, lambda pair: attention_job(layer, 0, pair))
        at(other_step, 1, lambda _: qkv_job(layer, 1))
        at(other_step + 1, pairs_half, lambda pair: attention_job(layer, 1, pair))
        at(out_step, 1, lambda _: out_job(layer))
        at(norm_two_step, 1, lambda _: second_job(layer))
        at(ffn_step, blocks_hidden, lambda inside: ffn_job(layer, 0, inside, slot))
        at(ffn_step + blocks_hidden, blocks_hidden, lambda inside: ffn_job(layer, 1, inside, slot))
        at(end_step, 1, lambda _: end_job(layer, slot))

    swap_start(0, tokens_ref, tokens_buf)
    halo[...] = jnp.zeros_like(halo)
    segments_copy.start()
    qv_copy.start()
    up_copy.start()
    for unit in range(Y_AHEAD):
        hop_start(0, unit)
    segments_copy.wait()
    window = jnp.where(core == y, segments_ref[...], segments_in[...])

    @pl.when(core == 0)
    def _():
        segk_out[:, 0:BAND] = jnp.full((1, BAND), -1, jnp.int32)
        segk_out[:, BAND:] = window[:, 0:rows_all]

    @pl.when(core == 1)
    def _():
        segk_out[...] = window[:, rows_all - BAND :]

    fill_band_bias(segk_out, bias_buf)
    qv_copy.wait()
    up_copy.wait()
    swap_wait(0, tokens_ref, tokens_buf)
    for tile in tiles:
        resid[tile, :] = tokens_buf[tile, :].astype(jnp.float32)
    cot_tick = period + other_step + 4

    def past(t, begin):
        return (t - begin) * (t > begin).astype(jnp.int32)

    def beat_at(t):
        return (10 * t - 4 * past(t, 10) - past(t, 22)) // 10

    for ahead in range(LOADS_AHEAD):
        prefetch(jnp.int32(ahead))

    def tick(t, carry):
        @pl.when((t == 0) | (beat_at(t) != beat_at(t - 1)))
        def _():
            beat(beat_at(t))

        @pl.when(t == cot_tick)
        def _():
            swap_start(1, cot_ref, cot_out)

        @pl.when((t == cot_tick + 4) & (swaps == 0))
        def _():
            pltpu.make_async_copy(cot_ref, tokens_buf, swap_sem.at[1]).wait()
            pltpu.make_async_copy(tokens_buf, cot_out, swap_sem.at[1]).start()

        @pl.when(t + LOADS_AHEAD < jobs)
        def _():
            prefetch(t + LOADS_AHEAD)

        job(t)
        return carry

    lax.fori_loop(0, jobs, tick, 0)
    for tile in tiles:
        normed_two[tile, :] = resid[tile, :].astype(low)
    last_store = store(0, normed_two, out_act_ref)
    last_store.start()
    last_store.wait()
    swap_wait(1, cot_ref, cot_out)
    for unit in range(units):
        block_ref = down_arrived.at[0, pl.ds(0, block), :]
        pltpu.make_async_copy(block_ref, block_ref, unit_store_sem.at[unit]).wait()


def run_forward(tokens, cotangent, segments, weights, biases, out_bias, gain, shift, block):
    rows, width = tokens.shape
    layers, hidden_half = weights[-1].shape[0], weights[-1].shape[1]
    low, wide = jnp.bfloat16, jnp.float32
    anywhere = pl.BlockSpec(memory_space=pl.ANY)
    in_vmem = pl.BlockSpec(memory_space=pltpu.VMEM)
    vmem = pltpu.VMEM
    units = layers * UNITS_LAYER
    shape = jax.ShapeDtypeStruct
    saved = [
        shape((layers, 2, rows, hidden_half), low),
        shape((layers, 2, rows, hidden_half), low),
        shape((layers, rows, width), low),
        shape((layers, rows, width), wide),
        shape((layers, 2, rows, block), low),
        shape((layers, 2, rows, 3 * block), low),
        shape((layers, 2, 2, BAND, block), low),
        shape((layers, 2, rows, LANES), wide),
        shape((layers, rows, width), low),
        shape((layers, rows, width), wide),
    ]
    others = [shape(member.shape, low) for member in weights]
    return pl.pallas_call(
        functools.partial(forward_kernel, layers, block, hidden_half),
        in_specs=[anywhere] * 2 + [in_vmem] + [anywhere] * 4 + [in_vmem] * 5,
        out_specs=[anywhere] * 2 + [in_vmem] + [anywhere] * (len(others) + len(saved)),
        out_shape=[
            shape((rows, width), low),
            shape((rows, width), low),
            shape((1, rows + BAND), jnp.int32),
        ]
        + others
        + saved,
        scratch_shapes=[
            vmem((rows, width), low),
            vmem(segments.shape, jnp.int32),
            vmem(biases[0].shape, wide),
            vmem(biases[1].shape, wide),
            vmem((rows, width), wide),
            vmem((rows, width), wide),
            vmem((rows, width), low),
            vmem((rows, width), low),
            vmem((2, 3, rows, block), low),
            vmem((layers, 2, 2, BAND, block), low),
            vmem((2, rows, block), low),
            vmem((2, rows, LANES), wide),
            vmem((2, rows, block), low),
            vmem((2, rows, block), low),
            vmem((3, width, block), low),
            vmem((block, width), low),
            vmem((hidden_half // block, width, block), low),
            vmem((hidden_half // block, block, width), low),
        ]
        + [vmem(member.shape, low) for member in weights]
        + [
            vmem((rows // BAND, BAND, 2 * BAND), wide),
            pltpu.SemaphoreType.DMA((5,)),
            pltpu.SemaphoreType.DMA((5,)),
            pltpu.SemaphoreType.DMA((2,)),
            pltpu.SemaphoreType.DMA((4, units)),
            pltpu.SemaphoreType.DMA((4, units)),
            pltpu.SemaphoreType.DMA((layers, 2)),
            pltpu.SemaphoreType.DMA((layers, 2)),
            pltpu.SemaphoreType.DMA((hidden_half // block + 2, 2)),
            pltpu.SemaphoreType.DMA((16,)),
            pltpu.SemaphoreType.DMA((2, 2)),
            pltpu.SemaphoreType.DMA((units,)),
        ],
        compiler_params=pltpu.CompilerParams(
            collective_id=1, has_side_effects=True, vmem_limit_bytes=VMEM_ASKED
        ),
        name="forward",
    )(tokens, cotangent, segments, *weights, *biases, out_bias, gain, shift)


SLOTS = 8
CORE_SLOTS = 4
RESULT_SLOTS = 11
STAGED = 2
FIRST = 0
LAGS = dict(
    core=1, first=3, second=5, third=7, fourth=9, fifth=11, sixth=13, whole=14, stored=15
)
VECTOR_STEP = 3
VECTOR_ROWS = 12
MESH = pl.DeviceIdType.MESH
FFN_STEPS = 4
QKV_STEPS = 3


def added(left, right):
    return (left.astype(jnp.float32) + right.astype(jnp.float32)).astype(jnp.bfloat16)


def backward_kernel(layers, block, hidden_half, *refs):
    (
        cot_ref,
        gain_ref,
        segk_ref,
        out_act_ref,
        act_ref,
        slope_ref,
        normed_two_ref,
        middle_ref,
        attended_ref,
        proj_ref,
        halo_ref,
        totals_ref,
        normed_ref,
        resid_ref,
        qkv_own,
        qkv_other,
        out_own,
        out_other,
        up_own,
        up_other,
        down_own,
        down_other,
        out_act_out,
        grad_in_ref,
        out_down,
        out_up,
        out_out,
        out_qkv,
        vector_out,
        grad_branch,
        grad_attn,
        grad_before,
        grad_proj,
        grad_res,
        collected,
        grad_attended,
        qkv_buf,
        halo_buf,
        totals_buf,
        kept_kv,
        halo_send,
        halo_in,
        rows_weight,
        columns_weight,
        slope_buf,
        wide_buf,
        bias_buf,
        sums_buf,
        pair_buf,
        one_buf,
        part_buf,
        core_in,
        sent,
        held,
        kept,
        first_in,
        second_in,
        third_in,
        result,
        vec_in,
        load_sem,
        io_sem,
        halo_send_sem,
        halo_recv_sem,
        staged_sem,
        send_sems,
        recv_sems,
        store_sem,
        vec_send,
        vec_recv,
        swap_send,
        swap_recv,
    ) = refs
    half, quarter = block // 2, block // 4
    width = 2 * block
    rows_all = grad_branch.shape[0]
    pairs_half = block // LANES
    pairs = 2 * pairs_half
    low = jnp.bfloat16
    place = lax.axis_index("dp")
    y = lax.axis_index("tensor")
    core = place % 2
    x = (place // 2) % 2
    z = place // 4
    z_low = z % 2
    inner = (z + 1) // 2 % 2
    core_partner = {"dp": place + 1 - 2 * core, "tensor": y}
    x_partner = {"dp": place + 2 - 4 * x, "tensor": y}
    y_partner = {"dp": place, "tensor": 1 - y}
    z_partner = {"dp": place + 4 - 8 * z_low, "tensor": y}
    middle_partner = {"dp": place + 4 * (3 - 2 * z), "tensor": y}
    swap_partner = {"dp": place + 1 - 2 * core, "tensor": 1 - y}

    barrier = pltpu.get_barrier_semaphore()
    for partner in (core_partner, x_partner, y_partner, z_partner, swap_partner):
        pl.semaphore_signal(barrier, inc=1, device_id=partner, device_id_type=MESH)

    @pl.when(inner == 1)
    def _():
        pl.semaphore_signal(barrier, inc=1, device_id=middle_partner, device_id_type=MESH)
        pl.semaphore_wait(barrier, 6)

    @pl.when(inner == 0)
    def _():
        pl.semaphore_wait(barrier, 5)

    blocks_hidden = hidden_half // block
    plan = (
        ("rows", blocks_hidden, 2),
        ("columns", 2, blocks_hidden),
        ("rows", 1, 2),
        ("columns", 2, 3),
    )
    starts = []
    per_layer = 0
    for _, down_count, across_count in plan:
        starts.append(per_layer)
        per_layer += down_count * across_count
    chunks = layers * per_layer
    out_refs = (out_down, out_up, out_out, out_qkv)

    def block_of(index):
        return pl.ds(pl.multiple_of(index * block, block), block)

    def for_matrix(chunk, action):
        layer = layers - 1 - chunk // per_layer
        inside = chunk % per_layer
        for member, (_, down_count, across_count) in enumerate(plan):
            begin = starts[member]

            @pl.when((inside >= begin) & (inside < begin + down_count * across_count))
            def _(member=member, begin=begin, across_count=across_count):
                local = inside - begin
                action(member, layer, local // across_count, local % across_count)

    def operands_of(member, layer, i, j):
        if member == 0:
            return (
                grad_branch.at[:, block_of(j)],
                act_ref.at[layer, 0, :, block_of(i)],
                act_ref.at[layer, 1, :, block_of(i)],
            )
        if member == 1:
            return (
                normed_two_ref.at[layer, :, block_of(i)],
                grad_before.at[j // 2, :, block_of(j % 2)],
                grad_before.at[blocks_hidden // 2 + j // 2, :, block_of(j % 2)],
            )
        if member == 2:
            return (
                grad_attn.at[:, block_of(j)],
                attended_ref.at[layer, 0, :, block_of(i)],
                attended_ref.at[layer, 1, :, block_of(i)],
            )
        return (
            normed_ref.at[layer, :, block_of(i)],
            grad_proj.at[:, block_of(j)],
            grad_proj.at[:, block_of(3 + j)],
        )

    def staged_copies(chunk, shared, own, other):
        slot = chunk % STAGED
        return (
            pltpu.make_async_copy(own, pair_buf.at[slot, 0], staged_sem.at[slot, 0]),
            pltpu.make_async_copy(other, pair_buf.at[slot, 1], staged_sem.at[slot, 1]),
            pltpu.make_async_copy(shared, one_buf.at[slot], staged_sem.at[slot, 2]),
        )

    def stage_operands(chunk):
        def action(member, layer, i, j):
            for copy in staged_copies(chunk, *operands_of(member, layer, i, j)):
                copy.start()

        for_matrix(chunk, action)

    def remote(step, chunk, source, target, partner):
        slot = chunk % SLOTS
        return pltpu.make_async_remote_copy(
            src_ref=source,
            dst_ref=target,
            send_sem=send_sems.at[step, slot],
            recv_sem=recv_sems.at[step, slot],
            device_id=partner,
            device_id_type=MESH,
        )

    def x_first(chunk):
        return ((5 * chunk) % 8 < 3) | (chunk >= chunks - 1)

    def core_copy(chunk):
        return remote(
            0,
            chunk,
            part_buf.at[chunk % STAGED, :, aligned(1 - core, half)],
            core_in.at[chunk % CORE_SLOTS],
            core_partner,
        )

    low_middle = z - 1
    far_middle = 2 - z

    def first_copy(chunk, partner):
        slot = chunk % SLOTS
        return remote(1, chunk, sent.at[slot], first_in.at[slot], partner)

    def y_copy(chunk):
        slot = chunk % SLOTS
        return remote(2, chunk, kept.at[slot, 1], second_in.at[slot, 0], y_partner)

    def pair_copy(chunk):
        slot = chunk % SLOTS
        return remote(2, chunk, kept.at[slot], second_in.at[slot], z_partner)

    def single_copy(chunk):
        slot = chunk % SLOTS
        return remote(3, chunk, kept.at[slot, 0], third_in.at[slot, 0], z_partner)

    def split_copy(chunk):
        slot = chunk % SLOTS
        return remote(3, chunk, kept.at[slot, far_middle], third_in.at[slot, 0], middle_partner)

    def middle_copy(chunk):
        slot = chunk % SLOTS
        return remote(4, chunk, kept.at[slot, 0], third_in.at[slot, 1], middle_partner)

    def across_copy(chunk):
        slot = chunk % SLOTS
        return remote(4, chunk, kept.at[slot, low_middle], third_in.at[slot, 1], x_partner)

    def result_copy(step, chunk, rows, partner):
        piece = result.at[chunk % RESULT_SLOTS, rows]
        return remote(step, chunk, piece, piece, partner)

    x_rows = aligned(2 * core + x, quarter)
    core_rows = aligned(core, half)

    def middle_rows():
        return aligned(2 * core + low_middle, quarter)

    def store_copy(chunk, target):
        slot = chunk % RESULT_SLOTS
        return pltpu.make_async_copy(result.at[slot], target, store_sem.at[slot])

    def multiply(chunk):
        slot = chunk % STAGED
        for copy in staged_copies(chunk, one_buf.at[slot], pair_buf.at[slot, 0], pair_buf.at[slot, 1]):
            copy.wait()
        inside = chunk % per_layer
        by_rows = (inside < starts[1]) | ((inside >= starts[2]) & (inside < starts[3]))

        @pl.when(by_rows)
        def _():
            single = one_buf[slot]
            for which in range(2):
                part_buf[slot, which] = dot_tn(pair_buf[slot, which], single).astype(low)

        @pl.when(jnp.logical_not(by_rows))
        def _():
            single = one_buf[slot]
            for which in range(2):
                part_buf[slot, which] = dot_tn(single, pair_buf[slot, which]).astype(low)

        core_copy(chunk).start()

    def branch(chunk, by_x, by_y):
        is_x = x_first(chunk)

        @pl.when(is_x)
        def _():
            by_x()

        @pl.when(jnp.logical_not(is_x))
        def _():
            by_y()

    def on_middle(action):
        @pl.when(inner == 1)
        def _():
            action()

    def by_place(at_end, at_middle):
        @pl.when(inner == 0)
        def _():
            at_end()

        on_middle(at_middle)

    def after_core(chunk):
        slot, core_slot, part_slot = chunk % SLOTS, chunk % CORE_SLOTS, chunk % STAGED
        core_copy(chunk).wait()
        is_x = x_first(chunk).astype(jnp.int32)

        def summed(which, row):
            near = part_buf[part_slot, which, aligned(2 * core + row, quarter), :]
            return added(near, core_in[core_slot, which, aligned(row, quarter), :])

        for index in range(2):
            sent[slot, index] = summed(
                is_x * index + (1 - is_x), is_x * (1 - x) + (1 - is_x) * index
            )
        branch(
            chunk,
            lambda: first_copy(chunk, x_partner).start(),
            lambda: first_copy(chunk, y_partner).start(),
        )
        for index in range(2):
            held[slot, index] = summed(is_x * index, is_x * x + (1 - is_x) * index)

    def after_first(chunk):
        slot = chunk % SLOTS
        first_copy(chunk, y_partner).wait()
        for index in (1, 0):
            kept[slot, index] = added(held[slot, index], first_in[slot, index])

        def by_y():
            @pl.when(inner == 0)
            def _():
                pair_copy(chunk).start()

        branch(chunk, lambda: y_copy(chunk).start(), by_y)

    def after_second(chunk):
        slot = chunk % SLOTS

        def by_x():
            y_copy(chunk).wait()
            kept[slot, 0] = added(kept[slot, 0], second_in[slot, 0])

            @pl.when(inner == 0)
            def _():
                single_copy(chunk).start()

        def at_middle():
            pair_copy(chunk).wait_recv()
            kept[slot, far_middle] = added(kept[slot, far_middle], second_in[slot, far_middle])
            split_copy(chunk).start()
            kept[slot, low_middle] = added(kept[slot, low_middle], second_in[slot, low_middle])

        branch(chunk, by_x, lambda: by_place(lambda: pair_copy(chunk).wait_send(), at_middle))

    def after_third(chunk):
        slot = chunk % SLOTS

        def one_at_middle():
            single_copy(chunk).wait_recv()
            kept[slot, 0] = added(kept[slot, 0], third_in[slot, 0])
            middle_copy(chunk).start()

        def by_y():
            split_copy(chunk).wait()
            kept[slot, low_middle] = added(kept[slot, low_middle], third_in[slot, 0])
            across_copy(chunk).start()

        branch(
            chunk,
            lambda: by_place(lambda: single_copy(chunk).wait_send(), one_at_middle),
            lambda: on_middle(by_y),
        )

    def after_fourth(chunk):
        slot, result_slot = chunk % SLOTS, chunk % RESULT_SLOTS

        def by_x():
            middle_copy(chunk).wait()
            result[result_slot, x_rows, :] = added(kept[slot, 0], third_in[slot, 1])
            result_copy(5, chunk, x_rows, z_partner).start()

        def by_y():
            across_copy(chunk).wait()
            result[result_slot, middle_rows(), :] = added(
                kept[slot, low_middle], third_in[slot, 1]
            )
            result_copy(5, chunk, middle_rows(), middle_partner).start()

        branch(chunk, lambda: on_middle(by_x), lambda: on_middle(by_y))

    def after_fifth(chunk):
        def by_x():
            back = result_copy(5, chunk, x_rows, z_partner)
            by_place(back.wait_recv, back.wait_send)
            result_copy(6, chunk, x_rows, x_partner).start()

        def by_y():
            result_copy(5, chunk, middle_rows(), middle_partner).wait()
            result_copy(6, chunk, core_rows, z_partner).start()

        branch(chunk, by_x, lambda: on_middle(by_y))

    def after_sixth(chunk):
        def by_y():
            back = result_copy(6, chunk, core_rows, z_partner)
            by_place(back.wait_recv, back.wait_send)

        branch(chunk, lambda: result_copy(6, chunk, x_rows, x_partner).wait(), by_y)
        result_copy(7, chunk, core_rows, core_partner).start()

    def after_whole(chunk):
        result_copy(7, chunk, core_rows, core_partner).wait()

        def action(member, layer, i, j):
            if member == 3:
                target = out_qkv.at[layer, j, block_of(i)]
            else:
                target = out_refs[member].at[layer, block_of(i), block_of(j)]
            store_copy(chunk, target).start()

        for_matrix(chunk, action)

    def after_store(chunk):
        store_copy(chunk, result.at[chunk % RESULT_SLOTS]).wait()

    vector_partners = (core_partner, y_partner, x_partner, z_partner, middle_partner, z_partner)

    def vector_copy(step):
        target = vec_in.at[min(step, 4)]
        return pltpu.make_async_remote_copy(
            src_ref=vector_out,
            dst_ref=target,
            send_sem=vec_send.at[step],
            recv_sem=vec_recv.at[step],
            device_id=vector_partners[step],
            device_id_type=MESH,
        )

    def add_vector(step):
        vector_out[...] = vector_out[...] + vec_in[step]

    def vector_tick(step):
        if step == 0:
            vector_copy(0).start()
        elif step <= 3:
            vector_copy(step - 1).wait()
            add_vector(step - 1)
            if step < 3:
                vector_copy(step).start()
            else:

                @pl.when(inner == 0)
                def _():
                    vector_copy(3).start()

        elif step == 4:

            @pl.when(inner == 0)
            def _():
                vector_copy(3).wait_send()

            @pl.when(inner == 1)
            def _():
                vector_copy(3).wait_recv()
                add_vector(3)
                vector_copy(4).start()

        elif step == 5:

            @pl.when(inner == 1)
            def _():
                vector_copy(4).wait()
                add_vector(4)
                vector_copy(5).start()

        else:

            @pl.when(inner == 1)
            def _():
                vector_copy(5).wait_send()

            @pl.when(inner == 0)
            def _():
                vector_copy(5).wait_recv()
                vector_out[...] = vec_in[4]

    norm_two_step = FFN_STEPS
    out_step = norm_two_step + 1
    attention_step = out_step + 1
    qkv_step = attention_step + pairs + 1
    norm_one_step = qkv_step + QKV_STEPS
    period = norm_one_step + 1
    jobs = layers * period
    hidden_step = 2 * hidden_half // FFN_STEPS

    def loads(kind, slot, *sources):
        targets = {
            "ffn": (rows_weight.at[slot], columns_weight.at[slot], slope_buf.at[slot]),
            "wide": (wide_buf,),
            "out": (rows_weight.at[slot, pl.ds(0, block)], rows_weight.at[slot, pl.ds(block, block)]),
            "attention": (
                qkv_buf.at[slot, 0],
                qkv_buf.at[slot, 1],
                qkv_buf.at[slot, 2],
                halo_buf.at[slot, 0],
                halo_buf.at[slot, 1],
                totals_buf.at[slot],
            ),
            "qkv": (
                columns_weight.at[slot, :, pl.ds(0, block)],
                columns_weight.at[slot, :, pl.ds(block, block)],
            ),
        }[kind]
        sources = sources or targets
        return [
            pltpu.make_async_copy(source, target, load_sem.at[slot, index])
            for index, (source, target) in enumerate(zip(sources, targets))
        ]

    def prefetch(t):
        slot = t % 2
        layer = layers - 1 - t // period
        step = t % period

        for which, (up_ref, down_ref) in enumerate(((up_own, down_own), (up_other, down_other))):

            @pl.when((step < FFN_STEPS) & (step // (FFN_STEPS // 2) == which))
            def _(which=which, up_ref=up_ref, down_ref=down_ref):
                cut = aligned(step % (FFN_STEPS // 2), hidden_step)
                for copy in loads(
                    "ffn",
                    slot,
                    down_ref.at[layer, cut, :],
                    up_ref.at[layer, :, cut],
                    slope_ref.at[layer, which, :, cut],
                ):
                    copy.start()

        for at, source in ((norm_two_step, middle_ref), (norm_one_step, resid_ref)):

            @pl.when(step == at)
            def _(source=source):
                for copy in loads("wide", slot, source.at[layer]):
                    copy.start()

        @pl.when(step == out_step)
        def _():
            for copy in loads("out", slot, out_own.at[layer], out_other.at[layer]):
                copy.start()

        @pl.when((step >= attention_step) & (step < attention_step + pairs))
        def _():
            pair = step - attention_step
            which, inside = pair // pairs_half, pair % pairs_half

            def lanes(third):
                return aligned(third * pairs_half + inside, LANES)

            for copy in loads(
                "attention",
                slot,
                *[proj_ref.at[layer, which, :, lanes(third)] for third in range(3)],
                *[halo_ref.at[layer, which, third, :, lanes(0)] for third in range(2)],
                totals_ref.at[layer, which],
            ):
                copy.start()

        @pl.when((step >= qkv_step) & (step < qkv_step + QKV_STEPS))
        def _():
            for part in range(2):
                index = 2 * (step - qkv_step) + part
                for which, source in enumerate((qkv_own, qkv_other)):

                    @pl.when(index // 3 == which)
                    def _(part=part, index=index, source=source):
                        pltpu.make_async_copy(
                            source.at[layer, index % 3],
                            columns_weight.at[slot, :, pl.ds(part * block, block)],
                            load_sem.at[slot, part],
                        ).start()

    def wait_loads(kind, slot):
        for copy in loads(kind, slot):
            copy.wait()

    tiles = [slice(r, r + BAND) for r in range(0, rows_all, BAND)]
    fine_tiles = [slice(r, r + LANES) for r in range(0, rows_all, LANES)]

    def vector_row(layer, row):
        return pl.ds(layer * VECTOR_ROWS + row, 1)

    def column_sum(values):
        return jnp.sum(values.astype(jnp.float32), axis=0, keepdims=True)

    def ffn_job(layer, step, slot):
        wait_loads("ffn", slot)
        sums = 0.0
        for tile in tiles:
            grad_hidden = dot_nt(grad_branch[tile, :], rows_weight[slot])
            before = (grad_hidden * slope_buf[slot, tile, :].astype(jnp.float32)).astype(low)
            grad_before[step, tile, :] = before
            sums = sums + column_sum(before)
            product = dot_nt(before, columns_weight[slot])

            @pl.when(step == 0)
            def _(tile=tile, product=product):
                collected[tile, :] = product

            @pl.when(step > 0)
            def _(tile=tile, product=product):
                collected[tile, :] = collected[tile, :] + product

        per_half = FFN_STEPS // 2
        which = step // per_half
        owner = which + y - 2 * which * y
        vector_out[vector_row(layer, 2 + owner * per_half + step % per_half), :] = sums

    def norm_job(layer, index, slot):
        wait_loads("wide", slot)
        gain = gain_ref[layer, pl.ds(index, 1), :]
        gain_sum, shift_sum, attn_sum, branch_sum = 0.0, 0.0, 0.0, 0.0
        for tile in fine_tiles:
            incoming = collected[tile, :]
            values = wide_buf[tile, :]
            average = jnp.mean(values, axis=-1, keepdims=True)
            centred = values - average
            inverse = lax.rsqrt(jnp.mean(centred * centred, axis=-1, keepdims=True) + epsilon)
            unit = centred * inverse
            scaled = incoming * gain
            first_mean = jnp.mean(scaled, axis=-1, keepdims=True)
            second_mean = jnp.mean(scaled * unit, axis=-1, keepdims=True)
            total = grad_res[tile, :] + inverse * (scaled - first_mean - unit * second_mean)
            grad_res[tile, :] = total
            rounded = total.astype(low)
            gain_sum = gain_sum + column_sum(incoming * unit)
            shift_sum = shift_sum + column_sum(incoming)
            if index == 1:
                attn_sum = attn_sum + column_sum(rounded)
                branch_sum = branch_sum + column_sum(grad_branch[tile, :])
                grad_attn[tile, :] = rounded
            else:
                grad_branch[tile, :] = rounded
        vector_out[vector_row(layer, 8 + index), :] = gain_sum
        vector_out[vector_row(layer, 10 + index), :] = shift_sum
        if index == 1:
            vector_out[vector_row(layer, 6), :] = attn_sum
            vector_out[vector_row(layer, 7), :] = branch_sum

    def out_job(slot):
        wait_loads("out", slot)
        for tile in tiles:
            grad_attended[tile, :] = dot_nt(grad_attn[tile, :], rows_weight[slot]).astype(low)

    def halo_copy(pair):
        return pltpu.make_async_remote_copy(
            src_ref=halo_send.at[pair % 2],
            dst_ref=halo_in.at[pair],
            send_sem=halo_send_sem.at[pair],
            recv_sem=halo_recv_sem.at[pair],
            device_id=core_partner,
            device_id_type=MESH,
        )

    def proj_lanes(pair, third):
        which, inside = pair // pairs_half, pair % pairs_half
        return aligned(which * 3 * pairs_half + third * pairs_half + inside, LANES)

    def attention_job(pair, slot):
        wait_loads("attention", slot)
        lane = lax.broadcasted_iota(jnp.int32, (BAND, LANES), 1)
        scaling = HEAD_DIM ** (-0.5)
        count = len(tiles)
        key_parts = [None] * (count + 1)
        value_parts = [None] * (count + 1)
        here = aligned(pair, LANES)
        for index, tile in enumerate(tiles):
            query = qkv_buf[slot, 0, tile, :]
            grad = grad_attended[tile, here]
            keys = band_rows(halo_buf[slot, 0], qkv_buf[slot, 1], index)
            values = band_rows(halo_buf[slot, 1], qkv_buf[slot, 2], index)
            grad_query = []
            grad_keys = 0.0
            grad_values = 0.0
            for head in range(2):
                mine = (lane // HEAD_DIM) == head
                query_head = jnp.where(mine, query, 0)
                grad_head = jnp.where(mine, grad, 0)
                scores = dot_nt(query_head, keys) * scaling + bias_buf[index]
                total = jnp.sum(
                    jnp.where(
                        lane == 2 * (pair % pairs_half) + head, totals_buf[slot, tile, :], 0.0
                    ),
                    axis=-1,
                    keepdims=True,
                )
                exact = jnp.exp(scores - total)
                grad_probs = dot_nt(grad_head, values)
                row_terms = jnp.sum(exact * grad_probs, axis=-1, keepdims=True)
                grad_scores = (exact * (grad_probs - row_terms)).astype(low)
                grad_query.append(jnp.dot(grad_scores, keys, preferred_element_type=jnp.float32))
                grad_keys = grad_keys + dot_tn(grad_scores, query_head)
                grad_values = grad_values + dot_tn(exact.astype(low), grad_head)
            grad_proj[tile, proj_lanes(pair, 0)] = (
                jnp.where(lane < HEAD_DIM, grad_query[0], grad_query[1]) * scaling
            ).astype(low)
            grad_keys = grad_keys * scaling
            for part in range(2):
                cut = slice(part * BAND, (part + 1) * BAND)
                old_k, old_v = key_parts[index + part], value_parts[index + part]
                key_parts[index + part] = grad_keys[cut] if old_k is None else old_k + grad_keys[cut]
                value_parts[index + part] = (
                    grad_values[cut] if old_v is None else old_v + grad_values[cut]
                )
        for index in range(count - 1):
            grad_proj[tiles[index], proj_lanes(pair, 1)] = key_parts[index + 1].astype(low)
            grad_proj[tiles[index], proj_lanes(pair, 2)] = value_parts[index + 1].astype(low)
        kept_kv[pair % 2, 0] = key_parts[count]
        kept_kv[pair % 2, 1] = value_parts[count]

        @pl.when(core == 1)
        def _():
            halo_send[pair % 2, 0] = key_parts[0].astype(low)
            halo_send[pair % 2, 1] = value_parts[0].astype(low)
            halo_copy(pair).start()

    def finish_pair(pair):
        last = tiles[-1]

        @pl.when(core == 0)
        def _():
            halo_copy(pair).wait_recv()
            for third in range(2):
                grad_proj[last, proj_lanes(pair, third + 1)] = (
                    kept_kv[pair % 2, third] + halo_in[pair, third].astype(jnp.float32)
                ).astype(low)

        @pl.when(core == 1)
        def _():
            halo_copy(pair).wait_send()
            for third in range(2):
                grad_proj[last, proj_lanes(pair, third + 1)] = kept_kv[pair % 2, third].astype(low)

    def qkv_job(layer, step, slot):
        wait_loads("qkv", slot)
        sums = 0.0
        for tile in tiles:
            grad = grad_proj[tile, aligned(step, width)]
            sums = sums + column_sum(grad)
            product = dot_nt(grad, columns_weight[slot])

            @pl.when(step == 0)
            def _(tile=tile, product=product):
                collected[tile, :] = product

            @pl.when(step > 0)
            def _(tile=tile, product=product):
                collected[tile, :] = collected[tile, :] + product

        sums_buf[...] = sums
        for when, part, which, row in ((0, 0, 0, 0), (1, 0, 0, 1), (1, 1, 1, 0), (2, 1, 1, 1)):

            @pl.when(step == when)
            def _(part=part, which=which, row=row):
                owner = 1 - y if which else y
                vector_out[vector_row(layer, row), block_of(owner)] = sums_buf[
                    :, part * block : (part + 1) * block
                ]

    def job(t):
        slot = t % 2
        layer = layers - 1 - t // period
        step = t % period

        @pl.when(step < FFN_STEPS)
        def _():
            ffn_job(layer, step, slot)

        @pl.when(step == norm_two_step)
        def _():
            norm_job(layer, 1, slot)

        @pl.when(step == out_step)
        def _():
            out_job(slot)

        @pl.when((step > attention_step) & (step <= attention_step + pairs))
        def _():
            finish_pair(step - attention_step - 1)

        @pl.when((step >= attention_step) & (step < attention_step + pairs))
        def _():
            attention_job(step - attention_step, slot)

        @pl.when((step >= qkv_step) & (step < qkv_step + QKV_STEPS))
        def _():
            qkv_job(layer, step - qkv_step, slot)

        @pl.when(step == norm_one_step)
        def _():
            norm_job(layer, 0, slot)

    stages = (
        (LAGS["core"], after_core),
        (0, multiply),
        (None, job),
        (LAGS["first"], after_first),
        (LAGS["second"], after_second),
        (LAGS["third"], after_third),
        (LAGS["fourth"], after_fourth),
        (LAGS["fifth"], after_fifth),
        (LAGS["sixth"], after_sixth),
        (LAGS["stored"], after_store),
        (LAGS["whole"], after_whole),
    )

    swaps = core + y - 2 * core * y

    def swap_copy(index, source, target):
        return pltpu.make_async_remote_copy(
            src_ref=source,
            dst_ref=target,
            send_sem=swap_send.at[index],
            recv_sem=swap_recv.at[index],
            device_id=swap_partner,
            device_id_type=MESH,
        )

    def swap_start(index, source, target):
        @pl.when(swaps == 1)
        def _():
            swap_copy(index, source, target).start()

        if index:

            @pl.when(swaps == 0)
            def _():
                pltpu.make_async_copy(source, target, io_sem.at[1]).start()

    def swap_wait(index, source, target):
        @pl.when(swaps == 1)
        def _():
            swap_copy(index, source, target).wait()

        if index:

            @pl.when(swaps == 0)
            def _():
                pltpu.make_async_copy(source, target, io_sem.at[1]).wait()

    first_load = pltpu.make_async_copy(cot_ref, grad_branch, io_sem.at[0])
    first_load.start()
    prefetch(0)
    fill_band_bias(segk_ref, bias_buf)
    first_load.wait()
    for tile in tiles:
        grad_res[tile, :] = grad_branch[tile, :].astype(jnp.float32)
    stage_operands(0)
    swap_start(0, out_act_ref, out_act_out)
    vector_ticks = [jobs + VECTOR_STEP * step for step in range(7)]

    def tick(t, carry):
        @pl.when(t + 1 < jobs)
        def _():
            prefetch(t + 1)

        ahead = t + 1 - FIRST

        @pl.when((ahead > 0) & (ahead < chunks))
        def _():
            stage_operands(ahead)

        for lag, action in stages:
            if lag is None:

                @pl.when(t < jobs)
                def _():
                    job(t)

                continue
            chunk = t - FIRST - lag

            @pl.when((chunk >= 0) & (chunk < chunks))
            def _(chunk=chunk, action=action):
                action(chunk)

        @pl.when(t == chunks + FIRST + LAGS["second"] - 1)
        def _():
            swap_start(1, grad_branch, grad_in_ref)

        for step, when in enumerate(vector_ticks):

            @pl.when(t == when)
            def _(step=step):
                vector_tick(step)

        return carry

    lax.fori_loop(0, max(chunks + FIRST + LAGS["stored"], vector_ticks[-1] + 1), tick, 0)
    swap_wait(0, out_act_ref, out_act_out)
    swap_wait(1, grad_branch, grad_in_ref)


def run_backward(cotangent, gain, segk, out_act, saved, weights, block):
    rows, width = cotangent.shape
    layers, hidden_half = weights[-1].shape[0], weights[-1].shape[1]
    half, quarter = block // 2, block // 4
    low, wide = jnp.bfloat16, jnp.float32
    pairs = width // LANES
    anywhere = pl.BlockSpec(memory_space=pl.ANY)
    in_vmem = pl.BlockSpec(memory_space=pltpu.VMEM)
    vector = (layers * VECTOR_ROWS, width)
    hidden_step = 2 * hidden_half // FFN_STEPS
    vmem = pltpu.VMEM
    return pl.pallas_call(
        functools.partial(backward_kernel, layers, block, hidden_half),
        in_specs=[anywhere] + [in_vmem] * 2 + [anywhere] * (1 + len(saved) + len(weights)),
        out_specs=[anywhere] * 6 + [in_vmem],
        out_shape=[
            jax.ShapeDtypeStruct((rows, width), low),
            jax.ShapeDtypeStruct((rows, width), low),
            jax.ShapeDtypeStruct((layers, hidden_half, width), low),
            jax.ShapeDtypeStruct((layers, width, hidden_half), low),
            jax.ShapeDtypeStruct((layers, block, width), low),
            jax.ShapeDtypeStruct((layers, 3, width, block), low),
            jax.ShapeDtypeStruct(vector, wide),
        ],
        scratch_shapes=[
            vmem((rows, width), low),
            vmem((rows, width), low),
            vmem((FFN_STEPS, rows, hidden_step), low),
            vmem((rows, 6 * block), low),
            vmem((rows, width), wide),
            vmem((rows, width), wide),
            vmem((rows, width), low),
            vmem((2, 3, rows, LANES), low),
            vmem((2, 2, BAND, LANES), low),
            vmem((2, rows, LANES), wide),
            vmem((2, 2, BAND, LANES), wide),
            vmem((2, 2, BAND, LANES), low),
            vmem((pairs, 2, BAND, LANES), low),
            vmem((2, hidden_step, width), low),
            vmem((2, width, hidden_step), low),
            vmem((2, rows, hidden_step), low),
            vmem((rows, width), wide),
            vmem((rows // BAND, BAND, 2 * BAND), wide),
            vmem((1, width), wide),
            vmem((STAGED, 2, rows, block), low),
            vmem((STAGED, rows, block), low),
            vmem((STAGED, 2, block, block), low),
            vmem((CORE_SLOTS, 2, half, block), low),
            vmem((SLOTS, 2, quarter, block), low),
            vmem((SLOTS, 2, quarter, block), low),
            vmem((SLOTS, 2, quarter, block), low),
            vmem((SLOTS, 2, quarter, block), low),
            vmem((SLOTS, 2, quarter, block), low),
            vmem((SLOTS, 2, quarter, block), low),
            vmem((RESULT_SLOTS, block, block), low),
            vmem((5,) + vector, wide),
            pltpu.SemaphoreType.DMA((2, 6)),
            pltpu.SemaphoreType.DMA((2,)),
            pltpu.SemaphoreType.DMA((pairs,)),
            pltpu.SemaphoreType.DMA((pairs,)),
            pltpu.SemaphoreType.DMA((STAGED, 3)),
            pltpu.SemaphoreType.DMA((8, SLOTS)),
            pltpu.SemaphoreType.DMA((8, SLOTS)),
            pltpu.SemaphoreType.DMA((RESULT_SLOTS,)),
            pltpu.SemaphoreType.DMA((6,)),
            pltpu.SemaphoreType.DMA((6,)),
            pltpu.SemaphoreType.DMA((2,)),
            pltpu.SemaphoreType.DMA((2,)),
        ],
        compiler_params=pltpu.CompilerParams(
            collective_id=0, has_side_effects=True, vmem_limit_bytes=VMEM_ASKED
        ),
        name="backward",
    )(cotangent, gain, segk, out_act, *saved, *weights)


FINISH_DEPTH = 4


def finish_kernel(layers, steps, *refs):
    count = len(steps)
    ins, refs = refs[:count], refs[count:]
    vector_ref, refs = refs[0], refs[1:]
    (act_own, act_swapped, grad_in_ref), refs = refs[:3], refs[3:]
    outs, refs = refs[:count], refs[count:]
    qv_out, up_out, bias_out, gain_out, shift_out = refs[:5]
    (act_out, grad_in_out), refs = refs[5:7], refs[7:]
    in_bufs, refs = refs[:count], refs[count:]
    out_bufs, (moved_buf, in_sem, out_sem, copy_sem) = refs[:count], refs[count:]
    y = lax.axis_index("tensor")
    core = lax.axis_index("dp") % 2

    def fetch(index, source):
        return pltpu.make_async_copy(source, moved_buf.at[index], copy_sem.at[index])

    def put(index, target):
        return pltpu.make_async_copy(moved_buf.at[index], target, copy_sem.at[index])

    @pl.when(core == y)
    def _():
        fetch(0, act_own).start()

    @pl.when(core != y)
    def _():
        fetch(0, act_swapped).start()

    fetch(1, grad_in_ref).start()
    plan = []
    for member, (rows, parts) in enumerate(steps):
        for layer in range(layers):
            for part in range(parts):
                plan.append((member, layer, part * rows, rows, (layer * parts + part) % FINISH_DEPTH))

    def view(ref, layer, begin, rows):
        if len(ref.shape) == 4:
            return ref.at[layer, begin // rows]
        return ref.at[layer, pl.ds(begin, rows)]

    def load(entry):
        member, layer, begin, rows, slot = entry
        return pltpu.make_async_copy(
            view(ins[member], layer, begin, rows), in_bufs[member].at[slot], in_sem.at[member, slot]
        )

    def save(entry):
        member, layer, begin, rows, slot = entry
        return pltpu.make_async_copy(
            out_bufs[member].at[slot], view(outs[member], layer, begin, rows), out_sem.at[member, slot]
        )

    for entry in plan[:FINISH_DEPTH]:
        load(entry).start()
    half = qv_out.shape[2]
    for layer in range(layers):
        base = layer * VECTOR_ROWS
        for index in range(2):
            mine = pl.ds(pl.multiple_of(y * half, half), half)
            qv_out[layer, pl.ds(index, 1), :] = vector_ref[pl.ds(base + index, 1), mine]
            width = vector_ref.shape[1]
            up_out[pl.ds(layer, 1), index * width : (index + 1) * width] = vector_ref[
                pl.ds(base + 2 + 2 * y + index, 1), :
            ]
            for row, target in ((6, bias_out), (8, gain_out), (10, shift_out)):
                target[layer, pl.ds(index, 1), :] = vector_ref[pl.ds(base + row + index, 1), :]
    for index, target in enumerate((act_out, grad_in_out)):
        fetch(index, target).wait()
        put(index, target).start()
    busy = {}
    for place, entry in enumerate(plan):
        member, slot = entry[0], entry[4]
        load(entry).wait()
        if (member, slot) in busy:
            save(busy.pop((member, slot))).wait()
        out_bufs[member][slot] = in_bufs[member][slot].astype(jnp.float32)
        save(entry).start()
        busy[(member, slot)] = entry
        if place + FINISH_DEPTH < len(plan):
            load(plan[place + FINISH_DEPTH]).start()
    for entry in busy.values():
        save(entry).wait()
    for index, target in enumerate((act_out, grad_in_out)):
        put(index, target).wait()


def run_finish(reduced, vector, acts, grad_in, block):
    layers, width = reduced[0].shape[0], vector.shape[1]
    hidden_half = reduced[0].shape[1]
    wide, low = jnp.float32, jnp.bfloat16
    shape = jax.ShapeDtypeStruct
    anywhere = pl.BlockSpec(memory_space=pl.ANY)
    in_vmem = pl.BlockSpec(memory_space=pltpu.VMEM)
    steps = (
        (block, hidden_half // block),
        (block // 2, width * 2 // block),
        (block, 1),
        (width, 3),
    )
    blocks = ((block, width), (block // 2, hidden_half), (block, width), (width, block))
    deep = lambda kind: [pltpu.VMEM((FINISH_DEPTH,) + size, kind) for size in blocks]
    return pl.pallas_call(
        functools.partial(finish_kernel, layers, steps),
        in_specs=[anywhere] * len(reduced) + [in_vmem] + [anywhere] * 3,
        out_specs=[anywhere] * len(reduced) + [in_vmem] * 5 + [anywhere] * 2,
        out_shape=[shape(member.shape, wide) for member in reduced]
        + [
            shape((layers, 2, block), wide),
            shape((layers, hidden_half), wide),
            shape((layers, 2, width), wide),
            shape((layers, 2, width), wide),
            shape((layers, 2, width), wide),
        ]
        + [shape(grad_in.shape, low)] * 2,
        scratch_shapes=deep(low)
        + deep(wide)
        + [
            pltpu.VMEM((2,) + grad_in.shape, low),
            pltpu.SemaphoreType.DMA((4, FINISH_DEPTH)),
            pltpu.SemaphoreType.DMA((4, FINISH_DEPTH)),
            pltpu.SemaphoreType.DMA((2,)),
        ],
        compiler_params=pltpu.CompilerParams(vmem_limit_bytes=VMEM_ASKED),
        name="finish",
    )(*reduced, vector, *acts, grad_in)


def local_split(
    tokens_in,
    segments,
    w_qkv,
    qv_bias,
    w_out,
    w_up,
    up_bias,
    w_down,
    out_bias,
    ln_gain,
    ln_bias,
    cotangent,
):
    block = w_qkv.shape[3]
    weights = (w_qkv.transpose(0, 2, 1, 3), w_out, w_up, w_down)
    act_own, cot, segk, *rest = run_forward(
        tokens_in,
        cotangent,
        segments,
        weights,
        (qv_bias, up_bias),
        out_bias,
        ln_gain,
        ln_bias,
        block,
    )
    others, saved = rest[: len(weights)], rest[len(weights) :]
    both = [member for pair in zip(weights, others) for member in pair]
    act_swapped, grad_in, *reduced, summed = run_backward(
        cot, ln_gain, segk, act_own, saved, both, block
    )
    *grads, grad_qv, grad_up_bias, grad_bias, grad_gain, grad_shift, out_act, grad_in = run_finish(
        reduced, summed, (act_own, act_swapped), grad_in, block
    )
    grad_down, grad_up, grad_out, grad_qkv = grads
    return (
        out_act,
        grad_in,
        grad_qkv.transpose(0, 2, 1, 3),
        grad_qv,
        grad_out,
        grad_up,
        grad_up_bias,
        grad_down,
        grad_bias,
        grad_gain,
        grad_shift,
    )


def solution(mesh):
    sizes = (mesh.shape["dp"], mesh.shape["tensor"])
    local = local_split if sizes == (16, 2) else local_general
    return jax.shard_map(
        local,
        mesh=mesh,
        in_specs=(
            P(("dp", "tensor"), None),
            P("dp", None),
            P(None, None, None, "tensor"),
            P(None, None, "tensor"),
            P(None, "tensor", None),
            P(None, None, "tensor"),
            P(None, "tensor"),
            P(None, "tensor", None),
            P(),
            P(),
            P(),
            P(("dp", "tensor"), None),
        ),
        out_specs=(
            P(("dp", "tensor"), None),
            P(("dp", "tensor"), None),
            P(None, None, None, "tensor"),
            P(None, None, "tensor"),
            P(None, "tensor", None),
            P(None, None, "tensor"),
            P(None, "tensor"),
            P(None, "tensor", None),
            P(),
            P(),
            P(),
        ),
        check_vma=False,
    )
```

```python
import functools

import jax
import jax.numpy as jnp
from jax import lax
from jax.experimental import pallas as pl
from jax.experimental.pallas import tpu as pltpu
from jax.sharding import PartitionSpec as P

HEAD_DIM = 64


epsilon = 1e-05
gelu_coeff = 0.7978845608028654
cubic_coeff = 0.044715
masked_score = -1e30


def as_sent(shard):

    def short(part):
        return part.astype(jnp.bfloat16) if part.dtype == jnp.float32 else part

    return jax.tree.map(short, shard)


def layer_norm(values, gain, shift):
    average = jnp.mean(values, axis=-1, keepdims=True)
    centred = values - average
    inverse = lax.rsqrt(jnp.mean(centred * centred, axis=-1, keepdims=True) + epsilon)
    unit_rows = centred * inverse
    return (unit_rows * gain + shift, unit_rows, inverse)


def norm_backward(incoming, unit_rows, inverse, gain):
    scaled = incoming * gain
    first_mean = jnp.mean(scaled, axis=-1, keepdims=True)
    second_mean = jnp.mean(scaled * unit_rows, axis=-1, keepdims=True)
    through = inverse * (scaled - first_mean - unit_rows * second_mean)
    return (through, jnp.sum(incoming * unit_rows, axis=0), jnp.sum(incoming, axis=0))


def gelu_tanh(before):
    tanh_input = gelu_coeff * (before + cubic_coeff * before * before * before)
    return 0.5 * before * (1.0 + jnp.tanh(tanh_input))


def gelu_slope(before):
    tanh_input = gelu_coeff * (before + cubic_coeff * before * before * before)
    tangent = jnp.tanh(tanh_input)
    return 0.5 * (1.0 + tangent) + 0.5 * before * (1.0 - tangent * tangent) * gelu_coeff * (
        1.0 + 3.0 * cubic_coeff * before * before
    )


def masked_scores(query_block, key_seq, segment_row, offset, block_rows):
    window = key_seq.shape[0]
    scores = jnp.einsum(
        "qhe,khe->hqk", query_block, key_seq, preferred_element_type=jnp.float32
    ) * HEAD_DIM ** (-0.5)
    query_place = offset + lax.iota(jnp.int32, block_rows)
    key_place = lax.iota(jnp.int32, window)
    query_segment = segment_row[offset : offset + block_rows]
    allowed = (query_place[:, None] >= key_place[None, :]) & (
        query_segment[:, None] == segment_row[None, :]
    )
    return jnp.where(allowed[None], scores, masked_score)


def split_heads(flat_rows, seq_count):
    return flat_rows.reshape(
        seq_count, flat_rows.shape[0] // seq_count, flat_rows.shape[1] // HEAD_DIM, HEAD_DIM
    )


def attend_forward(query_rows, key_rows, value_rows, segments):
    seq_count, window = segments.shape
    block_rows = min(512, window)

    def one_sequence(member):
        query_seq, key_seq, value_seq, segment_row = member
        outputs = []
        totals = []
        for block_index in range(window // block_rows):
            offset = block_index * block_rows
            scores = masked_scores(
                query_seq[offset : offset + block_rows], key_seq, segment_row, offset, block_rows
            )
            highest = jnp.max(scores, axis=-1, keepdims=True)
            raised = jnp.exp(scores - highest)
            summed = jnp.sum(raised, axis=-1, keepdims=True)
            softmax_low = (raised / summed).astype(jnp.bfloat16)
            block_out = jnp.einsum(
                "hqk,khe->qhe", softmax_low, value_seq, preferred_element_type=jnp.float32
            )
            outputs.append(block_out.astype(jnp.bfloat16))
            totals.append(highest[..., 0] + jnp.log(summed[..., 0]))
        return (jnp.concatenate(outputs, axis=0), jnp.stack(totals, axis=0))

    attended, log_totals = lax.map(
        one_sequence,
        (
            split_heads(query_rows, seq_count),
            split_heads(key_rows, seq_count),
            split_heads(value_rows, seq_count),
            segments,
        ),
    )
    return (attended.reshape(query_rows.shape), log_totals)


def attend_backward(query_rows, key_rows, value_rows, segments, log_totals, grad_attended):
    seq_count, window = segments.shape
    block_rows = min(512, window)
    scaling = HEAD_DIM ** (-0.5)

    def one_sequence(member):
        query_seq, key_seq, value_seq, segment_row, totals_seq, grad_seq = member
        query_parts = []
        grad_keys = jnp.zeros(key_seq.shape, jnp.float32)
        grad_values = jnp.zeros(value_seq.shape, jnp.float32)
        for block_index in range(window // block_rows):
            offset = block_index * block_rows
            query_block = query_seq[offset : offset + block_rows]
            grad_block = grad_seq[offset : offset + block_rows]
            scores = masked_scores(query_block, key_seq, segment_row, offset, block_rows)
            softmax_exact = jnp.exp(scores - totals_seq[block_index][..., None])
            softmax_low = softmax_exact.astype(jnp.bfloat16)
            grad_softmax = jnp.einsum(
                "qhe,khe->hqk", grad_block, value_seq, preferred_element_type=jnp.float32
            )
            row_terms = jnp.sum(softmax_exact * grad_softmax, axis=-1, keepdims=True)
            grad_scores = (softmax_exact * (grad_softmax - row_terms)).astype(jnp.bfloat16)
            query_parts.append(
                jnp.einsum("hqk,khe->qhe", grad_scores, key_seq, preferred_element_type=jnp.float32)
                * scaling
            )
            grad_keys = (
                grad_keys
                + jnp.einsum(
                    "hqk,qhe->khe", grad_scores, query_block, preferred_element_type=jnp.float32
                )
                * scaling
            )
            grad_values = grad_values + jnp.einsum(
                "hqk,qhe->khe", softmax_low, grad_block, preferred_element_type=jnp.float32
            )
        grad_query = jnp.concatenate(query_parts, axis=0)
        return (
            grad_query.astype(jnp.bfloat16),
            grad_keys.astype(jnp.bfloat16),
            grad_values.astype(jnp.bfloat16),
        )

    grad_query, grad_keys, grad_values = lax.map(
        one_sequence,
        (
            split_heads(query_rows, seq_count),
            split_heads(key_rows, seq_count),
            split_heads(value_rows, seq_count),
            segments,
            log_totals,
            split_heads(grad_attended, seq_count),
        ),
    )
    return (
        grad_query.reshape(query_rows.shape),
        grad_keys.reshape(query_rows.shape),
        grad_values.reshape(query_rows.shape),
    )


def layer_forward(residual, segments, weights):
    w_qkv, qv_bias, w_out, w_up, up_bias, w_down, out_bias, gains, shifts = weights
    row_count = residual.shape[0]
    normed, unit_one, inverse_one = layer_norm(residual, gains[0], shifts[0])
    normed_all = lax.all_gather(normed.astype(jnp.bfloat16), "tensor", axis=0, tiled=True)
    projected = jnp.einsum("td,dsc->tsc", normed_all, w_qkv, preferred_element_type=jnp.float32)
    query_rows = (projected[:, 0] + qv_bias[0]).astype(jnp.bfloat16)
    key_rows = projected[:, 1].astype(jnp.bfloat16)
    value_rows = (projected[:, 2] + qv_bias[1]).astype(jnp.bfloat16)
    attended, log_totals = attend_forward(query_rows, key_rows, value_rows, segments)
    middle = (
        residual
        + lax.psum_scatter(
            jnp.dot(
                lax.slice_in_dim(attended, 0, row_count * lax.axis_size("tensor"), axis=0),
                w_out,
                preferred_element_type=jnp.float32,
            ).astype(jnp.bfloat16),
            "tensor",
            scatter_dimension=0,
            tiled=True,
        ).astype(jnp.float32)
        + out_bias[0]
    )
    normed_two, unit_two, inverse_two = layer_norm(middle, gains[1], shifts[1])
    normed_low = normed_two.astype(jnp.bfloat16)
    ffn_rows = lax.all_gather(normed_low, "tensor", axis=0, tiled=True)
    before = jnp.dot(ffn_rows, w_up, preferred_element_type=jnp.float32) + up_bias
    activated = gelu_tanh(before).astype(jnp.bfloat16)
    ffn_branch = lax.psum_scatter(
        jnp.dot(
            lax.slice_in_dim(activated, 0, row_count * lax.axis_size("tensor"), axis=0),
            w_down,
            preferred_element_type=jnp.float32,
        ).astype(jnp.bfloat16),
        "tensor",
        scatter_dimension=0,
        tiled=True,
    ).astype(jnp.float32)
    kept_ffn = (w_up, w_down)
    result = middle + ffn_branch + out_bias[1]
    kept_state = (
        unit_one,
        inverse_one,
        normed_all,
        query_rows,
        key_rows,
        value_rows,
        attended,
        log_totals,
        unit_two,
        inverse_two,
        ffn_rows,
        before,
        activated,
        kept_ffn,
    )
    return (result, kept_state)


def layer_backward(grad_residual, segments, weights, kept_state):
    w_qkv, qv_bias, w_out, w_up, up_bias, w_down, out_bias, gains, shifts = weights
    (
        unit_one,
        inverse_one,
        normed_all,
        query_rows,
        key_rows,
        value_rows,
        attended,
        log_totals,
        unit_two,
        inverse_two,
        ffn_rows,
        before,
        activated,
        kept_ffn,
    ) = kept_state
    up_used, down_used = kept_ffn
    row_count = grad_residual.shape[0]
    grad_branch = grad_residual.astype(jnp.bfloat16)
    bias_down = jnp.sum(grad_branch, axis=0, dtype=jnp.float32)
    grad_rows = lax.all_gather(grad_branch, "tensor", axis=0, tiled=True)
    grad_hidden = jnp.einsum("td,fd->tf", grad_rows, down_used, preferred_element_type=jnp.float32)
    grad_before = (grad_hidden * gelu_slope(before)).astype(jnp.bfloat16)
    grad_down = jnp.einsum("tf,td->fd", activated, grad_rows, preferred_element_type=jnp.float32)
    grad_up = jnp.einsum("td,tf->df", ffn_rows, grad_before, preferred_element_type=jnp.float32)
    grad_up_bias = jnp.sum(grad_before, axis=0, dtype=jnp.float32)
    piece_rows = lax.slice_in_dim(grad_before, 0, row_count * lax.axis_size("tensor"), axis=0)
    grad_normed_two = lax.psum_scatter(
        jnp.einsum("tf,df->td", piece_rows, w_up, preferred_element_type=jnp.float32).astype(
            jnp.bfloat16
        ),
        "tensor",
        scatter_dimension=0,
        tiled=True,
    ).astype(jnp.float32)
    through_two, gain_two, shift_two = norm_backward(
        grad_normed_two, unit_two, inverse_two, gains[1]
    )
    grad_middle = grad_residual + through_two
    grad_attn_branch = grad_middle.astype(jnp.bfloat16)
    bias_attn = jnp.sum(grad_attn_branch, axis=0, dtype=jnp.float32)
    grad_attn_all = lax.all_gather(grad_attn_branch, "tensor", axis=0, tiled=True)
    grad_out_w = jnp.einsum(
        "tc,td->cd", attended, grad_attn_all, preferred_element_type=jnp.float32
    )
    grad_attended = jnp.einsum(
        "td,cd->tc", grad_attn_all, w_out, preferred_element_type=jnp.float32
    ).astype(jnp.bfloat16)
    grad_query, grad_keys, grad_values = attend_backward(
        query_rows, key_rows, value_rows, segments, log_totals, grad_attended
    )
    grad_projected = jnp.stack((grad_query, grad_keys, grad_values), axis=1)
    grad_qkv = jnp.einsum(
        "td,tsc->dsc", normed_all, grad_projected, preferred_element_type=jnp.float32
    )
    grad_qv_bias = jnp.stack(
        (
            jnp.sum(grad_query, axis=0, dtype=jnp.float32),
            jnp.sum(grad_values, axis=0, dtype=jnp.float32),
        )
    )
    piece_rows = lax.slice_in_dim(grad_projected, 0, row_count * lax.axis_size("tensor"), axis=0)
    grad_normed = lax.psum_scatter(
        jnp.einsum("tsc,dsc->td", piece_rows, w_qkv, preferred_element_type=jnp.float32).astype(
            jnp.bfloat16
        ),
        "tensor",
        scatter_dimension=0,
        tiled=True,
    ).astype(jnp.float32)
    through_one, gain_one, shift_one = norm_backward(grad_normed, unit_one, inverse_one, gains[0])
    grad_input = grad_middle + through_one
    spread = (grad_qkv, grad_qv_bias, grad_out_w, grad_up, grad_up_bias, grad_down)
    shared = (
        jnp.stack((bias_attn, bias_down)),
        jnp.stack((gain_one, gain_two)),
        jnp.stack((shift_one, shift_two)),
    )
    return (grad_input, spread, shared)


def local_general(
    tokens_in,
    segments,
    w_qkv,
    qv_bias,
    w_out,
    w_up,
    up_bias,
    w_down,
    out_bias,
    ln_gain,
    ln_bias,
    cotangent,
):
    layers_total = w_qkv.shape[0]
    all_params = (w_qkv, qv_bias, w_out, w_up, up_bias, w_down, out_bias, ln_gain, ln_bias)
    residual = tokens_in.astype(jnp.float32)
    kept_layers = []
    for layer_index in range(layers_total):
        weights = tuple((member_array[layer_index] for member_array in all_params))
        residual, kept_state = layer_forward(residual, segments, weights)
        kept_layers.append(kept_state)
    out_act = residual.astype(jnp.bfloat16)
    grad_residual = cotangent.astype(jnp.float32)
    spread_layers = []
    shared_layers = []
    for layer_index in reversed(range(layers_total)):
        weights = tuple((member_array[layer_index] for member_array in all_params))
        grad_residual, spread, shared = layer_backward(
            grad_residual, segments, weights, kept_layers[layer_index]
        )
        spread_layers.insert(0, spread)
        shared_layers.insert(0, shared)
    spread_stack = tuple(
        (
            jnp.stack([spread_layers[layer_index][position] for layer_index in range(layers_total)])
            for position in range(6)
        )
    )
    spread_stack = jax.tree.map(
        lambda part: part.astype(jnp.float32), lax.psum(as_sent(spread_stack), "dp")
    )
    shared_stack = tuple(
        (
            jnp.stack([shared_layers[layer_index][position] for layer_index in range(layers_total)])
            for position in range(3)
        )
    )
    shared_stack = lax.psum(shared_stack, ("dp", "tensor"))
    grad_in = grad_residual.astype(jnp.bfloat16)
    return (out_act, grad_in) + tuple(spread_stack) + tuple(shared_stack)


BAND = 256
LANES = 128
VMEM_ASKED = 60 * 2**20


def dot_nt(left, right):
    return lax.dot_general(left, right, (((1,), (1,)), ((), ())), preferred_element_type=jnp.float32)


def dot_tn(left, right):
    return lax.dot_general(left, right, (((0,), (0,)), ((), ())), preferred_element_type=jnp.float32)


def dot_low(left, right):
    return jnp.dot(left, right, preferred_element_type=jnp.float32)


UNITS_LAYER = 12
Y_AHEAD = 4
HOP_BEATS = (1, 3, 5, 6)
IDLE_STEPS = 2
LOADS_AHEAD = 2


def fill_band_bias(segk_ref, bias_ref):
    wide = segk_ref.shape[1]
    values = lax.broadcasted_iota(jnp.int32, (16, wide), 0)
    member = (values == segk_ref[...]).astype(jnp.float32).astype(jnp.bfloat16)
    for block in range(bias_ref.shape[0]):
        queries = member[:, (block + 1) * BAND : (block + 2) * BAND]
        keys = member[:, block * BAND : (block + 2) * BAND]
        row_place = lax.broadcasted_iota(jnp.int32, (BAND, 2 * BAND), 0) + BAND
        column_place = lax.broadcasted_iota(jnp.int32, (BAND, 2 * BAND), 1)
        allowed = (dot_tn(queries, keys) > 0.5) & (column_place <= row_place)
        bias_ref[block] = jnp.where(allowed, 0.0, masked_score)


def band_rows(halo, rows, block):
    if block == 0:
        return jnp.concatenate([halo, rows[0:BAND, :]], axis=0)
    return rows[(block - 1) * BAND : (block + 1) * BAND, :]


def aligned(index, size):
    return pl.ds(pl.multiple_of(index * size, size), size)


def forward_kernel(layers, block, hidden_half, *refs):
    (
        tokens_ref,
        cot_ref,
        segments_ref,
        qkv_own,
        out_own,
        up_own,
        down_own,
        qv_bias_ref,
        up_bias_ref,
        out_bias_ref,
        gain_ref,
        shift_ref,
        out_act_ref,
        cot_out,
        segk_out,
        qkv_other,
        out_other,
        up_other,
        down_other,
        act_out,
        slope_out,
        normed_two_out,
        middle_out,
        attended_out,
        proj_out,
        halo_out,
        totals_out,
        normed_out,
        resid_out,
        tokens_buf,
        segments_in,
        qv_bias_in,
        up_bias_in,
        resid,
        collected,
        normed,
        normed_two,
        proj,
        halo,
        attended,
        totals,
        act_buf,
        slope_buf,
        qkv_weight,
        out_weight,
        up_weight,
        down_weight,
        qkv_arrived,
        out_arrived,
        up_arrived,
        down_arrived,
        bias_buf,
        start_send,
        start_recv,
        swap_sem,
        relay_send,
        relay_recv,
        halo_send_sem,
        halo_recv_sem,
        load_sem,
        store_sem,
        pair_store_sem,
        unit_store_sem,
    ) = refs
    width = 2 * block
    rows_all = tokens_buf.shape[0]
    pairs_half = block // LANES
    blocks_hidden = hidden_half // block
    low = jnp.bfloat16
    place = lax.axis_index("dp")
    y = lax.axis_index("tensor")
    core = place % 2
    x = (place // 2) % 2
    z = place // 4
    z_low = z % 2
    core_partner = {"dp": place + 1 - 2 * core, "tensor": y}
    x_partner = {"dp": place + 2 - 4 * x, "tensor": y}
    y_partner = {"dp": place, "tensor": 1 - y}
    z_partner = {"dp": place + 4 - 8 * z_low, "tensor": y}
    swap_partner = {"dp": place + 1 - 2 * core, "tensor": 1 - y}
    swaps = core + y - 2 * core * y

    barrier = pltpu.get_barrier_semaphore()
    for partner in (core_partner, x_partner, y_partner, z_partner, swap_partner):
        pl.semaphore_signal(barrier, inc=1, device_id=partner, device_id_type=MESH)
    pl.semaphore_wait(barrier, 5)

    def remote(source, target, send, recv, partner):
        return pltpu.make_async_remote_copy(
            src_ref=source,
            dst_ref=target,
            send_sem=send,
            recv_sem=recv,
            device_id=partner,
            device_id_type=MESH,
        )

    def swap_copy(index, source, target):
        return remote(source, target, start_send.at[index], start_recv.at[index], swap_partner)

    def swap_start(index, source, target):
        @pl.when(swaps == 1)
        def _():
            swap_copy(index, source, target).start()

        @pl.when(swaps == 0)
        def _():
            pltpu.make_async_copy(source, tokens_buf, swap_sem.at[index]).start()

    def swap_wait(index, source, target):
        @pl.when(swaps == 1)
        def _():
            swap_copy(index, source, target).wait()

        @pl.when(swaps == 0)
        def _():
            pltpu.make_async_copy(source, tokens_buf, swap_sem.at[index]).wait()

    segments_copy = remote(
        segments_ref, segments_in, start_send.at[2], start_recv.at[2], core_partner
    )
    qv_copy = remote(qv_bias_ref, qv_bias_in, start_send.at[3], start_recv.at[3], y_partner)
    up_copy = remote(up_bias_ref, up_bias_in, start_send.at[4], start_recv.at[4], y_partner)

    units = layers * UNITS_LAYER

    def for_unit(unit, action):
        layer, inside = unit // UNITS_LAYER, unit % UNITS_LAYER

        @pl.when(inside < 3)
        def _():
            action(*[ref.at[layer, inside] for ref in (qkv_own, qkv_arrived, qkv_other)])

        @pl.when(inside == 3)
        def _():
            action(*[ref.at[layer] for ref in (out_own, out_arrived, out_other)])

        cut = aligned((inside - 4) // 2, block)

        @pl.when((inside >= 4) & (inside % 2 == 0))
        def _():
            action(*[ref.at[layer, :, cut] for ref in (up_own, up_arrived, up_other)])

        @pl.when((inside >= 4) & (inside % 2 == 1))
        def _():
            action(*[ref.at[layer, cut, :] for ref in (down_own, down_arrived, down_other)])

    def hop_copy(hop, unit, source, target):
        partner = (y_partner, x_partner, z_partner, core_partner)[hop]
        return remote(source, target, relay_send.at[hop, unit], relay_recv.at[hop, unit], partner)

    def piece_of(view, hop, short):
        rows = view.shape[0]
        if hop == 3:
            return view.at[aligned(core, rows // 2)]
        if hop == 2:
            return view.at[aligned(2 * core + z_low, rows // 4)]
        if short:
            return view.at[aligned(4 * core + 2 * z_low + x, rows // 8)]
        return view.at[aligned(2 * core + x, rows // 4)]

    def by_length(unit, hop, action):
        if hop == 3:
            action(False)
            return

        whole = (unit % 3 == 0) & (unit > 0)

        @pl.when(jnp.logical_not(whole))
        def _():
            action(True)

        if hop < 2:

            @pl.when(whole)
            def _():
                action(False)

    def hop_start(hop, unit):
        def go(own, arrived, _):
            def one(short):
                source = piece_of(own if hop == 0 else arrived, hop, short)
                hop_copy(hop, unit, source, piece_of(arrived, hop, short)).start()

            by_length(unit, hop, one)

        for_unit(unit, go)

    def hop_wait(hop, unit):
        def one(short):
            piece = piece_of(down_arrived.at[0, pl.ds(0, block), :], hop, short)
            hop_copy(hop, unit, piece, piece).wait()

        by_length(unit, hop, one)

    def when_unit(unit, action):
        @pl.when((unit >= 0) & (unit < units))
        def _():
            action(unit)

    def beat(b):
        def after_y(unit):
            hop_wait(0, unit)
            hop_start(1, unit)

        def after_x(unit):
            hop_wait(1, unit)
            hop_start(2, unit)

        def after_z(unit):
            hop_wait(2, unit)
            hop_start(3, unit)

        def after_all(unit):
            hop_wait(3, unit)

            def keep(_, arrived, other):
                pltpu.make_async_copy(arrived, other, unit_store_sem.at[unit]).start()

            for_unit(unit, keep)

        when_unit(b + Y_AHEAD, lambda unit: hop_start(0, unit))
        for lag, action in zip(HOP_BEATS, (after_y, after_x, after_z, after_all)):
            when_unit(b - lag, action)

    other_step = 2 + pairs_half + IDLE_STEPS
    out_step = other_step + 1 + pairs_half
    norm_two_step = out_step + 1
    ffn_step = norm_two_step + 1
    end_step = ffn_step + 2 * blocks_hidden
    period = end_step + 1
    jobs = layers * period

    def loads(kind, slot, *sources):
        place, targets = {
            "qkv": (blocks_hidden, (qkv_weight,)),
            "out": (blocks_hidden + 1, (out_weight,)),
            "ffn": (slot, (up_weight.at[slot], down_weight.at[slot])),
        }[kind]
        sources = sources or targets
        return [
            pltpu.make_async_copy(source, target, load_sem.at[place, index])
            for index, (source, target) in enumerate(zip(sources, targets))
        ]

    def start_all(copies):
        for copy in copies:
            copy.start()

    def wait_all(copies):
        for copy in copies:
            copy.wait()

    def prefetch(t):
        layer, step = t // period, t % period

        @pl.when(step == 1)
        def _():
            start_all(loads("qkv", 0, qkv_own.at[layer]))

        @pl.when(step == out_step)
        def _():
            start_all(loads("out", 0, out_own.at[layer]))

        @pl.when((step >= ffn_step) & (step < ffn_step + blocks_hidden))
        def _():
            inside = step - ffn_step
            cut = aligned(inside, block)
            start_all(
                loads("ffn", inside, up_own.at[layer, :, cut], down_own.at[layer, cut, :])
            )

    tiles = [slice(r, r + BAND) for r in range(0, rows_all, BAND)]
    fine_tiles = [slice(r, r + LANES) for r in range(0, rows_all, LANES)]

    def normalize(layer, index, target):
        gain = gain_ref[layer, pl.ds(index, 1), :]
        shift = shift_ref[layer, pl.ds(index, 1), :]
        for tile in fine_tiles:
            values, _, _ = layer_norm(resid[tile, :], gain, shift)
            target[tile, :] = values.astype(low)

    def store(index, source, target):
        return pltpu.make_async_copy(source, target, store_sem.at[index])

    def first_stores(layer):
        return [store(0, resid, resid_out.at[layer]), store(1, normed, normed_out.at[layer])]

    def proj_stores(layer, which):
        return [
            store(
                2 + 3 * which + third,
                proj.at[which, third],
                proj_out.at[layer, which, :, pl.ds(third * block, block)],
            )
            for third in range(3)
        ]

    def halo_store(layer, which):
        return store(8 + which, halo.at[layer, which], halo_out.at[layer, which])

    def attended_stores(layer, which):
        return [
            store(10 + which, attended.at[which], attended_out.at[layer, which]),
            store(12 + which, totals.at[which], totals_out.at[layer, which]),
        ]

    def second_stores(layer):
        return [
            store(14, resid, middle_out.at[layer]),
            store(15, normed_two, normed_two_out.at[layer]),
        ]

    def ffn_stores(layer, index, slot):
        which, inside = index // blocks_hidden, index % blocks_hidden
        cut = aligned(inside, block)
        return [
            pltpu.make_async_copy(
                buf.at[slot], out.at[layer, which, :, cut], pair_store_sem.at[slot, kind]
            )
            for kind, (buf, out) in enumerate(((act_buf, act_out), (slope_buf, slope_out)))
        ]

    def halo_copy(layer, which):
        return remote(
            proj.at[which, pl.ds(1, 2), pl.ds(rows_all - BAND, BAND)],
            halo.at[layer, which],
            halo_send_sem.at[layer, which],
            halo_recv_sem.at[layer, which],
            core_partner,
        )

    def first_job(layer):
        normalize(layer, 0, normed)
        start_all(first_stores(layer))

    def qkv_job(layer, which):
        if not which:
            wait_all(loads("qkv", 0))
        bias = qv_bias_in if which else qv_bias_ref
        for third in (1, 2, 0):
            for tile in tiles:
                weight = qkv_arrived[layer, third] if which else qkv_weight[third]
                product = dot_low(normed[tile, :], weight)
                if third != 1:
                    product = product + bias[layer, pl.ds(third // 2, 1), :]
                proj[which, third, tile, :] = product.astype(low)
            if third == 2:

                @pl.when(core == 0)
                def _():
                    halo_copy(layer, which).start()

        start_all(proj_stores(layer, which))

    def attention_job(layer, which, pair):
        @pl.when(pair == 0)
        def _():
            totals[which] = jnp.zeros_like(totals[which])

        lane = lax.broadcasted_iota(jnp.int32, (BAND, LANES), 1)
        here = aligned(pair, LANES)
        for index, tile in reversed(list(enumerate(tiles))):
            if index == 0:

                @pl.when(pair == 0)
                def _():
                    @pl.when(core == 0)
                    def _():
                        halo_copy(layer, which).wait_send()

                    @pl.when(core == 1)
                    def _():
                        halo_copy(layer, which).wait_recv()

                    halo_store(layer, which).start()

            query = proj[which, 0, tile, here]
            first = [halo[layer, which, part, :, here] if index == 0 else None for part in range(2)]
            keys = band_rows(first[0], proj[which, 1, :, here], index)
            values = band_rows(first[1], proj[which, 2, :, here], index)
            parts = []
            kept = totals[which, tile, :]
            for head in range(2):
                mine = (lane // HEAD_DIM) == head
                scores = (
                    dot_nt(jnp.where(mine, query, 0), keys) * HEAD_DIM ** (-0.5) + bias_buf[index]
                )
                highest = jnp.max(scores, axis=-1, keepdims=True)
                raised = jnp.exp(scores - highest)
                summed = jnp.sum(raised, axis=-1, keepdims=True)
                parts.append(dot_low(raised.astype(low), values) / summed)
                kept = jnp.where(lane == 2 * pair + head, highest + jnp.log(summed), kept)
            totals[which, tile, :] = kept
            attended[which, tile, here] = jnp.where(lane < HEAD_DIM, parts[0], parts[1]).astype(low)

        @pl.when(pair == pairs_half - 1)
        def _():
            start_all(attended_stores(layer, which))

    def out_job(layer):
        wait_all(loads("out", 0))
        wait_all(first_stores(layer))
        for which in range(2):
            wait_all(proj_stores(layer, which))
            halo_store(layer, which).wait()
        bias = out_bias_ref[layer, pl.ds(0, 1), :]
        for tile in tiles:
            branch = dot_low(attended[0, tile, :], out_weight[...])
            branch = branch + dot_low(attended[1, tile, :], out_arrived[layer])
            resid[tile, :] = resid[tile, :] + branch + bias

    def second_job(layer):
        normalize(layer, 1, normed_two)
        start_all(second_stores(layer))

    def ffn_job(layer, which, inside, slot):
        index = which * blocks_hidden + inside
        if not which:
            wait_all(loads("ffn", inside))

        @pl.when(index >= 2)
        def _():
            wait_all(ffn_stores(layer, index - 2, slot))

        bias = (up_bias_in if which else up_bias_ref)[pl.ds(layer, 1), aligned(inside, block)]
        cut = aligned(inside, block)
        for tile in tiles:
            up_block = up_arrived[layer, :, cut] if which else up_weight[inside]
            before = dot_low(normed_two[tile, :], up_block) + bias
            square = before * before
            tangent = jnp.tanh(gelu_coeff * before * (1.0 + cubic_coeff * square))
            raised = 0.5 * (1.0 + tangent)
            activated = (before * raised).astype(low)
            act_buf[slot, tile, :] = activated
            slope_buf[slot, tile, :] = (
                raised
                + 0.5
                * before
                * (1.0 - tangent * tangent)
                * gelu_coeff
                * (1.0 + 3.0 * cubic_coeff * square)
            ).astype(low)
            down_block = down_arrived[layer, cut, :] if which else down_weight[inside]
            product = dot_low(activated, down_block)
            if which:
                collected[tile, :] = collected[tile, :] + product
                continue

            @pl.when(inside == 0)
            def _(tile=tile, product=product):
                collected[tile, :] = product

            @pl.when(inside > 0)
            def _(tile=tile, product=product):
                collected[tile, :] = collected[tile, :] + product

        start_all(ffn_stores(layer, index, slot))

    def end_job(layer, slot):
        wait_all(ffn_stores(layer, 2 * blocks_hidden - 2, slot))
        wait_all(ffn_stores(layer, 2 * blocks_hidden - 1, 1 - slot))
        wait_all(second_stores(layer))
        for which in range(2):
            wait_all(attended_stores(layer, which))
        bias = out_bias_ref[layer, pl.ds(1, 1), :]
        for tile in tiles:
            resid[tile, :] = resid[tile, :] + collected[tile, :] + bias

    def job(t):
        slot = t % 2
        layer, step = t // period, t % period

        def at(first, count, action):
            @pl.when((step >= first) & (step < first + count))
            def _():
                action(step - first)

        at(0, 1, lambda _: first_job(layer))
        later = (layer > 0).astype(jnp.int32)
        other_at = other_step + later * (2 - other_step)
        other_first = other_step + 1 + later * (2 + pairs_half - other_step)
        at(1, 1, lambda _: qkv_job(layer, 0))
        at(2 + later, pairs_half, lambda pair: attention_job(layer, 0, pair))
        at(other_at, 1, lambda _: qkv_job(layer, 1))
        at(other_first, pairs_half, lambda pair: attention_job(layer, 1, pair))
        at(out_step, 1, lambda _: out_job(layer))
        at(norm_two_step, 1, lambda _: second_job(layer))
        at(ffn_step, blocks_hidden, lambda inside: ffn_job(layer, 0, inside, slot))
        at(ffn_step + blocks_hidden, blocks_hidden, lambda inside: ffn_job(layer, 1, inside, slot))
        at(end_step, 1, lambda _: end_job(layer, slot))

    swap_start(0, tokens_ref, tokens_buf)
    halo[...] = jnp.zeros_like(halo)
    segments_copy.start()
    qv_copy.start()
    up_copy.start()
    for unit in range(Y_AHEAD):
        hop_start(0, unit)
    segments_copy.wait()
    window = jnp.where(core == y, segments_ref[...], segments_in[...])

    @pl.when(core == 0)
    def _():
        segk_out[:, 0:BAND] = jnp.full((1, BAND), -1, jnp.int32)
        segk_out[:, BAND:] = window[:, 0:rows_all]

    @pl.when(core == 1)
    def _():
        segk_out[...] = window[:, rows_all - BAND :]

    fill_band_bias(segk_out, bias_buf)
    qv_copy.wait()
    up_copy.wait()
    swap_wait(0, tokens_ref, tokens_buf)
    for tile in tiles:
        resid[tile, :] = tokens_buf[tile, :].astype(jnp.float32)
    cot_tick = period + other_step + 4

    def past(t, begin):
        return (t - begin) * (t > begin).astype(jnp.int32)

    def beat_at(t):
        return (10 * t - 4 * past(t, 12) - past(t, 22)) // 10

    for ahead in range(LOADS_AHEAD):
        prefetch(jnp.int32(ahead))

    def tick(t, carry):
        @pl.when((t == 0) | (beat_at(t) != beat_at(t - 1)))
        def _():
            beat(beat_at(t))

        @pl.when(t == cot_tick)
        def _():
            swap_start(1, cot_ref, cot_out)

        @pl.when((t == cot_tick + 4) & (swaps == 0))
        def _():
            pltpu.make_async_copy(cot_ref, tokens_buf, swap_sem.at[1]).wait()
            pltpu.make_async_copy(tokens_buf, cot_out, swap_sem.at[1]).start()

        @pl.when(t + LOADS_AHEAD < jobs)
        def _():
            prefetch(t + LOADS_AHEAD)

        job(t)
        return carry

    lax.fori_loop(0, jobs, tick, 0)
    for tile in tiles:
        normed_two[tile, :] = resid[tile, :].astype(low)
    last_store = store(0, normed_two, out_act_ref)
    last_store.start()
    last_store.wait()
    swap_wait(1, cot_ref, cot_out)
    for unit in range(units):
        block_ref = down_arrived.at[0, pl.ds(0, block), :]
        pltpu.make_async_copy(block_ref, block_ref, unit_store_sem.at[unit]).wait()


def run_forward(tokens, cotangent, segments, weights, biases, out_bias, gain, shift, block):
    rows, width = tokens.shape
    layers, hidden_half = weights[-1].shape[0], weights[-1].shape[1]
    low, wide = jnp.bfloat16, jnp.float32
    anywhere = pl.BlockSpec(memory_space=pl.ANY)
    in_vmem = pl.BlockSpec(memory_space=pltpu.VMEM)
    vmem = pltpu.VMEM
    units = layers * UNITS_LAYER
    shape = jax.ShapeDtypeStruct
    saved = [
        shape((layers, 2, rows, hidden_half), low),
        shape((layers, 2, rows, hidden_half), low),
        shape((layers, rows, width), low),
        shape((layers, rows, width), wide),
        shape((layers, 2, rows, block), low),
        shape((layers, 2, rows, 3 * block), low),
        shape((layers, 2, 2, BAND, block), low),
        shape((layers, 2, rows, LANES), wide),
        shape((layers, rows, width), low),
        shape((layers, rows, width), wide),
    ]
    others = [shape(member.shape, low) for member in weights]
    return pl.pallas_call(
        functools.partial(forward_kernel, layers, block, hidden_half),
        in_specs=[anywhere] * 2 + [in_vmem] + [anywhere] * 4 + [in_vmem] * 5,
        out_specs=[anywhere] * 2 + [in_vmem] + [anywhere] * (len(others) + len(saved)),
        out_shape=[
            shape((rows, width), low),
            shape((rows, width), low),
            shape((1, rows + BAND), jnp.int32),
        ]
        + others
        + saved,
        scratch_shapes=[
            vmem((rows, width), low),
            vmem(segments.shape, jnp.int32),
            vmem(biases[0].shape, wide),
            vmem(biases[1].shape, wide),
            vmem((rows, width), wide),
            vmem((rows, width), wide),
            vmem((rows, width), low),
            vmem((rows, width), low),
            vmem((2, 3, rows, block), low),
            vmem((layers, 2, 2, BAND, block), low),
            vmem((2, rows, block), low),
            vmem((2, rows, LANES), wide),
            vmem((2, rows, block), low),
            vmem((2, rows, block), low),
            vmem((3, width, block), low),
            vmem((block, width), low),
            vmem((hidden_half // block, width, block), low),
            vmem((hidden_half // block, block, width), low),
        ]
        + [vmem(member.shape, low) for member in weights]
        + [
            vmem((rows // BAND, BAND, 2 * BAND), wide),
            pltpu.SemaphoreType.DMA((5,)),
            pltpu.SemaphoreType.DMA((5,)),
            pltpu.SemaphoreType.DMA((2,)),
            pltpu.SemaphoreType.DMA((4, units)),
            pltpu.SemaphoreType.DMA((4, units)),
            pltpu.SemaphoreType.DMA((layers, 2)),
            pltpu.SemaphoreType.DMA((layers, 2)),
            pltpu.SemaphoreType.DMA((hidden_half // block + 2, 2)),
            pltpu.SemaphoreType.DMA((16,)),
            pltpu.SemaphoreType.DMA((2, 2)),
            pltpu.SemaphoreType.DMA((units,)),
        ],
        compiler_params=pltpu.CompilerParams(
            collective_id=1, has_side_effects=True, vmem_limit_bytes=VMEM_ASKED
        ),
        name="forward",
    )(tokens, cotangent, segments, *weights, *biases, out_bias, gain, shift)


SLOTS = 8
CORE_SLOTS = 4
RESULT_SLOTS = 11
STAGED = 2
FIRST = 0
LAGS = dict(
    core=1, first=3, second=5, third=7, fourth=9, fifth=11, sixth=13, whole=14, stored=15
)
VECTOR_STEP = 3
VECTOR_ROWS = 12
MESH = pl.DeviceIdType.MESH
FFN_STEPS = 4
QKV_STEPS = 3


def added(left, right):
    return (left.astype(jnp.float32) + right.astype(jnp.float32)).astype(jnp.bfloat16)


def backward_kernel(layers, block, hidden_half, *refs):
    (
        cot_ref,
        gain_ref,
        segk_ref,
        out_act_ref,
        act_ref,
        slope_ref,
        normed_two_ref,
        middle_ref,
        attended_ref,
        proj_ref,
        halo_ref,
        totals_ref,
        normed_ref,
        resid_ref,
        qkv_own,
        qkv_other,
        out_own,
        out_other,
        up_own,
        up_other,
        down_own,
        down_other,
        out_act_out,
        grad_in_ref,
        out_down,
        out_up,
        out_out,
        out_qkv,
        vector_out,
        grad_branch,
        grad_attn,
        grad_before,
        grad_proj,
        grad_res,
        collected,
        grad_attended,
        qkv_buf,
        halo_buf,
        totals_buf,
        kept_kv,
        halo_send,
        halo_in,
        rows_weight,
        columns_weight,
        slope_buf,
        wide_buf,
        bias_buf,
        sums_buf,
        pair_buf,
        one_buf,
        part_buf,
        core_in,
        sent,
        held,
        kept,
        first_in,
        second_in,
        third_in,
        result,
        vec_in,
        load_sem,
        io_sem,
        halo_send_sem,
        halo_recv_sem,
        staged_sem,
        send_sems,
        recv_sems,
        store_sem,
        vec_send,
        vec_recv,
        swap_send,
        swap_recv,
    ) = refs
    half, quarter = block // 2, block // 4
    width = 2 * block
    rows_all = grad_branch.shape[0]
    pairs_half = block // LANES
    pairs = 2 * pairs_half
    low = jnp.bfloat16
    place = lax.axis_index("dp")
    y = lax.axis_index("tensor")
    core = place % 2
    x = (place // 2) % 2
    z = place // 4
    z_low = z % 2
    inner = (z + 1) // 2 % 2
    core_partner = {"dp": place + 1 - 2 * core, "tensor": y}
    x_partner = {"dp": place + 2 - 4 * x, "tensor": y}
    y_partner = {"dp": place, "tensor": 1 - y}
    z_partner = {"dp": place + 4 - 8 * z_low, "tensor": y}
    middle_partner = {"dp": place + 4 * (3 - 2 * z), "tensor": y}
    swap_partner = {"dp": place + 1 - 2 * core, "tensor": 1 - y}

    barrier = pltpu.get_barrier_semaphore()
    for partner in (core_partner, x_partner, y_partner, z_partner, swap_partner):
        pl.semaphore_signal(barrier, inc=1, device_id=partner, device_id_type=MESH)

    @pl.when(inner == 1)
    def _():
        pl.semaphore_signal(barrier, inc=1, device_id=middle_partner, device_id_type=MESH)
        pl.semaphore_wait(barrier, 6)

    @pl.when(inner == 0)
    def _():
        pl.semaphore_wait(barrier, 5)

    blocks_hidden = hidden_half // block
    plan = (
        ("rows", blocks_hidden, 2),
        ("columns", 2, blocks_hidden),
        ("rows", 1, 2),
        ("columns", 2, 3),
    )
    starts = []
    per_layer = 0
    for _, down_count, across_count in plan:
        starts.append(per_layer)
        per_layer += down_count * across_count
    chunks = layers * per_layer
    out_refs = (out_down, out_up, out_out, out_qkv)

    def block_of(index):
        return pl.ds(pl.multiple_of(index * block, block), block)

    def for_matrix(chunk, action):
        layer = layers - 1 - chunk // per_layer
        inside = chunk % per_layer
        for member, (_, down_count, across_count) in enumerate(plan):
            begin = starts[member]

            @pl.when((inside >= begin) & (inside < begin + down_count * across_count))
            def _(member=member, begin=begin, across_count=across_count):
                local = inside - begin
                action(member, layer, local // across_count, local % across_count)

    def operands_of(member, layer, i, j):
        if member == 0:
            return (
                grad_branch.at[:, block_of(j)],
                act_ref.at[layer, 0, :, block_of(i)],
                act_ref.at[layer, 1, :, block_of(i)],
            )
        if member == 1:
            return (
                normed_two_ref.at[layer, :, block_of(i)],
                grad_before.at[j // 2, :, block_of(j % 2)],
                grad_before.at[blocks_hidden // 2 + j // 2, :, block_of(j % 2)],
            )
        if member == 2:
            return (
                grad_attn.at[:, block_of(j)],
                attended_ref.at[layer, 0, :, block_of(i)],
                attended_ref.at[layer, 1, :, block_of(i)],
            )
        return (
            normed_ref.at[layer, :, block_of(i)],
            grad_proj.at[:, block_of(j)],
            grad_proj.at[:, block_of(3 + j)],
        )

    def staged_copies(chunk, shared, own, other):
        slot = chunk % STAGED
        return (
            pltpu.make_async_copy(own, pair_buf.at[slot, 0], staged_sem.at[slot, 0]),
            pltpu.make_async_copy(other, pair_buf.at[slot, 1], staged_sem.at[slot, 1]),
            pltpu.make_async_copy(shared, one_buf.at[slot], staged_sem.at[slot, 2]),
        )

    def stage_operands(chunk):
        def action(member, layer, i, j):
            for copy in staged_copies(chunk, *operands_of(member, layer, i, j)):
                copy.start()

        for_matrix(chunk, action)

    def remote(step, chunk, source, target, partner):
        slot = chunk % SLOTS
        return pltpu.make_async_remote_copy(
            src_ref=source,
            dst_ref=target,
            send_sem=send_sems.at[step, slot],
            recv_sem=recv_sems.at[step, slot],
            device_id=partner,
            device_id_type=MESH,
        )

    def x_first(chunk):
        return ((5 * chunk) % 8 < 3) | (chunk >= chunks - 1)

    def core_copy(chunk):
        return remote(
            0,
            chunk,
            part_buf.at[chunk % STAGED, :, aligned(1 - core, half)],
            core_in.at[chunk % CORE_SLOTS],
            core_partner,
        )

    low_middle = z - 1
    far_middle = 2 - z

    def first_copy(chunk, partner):
        slot = chunk % SLOTS
        return remote(1, chunk, sent.at[slot], first_in.at[slot], partner)

    def y_copy(chunk):
        slot = chunk % SLOTS
        return remote(2, chunk, kept.at[slot, 1], second_in.at[slot, 0], y_partner)

    def pair_copy(chunk):
        slot = chunk % SLOTS
        return remote(2, chunk, kept.at[slot], second_in.at[slot], z_partner)

    def single_copy(chunk):
        slot = chunk % SLOTS
        return remote(3, chunk, kept.at[slot, 0], third_in.at[slot, 0], z_partner)

    def split_copy(chunk):
        slot = chunk % SLOTS
        return remote(3, chunk, kept.at[slot, far_middle], third_in.at[slot, 0], middle_partner)

    def middle_copy(chunk):
        slot = chunk % SLOTS
        return remote(4, chunk, kept.at[slot, 0], third_in.at[slot, 1], middle_partner)

    def across_copy(chunk):
        slot = chunk % SLOTS
        return remote(4, chunk, kept.at[slot, low_middle], third_in.at[slot, 1], x_partner)

    def result_copy(step, chunk, rows, partner):
        piece = result.at[chunk % RESULT_SLOTS, rows]
        return remote(step, chunk, piece, piece, partner)

    x_rows = aligned(2 * core + x, quarter)
    core_rows = aligned(core, half)

    def middle_rows():
        return aligned(2 * core + low_middle, quarter)

    def store_copy(chunk, target):
        slot = chunk % RESULT_SLOTS
        return pltpu.make_async_copy(result.at[slot], target, store_sem.at[slot])

    def multiply(chunk):
        slot = chunk % STAGED
        for copy in staged_copies(chunk, one_buf.at[slot], pair_buf.at[slot, 0], pair_buf.at[slot, 1]):
            copy.wait()
        inside = chunk % per_layer
        by_rows = (inside < starts[1]) | ((inside >= starts[2]) & (inside < starts[3]))

        @pl.when(by_rows)
        def _():
            single = one_buf[slot]
            for which in range(2):
                part_buf[slot, which] = dot_tn(pair_buf[slot, which], single).astype(low)

        @pl.when(jnp.logical_not(by_rows))
        def _():
            single = one_buf[slot]
            for which in range(2):
                part_buf[slot, which] = dot_tn(single, pair_buf[slot, which]).astype(low)

        core_copy(chunk).start()

    def branch(chunk, by_x, by_y):
        is_x = x_first(chunk)

        @pl.when(is_x)
        def _():
            by_x()

        @pl.when(jnp.logical_not(is_x))
        def _():
            by_y()

    def on_middle(action):
        @pl.when(inner == 1)
        def _():
            action()

    def by_place(at_end, at_middle):
        @pl.when(inner == 0)
        def _():
            at_end()

        on_middle(at_middle)

    def after_core(chunk):
        slot, core_slot, part_slot = chunk % SLOTS, chunk % CORE_SLOTS, chunk % STAGED
        core_copy(chunk).wait()
        is_x = x_first(chunk).astype(jnp.int32)

        def summed(which, row):
            near = part_buf[part_slot, which, aligned(2 * core + row, quarter), :]
            return added(near, core_in[core_slot, which, aligned(row, quarter), :])

        for index in range(2):
            sent[slot, index] = summed(
                is_x * index + (1 - is_x), is_x * (1 - x) + (1 - is_x) * index
            )
        branch(
            chunk,
            lambda: first_copy(chunk, x_partner).start(),
            lambda: first_copy(chunk, y_partner).start(),
        )
        for index in range(2):
            held[slot, index] = summed(is_x * index, is_x * x + (1 - is_x) * index)

    def after_first(chunk):
        slot = chunk % SLOTS
        first_copy(chunk, y_partner).wait()
        for index in (1, 0):
            kept[slot, index] = added(held[slot, index], first_in[slot, index])

        def by_y():
            @pl.when(inner == 0)
            def _():
                pair_copy(chunk).start()

        branch(chunk, lambda: y_copy(chunk).start(), by_y)

    def after_second(chunk):
        slot = chunk % SLOTS

        def by_x():
            y_copy(chunk).wait()
            kept[slot, 0] = added(kept[slot, 0], second_in[slot, 0])

            @pl.when(inner == 0)
            def _():
                single_copy(chunk).start()

        def at_middle():
            pair_copy(chunk).wait_recv()
            kept[slot, far_middle] = added(kept[slot, far_middle], second_in[slot, far_middle])
            split_copy(chunk).start()
            kept[slot, low_middle] = added(kept[slot, low_middle], second_in[slot, low_middle])

        branch(chunk, by_x, lambda: by_place(lambda: pair_copy(chunk).wait_send(), at_middle))

    def after_third(chunk):
        slot = chunk % SLOTS

        def one_at_middle():
            single_copy(chunk).wait_recv()
            kept[slot, 0] = added(kept[slot, 0], third_in[slot, 0])
            middle_copy(chunk).start()

        def by_y():
            split_copy(chunk).wait()
            kept[slot, low_middle] = added(kept[slot, low_middle], third_in[slot, 0])
            across_copy(chunk).start()

        branch(
            chunk,
            lambda: by_place(lambda: single_copy(chunk).wait_send(), one_at_middle),
            lambda: on_middle(by_y),
        )

    def after_fourth(chunk):
        slot, result_slot = chunk % SLOTS, chunk % RESULT_SLOTS

        def by_x():
            middle_copy(chunk).wait()
            result[result_slot, x_rows, :] = added(kept[slot, 0], third_in[slot, 1])
            result_copy(5, chunk, x_rows, z_partner).start()

        def by_y():
            across_copy(chunk).wait()
            result[result_slot, middle_rows(), :] = added(
                kept[slot, low_middle], third_in[slot, 1]
            )
            result_copy(5, chunk, middle_rows(), middle_partner).start()

        branch(chunk, lambda: on_middle(by_x), lambda: on_middle(by_y))

    def after_fifth(chunk):
        def by_x():
            back = result_copy(5, chunk, x_rows, z_partner)
            by_place(back.wait_recv, back.wait_send)
            result_copy(6, chunk, x_rows, x_partner).start()

        def by_y():
            result_copy(5, chunk, middle_rows(), middle_partner).wait()
            result_copy(6, chunk, core_rows, z_partner).start()

        branch(chunk, by_x, lambda: on_middle(by_y))

    def after_sixth(chunk):
        def by_y():
            back = result_copy(6, chunk, core_rows, z_partner)
            by_place(back.wait_recv, back.wait_send)

        branch(chunk, lambda: result_copy(6, chunk, x_rows, x_partner).wait(), by_y)
        result_copy(7, chunk, core_rows, core_partner).start()

    def after_whole(chunk):
        result_copy(7, chunk, core_rows, core_partner).wait()

        def action(member, layer, i, j):
            if member == 3:
                target = out_qkv.at[layer, j, block_of(i)]
            else:
                target = out_refs[member].at[layer, block_of(i), block_of(j)]
            store_copy(chunk, target).start()

        for_matrix(chunk, action)

    def after_store(chunk):
        store_copy(chunk, result.at[chunk % RESULT_SLOTS]).wait()

    vector_partners = (core_partner, y_partner, x_partner, z_partner, middle_partner, z_partner)

    def vector_copy(step):
        target = vec_in.at[min(step, 4)]
        return pltpu.make_async_remote_copy(
            src_ref=vector_out,
            dst_ref=target,
            send_sem=vec_send.at[step],
            recv_sem=vec_recv.at[step],
            device_id=vector_partners[step],
            device_id_type=MESH,
        )

    def add_vector(step):
        vector_out[...] = vector_out[...] + vec_in[step]

    def vector_tick(step):
        if step == 0:
            vector_copy(0).start()
        elif step <= 3:
            vector_copy(step - 1).wait()
            add_vector(step - 1)
            if step < 3:
                vector_copy(step).start()
            else:

                @pl.when(inner == 0)
                def _():
                    vector_copy(3).start()

        elif step == 4:

            @pl.when(inner == 0)
            def _():
                vector_copy(3).wait_send()

            @pl.when(inner == 1)
            def _():
                vector_copy(3).wait_recv()
                add_vector(3)
                vector_copy(4).start()

        elif step == 5:

            @pl.when(inner == 1)
            def _():
                vector_copy(4).wait()
                add_vector(4)
                vector_copy(5).start()

        else:

            @pl.when(inner == 1)
            def _():
                vector_copy(5).wait_send()

            @pl.when(inner == 0)
            def _():
                vector_copy(5).wait_recv()
                vector_out[...] = vec_in[4]

    norm_two_step = FFN_STEPS
    out_step = norm_two_step + 1
    attention_step = out_step + 1
    qkv_step = attention_step + pairs + 1
    norm_one_step = qkv_step + QKV_STEPS
    period = norm_one_step + 1
    jobs = layers * period
    hidden_step = 2 * hidden_half // FFN_STEPS

    def loads(kind, slot, *sources):
        targets = {
            "ffn": (rows_weight.at[slot], columns_weight.at[slot], slope_buf.at[slot]),
            "wide": (wide_buf,),
            "out": (rows_weight.at[slot, pl.ds(0, block)], rows_weight.at[slot, pl.ds(block, block)]),
            "attention": (
                qkv_buf.at[slot, 0],
                qkv_buf.at[slot, 1],
                qkv_buf.at[slot, 2],
                halo_buf.at[slot, 0],
                halo_buf.at[slot, 1],
                totals_buf.at[slot],
            ),
            "qkv": (
                columns_weight.at[slot, :, pl.ds(0, block)],
                columns_weight.at[slot, :, pl.ds(block, block)],
            ),
        }[kind]
        sources = sources or targets
        return [
            pltpu.make_async_copy(source, target, load_sem.at[slot, index])
            for index, (source, target) in enumerate(zip(sources, targets))
        ]

    def prefetch(t):
        slot = t % 2
        layer = layers - 1 - t // period
        step = t % period

        for which, (up_ref, down_ref) in enumerate(((up_own, down_own), (up_other, down_other))):

            @pl.when((step < FFN_STEPS) & (step // (FFN_STEPS // 2) == which))
            def _(which=which, up_ref=up_ref, down_ref=down_ref):
                cut = aligned(step % (FFN_STEPS // 2), hidden_step)
                for copy in loads(
                    "ffn",
                    slot,
                    down_ref.at[layer, cut, :],
                    up_ref.at[layer, :, cut],
                    slope_ref.at[layer, which, :, cut],
                ):
                    copy.start()

        for at, source in ((norm_two_step, middle_ref), (norm_one_step, resid_ref)):

            @pl.when(step == at)
            def _(source=source):
                for copy in loads("wide", slot, source.at[layer]):
                    copy.start()

        @pl.when(step == out_step)
        def _():
            for copy in loads("out", slot, out_own.at[layer], out_other.at[layer]):
                copy.start()

        @pl.when((step >= attention_step) & (step < attention_step + pairs))
        def _():
            pair = step - attention_step
            which, inside = pair // pairs_half, pair % pairs_half

            def lanes(third):
                return aligned(third * pairs_half + inside, LANES)

            for copy in loads(
                "attention",
                slot,
                *[proj_ref.at[layer, which, :, lanes(third)] for third in range(3)],
                *[halo_ref.at[layer, which, third, :, lanes(0)] for third in range(2)],
                totals_ref.at[layer, which],
            ):
                copy.start()

        @pl.when((step >= qkv_step) & (step < qkv_step + QKV_STEPS))
        def _():
            for part in range(2):
                index = 2 * (step - qkv_step) + part
                for which, source in enumerate((qkv_own, qkv_other)):

                    @pl.when(index // 3 == which)
                    def _(part=part, index=index, source=source):
                        pltpu.make_async_copy(
                            source.at[layer, index % 3],
                            columns_weight.at[slot, :, pl.ds(part * block, block)],
                            load_sem.at[slot, part],
                        ).start()

    def wait_loads(kind, slot):
        for copy in loads(kind, slot):
            copy.wait()

    tiles = [slice(r, r + BAND) for r in range(0, rows_all, BAND)]
    fine_tiles = [slice(r, r + LANES) for r in range(0, rows_all, LANES)]

    def vector_row(layer, row):
        return pl.ds(layer * VECTOR_ROWS + row, 1)

    def column_sum(values):
        return jnp.sum(values.astype(jnp.float32), axis=0, keepdims=True)

    def ffn_job(layer, step, slot):
        wait_loads("ffn", slot)
        sums = 0.0
        for tile in tiles:
            grad_hidden = dot_nt(grad_branch[tile, :], rows_weight[slot])
            before = (grad_hidden * slope_buf[slot, tile, :].astype(jnp.float32)).astype(low)
            grad_before[step, tile, :] = before
            sums = sums + column_sum(before)
            product = dot_nt(before, columns_weight[slot])

            @pl.when(step == 0)
            def _(tile=tile, product=product):
                collected[tile, :] = product

            @pl.when(step > 0)
            def _(tile=tile, product=product):
                collected[tile, :] = collected[tile, :] + product

        per_half = FFN_STEPS // 2
        which = step // per_half
        owner = which + y - 2 * which * y
        vector_out[vector_row(layer, 2 + owner * per_half + step % per_half), :] = sums

    def norm_job(layer, index, slot):
        wait_loads("wide", slot)
        gain = gain_ref[layer, pl.ds(index, 1), :]
        gain_sum, shift_sum, attn_sum, branch_sum = 0.0, 0.0, 0.0, 0.0
        for tile in fine_tiles:
            incoming = collected[tile, :]
            values = wide_buf[tile, :]
            average = jnp.mean(values, axis=-1, keepdims=True)
            centred = values - average
            inverse = lax.rsqrt(jnp.mean(centred * centred, axis=-1, keepdims=True) + epsilon)
            unit = centred * inverse
            scaled = incoming * gain
            first_mean = jnp.mean(scaled, axis=-1, keepdims=True)
            second_mean = jnp.mean(scaled * unit, axis=-1, keepdims=True)
            total = grad_res[tile, :] + inverse * (scaled - first_mean - unit * second_mean)
            grad_res[tile, :] = total
            rounded = total.astype(low)
            gain_sum = gain_sum + column_sum(incoming * unit)
            shift_sum = shift_sum + column_sum(incoming)
            if index == 1:
                attn_sum = attn_sum + column_sum(rounded)
                branch_sum = branch_sum + column_sum(grad_branch[tile, :])
                grad_attn[tile, :] = rounded
            else:
                grad_branch[tile, :] = rounded
        vector_out[vector_row(layer, 8 + index), :] = gain_sum
        vector_out[vector_row(layer, 10 + index), :] = shift_sum
        if index == 1:
            vector_out[vector_row(layer, 6), :] = attn_sum
            vector_out[vector_row(layer, 7), :] = branch_sum

    def out_job(slot):
        wait_loads("out", slot)
        for tile in tiles:
            grad_attended[tile, :] = dot_nt(grad_attn[tile, :], rows_weight[slot]).astype(low)

    def halo_copy(pair):
        return pltpu.make_async_remote_copy(
            src_ref=halo_send.at[pair % 2],
            dst_ref=halo_in.at[pair],
            send_sem=halo_send_sem.at[pair],
            recv_sem=halo_recv_sem.at[pair],
            device_id=core_partner,
            device_id_type=MESH,
        )

    def proj_lanes(pair, third):
        which, inside = pair // pairs_half, pair % pairs_half
        return aligned(which * 3 * pairs_half + third * pairs_half + inside, LANES)

    def attention_job(pair, slot):
        wait_loads("attention", slot)
        lane = lax.broadcasted_iota(jnp.int32, (BAND, LANES), 1)
        scaling = HEAD_DIM ** (-0.5)
        count = len(tiles)
        key_parts = [None] * (count + 1)
        value_parts = [None] * (count + 1)
        here = aligned(pair, LANES)
        for index, tile in enumerate(tiles):
            query = qkv_buf[slot, 0, tile, :]
            grad = grad_attended[tile, here]
            keys = band_rows(halo_buf[slot, 0], qkv_buf[slot, 1], index)
            values = band_rows(halo_buf[slot, 1], qkv_buf[slot, 2], index)
            grad_query = []
            grad_keys = 0.0
            grad_values = 0.0
            for head in range(2):
                mine = (lane // HEAD_DIM) == head
                query_head = jnp.where(mine, query, 0)
                grad_head = jnp.where(mine, grad, 0)
                scores = dot_nt(query_head, keys) * scaling + bias_buf[index]
                total = jnp.sum(
                    jnp.where(
                        lane == 2 * (pair % pairs_half) + head, totals_buf[slot, tile, :], 0.0
                    ),
                    axis=-1,
                    keepdims=True,
                )
                exact = jnp.exp(scores - total)
                grad_probs = dot_nt(grad_head, values)
                row_terms = jnp.sum(exact * grad_probs, axis=-1, keepdims=True)
                grad_scores = (exact * (grad_probs - row_terms)).astype(low)
                grad_query.append(jnp.dot(grad_scores, keys, preferred_element_type=jnp.float32))
                grad_keys = grad_keys + dot_tn(grad_scores, query_head)
                grad_values = grad_values + dot_tn(exact.astype(low), grad_head)
            grad_proj[tile, proj_lanes(pair, 0)] = (
                jnp.where(lane < HEAD_DIM, grad_query[0], grad_query[1]) * scaling
            ).astype(low)
            grad_keys = grad_keys * scaling
            for part in range(2):
                cut = slice(part * BAND, (part + 1) * BAND)
                old_k, old_v = key_parts[index + part], value_parts[index + part]
                key_parts[index + part] = grad_keys[cut] if old_k is None else old_k + grad_keys[cut]
                value_parts[index + part] = (
                    grad_values[cut] if old_v is None else old_v + grad_values[cut]
                )
        for index in range(count - 1):
            grad_proj[tiles[index], proj_lanes(pair, 1)] = key_parts[index + 1].astype(low)
            grad_proj[tiles[index], proj_lanes(pair, 2)] = value_parts[index + 1].astype(low)
        kept_kv[pair % 2, 0] = key_parts[count]
        kept_kv[pair % 2, 1] = value_parts[count]

        @pl.when(core == 1)
        def _():
            halo_send[pair % 2, 0] = key_parts[0].astype(low)
            halo_send[pair % 2, 1] = value_parts[0].astype(low)
            halo_copy(pair).start()

    def finish_pair(pair):
        last = tiles[-1]

        @pl.when(core == 0)
        def _():
            halo_copy(pair).wait_recv()
            for third in range(2):
                grad_proj[last, proj_lanes(pair, third + 1)] = (
                    kept_kv[pair % 2, third] + halo_in[pair, third].astype(jnp.float32)
                ).astype(low)

        @pl.when(core == 1)
        def _():
            halo_copy(pair).wait_send()
            for third in range(2):
                grad_proj[last, proj_lanes(pair, third + 1)] = kept_kv[pair % 2, third].astype(low)

    def qkv_job(layer, step, slot):
        wait_loads("qkv", slot)
        sums = 0.0
        for tile in tiles:
            grad = grad_proj[tile, aligned(step, width)]
            sums = sums + column_sum(grad)
            product = dot_nt(grad, columns_weight[slot])

            @pl.when(step == 0)
            def _(tile=tile, product=product):
                collected[tile, :] = product

            @pl.when(step > 0)
            def _(tile=tile, product=product):
                collected[tile, :] = collected[tile, :] + product

        sums_buf[...] = sums
        for when, part, which, row in ((0, 0, 0, 0), (1, 0, 0, 1), (1, 1, 1, 0), (2, 1, 1, 1)):

            @pl.when(step == when)
            def _(part=part, which=which, row=row):
                owner = 1 - y if which else y
                vector_out[vector_row(layer, row), block_of(owner)] = sums_buf[
                    :, part * block : (part + 1) * block
                ]

    def job(t):
        slot = t % 2
        layer = layers - 1 - t // period
        step = t % period

        @pl.when(step < FFN_STEPS)
        def _():
            ffn_job(layer, step, slot)

        @pl.when(step == norm_two_step)
        def _():
            norm_job(layer, 1, slot)

        @pl.when(step == out_step)
        def _():
            out_job(slot)

        @pl.when((step > attention_step) & (step <= attention_step + pairs))
        def _():
            finish_pair(step - attention_step - 1)

        @pl.when((step >= attention_step) & (step < attention_step + pairs))
        def _():
            attention_job(step - attention_step, slot)

        @pl.when((step >= qkv_step) & (step < qkv_step + QKV_STEPS))
        def _():
            qkv_job(layer, step - qkv_step, slot)

        @pl.when(step == norm_one_step)
        def _():
            norm_job(layer, 0, slot)

    stages = (
        (LAGS["core"], after_core),
        (0, multiply),
        (None, job),
        (LAGS["first"], after_first),
        (LAGS["second"], after_second),
        (LAGS["third"], after_third),
        (LAGS["fourth"], after_fourth),
        (LAGS["fifth"], after_fifth),
        (LAGS["sixth"], after_sixth),
        (LAGS["stored"], after_store),
        (LAGS["whole"], after_whole),
    )

    swaps = core + y - 2 * core * y

    def swap_copy(index, source, target):
        return pltpu.make_async_remote_copy(
            src_ref=source,
            dst_ref=target,
            send_sem=swap_send.at[index],
            recv_sem=swap_recv.at[index],
            device_id=swap_partner,
            device_id_type=MESH,
        )

    def swap_start(index, source, target):
        @pl.when(swaps == 1)
        def _():
            swap_copy(index, source, target).start()

        if index:

            @pl.when(swaps == 0)
            def _():
                pltpu.make_async_copy(source, target, io_sem.at[1]).start()

    def swap_wait(index, source, target):
        @pl.when(swaps == 1)
        def _():
            swap_copy(index, source, target).wait()

        if index:

            @pl.when(swaps == 0)
            def _():
                pltpu.make_async_copy(source, target, io_sem.at[1]).wait()

    first_load = pltpu.make_async_copy(cot_ref, grad_branch, io_sem.at[0])
    first_load.start()
    prefetch(0)
    fill_band_bias(segk_ref, bias_buf)
    first_load.wait()
    for tile in tiles:
        grad_res[tile, :] = grad_branch[tile, :].astype(jnp.float32)
    stage_operands(0)
    swap_start(0, out_act_ref, out_act_out)
    vector_ticks = [jobs + VECTOR_STEP * step for step in range(7)]

    def tick(t, carry):
        @pl.when(t + 1 < jobs)
        def _():
            prefetch(t + 1)

        ahead = t + 1 - FIRST

        @pl.when((ahead > 0) & (ahead < chunks))
        def _():
            stage_operands(ahead)

        for lag, action in stages:
            if lag is None:

                @pl.when(t < jobs)
                def _():
                    job(t)

                continue
            chunk = t - FIRST - lag

            @pl.when((chunk >= 0) & (chunk < chunks))
            def _(chunk=chunk, action=action):
                action(chunk)

        @pl.when(t == chunks + FIRST + LAGS["second"] - 1)
        def _():
            swap_start(1, grad_branch, grad_in_ref)

        for step, when in enumerate(vector_ticks):

            @pl.when(t == when)
            def _(step=step):
                vector_tick(step)

        return carry

    lax.fori_loop(0, max(chunks + FIRST + LAGS["stored"], vector_ticks[-1] + 1), tick, 0)
    swap_wait(0, out_act_ref, out_act_out)
    swap_wait(1, grad_branch, grad_in_ref)


def run_backward(cotangent, gain, segk, out_act, saved, weights, block):
    rows, width = cotangent.shape
    layers, hidden_half = weights[-1].shape[0], weights[-1].shape[1]
    half, quarter = block // 2, block // 4
    low, wide = jnp.bfloat16, jnp.float32
    pairs = width // LANES
    anywhere = pl.BlockSpec(memory_space=pl.ANY)
    in_vmem = pl.BlockSpec(memory_space=pltpu.VMEM)
    vector = (layers * VECTOR_ROWS, width)
    hidden_step = 2 * hidden_half // FFN_STEPS
    vmem = pltpu.VMEM
    return pl.pallas_call(
        functools.partial(backward_kernel, layers, block, hidden_half),
        in_specs=[anywhere] + [in_vmem] * 2 + [anywhere] * (1 + len(saved) + len(weights)),
        out_specs=[anywhere] * 6 + [in_vmem],
        out_shape=[
            jax.ShapeDtypeStruct((rows, width), low),
            jax.ShapeDtypeStruct((rows, width), low),
            jax.ShapeDtypeStruct((layers, hidden_half, width), low),
            jax.ShapeDtypeStruct((layers, width, hidden_half), low),
            jax.ShapeDtypeStruct((layers, block, width), low),
            jax.ShapeDtypeStruct((layers, 3, width, block), low),
            jax.ShapeDtypeStruct(vector, wide),
        ],
        scratch_shapes=[
            vmem((rows, width), low),
            vmem((rows, width), low),
            vmem((FFN_STEPS, rows, hidden_step), low),
            vmem((rows, 6 * block), low),
            vmem((rows, width), wide),
            vmem((rows, width), wide),
            vmem((rows, width), low),
            vmem((2, 3, rows, LANES), low),
            vmem((2, 2, BAND, LANES), low),
            vmem((2, rows, LANES), wide),
            vmem((2, 2, BAND, LANES), wide),
            vmem((2, 2, BAND, LANES), low),
            vmem((pairs, 2, BAND, LANES), low),
            vmem((2, hidden_step, width), low),
            vmem((2, width, hidden_step), low),
            vmem((2, rows, hidden_step), low),
            vmem((rows, width), wide),
            vmem((rows // BAND, BAND, 2 * BAND), wide),
            vmem((1, width), wide),
            vmem((STAGED, 2, rows, block), low),
            vmem((STAGED, rows, block), low),
            vmem((STAGED, 2, block, block), low),
            vmem((CORE_SLOTS, 2, half, block), low),
            vmem((SLOTS, 2, quarter, block), low),
            vmem((SLOTS, 2, quarter, block), low),
            vmem((SLOTS, 2, quarter, block), low),
            vmem((SLOTS, 2, quarter, block), low),
            vmem((SLOTS, 2, quarter, block), low),
            vmem((SLOTS, 2, quarter, block), low),
            vmem((RESULT_SLOTS, block, block), low),
            vmem((5,) + vector, wide),
            pltpu.SemaphoreType.DMA((2, 6)),
            pltpu.SemaphoreType.DMA((2,)),
            pltpu.SemaphoreType.DMA((pairs,)),
            pltpu.SemaphoreType.DMA((pairs,)),
            pltpu.SemaphoreType.DMA((STAGED, 3)),
            pltpu.SemaphoreType.DMA((8, SLOTS)),
            pltpu.SemaphoreType.DMA((8, SLOTS)),
            pltpu.SemaphoreType.DMA((RESULT_SLOTS,)),
            pltpu.SemaphoreType.DMA((6,)),
            pltpu.SemaphoreType.DMA((6,)),
            pltpu.SemaphoreType.DMA((2,)),
            pltpu.SemaphoreType.DMA((2,)),
        ],
        compiler_params=pltpu.CompilerParams(
            collective_id=0, has_side_effects=True, vmem_limit_bytes=VMEM_ASKED
        ),
        name="backward",
    )(cotangent, gain, segk, out_act, *saved, *weights)


FINISH_DEPTH = 4


def finish_kernel(layers, steps, *refs):
    count = len(steps)
    ins, refs = refs[:count], refs[count:]
    vector_ref, refs = refs[0], refs[1:]
    (act_own, act_swapped, grad_in_ref), refs = refs[:3], refs[3:]
    outs, refs = refs[:count], refs[count:]
    qv_out, up_out, bias_out, gain_out, shift_out = refs[:5]
    (act_out, grad_in_out), refs = refs[5:7], refs[7:]
    in_bufs, refs = refs[:count], refs[count:]
    out_bufs, (moved_buf, in_sem, out_sem, copy_sem) = refs[:count], refs[count:]
    y = lax.axis_index("tensor")
    core = lax.axis_index("dp") % 2

    def fetch(index, source):
        return pltpu.make_async_copy(source, moved_buf.at[index], copy_sem.at[index])

    def put(index, target):
        return pltpu.make_async_copy(moved_buf.at[index], target, copy_sem.at[index])

    @pl.when(core == y)
    def _():
        fetch(0, act_own).start()

    @pl.when(core != y)
    def _():
        fetch(0, act_swapped).start()

    fetch(1, grad_in_ref).start()
    plan = []
    for member, (rows, parts) in enumerate(steps):
        for layer in range(layers):
            for part in range(parts):
                plan.append((member, layer, part * rows, rows, (layer * parts + part) % FINISH_DEPTH))

    def view(ref, layer, begin, rows):
        if len(ref.shape) == 4:
            return ref.at[layer, begin // rows]
        return ref.at[layer, pl.ds(begin, rows)]

    def load(entry):
        member, layer, begin, rows, slot = entry
        return pltpu.make_async_copy(
            view(ins[member], layer, begin, rows), in_bufs[member].at[slot], in_sem.at[member, slot]
        )

    def save(entry):
        member, layer, begin, rows, slot = entry
        return pltpu.make_async_copy(
            out_bufs[member].at[slot], view(outs[member], layer, begin, rows), out_sem.at[member, slot]
        )

    for entry in plan[:FINISH_DEPTH]:
        load(entry).start()
    half = qv_out.shape[2]
    for layer in range(layers):
        base = layer * VECTOR_ROWS
        for index in range(2):
            mine = pl.ds(pl.multiple_of(y * half, half), half)
            qv_out[layer, pl.ds(index, 1), :] = vector_ref[pl.ds(base + index, 1), mine]
            width = vector_ref.shape[1]
            up_out[pl.ds(layer, 1), index * width : (index + 1) * width] = vector_ref[
                pl.ds(base + 2 + 2 * y + index, 1), :
            ]
            for row, target in ((6, bias_out), (8, gain_out), (10, shift_out)):
                target[layer, pl.ds(index, 1), :] = vector_ref[pl.ds(base + row + index, 1), :]
    for index, target in enumerate((act_out, grad_in_out)):
        fetch(index, target).wait()
        put(index, target).start()
    busy = {}
    for place, entry in enumerate(plan):
        member, slot = entry[0], entry[4]
        load(entry).wait()
        if (member, slot) in busy:
            save(busy.pop((member, slot))).wait()
        out_bufs[member][slot] = in_bufs[member][slot].astype(jnp.float32)
        save(entry).start()
        busy[(member, slot)] = entry
        if place + FINISH_DEPTH < len(plan):
            load(plan[place + FINISH_DEPTH]).start()
    for entry in busy.values():
        save(entry).wait()
    for index, target in enumerate((act_out, grad_in_out)):
        put(index, target).wait()


def run_finish(reduced, vector, acts, grad_in, block):
    layers, width = reduced[0].shape[0], vector.shape[1]
    hidden_half = reduced[0].shape[1]
    wide, low = jnp.float32, jnp.bfloat16
    shape = jax.ShapeDtypeStruct
    anywhere = pl.BlockSpec(memory_space=pl.ANY)
    in_vmem = pl.BlockSpec(memory_space=pltpu.VMEM)
    steps = (
        (block, hidden_half // block),
        (block // 2, width * 2 // block),
        (block, 1),
        (width, 3),
    )
    blocks = ((block, width), (block // 2, hidden_half), (block, width), (width, block))
    deep = lambda kind: [pltpu.VMEM((FINISH_DEPTH,) + size, kind) for size in blocks]
    return pl.pallas_call(
        functools.partial(finish_kernel, layers, steps),
        in_specs=[anywhere] * len(reduced) + [in_vmem] + [anywhere] * 3,
        out_specs=[anywhere] * len(reduced) + [in_vmem] * 5 + [anywhere] * 2,
        out_shape=[shape(member.shape, wide) for member in reduced]
        + [
            shape((layers, 2, block), wide),
            shape((layers, hidden_half), wide),
            shape((layers, 2, width), wide),
            shape((layers, 2, width), wide),
            shape((layers, 2, width), wide),
        ]
        + [shape(grad_in.shape, low)] * 2,
        scratch_shapes=deep(low)
        + deep(wide)
        + [
            pltpu.VMEM((2,) + grad_in.shape, low),
            pltpu.SemaphoreType.DMA((4, FINISH_DEPTH)),
            pltpu.SemaphoreType.DMA((4, FINISH_DEPTH)),
            pltpu.SemaphoreType.DMA((2,)),
        ],
        compiler_params=pltpu.CompilerParams(vmem_limit_bytes=VMEM_ASKED),
        name="finish",
    )(*reduced, vector, *acts, grad_in)


def local_split(
    tokens_in,
    segments,
    w_qkv,
    qv_bias,
    w_out,
    w_up,
    up_bias,
    w_down,
    out_bias,
    ln_gain,
    ln_bias,
    cotangent,
):
    block = w_qkv.shape[3]
    weights = (w_qkv.transpose(0, 2, 1, 3), w_out, w_up, w_down)
    act_own, cot, segk, *rest = run_forward(
        tokens_in,
        cotangent,
        segments,
        weights,
        (qv_bias, up_bias),
        out_bias,
        ln_gain,
        ln_bias,
        block,
    )
    others, saved = rest[: len(weights)], rest[len(weights) :]
    both = [member for pair in zip(weights, others) for member in pair]
    act_swapped, grad_in, *reduced, summed = run_backward(
        cot, ln_gain, segk, act_own, saved, both, block
    )
    *grads, grad_qv, grad_up_bias, grad_bias, grad_gain, grad_shift, out_act, grad_in = run_finish(
        reduced, summed, (act_own, act_swapped), grad_in, block
    )
    grad_down, grad_up, grad_out, grad_qkv = grads
    return (
        out_act,
        grad_in,
        grad_qkv.transpose(0, 2, 1, 3),
        grad_qv,
        grad_out,
        grad_up,
        grad_up_bias,
        grad_down,
        grad_bias,
        grad_gain,
        grad_shift,
    )


def solution(mesh):
    sizes = (mesh.shape["dp"], mesh.shape["tensor"])
    local = local_split if sizes == (16, 2) else local_general
    return jax.shard_map(
        local,
        mesh=mesh,
        in_specs=(
            P(("dp", "tensor"), None),
            P("dp", None),
            P(None, None, None, "tensor"),
            P(None, None, "tensor"),
            P(None, "tensor", None),
            P(None, None, "tensor"),
            P(None, "tensor"),
            P(None, "tensor", None),
            P(),
            P(),
            P(),
            P(("dp", "tensor"), None),
        ),
        out_specs=(
            P(("dp", "tensor"), None),
            P(("dp", "tensor"), None),
            P(None, None, None, "tensor"),
            P(None, None, "tensor"),
            P(None, "tensor", None),
            P(None, None, "tensor"),
            P(None, "tensor"),
            P(None, "tensor", None),
            P(),
            P(),
            P(),
        ),
        check_vma=False,
    )
```

```python
import functools

import jax
import jax.numpy as jnp
from jax import lax
from jax.experimental import pallas as pl
from jax.experimental.pallas import tpu as pltpu
from jax.sharding import PartitionSpec as P

HEAD_DIM = 64


epsilon = 1e-05
gelu_coeff = 0.7978845608028654
cubic_coeff = 0.044715
masked_score = -1e30


def as_sent(shard):

    def short(part):
        return part.astype(jnp.bfloat16) if part.dtype == jnp.float32 else part

    return jax.tree.map(short, shard)


def layer_norm(values, gain, shift):
    average = jnp.mean(values, axis=-1, keepdims=True)
    centred = values - average
    inverse = lax.rsqrt(jnp.mean(centred * centred, axis=-1, keepdims=True) + epsilon)
    unit_rows = centred * inverse
    return (unit_rows * gain + shift, unit_rows, inverse)


def norm_backward(incoming, unit_rows, inverse, gain):
    scaled = incoming * gain
    first_mean = jnp.mean(scaled, axis=-1, keepdims=True)
    second_mean = jnp.mean(scaled * unit_rows, axis=-1, keepdims=True)
    through = inverse * (scaled - first_mean - unit_rows * second_mean)
    return (through, jnp.sum(incoming * unit_rows, axis=0), jnp.sum(incoming, axis=0))


def gelu_tanh(before):
    tanh_input = gelu_coeff * (before + cubic_coeff * before * before * before)
    return 0.5 * before * (1.0 + jnp.tanh(tanh_input))


def gelu_slope(before):
    tanh_input = gelu_coeff * (before + cubic_coeff * before * before * before)
    tangent = jnp.tanh(tanh_input)
    return 0.5 * (1.0 + tangent) + 0.5 * before * (1.0 - tangent * tangent) * gelu_coeff * (
        1.0 + 3.0 * cubic_coeff * before * before
    )


def masked_scores(query_block, key_seq, segment_row, offset, block_rows):
    window = key_seq.shape[0]
    scores = jnp.einsum(
        "qhe,khe->hqk", query_block, key_seq, preferred_element_type=jnp.float32
    ) * HEAD_DIM ** (-0.5)
    query_place = offset + lax.iota(jnp.int32, block_rows)
    key_place = lax.iota(jnp.int32, window)
    query_segment = segment_row[offset : offset + block_rows]
    allowed = (query_place[:, None] >= key_place[None, :]) & (
        query_segment[:, None] == segment_row[None, :]
    )
    return jnp.where(allowed[None], scores, masked_score)


def split_heads(flat_rows, seq_count):
    return flat_rows.reshape(
        seq_count, flat_rows.shape[0] // seq_count, flat_rows.shape[1] // HEAD_DIM, HEAD_DIM
    )


def attend_forward(query_rows, key_rows, value_rows, segments):
    seq_count, window = segments.shape
    block_rows = min(512, window)

    def one_sequence(member):
        query_seq, key_seq, value_seq, segment_row = member
        outputs = []
        totals = []
        for block_index in range(window // block_rows):
            offset = block_index * block_rows
            scores = masked_scores(
                query_seq[offset : offset + block_rows], key_seq, segment_row, offset, block_rows
            )
            highest = jnp.max(scores, axis=-1, keepdims=True)
            raised = jnp.exp(scores - highest)
            summed = jnp.sum(raised, axis=-1, keepdims=True)
            softmax_low = (raised / summed).astype(jnp.bfloat16)
            block_out = jnp.einsum(
                "hqk,khe->qhe", softmax_low, value_seq, preferred_element_type=jnp.float32
            )
            outputs.append(block_out.astype(jnp.bfloat16))
            totals.append(highest[..., 0] + jnp.log(summed[..., 0]))
        return (jnp.concatenate(outputs, axis=0), jnp.stack(totals, axis=0))

    attended, log_totals = lax.map(
        one_sequence,
        (
            split_heads(query_rows, seq_count),
            split_heads(key_rows, seq_count),
            split_heads(value_rows, seq_count),
            segments,
        ),
    )
    return (attended.reshape(query_rows.shape), log_totals)


def attend_backward(query_rows, key_rows, value_rows, segments, log_totals, grad_attended):
    seq_count, window = segments.shape
    block_rows = min(512, window)
    scaling = HEAD_DIM ** (-0.5)

    def one_sequence(member):
        query_seq, key_seq, value_seq, segment_row, totals_seq, grad_seq = member
        query_parts = []
        grad_keys = jnp.zeros(key_seq.shape, jnp.float32)
        grad_values = jnp.zeros(value_seq.shape, jnp.float32)
        for block_index in range(window // block_rows):
            offset = block_index * block_rows
            query_block = query_seq[offset : offset + block_rows]
            grad_block = grad_seq[offset : offset + block_rows]
            scores = masked_scores(query_block, key_seq, segment_row, offset, block_rows)
            softmax_exact = jnp.exp(scores - totals_seq[block_index][..., None])
            softmax_low = softmax_exact.astype(jnp.bfloat16)
            grad_softmax = jnp.einsum(
                "qhe,khe->hqk", grad_block, value_seq, preferred_element_type=jnp.float32
            )
            row_terms = jnp.sum(softmax_exact * grad_softmax, axis=-1, keepdims=True)
            grad_scores = (softmax_exact * (grad_softmax - row_terms)).astype(jnp.bfloat16)
            query_parts.append(
                jnp.einsum("hqk,khe->qhe", grad_scores, key_seq, preferred_element_type=jnp.float32)
                * scaling
            )
            grad_keys = (
                grad_keys
                + jnp.einsum(
                    "hqk,qhe->khe", grad_scores, query_block, preferred_element_type=jnp.float32
                )
                * scaling
            )
            grad_values = grad_values + jnp.einsum(
                "hqk,qhe->khe", softmax_low, grad_block, preferred_element_type=jnp.float32
            )
        grad_query = jnp.concatenate(query_parts, axis=0)
        return (
            grad_query.astype(jnp.bfloat16),
            grad_keys.astype(jnp.bfloat16),
            grad_values.astype(jnp.bfloat16),
        )

    grad_query, grad_keys, grad_values = lax.map(
        one_sequence,
        (
            split_heads(query_rows, seq_count),
            split_heads(key_rows, seq_count),
            split_heads(value_rows, seq_count),
            segments,
            log_totals,
            split_heads(grad_attended, seq_count),
        ),
    )
    return (
        grad_query.reshape(query_rows.shape),
        grad_keys.reshape(query_rows.shape),
        grad_values.reshape(query_rows.shape),
    )


def layer_forward(residual, segments, weights):
    w_qkv, qv_bias, w_out, w_up, up_bias, w_down, out_bias, gains, shifts = weights
    row_count = residual.shape[0]
    normed, unit_one, inverse_one = layer_norm(residual, gains[0], shifts[0])
    normed_all = lax.all_gather(normed.astype(jnp.bfloat16), "tensor", axis=0, tiled=True)
    projected = jnp.einsum("td,dsc->tsc", normed_all, w_qkv, preferred_element_type=jnp.float32)
    query_rows = (projected[:, 0] + qv_bias[0]).astype(jnp.bfloat16)
    key_rows = projected[:, 1].astype(jnp.bfloat16)
    value_rows = (projected[:, 2] + qv_bias[1]).astype(jnp.bfloat16)
    attended, log_totals = attend_forward(query_rows, key_rows, value_rows, segments)
    middle = (
        residual
        + lax.psum_scatter(
            jnp.dot(
                lax.slice_in_dim(attended, 0, row_count * lax.axis_size("tensor"), axis=0),
                w_out,
                preferred_element_type=jnp.float32,
            ).astype(jnp.bfloat16),
            "tensor",
            scatter_dimension=0,
            tiled=True,
        ).astype(jnp.float32)
        + out_bias[0]
    )
    normed_two, unit_two, inverse_two = layer_norm(middle, gains[1], shifts[1])
    normed_low = normed_two.astype(jnp.bfloat16)
    ffn_rows = lax.all_gather(normed_low, "tensor", axis=0, tiled=True)
    before = jnp.dot(ffn_rows, w_up, preferred_element_type=jnp.float32) + up_bias
    activated = gelu_tanh(before).astype(jnp.bfloat16)
    ffn_branch = lax.psum_scatter(
        jnp.dot(
            lax.slice_in_dim(activated, 0, row_count * lax.axis_size("tensor"), axis=0),
            w_down,
            preferred_element_type=jnp.float32,
        ).astype(jnp.bfloat16),
        "tensor",
        scatter_dimension=0,
        tiled=True,
    ).astype(jnp.float32)
    kept_ffn = (w_up, w_down)
    result = middle + ffn_branch + out_bias[1]
    kept_state = (
        unit_one,
        inverse_one,
        normed_all,
        query_rows,
        key_rows,
        value_rows,
        attended,
        log_totals,
        unit_two,
        inverse_two,
        ffn_rows,
        before,
        activated,
        kept_ffn,
    )
    return (result, kept_state)


def layer_backward(grad_residual, segments, weights, kept_state):
    w_qkv, qv_bias, w_out, w_up, up_bias, w_down, out_bias, gains, shifts = weights
    (
        unit_one,
        inverse_one,
        normed_all,
        query_rows,
        key_rows,
        value_rows,
        attended,
        log_totals,
        unit_two,
        inverse_two,
        ffn_rows,
        before,
        activated,
        kept_ffn,
    ) = kept_state
    up_used, down_used = kept_ffn
    row_count = grad_residual.shape[0]
    grad_branch = grad_residual.astype(jnp.bfloat16)
    bias_down = jnp.sum(grad_branch, axis=0, dtype=jnp.float32)
    grad_rows = lax.all_gather(grad_branch, "tensor", axis=0, tiled=True)
    grad_hidden = jnp.einsum("td,fd->tf", grad_rows, down_used, preferred_element_type=jnp.float32)
    grad_before = (grad_hidden * gelu_slope(before)).astype(jnp.bfloat16)
    grad_down = jnp.einsum("tf,td->fd", activated, grad_rows, preferred_element_type=jnp.float32)
    grad_up = jnp.einsum("td,tf->df", ffn_rows, grad_before, preferred_element_type=jnp.float32)
    grad_up_bias = jnp.sum(grad_before, axis=0, dtype=jnp.float32)
    piece_rows = lax.slice_in_dim(grad_before, 0, row_count * lax.axis_size("tensor"), axis=0)
    grad_normed_two = lax.psum_scatter(
        jnp.einsum("tf,df->td", piece_rows, w_up, preferred_element_type=jnp.float32).astype(
            jnp.bfloat16
        ),
        "tensor",
        scatter_dimension=0,
        tiled=True,
    ).astype(jnp.float32)
    through_two, gain_two, shift_two = norm_backward(
        grad_normed_two, unit_two, inverse_two, gains[1]
    )
    grad_middle = grad_residual + through_two
    grad_attn_branch = grad_middle.astype(jnp.bfloat16)
    bias_attn = jnp.sum(grad_attn_branch, axis=0, dtype=jnp.float32)
    grad_attn_all = lax.all_gather(grad_attn_branch, "tensor", axis=0, tiled=True)
    grad_out_w = jnp.einsum(
        "tc,td->cd", attended, grad_attn_all, preferred_element_type=jnp.float32
    )
    grad_attended = jnp.einsum(
        "td,cd->tc", grad_attn_all, w_out, preferred_element_type=jnp.float32
    ).astype(jnp.bfloat16)
    grad_query, grad_keys, grad_values = attend_backward(
        query_rows, key_rows, value_rows, segments, log_totals, grad_attended
    )
    grad_projected = jnp.stack((grad_query, grad_keys, grad_values), axis=1)
    grad_qkv = jnp.einsum(
        "td,tsc->dsc", normed_all, grad_projected, preferred_element_type=jnp.float32
    )
    grad_qv_bias = jnp.stack(
        (
            jnp.sum(grad_query, axis=0, dtype=jnp.float32),
            jnp.sum(grad_values, axis=0, dtype=jnp.float32),
        )
    )
    piece_rows = lax.slice_in_dim(grad_projected, 0, row_count * lax.axis_size("tensor"), axis=0)
    grad_normed = lax.psum_scatter(
        jnp.einsum("tsc,dsc->td", piece_rows, w_qkv, preferred_element_type=jnp.float32).astype(
            jnp.bfloat16
        ),
        "tensor",
        scatter_dimension=0,
        tiled=True,
    ).astype(jnp.float32)
    through_one, gain_one, shift_one = norm_backward(grad_normed, unit_one, inverse_one, gains[0])
    grad_input = grad_middle + through_one
    spread = (grad_qkv, grad_qv_bias, grad_out_w, grad_up, grad_up_bias, grad_down)
    shared = (
        jnp.stack((bias_attn, bias_down)),
        jnp.stack((gain_one, gain_two)),
        jnp.stack((shift_one, shift_two)),
    )
    return (grad_input, spread, shared)


def local_general(
    tokens_in,
    segments,
    w_qkv,
    qv_bias,
    w_out,
    w_up,
    up_bias,
    w_down,
    out_bias,
    ln_gain,
    ln_bias,
    cotangent,
):
    layers_total = w_qkv.shape[0]
    all_params = (w_qkv, qv_bias, w_out, w_up, up_bias, w_down, out_bias, ln_gain, ln_bias)
    residual = tokens_in.astype(jnp.float32)
    kept_layers = []
    for layer_index in range(layers_total):
        weights = tuple((member_array[layer_index] for member_array in all_params))
        residual, kept_state = layer_forward(residual, segments, weights)
        kept_layers.append(kept_state)
    out_act = residual.astype(jnp.bfloat16)
    grad_residual = cotangent.astype(jnp.float32)
    spread_layers = []
    shared_layers = []
    for layer_index in reversed(range(layers_total)):
        weights = tuple((member_array[layer_index] for member_array in all_params))
        grad_residual, spread, shared = layer_backward(
            grad_residual, segments, weights, kept_layers[layer_index]
        )
        spread_layers.insert(0, spread)
        shared_layers.insert(0, shared)
    spread_stack = tuple(
        (
            jnp.stack([spread_layers[layer_index][position] for layer_index in range(layers_total)])
            for position in range(6)
        )
    )
    spread_stack = jax.tree.map(
        lambda part: part.astype(jnp.float32), lax.psum(as_sent(spread_stack), "dp")
    )
    shared_stack = tuple(
        (
            jnp.stack([shared_layers[layer_index][position] for layer_index in range(layers_total)])
            for position in range(3)
        )
    )
    shared_stack = lax.psum(shared_stack, ("dp", "tensor"))
    grad_in = grad_residual.astype(jnp.bfloat16)
    return (out_act, grad_in) + tuple(spread_stack) + tuple(shared_stack)


BAND = 256
LANES = 128
VMEM_ASKED = 60 * 2**20


def dot_nt(left, right):
    return lax.dot_general(left, right, (((1,), (1,)), ((), ())), preferred_element_type=jnp.float32)


def dot_tn(left, right):
    return lax.dot_general(left, right, (((0,), (0,)), ((), ())), preferred_element_type=jnp.float32)


def dot_low(left, right):
    return jnp.dot(left, right, preferred_element_type=jnp.float32)


UNITS_LAYER = 12
Y_AHEAD = 4
HOP_BEATS = (1, 3, 5, 6)
IDLE_STEPS = 2
LOADS_AHEAD = 2


def fill_band_bias(segk_ref, bias_ref):
    wide = segk_ref.shape[1]
    values = lax.broadcasted_iota(jnp.int32, (16, wide), 0)
    member = (values == segk_ref[...]).astype(jnp.float32).astype(jnp.bfloat16)
    for block in range(bias_ref.shape[0]):
        queries = member[:, (block + 1) * BAND : (block + 2) * BAND]
        keys = member[:, block * BAND : (block + 2) * BAND]
        row_place = lax.broadcasted_iota(jnp.int32, (BAND, 2 * BAND), 0) + BAND
        column_place = lax.broadcasted_iota(jnp.int32, (BAND, 2 * BAND), 1)
        allowed = (dot_tn(queries, keys) > 0.5) & (column_place <= row_place)
        bias_ref[block] = jnp.where(allowed, 0.0, masked_score)


def band_rows(halo, rows, block):
    if block == 0:
        return jnp.concatenate([halo, rows[0:BAND, :]], axis=0)
    return rows[(block - 1) * BAND : (block + 1) * BAND, :]


def aligned(index, size):
    return pl.ds(pl.multiple_of(index * size, size), size)


def forward_kernel(layers, block, hidden_half, *refs):
    (
        tokens_ref,
        cot_ref,
        segments_ref,
        qkv_own,
        out_own,
        up_own,
        down_own,
        qv_bias_ref,
        up_bias_ref,
        out_bias_ref,
        gain_ref,
        shift_ref,
        out_act_ref,
        cot_out,
        segk_out,
        qkv_other,
        out_other,
        up_other,
        down_other,
        act_out,
        slope_out,
        normed_two_out,
        middle_out,
        attended_out,
        proj_out,
        halo_out,
        totals_out,
        normed_out,
        resid_out,
        tokens_buf,
        segments_in,
        qv_bias_in,
        up_bias_in,
        resid,
        collected,
        normed,
        normed_two,
        proj,
        halo,
        attended,
        totals,
        act_buf,
        slope_buf,
        qkv_weight,
        out_weight,
        up_weight,
        down_weight,
        qkv_arrived,
        out_arrived,
        up_arrived,
        down_arrived,
        bias_buf,
        start_send,
        start_recv,
        swap_sem,
        relay_send,
        relay_recv,
        halo_send_sem,
        halo_recv_sem,
        load_sem,
        store_sem,
        pair_store_sem,
        unit_store_sem,
    ) = refs
    width = 2 * block
    rows_all = tokens_buf.shape[0]
    pairs_half = block // LANES
    blocks_hidden = hidden_half // block
    low = jnp.bfloat16
    place = lax.axis_index("dp")
    y = lax.axis_index("tensor")
    core = place % 2
    x = (place // 2) % 2
    z = place // 4
    z_low = z % 2
    core_partner = {"dp": place + 1 - 2 * core, "tensor": y}
    x_partner = {"dp": place + 2 - 4 * x, "tensor": y}
    y_partner = {"dp": place, "tensor": 1 - y}
    z_partner = {"dp": place + 4 - 8 * z_low, "tensor": y}
    swap_partner = {"dp": place + 1 - 2 * core, "tensor": 1 - y}
    swaps = core + y - 2 * core * y

    barrier = pltpu.get_barrier_semaphore()
    for partner in (core_partner, x_partner, y_partner, z_partner, swap_partner):
        pl.semaphore_signal(barrier, inc=1, device_id=partner, device_id_type=MESH)
    pl.semaphore_wait(barrier, 5)

    def remote(source, target, send, recv, partner):
        return pltpu.make_async_remote_copy(
            src_ref=source,
            dst_ref=target,
            send_sem=send,
            recv_sem=recv,
            device_id=partner,
            device_id_type=MESH,
        )

    def swap_copy(index, source, target):
        return remote(source, target, start_send.at[index], start_recv.at[index], swap_partner)

    def swap_start(index, source, target):
        @pl.when(swaps == 1)
        def _():
            swap_copy(index, source, target).start()

        @pl.when(swaps == 0)
        def _():
            pltpu.make_async_copy(source, tokens_buf, swap_sem.at[index]).start()

    def swap_wait(index, source, target):
        @pl.when(swaps == 1)
        def _():
            swap_copy(index, source, target).wait()

        @pl.when(swaps == 0)
        def _():
            pltpu.make_async_copy(source, tokens_buf, swap_sem.at[index]).wait()

    segments_copy = remote(
        segments_ref, segments_in, start_send.at[2], start_recv.at[2], core_partner
    )
    qv_copy = remote(qv_bias_ref, qv_bias_in, start_send.at[3], start_recv.at[3], y_partner)
    up_copy = remote(up_bias_ref, up_bias_in, start_send.at[4], start_recv.at[4], y_partner)

    units = layers * UNITS_LAYER

    def for_unit(unit, action):
        layer, inside = unit // UNITS_LAYER, unit % UNITS_LAYER

        @pl.when(inside < 3)
        def _():
            action(*[ref.at[layer, inside] for ref in (qkv_own, qkv_arrived, qkv_other)])

        @pl.when(inside == 3)
        def _():
            action(*[ref.at[layer] for ref in (out_own, out_arrived, out_other)])

        cut = aligned((inside - 4) // 2, block)

        @pl.when((inside >= 4) & (inside % 2 == 0))
        def _():
            action(*[ref.at[layer, :, cut] for ref in (up_own, up_arrived, up_other)])

        @pl.when((inside >= 4) & (inside % 2 == 1))
        def _():
            action(*[ref.at[layer, cut, :] for ref in (down_own, down_arrived, down_other)])

    def hop_copy(hop, unit, source, target):
        partner = (y_partner, x_partner, z_partner, core_partner)[hop]
        return remote(source, target, relay_send.at[hop, unit], relay_recv.at[hop, unit], partner)

    def piece_of(view, hop, short):
        rows = view.shape[0]
        if hop == 3:
            return view.at[aligned(core, rows // 2)]
        if hop == 2:
            return view.at[aligned(2 * core + z_low, rows // 4)]
        if short:
            return view.at[aligned(4 * core + 2 * z_low + x, rows // 8)]
        return view.at[aligned(2 * core + x, rows // 4)]

    def by_length(unit, hop, action):
        if hop == 3:
            action(False)
            return

        whole = (unit % 3 == 0) & (unit > 0)

        @pl.when(jnp.logical_not(whole))
        def _():
            action(True)

        if hop < 2:

            @pl.when(whole)
            def _():
                action(False)

    def hop_start(hop, unit):
        def go(own, arrived, _):
            def one(short):
                source = piece_of(own if hop == 0 else arrived, hop, short)
                hop_copy(hop, unit, source, piece_of(arrived, hop, short)).start()

            by_length(unit, hop, one)

        for_unit(unit, go)

    def hop_wait(hop, unit):
        def one(short):
            piece = piece_of(down_arrived.at[0, pl.ds(0, block), :], hop, short)
            hop_copy(hop, unit, piece, piece).wait()

        by_length(unit, hop, one)

    def when_unit(unit, action):
        @pl.when((unit >= 0) & (unit < units))
        def _():
            action(unit)

    def beat(b):
        def after_y(unit):
            hop_wait(0, unit)
            hop_start(1, unit)

        def after_x(unit):
            hop_wait(1, unit)
            hop_start(2, unit)

        def after_z(unit):
            hop_wait(2, unit)
            hop_start(3, unit)

        def after_all(unit):
            hop_wait(3, unit)

            def keep(_, arrived, other):
                pltpu.make_async_copy(arrived, other, unit_store_sem.at[unit]).start()

            for_unit(unit, keep)

        when_unit(b + Y_AHEAD, lambda unit: hop_start(0, unit))
        for lag, action in zip(HOP_BEATS, (after_y, after_x, after_z, after_all)):
            when_unit(b - lag, action)

    other_step = 2 + pairs_half + IDLE_STEPS
    out_step = other_step + 1 + pairs_half
    norm_two_step = out_step + 1
    ffn_step = norm_two_step + 1
    end_step = ffn_step + 2 * blocks_hidden
    period = end_step + 1
    jobs = layers * period

    def loads(kind, slot, *sources):
        place, targets = {
            "qkv": (blocks_hidden, (qkv_weight,)),
            "out": (blocks_hidden + 1, (out_weight,)),
            "ffn": (slot, (up_weight.at[slot], down_weight.at[slot])),
        }[kind]
        sources = sources or targets
        return [
            pltpu.make_async_copy(source, target, load_sem.at[place, index])
            for index, (source, target) in enumerate(zip(sources, targets))
        ]

    def start_all(copies):
        for copy in copies:
            copy.start()

    def wait_all(copies):
        for copy in copies:
            copy.wait()

    def prefetch(t):
        layer, step = t // period, t % period

        @pl.when(step == 1)
        def _():
            start_all(loads("qkv", 0, qkv_own.at[layer]))

        @pl.when(step == out_step)
        def _():
            start_all(loads("out", 0, out_own.at[layer]))

        @pl.when((step >= ffn_step) & (step < ffn_step + blocks_hidden))
        def _():
            inside = step - ffn_step
            cut = aligned(inside, block)
            start_all(
                loads("ffn", inside, up_own.at[layer, :, cut], down_own.at[layer, cut, :])
            )

    tiles = [slice(r, r + BAND) for r in range(0, rows_all, BAND)]
    fine_tiles = [slice(r, r + LANES) for r in range(0, rows_all, LANES)]

    def normalize(layer, index, target):
        gain = gain_ref[layer, pl.ds(index, 1), :]
        shift = shift_ref[layer, pl.ds(index, 1), :]
        for tile in fine_tiles:
            values, _, _ = layer_norm(resid[tile, :], gain, shift)
            target[tile, :] = values.astype(low)

    def store(index, source, target):
        return pltpu.make_async_copy(source, target, store_sem.at[index])

    def first_stores(layer):
        return [store(0, resid, resid_out.at[layer]), store(1, normed, normed_out.at[layer])]

    def proj_stores(layer, which):
        return [
            store(
                2 + 3 * which + third,
                proj.at[which, third],
                proj_out.at[layer, which, :, pl.ds(third * block, block)],
            )
            for third in range(3)
        ]

    def halo_store(layer, which):
        return store(8 + which, halo.at[layer, which], halo_out.at[layer, which])

    def attended_stores(layer, which):
        return [
            store(10 + which, attended.at[which], attended_out.at[layer, which]),
            store(12 + which, totals.at[which], totals_out.at[layer, which]),
        ]

    def second_stores(layer):
        return [
            store(14, resid, middle_out.at[layer]),
            store(15, normed_two, normed_two_out.at[layer]),
        ]

    def ffn_stores(layer, index, slot):
        which, inside = index // blocks_hidden, index % blocks_hidden
        cut = aligned(inside, block)
        return [
            pltpu.make_async_copy(
                buf.at[slot], out.at[layer, which, :, cut], pair_store_sem.at[slot, kind]
            )
            for kind, (buf, out) in enumerate(((act_buf, act_out), (slope_buf, slope_out)))
        ]

    def halo_copy(layer, which):
        return remote(
            proj.at[which, pl.ds(1, 2), pl.ds(rows_all - BAND, BAND)],
            halo.at[layer, which],
            halo_send_sem.at[layer, which],
            halo_recv_sem.at[layer, which],
            core_partner,
        )

    def first_job(layer):
        normalize(layer, 0, normed)
        start_all(first_stores(layer))

    def qkv_job(layer, which):
        if not which:
            wait_all(loads("qkv", 0))
        bias = qv_bias_in if which else qv_bias_ref
        for third in (1, 2, 0):
            for tile in tiles:
                weight = qkv_arrived[layer, third] if which else qkv_weight[third]
                product = dot_low(normed[tile, :], weight)
                if third != 1:
                    product = product + bias[layer, pl.ds(third // 2, 1), :]
                proj[which, third, tile, :] = product.astype(low)
            if third == 2:

                @pl.when(core == 0)
                def _():
                    halo_copy(layer, which).start()

        start_all(proj_stores(layer, which))

    def attention_job(layer, which, pair):
        @pl.when(pair == 0)
        def _():
            totals[which] = jnp.zeros_like(totals[which])

        lane = lax.broadcasted_iota(jnp.int32, (BAND, LANES), 1)
        here = aligned(pair, LANES)
        for index, tile in reversed(list(enumerate(tiles))):
            if index == 0:

                @pl.when(pair == 0)
                def _():
                    @pl.when(core == 0)
                    def _():
                        halo_copy(layer, which).wait_send()

                    @pl.when(core == 1)
                    def _():
                        halo_copy(layer, which).wait_recv()

                    halo_store(layer, which).start()

            query = proj[which, 0, tile, here]
            first = [halo[layer, which, part, :, here] if index == 0 else None for part in range(2)]
            keys = band_rows(first[0], proj[which, 1, :, here], index)
            values = band_rows(first[1], proj[which, 2, :, here], index)
            parts = []
            kept = totals[which, tile, :]
            for head in range(2):
                mine = (lane // HEAD_DIM) == head
                scores = (
                    dot_nt(jnp.where(mine, query, 0), keys) * HEAD_DIM ** (-0.5) + bias_buf[index]
                )
                highest = jnp.max(scores, axis=-1, keepdims=True)
                raised = jnp.exp(scores - highest)
                summed = jnp.sum(raised, axis=-1, keepdims=True)
                parts.append(dot_low(raised.astype(low), values) / summed)
                kept = jnp.where(lane == 2 * pair + head, highest + jnp.log(summed), kept)
            totals[which, tile, :] = kept
            attended[which, tile, here] = jnp.where(lane < HEAD_DIM, parts[0], parts[1]).astype(low)

        @pl.when(pair == pairs_half - 1)
        def _():
            start_all(attended_stores(layer, which))

    def out_job(layer):
        wait_all(loads("out", 0))
        wait_all(first_stores(layer))
        for which in range(2):
            wait_all(proj_stores(layer, which))
            halo_store(layer, which).wait()
        bias = out_bias_ref[layer, pl.ds(0, 1), :]
        for tile in tiles:
            branch = dot_low(attended[0, tile, :], out_weight[...])
            branch = branch + dot_low(attended[1, tile, :], out_arrived[layer])
            resid[tile, :] = resid[tile, :] + branch + bias

    def second_job(layer):
        normalize(layer, 1, normed_two)
        start_all(second_stores(layer))

    def ffn_job(layer, which, inside, slot):
        index = which * blocks_hidden + inside
        if not which:
            wait_all(loads("ffn", inside))

        @pl.when(index >= 2)
        def _():
            wait_all(ffn_stores(layer, index - 2, slot))

        bias = (up_bias_in if which else up_bias_ref)[pl.ds(layer, 1), aligned(inside, block)]
        cut = aligned(inside, block)
        for tile in tiles:
            up_block = up_arrived[layer, :, cut] if which else up_weight[inside]
            before = dot_low(normed_two[tile, :], up_block) + bias
            square = before * before
            tangent = jnp.tanh(gelu_coeff * before * (1.0 + cubic_coeff * square))
            raised = 0.5 * (1.0 + tangent)
            activated = (before * raised).astype(low)
            act_buf[slot, tile, :] = activated
            slope_buf[slot, tile, :] = (
                raised
                + 0.5
                * before
                * (1.0 - tangent * tangent)
                * gelu_coeff
                * (1.0 + 3.0 * cubic_coeff * square)
            ).astype(low)
            down_block = down_arrived[layer, cut, :] if which else down_weight[inside]
            product = dot_low(activated, down_block)
            if which:
                collected[tile, :] = collected[tile, :] + product
                continue

            @pl.when(inside == 0)
            def _(tile=tile, product=product):
                collected[tile, :] = product

            @pl.when(inside > 0)
            def _(tile=tile, product=product):
                collected[tile, :] = collected[tile, :] + product

        start_all(ffn_stores(layer, index, slot))

    def end_job(layer, slot):
        wait_all(ffn_stores(layer, 2 * blocks_hidden - 2, slot))
        wait_all(ffn_stores(layer, 2 * blocks_hidden - 1, 1 - slot))
        wait_all(second_stores(layer))
        for which in range(2):
            wait_all(attended_stores(layer, which))
        bias = out_bias_ref[layer, pl.ds(1, 1), :]
        for tile in tiles:
            resid[tile, :] = resid[tile, :] + collected[tile, :] + bias

    def job(t):
        slot = t % 2
        layer, step = t // period, t % period

        def at(first, count, action):
            @pl.when((step >= first) & (step < first + count))
            def _():
                action(step - first)

        at(0, 1, lambda _: first_job(layer))
        later = (layer > 0).astype(jnp.int32)
        other_at = other_step + later * (2 - other_step)
        other_first = other_step + 1 + later * (2 + pairs_half - other_step)
        at(1, 1, lambda _: qkv_job(layer, 0))
        at(2 + later, pairs_half, lambda pair: attention_job(layer, 0, pair))
        at(other_at, 1, lambda _: qkv_job(layer, 1))
        at(other_first, pairs_half, lambda pair: attention_job(layer, 1, pair))
        at(out_step, 1, lambda _: out_job(layer))
        at(norm_two_step, 1, lambda _: second_job(layer))
        at(ffn_step, blocks_hidden, lambda inside: ffn_job(layer, 0, inside, slot))
        at(ffn_step + blocks_hidden, blocks_hidden, lambda inside: ffn_job(layer, 1, inside, slot))
        at(end_step, 1, lambda _: end_job(layer, slot))

    swap_start(0, tokens_ref, tokens_buf)
    halo[...] = jnp.zeros_like(halo)
    segments_copy.start()
    qv_copy.start()
    up_copy.start()
    for unit in range(Y_AHEAD):
        hop_start(0, unit)
    segments_copy.wait()
    window = jnp.where(core == y, segments_ref[...], segments_in[...])

    @pl.when(core == 0)
    def _():
        segk_out[:, 0:BAND] = jnp.full((1, BAND), -1, jnp.int32)
        segk_out[:, BAND:] = window[:, 0:rows_all]

    @pl.when(core == 1)
    def _():
        segk_out[...] = window[:, rows_all - BAND :]

    fill_band_bias(segk_out, bias_buf)
    qv_copy.wait()
    up_copy.wait()
    swap_wait(0, tokens_ref, tokens_buf)
    for tile in tiles:
        resid[tile, :] = tokens_buf[tile, :].astype(jnp.float32)
    cot_tick = period + other_step + 4

    def past(t, begin):
        return (t - begin) * (t > begin).astype(jnp.int32)

    def beat_at(t):
        return (10 * t - 4 * past(t, 12) - past(t, 22)) // 10

    for ahead in range(LOADS_AHEAD):
        prefetch(jnp.int32(ahead))

    def tick(t, carry):
        @pl.when((t == 0) | (beat_at(t) != beat_at(t - 1)))
        def _():
            beat(beat_at(t))

        @pl.when(t == cot_tick)
        def _():
            swap_start(1, cot_ref, cot_out)

        @pl.when((t == cot_tick + 4) & (swaps == 0))
        def _():
            pltpu.make_async_copy(cot_ref, tokens_buf, swap_sem.at[1]).wait()
            pltpu.make_async_copy(tokens_buf, cot_out, swap_sem.at[1]).start()

        @pl.when(t + LOADS_AHEAD < jobs)
        def _():
            prefetch(t + LOADS_AHEAD)

        job(t)
        return carry

    lax.fori_loop(0, jobs, tick, 0)
    for tile in tiles:
        normed_two[tile, :] = resid[tile, :].astype(low)
    last_store = store(0, normed_two, out_act_ref)
    last_store.start()
    last_store.wait()
    swap_wait(1, cot_ref, cot_out)
    for unit in range(units):
        block_ref = down_arrived.at[0, pl.ds(0, block), :]
        pltpu.make_async_copy(block_ref, block_ref, unit_store_sem.at[unit]).wait()


def run_forward(tokens, cotangent, segments, weights, biases, out_bias, gain, shift, block):
    rows, width = tokens.shape
    layers, hidden_half = weights[-1].shape[0], weights[-1].shape[1]
    low, wide = jnp.bfloat16, jnp.float32
    anywhere = pl.BlockSpec(memory_space=pl.ANY)
    in_vmem = pl.BlockSpec(memory_space=pltpu.VMEM)
    vmem = pltpu.VMEM
    units = layers * UNITS_LAYER
    shape = jax.ShapeDtypeStruct
    saved = [
        shape((layers, 2, rows, hidden_half), low),
        shape((layers, 2, rows, hidden_half), low),
        shape((layers, rows, width), low),
        shape((layers, rows, width), wide),
        shape((layers, 2, rows, block), low),
        shape((layers, 2, rows, 3 * block), low),
        shape((layers, 2, 2, BAND, block), low),
        shape((layers, 2, rows, LANES), wide),
        shape((layers, rows, width), low),
        shape((layers, rows, width), wide),
    ]
    others = [shape(member.shape, low) for member in weights]
    return pl.pallas_call(
        functools.partial(forward_kernel, layers, block, hidden_half),
        in_specs=[anywhere] * 2 + [in_vmem] + [anywhere] * 4 + [in_vmem] * 5,
        out_specs=[anywhere] * 2 + [in_vmem] + [anywhere] * (len(others) + len(saved)),
        out_shape=[
            shape((rows, width), low),
            shape((rows, width), low),
            shape((1, rows + BAND), jnp.int32),
        ]
        + others
        + saved,
        scratch_shapes=[
            vmem((rows, width), low),
            vmem(segments.shape, jnp.int32),
            vmem(biases[0].shape, wide),
            vmem(biases[1].shape, wide),
            vmem((rows, width), wide),
            vmem((rows, width), wide),
            vmem((rows, width), low),
            vmem((rows, width), low),
            vmem((2, 3, rows, block), low),
            vmem((layers, 2, 2, BAND, block), low),
            vmem((2, rows, block), low),
            vmem((2, rows, LANES), wide),
            vmem((2, rows, block), low),
            vmem((2, rows, block), low),
            vmem((3, width, block), low),
            vmem((block, width), low),
            vmem((hidden_half // block, width, block), low),
            vmem((hidden_half // block, block, width), low),
        ]
        + [vmem(member.shape, low) for member in weights]
        + [
            vmem((rows // BAND, BAND, 2 * BAND), wide),
            pltpu.SemaphoreType.DMA((5,)),
            pltpu.SemaphoreType.DMA((5,)),
            pltpu.SemaphoreType.DMA((2,)),
            pltpu.SemaphoreType.DMA((4, units)),
            pltpu.SemaphoreType.DMA((4, units)),
            pltpu.SemaphoreType.DMA((layers, 2)),
            pltpu.SemaphoreType.DMA((layers, 2)),
            pltpu.SemaphoreType.DMA((hidden_half // block + 2, 2)),
            pltpu.SemaphoreType.DMA((16,)),
            pltpu.SemaphoreType.DMA((2, 2)),
            pltpu.SemaphoreType.DMA((units,)),
        ],
        compiler_params=pltpu.CompilerParams(
            collective_id=1, has_side_effects=True, vmem_limit_bytes=VMEM_ASKED
        ),
        name="forward",
    )(tokens, cotangent, segments, *weights, *biases, out_bias, gain, shift)


SLOTS = 8
CORE_SLOTS = 4
RESULT_SLOTS = 11
STAGED = 2
FIRST = 0
LAGS = dict(
    core=1, first=3, second=5, third=7, fourth=9, fifth=11, sixth=13, whole=14, stored=15
)
VECTOR_STEP = 3
VECTOR_ROWS = 12
MESH = pl.DeviceIdType.MESH
FFN_STEPS = 4
QKV_STEPS = 3


def added(left, right):
    return (left.astype(jnp.float32) + right.astype(jnp.float32)).astype(jnp.bfloat16)


def backward_kernel(layers, block, hidden_half, *refs):
    (
        cot_ref,
        gain_ref,
        segk_ref,
        out_act_ref,
        act_ref,
        slope_ref,
        normed_two_ref,
        middle_ref,
        attended_ref,
        proj_ref,
        halo_ref,
        totals_ref,
        normed_ref,
        resid_ref,
        qkv_own,
        qkv_other,
        out_own,
        out_other,
        up_own,
        up_other,
        down_own,
        down_other,
        out_act_out,
        grad_in_ref,
        out_down,
        out_up,
        out_out,
        out_qkv,
        vector_out,
        grad_branch,
        grad_attn,
        grad_before,
        grad_proj,
        grad_res,
        collected,
        grad_attended,
        qkv_buf,
        halo_buf,
        totals_buf,
        kept_kv,
        halo_send,
        halo_in,
        rows_weight,
        columns_weight,
        slope_buf,
        wide_buf,
        bias_buf,
        sums_buf,
        pair_buf,
        one_buf,
        part_buf,
        core_in,
        sent,
        held,
        kept,
        first_in,
        second_in,
        third_in,
        result,
        vec_in,
        load_sem,
        io_sem,
        halo_send_sem,
        halo_recv_sem,
        staged_sem,
        send_sems,
        recv_sems,
        store_sem,
        vec_send,
        vec_recv,
        swap_send,
        swap_recv,
    ) = refs
    half, quarter = block // 2, block // 4
    width = 2 * block
    rows_all = grad_branch.shape[0]
    pairs_half = block // LANES
    pairs = 2 * pairs_half
    low = jnp.bfloat16
    place = lax.axis_index("dp")
    y = lax.axis_index("tensor")
    core = place % 2
    x = (place // 2) % 2
    z = place // 4
    z_low = z % 2
    inner = (z + 1) // 2 % 2
    core_partner = {"dp": place + 1 - 2 * core, "tensor": y}
    x_partner = {"dp": place + 2 - 4 * x, "tensor": y}
    y_partner = {"dp": place, "tensor": 1 - y}
    z_partner = {"dp": place + 4 - 8 * z_low, "tensor": y}
    middle_partner = {"dp": place + 4 * (3 - 2 * z), "tensor": y}
    swap_partner = {"dp": place + 1 - 2 * core, "tensor": 1 - y}

    barrier = pltpu.get_barrier_semaphore()
    for partner in (core_partner, x_partner, y_partner, z_partner, swap_partner):
        pl.semaphore_signal(barrier, inc=1, device_id=partner, device_id_type=MESH)

    @pl.when(inner == 1)
    def _():
        pl.semaphore_signal(barrier, inc=1, device_id=middle_partner, device_id_type=MESH)
        pl.semaphore_wait(barrier, 6)

    @pl.when(inner == 0)
    def _():
        pl.semaphore_wait(barrier, 5)

    blocks_hidden = hidden_half // block
    plan = (
        ("rows", blocks_hidden, 2),
        ("columns", 2, blocks_hidden),
        ("rows", 1, 2),
        ("columns", 2, 3),
    )
    starts = []
    per_layer = 0
    for _, down_count, across_count in plan:
        starts.append(per_layer)
        per_layer += down_count * across_count
    chunks = layers * per_layer
    out_refs = (out_down, out_up, out_out, out_qkv)

    def block_of(index):
        return pl.ds(pl.multiple_of(index * block, block), block)

    def for_matrix(chunk, action):
        layer = layers - 1 - chunk // per_layer
        inside = chunk % per_layer
        for member, (_, down_count, across_count) in enumerate(plan):
            begin = starts[member]

            @pl.when((inside >= begin) & (inside < begin + down_count * across_count))
            def _(member=member, begin=begin, across_count=across_count):
                local = inside - begin
                action(member, layer, local // across_count, local % across_count)

    def operands_of(member, layer, i, j):
        if member == 0:
            return (
                grad_branch.at[:, block_of(j)],
                act_ref.at[layer, 0, :, block_of(i)],
                act_ref.at[layer, 1, :, block_of(i)],
            )
        if member == 1:
            return (
                normed_two_ref.at[layer, :, block_of(i)],
                grad_before.at[j // 2, :, block_of(j % 2)],
                grad_before.at[blocks_hidden // 2 + j // 2, :, block_of(j % 2)],
            )
        if member == 2:
            return (
                grad_attn.at[:, block_of(j)],
                attended_ref.at[layer, 0, :, block_of(i)],
                attended_ref.at[layer, 1, :, block_of(i)],
            )
        return (
            normed_ref.at[layer, :, block_of(i)],
            grad_proj.at[:, block_of(j)],
            grad_proj.at[:, block_of(3 + j)],
        )

    def staged_copies(chunk, shared, own, other):
        slot = chunk % STAGED
        return (
            pltpu.make_async_copy(own, pair_buf.at[slot, 0], staged_sem.at[slot, 0]),
            pltpu.make_async_copy(other, pair_buf.at[slot, 1], staged_sem.at[slot, 1]),
            pltpu.make_async_copy(shared, one_buf.at[slot], staged_sem.at[slot, 2]),
        )

    def stage_operands(chunk):
        def action(member, layer, i, j):
            for copy in staged_copies(chunk, *operands_of(member, layer, i, j)):
                copy.start()

        for_matrix(chunk, action)

    def remote(step, chunk, source, target, partner):
        slot = chunk % SLOTS
        return pltpu.make_async_remote_copy(
            src_ref=source,
            dst_ref=target,
            send_sem=send_sems.at[step, slot],
            recv_sem=recv_sems.at[step, slot],
            device_id=partner,
            device_id_type=MESH,
        )

    def x_first(chunk):
        left = chunks - 1 - chunk
        near = (chunk <= 10) & (chunk % 2 == 0) | (left <= 10) & (left % 2 == 0)
        far = (chunk > 10) & (left > 10)
        third = far & (chunk % 3 == 1) & ((chunk < 18) | (left < 19))
        fourth = far & (chunk % 4 == 0) & (chunk >= 18) & (left >= 19)
        return near | third | fourth

    def core_copy(chunk):
        return remote(
            0,
            chunk,
            part_buf.at[chunk % STAGED, :, aligned(1 - core, half)],
            core_in.at[chunk % CORE_SLOTS],
            core_partner,
        )

    low_middle = z - 1
    far_middle = 2 - z

    def first_copy(chunk, partner):
        slot = chunk % SLOTS
        return remote(1, chunk, sent.at[slot], first_in.at[slot], partner)

    def y_copy(chunk):
        slot = chunk % SLOTS
        return remote(2, chunk, kept.at[slot, 1], second_in.at[slot, 0], y_partner)

    def pair_copy(chunk):
        slot = chunk % SLOTS
        return remote(2, chunk, kept.at[slot], second_in.at[slot], z_partner)

    def single_copy(chunk):
        slot = chunk % SLOTS
        return remote(3, chunk, kept.at[slot, 0], third_in.at[slot, 0], z_partner)

    def split_copy(chunk):
        slot = chunk % SLOTS
        return remote(3, chunk, kept.at[slot, far_middle], third_in.at[slot, 0], middle_partner)

    def middle_copy(chunk):
        slot = chunk % SLOTS
        return remote(4, chunk, kept.at[slot, 0], third_in.at[slot, 1], middle_partner)

    def across_copy(chunk):
        slot = chunk % SLOTS
        return remote(4, chunk, kept.at[slot, low_middle], third_in.at[slot, 1], x_partner)

    def result_copy(step, chunk, rows, partner):
        piece = result.at[chunk % RESULT_SLOTS, rows]
        return remote(step, chunk, piece, piece, partner)

    x_rows = aligned(2 * core + x, quarter)
    core_rows = aligned(core, half)

    def middle_rows():
        return aligned(2 * core + low_middle, quarter)

    def store_copy(chunk, target):
        slot = chunk % RESULT_SLOTS
        return pltpu.make_async_copy(result.at[slot], target, store_sem.at[slot])

    def multiply(chunk):
        slot = chunk % STAGED
        for copy in staged_copies(chunk, one_buf.at[slot], pair_buf.at[slot, 0], pair_buf.at[slot, 1]):
            copy.wait()
        inside = chunk % per_layer
        by_rows = (inside < starts[1]) | ((inside >= starts[2]) & (inside < starts[3]))

        @pl.when(by_rows)
        def _():
            single = one_buf[slot]
            for which in range(2):
                part_buf[slot, which] = dot_tn(pair_buf[slot, which], single).astype(low)

        @pl.when(jnp.logical_not(by_rows))
        def _():
            single = one_buf[slot]
            for which in range(2):
                part_buf[slot, which] = dot_tn(single, pair_buf[slot, which]).astype(low)

        core_copy(chunk).start()

    def branch(chunk, by_x, by_y):
        is_x = x_first(chunk)

        @pl.when(is_x)
        def _():
            by_x()

        @pl.when(jnp.logical_not(is_x))
        def _():
            by_y()

    def on_middle(action):
        @pl.when(inner == 1)
        def _():
            action()

    def by_place(at_end, at_middle):
        @pl.when(inner == 0)
        def _():
            at_end()

        on_middle(at_middle)

    def after_core(chunk):
        slot, core_slot, part_slot = chunk % SLOTS, chunk % CORE_SLOTS, chunk % STAGED
        core_copy(chunk).wait()
        is_x = x_first(chunk).astype(jnp.int32)

        def summed(which, row):
            near = part_buf[part_slot, which, aligned(2 * core + row, quarter), :]
            return added(near, core_in[core_slot, which, aligned(row, quarter), :])

        for index in range(2):
            sent[slot, index] = summed(
                is_x * index + (1 - is_x), is_x * (1 - x) + (1 - is_x) * index
            )
        branch(
            chunk,
            lambda: first_copy(chunk, x_partner).start(),
            lambda: first_copy(chunk, y_partner).start(),
        )
        for index in range(2):
            held[slot, index] = summed(is_x * index, is_x * x + (1 - is_x) * index)

    def after_first(chunk):
        slot = chunk % SLOTS
        first_copy(chunk, y_partner).wait()
        for index in (1, 0):
            kept[slot, index] = added(held[slot, index], first_in[slot, index])

        def by_y():
            @pl.when(inner == 0)
            def _():
                pair_copy(chunk).start()

        branch(chunk, lambda: y_copy(chunk).start(), by_y)

    def after_second(chunk):
        slot = chunk % SLOTS

        def by_x():
            y_copy(chunk).wait()
            kept[slot, 0] = added(kept[slot, 0], second_in[slot, 0])

            @pl.when(inner == 0)
            def _():
                single_copy(chunk).start()

        def at_middle():
            pair_copy(chunk).wait_recv()
            kept[slot, far_middle] = added(kept[slot, far_middle], second_in[slot, far_middle])
            split_copy(chunk).start()
            kept[slot, low_middle] = added(kept[slot, low_middle], second_in[slot, low_middle])

        branch(chunk, by_x, lambda: by_place(lambda: pair_copy(chunk).wait_send(), at_middle))

    def after_third(chunk):
        slot = chunk % SLOTS

        def one_at_middle():
            single_copy(chunk).wait_recv()
            kept[slot, 0] = added(kept[slot, 0], third_in[slot, 0])
            middle_copy(chunk).start()

        def by_y():
            split_copy(chunk).wait()
            kept[slot, low_middle] = added(kept[slot, low_middle], third_in[slot, 0])
            across_copy(chunk).start()

        branch(
            chunk,
            lambda: by_place(lambda: single_copy(chunk).wait_send(), one_at_middle),
            lambda: on_middle(by_y),
        )

    def after_fourth(chunk):
        slot, result_slot = chunk % SLOTS, chunk % RESULT_SLOTS

        def by_x():
            middle_copy(chunk).wait()
            result[result_slot, x_rows, :] = added(kept[slot, 0], third_in[slot, 1])
            result_copy(5, chunk, x_rows, z_partner).start()

        def by_y():
            across_copy(chunk).wait()
            result[result_slot, middle_rows(), :] = added(
                kept[slot, low_middle], third_in[slot, 1]
            )
            result_copy(5, chunk, middle_rows(), middle_partner).start()

        branch(chunk, lambda: on_middle(by_x), lambda: on_middle(by_y))

    def after_fifth(chunk):
        def by_x():
            back = result_copy(5, chunk, x_rows, z_partner)
            by_place(back.wait_recv, back.wait_send)
            result_copy(6, chunk, x_rows, x_partner).start()

        def by_y():
            result_copy(5, chunk, middle_rows(), middle_partner).wait()
            result_copy(6, chunk, core_rows, z_partner).start()

        branch(chunk, by_x, lambda: on_middle(by_y))

    def after_sixth(chunk):
        def by_y():
            back = result_copy(6, chunk, core_rows, z_partner)
            by_place(back.wait_recv, back.wait_send)

        branch(chunk, lambda: result_copy(6, chunk, x_rows, x_partner).wait(), by_y)
        result_copy(7, chunk, core_rows, core_partner).start()

    def after_whole(chunk):
        result_copy(7, chunk, core_rows, core_partner).wait()

        def action(member, layer, i, j):
            if member == 3:
                target = out_qkv.at[layer, j, block_of(i)]
            else:
                target = out_refs[member].at[layer, block_of(i), block_of(j)]
            store_copy(chunk, target).start()

        for_matrix(chunk, action)

    def after_store(chunk):
        store_copy(chunk, result.at[chunk % RESULT_SLOTS]).wait()

    vector_partners = (core_partner, y_partner, x_partner, z_partner, middle_partner, z_partner)

    def vector_copy(step):
        target = vec_in.at[min(step, 4)]
        return pltpu.make_async_remote_copy(
            src_ref=vector_out,
            dst_ref=target,
            send_sem=vec_send.at[step],
            recv_sem=vec_recv.at[step],
            device_id=vector_partners[step],
            device_id_type=MESH,
        )

    def add_vector(step):
        vector_out[...] = vector_out[...] + vec_in[step]

    def vector_tick(step):
        if step == 0:
            vector_copy(0).start()
        elif step <= 3:
            vector_copy(step - 1).wait()
            add_vector(step - 1)
            if step < 3:
                vector_copy(step).start()
            else:

                @pl.when(inner == 0)
                def _():
                    vector_copy(3).start()

        elif step == 4:

            @pl.when(inner == 0)
            def _():
                vector_copy(3).wait_send()

            @pl.when(inner == 1)
            def _():
                vector_copy(3).wait_recv()
                add_vector(3)
                vector_copy(4).start()

        elif step == 5:

            @pl.when(inner == 1)
            def _():
                vector_copy(4).wait()
                add_vector(4)
                vector_copy(5).start()

        else:

            @pl.when(inner == 1)
            def _():
                vector_copy(5).wait_send()

            @pl.when(inner == 0)
            def _():
                vector_copy(5).wait_recv()
                vector_out[...] = vec_in[4]

    norm_two_step = FFN_STEPS
    out_step = norm_two_step + 1
    attention_step = out_step + 1
    qkv_step = attention_step + pairs + 1
    norm_one_step = qkv_step + QKV_STEPS
    period = norm_one_step + 1
    jobs = layers * period
    hidden_step = 2 * hidden_half // FFN_STEPS

    def loads(kind, slot, *sources):
        targets = {
            "ffn": (rows_weight.at[slot], columns_weight.at[slot], slope_buf.at[slot]),
            "wide": (wide_buf,),
            "out": (rows_weight.at[slot, pl.ds(0, block)], rows_weight.at[slot, pl.ds(block, block)]),
            "attention": (
                qkv_buf.at[slot, 0],
                qkv_buf.at[slot, 1],
                qkv_buf.at[slot, 2],
                halo_buf.at[slot, 0],
                halo_buf.at[slot, 1],
                totals_buf.at[slot],
            ),
            "qkv": (
                columns_weight.at[slot, :, pl.ds(0, block)],
                columns_weight.at[slot, :, pl.ds(block, block)],
            ),
        }[kind]
        sources = sources or targets
        return [
            pltpu.make_async_copy(source, target, load_sem.at[slot, index])
            for index, (source, target) in enumerate(zip(sources, targets))
        ]

    def prefetch(t):
        slot = t % 2
        layer = layers - 1 - t // period
        step = t % period

        for which, (up_ref, down_ref) in enumerate(((up_own, down_own), (up_other, down_other))):

            @pl.when((step < FFN_STEPS) & (step // (FFN_STEPS // 2) == which))
            def _(which=which, up_ref=up_ref, down_ref=down_ref):
                cut = aligned(step % (FFN_STEPS // 2), hidden_step)
                for copy in loads(
                    "ffn",
                    slot,
                    down_ref.at[layer, cut, :],
                    up_ref.at[layer, :, cut],
                    slope_ref.at[layer, which, :, cut],
                ):
                    copy.start()

        for at, source in ((norm_two_step, middle_ref), (norm_one_step, resid_ref)):

            @pl.when(step == at)
            def _(source=source):
                for copy in loads("wide", slot, source.at[layer]):
                    copy.start()

        @pl.when(step == out_step)
        def _():
            for copy in loads("out", slot, out_own.at[layer], out_other.at[layer]):
                copy.start()

        @pl.when((step >= attention_step) & (step < attention_step + pairs))
        def _():
            pair = step - attention_step
            which, inside = pair // pairs_half, pair % pairs_half

            def lanes(third):
                return aligned(third * pairs_half + inside, LANES)

            for copy in loads(
                "attention",
                slot,
                *[proj_ref.at[layer, which, :, lanes(third)] for third in range(3)],
                *[halo_ref.at[layer, which, third, :, lanes(0)] for third in range(2)],
                totals_ref.at[layer, which],
            ):
                copy.start()

        @pl.when((step >= qkv_step) & (step < qkv_step + QKV_STEPS))
        def _():
            for part in range(2):
                index = 2 * (step - qkv_step) + part
                for which, source in enumerate((qkv_own, qkv_other)):

                    @pl.when(index // 3 == which)
                    def _(part=part, index=index, source=source):
                        pltpu.make_async_copy(
                            source.at[layer, index % 3],
                            columns_weight.at[slot, :, pl.ds(part * block, block)],
                            load_sem.at[slot, part],
                        ).start()

    def wait_loads(kind, slot):
        for copy in loads(kind, slot):
            copy.wait()

    tiles = [slice(r, r + BAND) for r in range(0, rows_all, BAND)]
    fine_tiles = [slice(r, r + LANES) for r in range(0, rows_all, LANES)]

    def vector_row(layer, row):
        return pl.ds(layer * VECTOR_ROWS + row, 1)

    def column_sum(values):
        return jnp.sum(values.astype(jnp.float32), axis=0, keepdims=True)

    def ffn_job(layer, step, slot):
        wait_loads("ffn", slot)
        sums = 0.0
        for tile in tiles:
            grad_hidden = dot_nt(grad_branch[tile, :], rows_weight[slot])
            before = (grad_hidden * slope_buf[slot, tile, :].astype(jnp.float32)).astype(low)
            grad_before[step, tile, :] = before
            sums = sums + column_sum(before)
            product = dot_nt(before, columns_weight[slot])

            @pl.when(step == 0)
            def _(tile=tile, product=product):
                collected[tile, :] = product

            @pl.when(step > 0)
            def _(tile=tile, product=product):
                collected[tile, :] = collected[tile, :] + product

        per_half = FFN_STEPS // 2
        which = step // per_half
        owner = which + y - 2 * which * y
        vector_out[vector_row(layer, 2 + owner * per_half + step % per_half), :] = sums

    def norm_job(layer, index, slot):
        wait_loads("wide", slot)
        gain = gain_ref[layer, pl.ds(index, 1), :]
        gain_sum, shift_sum, attn_sum, branch_sum = 0.0, 0.0, 0.0, 0.0
        for tile in fine_tiles:
            incoming = collected[tile, :]
            values = wide_buf[tile, :]
            average = jnp.mean(values, axis=-1, keepdims=True)
            centred = values - average
            inverse = lax.rsqrt(jnp.mean(centred * centred, axis=-1, keepdims=True) + epsilon)
            unit = centred * inverse
            scaled = incoming * gain
            first_mean = jnp.mean(scaled, axis=-1, keepdims=True)
            second_mean = jnp.mean(scaled * unit, axis=-1, keepdims=True)
            total = grad_res[tile, :] + inverse * (scaled - first_mean - unit * second_mean)
            grad_res[tile, :] = total
            rounded = total.astype(low)
            gain_sum = gain_sum + column_sum(incoming * unit)
            shift_sum = shift_sum + column_sum(incoming)
            if index == 1:
                attn_sum = attn_sum + column_sum(rounded)
                branch_sum = branch_sum + column_sum(grad_branch[tile, :])
                grad_attn[tile, :] = rounded
            else:
                grad_branch[tile, :] = rounded
        vector_out[vector_row(layer, 8 + index), :] = gain_sum
        vector_out[vector_row(layer, 10 + index), :] = shift_sum
        if index == 1:
            vector_out[vector_row(layer, 6), :] = attn_sum
            vector_out[vector_row(layer, 7), :] = branch_sum

    def out_job(slot):
        wait_loads("out", slot)
        for tile in tiles:
            grad_attended[tile, :] = dot_nt(grad_attn[tile, :], rows_weight[slot]).astype(low)

    def halo_copy(pair):
        return pltpu.make_async_remote_copy(
            src_ref=halo_send.at[pair % 2],
            dst_ref=halo_in.at[pair],
            send_sem=halo_send_sem.at[pair],
            recv_sem=halo_recv_sem.at[pair],
            device_id=core_partner,
            device_id_type=MESH,
        )

    def proj_lanes(pair, third):
        which, inside = pair // pairs_half, pair % pairs_half
        return aligned(which * 3 * pairs_half + third * pairs_half + inside, LANES)

    def attention_job(pair, slot):
        wait_loads("attention", slot)
        lane = lax.broadcasted_iota(jnp.int32, (BAND, LANES), 1)
        scaling = HEAD_DIM ** (-0.5)
        count = len(tiles)
        key_parts = [None] * (count + 1)
        value_parts = [None] * (count + 1)
        here = aligned(pair, LANES)
        for index, tile in enumerate(tiles):
            query = qkv_buf[slot, 0, tile, :]
            grad = grad_attended[tile, here]
            keys = band_rows(halo_buf[slot, 0], qkv_buf[slot, 1], index)
            values = band_rows(halo_buf[slot, 1], qkv_buf[slot, 2], index)
            grad_query = []
            grad_keys = 0.0
            grad_values = 0.0
            for head in range(2):
                mine = (lane // HEAD_DIM) == head
                query_head = jnp.where(mine, query, 0)
                grad_head = jnp.where(mine, grad, 0)
                scores = dot_nt(query_head, keys) * scaling + bias_buf[index]
                total = jnp.sum(
                    jnp.where(
                        lane == 2 * (pair % pairs_half) + head, totals_buf[slot, tile, :], 0.0
                    ),
                    axis=-1,
                    keepdims=True,
                )
                exact = jnp.exp(scores - total)
                grad_probs = dot_nt(grad_head, values)
                row_terms = jnp.sum(exact * grad_probs, axis=-1, keepdims=True)
                grad_scores = (exact * (grad_probs - row_terms)).astype(low)
                grad_query.append(jnp.dot(grad_scores, keys, preferred_element_type=jnp.float32))
                grad_keys = grad_keys + dot_tn(grad_scores, query_head)
                grad_values = grad_values + dot_tn(exact.astype(low), grad_head)
            grad_proj[tile, proj_lanes(pair, 0)] = (
                jnp.where(lane < HEAD_DIM, grad_query[0], grad_query[1]) * scaling
            ).astype(low)
            grad_keys = grad_keys * scaling
            for part in range(2):
                cut = slice(part * BAND, (part + 1) * BAND)
                old_k, old_v = key_parts[index + part], value_parts[index + part]
                key_parts[index + part] = grad_keys[cut] if old_k is None else old_k + grad_keys[cut]
                value_parts[index + part] = (
                    grad_values[cut] if old_v is None else old_v + grad_values[cut]
                )
        for index in range(count - 1):
            grad_proj[tiles[index], proj_lanes(pair, 1)] = key_parts[index + 1].astype(low)
            grad_proj[tiles[index], proj_lanes(pair, 2)] = value_parts[index + 1].astype(low)
        kept_kv[pair % 2, 0] = key_parts[count]
        kept_kv[pair % 2, 1] = value_parts[count]

        @pl.when(core == 1)
        def _():
            halo_send[pair % 2, 0] = key_parts[0].astype(low)
            halo_send[pair % 2, 1] = value_parts[0].astype(low)
            halo_copy(pair).start()

    def finish_pair(pair):
        last = tiles[-1]

        @pl.when(core == 0)
        def _():
            halo_copy(pair).wait_recv()
            for third in range(2):
                grad_proj[last, proj_lanes(pair, third + 1)] = (
                    kept_kv[pair % 2, third] + halo_in[pair, third].astype(jnp.float32)
                ).astype(low)

        @pl.when(core == 1)
        def _():
            halo_copy(pair).wait_send()
            for third in range(2):
                grad_proj[last, proj_lanes(pair, third + 1)] = kept_kv[pair % 2, third].astype(low)

    def qkv_job(layer, step, slot):
        wait_loads("qkv", slot)
        sums = 0.0
        for tile in tiles:
            grad = grad_proj[tile, aligned(step, width)]
            sums = sums + column_sum(grad)
            product = dot_nt(grad, columns_weight[slot])

            @pl.when(step == 0)
            def _(tile=tile, product=product):
                collected[tile, :] = product

            @pl.when(step > 0)
            def _(tile=tile, product=product):
                collected[tile, :] = collected[tile, :] + product

        sums_buf[...] = sums
        for when, part, which, row in ((0, 0, 0, 0), (1, 0, 0, 1), (1, 1, 1, 0), (2, 1, 1, 1)):

            @pl.when(step == when)
            def _(part=part, which=which, row=row):
                owner = 1 - y if which else y
                vector_out[vector_row(layer, row), block_of(owner)] = sums_buf[
                    :, part * block : (part + 1) * block
                ]

    def job(t):
        slot = t % 2
        layer = layers - 1 - t // period
        step = t % period

        @pl.when(step < FFN_STEPS)
        def _():
            ffn_job(layer, step, slot)

        @pl.when(step == norm_two_step)
        def _():
            norm_job(layer, 1, slot)

        @pl.when(step == out_step)
        def _():
            out_job(slot)

        @pl.when((step > attention_step) & (step <= attention_step + pairs))
        def _():
            finish_pair(step - attention_step - 1)

        @pl.when((step >= attention_step) & (step < attention_step + pairs))
        def _():
            attention_job(step - attention_step, slot)

        @pl.when((step >= qkv_step) & (step < qkv_step + QKV_STEPS))
        def _():
            qkv_job(layer, step - qkv_step, slot)

        @pl.when(step == norm_one_step)
        def _():
            norm_job(layer, 0, slot)

    stages = (
        (LAGS["core"], after_core),
        (0, multiply),
        (None, job),
        (LAGS["first"], after_first),
        (LAGS["second"], after_second),
        (LAGS["third"], after_third),
        (LAGS["fourth"], after_fourth),
        (LAGS["fifth"], after_fifth),
        (LAGS["sixth"], after_sixth),
        (LAGS["stored"], after_store),
        (LAGS["whole"], after_whole),
    )

    swaps = core + y - 2 * core * y

    def swap_copy(index, source, target):
        return pltpu.make_async_remote_copy(
            src_ref=source,
            dst_ref=target,
            send_sem=swap_send.at[index],
            recv_sem=swap_recv.at[index],
            device_id=swap_partner,
            device_id_type=MESH,
        )

    def swap_start(index, source, target):
        @pl.when(swaps == 1)
        def _():
            swap_copy(index, source, target).start()

        if index:

            @pl.when(swaps == 0)
            def _():
                pltpu.make_async_copy(source, target, io_sem.at[1]).start()

    def swap_wait(index, source, target):
        @pl.when(swaps == 1)
        def _():
            swap_copy(index, source, target).wait()

        if index:

            @pl.when(swaps == 0)
            def _():
                pltpu.make_async_copy(source, target, io_sem.at[1]).wait()

    first_load = pltpu.make_async_copy(cot_ref, grad_branch, io_sem.at[0])
    first_load.start()
    prefetch(0)
    first_load.wait()
    stage_operands(0)
    vector_ticks = [jobs + VECTOR_STEP * step for step in range(7)]

    def tick(t, carry):
        @pl.when(t == 1)
        def _():
            fill_band_bias(segk_ref, bias_buf)
            for tile in tiles:
                grad_res[tile, :] = grad_branch[tile, :].astype(jnp.float32)

        @pl.when(t + 1 < jobs)
        def _():
            prefetch(t + 1)

        ahead = t + 1 - FIRST

        @pl.when((ahead > 0) & (ahead < chunks))
        def _():
            stage_operands(ahead)

        for lag, action in stages:
            if lag is None:

                @pl.when(t < jobs)
                def _():
                    job(t)

                continue
            chunk = t - FIRST - lag

            @pl.when((chunk >= 0) & (chunk < chunks))
            def _(chunk=chunk, action=action):
                action(chunk)

        @pl.when(t == chunks + FIRST + LAGS["second"] - 1)
        def _():
            swap_start(0, out_act_ref, out_act_out)
            swap_start(1, grad_branch, grad_in_ref)

        for step, when in enumerate(vector_ticks):

            @pl.when(t == when)
            def _(step=step):
                vector_tick(step)

        return carry

    lax.fori_loop(0, max(chunks + FIRST + LAGS["stored"], vector_ticks[-1] + 1), tick, 0)
    swap_wait(0, out_act_ref, out_act_out)
    swap_wait(1, grad_branch, grad_in_ref)


def run_backward(cotangent, gain, segk, out_act, saved, weights, block):
    rows, width = cotangent.shape
    layers, hidden_half = weights[-1].shape[0], weights[-1].shape[1]
    half, quarter = block // 2, block // 4
    low, wide = jnp.bfloat16, jnp.float32
    pairs = width // LANES
    anywhere = pl.BlockSpec(memory_space=pl.ANY)
    in_vmem = pl.BlockSpec(memory_space=pltpu.VMEM)
    vector = (layers * VECTOR_ROWS, width)
    hidden_step = 2 * hidden_half // FFN_STEPS
    vmem = pltpu.VMEM
    return pl.pallas_call(
        functools.partial(backward_kernel, layers, block, hidden_half),
        in_specs=[anywhere] + [in_vmem] * 2 + [anywhere] * (1 + len(saved) + len(weights)),
        out_specs=[anywhere] * 6 + [in_vmem],
        out_shape=[
            jax.ShapeDtypeStruct((rows, width), low),
            jax.ShapeDtypeStruct((rows, width), low),
            jax.ShapeDtypeStruct((layers, hidden_half, width), low),
            jax.ShapeDtypeStruct((layers, width, hidden_half), low),
            jax.ShapeDtypeStruct((layers, block, width), low),
            jax.ShapeDtypeStruct((layers, 3, width, block), low),
            jax.ShapeDtypeStruct(vector, wide),
        ],
        scratch_shapes=[
            vmem((rows, width), low),
            vmem((rows, width), low),
            vmem((FFN_STEPS, rows, hidden_step), low),
            vmem((rows, 6 * block), low),
            vmem((rows, width), wide),
            vmem((rows, width), wide),
            vmem((rows, width), low),
            vmem((2, 3, rows, LANES), low),
            vmem((2, 2, BAND, LANES), low),
            vmem((2, rows, LANES), wide),
            vmem((2, 2, BAND, LANES), wide),
            vmem((2, 2, BAND, LANES), low),
            vmem((pairs, 2, BAND, LANES), low),
            vmem((2, hidden_step, width), low),
            vmem((2, width, hidden_step), low),
            vmem((2, rows, hidden_step), low),
            vmem((rows, width), wide),
            vmem((rows // BAND, BAND, 2 * BAND), wide),
            vmem((1, width), wide),
            vmem((STAGED, 2, rows, block), low),
            vmem((STAGED, rows, block), low),
            vmem((STAGED, 2, block, block), low),
            vmem((CORE_SLOTS, 2, half, block), low),
            vmem((SLOTS, 2, quarter, block), low),
            vmem((SLOTS, 2, quarter, block), low),
            vmem((SLOTS, 2, quarter, block), low),
            vmem((SLOTS, 2, quarter, block), low),
            vmem((SLOTS, 2, quarter, block), low),
            vmem((SLOTS, 2, quarter, block), low),
            vmem((RESULT_SLOTS, block, block), low),
            vmem((5,) + vector, wide),
            pltpu.SemaphoreType.DMA((2, 6)),
            pltpu.SemaphoreType.DMA((2,)),
            pltpu.SemaphoreType.DMA((pairs,)),
            pltpu.SemaphoreType.DMA((pairs,)),
            pltpu.SemaphoreType.DMA((STAGED, 3)),
            pltpu.SemaphoreType.DMA((8, SLOTS)),
            pltpu.SemaphoreType.DMA((8, SLOTS)),
            pltpu.SemaphoreType.DMA((RESULT_SLOTS,)),
            pltpu.SemaphoreType.DMA((6,)),
            pltpu.SemaphoreType.DMA((6,)),
            pltpu.SemaphoreType.DMA((2,)),
            pltpu.SemaphoreType.DMA((2,)),
        ],
        compiler_params=pltpu.CompilerParams(
            collective_id=0, has_side_effects=True, vmem_limit_bytes=VMEM_ASKED
        ),
        name="backward",
    )(cotangent, gain, segk, out_act, *saved, *weights)


FINISH_DEPTH = 4


def finish_kernel(layers, steps, *refs):
    count = len(steps)
    ins, refs = refs[:count], refs[count:]
    vector_ref, refs = refs[0], refs[1:]
    (act_own, act_swapped, grad_in_ref), refs = refs[:3], refs[3:]
    outs, refs = refs[:count], refs[count:]
    qv_out, up_out, bias_out, gain_out, shift_out = refs[:5]
    (act_out, grad_in_out), refs = refs[5:7], refs[7:]
    in_bufs, refs = refs[:count], refs[count:]
    out_bufs, (moved_buf, in_sem, out_sem, copy_sem) = refs[:count], refs[count:]
    y = lax.axis_index("tensor")
    core = lax.axis_index("dp") % 2

    def fetch(index, source):
        return pltpu.make_async_copy(source, moved_buf.at[index], copy_sem.at[index])

    def put(index, target):
        return pltpu.make_async_copy(moved_buf.at[index], target, copy_sem.at[index])

    @pl.when(core == y)
    def _():
        fetch(0, act_own).start()

    @pl.when(core != y)
    def _():
        fetch(0, act_swapped).start()

    fetch(1, grad_in_ref).start()
    plan = []
    for member, (rows, parts) in enumerate(steps):
        for layer in range(layers):
            for part in range(parts):
                plan.append((member, layer, part * rows, rows, (layer * parts + part) % FINISH_DEPTH))

    def view(ref, layer, begin, rows):
        if len(ref.shape) == 4:
            return ref.at[layer, begin // rows]
        return ref.at[layer, pl.ds(begin, rows)]

    def load(entry):
        member, layer, begin, rows, slot = entry
        return pltpu.make_async_copy(
            view(ins[member], layer, begin, rows), in_bufs[member].at[slot], in_sem.at[member, slot]
        )

    def save(entry):
        member, layer, begin, rows, slot = entry
        return pltpu.make_async_copy(
            out_bufs[member].at[slot], view(outs[member], layer, begin, rows), out_sem.at[member, slot]
        )

    for entry in plan[:FINISH_DEPTH]:
        load(entry).start()
    half = qv_out.shape[2]
    for layer in range(layers):
        base = layer * VECTOR_ROWS
        for index in range(2):
            mine = pl.ds(pl.multiple_of(y * half, half), half)
            qv_out[layer, pl.ds(index, 1), :] = vector_ref[pl.ds(base + index, 1), mine]
            width = vector_ref.shape[1]
            up_out[pl.ds(layer, 1), index * width : (index + 1) * width] = vector_ref[
                pl.ds(base + 2 + 2 * y + index, 1), :
            ]
            for row, target in ((6, bias_out), (8, gain_out), (10, shift_out)):
                target[layer, pl.ds(index, 1), :] = vector_ref[pl.ds(base + row + index, 1), :]
    for index, target in enumerate((act_out, grad_in_out)):
        fetch(index, target).wait()
        put(index, target).start()
    busy = {}
    for place, entry in enumerate(plan):
        member, slot = entry[0], entry[4]
        load(entry).wait()
        if (member, slot) in busy:
            save(busy.pop((member, slot))).wait()
        out_bufs[member][slot] = in_bufs[member][slot].astype(jnp.float32)
        save(entry).start()
        busy[(member, slot)] = entry
        if place + FINISH_DEPTH < len(plan):
            load(plan[place + FINISH_DEPTH]).start()
    for entry in busy.values():
        save(entry).wait()
    for index, target in enumerate((act_out, grad_in_out)):
        put(index, target).wait()


def run_finish(reduced, vector, acts, grad_in, block):
    layers, width = reduced[0].shape[0], vector.shape[1]
    hidden_half = reduced[0].shape[1]
    wide, low = jnp.float32, jnp.bfloat16
    shape = jax.ShapeDtypeStruct
    anywhere = pl.BlockSpec(memory_space=pl.ANY)
    in_vmem = pl.BlockSpec(memory_space=pltpu.VMEM)
    steps = (
        (block, hidden_half // block),
        (block // 2, width * 2 // block),
        (block, 1),
        (width, 3),
    )
    blocks = ((block, width), (block // 2, hidden_half), (block, width), (width, block))
    deep = lambda kind: [pltpu.VMEM((FINISH_DEPTH,) + size, kind) for size in blocks]
    return pl.pallas_call(
        functools.partial(finish_kernel, layers, steps),
        in_specs=[anywhere] * len(reduced) + [in_vmem] + [anywhere] * 3,
        out_specs=[anywhere] * len(reduced) + [in_vmem] * 5 + [anywhere] * 2,
        out_shape=[shape(member.shape, wide) for member in reduced]
        + [
            shape((layers, 2, block), wide),
            shape((layers, hidden_half), wide),
            shape((layers, 2, width), wide),
            shape((layers, 2, width), wide),
            shape((layers, 2, width), wide),
        ]
        + [shape(grad_in.shape, low)] * 2,
        scratch_shapes=deep(low)
        + deep(wide)
        + [
            pltpu.VMEM((2,) + grad_in.shape, low),
            pltpu.SemaphoreType.DMA((4, FINISH_DEPTH)),
            pltpu.SemaphoreType.DMA((4, FINISH_DEPTH)),
            pltpu.SemaphoreType.DMA((2,)),
        ],
        compiler_params=pltpu.CompilerParams(vmem_limit_bytes=VMEM_ASKED),
        name="finish",
    )(*reduced, vector, *acts, grad_in)


def local_split(
    tokens_in,
    segments,
    w_qkv,
    qv_bias,
    w_out,
    w_up,
    up_bias,
    w_down,
    out_bias,
    ln_gain,
    ln_bias,
    cotangent,
):
    block = w_qkv.shape[3]
    weights = (w_qkv.transpose(0, 2, 1, 3), w_out, w_up, w_down)
    act_own, cot, segk, *rest = run_forward(
        tokens_in,
        cotangent,
        segments,
        weights,
        (qv_bias, up_bias),
        out_bias,
        ln_gain,
        ln_bias,
        block,
    )
    others, saved = rest[: len(weights)], rest[len(weights) :]
    both = [member for pair in zip(weights, others) for member in pair]
    act_swapped, grad_in, *reduced, summed = run_backward(
        cot, ln_gain, segk, act_own, saved, both, block
    )
    *grads, grad_qv, grad_up_bias, grad_bias, grad_gain, grad_shift, out_act, grad_in = run_finish(
        reduced, summed, (act_own, act_swapped), grad_in, block
    )
    grad_down, grad_up, grad_out, grad_qkv = grads
    return (
        out_act,
        grad_in,
        grad_qkv.transpose(0, 2, 1, 3),
        grad_qv,
        grad_out,
        grad_up,
        grad_up_bias,
        grad_down,
        grad_bias,
        grad_gain,
        grad_shift,
    )


def solution(mesh):
    sizes = (mesh.shape["dp"], mesh.shape["tensor"])
    local = local_split if sizes == (16, 2) else local_general
    return jax.shard_map(
        local,
        mesh=mesh,
        in_specs=(
            P(("dp", "tensor"), None),
            P("dp", None),
            P(None, None, None, "tensor"),
            P(None, None, "tensor"),
            P(None, "tensor", None),
            P(None, None, "tensor"),
            P(None, "tensor"),
            P(None, "tensor", None),
            P(),
            P(),
            P(),
            P(("dp", "tensor"), None),
        ),
        out_specs=(
            P(("dp", "tensor"), None),
            P(("dp", "tensor"), None),
            P(None, None, None, "tensor"),
            P(None, None, "tensor"),
            P(None, "tensor", None),
            P(None, None, "tensor"),
            P(None, "tensor"),
            P(None, "tensor", None),
            P(),
            P(),
            P(),
        ),
        check_vma=False,
    )
```

```python
import functools

import jax
import jax.numpy as jnp
from jax import lax
from jax.experimental import pallas as pl
from jax.experimental.pallas import tpu as pltpu
from jax.sharding import PartitionSpec as P

HEAD_DIM = 64


epsilon = 1e-05
gelu_coeff = 0.7978845608028654
cubic_coeff = 0.044715
masked_score = -1e30


def as_sent(shard):

    def short(part):
        return part.astype(jnp.bfloat16) if part.dtype == jnp.float32 else part

    return jax.tree.map(short, shard)


def layer_norm(values, gain, shift):
    average = jnp.mean(values, axis=-1, keepdims=True)
    centred = values - average
    inverse = lax.rsqrt(jnp.mean(centred * centred, axis=-1, keepdims=True) + epsilon)
    unit_rows = centred * inverse
    return (unit_rows * gain + shift, unit_rows, inverse)


def norm_backward(incoming, unit_rows, inverse, gain):
    scaled = incoming * gain
    first_mean = jnp.mean(scaled, axis=-1, keepdims=True)
    second_mean = jnp.mean(scaled * unit_rows, axis=-1, keepdims=True)
    through = inverse * (scaled - first_mean - unit_rows * second_mean)
    return (through, jnp.sum(incoming * unit_rows, axis=0), jnp.sum(incoming, axis=0))


def gelu_tanh(before):
    tanh_input = gelu_coeff * (before + cubic_coeff * before * before * before)
    return 0.5 * before * (1.0 + jnp.tanh(tanh_input))


def gelu_slope(before):
    tanh_input = gelu_coeff * (before + cubic_coeff * before * before * before)
    tangent = jnp.tanh(tanh_input)
    return 0.5 * (1.0 + tangent) + 0.5 * before * (1.0 - tangent * tangent) * gelu_coeff * (
        1.0 + 3.0 * cubic_coeff * before * before
    )


def masked_scores(query_block, key_seq, segment_row, offset, block_rows):
    window = key_seq.shape[0]
    scores = jnp.einsum(
        "qhe,khe->hqk", query_block, key_seq, preferred_element_type=jnp.float32
    ) * HEAD_DIM ** (-0.5)
    query_place = offset + lax.iota(jnp.int32, block_rows)
    key_place = lax.iota(jnp.int32, window)
    query_segment = segment_row[offset : offset + block_rows]
    allowed = (query_place[:, None] >= key_place[None, :]) & (
        query_segment[:, None] == segment_row[None, :]
    )
    return jnp.where(allowed[None], scores, masked_score)


def split_heads(flat_rows, seq_count):
    return flat_rows.reshape(
        seq_count, flat_rows.shape[0] // seq_count, flat_rows.shape[1] // HEAD_DIM, HEAD_DIM
    )


def attend_forward(query_rows, key_rows, value_rows, segments):
    seq_count, window = segments.shape
    block_rows = min(512, window)

    def one_sequence(member):
        query_seq, key_seq, value_seq, segment_row = member
        outputs = []
        totals = []
        for block_index in range(window // block_rows):
            offset = block_index * block_rows
            scores = masked_scores(
                query_seq[offset : offset + block_rows], key_seq, segment_row, offset, block_rows
            )
            highest = jnp.max(scores, axis=-1, keepdims=True)
            raised = jnp.exp(scores - highest)
            summed = jnp.sum(raised, axis=-1, keepdims=True)
            softmax_low = (raised / summed).astype(jnp.bfloat16)
            block_out = jnp.einsum(
                "hqk,khe->qhe", softmax_low, value_seq, preferred_element_type=jnp.float32
            )
            outputs.append(block_out.astype(jnp.bfloat16))
            totals.append(highest[..., 0] + jnp.log(summed[..., 0]))
        return (jnp.concatenate(outputs, axis=0), jnp.stack(totals, axis=0))

    attended, log_totals = lax.map(
        one_sequence,
        (
            split_heads(query_rows, seq_count),
            split_heads(key_rows, seq_count),
            split_heads(value_rows, seq_count),
            segments,
        ),
    )
    return (attended.reshape(query_rows.shape), log_totals)


def attend_backward(query_rows, key_rows, value_rows, segments, log_totals, grad_attended):
    seq_count, window = segments.shape
    block_rows = min(512, window)
    scaling = HEAD_DIM ** (-0.5)

    def one_sequence(member):
        query_seq, key_seq, value_seq, segment_row, totals_seq, grad_seq = member
        query_parts = []
        grad_keys = jnp.zeros(key_seq.shape, jnp.float32)
        grad_values = jnp.zeros(value_seq.shape, jnp.float32)
        for block_index in range(window // block_rows):
            offset = block_index * block_rows
            query_block = query_seq[offset : offset + block_rows]
            grad_block = grad_seq[offset : offset + block_rows]
            scores = masked_scores(query_block, key_seq, segment_row, offset, block_rows)
            softmax_exact = jnp.exp(scores - totals_seq[block_index][..., None])
            softmax_low = softmax_exact.astype(jnp.bfloat16)
            grad_softmax = jnp.einsum(
                "qhe,khe->hqk", grad_block, value_seq, preferred_element_type=jnp.float32
            )
            row_terms = jnp.sum(softmax_exact * grad_softmax, axis=-1, keepdims=True)
            grad_scores = (softmax_exact * (grad_softmax - row_terms)).astype(jnp.bfloat16)
            query_parts.append(
                jnp.einsum("hqk,khe->qhe", grad_scores, key_seq, preferred_element_type=jnp.float32)
                * scaling
            )
            grad_keys = (
                grad_keys
                + jnp.einsum(
                    "hqk,qhe->khe", grad_scores, query_block, preferred_element_type=jnp.float32
                )
                * scaling
            )
            grad_values = grad_values + jnp.einsum(
                "hqk,qhe->khe", softmax_low, grad_block, preferred_element_type=jnp.float32
            )
        grad_query = jnp.concatenate(query_parts, axis=0)
        return (
            grad_query.astype(jnp.bfloat16),
            grad_keys.astype(jnp.bfloat16),
            grad_values.astype(jnp.bfloat16),
        )

    grad_query, grad_keys, grad_values = lax.map(
        one_sequence,
        (
            split_heads(query_rows, seq_count),
            split_heads(key_rows, seq_count),
            split_heads(value_rows, seq_count),
            segments,
            log_totals,
            split_heads(grad_attended, seq_count),
        ),
    )
    return (
        grad_query.reshape(query_rows.shape),
        grad_keys.reshape(query_rows.shape),
        grad_values.reshape(query_rows.shape),
    )


def layer_forward(residual, segments, weights):
    w_qkv, qv_bias, w_out, w_up, up_bias, w_down, out_bias, gains, shifts = weights
    row_count = residual.shape[0]
    normed, unit_one, inverse_one = layer_norm(residual, gains[0], shifts[0])
    normed_all = lax.all_gather(normed.astype(jnp.bfloat16), "tensor", axis=0, tiled=True)
    projected = jnp.einsum("td,dsc->tsc", normed_all, w_qkv, preferred_element_type=jnp.float32)
    query_rows = (projected[:, 0] + qv_bias[0]).astype(jnp.bfloat16)
    key_rows = projected[:, 1].astype(jnp.bfloat16)
    value_rows = (projected[:, 2] + qv_bias[1]).astype(jnp.bfloat16)
    attended, log_totals = attend_forward(query_rows, key_rows, value_rows, segments)
    middle = (
        residual
        + lax.psum_scatter(
            jnp.dot(
                lax.slice_in_dim(attended, 0, row_count * lax.axis_size("tensor"), axis=0),
                w_out,
                preferred_element_type=jnp.float32,
            ).astype(jnp.bfloat16),
            "tensor",
            scatter_dimension=0,
            tiled=True,
        ).astype(jnp.float32)
        + out_bias[0]
    )
    normed_two, unit_two, inverse_two = layer_norm(middle, gains[1], shifts[1])
    normed_low = normed_two.astype(jnp.bfloat16)
    ffn_rows = lax.all_gather(normed_low, "tensor", axis=0, tiled=True)
    before = jnp.dot(ffn_rows, w_up, preferred_element_type=jnp.float32) + up_bias
    activated = gelu_tanh(before).astype(jnp.bfloat16)
    ffn_branch = lax.psum_scatter(
        jnp.dot(
            lax.slice_in_dim(activated, 0, row_count * lax.axis_size("tensor"), axis=0),
            w_down,
            preferred_element_type=jnp.float32,
        ).astype(jnp.bfloat16),
        "tensor",
        scatter_dimension=0,
        tiled=True,
    ).astype(jnp.float32)
    kept_ffn = (w_up, w_down)
    result = middle + ffn_branch + out_bias[1]
    kept_state = (
        unit_one,
        inverse_one,
        normed_all,
        query_rows,
        key_rows,
        value_rows,
        attended,
        log_totals,
        unit_two,
        inverse_two,
        ffn_rows,
        before,
        activated,
        kept_ffn,
    )
    return (result, kept_state)


def layer_backward(grad_residual, segments, weights, kept_state):
    w_qkv, qv_bias, w_out, w_up, up_bias, w_down, out_bias, gains, shifts = weights
    (
        unit_one,
        inverse_one,
        normed_all,
        query_rows,
        key_rows,
        value_rows,
        attended,
        log_totals,
        unit_two,
        inverse_two,
        ffn_rows,
        before,
        activated,
        kept_ffn,
    ) = kept_state
    up_used, down_used = kept_ffn
    row_count = grad_residual.shape[0]
    grad_branch = grad_residual.astype(jnp.bfloat16)
    bias_down = jnp.sum(grad_branch, axis=0, dtype=jnp.float32)
    grad_rows = lax.all_gather(grad_branch, "tensor", axis=0, tiled=True)
    grad_hidden = jnp.einsum("td,fd->tf", grad_rows, down_used, preferred_element_type=jnp.float32)
    grad_before = (grad_hidden * gelu_slope(before)).astype(jnp.bfloat16)
    grad_down = jnp.einsum("tf,td->fd", activated, grad_rows, preferred_element_type=jnp.float32)
    grad_up = jnp.einsum("td,tf->df", ffn_rows, grad_before, preferred_element_type=jnp.float32)
    grad_up_bias = jnp.sum(grad_before, axis=0, dtype=jnp.float32)
    piece_rows = lax.slice_in_dim(grad_before, 0, row_count * lax.axis_size("tensor"), axis=0)
    grad_normed_two = lax.psum_scatter(
        jnp.einsum("tf,df->td", piece_rows, w_up, preferred_element_type=jnp.float32).astype(
            jnp.bfloat16
        ),
        "tensor",
        scatter_dimension=0,
        tiled=True,
    ).astype(jnp.float32)
    through_two, gain_two, shift_two = norm_backward(
        grad_normed_two, unit_two, inverse_two, gains[1]
    )
    grad_middle = grad_residual + through_two
    grad_attn_branch = grad_middle.astype(jnp.bfloat16)
    bias_attn = jnp.sum(grad_attn_branch, axis=0, dtype=jnp.float32)
    grad_attn_all = lax.all_gather(grad_attn_branch, "tensor", axis=0, tiled=True)
    grad_out_w = jnp.einsum(
        "tc,td->cd", attended, grad_attn_all, preferred_element_type=jnp.float32
    )
    grad_attended = jnp.einsum(
        "td,cd->tc", grad_attn_all, w_out, preferred_element_type=jnp.float32
    ).astype(jnp.bfloat16)
    grad_query, grad_keys, grad_values = attend_backward(
        query_rows, key_rows, value_rows, segments, log_totals, grad_attended
    )
    grad_projected = jnp.stack((grad_query, grad_keys, grad_values), axis=1)
    grad_qkv = jnp.einsum(
        "td,tsc->dsc", normed_all, grad_projected, preferred_element_type=jnp.float32
    )
    grad_qv_bias = jnp.stack(
        (
            jnp.sum(grad_query, axis=0, dtype=jnp.float32),
            jnp.sum(grad_values, axis=0, dtype=jnp.float32),
        )
    )
    piece_rows = lax.slice_in_dim(grad_projected, 0, row_count * lax.axis_size("tensor"), axis=0)
    grad_normed = lax.psum_scatter(
        jnp.einsum("tsc,dsc->td", piece_rows, w_qkv, preferred_element_type=jnp.float32).astype(
            jnp.bfloat16
        ),
        "tensor",
        scatter_dimension=0,
        tiled=True,
    ).astype(jnp.float32)
    through_one, gain_one, shift_one = norm_backward(grad_normed, unit_one, inverse_one, gains[0])
    grad_input = grad_middle + through_one
    spread = (grad_qkv, grad_qv_bias, grad_out_w, grad_up, grad_up_bias, grad_down)
    shared = (
        jnp.stack((bias_attn, bias_down)),
        jnp.stack((gain_one, gain_two)),
        jnp.stack((shift_one, shift_two)),
    )
    return (grad_input, spread, shared)


def local_general(
    tokens_in,
    segments,
    w_qkv,
    qv_bias,
    w_out,
    w_up,
    up_bias,
    w_down,
    out_bias,
    ln_gain,
    ln_bias,
    cotangent,
):
    layers_total = w_qkv.shape[0]
    all_params = (w_qkv, qv_bias, w_out, w_up, up_bias, w_down, out_bias, ln_gain, ln_bias)
    residual = tokens_in.astype(jnp.float32)
    kept_layers = []
    for layer_index in range(layers_total):
        weights = tuple((member_array[layer_index] for member_array in all_params))
        residual, kept_state = layer_forward(residual, segments, weights)
        kept_layers.append(kept_state)
    out_act = residual.astype(jnp.bfloat16)
    grad_residual = cotangent.astype(jnp.float32)
    spread_layers = []
    shared_layers = []
    for layer_index in reversed(range(layers_total)):
        weights = tuple((member_array[layer_index] for member_array in all_params))
        grad_residual, spread, shared = layer_backward(
            grad_residual, segments, weights, kept_layers[layer_index]
        )
        spread_layers.insert(0, spread)
        shared_layers.insert(0, shared)
    spread_stack = tuple(
        (
            jnp.stack([spread_layers[layer_index][position] for layer_index in range(layers_total)])
            for position in range(6)
        )
    )
    spread_stack = jax.tree.map(
        lambda part: part.astype(jnp.float32), lax.psum(as_sent(spread_stack), "dp")
    )
    shared_stack = tuple(
        (
            jnp.stack([shared_layers[layer_index][position] for layer_index in range(layers_total)])
            for position in range(3)
        )
    )
    shared_stack = lax.psum(shared_stack, ("dp", "tensor"))
    grad_in = grad_residual.astype(jnp.bfloat16)
    return (out_act, grad_in) + tuple(spread_stack) + tuple(shared_stack)


BAND = 256
LANES = 128
VMEM_ASKED = 60 * 2**20


def dot_nt(left, right):
    return lax.dot_general(left, right, (((1,), (1,)), ((), ())), preferred_element_type=jnp.float32)


def dot_tn(left, right):
    return lax.dot_general(left, right, (((0,), (0,)), ((), ())), preferred_element_type=jnp.float32)


def dot_low(left, right):
    return jnp.dot(left, right, preferred_element_type=jnp.float32)


UNITS_LAYER = 12
Y_AHEAD = 1
HOP_BEATS = (1, 3, 5, 6)
IDLE_STEPS = 2
LOADS_AHEAD = 2


def fill_band_bias(segk_ref, bias_ref):
    wide = segk_ref.shape[1]
    values = lax.broadcasted_iota(jnp.int32, (16, wide), 0)
    member = (values == segk_ref[...]).astype(jnp.float32).astype(jnp.bfloat16)
    for block in range(bias_ref.shape[0]):
        queries = member[:, (block + 1) * BAND : (block + 2) * BAND]
        keys = member[:, block * BAND : (block + 2) * BAND]
        row_place = lax.broadcasted_iota(jnp.int32, (BAND, 2 * BAND), 0) + BAND
        column_place = lax.broadcasted_iota(jnp.int32, (BAND, 2 * BAND), 1)
        allowed = (dot_tn(queries, keys) > 0.5) & (column_place <= row_place)
        bias_ref[block] = jnp.where(allowed, 0.0, masked_score)


def band_rows(halo, rows, block):
    if block == 0:
        return jnp.concatenate([halo, rows[0:BAND, :]], axis=0)
    return rows[(block - 1) * BAND : (block + 1) * BAND, :]


def aligned(index, size):
    return pl.ds(pl.multiple_of(index * size, size), size)


def forward_kernel(layers, block, hidden_half, *refs):
    (
        tokens_ref,
        cot_ref,
        segments_ref,
        qkv_own,
        out_own,
        up_own,
        down_own,
        qv_bias_ref,
        up_bias_ref,
        out_bias_ref,
        gain_ref,
        shift_ref,
        out_act_ref,
        cot_out,
        segk_out,
        qkv_other,
        out_other,
        up_other,
        down_other,
        act_out,
        slope_out,
        normed_two_out,
        middle_out,
        attended_out,
        proj_out,
        halo_out,
        totals_out,
        normed_out,
        resid_out,
        tokens_buf,
        segments_in,
        qv_bias_in,
        up_bias_in,
        resid,
        collected,
        normed,
        normed_two,
        proj,
        halo,
        attended,
        totals,
        act_buf,
        slope_buf,
        qkv_weight,
        out_weight,
        up_weight,
        down_weight,
        qkv_arrived,
        out_arrived,
        up_arrived,
        down_arrived,
        bias_buf,
        start_send,
        start_recv,
        swap_sem,
        relay_send,
        relay_recv,
        halo_send_sem,
        halo_recv_sem,
        load_sem,
        store_sem,
        pair_store_sem,
        unit_store_sem,
    ) = refs
    width = 2 * block
    rows_all = tokens_buf.shape[0]
    pairs_half = block // LANES
    blocks_hidden = hidden_half // block
    low = jnp.bfloat16
    place = lax.axis_index("dp")
    y = lax.axis_index("tensor")
    core = place % 2
    x = (place // 2) % 2
    z = place // 4
    z_low = z % 2
    core_partner = {"dp": place + 1 - 2 * core, "tensor": y}
    x_partner = {"dp": place + 2 - 4 * x, "tensor": y}
    y_partner = {"dp": place, "tensor": 1 - y}
    z_partner = {"dp": place + 4 - 8 * z_low, "tensor": y}
    swap_partner = {"dp": place + 1 - 2 * core, "tensor": 1 - y}
    swaps = core + y - 2 * core * y

    barrier = pltpu.get_barrier_semaphore()
    for partner in (core_partner, x_partner, y_partner, z_partner, swap_partner):
        pl.semaphore_signal(barrier, inc=1, device_id=partner, device_id_type=MESH)
    def remote(source, target, send, recv, partner):
        return pltpu.make_async_remote_copy(
            src_ref=source,
            dst_ref=target,
            send_sem=send,
            recv_sem=recv,
            device_id=partner,
            device_id_type=MESH,
        )

    def swap_copy(index, source, target):
        return remote(source, target, start_send.at[index], start_recv.at[index], swap_partner)

    def swap_start(index, source, target):
        @pl.when(swaps == 1)
        def _():
            swap_copy(index, source, target).start()

        @pl.when(swaps == 0)
        def _():
            pltpu.make_async_copy(source, tokens_buf, swap_sem.at[index]).start()

    def swap_wait(index, source, target):
        @pl.when(swaps == 1)
        def _():
            swap_copy(index, source, target).wait()

        @pl.when(swaps == 0)
        def _():
            pltpu.make_async_copy(source, tokens_buf, swap_sem.at[index]).wait()

    segments_copy = remote(
        segments_ref, segments_in, start_send.at[2], start_recv.at[2], core_partner
    )
    qv_copy = remote(qv_bias_ref, qv_bias_in, start_send.at[3], start_recv.at[3], y_partner)
    up_copy = remote(up_bias_ref, up_bias_in, start_send.at[4], start_recv.at[4], y_partner)

    units = layers * UNITS_LAYER

    def for_unit(unit, action):
        layer, inside = unit // UNITS_LAYER, unit % UNITS_LAYER

        @pl.when(inside < 3)
        def _():
            action(*[ref.at[layer, inside] for ref in (qkv_own, qkv_arrived, qkv_other)])

        @pl.when(inside == 3)
        def _():
            action(*[ref.at[layer] for ref in (out_own, out_arrived, out_other)])

        cut = aligned((inside - 4) // 2, block)

        @pl.when((inside >= 4) & (inside % 2 == 0))
        def _():
            action(*[ref.at[layer, :, cut] for ref in (up_own, up_arrived, up_other)])

        @pl.when((inside >= 4) & (inside % 2 == 1))
        def _():
            action(*[ref.at[layer, cut, :] for ref in (down_own, down_arrived, down_other)])

    def hop_copy(hop, unit, source, target):
        partner = (y_partner, x_partner, z_partner, core_partner)[hop]
        return remote(source, target, relay_send.at[hop, unit], relay_recv.at[hop, unit], partner)

    def piece_of(view, hop, short):
        rows = view.shape[0]
        if hop == 3:
            return view.at[aligned(core, rows // 2)]
        if hop == 2:
            return view.at[aligned(2 * core + z_low, rows // 4)]
        if short:
            return view.at[aligned(4 * core + 2 * z_low + x, rows // 8)]
        return view.at[aligned(2 * core + x, rows // 4)]

    def by_length(unit, hop, action):
        if hop == 3:
            action(False)
            return

        whole = (unit % 3 == 0) & (unit > 0)

        @pl.when(jnp.logical_not(whole))
        def _():
            action(True)

        if hop < 2:

            @pl.when(whole)
            def _():
                action(False)

    def hop_start(hop, unit):
        def go(own, arrived, _):
            def one(short):
                source = piece_of(own if hop == 0 else arrived, hop, short)
                hop_copy(hop, unit, source, piece_of(arrived, hop, short)).start()

            by_length(unit, hop, one)

        for_unit(unit, go)

    def hop_wait(hop, unit):
        def one(short):
            piece = piece_of(down_arrived.at[0, pl.ds(0, block), :], hop, short)
            hop_copy(hop, unit, piece, piece).wait()

        by_length(unit, hop, one)

    def when_unit(unit, action):
        @pl.when((unit >= 0) & (unit < units))
        def _():
            action(unit)

    def beat(b):
        def after_y(unit):
            hop_wait(0, unit)
            hop_start(1, unit)

        def after_x(unit):
            hop_wait(1, unit)
            hop_start(2, unit)

        def after_z(unit):
            hop_wait(2, unit)
            hop_start(3, unit)

        def after_all(unit):
            hop_wait(3, unit)

            def keep(_, arrived, other):
                pltpu.make_async_copy(arrived, other, unit_store_sem.at[unit]).start()

            for_unit(unit, keep)

        when_unit(b + Y_AHEAD, lambda unit: hop_start(0, unit))
        for lag, action in zip(HOP_BEATS, (after_y, after_x, after_z, after_all)):
            when_unit(b - lag, action)

    other_step = 2 + pairs_half + IDLE_STEPS
    out_step = other_step + 1 + pairs_half
    norm_two_step = out_step + 1
    ffn_step = norm_two_step + 1
    end_step = ffn_step + 2 * blocks_hidden
    period = end_step + 1
    jobs = layers * period

    def loads(kind, slot, *sources):
        place, targets = {
            "qkv": (blocks_hidden, (qkv_weight,)),
            "out": (blocks_hidden + 1, (out_weight,)),
            "ffn": (slot, (up_weight.at[slot], down_weight.at[slot])),
        }[kind]
        sources = sources or targets
        return [
            pltpu.make_async_copy(source, target, load_sem.at[place, index])
            for index, (source, target) in enumerate(zip(sources, targets))
        ]

    def start_all(copies):
        for copy in copies:
            copy.start()

    def wait_all(copies):
        for copy in copies:
            copy.wait()

    def prefetch(t):
        layer, step = t // period, t % period

        @pl.when(step == 1)
        def _():
            start_all(loads("qkv", 0, qkv_own.at[layer]))

        @pl.when(step == out_step)
        def _():
            start_all(loads("out", 0, out_own.at[layer]))

        @pl.when((step >= ffn_step) & (step < ffn_step + blocks_hidden))
        def _():
            inside = step - ffn_step
            cut = aligned(inside, block)
            start_all(
                loads("ffn", inside, up_own.at[layer, :, cut], down_own.at[layer, cut, :])
            )

    tiles = [slice(r, r + BAND) for r in range(0, rows_all, BAND)]
    fine_tiles = [slice(r, r + LANES) for r in range(0, rows_all, LANES)]

    def normalize(layer, index, target):
        gain = gain_ref[layer, pl.ds(index, 1), :]
        shift = shift_ref[layer, pl.ds(index, 1), :]
        for tile in fine_tiles:
            values, _, _ = layer_norm(resid[tile, :], gain, shift)
            target[tile, :] = values.astype(low)

    def store(index, source, target):
        return pltpu.make_async_copy(source, target, store_sem.at[index])

    def first_stores(layer):
        return [store(0, resid, resid_out.at[layer]), store(1, normed, normed_out.at[layer])]

    def proj_stores(layer, which):
        return [
            store(
                2 + 3 * which + third,
                proj.at[which, third],
                proj_out.at[layer, which, :, pl.ds(third * block, block)],
            )
            for third in range(3)
        ]

    def halo_store(layer, which):
        return store(8 + which, halo.at[layer, which], halo_out.at[layer, which])

    def attended_stores(layer, which):
        return [
            store(10 + which, attended.at[which], attended_out.at[layer, which]),
            store(12 + which, totals.at[which], totals_out.at[layer, which]),
        ]

    def second_stores(layer):
        return [
            store(14, resid, middle_out.at[layer]),
            store(15, normed_two, normed_two_out.at[layer]),
        ]

    def ffn_stores(layer, index, slot):
        which, inside = index // blocks_hidden, index % blocks_hidden
        cut = aligned(inside, block)
        return [
            pltpu.make_async_copy(
                buf.at[slot], out.at[layer, which, :, cut], pair_store_sem.at[slot, kind]
            )
            for kind, (buf, out) in enumerate(((act_buf, act_out), (slope_buf, slope_out)))
        ]

    def halo_copy(layer, which):
        return remote(
            proj.at[which, pl.ds(1, 2), pl.ds(rows_all - BAND, BAND)],
            halo.at[layer, which],
            halo_send_sem.at[layer, which],
            halo_recv_sem.at[layer, which],
            core_partner,
        )

    def first_job(layer):
        normalize(layer, 0, normed)
        start_all(first_stores(layer))

    def qkv_job(layer, which):
        if not which:
            wait_all(loads("qkv", 0))
        bias = qv_bias_in if which else qv_bias_ref
        for third in (1, 2, 0):
            for tile in tiles:
                weight = qkv_arrived[layer, third] if which else qkv_weight[third]
                product = dot_low(normed[tile, :], weight)
                if third != 1:
                    product = product + bias[layer, pl.ds(third // 2, 1), :]
                proj[which, third, tile, :] = product.astype(low)
            if third == 2:

                @pl.when(core == 0)
                def _():
                    halo_copy(layer, which).start()

        start_all(proj_stores(layer, which))

    def attention_job(layer, which, pair):
        @pl.when(pair == 0)
        def _():
            totals[which] = jnp.zeros_like(totals[which])

        lane = lax.broadcasted_iota(jnp.int32, (BAND, LANES), 1)
        here = aligned(pair, LANES)
        for index, tile in reversed(list(enumerate(tiles))):
            if index == 0:

                @pl.when(pair == 0)
                def _():
                    @pl.when(core == 0)
                    def _():
                        halo_copy(layer, which).wait_send()

                    @pl.when(core == 1)
                    def _():
                        halo_copy(layer, which).wait_recv()

                    halo_store(layer, which).start()

            query = proj[which, 0, tile, here]
            first = [halo[layer, which, part, :, here] if index == 0 else None for part in range(2)]
            keys = band_rows(first[0], proj[which, 1, :, here], index)
            values = band_rows(first[1], proj[which, 2, :, here], index)
            parts = []
            kept = totals[which, tile, :]
            for head in range(2):
                mine = (lane // HEAD_DIM) == head
                scores = (
                    dot_nt(jnp.where(mine, query, 0), keys) * HEAD_DIM ** (-0.5) + bias_buf[index]
                )
                highest = jnp.max(scores, axis=-1, keepdims=True)
                raised = jnp.exp(scores - highest)
                summed = jnp.sum(raised, axis=-1, keepdims=True)
                parts.append(dot_low(raised.astype(low), values) / summed)
                kept = jnp.where(lane == 2 * pair + head, highest + jnp.log(summed), kept)
            totals[which, tile, :] = kept
            attended[which, tile, here] = jnp.where(lane < HEAD_DIM, parts[0], parts[1]).astype(low)

        @pl.when(pair == pairs_half - 1)
        def _():
            start_all(attended_stores(layer, which))

    def out_job(layer):
        wait_all(loads("out", 0))
        wait_all(first_stores(layer))
        for which in range(2):
            wait_all(proj_stores(layer, which))
            halo_store(layer, which).wait()
        bias = out_bias_ref[layer, pl.ds(0, 1), :]
        for tile in tiles:
            branch = dot_low(attended[0, tile, :], out_weight[...])
            branch = branch + dot_low(attended[1, tile, :], out_arrived[layer])
            resid[tile, :] = resid[tile, :] + branch + bias

    def second_job(layer):
        normalize(layer, 1, normed_two)
        start_all(second_stores(layer))

    def ffn_job(layer, which, inside, slot):
        index = which * blocks_hidden + inside
        if not which:
            wait_all(loads("ffn", inside))

        @pl.when(index >= 2)
        def _():
            wait_all(ffn_stores(layer, index - 2, slot))

        bias = (up_bias_in if which else up_bias_ref)[pl.ds(layer, 1), aligned(inside, block)]
        cut = aligned(inside, block)
        for tile in tiles:
            up_block = up_arrived[layer, :, cut] if which else up_weight[inside]
            before = dot_low(normed_two[tile, :], up_block) + bias
            square = before * before
            tangent = jnp.tanh(gelu_coeff * before * (1.0 + cubic_coeff * square))
            raised = 0.5 * (1.0 + tangent)
            activated = (before * raised).astype(low)
            act_buf[slot, tile, :] = activated
            slope_buf[slot, tile, :] = (
                raised
                + 0.5
                * before
                * (1.0 - tangent * tangent)
                * gelu_coeff
                * (1.0 + 3.0 * cubic_coeff * square)
            ).astype(low)
            down_block = down_arrived[layer, cut, :] if which else down_weight[inside]
            product = dot_low(activated, down_block)
            if which:
                collected[tile, :] = collected[tile, :] + product
                continue

            @pl.when(inside == 0)
            def _(tile=tile, product=product):
                collected[tile, :] = product

            @pl.when(inside > 0)
            def _(tile=tile, product=product):
                collected[tile, :] = collected[tile, :] + product

        start_all(ffn_stores(layer, index, slot))

    def end_job(layer, slot):
        wait_all(ffn_stores(layer, 2 * blocks_hidden - 2, slot))
        wait_all(ffn_stores(layer, 2 * blocks_hidden - 1, 1 - slot))
        wait_all(second_stores(layer))
        for which in range(2):
            wait_all(attended_stores(layer, which))
        bias = out_bias_ref[layer, pl.ds(1, 1), :]
        for tile in tiles:
            resid[tile, :] = resid[tile, :] + collected[tile, :] + bias

    def job(t):
        slot = t % 2
        layer, step = t // period, t % period

        def at(first, count, action):
            @pl.when((step >= first) & (step < first + count))
            def _():
                action(step - first)

        at(0, 1, lambda _: first_job(layer))
        later = (layer > 0).astype(jnp.int32)
        other_at = other_step + later * (2 - other_step)
        other_first = other_step + 1 + later * (2 + pairs_half - other_step)
        at(1, 1, lambda _: qkv_job(layer, 0))
        at(2 + later, pairs_half, lambda pair: attention_job(layer, 0, pair))
        at(other_at, 1, lambda _: qkv_job(layer, 1))
        at(other_first, pairs_half, lambda pair: attention_job(layer, 1, pair))
        at(out_step, 1, lambda _: out_job(layer))
        at(norm_two_step, 1, lambda _: second_job(layer))
        at(ffn_step, blocks_hidden, lambda inside: ffn_job(layer, 0, inside, slot))
        at(ffn_step + blocks_hidden, blocks_hidden, lambda inside: ffn_job(layer, 1, inside, slot))
        at(end_step, 1, lambda _: end_job(layer, slot))

    halo[...] = jnp.zeros_like(halo)
    pl.semaphore_wait(barrier, 5)
    swap_start(0, tokens_ref, tokens_buf)
    segments_copy.start()
    qv_copy.start()
    up_copy.start()
    for unit in range(Y_AHEAD):
        hop_start(0, unit)
    segments_copy.wait()
    window = jnp.where(core == y, segments_ref[...], segments_in[...])

    @pl.when(core == 0)
    def _():
        segk_out[:, 0:BAND] = jnp.full((1, BAND), -1, jnp.int32)
        segk_out[:, BAND:] = window[:, 0:rows_all]

    @pl.when(core == 1)
    def _():
        segk_out[...] = window[:, rows_all - BAND :]

    fill_band_bias(segk_out, bias_buf)
    qv_copy.wait()
    up_copy.wait()
    swap_wait(0, tokens_ref, tokens_buf)
    for tile in tiles:
        resid[tile, :] = tokens_buf[tile, :].astype(jnp.float32)
    cot_tick = period + other_step + 4

    def past(t, begin):
        return (t - begin) * (t > begin).astype(jnp.int32)

    def beat_at(t):
        return (10 * t - 4 * past(t, 12) - past(t, 22)) // 10

    for ahead in range(LOADS_AHEAD):
        prefetch(jnp.int32(ahead))

    def tick(t, carry):
        @pl.when((t == 0) | (beat_at(t) != beat_at(t - 1)))
        def _():
            beat(beat_at(t))

        @pl.when(t == cot_tick)
        def _():
            swap_start(1, cot_ref, cot_out)

        @pl.when((t == cot_tick + 4) & (swaps == 0))
        def _():
            pltpu.make_async_copy(cot_ref, tokens_buf, swap_sem.at[1]).wait()
            pltpu.make_async_copy(tokens_buf, cot_out, swap_sem.at[1]).start()

        @pl.when(t + LOADS_AHEAD < jobs)
        def _():
            prefetch(t + LOADS_AHEAD)

        job(t)
        return carry

    lax.fori_loop(0, jobs, tick, 0)
    for tile in tiles:
        normed_two[tile, :] = resid[tile, :].astype(low)
    last_store = store(0, normed_two, out_act_ref)
    last_store.start()
    last_store.wait()
    swap_wait(1, cot_ref, cot_out)
    for unit in range(units):
        block_ref = down_arrived.at[0, pl.ds(0, block), :]
        pltpu.make_async_copy(block_ref, block_ref, unit_store_sem.at[unit]).wait()


def run_forward(tokens, cotangent, segments, weights, biases, out_bias, gain, shift, block):
    rows, width = tokens.shape
    layers, hidden_half = weights[-1].shape[0], weights[-1].shape[1]
    low, wide = jnp.bfloat16, jnp.float32
    anywhere = pl.BlockSpec(memory_space=pl.ANY)
    in_vmem = pl.BlockSpec(memory_space=pltpu.VMEM)
    vmem = pltpu.VMEM
    units = layers * UNITS_LAYER
    shape = jax.ShapeDtypeStruct
    saved = [
        shape((layers, 2, rows, hidden_half), low),
        shape((layers, 2, rows, hidden_half), low),
        shape((layers, rows, width), low),
        shape((layers, rows, width), wide),
        shape((layers, 2, rows, block), low),
        shape((layers, 2, rows, 3 * block), low),
        shape((layers, 2, 2, BAND, block), low),
        shape((layers, 2, rows, LANES), wide),
        shape((layers, rows, width), low),
        shape((layers, rows, width), wide),
    ]
    others = [shape(member.shape, low) for member in weights]
    return pl.pallas_call(
        functools.partial(forward_kernel, layers, block, hidden_half),
        in_specs=[anywhere] * 2 + [in_vmem] + [anywhere] * 4 + [in_vmem] * 5,
        out_specs=[anywhere] * 2 + [in_vmem] + [anywhere] * (len(others) + len(saved)),
        out_shape=[
            shape((rows, width), low),
            shape((rows, width), low),
            shape((1, rows + BAND), jnp.int32),
        ]
        + others
        + saved,
        scratch_shapes=[
            vmem((rows, width), low),
            vmem(segments.shape, jnp.int32),
            vmem(biases[0].shape, wide),
            vmem(biases[1].shape, wide),
            vmem((rows, width), wide),
            vmem((rows, width), wide),
            vmem((rows, width), low),
            vmem((rows, width), low),
            vmem((2, 3, rows, block), low),
            vmem((layers, 2, 2, BAND, block), low),
            vmem((2, rows, block), low),
            vmem((2, rows, LANES), wide),
            vmem((2, rows, block), low),
            vmem((2, rows, block), low),
            vmem((3, width, block), low),
            vmem((block, width), low),
            vmem((hidden_half // block, width, block), low),
            vmem((hidden_half // block, block, width), low),
        ]
        + [vmem(member.shape, low) for member in weights]
        + [
            vmem((rows // BAND, BAND, 2 * BAND), wide),
            pltpu.SemaphoreType.DMA((5,)),
            pltpu.SemaphoreType.DMA((5,)),
            pltpu.SemaphoreType.DMA((2,)),
            pltpu.SemaphoreType.DMA((4, units)),
            pltpu.SemaphoreType.DMA((4, units)),
            pltpu.SemaphoreType.DMA((layers, 2)),
            pltpu.SemaphoreType.DMA((layers, 2)),
            pltpu.SemaphoreType.DMA((hidden_half // block + 2, 2)),
            pltpu.SemaphoreType.DMA((16,)),
            pltpu.SemaphoreType.DMA((2, 2)),
            pltpu.SemaphoreType.DMA((units,)),
        ],
        compiler_params=pltpu.CompilerParams(
            collective_id=1, has_side_effects=True, vmem_limit_bytes=VMEM_ASKED
        ),
        name="forward",
    )(tokens, cotangent, segments, *weights, *biases, out_bias, gain, shift)


SLOTS = 8
CORE_SLOTS = 4
RESULT_SLOTS = 11
STAGED = 2
FIRST = 0
LAGS = dict(
    core=1, first=3, second=5, third=7, fourth=9, fifth=11, sixth=13, whole=14, stored=15
)
VECTOR_STEP = 3
VECTOR_ROWS = 12
MESH = pl.DeviceIdType.MESH
FFN_STEPS = 4
QKV_STEPS = 3


def added(left, right):
    return (left.astype(jnp.float32) + right.astype(jnp.float32)).astype(jnp.bfloat16)


def backward_kernel(layers, block, hidden_half, *refs):
    (
        cot_ref,
        gain_ref,
        segk_ref,
        out_act_ref,
        act_ref,
        slope_ref,
        normed_two_ref,
        middle_ref,
        attended_ref,
        proj_ref,
        halo_ref,
        totals_ref,
        normed_ref,
        resid_ref,
        qkv_own,
        qkv_other,
        out_own,
        out_other,
        up_own,
        up_other,
        down_own,
        down_other,
        out_act_out,
        grad_in_ref,
        out_down,
        out_up,
        out_out,
        out_qkv,
        vector_out,
        grad_branch,
        grad_attn,
        grad_before,
        grad_proj,
        grad_res,
        collected,
        grad_attended,
        qkv_buf,
        halo_buf,
        totals_buf,
        kept_kv,
        halo_send,
        halo_in,
        rows_weight,
        columns_weight,
        slope_buf,
        wide_buf,
        bias_buf,
        sums_buf,
        pair_buf,
        one_buf,
        part_buf,
        core_in,
        sent,
        held,
        kept,
        first_in,
        second_in,
        third_in,
        result,
        vec_in,
        load_sem,
        io_sem,
        halo_send_sem,
        halo_recv_sem,
        staged_sem,
        send_sems,
        recv_sems,
        store_sem,
        vec_send,
        vec_recv,
        swap_send,
        swap_recv,
    ) = refs
    half, quarter = block // 2, block // 4
    width = 2 * block
    rows_all = grad_branch.shape[0]
    pairs_half = block // LANES
    pairs = 2 * pairs_half
    low = jnp.bfloat16
    place = lax.axis_index("dp")
    y = lax.axis_index("tensor")
    core = place % 2
    x = (place // 2) % 2
    z = place // 4
    z_low = z % 2
    inner = (z + 1) // 2 % 2
    core_partner = {"dp": place + 1 - 2 * core, "tensor": y}
    x_partner = {"dp": place + 2 - 4 * x, "tensor": y}
    y_partner = {"dp": place, "tensor": 1 - y}
    z_partner = {"dp": place + 4 - 8 * z_low, "tensor": y}
    middle_partner = {"dp": place + 4 * (3 - 2 * z), "tensor": y}
    swap_partner = {"dp": place + 1 - 2 * core, "tensor": 1 - y}

    barrier = pltpu.get_barrier_semaphore()
    for partner in (core_partner, x_partner, y_partner, z_partner, swap_partner):
        pl.semaphore_signal(barrier, inc=1, device_id=partner, device_id_type=MESH)

    @pl.when(inner == 1)
    def _():
        pl.semaphore_signal(barrier, inc=1, device_id=middle_partner, device_id_type=MESH)

    blocks_hidden = hidden_half // block
    plan = (
        ("rows", blocks_hidden, 2),
        ("columns", 2, blocks_hidden),
        ("rows", 1, 2),
        ("columns", 2, 3),
    )
    starts = []
    per_layer = 0
    for _, down_count, across_count in plan:
        starts.append(per_layer)
        per_layer += down_count * across_count
    chunks = layers * per_layer
    out_refs = (out_down, out_up, out_out, out_qkv)

    def block_of(index):
        return pl.ds(pl.multiple_of(index * block, block), block)

    def for_matrix(chunk, action):
        layer = layers - 1 - chunk // per_layer
        inside = chunk % per_layer
        for member, (_, down_count, across_count) in enumerate(plan):
            begin = starts[member]

            @pl.when((inside >= begin) & (inside < begin + down_count * across_count))
            def _(member=member, begin=begin, across_count=across_count):
                local = inside - begin
                action(member, layer, local // across_count, local % across_count)

    def operands_of(member, layer, i, j):
        if member == 0:
            return (
                grad_branch.at[:, block_of(j)],
                act_ref.at[layer, 0, :, block_of(i)],
                act_ref.at[layer, 1, :, block_of(i)],
            )
        if member == 1:
            return (
                normed_two_ref.at[layer, :, block_of(i)],
                grad_before.at[j // 2, :, block_of(j % 2)],
                grad_before.at[blocks_hidden // 2 + j // 2, :, block_of(j % 2)],
            )
        if member == 2:
            return (
                grad_attn.at[:, block_of(j)],
                attended_ref.at[layer, 0, :, block_of(i)],
                attended_ref.at[layer, 1, :, block_of(i)],
            )
        return (
            normed_ref.at[layer, :, block_of(i)],
            grad_proj.at[:, block_of(j)],
            grad_proj.at[:, block_of(3 + j)],
        )

    def staged_copies(chunk, shared, own, other):
        slot = chunk % STAGED
        return (
            pltpu.make_async_copy(own, pair_buf.at[slot, 0], staged_sem.at[slot, 0]),
            pltpu.make_async_copy(other, pair_buf.at[slot, 1], staged_sem.at[slot, 1]),
            pltpu.make_async_copy(shared, one_buf.at[slot], staged_sem.at[slot, 2]),
        )

    def stage_operands(chunk):
        def action(member, layer, i, j):
            for copy in staged_copies(chunk, *operands_of(member, layer, i, j)):
                copy.start()

        for_matrix(chunk, action)

    def remote(step, chunk, source, target, partner):
        slot = chunk % SLOTS
        return pltpu.make_async_remote_copy(
            src_ref=source,
            dst_ref=target,
            send_sem=send_sems.at[step, slot],
            recv_sem=recv_sems.at[step, slot],
            device_id=partner,
            device_id_type=MESH,
        )

    def x_first(chunk):
        left = chunks - 1 - chunk
        near = (chunk <= 10) & (chunk % 2 == 0) | (left <= 10) & (left % 2 == 0)
        far = (chunk > 10) & (left > 10)
        third = far & (chunk % 3 == 1) & ((chunk < 18) | (left < 19))
        fourth = far & (chunk % 4 == 0) & (chunk >= 18) & (left >= 19)
        return near | third | fourth

    def core_copy(chunk):
        return remote(
            0,
            chunk,
            part_buf.at[chunk % STAGED, :, aligned(1 - core, half)],
            core_in.at[chunk % CORE_SLOTS],
            core_partner,
        )

    low_middle = z - 1
    far_middle = 2 - z

    def first_copy(chunk, partner):
        slot = chunk % SLOTS
        return remote(1, chunk, sent.at[slot], first_in.at[slot], partner)

    def y_copy(chunk):
        slot = chunk % SLOTS
        return remote(2, chunk, kept.at[slot, 1], second_in.at[slot, 0], y_partner)

    def pair_copy(chunk):
        slot = chunk % SLOTS
        return remote(2, chunk, kept.at[slot], second_in.at[slot], z_partner)

    def single_copy(chunk):
        slot = chunk % SLOTS
        return remote(3, chunk, kept.at[slot, 0], third_in.at[slot, 0], z_partner)

    def split_copy(chunk):
        slot = chunk % SLOTS
        return remote(3, chunk, kept.at[slot, far_middle], third_in.at[slot, 0], middle_partner)

    def middle_copy(chunk):
        slot = chunk % SLOTS
        return remote(4, chunk, kept.at[slot, 0], third_in.at[slot, 1], middle_partner)

    def across_copy(chunk):
        slot = chunk % SLOTS
        return remote(4, chunk, kept.at[slot, low_middle], third_in.at[slot, 1], x_partner)

    def result_copy(step, chunk, rows, partner):
        piece = result.at[chunk % RESULT_SLOTS, rows]
        return remote(step, chunk, piece, piece, partner)

    x_rows = aligned(2 * core + x, quarter)
    core_rows = aligned(core, half)

    def middle_rows():
        return aligned(2 * core + low_middle, quarter)

    def store_copy(chunk, target):
        slot = chunk % RESULT_SLOTS
        return pltpu.make_async_copy(result.at[slot], target, store_sem.at[slot])

    def multiply(chunk):
        slot = chunk % STAGED
        for copy in staged_copies(chunk, one_buf.at[slot], pair_buf.at[slot, 0], pair_buf.at[slot, 1]):
            copy.wait()
        inside = chunk % per_layer
        by_rows = (inside < starts[1]) | ((inside >= starts[2]) & (inside < starts[3]))

        @pl.when(by_rows)
        def _():
            single = one_buf[slot]
            for which in range(2):
                part_buf[slot, which] = dot_tn(pair_buf[slot, which], single).astype(low)

        @pl.when(jnp.logical_not(by_rows))
        def _():
            single = one_buf[slot]
            for which in range(2):
                part_buf[slot, which] = dot_tn(single, pair_buf[slot, which]).astype(low)

        core_copy(chunk).start()

    def branch(chunk, by_x, by_y):
        is_x = x_first(chunk)

        @pl.when(is_x)
        def _():
            by_x()

        @pl.when(jnp.logical_not(is_x))
        def _():
            by_y()

    def on_middle(action):
        @pl.when(inner == 1)
        def _():
            action()

    def by_place(at_end, at_middle):
        @pl.when(inner == 0)
        def _():
            at_end()

        on_middle(at_middle)

    def after_core(chunk):
        slot, core_slot, part_slot = chunk % SLOTS, chunk % CORE_SLOTS, chunk % STAGED
        core_copy(chunk).wait()
        is_x = x_first(chunk).astype(jnp.int32)

        def summed(which, row):
            near = part_buf[part_slot, which, aligned(2 * core + row, quarter), :]
            return added(near, core_in[core_slot, which, aligned(row, quarter), :])

        for index in range(2):
            sent[slot, index] = summed(
                is_x * index + (1 - is_x), is_x * (1 - x) + (1 - is_x) * index
            )
        branch(
            chunk,
            lambda: first_copy(chunk, x_partner).start(),
            lambda: first_copy(chunk, y_partner).start(),
        )
        for index in range(2):
            held[slot, index] = summed(is_x * index, is_x * x + (1 - is_x) * index)

    def after_first(chunk):
        slot = chunk % SLOTS
        first_copy(chunk, y_partner).wait()
        for index in (1, 0):
            kept[slot, index] = added(held[slot, index], first_in[slot, index])

        def by_y():
            @pl.when(inner == 0)
            def _():
                pair_copy(chunk).start()

        branch(chunk, lambda: y_copy(chunk).start(), by_y)

    def after_second(chunk):
        slot = chunk % SLOTS

        def by_x():
            y_copy(chunk).wait()
            kept[slot, 0] = added(kept[slot, 0], second_in[slot, 0])

            @pl.when(inner == 0)
            def _():
                single_copy(chunk).start()

        def at_middle():
            pair_copy(chunk).wait_recv()
            kept[slot, far_middle] = added(kept[slot, far_middle], second_in[slot, far_middle])
            split_copy(chunk).start()
            kept[slot, low_middle] = added(kept[slot, low_middle], second_in[slot, low_middle])

        branch(chunk, by_x, lambda: by_place(lambda: pair_copy(chunk).wait_send(), at_middle))

    def after_third(chunk):
        slot = chunk % SLOTS

        def one_at_middle():
            single_copy(chunk).wait_recv()
            kept[slot, 0] = added(kept[slot, 0], third_in[slot, 0])
            middle_copy(chunk).start()

        def by_y():
            split_copy(chunk).wait()
            kept[slot, low_middle] = added(kept[slot, low_middle], third_in[slot, 0])
            across_copy(chunk).start()

        branch(
            chunk,
            lambda: by_place(lambda: single_copy(chunk).wait_send(), one_at_middle),
            lambda: on_middle(by_y),
        )

    def after_fourth(chunk):
        slot, result_slot = chunk % SLOTS, chunk % RESULT_SLOTS

        def by_x():
            middle_copy(chunk).wait()
            result[result_slot, x_rows, :] = added(kept[slot, 0], third_in[slot, 1])
            result_copy(5, chunk, x_rows, z_partner).start()

        def by_y():
            across_copy(chunk).wait()
            result[result_slot, middle_rows(), :] = added(
                kept[slot, low_middle], third_in[slot, 1]
            )
            result_copy(5, chunk, middle_rows(), middle_partner).start()

        branch(chunk, lambda: on_middle(by_x), lambda: on_middle(by_y))

    def after_fifth(chunk):
        def by_x():
            back = result_copy(5, chunk, x_rows, z_partner)
            by_place(back.wait_recv, back.wait_send)
            result_copy(6, chunk, x_rows, x_partner).start()

        def by_y():
            result_copy(5, chunk, middle_rows(), middle_partner).wait()
            result_copy(6, chunk, core_rows, z_partner).start()

        branch(chunk, by_x, lambda: on_middle(by_y))

    def after_sixth(chunk):
        def by_y():
            back = result_copy(6, chunk, core_rows, z_partner)
            by_place(back.wait_recv, back.wait_send)

        branch(chunk, lambda: result_copy(6, chunk, x_rows, x_partner).wait(), by_y)
        result_copy(7, chunk, core_rows, core_partner).start()

    def after_whole(chunk):
        result_copy(7, chunk, core_rows, core_partner).wait()

        def action(member, layer, i, j):
            if member == 3:
                target = out_qkv.at[layer, j, block_of(i)]
            else:
                target = out_refs[member].at[layer, block_of(i), block_of(j)]
            store_copy(chunk, target).start()

        for_matrix(chunk, action)

    def after_store(chunk):
        store_copy(chunk, result.at[chunk % RESULT_SLOTS]).wait()

    vector_partners = (core_partner, y_partner, x_partner, z_partner, middle_partner, z_partner)

    def vector_copy(step):
        target = vec_in.at[min(step, 4)]
        return pltpu.make_async_remote_copy(
            src_ref=vector_out,
            dst_ref=target,
            send_sem=vec_send.at[step],
            recv_sem=vec_recv.at[step],
            device_id=vector_partners[step],
            device_id_type=MESH,
        )

    def add_vector(step):
        vector_out[...] = vector_out[...] + vec_in[step]

    def vector_tick(step):
        if step == 0:
            vector_copy(0).start()
        elif step <= 3:
            vector_copy(step - 1).wait()
            add_vector(step - 1)
            if step < 3:
                vector_copy(step).start()
            else:

                @pl.when(inner == 0)
                def _():
                    vector_copy(3).start()

        elif step == 4:

            @pl.when(inner == 0)
            def _():
                vector_copy(3).wait_send()

            @pl.when(inner == 1)
            def _():
                vector_copy(3).wait_recv()
                add_vector(3)
                vector_copy(4).start()

        elif step == 5:

            @pl.when(inner == 1)
            def _():
                vector_copy(4).wait()
                add_vector(4)
                vector_copy(5).start()

        else:

            @pl.when(inner == 1)
            def _():
                vector_copy(5).wait_send()

            @pl.when(inner == 0)
            def _():
                vector_copy(5).wait_recv()
                vector_out[...] = vec_in[4]

    norm_two_step = FFN_STEPS
    out_step = norm_two_step + 1
    attention_step = out_step + 1
    qkv_step = attention_step + pairs + 1
    norm_one_step = qkv_step + QKV_STEPS
    period = norm_one_step + 1
    jobs = layers * period
    hidden_step = 2 * hidden_half // FFN_STEPS

    def loads(kind, slot, *sources):
        targets = {
            "ffn": (rows_weight.at[slot], columns_weight.at[slot], slope_buf.at[slot]),
            "wide": (wide_buf,),
            "out": (rows_weight.at[slot, pl.ds(0, block)], rows_weight.at[slot, pl.ds(block, block)]),
            "attention": (
                qkv_buf.at[slot, 0],
                qkv_buf.at[slot, 1],
                qkv_buf.at[slot, 2],
                halo_buf.at[slot, 0],
                halo_buf.at[slot, 1],
                totals_buf.at[slot],
            ),
            "qkv": (
                columns_weight.at[slot, :, pl.ds(0, block)],
                columns_weight.at[slot, :, pl.ds(block, block)],
            ),
        }[kind]
        sources = sources or targets
        return [
            pltpu.make_async_copy(source, target, load_sem.at[slot, index])
            for index, (source, target) in enumerate(zip(sources, targets))
        ]

    def prefetch(t):
        slot = t % 2
        layer = layers - 1 - t // period
        step = t % period

        for which, (up_ref, down_ref) in enumerate(((up_own, down_own), (up_other, down_other))):

            @pl.when((step < FFN_STEPS) & (step // (FFN_STEPS // 2) == which))
            def _(which=which, up_ref=up_ref, down_ref=down_ref):
                cut = aligned(step % (FFN_STEPS // 2), hidden_step)
                for copy in loads(
                    "ffn",
                    slot,
                    down_ref.at[layer, cut, :],
                    up_ref.at[layer, :, cut],
                    slope_ref.at[layer, which, :, cut],
                ):
                    copy.start()

        for at, source in ((norm_two_step, middle_ref), (norm_one_step, resid_ref)):

            @pl.when(step == at)
            def _(source=source):
                for copy in loads("wide", slot, source.at[layer]):
                    copy.start()

        @pl.when(step == out_step)
        def _():
            for copy in loads("out", slot, out_own.at[layer], out_other.at[layer]):
                copy.start()

        @pl.when((step >= attention_step) & (step < attention_step + pairs))
        def _():
            pair = step - attention_step
            which, inside = pair // pairs_half, pair % pairs_half

            def lanes(third):
                return aligned(third * pairs_half + inside, LANES)

            for copy in loads(
                "attention",
                slot,
                *[proj_ref.at[layer, which, :, lanes(third)] for third in range(3)],
                *[halo_ref.at[layer, which, third, :, lanes(0)] for third in range(2)],
                totals_ref.at[layer, which],
            ):
                copy.start()

        @pl.when((step >= qkv_step) & (step < qkv_step + QKV_STEPS))
        def _():
            for part in range(2):
                index = 2 * (step - qkv_step) + part
                for which, source in enumerate((qkv_own, qkv_other)):

                    @pl.when(index // 3 == which)
                    def _(part=part, index=index, source=source):
                        pltpu.make_async_copy(
                            source.at[layer, index % 3],
                            columns_weight.at[slot, :, pl.ds(part * block, block)],
                            load_sem.at[slot, part],
                        ).start()

    def wait_loads(kind, slot):
        for copy in loads(kind, slot):
            copy.wait()

    tiles = [slice(r, r + BAND) for r in range(0, rows_all, BAND)]
    fine_tiles = [slice(r, r + LANES) for r in range(0, rows_all, LANES)]

    def vector_row(layer, row):
        return pl.ds(layer * VECTOR_ROWS + row, 1)

    def column_sum(values):
        return jnp.sum(values.astype(jnp.float32), axis=0, keepdims=True)

    def ffn_job(layer, step, slot):
        wait_loads("ffn", slot)
        sums = 0.0
        for tile in tiles:
            grad_hidden = dot_nt(grad_branch[tile, :], rows_weight[slot])
            before = (grad_hidden * slope_buf[slot, tile, :].astype(jnp.float32)).astype(low)
            grad_before[step, tile, :] = before
            sums = sums + column_sum(before)
            product = dot_nt(before, columns_weight[slot])

            @pl.when(step == 0)
            def _(tile=tile, product=product):
                collected[tile, :] = product

            @pl.when(step > 0)
            def _(tile=tile, product=product):
                collected[tile, :] = collected[tile, :] + product

        per_half = FFN_STEPS // 2
        which = step // per_half
        owner = which + y - 2 * which * y
        vector_out[vector_row(layer, 2 + owner * per_half + step % per_half), :] = sums

    def norm_job(layer, index, slot):
        wait_loads("wide", slot)
        gain = gain_ref[layer, pl.ds(index, 1), :]
        gain_sum, shift_sum, attn_sum, branch_sum = 0.0, 0.0, 0.0, 0.0
        for tile in fine_tiles:
            incoming = collected[tile, :]
            values = wide_buf[tile, :]
            average = jnp.mean(values, axis=-1, keepdims=True)
            centred = values - average
            inverse = lax.rsqrt(jnp.mean(centred * centred, axis=-1, keepdims=True) + epsilon)
            unit = centred * inverse
            scaled = incoming * gain
            first_mean = jnp.mean(scaled, axis=-1, keepdims=True)
            second_mean = jnp.mean(scaled * unit, axis=-1, keepdims=True)
            total = grad_res[tile, :] + inverse * (scaled - first_mean - unit * second_mean)
            grad_res[tile, :] = total
            rounded = total.astype(low)
            gain_sum = gain_sum + column_sum(incoming * unit)
            shift_sum = shift_sum + column_sum(incoming)
            if index == 1:
                attn_sum = attn_sum + column_sum(rounded)
                branch_sum = branch_sum + column_sum(grad_branch[tile, :])
                grad_attn[tile, :] = rounded
            else:
                grad_branch[tile, :] = rounded
        vector_out[vector_row(layer, 8 + index), :] = gain_sum
        vector_out[vector_row(layer, 10 + index), :] = shift_sum
        if index == 1:
            vector_out[vector_row(layer, 6), :] = attn_sum
            vector_out[vector_row(layer, 7), :] = branch_sum

    def out_job(slot):
        wait_loads("out", slot)
        for tile in tiles:
            grad_attended[tile, :] = dot_nt(grad_attn[tile, :], rows_weight[slot]).astype(low)

    def halo_copy(pair):
        return pltpu.make_async_remote_copy(
            src_ref=halo_send.at[pair % 2],
            dst_ref=halo_in.at[pair],
            send_sem=halo_send_sem.at[pair],
            recv_sem=halo_recv_sem.at[pair],
            device_id=core_partner,
            device_id_type=MESH,
        )

    def proj_lanes(pair, third):
        which, inside = pair // pairs_half, pair % pairs_half
        return aligned(which * 3 * pairs_half + third * pairs_half + inside, LANES)

    def attention_job(pair, slot):
        wait_loads("attention", slot)
        lane = lax.broadcasted_iota(jnp.int32, (BAND, LANES), 1)
        scaling = HEAD_DIM ** (-0.5)
        count = len(tiles)
        key_parts = [None] * (count + 1)
        value_parts = [None] * (count + 1)
        here = aligned(pair, LANES)
        for index, tile in enumerate(tiles):
            query = qkv_buf[slot, 0, tile, :]
            grad = grad_attended[tile, here]
            keys = band_rows(halo_buf[slot, 0], qkv_buf[slot, 1], index)
            values = band_rows(halo_buf[slot, 1], qkv_buf[slot, 2], index)
            grad_query = []
            grad_keys = 0.0
            grad_values = 0.0
            for head in range(2):
                mine = (lane // HEAD_DIM) == head
                query_head = jnp.where(mine, query, 0)
                grad_head = jnp.where(mine, grad, 0)
                scores = dot_nt(query_head, keys) * scaling + bias_buf[index]
                total = jnp.sum(
                    jnp.where(
                        lane == 2 * (pair % pairs_half) + head, totals_buf[slot, tile, :], 0.0
                    ),
                    axis=-1,
                    keepdims=True,
                )
                exact = jnp.exp(scores - total)
                grad_probs = dot_nt(grad_head, values)
                row_terms = jnp.sum(exact * grad_probs, axis=-1, keepdims=True)
                grad_scores = (exact * (grad_probs - row_terms)).astype(low)
                grad_query.append(jnp.dot(grad_scores, keys, preferred_element_type=jnp.float32))
                grad_keys = grad_keys + dot_tn(grad_scores, query_head)
                grad_values = grad_values + dot_tn(exact.astype(low), grad_head)
            grad_proj[tile, proj_lanes(pair, 0)] = (
                jnp.where(lane < HEAD_DIM, grad_query[0], grad_query[1]) * scaling
            ).astype(low)
            grad_keys = grad_keys * scaling
            for part in range(2):
                cut = slice(part * BAND, (part + 1) * BAND)
                old_k, old_v = key_parts[index + part], value_parts[index + part]
                key_parts[index + part] = grad_keys[cut] if old_k is None else old_k + grad_keys[cut]
                value_parts[index + part] = (
                    grad_values[cut] if old_v is None else old_v + grad_values[cut]
                )
        for index in range(count - 1):
            grad_proj[tiles[index], proj_lanes(pair, 1)] = key_parts[index + 1].astype(low)
            grad_proj[tiles[index], proj_lanes(pair, 2)] = value_parts[index + 1].astype(low)
        kept_kv[pair % 2, 0] = key_parts[count]
        kept_kv[pair % 2, 1] = value_parts[count]

        @pl.when(core == 1)
        def _():
            halo_send[pair % 2, 0] = key_parts[0].astype(low)
            halo_send[pair % 2, 1] = value_parts[0].astype(low)
            halo_copy(pair).start()

    def finish_pair(pair):
        last = tiles[-1]

        @pl.when(core == 0)
        def _():
            halo_copy(pair).wait_recv()
            for third in range(2):
                grad_proj[last, proj_lanes(pair, third + 1)] = (
                    kept_kv[pair % 2, third] + halo_in[pair, third].astype(jnp.float32)
                ).astype(low)

        @pl.when(core == 1)
        def _():
            halo_copy(pair).wait_send()
            for third in range(2):
                grad_proj[last, proj_lanes(pair, third + 1)] = kept_kv[pair % 2, third].astype(low)

    def qkv_job(layer, step, slot):
        wait_loads("qkv", slot)
        sums = 0.0
        for tile in tiles:
            grad = grad_proj[tile, aligned(step, width)]
            sums = sums + column_sum(grad)
            product = dot_nt(grad, columns_weight[slot])

            @pl.when(step == 0)
            def _(tile=tile, product=product):
                collected[tile, :] = product

            @pl.when(step > 0)
            def _(tile=tile, product=product):
                collected[tile, :] = collected[tile, :] + product

        sums_buf[...] = sums
        for when, part, which, row in ((0, 0, 0, 0), (1, 0, 0, 1), (1, 1, 1, 0), (2, 1, 1, 1)):

            @pl.when(step == when)
            def _(part=part, which=which, row=row):
                owner = 1 - y if which else y
                vector_out[vector_row(layer, row), block_of(owner)] = sums_buf[
                    :, part * block : (part + 1) * block
                ]

    def job(t):
        slot = t % 2
        layer = layers - 1 - t // period
        step = t % period

        @pl.when(step < FFN_STEPS)
        def _():
            ffn_job(layer, step, slot)

        @pl.when(step == norm_two_step)
        def _():
            norm_job(layer, 1, slot)

        @pl.when(step == out_step)
        def _():
            out_job(slot)

        @pl.when((step > attention_step) & (step <= attention_step + pairs))
        def _():
            finish_pair(step - attention_step - 1)

        @pl.when((step >= attention_step) & (step < attention_step + pairs))
        def _():
            attention_job(step - attention_step, slot)

        @pl.when((step >= qkv_step) & (step < qkv_step + QKV_STEPS))
        def _():
            qkv_job(layer, step - qkv_step, slot)

        @pl.when(step == norm_one_step)
        def _():
            norm_job(layer, 0, slot)

    stages = (
        (LAGS["core"], after_core),
        (0, multiply),
        (None, job),
        (LAGS["first"], after_first),
        (LAGS["second"], after_second),
        (LAGS["third"], after_third),
        (LAGS["fourth"], after_fourth),
        (LAGS["fifth"], after_fifth),
        (LAGS["sixth"], after_sixth),
        (LAGS["stored"], after_store),
        (LAGS["whole"], after_whole),
    )

    swaps = core + y - 2 * core * y

    def swap_copy(index, source, target):
        return pltpu.make_async_remote_copy(
            src_ref=source,
            dst_ref=target,
            send_sem=swap_send.at[index],
            recv_sem=swap_recv.at[index],
            device_id=swap_partner,
            device_id_type=MESH,
        )

    def swap_start(index, source, target):
        @pl.when(swaps == 1)
        def _():
            swap_copy(index, source, target).start()

        if index:

            @pl.when(swaps == 0)
            def _():
                pltpu.make_async_copy(source, target, io_sem.at[1]).start()

    def swap_wait(index, source, target):
        @pl.when(swaps == 1)
        def _():
            swap_copy(index, source, target).wait()

        if index:

            @pl.when(swaps == 0)
            def _():
                pltpu.make_async_copy(source, target, io_sem.at[1]).wait()

    first_load = pltpu.make_async_copy(cot_ref, grad_branch, io_sem.at[0])
    first_load.start()
    prefetch(0)
    first_load.wait()
    stage_operands(0)

    @pl.when(inner == 1)
    def _():
        pl.semaphore_wait(barrier, 6)

    @pl.when(inner == 0)
    def _():
        pl.semaphore_wait(barrier, 5)
    vector_ticks = [jobs + VECTOR_STEP * step for step in range(7)]

    def tick(t, carry):
        @pl.when(t == 1)
        def _():
            fill_band_bias(segk_ref, bias_buf)
            for tile in tiles:
                grad_res[tile, :] = grad_branch[tile, :].astype(jnp.float32)

        @pl.when(t + 1 < jobs)
        def _():
            prefetch(t + 1)

        ahead = t + 1 - FIRST

        @pl.when((ahead > 0) & (ahead < chunks))
        def _():
            stage_operands(ahead)

        for lag, action in stages:
            if lag is None:

                @pl.when(t < jobs)
                def _():
                    job(t)

                continue
            chunk = t - FIRST - lag

            @pl.when((chunk >= 0) & (chunk < chunks))
            def _(chunk=chunk, action=action):
                action(chunk)

        @pl.when(t == chunks + FIRST + LAGS["second"] - 1)
        def _():
            swap_start(0, out_act_ref, out_act_out)
            swap_start(1, grad_branch, grad_in_ref)

        for step, when in enumerate(vector_ticks):

            @pl.when(t == when)
            def _(step=step):
                vector_tick(step)

        return carry

    lax.fori_loop(0, max(chunks + FIRST + LAGS["stored"], vector_ticks[-1] + 1), tick, 0)
    swap_wait(0, out_act_ref, out_act_out)
    swap_wait(1, grad_branch, grad_in_ref)


def run_backward(cotangent, gain, segk, out_act, saved, weights, block):
    rows, width = cotangent.shape
    layers, hidden_half = weights[-1].shape[0], weights[-1].shape[1]
    half, quarter = block // 2, block // 4
    low, wide = jnp.bfloat16, jnp.float32
    pairs = width // LANES
    anywhere = pl.BlockSpec(memory_space=pl.ANY)
    in_vmem = pl.BlockSpec(memory_space=pltpu.VMEM)
    vector = (layers * VECTOR_ROWS, width)
    hidden_step = 2 * hidden_half // FFN_STEPS
    vmem = pltpu.VMEM
    return pl.pallas_call(
        functools.partial(backward_kernel, layers, block, hidden_half),
        in_specs=[anywhere] + [in_vmem] * 2 + [anywhere] * (1 + len(saved) + len(weights)),
        out_specs=[anywhere] * 6 + [in_vmem],
        out_shape=[
            jax.ShapeDtypeStruct((rows, width), low),
            jax.ShapeDtypeStruct((rows, width), low),
            jax.ShapeDtypeStruct((layers, hidden_half, width), low),
            jax.ShapeDtypeStruct((layers, width, hidden_half), low),
            jax.ShapeDtypeStruct((layers, block, width), low),
            jax.ShapeDtypeStruct((layers, 3, width, block), low),
            jax.ShapeDtypeStruct(vector, wide),
        ],
        scratch_shapes=[
            vmem((rows, width), low),
            vmem((rows, width), low),
            vmem((FFN_STEPS, rows, hidden_step), low),
            vmem((rows, 6 * block), low),
            vmem((rows, width), wide),
            vmem((rows, width), wide),
            vmem((rows, width), low),
            vmem((2, 3, rows, LANES), low),
            vmem((2, 2, BAND, LANES), low),
            vmem((2, rows, LANES), wide),
            vmem((2, 2, BAND, LANES), wide),
            vmem((2, 2, BAND, LANES), low),
            vmem((pairs, 2, BAND, LANES), low),
            vmem((2, hidden_step, width), low),
            vmem((2, width, hidden_step), low),
            vmem((2, rows, hidden_step), low),
            vmem((rows, width), wide),
            vmem((rows // BAND, BAND, 2 * BAND), wide),
            vmem((1, width), wide),
            vmem((STAGED, 2, rows, block), low),
            vmem((STAGED, rows, block), low),
            vmem((STAGED, 2, block, block), low),
            vmem((CORE_SLOTS, 2, half, block), low),
            vmem((SLOTS, 2, quarter, block), low),
            vmem((SLOTS, 2, quarter, block), low),
            vmem((SLOTS, 2, quarter, block), low),
            vmem((SLOTS, 2, quarter, block), low),
            vmem((SLOTS, 2, quarter, block), low),
            vmem((SLOTS, 2, quarter, block), low),
            vmem((RESULT_SLOTS, block, block), low),
            vmem((5,) + vector, wide),
            pltpu.SemaphoreType.DMA((2, 6)),
            pltpu.SemaphoreType.DMA((2,)),
            pltpu.SemaphoreType.DMA((pairs,)),
            pltpu.SemaphoreType.DMA((pairs,)),
            pltpu.SemaphoreType.DMA((STAGED, 3)),
            pltpu.SemaphoreType.DMA((8, SLOTS)),
            pltpu.SemaphoreType.DMA((8, SLOTS)),
            pltpu.SemaphoreType.DMA((RESULT_SLOTS,)),
            pltpu.SemaphoreType.DMA((6,)),
            pltpu.SemaphoreType.DMA((6,)),
            pltpu.SemaphoreType.DMA((2,)),
            pltpu.SemaphoreType.DMA((2,)),
        ],
        compiler_params=pltpu.CompilerParams(
            collective_id=0, has_side_effects=True, vmem_limit_bytes=VMEM_ASKED
        ),
        name="backward",
    )(cotangent, gain, segk, out_act, *saved, *weights)


FINISH_DEPTH = 4


def finish_kernel(layers, steps, *refs):
    count = len(steps)
    ins, refs = refs[:count], refs[count:]
    vector_ref, refs = refs[0], refs[1:]
    (act_own, act_swapped, grad_in_ref), refs = refs[:3], refs[3:]
    outs, refs = refs[:count], refs[count:]
    qv_out, up_out, bias_out, gain_out, shift_out = refs[:5]
    (act_out, grad_in_out), refs = refs[5:7], refs[7:]
    in_bufs, refs = refs[:count], refs[count:]
    out_bufs, (moved_buf, in_sem, out_sem, copy_sem) = refs[:count], refs[count:]
    y = lax.axis_index("tensor")
    core = lax.axis_index("dp") % 2

    def fetch(index, source):
        return pltpu.make_async_copy(source, moved_buf.at[index], copy_sem.at[index])

    def put(index, target):
        return pltpu.make_async_copy(moved_buf.at[index], target, copy_sem.at[index])

    @pl.when(core == y)
    def _():
        fetch(0, act_own).start()

    @pl.when(core != y)
    def _():
        fetch(0, act_swapped).start()

    fetch(1, grad_in_ref).start()
    plan = []
    for member, (rows, parts) in enumerate(steps):
        for layer in range(layers):
            for part in range(parts):
                plan.append((member, layer, part * rows, rows, (layer * parts + part) % FINISH_DEPTH))

    def view(ref, layer, begin, rows):
        if len(ref.shape) == 4:
            return ref.at[layer, begin // rows]
        return ref.at[layer, pl.ds(begin, rows)]

    def load(entry):
        member, layer, begin, rows, slot = entry
        return pltpu.make_async_copy(
            view(ins[member], layer, begin, rows), in_bufs[member].at[slot], in_sem.at[member, slot]
        )

    def save(entry):
        member, layer, begin, rows, slot = entry
        return pltpu.make_async_copy(
            out_bufs[member].at[slot], view(outs[member], layer, begin, rows), out_sem.at[member, slot]
        )

    for entry in plan[:FINISH_DEPTH]:
        load(entry).start()
    half = qv_out.shape[2]
    for layer in range(layers):
        base = layer * VECTOR_ROWS
        for index in range(2):
            mine = pl.ds(pl.multiple_of(y * half, half), half)
            qv_out[layer, pl.ds(index, 1), :] = vector_ref[pl.ds(base + index, 1), mine]
            width = vector_ref.shape[1]
            up_out[pl.ds(layer, 1), index * width : (index + 1) * width] = vector_ref[
                pl.ds(base + 2 + 2 * y + index, 1), :
            ]
            for row, target in ((6, bias_out), (8, gain_out), (10, shift_out)):
                target[layer, pl.ds(index, 1), :] = vector_ref[pl.ds(base + row + index, 1), :]
    for index, target in enumerate((act_out, grad_in_out)):
        fetch(index, target).wait()
        put(index, target).start()
    busy = {}
    for place, entry in enumerate(plan):
        member, slot = entry[0], entry[4]
        load(entry).wait()
        if (member, slot) in busy:
            save(busy.pop((member, slot))).wait()
        out_bufs[member][slot] = in_bufs[member][slot].astype(jnp.float32)
        save(entry).start()
        busy[(member, slot)] = entry
        if place + FINISH_DEPTH < len(plan):
            load(plan[place + FINISH_DEPTH]).start()
    for entry in busy.values():
        save(entry).wait()
    for index, target in enumerate((act_out, grad_in_out)):
        put(index, target).wait()


def run_finish(reduced, vector, acts, grad_in, block):
    layers, width = reduced[0].shape[0], vector.shape[1]
    hidden_half = reduced[0].shape[1]
    wide, low = jnp.float32, jnp.bfloat16
    shape = jax.ShapeDtypeStruct
    anywhere = pl.BlockSpec(memory_space=pl.ANY)
    in_vmem = pl.BlockSpec(memory_space=pltpu.VMEM)
    steps = (
        (block, hidden_half // block),
        (block // 2, width * 2 // block),
        (block, 1),
        (width, 3),
    )
    blocks = ((block, width), (block // 2, hidden_half), (block, width), (width, block))
    deep = lambda kind: [pltpu.VMEM((FINISH_DEPTH,) + size, kind) for size in blocks]
    return pl.pallas_call(
        functools.partial(finish_kernel, layers, steps),
        in_specs=[anywhere] * len(reduced) + [in_vmem] + [anywhere] * 3,
        out_specs=[anywhere] * len(reduced) + [in_vmem] * 5 + [anywhere] * 2,
        out_shape=[shape(member.shape, wide) for member in reduced]
        + [
            shape((layers, 2, block), wide),
            shape((layers, hidden_half), wide),
            shape((layers, 2, width), wide),
            shape((layers, 2, width), wide),
            shape((layers, 2, width), wide),
        ]
        + [shape(grad_in.shape, low)] * 2,
        scratch_shapes=deep(low)
        + deep(wide)
        + [
            pltpu.VMEM((2,) + grad_in.shape, low),
            pltpu.SemaphoreType.DMA((4, FINISH_DEPTH)),
            pltpu.SemaphoreType.DMA((4, FINISH_DEPTH)),
            pltpu.SemaphoreType.DMA((2,)),
        ],
        compiler_params=pltpu.CompilerParams(vmem_limit_bytes=VMEM_ASKED),
        name="finish",
    )(*reduced, vector, *acts, grad_in)


def local_split(
    tokens_in,
    segments,
    w_qkv,
    qv_bias,
    w_out,
    w_up,
    up_bias,
    w_down,
    out_bias,
    ln_gain,
    ln_bias,
    cotangent,
):
    block = w_qkv.shape[3]
    weights = (w_qkv.transpose(0, 2, 1, 3), w_out, w_up, w_down)
    act_own, cot, segk, *rest = run_forward(
        tokens_in,
        cotangent,
        segments,
        weights,
        (qv_bias, up_bias),
        out_bias,
        ln_gain,
        ln_bias,
        block,
    )
    others, saved = rest[: len(weights)], rest[len(weights) :]
    both = [member for pair in zip(weights, others) for member in pair]
    act_swapped, grad_in, *reduced, summed = run_backward(
        cot, ln_gain, segk, act_own, saved, both, block
    )
    *grads, grad_qv, grad_up_bias, grad_bias, grad_gain, grad_shift, out_act, grad_in = run_finish(
        reduced, summed, (act_own, act_swapped), grad_in, block
    )
    grad_down, grad_up, grad_out, grad_qkv = grads
    return (
        out_act,
        grad_in,
        grad_qkv.transpose(0, 2, 1, 3),
        grad_qv,
        grad_out,
        grad_up,
        grad_up_bias,
        grad_down,
        grad_bias,
        grad_gain,
        grad_shift,
    )


def solution(mesh):
    sizes = (mesh.shape["dp"], mesh.shape["tensor"])
    local = local_split if sizes == (16, 2) else local_general
    return jax.shard_map(
        local,
        mesh=mesh,
        in_specs=(
            P(("dp", "tensor"), None),
            P("dp", None),
            P(None, None, None, "tensor"),
            P(None, None, "tensor"),
            P(None, "tensor", None),
            P(None, None, "tensor"),
            P(None, "tensor"),
            P(None, "tensor", None),
            P(),
            P(),
            P(),
            P(("dp", "tensor"), None),
        ),
        out_specs=(
            P(("dp", "tensor"), None),
            P(("dp", "tensor"), None),
            P(None, None, None, "tensor"),
            P(None, None, "tensor"),
            P(None, "tensor", None),
            P(None, None, "tensor"),
            P(None, "tensor"),
            P(None, "tensor", None),
            P(),
            P(),
            P(),
        ),
        check_vma=False,
    )
```

```python
import functools

import jax
import jax.numpy as jnp
from jax import lax
from jax.experimental import pallas as pl
from jax.experimental.pallas import tpu as pltpu
from jax.sharding import PartitionSpec as P

HEAD_DIM = 64


epsilon = 1e-05
gelu_coeff = 0.7978845608028654
cubic_coeff = 0.044715
masked_score = -1e30


def as_sent(shard):

    def short(part):
        return part.astype(jnp.bfloat16) if part.dtype == jnp.float32 else part

    return jax.tree.map(short, shard)


def layer_norm(values, gain, shift):
    average = jnp.mean(values, axis=-1, keepdims=True)
    centred = values - average
    inverse = lax.rsqrt(jnp.mean(centred * centred, axis=-1, keepdims=True) + epsilon)
    unit_rows = centred * inverse
    return (unit_rows * gain + shift, unit_rows, inverse)


def norm_backward(incoming, unit_rows, inverse, gain):
    scaled = incoming * gain
    first_mean = jnp.mean(scaled, axis=-1, keepdims=True)
    second_mean = jnp.mean(scaled * unit_rows, axis=-1, keepdims=True)
    through = inverse * (scaled - first_mean - unit_rows * second_mean)
    return (through, jnp.sum(incoming * unit_rows, axis=0), jnp.sum(incoming, axis=0))


def gelu_tanh(before):
    tanh_input = gelu_coeff * (before + cubic_coeff * before * before * before)
    return 0.5 * before * (1.0 + jnp.tanh(tanh_input))


def gelu_slope(before):
    tanh_input = gelu_coeff * (before + cubic_coeff * before * before * before)
    tangent = jnp.tanh(tanh_input)
    return 0.5 * (1.0 + tangent) + 0.5 * before * (1.0 - tangent * tangent) * gelu_coeff * (
        1.0 + 3.0 * cubic_coeff * before * before
    )


def masked_scores(query_block, key_seq, segment_row, offset, block_rows):
    window = key_seq.shape[0]
    scores = jnp.einsum(
        "qhe,khe->hqk", query_block, key_seq, preferred_element_type=jnp.float32
    ) * HEAD_DIM ** (-0.5)
    query_place = offset + lax.iota(jnp.int32, block_rows)
    key_place = lax.iota(jnp.int32, window)
    query_segment = segment_row[offset : offset + block_rows]
    allowed = (query_place[:, None] >= key_place[None, :]) & (
        query_segment[:, None] == segment_row[None, :]
    )
    return jnp.where(allowed[None], scores, masked_score)


def split_heads(flat_rows, seq_count):
    return flat_rows.reshape(
        seq_count, flat_rows.shape[0] // seq_count, flat_rows.shape[1] // HEAD_DIM, HEAD_DIM
    )


def attend_forward(query_rows, key_rows, value_rows, segments):
    seq_count, window = segments.shape
    block_rows = min(512, window)

    def one_sequence(member):
        query_seq, key_seq, value_seq, segment_row = member
        outputs = []
        totals = []
        for block_index in range(window // block_rows):
            offset = block_index * block_rows
            scores = masked_scores(
                query_seq[offset : offset + block_rows], key_seq, segment_row, offset, block_rows
            )
            highest = jnp.max(scores, axis=-1, keepdims=True)
            raised = jnp.exp(scores - highest)
            summed = jnp.sum(raised, axis=-1, keepdims=True)
            softmax_low = (raised / summed).astype(jnp.bfloat16)
            block_out = jnp.einsum(
                "hqk,khe->qhe", softmax_low, value_seq, preferred_element_type=jnp.float32
            )
            outputs.append(block_out.astype(jnp.bfloat16))
            totals.append(highest[..., 0] + jnp.log(summed[..., 0]))
        return (jnp.concatenate(outputs, axis=0), jnp.stack(totals, axis=0))

    attended, log_totals = lax.map(
        one_sequence,
        (
            split_heads(query_rows, seq_count),
            split_heads(key_rows, seq_count),
            split_heads(value_rows, seq_count),
            segments,
        ),
    )
    return (attended.reshape(query_rows.shape), log_totals)


def attend_backward(query_rows, key_rows, value_rows, segments, log_totals, grad_attended):
    seq_count, window = segments.shape
    block_rows = min(512, window)
    scaling = HEAD_DIM ** (-0.5)

    def one_sequence(member):
        query_seq, key_seq, value_seq, segment_row, totals_seq, grad_seq = member
        query_parts = []
        grad_keys = jnp.zeros(key_seq.shape, jnp.float32)
        grad_values = jnp.zeros(value_seq.shape, jnp.float32)
        for block_index in range(window // block_rows):
            offset = block_index * block_rows
            query_block = query_seq[offset : offset + block_rows]
            grad_block = grad_seq[offset : offset + block_rows]
            scores = masked_scores(query_block, key_seq, segment_row, offset, block_rows)
            softmax_exact = jnp.exp(scores - totals_seq[block_index][..., None])
            softmax_low = softmax_exact.astype(jnp.bfloat16)
            grad_softmax = jnp.einsum(
                "qhe,khe->hqk", grad_block, value_seq, preferred_element_type=jnp.float32
            )
            row_terms = jnp.sum(softmax_exact * grad_softmax, axis=-1, keepdims=True)
            grad_scores = (softmax_exact * (grad_softmax - row_terms)).astype(jnp.bfloat16)
            query_parts.append(
                jnp.einsum("hqk,khe->qhe", grad_scores, key_seq, preferred_element_type=jnp.float32)
                * scaling
            )
            grad_keys = (
                grad_keys
                + jnp.einsum(
                    "hqk,qhe->khe", grad_scores, query_block, preferred_element_type=jnp.float32
                )
                * scaling
            )
            grad_values = grad_values + jnp.einsum(
                "hqk,qhe->khe", softmax_low, grad_block, preferred_element_type=jnp.float32
            )
        grad_query = jnp.concatenate(query_parts, axis=0)
        return (
            grad_query.astype(jnp.bfloat16),
            grad_keys.astype(jnp.bfloat16),
            grad_values.astype(jnp.bfloat16),
        )

    grad_query, grad_keys, grad_values = lax.map(
        one_sequence,
        (
            split_heads(query_rows, seq_count),
            split_heads(key_rows, seq_count),
            split_heads(value_rows, seq_count),
            segments,
            log_totals,
            split_heads(grad_attended, seq_count),
        ),
    )
    return (
        grad_query.reshape(query_rows.shape),
        grad_keys.reshape(query_rows.shape),
        grad_values.reshape(query_rows.shape),
    )


def layer_forward(residual, segments, weights):
    w_qkv, qv_bias, w_out, w_up, up_bias, w_down, out_bias, gains, shifts = weights
    row_count = residual.shape[0]
    normed, unit_one, inverse_one = layer_norm(residual, gains[0], shifts[0])
    normed_all = lax.all_gather(normed.astype(jnp.bfloat16), "tensor", axis=0, tiled=True)
    projected = jnp.einsum("td,dsc->tsc", normed_all, w_qkv, preferred_element_type=jnp.float32)
    query_rows = (projected[:, 0] + qv_bias[0]).astype(jnp.bfloat16)
    key_rows = projected[:, 1].astype(jnp.bfloat16)
    value_rows = (projected[:, 2] + qv_bias[1]).astype(jnp.bfloat16)
    attended, log_totals = attend_forward(query_rows, key_rows, value_rows, segments)
    middle = (
        residual
        + lax.psum_scatter(
            jnp.dot(
                lax.slice_in_dim(attended, 0, row_count * lax.axis_size("tensor"), axis=0),
                w_out,
                preferred_element_type=jnp.float32,
            ).astype(jnp.bfloat16),
            "tensor",
            scatter_dimension=0,
            tiled=True,
        ).astype(jnp.float32)
        + out_bias[0]
    )
    normed_two, unit_two, inverse_two = layer_norm(middle, gains[1], shifts[1])
    normed_low = normed_two.astype(jnp.bfloat16)
    ffn_rows = lax.all_gather(normed_low, "tensor", axis=0, tiled=True)
    before = jnp.dot(ffn_rows, w_up, preferred_element_type=jnp.float32) + up_bias
    activated = gelu_tanh(before).astype(jnp.bfloat16)
    ffn_branch = lax.psum_scatter(
        jnp.dot(
            lax.slice_in_dim(activated, 0, row_count * lax.axis_size("tensor"), axis=0),
            w_down,
            preferred_element_type=jnp.float32,
        ).astype(jnp.bfloat16),
        "tensor",
        scatter_dimension=0,
        tiled=True,
    ).astype(jnp.float32)
    kept_ffn = (w_up, w_down)
    result = middle + ffn_branch + out_bias[1]
    kept_state = (
        unit_one,
        inverse_one,
        normed_all,
        query_rows,
        key_rows,
        value_rows,
        attended,
        log_totals,
        unit_two,
        inverse_two,
        ffn_rows,
        before,
        activated,
        kept_ffn,
    )
    return (result, kept_state)


def layer_backward(grad_residual, segments, weights, kept_state):
    w_qkv, qv_bias, w_out, w_up, up_bias, w_down, out_bias, gains, shifts = weights
    (
        unit_one,
        inverse_one,
        normed_all,
        query_rows,
        key_rows,
        value_rows,
        attended,
        log_totals,
        unit_two,
        inverse_two,
        ffn_rows,
        before,
        activated,
        kept_ffn,
    ) = kept_state
    up_used, down_used = kept_ffn
    row_count = grad_residual.shape[0]
    grad_branch = grad_residual.astype(jnp.bfloat16)
    bias_down = jnp.sum(grad_branch, axis=0, dtype=jnp.float32)
    grad_rows = lax.all_gather(grad_branch, "tensor", axis=0, tiled=True)
    grad_hidden = jnp.einsum("td,fd->tf", grad_rows, down_used, preferred_element_type=jnp.float32)
    grad_before = (grad_hidden * gelu_slope(before)).astype(jnp.bfloat16)
    grad_down = jnp.einsum("tf,td->fd", activated, grad_rows, preferred_element_type=jnp.float32)
    grad_up = jnp.einsum("td,tf->df", ffn_rows, grad_before, preferred_element_type=jnp.float32)
    grad_up_bias = jnp.sum(grad_before, axis=0, dtype=jnp.float32)
    piece_rows = lax.slice_in_dim(grad_before, 0, row_count * lax.axis_size("tensor"), axis=0)
    grad_normed_two = lax.psum_scatter(
        jnp.einsum("tf,df->td", piece_rows, w_up, preferred_element_type=jnp.float32).astype(
            jnp.bfloat16
        ),
        "tensor",
        scatter_dimension=0,
        tiled=True,
    ).astype(jnp.float32)
    through_two, gain_two, shift_two = norm_backward(
        grad_normed_two, unit_two, inverse_two, gains[1]
    )
    grad_middle = grad_residual + through_two
    grad_attn_branch = grad_middle.astype(jnp.bfloat16)
    bias_attn = jnp.sum(grad_attn_branch, axis=0, dtype=jnp.float32)
    grad_attn_all = lax.all_gather(grad_attn_branch, "tensor", axis=0, tiled=True)
    grad_out_w = jnp.einsum(
        "tc,td->cd", attended, grad_attn_all, preferred_element_type=jnp.float32
    )
    grad_attended = jnp.einsum(
        "td,cd->tc", grad_attn_all, w_out, preferred_element_type=jnp.float32
    ).astype(jnp.bfloat16)
    grad_query, grad_keys, grad_values = attend_backward(
        query_rows, key_rows, value_rows, segments, log_totals, grad_attended
    )
    grad_projected = jnp.stack((grad_query, grad_keys, grad_values), axis=1)
    grad_qkv = jnp.einsum(
        "td,tsc->dsc", normed_all, grad_projected, preferred_element_type=jnp.float32
    )
    grad_qv_bias = jnp.stack(
        (
            jnp.sum(grad_query, axis=0, dtype=jnp.float32),
            jnp.sum(grad_values, axis=0, dtype=jnp.float32),
        )
    )
    piece_rows = lax.slice_in_dim(grad_projected, 0, row_count * lax.axis_size("tensor"), axis=0)
    grad_normed = lax.psum_scatter(
        jnp.einsum("tsc,dsc->td", piece_rows, w_qkv, preferred_element_type=jnp.float32).astype(
            jnp.bfloat16
        ),
        "tensor",
        scatter_dimension=0,
        tiled=True,
    ).astype(jnp.float32)
    through_one, gain_one, shift_one = norm_backward(grad_normed, unit_one, inverse_one, gains[0])
    grad_input = grad_middle + through_one
    spread = (grad_qkv, grad_qv_bias, grad_out_w, grad_up, grad_up_bias, grad_down)
    shared = (
        jnp.stack((bias_attn, bias_down)),
        jnp.stack((gain_one, gain_two)),
        jnp.stack((shift_one, shift_two)),
    )
    return (grad_input, spread, shared)


def local_general(
    tokens_in,
    segments,
    w_qkv,
    qv_bias,
    w_out,
    w_up,
    up_bias,
    w_down,
    out_bias,
    ln_gain,
    ln_bias,
    cotangent,
):
    layers_total = w_qkv.shape[0]
    all_params = (w_qkv, qv_bias, w_out, w_up, up_bias, w_down, out_bias, ln_gain, ln_bias)
    residual = tokens_in.astype(jnp.float32)
    kept_layers = []
    for layer_index in range(layers_total):
        weights = tuple((member_array[layer_index] for member_array in all_params))
        residual, kept_state = layer_forward(residual, segments, weights)
        kept_layers.append(kept_state)
    out_act = residual.astype(jnp.bfloat16)
    grad_residual = cotangent.astype(jnp.float32)
    spread_layers = []
    shared_layers = []
    for layer_index in reversed(range(layers_total)):
        weights = tuple((member_array[layer_index] for member_array in all_params))
        grad_residual, spread, shared = layer_backward(
            grad_residual, segments, weights, kept_layers[layer_index]
        )
        spread_layers.insert(0, spread)
        shared_layers.insert(0, shared)
    spread_stack = tuple(
        (
            jnp.stack([spread_layers[layer_index][position] for layer_index in range(layers_total)])
            for position in range(6)
        )
    )
    spread_stack = jax.tree.map(
        lambda part: part.astype(jnp.float32), lax.psum(as_sent(spread_stack), "dp")
    )
    shared_stack = tuple(
        (
            jnp.stack([shared_layers[layer_index][position] for layer_index in range(layers_total)])
            for position in range(3)
        )
    )
    shared_stack = lax.psum(shared_stack, ("dp", "tensor"))
    grad_in = grad_residual.astype(jnp.bfloat16)
    return (out_act, grad_in) + tuple(spread_stack) + tuple(shared_stack)


BAND = 256
LANES = 128
VMEM_ASKED = 60 * 2**20


def dot_nt(left, right):
    return lax.dot_general(left, right, (((1,), (1,)), ((), ())), preferred_element_type=jnp.float32)


def dot_tn(left, right):
    return lax.dot_general(left, right, (((0,), (0,)), ((), ())), preferred_element_type=jnp.float32)


def dot_low(left, right):
    return jnp.dot(left, right, preferred_element_type=jnp.float32)


UNITS_LAYER = 12
Y_AHEAD = 1
HOP_BEATS = (1, 3, 5, 6)
IDLE_STEPS = 2
LOADS_AHEAD = 2


def fill_band_bias(segk_ref, bias_ref):
    wide = segk_ref.shape[1]
    values = lax.broadcasted_iota(jnp.int32, (16, wide), 0)
    member = (values == segk_ref[...]).astype(jnp.float32).astype(jnp.bfloat16)
    for block in range(bias_ref.shape[0]):
        queries = member[:, (block + 1) * BAND : (block + 2) * BAND]
        keys = member[:, block * BAND : (block + 2) * BAND]
        row_place = lax.broadcasted_iota(jnp.int32, (BAND, 2 * BAND), 0) + BAND
        column_place = lax.broadcasted_iota(jnp.int32, (BAND, 2 * BAND), 1)
        allowed = (dot_tn(queries, keys) > 0.5) & (column_place <= row_place)
        bias_ref[block] = jnp.where(allowed, 0.0, masked_score)


def band_rows(halo, rows, block):
    if block == 0:
        return jnp.concatenate([halo, rows[0:BAND, :]], axis=0)
    return rows[(block - 1) * BAND : (block + 1) * BAND, :]


def aligned(index, size):
    return pl.ds(pl.multiple_of(index * size, size), size)


def forward_kernel(layers, block, hidden_half, *refs):
    (
        tokens_ref,
        cot_ref,
        segments_ref,
        qkv_own,
        out_own,
        up_own,
        down_own,
        qv_bias_ref,
        up_bias_ref,
        out_bias_ref,
        gain_ref,
        shift_ref,
        out_act_ref,
        cot_out,
        segk_out,
        qkv_other,
        out_other,
        up_other,
        down_other,
        act_out,
        slope_out,
        normed_two_out,
        middle_out,
        attended_out,
        proj_out,
        halo_out,
        totals_out,
        normed_out,
        resid_out,
        tokens_buf,
        segments_in,
        qv_bias_in,
        up_bias_in,
        resid,
        collected,
        normed,
        normed_two,
        proj,
        halo,
        attended,
        totals,
        act_buf,
        slope_buf,
        qkv_weight,
        out_weight,
        up_weight,
        down_weight,
        qkv_arrived,
        out_arrived,
        up_arrived,
        down_arrived,
        bias_buf,
        start_send,
        start_recv,
        swap_sem,
        relay_send,
        relay_recv,
        halo_send_sem,
        halo_recv_sem,
        load_sem,
        store_sem,
        pair_store_sem,
        unit_store_sem,
    ) = refs
    width = 2 * block
    rows_all = tokens_buf.shape[0]
    pairs_half = block // LANES
    blocks_hidden = hidden_half // block
    low = jnp.bfloat16
    place = lax.axis_index("dp")
    y = lax.axis_index("tensor")
    core = place % 2
    x = (place // 2) % 2
    z = place // 4
    z_low = z % 2
    core_partner = {"dp": place + 1 - 2 * core, "tensor": y}
    x_partner = {"dp": place + 2 - 4 * x, "tensor": y}
    y_partner = {"dp": place, "tensor": 1 - y}
    z_partner = {"dp": place + 4 - 8 * z_low, "tensor": y}
    swap_partner = {"dp": place + 1 - 2 * core, "tensor": 1 - y}
    swaps = core + y - 2 * core * y

    barrier = pltpu.get_barrier_semaphore()
    for partner in (core_partner, x_partner, y_partner, z_partner, swap_partner):
        pl.semaphore_signal(barrier, inc=1, device_id=partner, device_id_type=MESH)
    def remote(source, target, send, recv, partner):
        return pltpu.make_async_remote_copy(
            src_ref=source,
            dst_ref=target,
            send_sem=send,
            recv_sem=recv,
            device_id=partner,
            device_id_type=MESH,
        )

    def swap_copy(index, source, target):
        return remote(source, target, start_send.at[index], start_recv.at[index], swap_partner)

    def swap_start(index, source, target):
        @pl.when(swaps == 1)
        def _():
            swap_copy(index, source, target).start()

        @pl.when(swaps == 0)
        def _():
            pltpu.make_async_copy(source, tokens_buf, swap_sem.at[index]).start()

    def swap_wait(index, source, target):
        @pl.when(swaps == 1)
        def _():
            swap_copy(index, source, target).wait()

        @pl.when(swaps == 0)
        def _():
            pltpu.make_async_copy(source, tokens_buf, swap_sem.at[index]).wait()

    segments_copy = remote(
        segments_ref, segments_in, start_send.at[2], start_recv.at[2], core_partner
    )
    qv_copy = remote(qv_bias_ref, qv_bias_in, start_send.at[3], start_recv.at[3], y_partner)
    up_copy = remote(up_bias_ref, up_bias_in, start_send.at[4], start_recv.at[4], y_partner)

    units = layers * UNITS_LAYER

    def for_unit(unit, action):
        layer, inside = unit // UNITS_LAYER, unit % UNITS_LAYER

        @pl.when(inside < 3)
        def _():
            action(*[ref.at[layer, inside] for ref in (qkv_own, qkv_arrived, qkv_other)])

        @pl.when(inside == 3)
        def _():
            action(*[ref.at[layer] for ref in (out_own, out_arrived, out_other)])

        cut = aligned((inside - 4) // 2, block)

        @pl.when((inside >= 4) & (inside % 2 == 0))
        def _():
            action(*[ref.at[layer, :, cut] for ref in (up_own, up_arrived, up_other)])

        @pl.when((inside >= 4) & (inside % 2 == 1))
        def _():
            action(*[ref.at[layer, cut, :] for ref in (down_own, down_arrived, down_other)])

    def hop_copy(hop, unit, source, target):
        partner = (y_partner, x_partner, z_partner, core_partner)[hop]
        return remote(source, target, relay_send.at[hop, unit], relay_recv.at[hop, unit], partner)

    def piece_of(view, hop, short):
        rows = view.shape[0]
        if hop == 3:
            return view.at[aligned(core, rows // 2)]
        if hop == 2:
            return view.at[aligned(2 * core + z_low, rows // 4)]
        if short:
            return view.at[aligned(4 * core + 2 * z_low + x, rows // 8)]
        return view.at[aligned(2 * core + x, rows // 4)]

    def by_length(unit, hop, action):
        if hop == 3:
            action(False)
            return

        whole = (unit % 3 == 0) & (unit > 0)

        @pl.when(jnp.logical_not(whole))
        def _():
            action(True)

        if hop < 2:

            @pl.when(whole)
            def _():
                action(False)

    def hop_start(hop, unit):
        def go(own, arrived, _):
            def one(short):
                source = piece_of(own if hop == 0 else arrived, hop, short)
                hop_copy(hop, unit, source, piece_of(arrived, hop, short)).start()

            by_length(unit, hop, one)

        for_unit(unit, go)

    def hop_wait(hop, unit):
        def one(short):
            piece = piece_of(down_arrived.at[0, pl.ds(0, block), :], hop, short)
            hop_copy(hop, unit, piece, piece).wait()

        by_length(unit, hop, one)

    def when_unit(unit, action):
        @pl.when((unit >= 0) & (unit < units))
        def _():
            action(unit)

    def beat(b):
        def after_y(unit):
            hop_wait(0, unit)
            hop_start(1, unit)

        def after_x(unit):
            hop_wait(1, unit)
            hop_start(2, unit)

        def after_z(unit):
            hop_wait(2, unit)
            hop_start(3, unit)

        def after_all(unit):
            hop_wait(3, unit)

            def keep(_, arrived, other):
                pltpu.make_async_copy(arrived, other, unit_store_sem.at[unit]).start()

            for_unit(unit, keep)

        when_unit(b + Y_AHEAD, lambda unit: hop_start(0, unit))
        for lag, action in zip(HOP_BEATS, (after_y, after_x, after_z, after_all)):
            when_unit(b - lag, action)

    other_step = 2 + pairs_half + IDLE_STEPS
    out_step = other_step + 1 + pairs_half
    norm_two_step = out_step + 1
    ffn_step = norm_two_step + 1
    end_step = ffn_step + 2 * blocks_hidden
    period = end_step + 1
    jobs = layers * period

    def loads(kind, slot, *sources):
        place, targets = {
            "qkv": (blocks_hidden, (qkv_weight,)),
            "out": (blocks_hidden + 1, (out_weight,)),
            "ffn": (slot, (up_weight.at[slot], down_weight.at[slot])),
        }[kind]
        sources = sources or targets
        return [
            pltpu.make_async_copy(source, target, load_sem.at[place, index])
            for index, (source, target) in enumerate(zip(sources, targets))
        ]

    def start_all(copies):
        for copy in copies:
            copy.start()

    def wait_all(copies):
        for copy in copies:
            copy.wait()

    def prefetch(t):
        layer, step = t // period, t % period

        @pl.when(step == 1)
        def _():
            start_all(loads("qkv", 0, qkv_own.at[layer]))

        @pl.when(step == out_step)
        def _():
            start_all(loads("out", 0, out_own.at[layer]))

        @pl.when((step >= ffn_step) & (step < ffn_step + blocks_hidden))
        def _():
            inside = step - ffn_step
            cut = aligned(inside, block)
            start_all(
                loads("ffn", inside, up_own.at[layer, :, cut], down_own.at[layer, cut, :])
            )

    tiles = [slice(r, r + BAND) for r in range(0, rows_all, BAND)]
    fine_tiles = [slice(r, r + LANES) for r in range(0, rows_all, LANES)]

    def normalize(layer, index, target):
        gain = gain_ref[layer, pl.ds(index, 1), :]
        shift = shift_ref[layer, pl.ds(index, 1), :]
        for tile in fine_tiles:
            values, _, _ = layer_norm(resid[tile, :], gain, shift)
            target[tile, :] = values.astype(low)

    def store(index, source, target):
        return pltpu.make_async_copy(source, target, store_sem.at[index])

    def first_stores(layer):
        return [store(0, resid, resid_out.at[layer]), store(1, normed, normed_out.at[layer])]

    def proj_stores(layer, which):
        return [
            store(
                2 + 3 * which + third,
                proj.at[which, third],
                proj_out.at[layer, which, :, pl.ds(third * block, block)],
            )
            for third in range(3)
        ]

    def halo_store(layer, which):
        return store(8 + which, halo.at[layer, which], halo_out.at[layer, which])

    def attended_stores(layer, which):
        return [
            store(10 + which, attended.at[which], attended_out.at[layer, which]),
            store(12 + which, totals.at[which], totals_out.at[layer, which]),
        ]

    def second_stores(layer):
        return [
            store(14, resid, middle_out.at[layer]),
            store(15, normed_two, normed_two_out.at[layer]),
        ]

    def ffn_stores(layer, index, slot):
        which, inside = index // blocks_hidden, index % blocks_hidden
        cut = aligned(inside, block)
        return [
            pltpu.make_async_copy(
                buf.at[slot], out.at[layer, which, :, cut], pair_store_sem.at[slot, kind]
            )
            for kind, (buf, out) in enumerate(((act_buf, act_out), (slope_buf, slope_out)))
        ]

    def halo_copy(layer, which):
        return remote(
            proj.at[which, pl.ds(1, 2), pl.ds(rows_all - BAND, BAND)],
            halo.at[layer, which],
            halo_send_sem.at[layer, which],
            halo_recv_sem.at[layer, which],
            core_partner,
        )

    def first_job(layer):
        normalize(layer, 0, normed)
        start_all(first_stores(layer))

    def qkv_job(layer, which):
        if not which:
            wait_all(loads("qkv", 0))
        bias = qv_bias_in if which else qv_bias_ref
        for third in (1, 2, 0):
            for tile in tiles:
                weight = qkv_arrived[layer, third] if which else qkv_weight[third]
                product = dot_low(normed[tile, :], weight)
                if third != 1:
                    product = product + bias[layer, pl.ds(third // 2, 1), :]
                proj[which, third, tile, :] = product.astype(low)
            if third == 2:

                @pl.when(core == 0)
                def _():
                    halo_copy(layer, which).start()

        start_all(proj_stores(layer, which))

    def attention_job(layer, which, pair):
        @pl.when(pair == 0)
        def _():
            totals[which] = jnp.zeros_like(totals[which])

        lane = lax.broadcasted_iota(jnp.int32, (BAND, LANES), 1)
        here = aligned(pair, LANES)
        for index, tile in reversed(list(enumerate(tiles))):
            if index == 0:

                @pl.when(pair == 0)
                def _():
                    @pl.when(core == 0)
                    def _():
                        halo_copy(layer, which).wait_send()

                    @pl.when(core == 1)
                    def _():
                        halo_copy(layer, which).wait_recv()

                    halo_store(layer, which).start()

            query = proj[which, 0, tile, here]
            first = [halo[layer, which, part, :, here] if index == 0 else None for part in range(2)]
            keys = band_rows(first[0], proj[which, 1, :, here], index)
            values = band_rows(first[1], proj[which, 2, :, here], index)
            parts = []
            kept = totals[which, tile, :]
            for head in range(2):
                mine = (lane // HEAD_DIM) == head
                scores = (
                    dot_nt(jnp.where(mine, query, 0), keys) * HEAD_DIM ** (-0.5) + bias_buf[index]
                )
                highest = jnp.max(scores, axis=-1, keepdims=True)
                raised = jnp.exp(scores - highest)
                summed = jnp.sum(raised, axis=-1, keepdims=True)
                parts.append(dot_low(raised.astype(low), values) / summed)
                kept = jnp.where(lane == 2 * pair + head, highest + jnp.log(summed), kept)
            totals[which, tile, :] = kept
            attended[which, tile, here] = jnp.where(lane < HEAD_DIM, parts[0], parts[1]).astype(low)

        @pl.when(pair == pairs_half - 1)
        def _():
            start_all(attended_stores(layer, which))

    def out_job(layer):
        wait_all(loads("out", 0))
        wait_all(first_stores(layer))
        for which in range(2):
            wait_all(proj_stores(layer, which))
            halo_store(layer, which).wait()
        bias = out_bias_ref[layer, pl.ds(0, 1), :]
        for tile in tiles:
            branch = dot_low(attended[0, tile, :], out_weight[...])
            branch = branch + dot_low(attended[1, tile, :], out_arrived[layer])
            resid[tile, :] = resid[tile, :] + branch + bias

    def second_job(layer):
        normalize(layer, 1, normed_two)
        start_all(second_stores(layer))

    def ffn_job(layer, which, inside, slot):
        index = which * blocks_hidden + inside
        if not which:
            wait_all(loads("ffn", inside))

        @pl.when(index >= 2)
        def _():
            wait_all(ffn_stores(layer, index - 2, slot))

        bias = (up_bias_in if which else up_bias_ref)[pl.ds(layer, 1), aligned(inside, block)]
        cut = aligned(inside, block)
        for tile in tiles:
            up_block = up_arrived[layer, :, cut] if which else up_weight[inside]
            before = dot_low(normed_two[tile, :], up_block) + bias
            square = before * before
            tangent = jnp.tanh(gelu_coeff * before * (1.0 + cubic_coeff * square))
            raised = 0.5 * (1.0 + tangent)
            activated = (before * raised).astype(low)
            act_buf[slot, tile, :] = activated
            slope_buf[slot, tile, :] = (
                raised
                + 0.5
                * before
                * (1.0 - tangent * tangent)
                * gelu_coeff
                * (1.0 + 3.0 * cubic_coeff * square)
            ).astype(low)
            down_block = down_arrived[layer, cut, :] if which else down_weight[inside]
            product = dot_low(activated, down_block)
            if which:
                collected[tile, :] = collected[tile, :] + product
                continue

            @pl.when(inside == 0)
            def _(tile=tile, product=product):
                collected[tile, :] = product

            @pl.when(inside > 0)
            def _(tile=tile, product=product):
                collected[tile, :] = collected[tile, :] + product

        start_all(ffn_stores(layer, index, slot))

    def end_job(layer, slot):
        wait_all(ffn_stores(layer, 2 * blocks_hidden - 2, slot))
        wait_all(ffn_stores(layer, 2 * blocks_hidden - 1, 1 - slot))
        wait_all(second_stores(layer))
        for which in range(2):
            wait_all(attended_stores(layer, which))
        bias = out_bias_ref[layer, pl.ds(1, 1), :]
        for tile in tiles:
            resid[tile, :] = resid[tile, :] + collected[tile, :] + bias

    def job(t):
        slot = t % 2
        layer, step = t // period, t % period

        def at(first, count, action):
            @pl.when((step >= first) & (step < first + count))
            def _():
                action(step - first)

        at(0, 1, lambda _: first_job(layer))
        later = (layer > 0).astype(jnp.int32)
        other_at = other_step + later * (2 - other_step)
        other_first = other_step + 1 + later * (2 + pairs_half - other_step)
        at(1, 1, lambda _: qkv_job(layer, 0))
        at(2 + later, pairs_half, lambda pair: attention_job(layer, 0, pair))
        at(other_at, 1, lambda _: qkv_job(layer, 1))
        at(other_first, pairs_half, lambda pair: attention_job(layer, 1, pair))
        at(out_step, 1, lambda _: out_job(layer))
        at(norm_two_step, 1, lambda _: second_job(layer))
        at(ffn_step, blocks_hidden, lambda inside: ffn_job(layer, 0, inside, slot))
        at(ffn_step + blocks_hidden, blocks_hidden, lambda inside: ffn_job(layer, 1, inside, slot))
        at(end_step, 1, lambda _: end_job(layer, slot))

    for ahead in range(LOADS_AHEAD):
        prefetch(jnp.int32(ahead))
    halo[...] = jnp.zeros_like(halo)
    pl.semaphore_wait(barrier, 5)
    swap_start(0, tokens_ref, tokens_buf)
    segments_copy.start()
    qv_copy.start()
    up_copy.start()
    for unit in range(Y_AHEAD):
        hop_start(0, unit)
    segments_copy.wait()
    window = jnp.where(core == y, segments_ref[...], segments_in[...])

    @pl.when(core == 0)
    def _():
        segk_out[:, 0:BAND] = jnp.full((1, BAND), -1, jnp.int32)
        segk_out[:, BAND:] = window[:, 0:rows_all]

    @pl.when(core == 1)
    def _():
        segk_out[...] = window[:, rows_all - BAND :]

    fill_band_bias(segk_out, bias_buf)
    qv_copy.wait()
    up_copy.wait()
    swap_wait(0, tokens_ref, tokens_buf)
    for tile in tiles:
        resid[tile, :] = tokens_buf[tile, :].astype(jnp.float32)
    cot_tick = period + other_step + 4

    def past(t, begin):
        return (t - begin) * (t > begin).astype(jnp.int32)

    def beat_at(t):
        return (10 * t - 4 * past(t, 12) - past(t, 22)) // 10

    def tick(t, carry):
        @pl.when((t == 0) | (beat_at(t) != beat_at(t - 1)))
        def _():
            beat(beat_at(t))

        @pl.when(t == cot_tick)
        def _():
            swap_start(1, cot_ref, cot_out)

        @pl.when((t == cot_tick + 4) & (swaps == 0))
        def _():
            pltpu.make_async_copy(cot_ref, tokens_buf, swap_sem.at[1]).wait()
            pltpu.make_async_copy(tokens_buf, cot_out, swap_sem.at[1]).start()

        @pl.when(t + LOADS_AHEAD < jobs)
        def _():
            prefetch(t + LOADS_AHEAD)

        job(t)
        return carry

    lax.fori_loop(0, jobs, tick, 0)
    for tile in tiles:
        normed_two[tile, :] = resid[tile, :].astype(low)
    last_store = store(0, normed_two, out_act_ref)
    last_store.start()
    last_store.wait()
    swap_wait(1, cot_ref, cot_out)
    for unit in range(units):
        block_ref = down_arrived.at[0, pl.ds(0, block), :]
        pltpu.make_async_copy(block_ref, block_ref, unit_store_sem.at[unit]).wait()


def run_forward(tokens, cotangent, segments, weights, biases, out_bias, gain, shift, block):
    rows, width = tokens.shape
    layers, hidden_half = weights[-1].shape[0], weights[-1].shape[1]
    low, wide = jnp.bfloat16, jnp.float32
    anywhere = pl.BlockSpec(memory_space=pl.ANY)
    in_vmem = pl.BlockSpec(memory_space=pltpu.VMEM)
    vmem = pltpu.VMEM
    units = layers * UNITS_LAYER
    shape = jax.ShapeDtypeStruct
    saved = [
        shape((layers, 2, rows, hidden_half), low),
        shape((layers, 2, rows, hidden_half), low),
        shape((layers, rows, width), low),
        shape((layers, rows, width), wide),
        shape((layers, 2, rows, block), low),
        shape((layers, 2, rows, 3 * block), low),
        shape((layers, 2, 2, BAND, block), low),
        shape((layers, 2, rows, LANES), wide),
        shape((layers, rows, width), low),
        shape((layers, rows, width), wide),
    ]
    others = [shape(member.shape, low) for member in weights]
    return pl.pallas_call(
        functools.partial(forward_kernel, layers, block, hidden_half),
        in_specs=[anywhere] * 2 + [in_vmem] + [anywhere] * 4 + [in_vmem] * 5,
        out_specs=[anywhere] * 2 + [in_vmem] + [anywhere] * (len(others) + len(saved)),
        out_shape=[
            shape((rows, width), low),
            shape((rows, width), low),
            shape((1, rows + BAND), jnp.int32),
        ]
        + others
        + saved,
        scratch_shapes=[
            vmem((rows, width), low),
            vmem(segments.shape, jnp.int32),
            vmem(biases[0].shape, wide),
            vmem(biases[1].shape, wide),
            vmem((rows, width), wide),
            vmem((rows, width), wide),
            vmem((rows, width), low),
            vmem((rows, width), low),
            vmem((2, 3, rows, block), low),
            vmem((layers, 2, 2, BAND, block), low),
            vmem((2, rows, block), low),
            vmem((2, rows, LANES), wide),
            vmem((2, rows, block), low),
            vmem((2, rows, block), low),
            vmem((3, width, block), low),
            vmem((block, width), low),
            vmem((hidden_half // block, width, block), low),
            vmem((hidden_half // block, block, width), low),
        ]
        + [vmem(member.shape, low) for member in weights]
        + [
            vmem((rows // BAND, BAND, 2 * BAND), wide),
            pltpu.SemaphoreType.DMA((5,)),
            pltpu.SemaphoreType.DMA((5,)),
            pltpu.SemaphoreType.DMA((2,)),
            pltpu.SemaphoreType.DMA((4, units)),
            pltpu.SemaphoreType.DMA((4, units)),
            pltpu.SemaphoreType.DMA((layers, 2)),
            pltpu.SemaphoreType.DMA((layers, 2)),
            pltpu.SemaphoreType.DMA((hidden_half // block + 2, 2)),
            pltpu.SemaphoreType.DMA((16,)),
            pltpu.SemaphoreType.DMA((2, 2)),
            pltpu.SemaphoreType.DMA((units,)),
        ],
        compiler_params=pltpu.CompilerParams(
            collective_id=1, has_side_effects=True, vmem_limit_bytes=VMEM_ASKED
        ),
        name="forward",
    )(tokens, cotangent, segments, *weights, *biases, out_bias, gain, shift)


SLOTS = 8
CORE_SLOTS = 4
RESULT_SLOTS = 11
STAGED = 2
FIRST = 0
LAGS = dict(
    core=1, first=3, second=5, third=7, fourth=9, fifth=11, sixth=13, whole=14, stored=15
)
VECTOR_STEP = 3
VECTOR_ROWS = 12
MESH = pl.DeviceIdType.MESH
FFN_STEPS = 4
QKV_STEPS = 3


def added(left, right):
    return (left.astype(jnp.float32) + right.astype(jnp.float32)).astype(jnp.bfloat16)


def backward_kernel(layers, block, hidden_half, *refs):
    (
        cot_ref,
        gain_ref,
        segk_ref,
        out_act_ref,
        act_ref,
        slope_ref,
        normed_two_ref,
        middle_ref,
        attended_ref,
        proj_ref,
        halo_ref,
        totals_ref,
        normed_ref,
        resid_ref,
        qkv_own,
        qkv_other,
        out_own,
        out_other,
        up_own,
        up_other,
        down_own,
        down_other,
        out_act_out,
        grad_in_ref,
        out_down,
        out_up,
        out_out,
        out_qkv,
        vector_out,
        grad_branch,
        grad_attn,
        grad_before,
        grad_proj,
        grad_res,
        collected,
        grad_attended,
        qkv_buf,
        halo_buf,
        totals_buf,
        kept_kv,
        halo_send,
        halo_in,
        rows_weight,
        columns_weight,
        slope_buf,
        wide_buf,
        bias_buf,
        sums_buf,
        pair_buf,
        one_buf,
        part_buf,
        core_in,
        sent,
        held,
        kept,
        first_in,
        second_in,
        third_in,
        result,
        vec_in,
        load_sem,
        io_sem,
        halo_send_sem,
        halo_recv_sem,
        staged_sem,
        send_sems,
        recv_sems,
        store_sem,
        vec_send,
        vec_recv,
        swap_send,
        swap_recv,
    ) = refs
    half, quarter = block // 2, block // 4
    width = 2 * block
    rows_all = grad_branch.shape[0]
    pairs_half = block // LANES
    pairs = 2 * pairs_half
    low = jnp.bfloat16
    place = lax.axis_index("dp")
    y = lax.axis_index("tensor")
    core = place % 2
    x = (place // 2) % 2
    z = place // 4
    z_low = z % 2
    inner = (z + 1) // 2 % 2
    core_partner = {"dp": place + 1 - 2 * core, "tensor": y}
    x_partner = {"dp": place + 2 - 4 * x, "tensor": y}
    y_partner = {"dp": place, "tensor": 1 - y}
    z_partner = {"dp": place + 4 - 8 * z_low, "tensor": y}
    middle_partner = {"dp": place + 4 * (3 - 2 * z), "tensor": y}
    swap_partner = {"dp": place + 1 - 2 * core, "tensor": 1 - y}

    barrier = pltpu.get_barrier_semaphore()
    for partner in (core_partner, x_partner, y_partner, z_partner, swap_partner):
        pl.semaphore_signal(barrier, inc=1, device_id=partner, device_id_type=MESH)

    @pl.when(inner == 1)
    def _():
        pl.semaphore_signal(barrier, inc=1, device_id=middle_partner, device_id_type=MESH)

    blocks_hidden = hidden_half // block
    plan = (
        ("rows", blocks_hidden, 2),
        ("columns", 2, blocks_hidden),
        ("rows", 1, 2),
        ("columns", 2, 3),
    )
    starts = []
    per_layer = 0
    for _, down_count, across_count in plan:
        starts.append(per_layer)
        per_layer += down_count * across_count
    chunks = layers * per_layer
    out_refs = (out_down, out_up, out_out, out_qkv)

    def block_of(index):
        return pl.ds(pl.multiple_of(index * block, block), block)

    def for_matrix(chunk, action):
        layer = layers - 1 - chunk // per_layer
        inside = chunk % per_layer
        for member, (_, down_count, across_count) in enumerate(plan):
            begin = starts[member]

            @pl.when((inside >= begin) & (inside < begin + down_count * across_count))
            def _(member=member, begin=begin, across_count=across_count):
                local = inside - begin
                action(member, layer, local // across_count, local % across_count)

    def operands_of(member, layer, i, j):
        if member == 0:
            return (
                grad_branch.at[:, block_of(j)],
                act_ref.at[layer, 0, :, block_of(i)],
                act_ref.at[layer, 1, :, block_of(i)],
            )
        if member == 1:
            return (
                normed_two_ref.at[layer, :, block_of(i)],
                grad_before.at[j // 2, :, block_of(j % 2)],
                grad_before.at[blocks_hidden // 2 + j // 2, :, block_of(j % 2)],
            )
        if member == 2:
            return (
                grad_attn.at[:, block_of(j)],
                attended_ref.at[layer, 0, :, block_of(i)],
                attended_ref.at[layer, 1, :, block_of(i)],
            )
        return (
            normed_ref.at[layer, :, block_of(i)],
            grad_proj.at[:, block_of(j)],
            grad_proj.at[:, block_of(3 + j)],
        )

    def staged_copies(chunk, shared, own, other):
        slot = chunk % STAGED
        return (
            pltpu.make_async_copy(own, pair_buf.at[slot, 0], staged_sem.at[slot, 0]),
            pltpu.make_async_copy(other, pair_buf.at[slot, 1], staged_sem.at[slot, 1]),
            pltpu.make_async_copy(shared, one_buf.at[slot], staged_sem.at[slot, 2]),
        )

    def stage_operands(chunk):
        def action(member, layer, i, j):
            for copy in staged_copies(chunk, *operands_of(member, layer, i, j)):
                copy.start()

        for_matrix(chunk, action)

    def remote(step, chunk, source, target, partner):
        slot = chunk % SLOTS
        return pltpu.make_async_remote_copy(
            src_ref=source,
            dst_ref=target,
            send_sem=send_sems.at[step, slot],
            recv_sem=recv_sems.at[step, slot],
            device_id=partner,
            device_id_type=MESH,
        )

    def x_first(chunk):
        left = chunks - 1 - chunk
        near = (chunk <= 10) & (chunk % 2 == 0) | (left <= 10) & (left % 2 == 0)
        far = (chunk > 10) & (left > 10)
        third = far & (chunk % 3 == 1) & ((chunk < 18) | (left < 19))
        fourth = far & (chunk % 4 == 0) & (chunk >= 18) & (left >= 19)
        return near | third | fourth

    def core_copy(chunk):
        return remote(
            0,
            chunk,
            part_buf.at[chunk % STAGED, :, aligned(1 - core, half)],
            core_in.at[chunk % CORE_SLOTS],
            core_partner,
        )

    low_middle = z - 1
    far_middle = 2 - z

    def first_copy(chunk, partner):
        slot = chunk % SLOTS
        return remote(1, chunk, sent.at[slot], first_in.at[slot], partner)

    def y_copy(chunk):
        slot = chunk % SLOTS
        return remote(2, chunk, kept.at[slot, 1], second_in.at[slot, 0], y_partner)

    def pair_copy(chunk):
        slot = chunk % SLOTS
        return remote(2, chunk, kept.at[slot], second_in.at[slot], z_partner)

    def single_copy(chunk):
        slot = chunk % SLOTS
        return remote(3, chunk, kept.at[slot, 0], third_in.at[slot, 0], z_partner)

    def split_copy(chunk):
        slot = chunk % SLOTS
        return remote(3, chunk, kept.at[slot, far_middle], third_in.at[slot, 0], middle_partner)

    def middle_copy(chunk):
        slot = chunk % SLOTS
        return remote(4, chunk, kept.at[slot, 0], third_in.at[slot, 1], middle_partner)

    def across_copy(chunk):
        slot = chunk % SLOTS
        return remote(4, chunk, kept.at[slot, low_middle], third_in.at[slot, 1], x_partner)

    def result_copy(step, chunk, rows, partner):
        piece = result.at[chunk % RESULT_SLOTS, rows]
        return remote(step, chunk, piece, piece, partner)

    x_rows = aligned(2 * core + x, quarter)
    core_rows = aligned(core, half)

    def middle_rows():
        return aligned(2 * core + low_middle, quarter)

    def store_copy(chunk, target):
        slot = chunk % RESULT_SLOTS
        return pltpu.make_async_copy(result.at[slot], target, store_sem.at[slot])

    def multiply(chunk):
        slot = chunk % STAGED
        for copy in staged_copies(chunk, one_buf.at[slot], pair_buf.at[slot, 0], pair_buf.at[slot, 1]):
            copy.wait()
        inside = chunk % per_layer
        by_rows = (inside < starts[1]) | ((inside >= starts[2]) & (inside < starts[3]))

        @pl.when(by_rows)
        def _():
            single = one_buf[slot]
            for which in range(2):
                part_buf[slot, which] = dot_tn(pair_buf[slot, which], single).astype(low)

        @pl.when(jnp.logical_not(by_rows))
        def _():
            single = one_buf[slot]
            for which in range(2):
                part_buf[slot, which] = dot_tn(single, pair_buf[slot, which]).astype(low)

        core_copy(chunk).start()

    def branch(chunk, by_x, by_y):
        is_x = x_first(chunk)

        @pl.when(is_x)
        def _():
            by_x()

        @pl.when(jnp.logical_not(is_x))
        def _():
            by_y()

    def on_middle(action):
        @pl.when(inner == 1)
        def _():
            action()

    def by_place(at_end, at_middle):
        @pl.when(inner == 0)
        def _():
            at_end()

        on_middle(at_middle)

    def after_core(chunk):
        slot, core_slot, part_slot = chunk % SLOTS, chunk % CORE_SLOTS, chunk % STAGED
        core_copy(chunk).wait()
        is_x = x_first(chunk).astype(jnp.int32)

        def summed(which, row):
            near = part_buf[part_slot, which, aligned(2 * core + row, quarter), :]
            return added(near, core_in[core_slot, which, aligned(row, quarter), :])

        for index in range(2):
            sent[slot, index] = summed(
                is_x * index + (1 - is_x), is_x * (1 - x) + (1 - is_x) * index
            )
        branch(
            chunk,
            lambda: first_copy(chunk, x_partner).start(),
            lambda: first_copy(chunk, y_partner).start(),
        )
        for index in range(2):
            held[slot, index] = summed(is_x * index, is_x * x + (1 - is_x) * index)

    def after_first(chunk):
        slot = chunk % SLOTS
        first_copy(chunk, y_partner).wait()
        for index in (1, 0):
            kept[slot, index] = added(held[slot, index], first_in[slot, index])

        def by_y():
            @pl.when(inner == 0)
            def _():
                pair_copy(chunk).start()

        branch(chunk, lambda: y_copy(chunk).start(), by_y)

    def after_second(chunk):
        slot = chunk % SLOTS

        def by_x():
            y_copy(chunk).wait()
            kept[slot, 0] = added(kept[slot, 0], second_in[slot, 0])

            @pl.when(inner == 0)
            def _():
                single_copy(chunk).start()

        def at_middle():
            pair_copy(chunk).wait_recv()
            kept[slot, far_middle] = added(kept[slot, far_middle], second_in[slot, far_middle])
            split_copy(chunk).start()
            kept[slot, low_middle] = added(kept[slot, low_middle], second_in[slot, low_middle])

        branch(chunk, by_x, lambda: by_place(lambda: pair_copy(chunk).wait_send(), at_middle))

    def after_third(chunk):
        slot = chunk % SLOTS

        def one_at_middle():
            single_copy(chunk).wait_recv()
            kept[slot, 0] = added(kept[slot, 0], third_in[slot, 0])
            middle_copy(chunk).start()

        def by_y():
            split_copy(chunk).wait()
            kept[slot, low_middle] = added(kept[slot, low_middle], third_in[slot, 0])
            across_copy(chunk).start()

        branch(
            chunk,
            lambda: by_place(lambda: single_copy(chunk).wait_send(), one_at_middle),
            lambda: on_middle(by_y),
        )

    def after_fourth(chunk):
        slot, result_slot = chunk % SLOTS, chunk % RESULT_SLOTS

        def by_x():
            middle_copy(chunk).wait()
            result[result_slot, x_rows, :] = added(kept[slot, 0], third_in[slot, 1])
            result_copy(5, chunk, x_rows, z_partner).start()

        def by_y():
            across_copy(chunk).wait()
            result[result_slot, middle_rows(), :] = added(
                kept[slot, low_middle], third_in[slot, 1]
            )
            result_copy(5, chunk, middle_rows(), middle_partner).start()

        branch(chunk, lambda: on_middle(by_x), lambda: on_middle(by_y))

    def after_fifth(chunk):
        def by_x():
            back = result_copy(5, chunk, x_rows, z_partner)
            by_place(back.wait_recv, back.wait_send)
            result_copy(6, chunk, x_rows, x_partner).start()

        def by_y():
            result_copy(5, chunk, middle_rows(), middle_partner).wait()
            result_copy(6, chunk, core_rows, z_partner).start()

        branch(chunk, by_x, lambda: on_middle(by_y))

    def after_sixth(chunk):
        def by_y():
            back = result_copy(6, chunk, core_rows, z_partner)
            by_place(back.wait_recv, back.wait_send)

        branch(chunk, lambda: result_copy(6, chunk, x_rows, x_partner).wait(), by_y)
        result_copy(7, chunk, core_rows, core_partner).start()

    def after_whole(chunk):
        result_copy(7, chunk, core_rows, core_partner).wait()

        def action(member, layer, i, j):
            if member == 3:
                target = out_qkv.at[layer, j, block_of(i)]
            else:
                target = out_refs[member].at[layer, block_of(i), block_of(j)]
            store_copy(chunk, target).start()

        for_matrix(chunk, action)

    def after_store(chunk):
        store_copy(chunk, result.at[chunk % RESULT_SLOTS]).wait()

    vector_partners = (core_partner, y_partner, x_partner, z_partner, middle_partner, z_partner)

    def vector_copy(step):
        target = vec_in.at[min(step, 4)]
        return pltpu.make_async_remote_copy(
            src_ref=vector_out,
            dst_ref=target,
            send_sem=vec_send.at[step],
            recv_sem=vec_recv.at[step],
            device_id=vector_partners[step],
            device_id_type=MESH,
        )

    def add_vector(step):
        vector_out[...] = vector_out[...] + vec_in[step]

    def vector_tick(step):
        if step == 0:
            vector_copy(0).start()
        elif step <= 3:
            vector_copy(step - 1).wait()
            add_vector(step - 1)
            if step < 3:
                vector_copy(step).start()
            else:

                @pl.when(inner == 0)
                def _():
                    vector_copy(3).start()

        elif step == 4:

            @pl.when(inner == 0)
            def _():
                vector_copy(3).wait_send()

            @pl.when(inner == 1)
            def _():
                vector_copy(3).wait_recv()
                add_vector(3)
                vector_copy(4).start()

        elif step == 5:

            @pl.when(inner == 1)
            def _():
                vector_copy(4).wait()
                add_vector(4)
                vector_copy(5).start()

        else:

            @pl.when(inner == 1)
            def _():
                vector_copy(5).wait_send()

            @pl.when(inner == 0)
            def _():
                vector_copy(5).wait_recv()
                vector_out[...] = vec_in[4]

    norm_two_step = FFN_STEPS
    out_step = norm_two_step + 1
    attention_step = out_step + 1
    qkv_step = attention_step + pairs + 1
    norm_one_step = qkv_step + QKV_STEPS
    period = norm_one_step + 1
    jobs = layers * period
    hidden_step = 2 * hidden_half // FFN_STEPS

    def loads(kind, slot, *sources):
        targets = {
            "ffn": (rows_weight.at[slot], columns_weight.at[slot], slope_buf.at[slot]),
            "wide": (wide_buf,),
            "out": (rows_weight.at[slot, pl.ds(0, block)], rows_weight.at[slot, pl.ds(block, block)]),
            "attention": (
                qkv_buf.at[slot, 0],
                qkv_buf.at[slot, 1],
                qkv_buf.at[slot, 2],
                halo_buf.at[slot, 0],
                halo_buf.at[slot, 1],
                totals_buf.at[slot],
            ),
            "qkv": (
                columns_weight.at[slot, :, pl.ds(0, block)],
                columns_weight.at[slot, :, pl.ds(block, block)],
            ),
        }[kind]
        sources = sources or targets
        return [
            pltpu.make_async_copy(source, target, load_sem.at[slot, index])
            for index, (source, target) in enumerate(zip(sources, targets))
        ]

    def prefetch(t):
        slot = t % 2
        layer = layers - 1 - t // period
        step = t % period

        for which, (up_ref, down_ref) in enumerate(((up_own, down_own), (up_other, down_other))):

            @pl.when((step < FFN_STEPS) & (step // (FFN_STEPS // 2) == which))
            def _(which=which, up_ref=up_ref, down_ref=down_ref):
                cut = aligned(step % (FFN_STEPS // 2), hidden_step)
                for copy in loads(
                    "ffn",
                    slot,
                    down_ref.at[layer, cut, :],
                    up_ref.at[layer, :, cut],
                    slope_ref.at[layer, which, :, cut],
                ):
                    copy.start()

        for at, source in ((norm_two_step, middle_ref), (norm_one_step, resid_ref)):

            @pl.when(step == at)
            def _(source=source):
                for copy in loads("wide", slot, source.at[layer]):
                    copy.start()

        @pl.when(step == out_step)
        def _():
            for copy in loads("out", slot, out_own.at[layer], out_other.at[layer]):
                copy.start()

        @pl.when((step >= attention_step) & (step < attention_step + pairs))
        def _():
            pair = step - attention_step
            which, inside = pair // pairs_half, pair % pairs_half

            def lanes(third):
                return aligned(third * pairs_half + inside, LANES)

            for copy in loads(
                "attention",
                slot,
                *[proj_ref.at[layer, which, :, lanes(third)] for third in range(3)],
                *[halo_ref.at[layer, which, third, :, lanes(0)] for third in range(2)],
                totals_ref.at[layer, which],
            ):
                copy.start()

        @pl.when((step >= qkv_step) & (step < qkv_step + QKV_STEPS))
        def _():
            for part in range(2):
                index = 2 * (step - qkv_step) + part
                for which, source in enumerate((qkv_own, qkv_other)):

                    @pl.when(index // 3 == which)
                    def _(part=part, index=index, source=source):
                        pltpu.make_async_copy(
                            source.at[layer, index % 3],
                            columns_weight.at[slot, :, pl.ds(part * block, block)],
                            load_sem.at[slot, part],
                        ).start()

    def wait_loads(kind, slot):
        for copy in loads(kind, slot):
            copy.wait()

    tiles = [slice(r, r + BAND) for r in range(0, rows_all, BAND)]
    fine_tiles = [slice(r, r + LANES) for r in range(0, rows_all, LANES)]

    def vector_row(layer, row):
        return pl.ds(layer * VECTOR_ROWS + row, 1)

    def column_sum(values):
        return jnp.sum(values.astype(jnp.float32), axis=0, keepdims=True)

    def ffn_job(layer, step, slot):
        wait_loads("ffn", slot)
        sums = 0.0
        for tile in tiles:
            grad_hidden = dot_nt(grad_branch[tile, :], rows_weight[slot])
            before = (grad_hidden * slope_buf[slot, tile, :].astype(jnp.float32)).astype(low)
            grad_before[step, tile, :] = before
            sums = sums + column_sum(before)
            product = dot_nt(before, columns_weight[slot])

            @pl.when(step == 0)
            def _(tile=tile, product=product):
                collected[tile, :] = product

            @pl.when(step > 0)
            def _(tile=tile, product=product):
                collected[tile, :] = collected[tile, :] + product

        per_half = FFN_STEPS // 2
        which = step // per_half
        owner = which + y - 2 * which * y
        vector_out[vector_row(layer, 2 + owner * per_half + step % per_half), :] = sums

    def norm_job(layer, index, slot):
        wait_loads("wide", slot)
        gain = gain_ref[layer, pl.ds(index, 1), :]
        gain_sum, shift_sum, attn_sum, branch_sum = 0.0, 0.0, 0.0, 0.0
        for tile in fine_tiles:
            incoming = collected[tile, :]
            values = wide_buf[tile, :]
            average = jnp.mean(values, axis=-1, keepdims=True)
            centred = values - average
            inverse = lax.rsqrt(jnp.mean(centred * centred, axis=-1, keepdims=True) + epsilon)
            unit = centred * inverse
            scaled = incoming * gain
            first_mean = jnp.mean(scaled, axis=-1, keepdims=True)
            second_mean = jnp.mean(scaled * unit, axis=-1, keepdims=True)
            total = grad_res[tile, :] + inverse * (scaled - first_mean - unit * second_mean)
            grad_res[tile, :] = total
            rounded = total.astype(low)
            gain_sum = gain_sum + column_sum(incoming * unit)
            shift_sum = shift_sum + column_sum(incoming)
            if index == 1:
                attn_sum = attn_sum + column_sum(rounded)
                branch_sum = branch_sum + column_sum(grad_branch[tile, :])
                grad_attn[tile, :] = rounded
            else:
                grad_branch[tile, :] = rounded
        vector_out[vector_row(layer, 8 + index), :] = gain_sum
        vector_out[vector_row(layer, 10 + index), :] = shift_sum
        if index == 1:
            vector_out[vector_row(layer, 6), :] = attn_sum
            vector_out[vector_row(layer, 7), :] = branch_sum

    def out_job(slot):
        wait_loads("out", slot)
        for tile in tiles:
            grad_attended[tile, :] = dot_nt(grad_attn[tile, :], rows_weight[slot]).astype(low)

    def halo_copy(pair):
        return pltpu.make_async_remote_copy(
            src_ref=halo_send.at[pair % 2],
            dst_ref=halo_in.at[pair],
            send_sem=halo_send_sem.at[pair],
            recv_sem=halo_recv_sem.at[pair],
            device_id=core_partner,
            device_id_type=MESH,
        )

    def proj_lanes(pair, third):
        which, inside = pair // pairs_half, pair % pairs_half
        return aligned(which * 3 * pairs_half + third * pairs_half + inside, LANES)

    def attention_job(pair, slot):
        wait_loads("attention", slot)
        lane = lax.broadcasted_iota(jnp.int32, (BAND, LANES), 1)
        scaling = HEAD_DIM ** (-0.5)
        count = len(tiles)
        key_parts = [None] * (count + 1)
        value_parts = [None] * (count + 1)
        here = aligned(pair, LANES)
        for index, tile in enumerate(tiles):
            query = qkv_buf[slot, 0, tile, :]
            grad = grad_attended[tile, here]
            keys = band_rows(halo_buf[slot, 0], qkv_buf[slot, 1], index)
            values = band_rows(halo_buf[slot, 1], qkv_buf[slot, 2], index)
            grad_query = []
            grad_keys = 0.0
            grad_values = 0.0
            for head in range(2):
                mine = (lane // HEAD_DIM) == head
                query_head = jnp.where(mine, query, 0)
                grad_head = jnp.where(mine, grad, 0)
                scores = dot_nt(query_head, keys) * scaling + bias_buf[index]
                total = jnp.sum(
                    jnp.where(
                        lane == 2 * (pair % pairs_half) + head, totals_buf[slot, tile, :], 0.0
                    ),
                    axis=-1,
                    keepdims=True,
                )
                exact = jnp.exp(scores - total)
                grad_probs = dot_nt(grad_head, values)
                row_terms = jnp.sum(exact * grad_probs, axis=-1, keepdims=True)
                grad_scores = (exact * (grad_probs - row_terms)).astype(low)
                grad_query.append(jnp.dot(grad_scores, keys, preferred_element_type=jnp.float32))
                grad_keys = grad_keys + dot_tn(grad_scores, query_head)
                grad_values = grad_values + dot_tn(exact.astype(low), grad_head)
            grad_proj[tile, proj_lanes(pair, 0)] = (
                jnp.where(lane < HEAD_DIM, grad_query[0], grad_query[1]) * scaling
            ).astype(low)
            grad_keys = grad_keys * scaling
            for part in range(2):
                cut = slice(part * BAND, (part + 1) * BAND)
                old_k, old_v = key_parts[index + part], value_parts[index + part]
                key_parts[index + part] = grad_keys[cut] if old_k is None else old_k + grad_keys[cut]
                value_parts[index + part] = (
                    grad_values[cut] if old_v is None else old_v + grad_values[cut]
                )
        for index in range(count - 1):
            grad_proj[tiles[index], proj_lanes(pair, 1)] = key_parts[index + 1].astype(low)
            grad_proj[tiles[index], proj_lanes(pair, 2)] = value_parts[index + 1].astype(low)
        kept_kv[pair % 2, 0] = key_parts[count]
        kept_kv[pair % 2, 1] = value_parts[count]

        @pl.when(core == 1)
        def _():
            halo_send[pair % 2, 0] = key_parts[0].astype(low)
            halo_send[pair % 2, 1] = value_parts[0].astype(low)
            halo_copy(pair).start()

    def finish_pair(pair):
        last = tiles[-1]

        @pl.when(core == 0)
        def _():
            halo_copy(pair).wait_recv()
            for third in range(2):
                grad_proj[last, proj_lanes(pair, third + 1)] = (
                    kept_kv[pair % 2, third] + halo_in[pair, third].astype(jnp.float32)
                ).astype(low)

        @pl.when(core == 1)
        def _():
            halo_copy(pair).wait_send()
            for third in range(2):
                grad_proj[last, proj_lanes(pair, third + 1)] = kept_kv[pair % 2, third].astype(low)

    def qkv_job(layer, step, slot):
        wait_loads("qkv", slot)
        sums = 0.0
        for tile in tiles:
            grad = grad_proj[tile, aligned(step, width)]
            sums = sums + column_sum(grad)
            product = dot_nt(grad, columns_weight[slot])

            @pl.when(step == 0)
            def _(tile=tile, product=product):
                collected[tile, :] = product

            @pl.when(step > 0)
            def _(tile=tile, product=product):
                collected[tile, :] = collected[tile, :] + product

        sums_buf[...] = sums
        for when, part, which, row in ((0, 0, 0, 0), (1, 0, 0, 1), (1, 1, 1, 0), (2, 1, 1, 1)):

            @pl.when(step == when)
            def _(part=part, which=which, row=row):
                owner = 1 - y if which else y
                vector_out[vector_row(layer, row), block_of(owner)] = sums_buf[
                    :, part * block : (part + 1) * block
                ]

    def job(t):
        slot = t % 2
        layer = layers - 1 - t // period
        step = t % period

        @pl.when(step < FFN_STEPS)
        def _():
            ffn_job(layer, step, slot)

        @pl.when(step == norm_two_step)
        def _():
            norm_job(layer, 1, slot)

        @pl.when(step == out_step)
        def _():
            out_job(slot)

        @pl.when((step > attention_step) & (step <= attention_step + pairs))
        def _():
            finish_pair(step - attention_step - 1)

        @pl.when((step >= attention_step) & (step < attention_step + pairs))
        def _():
            attention_job(step - attention_step, slot)

        @pl.when((step >= qkv_step) & (step < qkv_step + QKV_STEPS))
        def _():
            qkv_job(layer, step - qkv_step, slot)

        @pl.when(step == norm_one_step)
        def _():
            norm_job(layer, 0, slot)

    stages = (
        (LAGS["core"], after_core),
        (0, multiply),
        (None, job),
        (LAGS["first"], after_first),
        (LAGS["second"], after_second),
        (LAGS["third"], after_third),
        (LAGS["fourth"], after_fourth),
        (LAGS["fifth"], after_fifth),
        (LAGS["sixth"], after_sixth),
        (LAGS["stored"], after_store),
        (LAGS["whole"], after_whole),
    )

    swaps = core + y - 2 * core * y

    def swap_copy(index, source, target):
        return pltpu.make_async_remote_copy(
            src_ref=source,
            dst_ref=target,
            send_sem=swap_send.at[index],
            recv_sem=swap_recv.at[index],
            device_id=swap_partner,
            device_id_type=MESH,
        )

    def swap_start(index, source, target):
        @pl.when(swaps == 1)
        def _():
            swap_copy(index, source, target).start()

        if index:

            @pl.when(swaps == 0)
            def _():
                pltpu.make_async_copy(source, target, io_sem.at[1]).start()

    def swap_wait(index, source, target):
        @pl.when(swaps == 1)
        def _():
            swap_copy(index, source, target).wait()

        if index:

            @pl.when(swaps == 0)
            def _():
                pltpu.make_async_copy(source, target, io_sem.at[1]).wait()

    first_load = pltpu.make_async_copy(cot_ref, grad_branch, io_sem.at[0])
    first_load.start()
    first_load.wait()
    stage_operands(0)
    prefetch(0)

    @pl.when(inner == 1)
    def _():
        pl.semaphore_wait(barrier, 6)

    @pl.when(inner == 0)
    def _():
        pl.semaphore_wait(barrier, 5)
    vector_ticks = [jobs + VECTOR_STEP * step for step in range(7)]

    def tick(t, carry):
        @pl.when(t == 1)
        def _():
            fill_band_bias(segk_ref, bias_buf)
            for tile in tiles:
                grad_res[tile, :] = grad_branch[tile, :].astype(jnp.float32)

        @pl.when(t + 1 < jobs)
        def _():
            prefetch(t + 1)

        ahead = t + 1 - FIRST

        @pl.when((ahead > 0) & (ahead < chunks))
        def _():
            stage_operands(ahead)

        for lag, action in stages:
            if lag is None:

                @pl.when(t < jobs)
                def _():
                    job(t)

                continue
            chunk = t - FIRST - lag

            @pl.when((chunk >= 0) & (chunk < chunks))
            def _(chunk=chunk, action=action):
                action(chunk)

        @pl.when(t == chunks + FIRST + LAGS["second"] - 1)
        def _():
            swap_start(0, out_act_ref, out_act_out)
            swap_start(1, grad_branch, grad_in_ref)

        for step, when in enumerate(vector_ticks):

            @pl.when(t == when)
            def _(step=step):
                vector_tick(step)

        return carry

    lax.fori_loop(0, max(chunks + FIRST + LAGS["stored"], vector_ticks[-1] + 1), tick, 0)
    swap_wait(0, out_act_ref, out_act_out)
    swap_wait(1, grad_branch, grad_in_ref)


def run_backward(cotangent, gain, segk, out_act, saved, weights, block):
    rows, width = cotangent.shape
    layers, hidden_half = weights[-1].shape[0], weights[-1].shape[1]
    half, quarter = block // 2, block // 4
    low, wide = jnp.bfloat16, jnp.float32
    pairs = width // LANES
    anywhere = pl.BlockSpec(memory_space=pl.ANY)
    in_vmem = pl.BlockSpec(memory_space=pltpu.VMEM)
    vector = (layers * VECTOR_ROWS, width)
    hidden_step = 2 * hidden_half // FFN_STEPS
    vmem = pltpu.VMEM
    return pl.pallas_call(
        functools.partial(backward_kernel, layers, block, hidden_half),
        in_specs=[anywhere] + [in_vmem] * 2 + [anywhere] * (1 + len(saved) + len(weights)),
        out_specs=[anywhere] * 6 + [in_vmem],
        out_shape=[
            jax.ShapeDtypeStruct((rows, width), low),
            jax.ShapeDtypeStruct((rows, width), low),
            jax.ShapeDtypeStruct((layers, hidden_half, width), low),
            jax.ShapeDtypeStruct((layers, width, hidden_half), low),
            jax.ShapeDtypeStruct((layers, block, width), low),
            jax.ShapeDtypeStruct((layers, 3, width, block), low),
            jax.ShapeDtypeStruct(vector, wide),
        ],
        scratch_shapes=[
            vmem((rows, width), low),
            vmem((rows, width), low),
            vmem((FFN_STEPS, rows, hidden_step), low),
            vmem((rows, 6 * block), low),
            vmem((rows, width), wide),
            vmem((rows, width), wide),
            vmem((rows, width), low),
            vmem((2, 3, rows, LANES), low),
            vmem((2, 2, BAND, LANES), low),
            vmem((2, rows, LANES), wide),
            vmem((2, 2, BAND, LANES), wide),
            vmem((2, 2, BAND, LANES), low),
            vmem((pairs, 2, BAND, LANES), low),
            vmem((2, hidden_step, width), low),
            vmem((2, width, hidden_step), low),
            vmem((2, rows, hidden_step), low),
            vmem((rows, width), wide),
            vmem((rows // BAND, BAND, 2 * BAND), wide),
            vmem((1, width), wide),
            vmem((STAGED, 2, rows, block), low),
            vmem((STAGED, rows, block), low),
            vmem((STAGED, 2, block, block), low),
            vmem((CORE_SLOTS, 2, half, block), low),
            vmem((SLOTS, 2, quarter, block), low),
            vmem((SLOTS, 2, quarter, block), low),
            vmem((SLOTS, 2, quarter, block), low),
            vmem((SLOTS, 2, quarter, block), low),
            vmem((SLOTS, 2, quarter, block), low),
            vmem((SLOTS, 2, quarter, block), low),
            vmem((RESULT_SLOTS, block, block), low),
            vmem((5,) + vector, wide),
            pltpu.SemaphoreType.DMA((2, 6)),
            pltpu.SemaphoreType.DMA((2,)),
            pltpu.SemaphoreType.DMA((pairs,)),
            pltpu.SemaphoreType.DMA((pairs,)),
            pltpu.SemaphoreType.DMA((STAGED, 3)),
            pltpu.SemaphoreType.DMA((8, SLOTS)),
            pltpu.SemaphoreType.DMA((8, SLOTS)),
            pltpu.SemaphoreType.DMA((RESULT_SLOTS,)),
            pltpu.SemaphoreType.DMA((6,)),
            pltpu.SemaphoreType.DMA((6,)),
            pltpu.SemaphoreType.DMA((2,)),
            pltpu.SemaphoreType.DMA((2,)),
        ],
        compiler_params=pltpu.CompilerParams(
            collective_id=0, has_side_effects=True, vmem_limit_bytes=VMEM_ASKED
        ),
        name="backward",
    )(cotangent, gain, segk, out_act, *saved, *weights)


FINISH_DEPTH = 4


def finish_kernel(layers, steps, *refs):
    count = len(steps)
    ins, refs = refs[:count], refs[count:]
    vector_ref, refs = refs[0], refs[1:]
    (act_own, act_swapped, grad_in_ref), refs = refs[:3], refs[3:]
    outs, refs = refs[:count], refs[count:]
    qv_out, up_out, bias_out, gain_out, shift_out = refs[:5]
    (act_out, grad_in_out), refs = refs[5:7], refs[7:]
    in_bufs, refs = refs[:count], refs[count:]
    out_bufs, (moved_buf, in_sem, out_sem, copy_sem) = refs[:count], refs[count:]
    y = lax.axis_index("tensor")
    core = lax.axis_index("dp") % 2

    def fetch(index, source):
        return pltpu.make_async_copy(source, moved_buf.at[index], copy_sem.at[index])

    def put(index, target):
        return pltpu.make_async_copy(moved_buf.at[index], target, copy_sem.at[index])

    @pl.when(core == y)
    def _():
        fetch(0, act_own).start()

    @pl.when(core != y)
    def _():
        fetch(0, act_swapped).start()

    fetch(1, grad_in_ref).start()
    plan = []
    for member, (rows, parts) in enumerate(steps):
        for layer in range(layers):
            for part in range(parts):
                plan.append((member, layer, part * rows, rows, (layer * parts + part) % FINISH_DEPTH))

    def view(ref, layer, begin, rows):
        if len(ref.shape) == 4:
            return ref.at[layer, begin // rows]
        return ref.at[layer, pl.ds(begin, rows)]

    def load(entry):
        member, layer, begin, rows, slot = entry
        return pltpu.make_async_copy(
            view(ins[member], layer, begin, rows), in_bufs[member].at[slot], in_sem.at[member, slot]
        )

    def save(entry):
        member, layer, begin, rows, slot = entry
        return pltpu.make_async_copy(
            out_bufs[member].at[slot], view(outs[member], layer, begin, rows), out_sem.at[member, slot]
        )

    for entry in plan[:FINISH_DEPTH]:
        load(entry).start()
    half = qv_out.shape[2]
    for layer in range(layers):
        base = layer * VECTOR_ROWS
        for index in range(2):
            mine = pl.ds(pl.multiple_of(y * half, half), half)
            qv_out[layer, pl.ds(index, 1), :] = vector_ref[pl.ds(base + index, 1), mine]
            width = vector_ref.shape[1]
            up_out[pl.ds(layer, 1), index * width : (index + 1) * width] = vector_ref[
                pl.ds(base + 2 + 2 * y + index, 1), :
            ]
            for row, target in ((6, bias_out), (8, gain_out), (10, shift_out)):
                target[layer, pl.ds(index, 1), :] = vector_ref[pl.ds(base + row + index, 1), :]
    for index, target in enumerate((act_out, grad_in_out)):
        fetch(index, target).wait()
        put(index, target).start()
    busy = {}
    for place, entry in enumerate(plan):
        member, slot = entry[0], entry[4]
        load(entry).wait()
        if (member, slot) in busy:
            save(busy.pop((member, slot))).wait()
        out_bufs[member][slot] = in_bufs[member][slot].astype(jnp.float32)
        save(entry).start()
        busy[(member, slot)] = entry
        if place + FINISH_DEPTH < len(plan):
            load(plan[place + FINISH_DEPTH]).start()
    for entry in busy.values():
        save(entry).wait()
    for index, target in enumerate((act_out, grad_in_out)):
        put(index, target).wait()


def run_finish(reduced, vector, acts, grad_in, block):
    layers, width = reduced[0].shape[0], vector.shape[1]
    hidden_half = reduced[0].shape[1]
    wide, low = jnp.float32, jnp.bfloat16
    shape = jax.ShapeDtypeStruct
    anywhere = pl.BlockSpec(memory_space=pl.ANY)
    in_vmem = pl.BlockSpec(memory_space=pltpu.VMEM)
    steps = (
        (block, hidden_half // block),
        (block // 2, width * 2 // block),
        (block, 1),
        (width, 3),
    )
    blocks = ((block, width), (block // 2, hidden_half), (block, width), (width, block))
    deep = lambda kind: [pltpu.VMEM((FINISH_DEPTH,) + size, kind) for size in blocks]
    return pl.pallas_call(
        functools.partial(finish_kernel, layers, steps),
        in_specs=[anywhere] * len(reduced) + [in_vmem] + [anywhere] * 3,
        out_specs=[anywhere] * len(reduced) + [in_vmem] * 5 + [anywhere] * 2,
        out_shape=[shape(member.shape, wide) for member in reduced]
        + [
            shape((layers, 2, block), wide),
            shape((layers, hidden_half), wide),
            shape((layers, 2, width), wide),
            shape((layers, 2, width), wide),
            shape((layers, 2, width), wide),
        ]
        + [shape(grad_in.shape, low)] * 2,
        scratch_shapes=deep(low)
        + deep(wide)
        + [
            pltpu.VMEM((2,) + grad_in.shape, low),
            pltpu.SemaphoreType.DMA((4, FINISH_DEPTH)),
            pltpu.SemaphoreType.DMA((4, FINISH_DEPTH)),
            pltpu.SemaphoreType.DMA((2,)),
        ],
        compiler_params=pltpu.CompilerParams(vmem_limit_bytes=VMEM_ASKED),
        name="finish",
    )(*reduced, vector, *acts, grad_in)


def local_split(
    tokens_in,
    segments,
    w_qkv,
    qv_bias,
    w_out,
    w_up,
    up_bias,
    w_down,
    out_bias,
    ln_gain,
    ln_bias,
    cotangent,
):
    block = w_qkv.shape[3]
    weights = (w_qkv.transpose(0, 2, 1, 3), w_out, w_up, w_down)
    act_own, cot, segk, *rest = run_forward(
        tokens_in,
        cotangent,
        segments,
        weights,
        (qv_bias, up_bias),
        out_bias,
        ln_gain,
        ln_bias,
        block,
    )
    others, saved = rest[: len(weights)], rest[len(weights) :]
    both = [member for pair in zip(weights, others) for member in pair]
    act_swapped, grad_in, *reduced, summed = run_backward(
        cot, ln_gain, segk, act_own, saved, both, block
    )
    *grads, grad_qv, grad_up_bias, grad_bias, grad_gain, grad_shift, out_act, grad_in = run_finish(
        reduced, summed, (act_own, act_swapped), grad_in, block
    )
    grad_down, grad_up, grad_out, grad_qkv = grads
    return (
        out_act,
        grad_in,
        grad_qkv.transpose(0, 2, 1, 3),
        grad_qv,
        grad_out,
        grad_up,
        grad_up_bias,
        grad_down,
        grad_bias,
        grad_gain,
        grad_shift,
    )


def solution(mesh):
    sizes = (mesh.shape["dp"], mesh.shape["tensor"])
    local = local_split if sizes == (16, 2) else local_general
    return jax.shard_map(
        local,
        mesh=mesh,
        in_specs=(
            P(("dp", "tensor"), None),
            P("dp", None),
            P(None, None, None, "tensor"),
            P(None, None, "tensor"),
            P(None, "tensor", None),
            P(None, None, "tensor"),
            P(None, "tensor"),
            P(None, "tensor", None),
            P(),
            P(),
            P(),
            P(("dp", "tensor"), None),
        ),
        out_specs=(
            P(("dp", "tensor"), None),
            P(("dp", "tensor"), None),
            P(None, None, None, "tensor"),
            P(None, None, "tensor"),
            P(None, "tensor", None),
            P(None, None, "tensor"),
            P(None, "tensor"),
            P(None, "tensor", None),
            P(),
            P(),
            P(),
        ),
        check_vma=False,
    )
```
